32 devices in a mesh: items: 8 (over y, x, core), frames: 4 (over z).
Axes of the slice: x: 2, y: 2, z: 4, core: 2. Of those that a mesh axis runs over, the one named last changes fastest.
Arguments:
- media: bfloat16 [32, 4, 256, 1536], P('items', 'frames'), may hold values from -6 to 6
- cotangent: float32 [32, 64, 1536], P('items', 'frames'), may hold values from -6 to 6
- frame_count: int32 [32], replicated, may hold values from 1 to 4, as said below
- frame_start: int32 [32], replicated, may hold values from 0 to 3
- latents: float32 [64, 1536], replicated, may hold values from -6 to 6
- time_embed: float32 [4, 1536], replicated, may hold values from -6 to 6
- media_gain: float32 [1536], replicated, may hold values from 0.5 to 1.5
- media_bias: float32 [1536], replicated, may hold values from -4 to 4
- latent_gain: float32 [1536], replicated, may hold values from 0.5 to 1.5
- latent_bias: float32 [1536], replicated, may hold values from -4 to 4
- ffn_gain: float32 [1536], replicated, may hold values from 0.5 to 1.5
- ffn_bias: float32 [1536], replicated, may hold values from -4 to 4
- query_weight: bfloat16 [1536, 1536], P('items'), may hold values from -0.21875 to 0.21875
- key_weight: bfloat16 [1536, 1536], P('items'), may hold values from -0.21875 to 0.21875
- value_weight: bfloat16 [1536, 1536], P('items'), may hold values from -0.15625 to 0.15625
- out_weight: bfloat16 [1536, 1536], P('items'), may hold values from -0.875 to 0.875
- up_weight: bfloat16 [1536, 6144], P('items'), may hold values from -0.15625 to 0.15625
- down_weight: bfloat16 [6144, 1536], P('items'), may hold values from -0.078125 to 0.078125
Outputs:
- latents_out: float32 [32, 64, 1536], P('items', 'frames')
- entropy: float32 [32, 64], P('items', 'frames')
- media_grad: bfloat16 [32, 4, 256, 1536], P('items', 'frames')
- latents_grad: float32 [64, 1536], replicated
- time_grad: float32 [4, 1536], P(None, 'items')
- media_gain_grad: float32 [1536], P('items')
- media_bias_grad: float32 [1536], P('items')
- latent_gain_grad: float32 [1536], replicated
- latent_bias_grad: float32 [1536], replicated
- ffn_gain_grad: float32 [1536], replicated
- ffn_bias_grad: float32 [1536], replicated
- query_grad: float32 [1536, 1536], P('items')
- key_grad: float32 [1536, 1536], P('items')
- value_grad: float32 [1536, 1536], P('items')
- out_grad: float32 [1536, 1536], P('items')
- up_grad: float32 [1536, 6144], P('items')
- down_grad: float32 [6144, 1536], P('items')
The draws below stay inside these ranges and needn't reach their ends.
Inputs may be any that keep to these rules, and one draw needn't show every extreme that they name: `frame_count`: items whose index is 0 or 1 modulo 4 are single images with one frame; the others are clips of 2 to 4 frames, and each aligned block of 4 items holds a clip of all 4 frames.
All inputs are finite; a program needn't handle non-finite values.
Results may differ from the reference program's by a relative error of at most 0.0128.
The reference program's roundings to bfloat16 on the way count: a program that leaves them out, or rounds other values in their place, can miss the bound.
Values may be sent and summed in bfloat16 or wider, within the bound.
No kernel may reach another device: no remote copies, remote signals or barrier semaphores. Data moves between devices by JAX's collectives and lax.ppermute only.
A program may use at most 320 MiB of HBM per device.

```python
import jax
import jax.numpy as jnp
from jax import lax

D = 1536
HEADS = 16
HEAD_DIM = 96
FF = 6144
LAT = 64
PATCHES = 256
ITEM_DEV = 4
ITEMS = 32
FRAMES = 4


def draw_frame_count(key, part):
    key = jax.random.fold_in(key, 11)
    lengths = jax.random.randint(jax.random.fold_in(key, 1), (ITEMS,), 2, FRAMES + 1)
    picked = jax.random.randint(jax.random.fold_in(key, 2), (ITEMS // ITEM_DEV,), 0, ITEM_DEV // 2)
    full_place = 4 * (picked // 2) + 2 + picked % 2
    index = jnp.arange(ITEMS, dtype=jnp.int32)
    is_full = index % ITEM_DEV == jnp.repeat(full_place, ITEM_DEV)
    is_image = index % 4 < 2
    return jnp.where(is_image, 1, jnp.where(is_full, FRAMES, lengths)).astype(jnp.int32)


def draw_frame_start(key, part):
    key = jax.random.fold_in(key, 12)
    return jax.random.randint(key, (ITEMS,), 0, FRAMES).astype(jnp.int32)


def steps_of(stream_key, shape, split, smallest, top_value):
    level = 1.0
    for position, blocks in split:
        draws = jax.random.uniform(jax.random.fold_in(jax.random.fold_in(stream_key, 6), position), (blocks,), jnp.float32, smallest / len(split), top_value / len(split))
        level = level * jnp.repeat(jnp.exp(draws), shape[position] // blocks).reshape((-1,) + (1,) * (len(shape) - 1 - position))
    return level


def scatter_about(rng, dims, deviation, reach, shards=(), kind=jnp.bfloat16):
    factor_of = steps_of(rng, dims, shards, -0.22, 0.18) if shards else 1.0
    array = jax.random.normal(rng, dims, jnp.float32) * deviation * factor_of
    return jnp.minimum(jnp.maximum(array, -reach), reach).astype(kind)


def setup_inputs(seed: int = 0) -> dict:
    splits = jax.random.split(jax.random.key(seed), 19)
    return {
        "media": scatter_about(splits[0], (ITEMS, FRAMES, PATCHES, D), 1.0, 6.0, ((0, 8), (1, 4))),
        "cotangent": scatter_about(splits[1], (ITEMS, LAT, D), 1.0, 6.0, ((0, 8), (1, 4)), jnp.float32),
        "frame_count": draw_frame_count(jax.random.fold_in(splits[18], 71), 0),
        "frame_start": draw_frame_start(jax.random.fold_in(splits[18], 71), 0),
        "latents": scatter_about(splits[4], (LAT, D), 1.0, 6.0, (), jnp.float32),
        "time_embed": scatter_about(splits[5], (FRAMES, D), 1.0, 6.0, (), jnp.float32),
        "media_gain": jnp.clip(1.0 + 0.1 * jax.random.normal(splits[6], (D,), jnp.float32), 0.5, 1.5),
        "media_bias": scatter_about(splits[7], (D,), 0.3, 4.0, (), jnp.float32),
        "latent_gain": jnp.clip(1.0 + 0.1 * jax.random.normal(splits[8], (D,), jnp.float32), 0.5, 1.5),
        "latent_bias": scatter_about(splits[9], (D,), 0.3, 4.0, (), jnp.float32),
        "ffn_gain": jnp.clip(1.0 + 0.1 * jax.random.normal(splits[10], (D,), jnp.float32), 0.5, 1.5),
        "ffn_bias": scatter_about(splits[11], (D,), 0.3, 4.0, (), jnp.float32),
        "query_weight": scatter_about(splits[12], (D, D), (D // 2) ** -0.5, 0.21875, ((0, 8),)),
        "key_weight": scatter_about(splits[13], (D, D), (D // 2) ** -0.5, 0.21875, ((0, 8),)),
        "value_weight": scatter_about(splits[14], (D, D), D ** -0.5, 0.15625, ((0, 8),)),
        "out_weight": scatter_about(splits[15], (D, D), (D // 32) ** -0.5, 0.875, ((0, 8),)),
        "up_weight": scatter_about(splits[16], (D, FF), D ** -0.5, 0.15625, ((0, 8),)),
        "down_weight": scatter_about(splits[17], (FF, D), FF ** -0.5, 0.078125, ((0, 8),)),
    }


@jax.custom_vjp
def low(v):
    return lax.optimization_barrier(v.astype(jnp.bfloat16)).astype(jnp.float32)

@jax.custom_vjp
def low_back(v):
    return v

def low_keep(v):
    return (low(v), None)

def low_pass(kept, grad):
    return (grad,)

def back_keep(v):
    return (v, None)

def back_low(kept, grad):
    return (low(grad),)
low.defvjp(low_keep, low_pass)
low_back.defvjp(back_keep, back_low)
EPSILON = 1e-05
MASKED = -1e+30

def layer_norm(inputs, norm_gain, norm_bias):
    center = inputs - lax.optimization_barrier(jnp.mean(inputs, axis=-1, keepdims=True))
    spread = lax.optimization_barrier(jnp.mean(center * center, axis=-1, keepdims=True))
    return center * lax.rsqrt(spread + EPSILON) * norm_gain + norm_bias

def matmul(left_side, right_side):
    return jnp.dot(left_side, right_side, precision=lax.Precision.HIGHEST, preferred_element_type=jnp.float32)

def einsum_high(form, left_side, right_side):
    return jnp.einsum(form, left_side, right_side, precision=lax.Precision.HIGHEST, preferred_element_type=jnp.float32)

def forward(latents, time_embed, media_gain, media_bias, latent_gain, latent_bias, ffn_gain, ffn_bias, query_weight, key_weight, value_weight, out_weight, up_weight, down_weight, media_float, frame_count, frame_start):
    score_scale = HEAD_DIM ** (-0.5)
    lat_norm = low(layer_norm(latents, latent_gain, latent_bias))
    queries = low(low_back(matmul(lat_norm, query_weight))).reshape(LAT, HEADS, HEAD_DIM)
    lat_keys = low(low_back(matmul(lat_norm, key_weight))).reshape(LAT, HEADS, HEAD_DIM)
    lat_values = low(low_back(matmul(lat_norm, value_weight))).reshape(LAT, HEADS, HEAD_DIM)
    slot_ids = jnp.arange(FRAMES, dtype=jnp.int32)
    first_slot = (slot_ids == 0).astype(jnp.float32)

    def one_item(packed):
        media_item, item_count, item_start = packed
        offset = (slot_ids - item_start) % FRAMES
        valid_slot = (offset < item_count).astype(jnp.float32)
        slot_mask = valid_slot[:, None, None, None]
        with_time = media_item + jnp.take(time_embed, offset, axis=0)[:, None, :]
        normed = low(layer_norm(with_time, media_gain, media_bias)).reshape(FRAMES * PATCHES, D)
        media_keys = low(low_back(matmul(normed, key_weight))).reshape(FRAMES, PATCHES, HEADS, HEAD_DIM)
        media_values = low(low_back(matmul(normed, value_weight))).reshape(FRAMES, PATCHES, HEADS, HEAD_DIM)
        scores = low_back(score_scale * einsum_high('qhe,fphe->fhqp', queries, media_keys))
        lat_scores = low_back(score_scale * einsum_high('qhe,khe->hqk', queries, lat_keys))
        masked = jnp.where(slot_mask > 0, scores, MASKED)
        block_top = lax.optimization_barrier(jnp.max(masked, axis=3))
        joined_top = jnp.maximum(block_top, lax.optimization_barrier(jnp.max(lat_scores, axis=2))[None])
        block_top = jnp.where(first_slot[:, None, None] > 0, joined_top, block_top)
        block_exp = jnp.exp(masked - block_top[..., None]) * slot_mask
        lat_exp = jnp.exp(lat_scores - block_top[0][..., None])
        slot_first = first_slot[:, None, None]
        part_total = lax.optimization_barrier(jnp.sum(block_exp, axis=3)) + slot_first * lax.optimization_barrier(jnp.sum(lat_exp, axis=2))[None]
        part_moment = lax.optimization_barrier(jnp.sum(block_exp * scores, axis=3)) + slot_first * lax.optimization_barrier(jnp.sum(lat_exp * lat_scores, axis=2))[None]
        part_out = einsum_high('fhqp,fphe->fqhe', low(block_exp), media_values)
        part_out = part_out + first_slot[:, None, None, None] * einsum_high('hqk,khe->qhe', low(lat_exp), lat_values)[None]
        peak_score = lax.optimization_barrier(jnp.max(block_top, axis=0))
        factor = jnp.exp(block_top - peak_score[None])
        whole_sum = lax.optimization_barrier(jnp.sum(factor * part_total, axis=0))
        log_total = peak_score + jnp.log(whole_sum)
        mean_score = lax.optimization_barrier(jnp.sum(factor * part_moment, axis=0)) / whole_sum
        merged = einsum_high('fhq,fqhe->qhe', factor, part_out) / jnp.transpose(whole_sum)[:, :, None]
        entropy = lax.optimization_barrier(jnp.mean(log_total - mean_score, axis=0))
        attended = low(low_back(merged.reshape(LAT, D)))
        mid_rows = latents + low_back(matmul(attended, out_weight))
        ffn_in = low(layer_norm(mid_rows, ffn_gain, ffn_bias))
        upward = low_back(matmul(ffn_in, up_weight))
        hidden = low(jax.nn.gelu(upward, approximate=False))
        result = mid_rows + low_back(matmul(hidden, down_weight))
        return (result, entropy)
    return lax.map(jax.checkpoint(one_item), (media_float, frame_count, frame_start))

def reference(media, cotangent, frame_count, frame_start, latents, time_embed, media_gain, media_bias, latent_gain, latent_bias, ffn_gain, ffn_bias, query_weight, key_weight, value_weight, out_weight, up_weight, down_weight):
    inputs = (latents, time_embed, media_gain, media_bias, latent_gain, latent_bias, ffn_gain, ffn_bias, query_weight.astype(jnp.float32), key_weight.astype(jnp.float32), value_weight.astype(jnp.float32), out_weight.astype(jnp.float32), up_weight.astype(jnp.float32), down_weight.astype(jnp.float32), media.astype(jnp.float32))

    def primal(*values):
        return forward(*values, frame_count, frame_start)
    (outputs, entropies), pullback = jax.vjp(primal, *inputs)
    gradients = pullback((cotangent, jnp.zeros_like(entropies)))
    return (outputs, entropies, gradients[14].astype(jnp.bfloat16), gradients[0], gradients[1], gradients[2], gradients[3], gradients[4], gradients[5], gradients[6], gradients[7], gradients[8], gradients[9], gradients[10], gradients[11], gradients[12], gradients[13])
```

```python
import functools

import jax
import jax.numpy as jnp
from jax import lax
from jax.experimental import pallas as pl
from jax.experimental.pallas import tpu as pltpu
from jax.sharding import PartitionSpec as P

HEADS = 16
GROUP = 4
EPSILON = 1e-05
MASKED = -1e30
F32 = jnp.float32
BF16 = jnp.bfloat16
HIGHEST = lax.Precision.HIGHEST


def layer_norm(inputs, norm_gain, norm_bias):
    center = inputs - jnp.mean(inputs, axis=-1, keepdims=True)
    spread = jnp.mean(center * center, axis=-1, keepdims=True)
    return center * lax.rsqrt(spread + EPSILON) * norm_gain + norm_bias


def norm_back(inputs, norm_gain, norm_bias, gradient):
    unused, pullback = jax.vjp(layer_norm, inputs, norm_gain, norm_bias)
    return pullback(gradient)


def gelu_exact(inputs):
    return jax.nn.gelu(inputs, approximate=False)


def matmul(left_side, right_side):
    return jnp.dot(left_side, right_side, preferred_element_type=F32)


def transposed_left(left_side, right_side):
    return lax.dot_general(
        left_side, right_side, (((0,), (0,)), ((), ())), preferred_element_type=F32
    )


def transposed_right(left_side, right_side):
    return lax.dot_general(
        left_side, right_side, (((1,), (1,)), ((), ())), preferred_element_type=F32
    )


def bit_count(axis):
    return lax.axis_size(axis).bit_length() - 1


def swap(x, axis, bit):
    size = lax.axis_size(axis)
    return lax.ppermute(x, axis, [(i, i ^ (1 << bit)) for i in range(size)])


def bit_orders(axis):
    upper = list(range(1, bit_count(axis)))
    return upper, upper[::-1]


def halves(x):
    middle = x.shape[-1] // 2
    return x[..., :middle], x[..., middle:]


def gather_xor(x, axis):
    size = lax.axis_size(axis)
    bits = bit_count(axis)

    def one(part, order):
        state = part.reshape((1,) * bits + part.shape)
        for bit in order:
            state = jnp.concatenate([state, swap(state, axis, bit)], bits - 1 - bit)
        return state.reshape((size,) + part.shape)

    first, second = halves(x)
    upper, lower = bit_orders(axis)
    return jnp.concatenate([one(first, upper + [0]), one(second, lower + [0])], -1)


def scatter_xor(x, axis, wire):
    bits = bit_count(axis)

    def one(part, order):
        state = part.reshape((2,) * bits + part.shape[1:])
        for bit in order:
            place = bits - 1 - bit
            keep = lax.slice_in_dim(state, 0, 1, axis=place)
            send = lax.slice_in_dim(state, 1, 2, axis=place)
            state = keep + swap(send.astype(wire), axis, bit).astype(F32)
        return state.reshape(part.shape[1:])

    first, second = halves(x)
    upper, lower = bit_orders(axis)
    return jnp.concatenate([one(first, [0] + upper), one(second, [0] + lower)], -1)


def sum_xor(x, axis):
    def one(part, order):
        for bit in order:
            part = part + swap(part, axis, bit)
        return part

    first, second = halves(x)
    upper, lower = bit_orders(axis)
    return jnp.concatenate([one(first, [0] + upper), one(second, [0] + lower)], -1)


def xor_pick(x, index, count):
    return jnp.stack([lax.dynamic_index_in_dim(x, index ^ d, 0, False) for d in range(count)])


def shift_from(x, axis, step):
    size = lax.axis_size(axis)
    return lax.ppermute(x, axis, [((i + step) % size, i) for i in range(size)])


def gather_shift(x, axis):
    size = lax.axis_size(axis)
    return jnp.stack([x] + [shift_from(x, axis, s) for s in range(1, size)])


def gather_order(x, axis):
    size = lax.axis_size(axis)
    spread = gather_shift(x, axis)
    return lax.dynamic_slice_in_dim(
        jnp.concatenate([spread, spread], 0), (size - lax.axis_index(axis)) % size, size, 0
    )


def sum_all(x, axis):
    total = x
    for s in range(1, lax.axis_size(axis)):
        total = total + shift_from(x, axis, s)
    return total


def scatter_shift(pieces, axis):
    size = lax.axis_size(axis)
    me = lax.axis_index(axis)
    out = []
    for s in range(size):
        piece = lax.dynamic_index_in_dim(pieces, (me + s) % size, 0, False)
        if s:
            piece = lax.ppermute(piece, axis, [(i, (i + s) % size) for i in range(size)])
        out.append(piece)
    return out


def reduce_rows(x, axis):
    size = lax.axis_size(axis)
    rows = x.shape[0] // size
    pieces = scatter_shift(x.reshape((size, rows) + x.shape[1:]), axis)
    total = functools.reduce(jnp.add, [p.astype(F32) for p in pieces])
    return gather_order(total.astype(BF16), axis).reshape(x.shape).astype(F32)


def exchange_rows(x, axis):
    size = lax.axis_size(axis)
    me = lax.axis_index(axis)
    out = []
    for d in range(size):
        piece = lax.dynamic_index_in_dim(x, me ^ d, 0, False)
        if d:
            piece = lax.ppermute(piece, axis, [(i, i ^ d) for i in range(size)])
        out.append(piece)
    return jnp.stack(out)


def head_masks(rows, width, head_size):
    lane = lax.broadcasted_iota(jnp.int32, (rows, width), 1)
    return [
        jnp.logical_and(lane >= h * head_size, lane < (h + 1) * head_size)
        for h in range(width // head_size)
    ]


def spread_heads(block, masks):
    return jnp.concatenate([jnp.where(m, block, jnp.zeros_like(block)) for m in masks], 0)


def collect_heads(block, masks):
    rows = block.shape[0] // len(masks)
    total = jnp.where(masks[0], block[:rows], 0.0)
    for h in range(1, len(masks)):
        total = total + jnp.where(masks[h], block[h * rows : (h + 1) * rows], 0.0)
    return total


def forward_kernel(
    flag_ref, key_ref, value_ref, query_ref, out_ref, stat_ref, *, items, patches, scale, head_size
):
    lats, width = query_ref.shape
    masks = head_masks(lats, width, head_size)
    queries = spread_heads(query_ref[...].astype(F32), masks).astype(BF16)
    first = flag_ref[items] > 0
    base = items * patches
    lat_keys = key_ref[base : base + lats, :]
    lat_values = value_ref[base : base + lats, :]
    lat_scores = scale * transposed_right(lat_keys, queries)
    lat_max = jnp.max(lat_scores, axis=0, keepdims=True)
    for i in range(items):
        valid = flag_ref[i] > 0
        rows = slice(i * patches, (i + 1) * patches)
        scores = scale * transposed_right(key_ref[rows, :], queries)
        masked = jnp.where(valid, scores, MASKED)
        top = jnp.max(masked, axis=0, keepdims=True)
        top = jnp.where(first, jnp.maximum(top, lat_max), top)
        block_exp = jnp.where(valid, jnp.exp(masked - top), 0.0)
        lat_exp = jnp.where(first, jnp.exp(lat_scores - jnp.where(first, top, lat_max)), 0.0)
        total = jnp.sum(block_exp, axis=0, keepdims=True) + jnp.sum(lat_exp, axis=0, keepdims=True)
        moment = jnp.sum(block_exp * scores, axis=0, keepdims=True) + jnp.sum(
            lat_exp * lat_scores, axis=0, keepdims=True
        )
        part = transposed_left(block_exp.astype(BF16), value_ref[rows, :]) + transposed_left(
            lat_exp.astype(BF16), lat_values
        )
        out_ref[i * lats : (i + 1) * lats, :] = collect_heads(part, masks).astype(out_ref.dtype)
        stat_ref[0, i, 0:1, :] = top
        stat_ref[0, i, 1:2, :] = total
        stat_ref[0, i, 2:3, :] = moment
        stat_ref[0, i, 3:8, :] = jnp.zeros((5, stat_ref.shape[3]), F32)


def backward_kernel(
    flag_ref,
    key_ref,
    value_ref,
    query_ref,
    grad_ref,
    stat_ref,
    both_ref,
    sums_ref,
    held_ref,
    *,
    items,
    patches,
    scale,
    head_size,
):
    lats, width = query_ref.shape

    @pl.when(pl.program_id(1) == 1)
    def _():
        both_ref[...] = held_ref[...]

    @pl.when(pl.program_id(1) == 0)
    def _():
        masks = head_masks(lats, width, head_size)
        queries = spread_heads(query_ref[...].astype(F32), masks).astype(BF16)
        first = flag_ref[items] > 0
        base = items * patches
        lat_keys = key_ref[base : base + lats, :]
        lat_values = value_ref[base : base + lats, :]
        lat_scores = scale * transposed_right(lat_keys, queries)
        grad_query = jnp.zeros((queries.shape[0], width), F32)
        lat_grad_key = jnp.zeros((lats, width), F32)
        lat_grad_value = jnp.zeros((lats, width), F32)
        for i in range(items):
            valid = flag_ref[i] > 0
            rows = slice(i * patches, (i + 1) * patches)
            top = stat_ref[0, i, 0:1, :]
            log_total = stat_ref[0, i, 1:2, :]
            delta = stat_ref[0, i, 2:3, :]
            rescale = jnp.exp(top - log_total)
            keys = key_ref[rows, :]
            values = value_ref[rows, :]
            grads = spread_heads(
                grad_ref[i * lats : (i + 1) * lats, :].astype(F32), masks
            ).astype(BF16)
            masked = jnp.where(valid, scale * transposed_right(keys, queries), MASKED)
            probs = jnp.where(valid, jnp.exp(masked - log_total), 0.0)
            block_exp = jnp.where(valid, jnp.exp(masked - top), 0.0)
            weights = (block_exp.astype(BF16).astype(F32) * rescale).astype(BF16)
            grad_probs = transposed_right(values, grads)
            grad_scores = (probs * (grad_probs - delta)).astype(BF16)
            both_ref[rows, :] = (scale * matmul(grad_scores, queries)).astype(BF16)
            held_ref[rows, :] = matmul(weights, grads).astype(BF16)
            grad_query = grad_query + transposed_left(grad_scores, keys)

            lat_probs = jnp.where(first, jnp.exp(lat_scores - log_total), 0.0)
            lat_exp = jnp.where(first, jnp.exp(lat_scores - top), 0.0)
            lat_weights = (lat_exp.astype(BF16).astype(F32) * rescale).astype(BF16)
            lat_grad_probs = transposed_right(lat_values, grads)
            lat_grad_scores = (lat_probs * (lat_grad_probs - delta)).astype(BF16)
            lat_grad_key = lat_grad_key + matmul(lat_grad_scores, queries)
            lat_grad_value = lat_grad_value + matmul(lat_weights, grads)
            grad_query = grad_query + transposed_left(lat_grad_scores, lat_keys)
        sums_ref[0] = scale * collect_heads(grad_query, masks)
        sums_ref[1] = scale * lat_grad_key
        sums_ref[2] = lat_grad_value


def attend(flags, rows, queries, items, patches):
    lats, model_width = queries.shape
    head_size = model_width // HEADS
    width = GROUP * head_size
    groups = HEADS // GROUP
    tokens = rows.shape[0]
    stack = GROUP * lats
    work = items * groups * stack * width * (patches + lats) * 4
    return pl.pallas_call(
        functools.partial(
            forward_kernel,
            items=items,
            patches=patches,
            scale=head_size**-0.5,
            head_size=head_size,
        ),
        grid=(groups,),
        in_specs=[
            pl.BlockSpec(memory_space=pltpu.SMEM),
            pl.BlockSpec((tokens, width), lambda g: (0, g)),
            pl.BlockSpec((tokens, width), lambda g: (0, g + groups)),
            pl.BlockSpec((lats, width), lambda g: (0, g)),
        ],
        out_specs=[
            pl.BlockSpec((items * lats, width), lambda g: (0, g)),
            pl.BlockSpec((1, items, 8, stack), lambda g: (g, 0, 0, 0)),
        ],
        out_shape=[
            jax.ShapeDtypeStruct((items * lats, model_width), BF16),
            jax.ShapeDtypeStruct((groups, items, 8, stack), F32),
        ],
        cost_estimate=pl.CostEstimate(
            flops=work, bytes_accessed=rows.size * 2 + items * lats * model_width * 2,
            transcendentals=items * groups * stack * patches,
        ),
        compiler_params=pltpu.CompilerParams(vmem_limit_bytes=40 * 2**20),
    )(flags, rows, rows, queries)


def attend_back(flags, rows, queries, grads, stats, items, patches):
    lats, model_width = queries.shape
    head_size = model_width // HEADS
    width = GROUP * head_size
    groups = HEADS // GROUP
    tokens = rows.shape[0]
    stack = GROUP * lats
    work = items * groups * stack * width * (patches + lats) * 10
    return pl.pallas_call(
        functools.partial(
            backward_kernel,
            items=items,
            patches=patches,
            scale=head_size**-0.5,
            head_size=head_size,
        ),
        grid=(groups, 2),
        in_specs=[
            pl.BlockSpec(memory_space=pltpu.SMEM),
            pl.BlockSpec((tokens, width), lambda g, s: (0, g)),
            pl.BlockSpec((tokens, width), lambda g, s: (0, g + groups)),
            pl.BlockSpec((lats, width), lambda g, s: (0, g)),
            pl.BlockSpec((items * lats, width), lambda g, s: (0, g)),
            pl.BlockSpec((1, items, 8, stack), lambda g, s: (g, 0, 0, 0)),
        ],
        out_specs=[
            pl.BlockSpec((items * patches, width), lambda g, s: (0, g + s * groups)),
            pl.BlockSpec((3, lats, width), lambda g, s: (0, 0, g)),
        ],
        out_shape=[
            jax.ShapeDtypeStruct((items * patches, 2 * model_width), BF16),
            jax.ShapeDtypeStruct((3, lats, model_width), F32),
        ],
        scratch_shapes=[pltpu.VMEM((items * patches, width), BF16)],
        cost_estimate=pl.CostEstimate(
            flops=work, bytes_accessed=rows.size * 4,
            transcendentals=2 * items * groups * stack * patches,
        ),
        compiler_params=pltpu.CompilerParams(vmem_limit_bytes=40 * 2**20),
    )(flags, rows, rows, queries, grads, stats)


def body(
    media,
    cotangent,
    frame_count,
    frame_start,
    latents,
    time_embed,
    media_gain,
    media_bias,
    latent_gain,
    latent_bias,
    ffn_gain,
    ffn_bias,
    query_weight,
    key_weight,
    value_weight,
    out_weight,
    up_weight,
    down_weight,
):
    items = media.shape[0]
    patches = media.shape[2]
    width = media.shape[3]
    lats = latents.shape[0]
    frame_total = time_embed.shape[0]
    row_total = cotangent.shape[1]
    own = items * row_total
    groups = HEADS // GROUP
    head_size = width // HEADS
    tokens = items * patches
    shard = query_weight.shape[0]
    hidden_shard = down_weight.shape[0]
    item_size = lax.axis_size("items")
    frame_size = lax.axis_size("frames")
    item_index = lax.axis_index("items")
    slot = lax.axis_index("frames")
    row_base = slot * row_total

    kv_full = lax.all_gather(
        jnp.concatenate([key_weight, value_weight], 1), "items", axis=0, tiled=True
    )
    out_full = lax.all_gather(out_weight, "items", axis=0, tiled=True)
    grad_out = cotangent.reshape(own, width)
    grad_low = grad_out.astype(BF16)
    low_every = lax.all_gather(gather_shift(grad_low, "frames"), "items", axis=0)
    up_parts = exchange_rows(
        jnp.transpose(up_weight.reshape(shard, item_size, hidden_shard), (1, 0, 2)), "items"
    )
    up_slice = xor_pick(up_parts, item_index, item_size).reshape(width, hidden_shard)

    counts = lax.dynamic_slice_in_dim(frame_count, item_index * items, items)
    starts = lax.dynamic_slice_in_dim(frame_start, item_index * items, items)
    offset = (slot - starts) % frame_total
    flags = jnp.concatenate(
        [(offset < counts).astype(jnp.int32), (slot == 0).astype(jnp.int32)[None]]
    )
    picker = (offset[:, None] == jnp.arange(frame_total, dtype=jnp.int32)[None, :]).astype(F32)
    time_rows = jnp.dot(picker, time_embed, precision=HIGHEST, preferred_element_type=F32)
    with_time = media[:, 0].astype(F32) + time_rows[:, None, :]
    normed = layer_norm(with_time, media_gain, media_bias).astype(BF16)
    flat_norm = normed.reshape(tokens, width)
    lat_norm = layer_norm(latents, latent_gain, latent_bias).astype(BF16)
    col_base = item_index * shard
    lat_cols = lax.dynamic_slice_in_dim(lat_norm, col_base, shard, 1)
    queries = sum_xor(matmul(lat_cols, query_weight), "items").astype(BF16)

    rows = matmul(jnp.concatenate([flat_norm, lat_norm], 0), kv_full).astype(BF16)
    part_out, stats = attend(flags, rows, queries, items, patches)

    pieces = jnp.transpose(
        part_out.reshape(items, frame_size, row_total, width), (1, 0, 2, 3)
    ).reshape(frame_size, own, width)
    part_every = jnp.stack(scatter_shift(pieces, "frames"))
    stat_every = jnp.stack(
        [stats]
        + [
            lax.ppermute(
                stats, "frames", [(i, (i + s) % frame_size) for i in range(frame_size)]
            )
            for s in range(1, frame_size)
        ]
    )
    top_every, total_every, moment_every = (
        stat_every[:, :, :, 0],
        stat_every[:, :, :, 1],
        stat_every[:, :, :, 2],
    )
    peak = jnp.max(top_every, axis=0)
    factor = jnp.exp(top_every - peak[None])
    whole = jnp.sum(factor * total_every, axis=0)
    log_total = peak + jnp.log(whole)
    mean_score = jnp.sum(factor * moment_every, axis=0) / whole
    entropy_all = jnp.mean(
        (log_total - mean_score).reshape(groups, items, GROUP, lats), axis=(0, 2)
    )
    entropy = lax.dynamic_slice_in_dim(entropy_all, row_base, row_total, 1)
    share = (factor / whole[None]).reshape(frame_size, groups, items, GROUP, lats)
    share = lax.dynamic_slice_in_dim(share, row_base, row_total, 4)
    share = jnp.transpose(share, (0, 2, 4, 1, 3)).reshape(frame_size * own, HEADS)
    head_of = jnp.arange(width, dtype=jnp.int32) // head_size
    expand = (jnp.arange(HEADS, dtype=jnp.int32)[:, None] == head_of[None, :]).astype(F32)
    share_wide = jnp.dot(share, expand, precision=HIGHEST, preferred_element_type=F32)
    merged = jnp.sum(
        part_every.astype(F32) * share_wide.reshape(frame_size, own, width), axis=0
    )
    attended = merged.astype(BF16)

    base_rows = lax.dynamic_slice_in_dim(latents, row_base, row_total, 0)
    mid_rows = (
        base_rows[None] + matmul(attended, out_full).reshape(items, row_total, width)
    ).reshape(own, width)
    ffn_in = layer_norm(mid_rows, ffn_gain, ffn_bias).astype(BF16)
    ffn_shift = gather_shift(ffn_in, "frames")[1:]
    ffn_plane = gather_xor(ffn_in, "items").reshape(-1, width)

    low_plane = xor_pick(low_every[:, 0], item_index, item_size).reshape(-1, width)
    upward = matmul(ffn_plane, up_slice)
    hidden = gelu_exact(upward).astype(BF16)
    grad_hidden = transposed_right(low_plane, down_weight)
    grad_up = jax.vjp(gelu_exact, upward)[1](grad_hidden)[0].astype(BF16)
    grad_ffn = scatter_xor(
        transposed_right(grad_up, up_slice).reshape(item_size, own, width), "items", BF16
    )
    result = mid_rows + scatter_xor(
        matmul(hidden, down_weight).reshape(item_size, own, width), "items", BF16
    )

    grad_mid_norm, grad_ffn_gain, grad_ffn_bias = norm_back(mid_rows, ffn_gain, ffn_bias, grad_ffn)
    grad_mid = grad_out + grad_mid_norm
    grad_branch = grad_mid.astype(BF16)
    grad_att = transposed_right(grad_branch, out_full).astype(BF16)
    delta = lax.dot_general(
        merged * grad_att.astype(F32),
        expand,
        (((1,), (1,)), ((), ())),
        precision=HIGHEST,
        preferred_element_type=F32,
    )
    att_all = jnp.transpose(
        gather_order(grad_att, "frames").reshape(frame_size, items, row_total, width),
        (1, 0, 2, 3),
    ).reshape(items * lats, width)
    delta_all = jnp.transpose(
        gather_order(delta, "frames").reshape(frame_size, items, row_total, groups, GROUP),
        (3, 1, 4, 0, 2),
    ).reshape(groups, items, 1, GROUP * lats)
    back_stats = jnp.concatenate(
        [
            stats[:, :, 0:1],
            log_total[:, :, None],
            delta_all,
            jnp.zeros((groups, items, 5, GROUP * lats), F32),
        ],
        2,
    )

    grad_rows, grad_sums = attend_back(
        flags, rows, queries, att_all, back_stats, items, patches
    )
    kv_term = transposed_left(flat_norm, grad_rows).astype(BF16)
    kv_shard = lax.psum_scatter(kv_term, "items", scatter_dimension=0, tiled=True)

    grad_base = jnp.sum(grad_mid.reshape(items, row_total, width), axis=0)
    base_full = lax.dynamic_update_slice_in_dim(
        jnp.zeros((lats, width), F32), grad_base, row_base, 0
    )
    extra = jnp.concatenate(
        [
            grad_sums.reshape(3 * lats, width),
            base_full,
            grad_ffn_gain[None],
            grad_ffn_bias[None],
            jnp.zeros((6, width), F32),
        ],
        0,
    )
    extra_rows = extra.shape[0]

    def by_columns(x):
        split = jnp.transpose(x.reshape(-1, item_size, shard), (1, 0, 2))
        return xor_pick(split, item_index, item_size)

    extra_cols = sum_all(scatter_xor(by_columns(extra), "items", F32), "frames")
    low_cols = extra_cols[: 3 * lats].astype(BF16)

    def whole_columns(x):
        spread = xor_pick(gather_xor(x, "items"), item_index, item_size)
        return jnp.transpose(spread, (1, 0, 2)).reshape(x.shape[0], width)

    low_full = whole_columns(low_cols)
    query_low, lat_key_low, lat_value_low = (
        low_full[:lats],
        low_full[lats : 2 * lats],
        low_full[2 * lats :],
    )
    lat_cols_grad = (
        transposed_right(query_low, query_weight)
        + transposed_right(lat_key_low, key_weight)
        + transposed_right(lat_value_low, value_weight)
    )
    tail_full = whole_columns(jnp.concatenate([lat_cols_grad, extra_cols[3 * lats :]], 0))
    grad_lat_in, latent_gain_grad, latent_bias_grad = norm_back(
        latents, latent_gain, latent_bias, tail_full[:lats]
    )
    latents_grad = tail_full[lats : 2 * lats] + grad_lat_in
    ffn_gain_grad = tail_full[2 * lats]
    ffn_bias_grad = tail_full[2 * lats + 1]

    grad_norm = transposed_right(grad_rows, kv_full)
    grad_time_in, grad_media_gain, grad_media_bias = norm_back(
        with_time, media_gain, media_bias, grad_norm.reshape(items, patches, width)
    )
    media_grad = grad_time_in.astype(BF16)[:, None]
    grad_time = lax.dot_general(
        picker,
        jnp.sum(grad_time_in, axis=1),
        (((0,), (0,)), ((), ())),
        precision=HIGHEST,
        preferred_element_type=F32,
    )
    small = jnp.concatenate([grad_time, grad_media_gain[None], grad_media_bias[None]], 0)
    small = jnp.concatenate([small, jnp.zeros((-small.shape[0] % 8, width), F32)], 0)
    small_cols = sum_all(scatter_xor(by_columns(small), "items", F32), "frames")

    ffn_other = lax.all_gather(ffn_shift, "items", axis=0).reshape(-1, width)
    low_other = low_every[:, 1:].reshape(-1, width)
    upward_other = matmul(ffn_other, up_slice)
    hidden_other = gelu_exact(upward_other).astype(BF16)
    grad_up_other = jax.vjp(gelu_exact, upward_other)[1](
        transposed_right(low_other, down_weight)
    )[0].astype(BF16)
    down_grad = transposed_left(hidden, low_plane) + transposed_left(hidden_other, low_other)
    up_part = (
        transposed_left(ffn_plane, grad_up) + transposed_left(ffn_other, grad_up_other)
    ).astype(BF16)
    up_back = exchange_rows(up_part.reshape(item_size, shard, hidden_shard), "items")
    up_grad = (
        jnp.transpose(xor_pick(up_back, item_index, item_size), (1, 0, 2))
        .reshape(shard, item_size * hidden_shard)
        .astype(F32)
    )

    att_plane = exchange_rows(
        jnp.transpose(attended.reshape(own, item_size, shard), (1, 0, 2)), "items"
    ).reshape(-1, shard)
    branch_plane = gather_xor(grad_branch, "items").reshape(-1, width)
    out_grad = reduce_rows(transposed_left(att_plane, branch_plane).astype(BF16), "frames")

    kv_sum = reduce_rows(kv_shard, "frames")
    query_grad = transposed_left(lat_cols, query_low)
    key_grad = kv_sum[:, :width] + transposed_left(lat_cols, lat_key_low)
    value_grad = kv_sum[:, width:] + transposed_left(lat_cols, lat_value_low)
    return (
        result.reshape(items, row_total, width),
        entropy,
        media_grad,
        latents_grad,
        small_cols[:frame_total],
        small_cols[frame_total],
        small_cols[frame_total + 1],
        latent_gain_grad,
        latent_bias_grad,
        ffn_gain_grad,
        ffn_bias_grad,
        query_grad,
        key_grad,
        value_grad,
        out_grad,
        up_grad,
        down_grad,
    )


def solution(mesh):
    return jax.shard_map(
        body,
        mesh=mesh,
        in_specs=(
            P("items", "frames", None, None),
            P("items", "frames", None),
            P(),
            P(),
            P(),
            P(),
            P(),
            P(),
            P(),
            P(),
            P(),
            P(),
            P("items", None),
            P("items", None),
            P("items", None),
            P("items", None),
            P("items", None),
            P("items", None),
        ),
        out_specs=(
            P("items", "frames", None),
            P("items", "frames"),
            P("items", "frames", None, None),
            P(),
            P(None, "items"),
            P("items"),
            P("items"),
            P(),
            P(),
            P(),
            P(),
            P("items", None),
            P("items", None),
            P("items", None),
            P("items", None),
            P("items", None),
            P("items", None),
        ),
        check_vma=False,
    )
```

```python
import functools

import jax
import jax.numpy as jnp
from jax import lax
from jax.experimental import pallas as pl
from jax.experimental.pallas import tpu as pltpu
from jax.sharding import PartitionSpec as P

HEADS = 16
GROUP = 4
CHUNKS = 2
EPSILON = 1e-05
MASKED = -1e30
F32 = jnp.float32
BF16 = jnp.bfloat16
HIGHEST = lax.Precision.HIGHEST


def layer_norm(inputs, norm_gain, norm_bias):
    center = inputs - jnp.mean(inputs, axis=-1, keepdims=True)
    spread = jnp.mean(center * center, axis=-1, keepdims=True)
    return center * lax.rsqrt(spread + EPSILON) * norm_gain + norm_bias


def norm_back(inputs, norm_gain, norm_bias, gradient):
    unused, pullback = jax.vjp(layer_norm, inputs, norm_gain, norm_bias)
    return pullback(gradient)


def gelu_exact(inputs):
    return jax.nn.gelu(inputs, approximate=False)


def matmul(left_side, right_side):
    return jnp.dot(left_side, right_side, preferred_element_type=F32)


def transposed_left(left_side, right_side):
    return lax.dot_general(
        left_side, right_side, (((0,), (0,)), ((), ())), preferred_element_type=F32
    )


def transposed_right(left_side, right_side):
    return lax.dot_general(
        left_side, right_side, (((1,), (1,)), ((), ())), preferred_element_type=F32
    )


def even_distances(axis):
    return list(range(2, lax.axis_size(axis), 2))


def block_order(axis):
    size = lax.axis_size(axis)
    return list(range(0, size, 2)) + list(range(1, size, 2))


def swap(x, axis, distance):
    size = lax.axis_size(axis)
    return lax.ppermute(x, axis, [(i, i ^ distance) for i in range(size)])


def gather_blocks(x, axis):
    here = jnp.stack([x] + [swap(x, axis, d) for d in even_distances(axis)])
    return jnp.concatenate([here, swap(here, axis, 1)], 0)


def scatter_pair(keep, send, axis):
    return keep.astype(F32) + swap(send, axis, 1).astype(F32)


def scatter_chips(x, axis, wire):
    total = x[0]
    for k, d in enumerate(even_distances(axis)):
        total = total + swap(x[k + 1].astype(wire), axis, d).astype(F32)
    return total


def scatter_blocks(x, axis, wire):
    half = x.shape[0] // 2
    return scatter_chips(scatter_pair(x[:half], x[half:].astype(wire), axis), axis, wire)


def to_blocks(x, axis):
    me = lax.axis_index(axis)
    return jnp.stack([lax.dynamic_index_in_dim(x, me ^ d, 0, False) for d in block_order(axis)])


def from_blocks(x, axis):
    me = lax.axis_index(axis)
    half = x.shape[0] // 2

    def place(k):
        d = me ^ k
        return jnp.where(d % 2 == 0, 0, half) + d // 2

    return jnp.stack([lax.dynamic_index_in_dim(x, place(k), 0, False) for k in range(2 * half)])


def sum_butterfly(x, axis):
    distance = 1
    while distance < lax.axis_size(axis):
        x = x + swap(x, axis, distance)
        distance *= 2
    return x


def shift_from(x, axis, step):
    size = lax.axis_size(axis)
    return lax.ppermute(x, axis, [((i + step) % size, i) for i in range(size)])


def gather_shift(x, axis):
    size = lax.axis_size(axis)
    return jnp.stack([x] + [shift_from(x, axis, s) for s in range(1, size)])


def gather_order(x, axis):
    size = lax.axis_size(axis)
    spread = gather_shift(x, axis)
    return lax.dynamic_slice_in_dim(
        jnp.concatenate([spread, spread], 0), (size - lax.axis_index(axis)) % size, size, 0
    )


def gather_exchange(x, axis):
    size = lax.axis_size(axis)
    return lax.all_to_all(jnp.broadcast_to(x[None], (size,) + x.shape), axis, 0, 0)


def sum_all(x, axis):
    total = x
    for s in range(1, lax.axis_size(axis)):
        total = total + shift_from(x, axis, s)
    return total


def reduce_rows(x, axis):
    size = lax.axis_size(axis)
    me = lax.axis_index(axis)
    rows = x.shape[0] // size
    total = lax.dynamic_slice_in_dim(x, me * rows, rows, 0)
    for s in range(1, size):
        piece = lax.dynamic_slice_in_dim(x, ((me + s) % size) * rows, rows, 0).astype(BF16)
        piece = lax.ppermute(piece, axis, [(i, (i + s) % size) for i in range(size)])
        total = total + piece.astype(F32)
    return gather_order(total.astype(BF16), axis).reshape(x.shape).astype(F32)


def after(x, *others):
    return lax.optimization_barrier((x,) + others)[0]


def head_masks(rows, width, head_size):
    lane = lax.broadcasted_iota(jnp.int32, (rows, width), 1)
    return [
        jnp.logical_and(lane >= h * head_size, lane < (h + 1) * head_size)
        for h in range(width // head_size)
    ]


def spread_heads(block, masks):
    return jnp.concatenate([jnp.where(m, block, jnp.zeros_like(block)) for m in masks], 0)


def collect_heads(block, masks):
    rows = block.shape[0] // len(masks)
    total = jnp.where(masks[0], block[:rows], 0.0)
    for h in range(1, len(masks)):
        total = total + jnp.where(masks[h], block[h * rows : (h + 1) * rows], 0.0)
    return total


def forward_kernel(
    flag_ref, key_ref, value_ref, query_ref, out_ref, stat_ref, *, items, patches, scale, head_size
):
    lats, width = query_ref.shape
    masks = head_masks(lats, width, head_size)
    queries = spread_heads(query_ref[...].astype(F32), masks).astype(BF16)
    first = flag_ref[items] > 0
    base = items * patches
    lat_keys = key_ref[base : base + lats, :]
    lat_values = value_ref[base : base + lats, :]
    lat_scores = scale * transposed_right(lat_keys, queries)
    lat_max = jnp.max(lat_scores, axis=0, keepdims=True)
    for i in range(items):
        valid = flag_ref[i] > 0
        rows = slice(i * patches, (i + 1) * patches)
        scores = scale * transposed_right(key_ref[rows, :], queries)
        masked = jnp.where(valid, scores, MASKED)
        top = jnp.max(masked, axis=0, keepdims=True)
        top = jnp.where(first, jnp.maximum(top, lat_max), top)
        block_exp = jnp.where(valid, jnp.exp(masked - top), 0.0)
        lat_exp = jnp.where(first, jnp.exp(lat_scores - jnp.where(first, top, lat_max)), 0.0)
        total = jnp.sum(block_exp, axis=0, keepdims=True) + jnp.sum(lat_exp, axis=0, keepdims=True)
        moment = jnp.sum(block_exp * scores, axis=0, keepdims=True) + jnp.sum(
            lat_exp * lat_scores, axis=0, keepdims=True
        )
        part = transposed_left(block_exp.astype(BF16), value_ref[rows, :]) + transposed_left(
            lat_exp.astype(BF16), lat_values
        )
        out_ref[i * lats : (i + 1) * lats, :] = collect_heads(part, masks).astype(out_ref.dtype)
        stat_ref[0, i, 0:1, :] = top
        stat_ref[0, i, 1:2, :] = total
        stat_ref[0, i, 2:3, :] = moment
        stat_ref[0, i, 3:8, :] = jnp.zeros((5, stat_ref.shape[3]), F32)


def backward_kernel(
    flag_ref,
    key_ref,
    value_ref,
    query_ref,
    grad_ref,
    stat_ref,
    both_ref,
    sums_ref,
    held_ref,
    *,
    items,
    patches,
    scale,
    head_size,
):
    lats, width = query_ref.shape

    @pl.when(pl.program_id(1) == 1)
    def _():
        both_ref[...] = held_ref[...]

    @pl.when(pl.program_id(1) == 0)
    def _():
        masks = head_masks(lats, width, head_size)
        queries = spread_heads(query_ref[...].astype(F32), masks).astype(BF16)
        first = flag_ref[items] > 0
        base = items * patches
        lat_keys = key_ref[base : base + lats, :]
        lat_values = value_ref[base : base + lats, :]
        lat_scores = scale * transposed_right(lat_keys, queries)
        grad_query = jnp.zeros((queries.shape[0], width), F32)
        lat_grad_key = jnp.zeros((lats, width), F32)
        lat_grad_value = jnp.zeros((lats, width), F32)
        for i in range(items):
            valid = flag_ref[i] > 0
            rows = slice(i * patches, (i + 1) * patches)
            top = stat_ref[0, i, 0:1, :]
            log_total = stat_ref[0, i, 1:2, :]
            delta = stat_ref[0, i, 2:3, :]
            rescale = jnp.exp(top - log_total)
            keys = key_ref[rows, :]
            values = value_ref[rows, :]
            grads = spread_heads(
                grad_ref[i * lats : (i + 1) * lats, :].astype(F32), masks
            ).astype(BF16)
            masked = jnp.where(valid, scale * transposed_right(keys, queries), MASKED)
            probs = jnp.where(valid, jnp.exp(masked - log_total), 0.0)
            block_exp = jnp.where(valid, jnp.exp(masked - top), 0.0)
            weights = (block_exp.astype(BF16).astype(F32) * rescale).astype(BF16)
            grad_probs = transposed_right(values, grads)
            grad_scores = (probs * (grad_probs - delta)).astype(BF16)
            both_ref[rows, :] = (scale * matmul(grad_scores, queries)).astype(BF16)
            held_ref[rows, :] = matmul(weights, grads).astype(BF16)
            grad_query = grad_query + transposed_left(grad_scores, keys)

            lat_probs = jnp.where(first, jnp.exp(lat_scores - log_total), 0.0)
            lat_exp = jnp.where(first, jnp.exp(lat_scores - top), 0.0)
            lat_weights = (lat_exp.astype(BF16).astype(F32) * rescale).astype(BF16)
            lat_grad_probs = transposed_right(lat_values, grads)
            lat_grad_scores = (lat_probs * (lat_grad_probs - delta)).astype(BF16)
            lat_grad_key = lat_grad_key + matmul(lat_grad_scores, queries)
            lat_grad_value = lat_grad_value + matmul(lat_weights, grads)
            grad_query = grad_query + transposed_left(lat_grad_scores, lat_keys)
        sums_ref[0] = scale * collect_heads(grad_query, masks)
        sums_ref[1] = scale * lat_grad_key
        sums_ref[2] = lat_grad_value


def attend(flags, rows, queries, items, patches, head_size):
    lats, model_width = queries.shape
    width = GROUP * head_size
    groups = model_width // width
    tokens = rows.shape[0]
    stack = GROUP * lats
    work = items * groups * stack * width * (patches + lats) * 4
    return pl.pallas_call(
        functools.partial(
            forward_kernel,
            items=items,
            patches=patches,
            scale=head_size**-0.5,
            head_size=head_size,
        ),
        grid=(groups,),
        in_specs=[
            pl.BlockSpec(memory_space=pltpu.SMEM),
            pl.BlockSpec((tokens, width), lambda g: (0, g)),
            pl.BlockSpec((tokens, width), lambda g: (0, g + groups)),
            pl.BlockSpec((lats, width), lambda g: (0, g)),
        ],
        out_specs=[
            pl.BlockSpec((items * lats, width), lambda g: (0, g)),
            pl.BlockSpec((1, items, 8, stack), lambda g: (g, 0, 0, 0)),
        ],
        out_shape=[
            jax.ShapeDtypeStruct((items * lats, model_width), BF16),
            jax.ShapeDtypeStruct((groups, items, 8, stack), F32),
        ],
        cost_estimate=pl.CostEstimate(
            flops=work, bytes_accessed=rows.size * 2 + items * lats * model_width * 2,
            transcendentals=items * groups * stack * patches,
        ),
        compiler_params=pltpu.CompilerParams(vmem_limit_bytes=40 * 2**20),
    )(flags, rows, rows, queries)


def attend_back(flags, rows, queries, grads, stats, items, patches, head_size):
    lats, model_width = queries.shape
    width = GROUP * head_size
    groups = model_width // width
    tokens = rows.shape[0]
    stack = GROUP * lats
    work = items * groups * stack * width * (patches + lats) * 10
    return pl.pallas_call(
        functools.partial(
            backward_kernel,
            items=items,
            patches=patches,
            scale=head_size**-0.5,
            head_size=head_size,
        ),
        grid=(groups, 2),
        in_specs=[
            pl.BlockSpec(memory_space=pltpu.SMEM),
            pl.BlockSpec((tokens, width), lambda g, s: (0, g)),
            pl.BlockSpec((tokens, width), lambda g, s: (0, g + groups)),
            pl.BlockSpec((lats, width), lambda g, s: (0, g)),
            pl.BlockSpec((items * lats, width), lambda g, s: (0, g)),
            pl.BlockSpec((1, items, 8, stack), lambda g, s: (g, 0, 0, 0)),
        ],
        out_specs=[
            pl.BlockSpec((items * patches, width), lambda g, s: (0, g + s * groups)),
            pl.BlockSpec((3, lats, width), lambda g, s: (0, 0, g)),
        ],
        out_shape=[
            jax.ShapeDtypeStruct((items * patches, 2 * model_width), BF16),
            jax.ShapeDtypeStruct((3, lats, model_width), F32),
        ],
        scratch_shapes=[pltpu.VMEM((items * patches, width), BF16)],
        cost_estimate=pl.CostEstimate(
            flops=work, bytes_accessed=rows.size * 4,
            transcendentals=2 * items * groups * stack * patches,
        ),
        compiler_params=pltpu.CompilerParams(vmem_limit_bytes=40 * 2**20),
    )(flags, rows, rows, queries, grads, stats)


def body(
    media,
    cotangent,
    frame_count,
    frame_start,
    latents,
    time_embed,
    media_gain,
    media_bias,
    latent_gain,
    latent_bias,
    ffn_gain,
    ffn_bias,
    query_weight,
    key_weight,
    value_weight,
    out_weight,
    up_weight,
    down_weight,
):
    items = media.shape[0]
    patches = media.shape[2]
    width = media.shape[3]
    lats = latents.shape[0]
    frame_total = time_embed.shape[0]
    row_total = cotangent.shape[1]
    own = items * row_total
    head_size = width // HEADS
    half = width // CHUNKS
    chunk_heads = HEADS // CHUNKS
    groups = chunk_heads // GROUP
    tokens = items * patches
    shard = query_weight.shape[0]
    hidden_shard = down_weight.shape[0]
    item_size = lax.axis_size("items")
    frame_size = lax.axis_size("frames")
    item_index = lax.axis_index("items")
    slot = lax.axis_index("frames")
    row_base = slot * row_total
    chunk_slices = [slice(c * half, (c + 1) * half) for c in range(CHUNKS)]

    kv_full = lax.all_gather(
        jnp.concatenate([w[:, c] for c in chunk_slices for w in (key_weight, value_weight)], 1),
        "items",
        axis=0,
        tiled=True,
    )
    out_full = lax.all_gather(after(out_weight, kv_full), "items", axis=0, tiled=True)
    up_slice = lax.all_to_all(after(up_weight, kv_full), "items", 1, 0, tiled=True)
    grad_out = cotangent.reshape(own, width)
    grad_low = grad_out.astype(BF16)
    low_every = lax.all_gather(after(grad_low, out_full), "items", axis=0)
    low_plane = to_blocks(low_every, "items").reshape(-1, width)
    low_other = lax.all_gather(
        after(gather_shift(grad_low, "frames")[1:], low_every), "items", axis=0
    ).reshape(-1, width)

    lat_norm = layer_norm(latents, latent_gain, latent_bias).astype(BF16)
    lat_cols = lax.dynamic_slice_in_dim(lat_norm, item_index * shard, shard, 1)
    queries = sum_butterfly(matmul(lat_cols, query_weight), "items").astype(BF16)
    counts = lax.dynamic_slice_in_dim(frame_count, item_index * items, items)
    starts = lax.dynamic_slice_in_dim(frame_start, item_index * items, items)
    offset = (slot - starts) % frame_total
    flags = jnp.concatenate(
        [(offset < counts).astype(jnp.int32), (slot == 0).astype(jnp.int32)[None]]
    )
    picker = (offset[:, None] == jnp.arange(frame_total, dtype=jnp.int32)[None, :]).astype(F32)
    time_rows = jnp.dot(picker, time_embed, precision=HIGHEST, preferred_element_type=F32)
    with_time = media[:, 0].astype(F32) + time_rows[:, None, :]
    normed = layer_norm(with_time, media_gain, media_bias).astype(BF16)
    flat_norm = normed.reshape(tokens, width)
    all_rows = jnp.concatenate([flat_norm, lat_norm], 0)
    norm_blocks = jnp.concatenate(
        [
            lax.dynamic_slice_in_dim(flat_norm, (item_index ^ d) * shard, shard, 1)
            for d in block_order("items")
        ],
        1,
    )
    norm_keep, norm_send = norm_blocks[:, : width // 2], norm_blocks[:, width // 2 :]

    head_of = jnp.arange(half, dtype=jnp.int32) // head_size
    expand = (jnp.arange(chunk_heads, dtype=jnp.int32)[:, None] == head_of[None, :]).astype(F32)
    rows, kept_stats, merged, spread = [], [], [], []
    for c, columns in enumerate(chunk_slices):
        chunk_rows = matmul(all_rows, kv_full[:, 2 * c * half : 2 * (c + 1) * half]).astype(BF16)
        part_out, stats = attend(
            flags, chunk_rows, queries[:, columns], items, patches, head_size
        )
        pieces = jnp.transpose(
            part_out.reshape(items, frame_size, row_total, half), (1, 0, 2, 3)
        ).reshape(frame_size, own, half)
        part_every = lax.all_to_all(pieces, "frames", 0, 0)
        stat_every = gather_order(stats, "frames")
        top_every, total_every, moment_every = (
            stat_every[:, :, :, 0],
            stat_every[:, :, :, 1],
            stat_every[:, :, :, 2],
        )
        peak = jnp.max(top_every, axis=0)
        factor = jnp.exp(top_every - peak[None])
        whole = jnp.sum(factor * total_every, axis=0)
        log_total = peak + jnp.log(whole)
        mean_score = jnp.sum(factor * moment_every, axis=0) / whole
        spread.append(
            jnp.sum((log_total - mean_score).reshape(groups, items, GROUP, lats), axis=(0, 2))
        )
        share = (factor / whole[None]).reshape(frame_size, groups, items, GROUP, lats)
        share = lax.dynamic_slice_in_dim(share, row_base, row_total, 4)
        share = jnp.transpose(share, (0, 2, 4, 1, 3)).reshape(frame_size * own, chunk_heads)
        share_wide = jnp.dot(share, expand, precision=HIGHEST, preferred_element_type=F32)
        merged.append(
            jnp.sum(part_every.astype(F32) * share_wide.reshape(frame_size, own, half), axis=0)
        )
        rows.append(chunk_rows)
        kept_stats.append((stats[:, :, 0:1], log_total[:, :, None]))
    entropy = lax.dynamic_slice_in_dim(sum(spread) * (1.0 / HEADS), row_base, row_total, 1)
    attended = jnp.concatenate([m.astype(BF16) for m in merged], 1)

    base_rows = lax.dynamic_slice_in_dim(latents, row_base, row_total, 0)
    mid_rows = (
        base_rows[None] + matmul(attended, out_full).reshape(items, row_total, width)
    ).reshape(own, width)
    ffn_in = layer_norm(mid_rows, ffn_gain, ffn_bias).astype(BF16)
    ffn_plane = gather_blocks(ffn_in, "items").reshape(-1, width)
    ffn_shift = gather_shift(ffn_in, "frames")[1:]

    upward = matmul(ffn_plane, up_slice)
    hidden = gelu_exact(upward).astype(BF16)
    grad_hidden = transposed_right(low_plane, down_weight)
    grad_up = jax.vjp(gelu_exact, upward)[1](grad_hidden)[0].astype(BF16)
    grad_ffn = scatter_blocks(
        transposed_right(grad_up, up_slice).reshape(item_size, own, width), "items", BF16
    )

    grad_mid_norm, grad_ffn_gain, grad_ffn_bias = norm_back(mid_rows, ffn_gain, ffn_bias, grad_ffn)
    grad_mid = grad_out + grad_mid_norm
    grad_branch = grad_mid.astype(BF16)
    grad_att = transposed_right(grad_branch, out_full).astype(BF16)
    att_every = gather_exchange(grad_att, "frames").reshape(frame_size, items, row_total, width)
    att_all = jnp.transpose(att_every, (1, 0, 2, 3)).reshape(items * lats, width)
    delta = jnp.concatenate(
        [
            lax.dot_general(
                merged[c] * grad_att[:, columns].astype(F32),
                expand,
                (((1,), (1,)), ((), ())),
                precision=HIGHEST,
                preferred_element_type=F32,
            )
            for c, columns in enumerate(chunk_slices)
        ],
        1,
    )
    delta_all = jnp.transpose(
        gather_order(delta, "frames").reshape(
            frame_size, items, row_total, CHUNKS * groups, GROUP
        ),
        (3, 1, 4, 0, 2),
    ).reshape(CHUNKS, groups, items, 1, GROUP * lats)

    grad_rows, grad_sums, kv_chunks = [], [], []
    for c, columns in enumerate(chunk_slices):
        top, log_total = kept_stats[c]
        back_stats = jnp.concatenate(
            [
                top,
                log_total,
                delta_all[c],
                jnp.zeros((groups, items, 5, GROUP * lats), F32),
            ],
            2,
        )
        chunk_grad, chunk_sums = attend_back(
            flags,
            rows[c],
            queries[:, columns],
            att_all[:, columns],
            back_stats,
            items,
            patches,
            head_size,
        )
        send = transposed_left(norm_send, chunk_grad).astype(BF16)
        pair = scatter_pair(transposed_left(norm_keep, chunk_grad), send, "items")
        kv_chunks.append(
            scatter_chips(pair.reshape(item_size // 2, shard, 2 * half), "items", BF16)
        )
        grad_rows.append(chunk_grad)
        grad_sums.append(chunk_sums.reshape(3 * lats, half))

    result = mid_rows + scatter_blocks(
        matmul(hidden, down_weight).reshape(item_size, own, width), "items", BF16
    )

    grad_base = jnp.sum(grad_mid.reshape(items, row_total, width), axis=0)
    base_full = lax.dynamic_update_slice_in_dim(
        jnp.zeros((lats, width), F32), grad_base, row_base, 0
    )
    extra = jnp.concatenate(
        [
            jnp.concatenate(grad_sums, 1),
            base_full,
            grad_ffn_gain[None],
            grad_ffn_bias[None],
            jnp.zeros((6, width), F32),
        ],
        0,
    )

    def column_blocks(x):
        return to_blocks(jnp.transpose(x.reshape(-1, item_size, shard), (1, 0, 2)), "items")

    def whole_columns(x):
        blocks = from_blocks(gather_blocks(x, "items"), "items")
        return jnp.transpose(blocks, (1, 0, 2)).reshape(x.shape[0], width)

    extra_cols = sum_all(scatter_blocks(column_blocks(extra), "items", F32), "frames")
    low_full = whole_columns(extra_cols[: 3 * lats].astype(BF16))
    query_low, lat_key_low, lat_value_low = (
        low_full[:lats],
        low_full[lats : 2 * lats],
        low_full[2 * lats :],
    )
    lat_cols_grad = (
        transposed_right(query_low, query_weight)
        + transposed_right(lat_key_low, key_weight)
        + transposed_right(lat_value_low, value_weight)
    )
    tail_full = whole_columns(jnp.concatenate([lat_cols_grad, extra_cols[3 * lats :]], 0))
    grad_lat_in, latent_gain_grad, latent_bias_grad = norm_back(
        latents, latent_gain, latent_bias, tail_full[:lats]
    )
    latents_grad = tail_full[lats : 2 * lats] + grad_lat_in
    ffn_gain_grad = tail_full[2 * lats]
    ffn_bias_grad = tail_full[2 * lats + 1]

    grad_norm = transposed_right(jnp.concatenate(grad_rows, 1), kv_full)
    grad_time_in, grad_media_gain, grad_media_bias = norm_back(
        with_time, media_gain, media_bias, grad_norm.reshape(items, patches, width)
    )
    media_grad = grad_time_in.astype(BF16)[:, None]
    grad_time = lax.dot_general(
        picker,
        jnp.sum(grad_time_in, axis=1),
        (((0,), (0,)), ((), ())),
        precision=HIGHEST,
        preferred_element_type=F32,
    )
    small = jnp.concatenate([grad_time, grad_media_gain[None], grad_media_bias[None]], 0)
    small = jnp.concatenate([small, jnp.zeros((-small.shape[0] % 8, width), F32)], 0)
    small_cols = lax.dynamic_slice_in_dim(
        sum_all(sum_butterfly(small, "items"), "frames"), item_index * shard, shard, 1
    )

    ffn_other = lax.all_gather(after(ffn_shift, low_other), "items", axis=0)
    branch_plane = lax.all_gather(
        after(grad_branch, ffn_other), "items", axis=0, tiled=True
    )
    ffn_other = ffn_other.reshape(-1, width)
    upward_other = matmul(ffn_other, up_slice)
    hidden_other = gelu_exact(upward_other).astype(BF16)
    grad_up_other = jax.vjp(gelu_exact, upward_other)[1](
        transposed_right(low_other, down_weight)
    )[0].astype(BF16)
    down_grad = transposed_left(hidden, low_plane) + transposed_left(hidden_other, low_other)
    up_part = (
        transposed_left(ffn_plane, grad_up) + transposed_left(ffn_other, grad_up_other)
    ).astype(BF16)
    up_grad = lax.all_to_all(up_part, "items", 0, 1, tiled=True).astype(F32)

    att_plane = lax.all_to_all(attended, "items", 1, 0, tiled=True)
    out_part = transposed_left(att_plane, branch_plane)

    lat_pair = [
        jnp.concatenate([lat_key_low[:, c], lat_value_low[:, c]], 1) for c in chunk_slices
    ]
    first = reduce_rows(jnp.concatenate([kv_chunks[0], out_part], 1), "frames")
    sums = [first[:, : 2 * half]] + [reduce_rows(k, "frames") for k in kv_chunks[1:]]
    out_grad = first[:, 2 * half :]
    sums = [total + transposed_left(lat_cols, low) for total, low in zip(sums, lat_pair)]
    key_grad = jnp.concatenate([total[:, :half] for total in sums], 1)
    value_grad = jnp.concatenate([total[:, half:] for total in sums], 1)
    query_grad = transposed_left(lat_cols, query_low)
    return (
        result.reshape(items, row_total, width),
        entropy,
        media_grad,
        latents_grad,
        small_cols[:frame_total],
        small_cols[frame_total],
        small_cols[frame_total + 1],
        latent_gain_grad,
        latent_bias_grad,
        ffn_gain_grad,
        ffn_bias_grad,
        query_grad,
        key_grad,
        value_grad,
        out_grad,
        up_grad,
        down_grad,
    )


def solution(mesh):
    return jax.shard_map(
        body,
        mesh=mesh,
        in_specs=(
            P("items", "frames", None, None),
            P("items", "frames", None),
            P(),
            P(),
            P(),
            P(),
            P(),
            P(),
            P(),
            P(),
            P(),
            P(),
            P("items", None),
            P("items", None),
            P("items", None),
            P("items", None),
            P("items", None),
            P("items", None),
        ),
        out_specs=(
            P("items", "frames", None),
            P("items", "frames"),
            P("items", "frames", None, None),
            P(),
            P(None, "items"),
            P("items"),
            P("items"),
            P(),
            P(),
            P(),
            P(),
            P("items", None),
            P("items", None),
            P("items", None),
            P("items", None),
            P("items", None),
            P("items", None),
        ),
        check_vma=False,
    )
```

```python
import functools

import jax
import jax.numpy as jnp
from jax import lax
from jax.experimental import pallas as pl
from jax.experimental.pallas import tpu as pltpu
from jax.sharding import PartitionSpec as P

HEADS = 16
GROUP = 4
CHUNKS = 2
LANES = 128
EPSILON = 1e-05
MASKED = -1e30
F32 = jnp.float32
BF16 = jnp.bfloat16
HIGHEST = lax.Precision.HIGHEST


def layer_norm(inputs, norm_gain, norm_bias):
    center = inputs - jnp.mean(inputs, axis=-1, keepdims=True)
    spread = jnp.mean(center * center, axis=-1, keepdims=True)
    return center * lax.rsqrt(spread + EPSILON) * norm_gain + norm_bias


def norm_back(inputs, norm_gain, norm_bias, gradient):
    unused, pullback = jax.vjp(layer_norm, inputs, norm_gain, norm_bias)
    return pullback(gradient)


def matmul(left_side, right_side):
    return jnp.dot(left_side, right_side, preferred_element_type=F32)


def transposed_left(left_side, right_side):
    return lax.dot_general(
        left_side, right_side, (((0,), (0,)), ((), ())), preferred_element_type=F32
    )


def transposed_right(left_side, right_side):
    return lax.dot_general(
        left_side, right_side, (((1,), (1,)), ((), ())), preferred_element_type=F32
    )


def gather_exchange(x, axis):
    size = lax.axis_size(axis)
    return lax.all_to_all(jnp.broadcast_to(x[None], (size,) + x.shape), axis, 0, 0)


def scatter_exchange(pieces, axis):
    return jnp.sum(lax.all_to_all(pieces, axis, 0, 0).astype(F32), axis=0)


def core_groups(axis):
    size = lax.axis_size(axis)
    return [list(range(core, size, 2)) for core in range(2)]


def swap_cores(x, axis):
    return lax.ppermute(x, axis, [(i, i ^ 1) for i in range(lax.axis_size(axis))])


def shift_from(x, axis, step):
    size = lax.axis_size(axis)
    return lax.ppermute(x, axis, [((i + step) % size, i) for i in range(size)])


def others(x, axis):
    return jnp.stack([shift_from(x, axis, s) for s in range(1, lax.axis_size(axis))])


def reduce_rows(x, axis):
    size = lax.axis_size(axis)
    pieces = x.astype(BF16).reshape((size, x.shape[0] // size) + x.shape[1:])
    total = scatter_exchange(pieces, axis).astype(BF16)
    return gather_exchange(total, axis).reshape(x.shape).astype(F32)


def after(x, *earlier):
    return lax.optimization_barrier((x,) + earlier)[0]


def split_terms(x):
    high = x.astype(BF16)
    rest = x - high.astype(F32)
    middle = rest.astype(BF16)
    return high, middle, (rest - middle.astype(F32)).astype(BF16)


def iota(shape, dim):
    return lax.broadcasted_iota(jnp.int32, shape, dim)


def head_masks(rows, width, head_size):
    lane = iota((rows, width), 1)
    return [
        jnp.logical_and(lane >= h * head_size, lane < (h + 1) * head_size)
        for h in range(width // head_size)
    ]


def spread_heads(block, masks):
    return jnp.concatenate([jnp.where(m, block, jnp.zeros_like(block)) for m in masks], 0)


def collect_heads(block, masks):
    rows = block.shape[0] // len(masks)
    total = jnp.where(masks[0], block[:rows], 0.0)
    for h in range(1, len(masks)):
        total = total + jnp.where(masks[h], block[h * rows : (h + 1) * rows], 0.0)
    return total


def head_expand(width, head_size):
    row, column = iota((LANES, width), 0), iota((LANES, width), 1)
    return jnp.logical_and(column >= row * head_size, column < (row + 1) * head_size).astype(F32)


def forward_kernel(
    flag_ref,
    row_ref,
    key_weight_ref,
    value_weight_ref,
    query_ref,
    key_ref,
    value_ref,
    message_ref,
    top_ref,
    *,
    items,
    patches,
    scale,
    head_size,
    heads,
):
    lats, width = query_ref.shape
    frames, own = message_ref.shape[:2]
    row_total = own // items
    masks = head_masks(lats, width, head_size)
    queries = spread_heads(query_ref[...].astype(F32), masks).astype(BF16)
    key_ref[...] = matmul(row_ref[...], key_weight_ref[...]).astype(BF16)
    value_ref[...] = matmul(row_ref[...], value_weight_ref[...]).astype(BF16)
    first = flag_ref[items] > 0
    base = items * patches
    lat_keys = key_ref[base : base + lats, :]
    lat_values = value_ref[base : base + lats, :]
    lat_scores = scale * transposed_right(lat_keys, queries)
    lat_max = jnp.max(lat_scores, axis=0, keepdims=True)
    group = pl.program_id(0)
    term, lane = iota((16, GROUP * LANES), 0), iota((16, GROUP * LANES), 1)
    place = jnp.logical_and(
        lane % LANES == term * heads + group * GROUP + lane // LANES, term < 9
    ).astype(BF16)
    outs, marks = [], []
    for i in range(items):
        valid = flag_ref[i] > 0
        rows = slice(i * patches, (i + 1) * patches)
        scores = scale * transposed_right(key_ref[rows, :], queries)
        masked = jnp.where(valid, scores, MASKED)
        top = jnp.max(masked, axis=0, keepdims=True)
        top = jnp.where(first, jnp.maximum(top, lat_max), top)
        block_exp = jnp.where(valid, jnp.exp(masked - top), 0.0)
        lat_exp = jnp.where(first, jnp.exp(lat_scores - jnp.where(first, top, lat_max)), 0.0)
        total = jnp.sum(block_exp, axis=0, keepdims=True) + jnp.sum(lat_exp, axis=0, keepdims=True)
        moment = jnp.sum(block_exp * scores, axis=0, keepdims=True) + jnp.sum(
            lat_exp * lat_scores, axis=0, keepdims=True
        )
        part = transposed_left(block_exp.astype(BF16), value_ref[rows, :]) + transposed_left(
            lat_exp.astype(BF16), lat_values
        )
        outs.append(collect_heads(part, masks))
        top_ref[0, i] = jnp.broadcast_to(top, top_ref.shape[2:])
        terms = jnp.concatenate(
            [t.astype(F32) for x in (top, total, moment) for t in split_terms(x)]
            + [jnp.zeros((7, top.shape[1]), F32)],
            0,
        ).astype(BF16)
        wide = transposed_left(terms, place)
        mark = wide[:lats, :LANES]
        for h in range(1, GROUP):
            mark = mark + wide[h * lats : (h + 1) * lats, h * LANES : (h + 1) * LANES]
        marks.append(mark)

    end = message_ref.shape[2] - LANES
    for f in range(frames):
        q = slice(f * row_total, (f + 1) * row_total)
        block = jnp.concatenate([x[q] for x in outs], 0).astype(BF16)
        mark = jnp.concatenate([x[q] for x in marks], 0).astype(BF16)
        for g in range(end // width):

            @pl.when(group == g)
            def _():
                message_ref[f, :, g * width : (g + 1) * width] = block
                if g == 0:
                    message_ref[f, :, end:] = mark
                else:
                    message_ref[f, :, end:] = message_ref[f, :, end:] + mark


def merge_kernel(
    *refs,
    chunks,
    items,
    head_size,
    heads,
):
    message_refs = refs[:chunks]
    base_ref, weight_ref, gain_ref, bias_ref = refs[chunks : chunks + 4]
    merged_ref, attended_ref, mid_ref, ffn_ref, log_ref, entropy_ref = refs[chunks + 4 :]
    frames, own, columns = message_refs[0].shape
    half = columns - LANES
    lane, column = iota((LANES, 3 * LANES), 0), iota((LANES, 3 * LANES), 1)
    gather = jnp.logical_and(
        jnp.logical_and(lane // heads // 3 == column // LANES, lane % heads == column % LANES),
        lane < 9 * heads,
    ).astype(BF16)
    expand = head_expand(half, head_size)
    live = iota((own, LANES), 1) < heads
    spread = jnp.zeros((own, LANES), F32)
    for c, message_ref in enumerate(message_refs):
        stats = [matmul(message_ref[s, :, half:], gather) for s in range(frames)]
        tops = [x[:, :LANES] for x in stats]
        peak = functools.reduce(jnp.maximum, tops)
        factors = [jnp.exp(t - peak) for t in tops]
        whole = sum(f * x[:, LANES : 2 * LANES] for f, x in zip(factors, stats))
        moment = sum(f * x[:, 2 * LANES :] for f, x in zip(factors, stats))
        whole = jnp.where(live, whole, 1.0)
        log_total = jnp.where(live, peak + jnp.log(whole), 0.0)
        log_ref[c] = log_total
        spread = spread + jnp.where(live, log_total - moment / whole, 0.0)
        merged = jnp.zeros((own, half), F32)
        for s in range(frames):
            share = jnp.where(live, factors[s] / whole, 0.0)
            wide = jnp.dot(share, expand, precision=HIGHEST, preferred_element_type=F32)
            merged = merged + message_ref[s, :, :half].astype(F32) * wide
        merged_ref[:, c * half : (c + 1) * half] = merged
        attended_ref[:, c * half : (c + 1) * half] = merged.astype(BF16)
    entropy_ref[...] = jnp.broadcast_to(
        jnp.sum(spread, axis=1, keepdims=True) * (1.0 / HEADS), entropy_ref.shape
    )
    base = jnp.concatenate([base_ref[...]] * items, 0)
    mid = base + matmul(attended_ref[...], weight_ref[...])
    mid_ref[...] = mid
    normed = layer_norm(mid, gain_ref[...], bias_ref[...]).astype(BF16)
    for d in range(ffn_ref.shape[0]):
        ffn_ref[d] = normed


def gelu_parts(x):
    share = 0.5 * (1.0 + lax.erf(x * (0.5**0.5)))
    slope = share + x * jnp.exp(-0.5 * x * x) * ((2.0 * jnp.pi) ** -0.5)
    return x * share, slope


def feed_kernel(row_ref, low_ref, up_ref, down_ref, grad_ref, result_ref):
    upward = matmul(row_ref[...], up_ref[...])
    hidden, slope = gelu_parts(upward)
    grad_up = (slope * transposed_right(low_ref[...], down_ref[...])).astype(BF16)
    grad_ref[...] = transposed_right(grad_up, up_ref[...]).astype(BF16)
    result_ref[...] = matmul(hidden.astype(BF16), down_ref[...]).astype(BF16)


def feed_grad_kernel(
    plane_ref, plane_low_ref, other_ref, other_low_ref, up_ref, down_ref, down_grad_ref, up_grad_ref,
    total_ref, *, plane_blocks,
):
    step = pl.program_id(0)
    near = step < plane_blocks
    rows = jnp.where(near, plane_ref[...], other_ref[...])
    low = jnp.where(near, plane_low_ref[...], other_low_ref[...])
    hidden, slope = gelu_parts(matmul(rows, up_ref[...]))
    grad_up = (slope * transposed_right(low, down_ref[...])).astype(BF16)
    down_part = transposed_left(hidden.astype(BF16), low)
    up_part = transposed_left(rows, grad_up)

    @pl.when(step == 0)
    def _():
        down_grad_ref[...] = down_part
        total_ref[...] = up_part

    @pl.when(step > 0)
    def _():
        down_grad_ref[...] += down_part
        total_ref[...] += up_part

    @pl.when(step == pl.num_programs(0) - 1)
    def _():
        up_grad_ref[...] = total_ref[...].astype(BF16)


def turn_kernel(
    part_ref,
    mid_ref,
    cotangent_ref,
    gain_ref,
    merged_ref,
    log_ref,
    weight_ref,
    message_ref,
    branch_ref,
    base_ref,
    sums_ref,
    *,
    items,
    chunks,
    head_size,
    heads,
):
    own, width = mid_ref.shape
    half = width // chunks
    gradient = functools.reduce(
        jnp.add, [part_ref[d].astype(F32) for d in range(part_ref.shape[0])]
    )
    mid = mid_ref[...]
    center = mid - jnp.mean(mid, axis=1, keepdims=True)
    rate = lax.rsqrt(jnp.mean(center * center, axis=1, keepdims=True) + EPSILON)
    unit = center * rate
    scaled = gradient * gain_ref[...]
    inner = scaled - jnp.mean(scaled, axis=1, keepdims=True)
    grad_mid = cotangent_ref[...] + rate * (
        inner - unit * jnp.mean(scaled * unit, axis=1, keepdims=True)
    )
    sums_ref[...] = jnp.zeros(sums_ref.shape, F32)
    sums_ref[0:1, :] = jnp.sum(gradient * unit, axis=0, keepdims=True)
    sums_ref[1:2, :] = jnp.sum(gradient, axis=0, keepdims=True)
    row_total = own // items
    base_ref[...] = functools.reduce(
        jnp.add, [grad_mid[i * row_total : (i + 1) * row_total] for i in range(items)]
    )
    branch = grad_mid.astype(BF16)
    branch_ref[...] = branch
    grad_att = transposed_right(branch, weight_ref[...]).astype(BF16)
    expand = head_expand(half, head_size)
    lane, column = iota((6 * LANES, LANES), 0), iota((6 * LANES, LANES), 1)
    place = jnp.logical_and(
        lane % LANES < heads, column == (lane // LANES) * heads + lane % LANES
    ).astype(BF16)
    marks = []
    for c in range(chunks):
        columns = slice(c * half, (c + 1) * half)
        delta = lax.dot_general(
            merged_ref[:, columns] * grad_att[:, columns].astype(F32),
            expand,
            (((1,), (1,)), ((), ())),
            precision=HIGHEST,
            preferred_element_type=F32,
        )
        terms = jnp.concatenate(
            [t for x in (log_ref[c], delta) for t in split_terms(x)], 1
        )
        marks.append(matmul(terms, place).astype(BF16))
    for f in range(message_ref.shape[0]):
        message_ref[f, :, :width] = grad_att
        for c in range(chunks):
            message_ref[f, :, width + c * LANES : width + (c + 1) * LANES] = marks[c]


def backward_kernel(
    flag_ref,
    key_ref,
    value_ref,
    query_ref,
    grad_ref,
    mark_ref,
    top_ref,
    both_ref,
    sums_ref,
    held_ref,
    *,
    items,
    patches,
    scale,
    head_size,
    heads,
):
    lats, width = query_ref.shape
    frames, own = grad_ref.shape[:2]
    row_total = own // items

    @pl.when(pl.program_id(1) == 1)
    def _():
        both_ref[...] = held_ref[...]

    @pl.when(pl.program_id(1) == 0)
    def _():
        masks = head_masks(lats, width, head_size)
        queries = spread_heads(query_ref[...].astype(F32), masks).astype(BF16)
        first = flag_ref[items] > 0
        base = items * patches
        lat_keys = key_ref[base : base + lats, :]
        lat_values = value_ref[base : base + lats, :]
        lat_scores = scale * transposed_right(lat_keys, queries)
        row, lane = iota((GROUP * 8, LANES), 0), iota((GROUP * 8, LANES), 1)
        pick = jnp.logical_and(
            jnp.logical_and(
                lane // heads // 3 == row % 8,
                lane % heads == pl.program_id(0) * GROUP + row // 8,
            ),
            lane < 6 * heads,
        ).astype(BF16)
        received = [grad_ref[f].astype(F32) for f in range(frames)]
        marks = [mark_ref[f].astype(F32) for f in range(frames)]
        grad_query = jnp.zeros((queries.shape[0], width), F32)
        lat_grad_key = jnp.zeros((lats, width), F32)
        lat_grad_value = jnp.zeros((lats, width), F32)
        for i in range(items):
            valid = flag_ref[i] > 0
            rows = slice(i * patches, (i + 1) * patches)
            mine = slice(i * row_total, (i + 1) * row_total)
            mark = jnp.concatenate([x[mine] for x in marks], 0).astype(BF16)
            stats = transposed_right(pick, mark)
            stats = jnp.concatenate([stats[h * 8 : (h + 1) * 8] for h in range(GROUP)], 1)
            log_total = stats[0:1]
            delta = stats[1:2]
            top = top_ref[0, i, 0:1, :]
            rescale = jnp.exp(top - log_total)
            keys = key_ref[rows, :]
            values = value_ref[rows, :]
            grads = spread_heads(
                jnp.concatenate([x[mine] for x in received], 0), masks
            ).astype(BF16)
            masked = jnp.where(valid, scale * transposed_right(keys, queries), MASKED)
            probs = jnp.where(valid, jnp.exp(masked - log_total), 0.0)
            block_exp = jnp.where(valid, jnp.exp(masked - top), 0.0)
            weights = (block_exp.astype(BF16).astype(F32) * rescale).astype(BF16)
            grad_probs = transposed_right(values, grads)
            grad_scores = (probs * (grad_probs - delta)).astype(BF16)
            both_ref[rows, :] = (scale * matmul(grad_scores, queries)).astype(BF16)
            held_ref[rows, :] = matmul(weights, grads).astype(BF16)
            grad_query = grad_query + transposed_left(grad_scores, keys)

            lat_probs = jnp.where(first, jnp.exp(lat_scores - log_total), 0.0)
            lat_exp = jnp.where(first, jnp.exp(lat_scores - top), 0.0)
            lat_weights = (lat_exp.astype(BF16).astype(F32) * rescale).astype(BF16)
            lat_weights = jnp.where(first, lat_weights, jnp.zeros_like(lat_weights))
            lat_grad_probs = transposed_right(lat_values, grads)
            lat_grad_scores = (lat_probs * (lat_grad_probs - delta)).astype(BF16)
            lat_grad_key = lat_grad_key + matmul(lat_grad_scores, queries)
            lat_grad_value = lat_grad_value + matmul(lat_weights, grads)
            grad_query = grad_query + transposed_left(lat_grad_scores, lat_keys)
        sums_ref[0] = scale * collect_heads(grad_query, masks)
        sums_ref[1] = scale * lat_grad_key
        sums_ref[2] = lat_grad_value


def body(
    media,
    cotangent,
    frame_count,
    frame_start,
    latents,
    time_embed,
    media_gain,
    media_bias,
    latent_gain,
    latent_bias,
    ffn_gain,
    ffn_bias,
    query_weight,
    key_weight,
    value_weight,
    out_weight,
    up_weight,
    down_weight,
):
    items = media.shape[0]
    patches = media.shape[2]
    width = media.shape[3]
    lats = latents.shape[0]
    frame_total = time_embed.shape[0]
    row_total = cotangent.shape[1]
    own = items * row_total
    head_size = width // HEADS
    half = width // CHUNKS
    chunk_heads = HEADS // CHUNKS
    group_width = GROUP * head_size
    groups = chunk_heads // GROUP
    stack = GROUP * lats
    tokens = items * patches
    all_tokens = tokens + lats
    shard = query_weight.shape[0]
    hidden_shard = down_weight.shape[0]
    item_size = lax.axis_size("items")
    frame_size = lax.axis_size("frames")
    plane = item_size * own
    item_index = lax.axis_index("items")
    slot = lax.axis_index("frames")
    row_base = slot * row_total
    params = pltpu.CompilerParams(vmem_limit_bytes=56 * 2**20)
    smem = pl.BlockSpec(memory_space=pltpu.SMEM)
    sizes = dict(items=items, head_size=head_size, heads=chunk_heads)

    def struct(shape, kind):
        return jax.ShapeDtypeStruct(shape, kind)

    def cost(flops, *arrays):
        return pl.CostEstimate(
            flops=flops,
            bytes_accessed=sum(a.size * a.dtype.itemsize for a in arrays),
            transcendentals=0,
        )

    lat_norm = layer_norm(latents, latent_gain, latent_bias).astype(BF16)
    lat_cols = lax.dynamic_slice_in_dim(lat_norm, item_index * shard, shard, 1)

    def column_blocks(x):
        return jnp.transpose(x.reshape(-1, item_size, shard), (1, 0, 2))

    def whole_columns(x):
        blocks = gather_exchange(x, "items")
        return jnp.transpose(blocks, (1, 0, 2)).reshape(x.shape[0], width)

    queries = whole_columns(
        scatter_exchange(column_blocks(matmul(lat_cols, query_weight)), "items").astype(BF16)
    )

    kv_full = lax.all_gather(
        jnp.concatenate([key_weight, value_weight], 1), "items", axis=0, tiled=True
    )
    out_full = lax.all_gather(after(out_weight, kv_full), "items", axis=0, tiled=True)
    up_slice = lax.all_to_all(after(up_weight, kv_full), "items", 1, 0, tiled=True)
    grad_out = cotangent.reshape(own, width)
    grad_low = grad_out.astype(BF16)
    low_plane = lax.all_gather(after(grad_low, out_full), "items", axis=0, tiled=True)
    low_other = lax.all_gather(
        after(others(grad_low, "frames"), low_plane), "items", axis=0
    ).reshape(-1, width)

    counts = lax.dynamic_slice_in_dim(frame_count, item_index * items, items)
    starts = lax.dynamic_slice_in_dim(frame_start, item_index * items, items)
    offset = (slot - starts) % frame_total
    flags = jnp.concatenate(
        [(offset < counts).astype(jnp.int32), (slot == 0).astype(jnp.int32)[None]]
    )
    picker = (offset[:, None] == jnp.arange(frame_total, dtype=jnp.int32)[None, :]).astype(F32)
    time_rows = jnp.dot(picker, time_embed, precision=HIGHEST, preferred_element_type=F32)
    with_time = media[:, 0].astype(F32) + time_rows[:, None, :]
    normed = layer_norm(with_time, media_gain, media_bias).astype(BF16)
    flat_norm = normed.reshape(tokens, width)
    by_core = flat_norm.reshape(tokens, item_size // 2, 2, shard)
    core = item_index % 2
    norm_keep = lax.dynamic_index_in_dim(by_core, core, 2, False).reshape(tokens, -1)
    norm_send = lax.dynamic_index_in_dim(by_core, 1 - core, 2, False).reshape(tokens, -1)
    all_rows = after(jnp.concatenate([flat_norm, lat_norm], 0), norm_keep, norm_send)

    keys, values, tops, messages = [], [], [], []
    for c in range(CHUNKS):

        def block_of(g, c=c):
            return (0, c * groups + g)

        def value_block_of(g, c=c):
            return (0, (CHUNKS + c) * groups + g)

        key_rows, value_rows, message, top = pl.pallas_call(
            functools.partial(
                forward_kernel, patches=patches, scale=head_size**-0.5, **sizes
            ),
            grid=(groups,),
            in_specs=[
                smem,
                pl.BlockSpec((all_tokens, width), lambda g: (0, 0)),
                pl.BlockSpec((width, group_width), block_of),
                pl.BlockSpec((width, group_width), value_block_of),
                pl.BlockSpec((lats, group_width), block_of),
            ],
            out_specs=[
                pl.BlockSpec((all_tokens, group_width), lambda g: (0, g)),
                pl.BlockSpec((all_tokens, group_width), lambda g: (0, g)),
                pl.BlockSpec((frame_size, own, half + LANES), lambda g: (0, 0, 0)),
                pl.BlockSpec((1, items, 8, stack), lambda g: (g, 0, 0, 0)),
            ],
            out_shape=[
                struct((all_tokens, half), BF16),
                struct((all_tokens, half), BF16),
                struct((frame_size, own, half + LANES), BF16),
                struct((groups, items, 8, stack), F32),
            ],
            cost_estimate=cost(4 * all_tokens * width * half, all_rows, kv_full),
            compiler_params=params,
        )(flags, all_rows, kv_full, kv_full, queries)
        keys.append(key_rows)
        values.append(value_rows)
        tops.append(top)
        messages.append(lax.all_to_all(message, "frames", 0, 0))

    base_rows = lax.dynamic_slice_in_dim(latents, row_base, row_total, 0)
    messages[0] = after(messages[0], up_slice)
    merged, attended, mid_rows, ffn_copies, logs, entropy_wide = pl.pallas_call(
        functools.partial(merge_kernel, chunks=CHUNKS, **sizes),
        out_shape=[
            struct((own, width), F32),
            struct((own, width), BF16),
            struct((own, width), F32),
            struct((item_size, own, width), BF16),
            struct((CHUNKS, own, LANES), F32),
            struct((own, LANES), F32),
        ],
        cost_estimate=cost(2 * own * width * width, out_full, *messages),
        compiler_params=params,
    )(*messages, base_rows, out_full, ffn_gain[None], ffn_bias[None])
    entropy = entropy_wide[:, 0].reshape(items, row_total)

    ffn_plane = lax.all_to_all(ffn_copies, "items", 0, 0).reshape(plane, width)
    ffn_shift = others(after(ffn_copies, ffn_plane)[0], "frames")
    grad_part, result_part = pl.pallas_call(
        feed_kernel,
        out_shape=[struct((plane, width), BF16), struct((plane, width), BF16)],
        cost_estimate=cost(
            10 * plane * width * hidden_shard, ffn_plane, low_plane, up_slice, down_weight
        ),
        compiler_params=params,
    )(ffn_plane, low_plane, up_slice, down_weight)
    grad_pieces = lax.all_to_all(grad_part.reshape(item_size, own, width), "items", 0, 0)

    turn, grad_branch, grad_base, ffn_sums = pl.pallas_call(
        functools.partial(turn_kernel, chunks=CHUNKS, **sizes),
        out_shape=[
            struct((frame_size, own, width + CHUNKS * LANES), BF16),
            struct((own, width), BF16),
            struct((row_total, width), F32),
            struct((8, width), F32),
        ],
        cost_estimate=cost(2 * own * width * width, out_full, grad_pieces, mid_rows),
        compiler_params=params,
    )(grad_pieces, mid_rows, grad_out, ffn_gain[None], merged, logs, out_full)
    turn_every = lax.all_to_all(turn, "frames", 0, 0)

    grad_rows, grad_sums, sends, kv_chunks = [], [], [], []
    for c in range(CHUNKS):

        def block_of(g, s, c=c):
            return (0, c * groups + g)

        chunk_grad, chunk_sums = pl.pallas_call(
            functools.partial(
                backward_kernel, patches=patches, scale=head_size**-0.5, **sizes
            ),
            grid=(groups, 2),
            in_specs=[
                smem,
                pl.BlockSpec((all_tokens, group_width), lambda g, s: (0, g)),
                pl.BlockSpec((all_tokens, group_width), lambda g, s: (0, g)),
                pl.BlockSpec((lats, group_width), block_of),
                pl.BlockSpec(
                    (frame_size, own, group_width), lambda g, s, c=c: (0, 0, c * groups + g)
                ),
                pl.BlockSpec(
                    (frame_size, own, LANES), lambda g, s, c=c: (0, 0, width // LANES + c)
                ),
                pl.BlockSpec((1, items, 8, stack), lambda g, s: (g, 0, 0, 0)),
            ],
            out_specs=[
                pl.BlockSpec((tokens, group_width), lambda g, s: (0, g + s * groups)),
                pl.BlockSpec((3, lats, group_width), lambda g, s: (0, 0, g)),
            ],
            out_shape=[
                struct((tokens, 2 * half), BF16),
                struct((3, lats, half), F32),
            ],
            scratch_shapes=[pltpu.VMEM((tokens, group_width), BF16)],
            cost_estimate=cost(
                10 * items * groups * stack * group_width * (patches + lats),
                keys[c],
                values[c],
                turn_every,
            ),
            compiler_params=params,
        )(flags, keys[c], values[c], queries, turn_every, turn_every, tops[c])
        if c:
            chunk_grad = after(chunk_grad, sends[-1])
        send = transposed_left(norm_send, chunk_grad).astype(BF16)
        pair = transposed_left(norm_keep, chunk_grad) + swap_cores(send, "items").astype(F32)
        pieces = pair.astype(BF16).reshape(item_size // 2, shard, 2 * half)
        pieces = lax.all_to_all(
            pieces, "items", 0, 0, axis_index_groups=core_groups("items")
        )
        kv_chunks.append(jnp.sum(pieces.astype(F32), axis=0))
        grad_rows.append(chunk_grad)
        grad_sums.append(chunk_sums.reshape(3 * lats, half))
        sends.append(send)

    base_full = lax.dynamic_update_slice_in_dim(
        jnp.zeros((lats, width), F32), grad_base, row_base, 0
    )
    extra = jnp.concatenate([jnp.concatenate(grad_sums, 1), base_full, ffn_sums], 0)
    extra_cols = scatter_exchange(column_blocks(extra), "items")
    extra_cols = jnp.sum(gather_exchange(extra_cols, "frames"), axis=0)
    low_full = whole_columns(extra_cols[: 3 * lats].astype(BF16))
    query_low, lat_key_low, lat_value_low = (
        low_full[:lats],
        low_full[lats : 2 * lats],
        low_full[2 * lats :],
    )
    lat_cols_grad = (
        transposed_right(query_low, query_weight)
        + transposed_right(lat_key_low, key_weight)
        + transposed_right(lat_value_low, value_weight)
    )
    tail_full = whole_columns(jnp.concatenate([lat_cols_grad, extra_cols[3 * lats :]], 0))
    grad_lat_in, latent_gain_grad, latent_bias_grad = norm_back(
        latents, latent_gain, latent_bias, tail_full[:lats]
    )
    latents_grad = tail_full[lats : 2 * lats] + grad_lat_in
    ffn_gain_grad = tail_full[2 * lats]
    ffn_bias_grad = tail_full[2 * lats + 1]

    result = mid_rows + scatter_exchange(
        after(result_part, sends[0]).reshape(item_size, own, width), "items"
    )

    last = after(grad_rows[-1], sends[-1])
    grad_norm = sum(
        transposed_right(
            g[:, k * half : (k + 1) * half],
            kv_full[:, k * width + c * half : k * width + (c + 1) * half],
        )
        for c, g in enumerate(grad_rows[:-1] + [last])
        for k in range(2)
    )
    grad_time_in, grad_media_gain, grad_media_bias = norm_back(
        with_time, media_gain, media_bias, grad_norm.reshape(items, patches, width)
    )
    media_grad = grad_time_in.astype(BF16)[:, None]
    grad_time = lax.dot_general(
        picker,
        jnp.sum(grad_time_in, axis=1),
        (((0,), (0,)), ((), ())),
        precision=HIGHEST,
        preferred_element_type=F32,
    )
    small = jnp.concatenate([grad_time, grad_media_gain[None], grad_media_bias[None]], 0)
    small = jnp.concatenate([small, jnp.zeros((-small.shape[0] % 8, width), F32)], 0)
    small_cols = scatter_exchange(column_blocks(small), "items")
    small_cols = jnp.sum(gather_exchange(small_cols, "frames"), axis=0)

    ffn_other = lax.all_gather(after(ffn_shift, low_other), "items", axis=0)
    branch_plane = lax.all_gather(after(grad_branch, ffn_other), "items", axis=0, tiled=True)
    ffn_other = after(ffn_other.reshape(-1, width), sends[-1])
    block = min(256, plane)
    plane_blocks = plane // block
    blocks = plane_blocks * frame_size
    near = pl.BlockSpec((block, width), lambda i: (jnp.minimum(i, plane_blocks - 1), 0))
    far = pl.BlockSpec((block, width), lambda i: (jnp.maximum(i - plane_blocks, 0), 0))
    down_grad, up_part = pl.pallas_call(
        functools.partial(feed_grad_kernel, plane_blocks=plane_blocks),
        grid=(blocks,),
        in_specs=[
            near,
            near,
            far,
            far,
            pl.BlockSpec((width, hidden_shard), lambda i: (0, 0)),
            pl.BlockSpec((hidden_shard, width), lambda i: (0, 0)),
        ],
        out_specs=[
            pl.BlockSpec((hidden_shard, width), lambda i: (0, 0)),
            pl.BlockSpec((width, hidden_shard), lambda i: (0, 0)),
        ],
        out_shape=[struct((hidden_shard, width), F32), struct((width, hidden_shard), BF16)],
        scratch_shapes=[pltpu.VMEM((width, hidden_shard), F32)],
        cost_estimate=cost(
            8 * plane * frame_size * width * hidden_shard, ffn_other, low_other, up_slice
        ),
        compiler_params=params,
    )(ffn_plane, low_plane, ffn_other, low_other, up_slice, down_weight)
    up_grad = lax.all_to_all(up_part, "items", 0, 1, tiled=True).astype(F32)

    att_plane = lax.all_to_all(after(attended, sends[0]), "items", 1, 0, tiled=True)
    out_part = transposed_left(att_plane, branch_plane)

    first = reduce_rows(kv_chunks[0], "frames")
    rest = reduce_rows(jnp.concatenate(kv_chunks[1:] + [out_part], 1), "frames")
    sums = [first] + [rest[:, 2 * half * k : 2 * half * (k + 1)] for k in range(CHUNKS - 1)]
    out_grad = rest[:, 2 * half * (CHUNKS - 1) :]
    key_grad = jnp.concatenate([total[:, :half] for total in sums], 1) + transposed_left(
        lat_cols, lat_key_low
    )
    value_grad = jnp.concatenate([total[:, half:] for total in sums], 1) + transposed_left(
        lat_cols, lat_value_low
    )
    query_grad = transposed_left(lat_cols, query_low)
    return (
        result.reshape(items, row_total, width),
        entropy,
        media_grad,
        latents_grad,
        small_cols[:frame_total],
        small_cols[frame_total],
        small_cols[frame_total + 1],
        latent_gain_grad,
        latent_bias_grad,
        ffn_gain_grad,
        ffn_bias_grad,
        query_grad,
        key_grad,
        value_grad,
        out_grad,
        up_grad,
        down_grad,
    )


def solution(mesh):
    return jax.shard_map(
        body,
        mesh=mesh,
        in_specs=(
            P("items", "frames", None, None),
            P("items", "frames", None),
            P(),
            P(),
            P(),
            P(),
            P(),
            P(),
            P(),
            P(),
            P(),
            P(),
            P("items", None),
            P("items", None),
            P("items", None),
            P("items", None),
            P("items", None),
            P("items", None),
        ),
        out_specs=(
            P("items", "frames", None),
            P("items", "frames"),
            P("items", "frames", None, None),
            P(),
            P(None, "items"),
            P("items"),
            P("items"),
            P(),
            P(),
            P(),
            P(),
            P("items", None),
            P("items", None),
            P("items", None),
            P("items", None),
            P("items", None),
            P("items", None),
        ),
        check_vma=False,
    )
```

```python
import functools

import jax
import jax.numpy as jnp
from jax import lax
from jax.experimental import pallas as pl
from jax.experimental.pallas import tpu as pltpu
from jax.sharding import PartitionSpec as P

HEADS = 16
GROUP = 4
CHUNKS = 2
LANES = 128
EPSILON = 1e-05
MASKED = -1e30
F32 = jnp.float32
BF16 = jnp.bfloat16
HIGHEST = lax.Precision.HIGHEST


def layer_norm(inputs, norm_gain, norm_bias):
    center = inputs - jnp.mean(inputs, axis=-1, keepdims=True)
    spread = jnp.mean(center * center, axis=-1, keepdims=True)
    return center * lax.rsqrt(spread + EPSILON) * norm_gain + norm_bias


def matmul(left_side, right_side):
    return jnp.dot(left_side, right_side, preferred_element_type=F32)


def transposed_left(left_side, right_side):
    return lax.dot_general(
        left_side, right_side, (((0,), (0,)), ((), ())), preferred_element_type=F32
    )


def transposed_right(left_side, right_side):
    return lax.dot_general(
        left_side, right_side, (((1,), (1,)), ((), ())), preferred_element_type=F32
    )


def send_on(x, axis, step):
    size = lax.axis_size(axis)
    return lax.ppermute(x, axis, [(i, (i + step) % size) for i in range(size)])


def send_across(x, axis, distance):
    return lax.ppermute(x, axis, [(i, i ^ distance) for i in range(lax.axis_size(axis))])


def spread_on(x, axis):
    return [x] + [send_on(x, axis, s) for s in range(1, lax.axis_size(axis))]


def spread_across(x, axis):
    return [x] + [send_across(x, axis, d) for d in range(1, lax.axis_size(axis))]


def collect_across(pieces, axis):
    return [pieces[0]] + [send_across(p, axis, d) for d, p in enumerate(pieces) if d]


def total_of(pieces):
    return functools.reduce(jnp.add, [p.astype(F32) for p in pieces])


def reduce_rows(x, axis):
    size = lax.axis_size(axis)
    me = lax.axis_index(axis)
    rows = x.shape[0] // size
    own = []
    for s in range(size):
        piece = lax.dynamic_slice_in_dim(x, ((me + s) % size) * rows, rows, 0)
        own.append(send_on(piece.astype(BF16), axis, s) if s else piece)
    return spread_on(total_of(own).astype(BF16), axis)


def after(x, *earlier):
    return lax.optimization_barrier((x,) + earlier)[0]


def split_terms(x):
    high = x.astype(BF16)
    rest = x - high.astype(F32)
    middle = rest.astype(BF16)
    return high, middle, (rest - middle.astype(F32)).astype(BF16)


def iota(shape, dim):
    return lax.broadcasted_iota(jnp.int32, shape, dim)


def head_masks(rows, width, head_size):
    lane = iota((rows, width), 1)
    return [
        jnp.logical_and(lane >= h * head_size, lane < (h + 1) * head_size)
        for h in range(width // head_size)
    ]


def spread_heads(block, masks):
    return jnp.concatenate([jnp.where(m, block, jnp.zeros_like(block)) for m in masks], 0)


def collect_heads(block, masks):
    rows = block.shape[0] // len(masks)
    total = jnp.where(masks[0], block[:rows], 0.0)
    for h in range(1, len(masks)):
        total = total + jnp.where(masks[h], block[h * rows : (h + 1) * rows], 0.0)
    return total


def head_expand(width, head_size):
    row, column = iota((LANES, width), 0), iota((LANES, width), 1)
    return jnp.logical_and(column >= row * head_size, column < (row + 1) * head_size).astype(F32)


def live_rows(flag_ref, item, items, patches, lats, columns):
    row = iota((patches + lats, columns), 0)
    media = jnp.logical_and(row < patches, flag_ref[item] > 0)
    return jnp.logical_or(media, jnp.logical_and(row >= patches, flag_ref[items] > 0))


def norm_kernel(media_ref, time_ref, gain_ref, bias_ref, lat_ref, out_ref, *, steps, per_item):
    step = pl.program_id(0)

    @pl.when(step < steps)
    def _():
        rows = media_ref[...].astype(F32) + time_ref[pl.ds(step // per_item, 1), :]
        out_ref[...] = layer_norm(rows, gain_ref[...], bias_ref[...]).astype(BF16)

    @pl.when(step == steps)
    def _():
        out_ref[...] = lat_ref[...]


def forward_kernel(
    flag_ref, row_ref, weight_ref, query_ref, both_ref, top_ref, *refs,
    items, patches, scale, head_size, heads,
):
    message_refs, (part_ref, mark_ref) = refs[:-2], refs[-2:]
    lats, width = query_ref.shape
    frames = len(message_refs)
    own = message_refs[0].shape[0]
    row_total = own // items
    masks = head_masks(lats, width, head_size)
    queries = spread_heads(query_ref[...].astype(F32), masks).astype(BF16)
    both_ref[...] = matmul(row_ref[...], weight_ref[...]).astype(BF16)
    base = items * patches
    lat_both = both_ref[base : base + lats, :]
    group = pl.program_id(0)
    term, lane = iota((16, GROUP * LANES), 0), iota((16, GROUP * LANES), 1)
    place = jnp.logical_and(
        lane % LANES == term * heads + group * GROUP + lane // LANES, term < 9
    ).astype(BF16)
    for i in range(items):
        both = jnp.concatenate([both_ref[i * patches : (i + 1) * patches, :], lat_both], 0)
        live = live_rows(flag_ref, i, items, patches, lats, queries.shape[0])
        scores = scale * transposed_right(both[:, :width], queries)
        masked = jnp.where(live, scores, MASKED)
        top = jnp.max(masked, axis=0, keepdims=True)
        block_exp = jnp.where(live, jnp.exp(masked - top), 0.0)
        total = jnp.sum(block_exp, axis=0, keepdims=True)
        moment = jnp.sum(block_exp * scores, axis=0, keepdims=True)
        part = transposed_left(block_exp.astype(BF16), both[:, width:])
        part_ref[i] = collect_heads(part, masks)
        top_ref[0, i] = jnp.broadcast_to(top, top_ref.shape[2:])
        terms = jnp.concatenate(
            [t.astype(F32) for x in (top, total, moment) for t in split_terms(x)]
            + [jnp.zeros((7, top.shape[1]), F32)],
            0,
        ).astype(BF16)
        wide = transposed_left(terms, place)
        mark = wide[:lats, :LANES]
        for h in range(1, GROUP):
            mark = mark + wide[h * lats : (h + 1) * lats, h * LANES : (h + 1) * LANES]
        mark_ref[i] = mark

    end = message_refs[0].shape[1] - LANES
    for s, message_ref in enumerate(message_refs):
        start = pl.multiple_of(lax.rem(flag_ref[items + 1] + s, frames) * row_total, row_total)
        rows = pl.ds(start, row_total)
        block = jnp.concatenate([part_ref[i, rows, :] for i in range(items)], 0).astype(BF16)
        mark = jnp.concatenate([mark_ref[i, rows, :] for i in range(items)], 0).astype(BF16)
        for g in range(end // width):

            @pl.when(group == g)
            def _():
                message_ref[:, g * width : (g + 1) * width] = block
                if g == 0:
                    message_ref[:, end:] = mark
                else:
                    message_ref[:, end:] = message_ref[:, end:] + mark


def merge_kernel(*refs, chunks, frames, items, head_size, heads):
    message_refs = refs[: chunks * frames]
    base_ref, weight_ref, gain_ref, bias_ref = refs[chunks * frames : chunks * frames + 4]
    merged_ref, attended_ref, mid_ref, ffn_ref, log_ref, entropy_ref = refs[chunks * frames + 4 :]
    own, columns = message_refs[0].shape
    half = columns - LANES
    lane, column = iota((LANES, 3 * LANES), 0), iota((LANES, 3 * LANES), 1)
    gather = jnp.logical_and(
        jnp.logical_and(lane // heads // 3 == column // LANES, lane % heads == column % LANES),
        lane < 9 * heads,
    ).astype(BF16)
    expand = head_expand(half, head_size)
    live = iota((own, LANES), 1) < heads
    spread = jnp.zeros((own, LANES), F32)
    for c in range(chunks):
        sources = message_refs[c * frames : (c + 1) * frames]
        stats = [matmul(x[:, half:], gather) for x in sources]
        tops = [x[:, :LANES] for x in stats]
        peak = functools.reduce(jnp.maximum, tops)
        factors = [jnp.exp(t - peak) for t in tops]
        whole = sum(f * x[:, LANES : 2 * LANES] for f, x in zip(factors, stats))
        moment = sum(f * x[:, 2 * LANES :] for f, x in zip(factors, stats))
        whole = jnp.where(live, whole, 1.0)
        log_total = jnp.where(live, peak + jnp.log(whole), 0.0)
        log_ref[c] = log_total
        spread = spread + jnp.where(live, log_total - moment / whole, 0.0)
        merged = jnp.zeros((own, half), F32)
        for x, factor in zip(sources, factors):
            share = jnp.where(live, factor / whole, 0.0)
            wide = jnp.dot(share, expand, precision=HIGHEST, preferred_element_type=F32)
            merged = merged + x[:, :half].astype(F32) * wide
        merged_ref[:, c * half : (c + 1) * half] = merged
        attended_ref[:, c * half : (c + 1) * half] = merged.astype(BF16)
    entropy_ref[...] = jnp.broadcast_to(
        jnp.sum(spread, axis=1, keepdims=True) * (1.0 / HEADS), entropy_ref.shape
    )
    base = jnp.concatenate([base_ref[...]] * items, 0)
    mid = base + matmul(attended_ref[...], weight_ref[...])
    mid_ref[...] = mid
    ffn_ref[...] = layer_norm(mid, gain_ref[...], bias_ref[...]).astype(BF16)


def gelu_parts(x):
    share = 0.5 * (1.0 + lax.erf(x * (0.5**0.5)))
    slope = share + x * jnp.exp(-0.5 * x * x) * ((2.0 * jnp.pi) ** -0.5)
    return x * share, slope


def feed_kernel(*refs, devices):
    row_refs, low_refs = refs[:devices], refs[devices : 2 * devices]
    up_ref, down_ref = refs[2 * devices : 2 * devices + 2]
    plane_ref, plane_low_ref = refs[2 * devices + 2 : 2 * devices + 4]
    grad_refs = refs[2 * devices + 4 : 3 * devices + 4]
    result_refs = refs[3 * devices + 4 :]
    own = row_refs[0].shape[0]
    for d in range(devices):
        plane_ref[d * own : (d + 1) * own, :] = row_refs[d][...]
        plane_low_ref[d * own : (d + 1) * own, :] = low_refs[d][...]
    upward = matmul(plane_ref[...], up_ref[...])
    hidden, slope = gelu_parts(upward)
    grad_up = (slope * transposed_right(plane_low_ref[...], down_ref[...])).astype(BF16)
    grad = transposed_right(grad_up, up_ref[...]).astype(BF16)
    result = matmul(hidden.astype(BF16), down_ref[...]).astype(BF16)
    for d in range(devices):
        grad_refs[d][...] = grad[d * own : (d + 1) * own, :]
        result_refs[d][...] = result[d * own : (d + 1) * own, :]


def feed_grad_kernel(
    plane_ref, plane_low_ref, other_ref, other_low_ref, up_ref, down_ref, down_grad_ref, up_grad_ref,
    total_ref, *, plane_blocks,
):
    step = pl.program_id(0)
    near = step < plane_blocks
    rows = jnp.where(near, plane_ref[...], other_ref[...])
    low = jnp.where(near, plane_low_ref[...], other_low_ref[...])
    hidden, slope = gelu_parts(matmul(rows, up_ref[...]))
    grad_up = (slope * transposed_right(low, down_ref[...])).astype(BF16)
    down_part = transposed_left(hidden.astype(BF16), low)
    up_part = transposed_left(rows, grad_up)

    @pl.when(step == 0)
    def _():
        down_grad_ref[...] = down_part
        total_ref[...] = up_part

    @pl.when(step > 0)
    def _():
        down_grad_ref[...] += down_part
        total_ref[...] += up_part

    @pl.when(step == pl.num_programs(0) - 1)
    def _():
        up_grad_ref[...] = total_ref[...].astype(BF16)


def norm_backward(rows, gain, gradient):
    center = rows - jnp.mean(rows, axis=1, keepdims=True)
    rate = lax.rsqrt(jnp.mean(center * center, axis=1, keepdims=True) + EPSILON)
    unit = center * rate
    scaled = gradient * gain
    inner = scaled - jnp.mean(scaled, axis=1, keepdims=True)
    back = rate * (inner - unit * jnp.mean(scaled * unit, axis=1, keepdims=True))
    return (
        back,
        jnp.sum(gradient * unit, axis=0, keepdims=True),
        jnp.sum(gradient, axis=0, keepdims=True),
    )


def turn_kernel(*refs, devices, items, chunks, head_size, heads):
    part_refs = refs[:devices]
    mid_ref, cotangent_ref, gain_ref, merged_ref, log_ref, weight_ref = refs[
        devices : devices + 6
    ]
    message_ref, branch_ref, base_ref, sums_ref = refs[devices + 6 :]
    own, width = mid_ref.shape
    half = width // chunks
    gradient = total_of([x[...] for x in part_refs])
    back, gain_sum, bias_sum = norm_backward(mid_ref[...], gain_ref[...], gradient)
    grad_mid = cotangent_ref[...] + back
    sums_ref[...] = jnp.zeros(sums_ref.shape, F32)
    sums_ref[0:1, :] = gain_sum
    sums_ref[1:2, :] = bias_sum
    row_total = own // items
    base_ref[...] = total_of(
        [grad_mid[i * row_total : (i + 1) * row_total] for i in range(items)]
    )
    branch = grad_mid.astype(BF16)
    branch_ref[...] = branch
    grad_att = transposed_right(branch, weight_ref[...]).astype(BF16)
    expand = head_expand(half, head_size)
    lane, column = iota((6 * LANES, LANES), 0), iota((6 * LANES, LANES), 1)
    place = jnp.logical_and(
        lane % LANES < heads, column == (lane // LANES) * heads + lane % LANES
    ).astype(BF16)
    message_ref[:, :width] = grad_att
    for c in range(chunks):
        columns = slice(c * half, (c + 1) * half)
        delta = lax.dot_general(
            merged_ref[:, columns] * grad_att[:, columns].astype(F32),
            expand,
            (((1,), (1,)), ((), ())),
            precision=HIGHEST,
            preferred_element_type=F32,
        )
        terms = jnp.concatenate([t for x in (log_ref[c], delta) for t in split_terms(x)], 1)
        message_ref[:, width + c * LANES : width + (c + 1) * LANES] = matmul(
            terms, place
        ).astype(BF16)


def backward_kernel(
    *refs, frames, items, patches, scale, head_size, heads,
):
    flag_ref, both_ref, query_ref, top_ref = refs[:4]
    grad_refs = refs[4 : 4 + frames]
    mark_refs = refs[4 + frames : 4 + 2 * frames]
    out_ref, sum_ref, held_ref, note_ref = refs[4 + 2 * frames :]
    lats, width = query_ref.shape
    own = grad_refs[0].shape[0]
    row_total = own // items
    base = items * patches
    for s in range(frames):
        source = lax.rem(flag_ref[items + 1] + (frames - s), frames)
        rows = pl.ds(pl.multiple_of(source * row_total, row_total), row_total)
        block = grad_refs[s][...].astype(F32)
        mark = mark_refs[s][...].astype(F32)
        for i in range(items):
            held_ref[i, rows, :] = block[i * row_total : (i + 1) * row_total]
            note_ref[i, rows, :] = mark[i * row_total : (i + 1) * row_total]
    masks = head_masks(lats, width, head_size)
    queries = spread_heads(query_ref[...].astype(F32), masks).astype(BF16)
    lat_both = both_ref[base : base + lats, :]
    row, lane = iota((GROUP * 8, LANES), 0), iota((GROUP * 8, LANES), 1)
    pick = jnp.logical_and(
        jnp.logical_and(
            lane // heads // 3 == row % 8,
            lane % heads == pl.program_id(0) * GROUP + row // 8,
        ),
        lane < 6 * heads,
    ).astype(BF16)
    grad_query = jnp.zeros((queries.shape[0], width), F32)
    lat_grad_key = jnp.zeros((lats, width), F32)
    lat_grad_value = jnp.zeros((lats, width), F32)
    for i in range(items):
        rows = slice(i * patches, (i + 1) * patches)
        stats = transposed_right(pick, note_ref[i].astype(BF16))
        stats = jnp.concatenate([stats[h * 8 : (h + 1) * 8] for h in range(GROUP)], 1)
        log_total = stats[0:1]
        delta = stats[1:2]
        top = top_ref[0, i, 0:1, :]
        rescale = jnp.exp(top - log_total)
        both = jnp.concatenate([both_ref[rows, :], lat_both], 0)
        keys, values = both[:, :width], both[:, width:]
        grads = spread_heads(held_ref[i], masks).astype(BF16)
        live = live_rows(flag_ref, i, items, patches, lats, queries.shape[0])
        masked = jnp.where(live, scale * transposed_right(keys, queries), MASKED)
        probs = jnp.where(live, jnp.exp(masked - log_total), 0.0)
        block_exp = jnp.where(live, jnp.exp(masked - top), 0.0)
        weights = (block_exp.astype(BF16).astype(F32) * rescale).astype(BF16)
        grad_scores = (probs * (transposed_right(values, grads) - delta)).astype(BF16)
        grad_key = scale * matmul(grad_scores, queries)
        grad_value = matmul(weights, grads)
        out_ref[rows, :width] = grad_key[:patches].astype(BF16)
        out_ref[rows, width:] = grad_value[:patches].astype(BF16)
        grad_query = grad_query + transposed_left(grad_scores, keys)
        lat_grad_key = lat_grad_key + grad_key[patches:]
        lat_grad_value = lat_grad_value + grad_value[patches:]
    out_ref[base : base + lats, :width] = lat_grad_key.astype(BF16)
    out_ref[base : base + lats, width:] = lat_grad_value.astype(BF16)
    sum_ref[...] = scale * collect_heads(grad_query, masks)


def media_kernel(flag_ref, *refs, chunks, items, frames):
    grad_refs = refs[:chunks]
    weight_ref, media_ref, time_ref, gain_ref, out_ref, sums_ref = refs[chunks:]
    step = pl.program_id(0)
    span = weight_ref.shape[1] // chunks
    gradient = transposed_right(grad_refs[0][...], weight_ref[:, :span])
    for c in range(1, chunks):
        gradient = gradient + transposed_right(
            grad_refs[c][...], weight_ref[:, c * span : (c + 1) * span]
        )
    rows = media_ref[...].astype(F32) + time_ref[pl.ds(step, 1), :]
    back, gain_sum, bias_sum = norm_backward(rows, gain_ref[...], gradient)
    out_ref[...] = back.astype(BF16)

    @pl.when(step == 0)
    def _():
        sums_ref[...] = jnp.zeros(sums_ref.shape, F32)

    time_sum = jnp.sum(back, axis=0, keepdims=True)
    offset = flag_ref[items + 2 + step]
    place = iota((frames, 1), 0) == offset
    sums_ref[0:frames, :] += jnp.where(place, time_sum, 0.0)
    sums_ref[8:9, :] += gain_sum
    sums_ref[9:10, :] += bias_sum


def latent_kernel(
    flag_ref, *refs, chunks, items,
):
    grad_refs = refs[:chunks]
    query_refs = refs[chunks : 2 * chunks]
    (
        weight_ref, query_weight_ref, latent_ref, gain_ref, base_ref, ffn_ref, media_ref, out_ref,
    ) = refs[2 * chunks :]
    lats, width = latent_ref.shape
    span = weight_ref.shape[1] // chunks
    half = width // chunks
    gradient = jnp.zeros((lats, width), F32)
    for c in range(chunks):
        gradient = gradient + transposed_right(
            grad_refs[c][...], weight_ref[:, c * span : (c + 1) * span]
        )
        gradient = gradient + transposed_right(
            query_refs[c][...].astype(BF16), query_weight_ref[:, c * half : (c + 1) * half]
        )
        out_ref[lats : 2 * lats, c * half : (c + 1) * half] = query_refs[c][...]
    back, gain_sum, bias_sum = norm_backward(latent_ref[...], gain_ref[...], gradient)
    out_ref[:lats, :] = back
    row_total = base_ref.shape[0]
    start = pl.multiple_of(flag_ref[items + 1] * row_total, row_total)
    out_ref[pl.ds(start, row_total), :] += base_ref[...]
    at = 2 * lats
    out_ref[at : at + 16, :] = media_ref[...]
    out_ref[at + 16 : at + 24, :] = ffn_ref[...]
    out_ref[at + 18 : at + 19, :] = gain_sum
    out_ref[at + 19 : at + 20, :] = bias_sum
    out_ref[at + 24 :, :] = jnp.zeros((out_ref.shape[0] - at - 24, width), F32)


def place_kernel(flag_ref, *refs, chunks, frames, items, groups):
    chunk_refs = refs[: chunks * frames]
    more_refs = refs[chunks * frames : (chunks + 1) * frames]
    key_ref, value_ref, out_ref = refs[(chunks + 1) * frames :]
    width = key_ref.shape[2] // (chunks * groups)
    for s in range(frames):
        source = lax.rem(flag_ref[items + 1] + (frames - s), frames)
        out_ref[source] = more_refs[s][...].astype(F32)
        for c in range(chunks):
            for g in range(groups):
                at = (c * groups + g) * width
                block = chunk_refs[c * frames + s][:, 2 * g * width : 2 * (g + 1) * width]
                block = block.astype(F32)
                key_ref[source, :, at : at + width] = block[:, :width]
                value_ref[source, :, at : at + width] = block[:, width:]


def body(
    media,
    cotangent,
    frame_count,
    frame_start,
    latents,
    time_embed,
    media_gain,
    media_bias,
    latent_gain,
    latent_bias,
    ffn_gain,
    ffn_bias,
    query_weight,
    key_weight,
    value_weight,
    out_weight,
    up_weight,
    down_weight,
):
    items = media.shape[0]
    patches = media.shape[2]
    width = media.shape[3]
    lats = latents.shape[0]
    frame_total = time_embed.shape[0]
    row_total = cotangent.shape[1]
    own = items * row_total
    head_size = width // HEADS
    half = width // CHUNKS
    chunk_heads = HEADS // CHUNKS
    group_width = GROUP * head_size
    groups = chunk_heads // GROUP
    stack = GROUP * lats
    tokens = items * patches
    all_tokens = tokens + lats
    shard = query_weight.shape[0]
    hidden_shard = down_weight.shape[0]
    item_size = lax.axis_size("items")
    frame_size = lax.axis_size("frames")
    plane = item_size * own
    item_index = lax.axis_index("items")
    slot = lax.axis_index("frames")
    row_base = slot * row_total
    params = pltpu.CompilerParams(vmem_limit_bytes=56 * 2**20)
    smem = pl.BlockSpec(memory_space=pltpu.SMEM)
    whole = pl.BlockSpec(memory_space=pltpu.VMEM)
    sizes = dict(items=items, head_size=head_size, heads=chunk_heads)

    def struct(shape, kind):
        return jax.ShapeDtypeStruct(shape, kind)

    def cost(flops, *arrays):
        return pl.CostEstimate(
            flops=flops,
            bytes_accessed=sum(a.size * a.dtype.itemsize for a in arrays),
            transcendentals=0,
        )

    kv_full = lax.all_gather(
        jnp.concatenate(
            [
                w[:, g * group_width : (g + 1) * group_width]
                for g in range(HEADS // GROUP)
                for w in (key_weight, value_weight)
            ],
            1,
        ),
        "items",
        axis=0,
        tiled=True,
    )

    lat_norm = layer_norm(latents, latent_gain, latent_bias).astype(BF16)
    lat_cols = lax.dynamic_slice_in_dim(lat_norm, item_index * shard, shard, 1)
    query_part = matmul(lat_cols, query_weight)
    distance = 1
    while distance < item_size:
        query_part = query_part + send_across(query_part, "items", distance)
        distance *= 2
    queries = query_part.astype(BF16)

    counts = lax.dynamic_slice_in_dim(frame_count, item_index * items, items)
    starts = lax.dynamic_slice_in_dim(frame_start, item_index * items, items)
    offset = (slot - starts) % frame_total
    flags = jnp.concatenate(
        [
            (offset < counts).astype(jnp.int32),
            (slot == 0).astype(jnp.int32)[None],
            slot.astype(jnp.int32)[None],
            offset.astype(jnp.int32),
        ]
    )
    picker = (offset[:, None] == jnp.arange(frame_total, dtype=jnp.int32)[None, :]).astype(F32)
    time_rows = jnp.dot(picker, time_embed, precision=HIGHEST, preferred_element_type=F32)
    flat_media = media.reshape(tokens, width)
    steps = tokens // lats
    all_rows = pl.pallas_call(
        functools.partial(norm_kernel, steps=steps, per_item=patches // lats),
        grid=(steps + 1,),
        in_specs=[
            pl.BlockSpec((lats, width), lambda i: (jnp.minimum(i, steps - 1), 0)),
            whole,
            whole,
            whole,
            whole,
        ],
        out_specs=pl.BlockSpec((lats, width), lambda i: (i, 0)),
        out_shape=struct((all_tokens, width), BF16),
        cost_estimate=cost(0, flat_media, flat_media),
        compiler_params=params,
    )(flat_media, time_rows, media_gain[None], media_bias[None], lat_norm)

    grad_out = cotangent.reshape(own, width)
    grad_low = grad_out.astype(BF16)
    low_blocks = spread_across(grad_low, "items")
    low_shift = jnp.stack(spread_on(grad_low, "frames")[1:])
    out_full = lax.all_gather(after(out_weight, all_rows), "items", axis=0, tiled=True)

    boths, tops, messages = [], [], []
    for c in range(CHUNKS):

        def block_of(g, c=c):
            return (0, c * groups + g)

        both, top, *parts = pl.pallas_call(
            functools.partial(
                forward_kernel, patches=patches, scale=head_size**-0.5, **sizes
            ),
            grid=(groups,),
            in_specs=[
                smem,
                pl.BlockSpec((all_tokens, width), lambda g: (0, 0)),
                pl.BlockSpec((width, 2 * group_width), block_of),
                pl.BlockSpec((lats, group_width), block_of),
            ],
            out_specs=[
                pl.BlockSpec((all_tokens, 2 * group_width), lambda g: (0, g)),
                pl.BlockSpec((1, items, 8, stack), lambda g: (g, 0, 0, 0)),
            ]
            + [pl.BlockSpec((own, half + LANES), lambda g: (0, 0))] * frame_size,
            out_shape=[
                struct((all_tokens, 2 * half), BF16),
                struct((groups, items, 8, stack), F32),
            ]
            + [struct((own, half + LANES), BF16)] * frame_size,
            scratch_shapes=[
                pltpu.VMEM((items, lats, group_width), F32),
                pltpu.VMEM((items, lats, LANES), F32),
            ],
            cost_estimate=cost(4 * all_tokens * width * half, all_rows, kv_full),
            compiler_params=params,
        )(flags, all_rows, kv_full, queries)
        boths.append(both)
        tops.append(top)
        messages += [p if s == 0 else send_on(p, "frames", s) for s, p in enumerate(parts)]
    up_slice = lax.all_to_all(after(up_weight, boths[0]), "items", 1, 0, tiled=True)
    low_other = lax.all_gather(after(low_shift, boths[0]), "items", axis=0).reshape(-1, width)
    query_full = lax.all_gather(after(query_weight, boths[1]), "items", axis=0, tiled=True)

    base_rows = lax.dynamic_slice_in_dim(latents, row_base, row_total, 0)
    merged, attended, mid_rows, ffn_in, logs, entropy_wide = pl.pallas_call(
        functools.partial(merge_kernel, chunks=CHUNKS, frames=frame_size, **sizes),
        out_shape=[
            struct((own, width), F32),
            struct((own, width), BF16),
            struct((own, width), F32),
            struct((own, width), BF16),
            struct((CHUNKS, own, LANES), F32),
            struct((own, LANES), F32),
        ],
        cost_estimate=cost(2 * own * width * width, out_full, *messages),
        compiler_params=params,
    )(*messages, base_rows, out_full, ffn_gain[None], ffn_bias[None])
    entropy = entropy_wide[:, 0].reshape(items, row_total)

    ffn_blocks = spread_across(ffn_in, "items")
    ffn_plane, low_plane, *parts = pl.pallas_call(
        functools.partial(feed_kernel, devices=item_size),
        out_shape=[struct((plane, width), BF16)] * 2 + [struct((own, width), BF16)] * (2 * item_size),
        cost_estimate=cost(
            10 * plane * width * hidden_shard, up_slice, down_weight, *ffn_blocks
        ),
        compiler_params=params,
    )(*ffn_blocks, *low_blocks, up_slice, down_weight)
    ffn_shift = jnp.stack(spread_on(after(ffn_in, parts[0]), "frames")[1:])
    grad_blocks = collect_across(parts[:item_size], "items")

    turn, grad_branch, grad_base, ffn_sums = pl.pallas_call(
        functools.partial(turn_kernel, devices=item_size, chunks=CHUNKS, **sizes),
        out_shape=[
            struct((own, width + CHUNKS * LANES), BF16),
            struct((own, width), BF16),
            struct((row_total, width), F32),
            struct((8, width), F32),
        ],
        cost_estimate=cost(2 * own * width * width, out_full, mid_rows, *grad_blocks),
        compiler_params=params,
    )(*grad_blocks, mid_rows, grad_out, ffn_gain[None], merged, logs, out_full)
    turns = spread_on(turn, "frames")

    chip, core = item_index // 2, item_index % 2
    chunk_grads, chunk_queries, terms, kv_chunks = [], [], [], []
    for c in range(CHUNKS):

        def block_of(g, c=c):
            return (0, c * groups + g)

        chunk_grad, chunk_query = pl.pallas_call(
            functools.partial(
                backward_kernel, frames=frame_size, patches=patches, scale=head_size**-0.5, **sizes
            ),
            grid=(groups,),
            in_specs=[
                smem,
                pl.BlockSpec((all_tokens, 2 * group_width), lambda g: (0, g)),
                pl.BlockSpec((lats, group_width), block_of),
                pl.BlockSpec((1, items, 8, stack), lambda g: (g, 0, 0, 0)),
            ]
            + [pl.BlockSpec((own, group_width), block_of)] * frame_size
            + [pl.BlockSpec((own, LANES), lambda g, c=c: (0, width // LANES + c))] * frame_size,
            out_specs=[
                pl.BlockSpec((all_tokens, 2 * group_width), lambda g: (0, g)),
                pl.BlockSpec((lats, group_width), lambda g: (0, g)),
            ],
            out_shape=[
                struct((all_tokens, 2 * half), BF16),
                struct((lats, half), F32),
            ],
            scratch_shapes=[
                pltpu.VMEM((items, lats, group_width), F32),
                pltpu.VMEM((items, lats, LANES), F32),
            ],
            cost_estimate=cost(
                10 * items * groups * stack * group_width * (patches + lats), boths[c], boths[c]
            ),
            compiler_params=params,
        )(flags, after(boths[c], *terms), queries, tops[c], *turns, *turns)
        term = transposed_left(all_rows, chunk_grad).astype(BF16)
        blocks = term.reshape(item_size // 2, 2, shard, 2 * half)

        def block(k, which):
            return lax.dynamic_slice(
                blocks, (chip ^ k, which, 0, 0), (1, 1, shard, 2 * half)
            ).reshape(shard, 2 * half)

        received = send_across(
            jnp.stack([block(k, 1 - core) for k in range(item_size // 2)]), "items", 1
        )
        pieces = []
        for k in range(item_size // 2):
            piece = block(k, core).astype(F32) + received[k].astype(F32)
            pieces.append(send_across(piece.astype(BF16), "items", 2 * k) if k else piece)
        kv_chunks.append(total_of(pieces))
        chunk_grads.append(chunk_grad)
        chunk_queries.append(chunk_query)
        terms.append(term)

    media_grad, media_sums = pl.pallas_call(
        functools.partial(media_kernel, chunks=CHUNKS, items=items, frames=frame_total),
        grid=(items,),
        in_specs=[smem]
        + [pl.BlockSpec((patches, 2 * half), lambda i: (i, 0))] * CHUNKS
        + [
            whole,
            pl.BlockSpec((patches, width), lambda i: (i, 0)),
            whole,
            whole,
        ],
        out_specs=[
            pl.BlockSpec((patches, width), lambda i: (i, 0)),
            pl.BlockSpec((16, width), lambda i: (0, 0)),
        ],
        out_shape=[struct((tokens, width), BF16), struct((16, width), F32)],
        cost_estimate=cost(4 * tokens * width * width, kv_full, *chunk_grads),
        compiler_params=params,
    )(
        flags,
        *[after(g, terms[-1]) for g in chunk_grads],
        kv_full,
        flat_media,
        time_rows,
        media_gain[None],
    )

    sum_rows = 2 * lats + 24
    sum_rows += -sum_rows % (8 * item_size)
    last_block = pl.BlockSpec((lats, 2 * half), lambda i: (tokens // lats, 0))
    payload = pl.pallas_call(
        functools.partial(latent_kernel, chunks=CHUNKS, items=items),
        grid=(1,),
        in_specs=[smem] + [last_block] * CHUNKS + [whole] * (CHUNKS + 7),
        out_specs=whole,
        out_shape=struct((sum_rows, width), F32),
        cost_estimate=cost(6 * lats * width * width, kv_full, query_full),
        compiler_params=params,
    )(
        flags,
        *chunk_grads,
        *chunk_queries,
        kv_full,
        query_full,
        latents,
        latent_gain[None],
        grad_base,
        ffn_sums,
        media_sums,
    )
    payload_part = lax.psum_scatter(payload, "items", scatter_dimension=0, tiled=True)
    sums = lax.all_gather(
        total_of(spread_on(payload_part, "frames")), "items", axis=0, tiled=True
    )
    latents_grad = sums[:lats]
    query_grad = transposed_left(lat_cols, sums[lats : 2 * lats].astype(BF16))
    at = 2 * lats
    column_sums = lax.dynamic_slice_in_dim(sums[at : at + 16], item_index * shard, shard, 1)

    result = mid_rows + total_of(
        collect_across([after(p, terms[-1]) for p in parts[item_size:]], "items")
    )

    ffn_other = lax.all_gather(ffn_shift, "items", axis=0)
    branch_plane = lax.all_gather(after(grad_branch, ffn_other), "items", axis=0, tiled=True)
    ffn_other = after(ffn_other.reshape(-1, width), payload)
    block_rows = min(256, plane)
    plane_blocks = plane // block_rows
    near = pl.BlockSpec((block_rows, width), lambda i: (jnp.minimum(i, plane_blocks - 1), 0))
    far = pl.BlockSpec((block_rows, width), lambda i: (jnp.maximum(i - plane_blocks, 0), 0))
    down_grad, up_part = pl.pallas_call(
        functools.partial(feed_grad_kernel, plane_blocks=plane_blocks),
        grid=(plane_blocks * frame_size,),
        in_specs=[near, near, far, far, whole, whole],
        out_specs=[
            pl.BlockSpec((hidden_shard, width), lambda i: (0, 0)),
            pl.BlockSpec((width, hidden_shard), lambda i: (0, 0)),
        ],
        out_shape=[struct((hidden_shard, width), F32), struct((width, hidden_shard), BF16)],
        scratch_shapes=[pltpu.VMEM((width, hidden_shard), F32)],
        cost_estimate=cost(
            8 * plane * frame_size * width * hidden_shard, ffn_other, low_other, up_slice
        ),
        compiler_params=params,
    )(ffn_plane, low_plane, ffn_other, low_other, up_slice, down_weight)
    up_grad = lax.all_to_all(up_part, "items", 0, 1, tiled=True).astype(F32)

    att_plane = lax.all_to_all(after(attended, terms[0]), "items", 1, 0, tiled=True)
    out_part = transposed_left(att_plane, branch_plane)

    placed = []
    for k in kv_chunks + [out_part]:
        placed += reduce_rows(k, "frames")
    key_grad, value_grad, out_grad = pl.pallas_call(
        functools.partial(
            place_kernel, chunks=CHUNKS, frames=frame_size, items=items, groups=groups
        ),
        in_specs=[smem] + [whole] * len(placed),
        out_specs=[whole] * 3,
        out_shape=[struct((frame_size, shard // frame_size, width), F32)] * 3,
        cost_estimate=cost(0, *placed),
        compiler_params=params,
    )(flags, *placed)
    return (
        result.reshape(items, row_total, width),
        entropy,
        media_grad.reshape(media.shape),
        latents_grad,
        column_sums[:frame_total],
        column_sums[8],
        column_sums[9],
        sums[at + 18],
        sums[at + 19],
        sums[at + 16],
        sums[at + 17],
        query_grad,
        key_grad.reshape(shard, width),
        value_grad.reshape(shard, width),
        out_grad.reshape(shard, width),
        up_grad,
        down_grad,
    )


def solution(mesh):
    return jax.shard_map(
        body,
        mesh=mesh,
        in_specs=(
            P("items", "frames", None, None),
            P("items", "frames", None),
            P(),
            P(),
            P(),
            P(),
            P(),
            P(),
            P(),
            P(),
            P(),
            P(),
            P("items", None),
            P("items", None),
            P("items", None),
            P("items", None),
            P("items", None),
            P("items", None),
        ),
        out_specs=(
            P("items", "frames", None),
            P("items", "frames"),
            P("items", "frames", None, None),
            P(),
            P(None, "items"),
            P("items"),
            P("items"),
            P(),
            P(),
            P(),
            P(),
            P("items", None),
            P("items", None),
            P("items", None),
            P("items", None),
            P("items", None),
            P("items", None),
        ),
        check_vma=False,
    )
```

```python
import functools

import jax
import jax.numpy as jnp
from jax import lax
from jax.experimental import pallas as pl
from jax.experimental.pallas import tpu as pltpu
from jax.sharding import PartitionSpec as P

HEADS = 16
GROUP = 4
CHUNKS = 2
LANES = 128
EPSILON = 1e-05
MASKED = -1e30
F32 = jnp.float32
BF16 = jnp.bfloat16
HIGHEST = lax.Precision.HIGHEST


def layer_norm(inputs, norm_gain, norm_bias):
    center = inputs - jnp.mean(inputs, axis=-1, keepdims=True)
    spread = jnp.mean(center * center, axis=-1, keepdims=True)
    return center * lax.rsqrt(spread + EPSILON) * norm_gain + norm_bias


def matmul(left_side, right_side):
    return jnp.dot(left_side, right_side, preferred_element_type=F32)


def transposed_left(left_side, right_side):
    return lax.dot_general(
        left_side, right_side, (((0,), (0,)), ((), ())), preferred_element_type=F32
    )


def transposed_right(left_side, right_side):
    return lax.dot_general(
        left_side, right_side, (((1,), (1,)), ((), ())), preferred_element_type=F32
    )


def send_on(x, axis, step):
    size = lax.axis_size(axis)
    return lax.ppermute(x, axis, [(i, (i + step) % size) for i in range(size)])


def send_across(x, axis, distance):
    return lax.ppermute(x, axis, [(i, i ^ distance) for i in range(lax.axis_size(axis))])


def spread_on(x, axis):
    return [x] + [send_on(x, axis, s) for s in range(1, lax.axis_size(axis))]


def spread_across(x, axis):
    return [x] + [send_across(x, axis, d) for d in range(1, lax.axis_size(axis))]


def collect_across(pieces, axis):
    return [pieces[0]] + [send_across(p, axis, d) for d, p in enumerate(pieces) if d]


def total_of(pieces):
    return functools.reduce(jnp.add, [p.astype(F32) for p in pieces])


def reduce_rows(x, axis):
    size = lax.axis_size(axis)
    me = lax.axis_index(axis)
    rows = x.shape[0] // size
    own = []
    for s in range(size):
        piece = lax.dynamic_slice_in_dim(x, ((me + s) % size) * rows, rows, 0)
        own.append(send_on(piece.astype(BF16), axis, s) if s else piece)
    return spread_on(total_of(own).astype(BF16), axis)


def after(x, *earlier):
    return lax.optimization_barrier((x,) + earlier)[0]


def split_terms(x):
    high = x.astype(BF16)
    rest = x - high.astype(F32)
    middle = rest.astype(BF16)
    return high, middle, (rest - middle.astype(F32)).astype(BF16)


def iota(shape, dim):
    return lax.broadcasted_iota(jnp.int32, shape, dim)


def head_masks(rows, width, head_size):
    lane = iota((rows, width), 1)
    return [
        jnp.logical_and(lane >= h * head_size, lane < (h + 1) * head_size)
        for h in range(width // head_size)
    ]


def spread_heads(block, masks):
    return jnp.concatenate([jnp.where(m, block, jnp.zeros_like(block)) for m in masks], 0)


def collect_heads(block, masks):
    rows = block.shape[0] // len(masks)
    total = jnp.where(masks[0], block[:rows], 0.0)
    for h in range(1, len(masks)):
        total = total + jnp.where(masks[h], block[h * rows : (h + 1) * rows], 0.0)
    return total


def head_expand(width, head_size):
    row, column = iota((LANES, width), 0), iota((LANES, width), 1)
    return jnp.logical_and(column >= row * head_size, column < (row + 1) * head_size).astype(F32)


def live_rows(flag_ref, item, items, patches, lats, columns):
    row = iota((patches + lats, columns), 0)
    media = jnp.logical_and(row < patches, flag_ref[item] > 0)
    return jnp.logical_or(media, jnp.logical_and(row >= patches, flag_ref[items] > 0))


def norm_kernel(media_ref, time_ref, gain_ref, bias_ref, lat_ref, out_ref, *, steps, per_item):
    step = pl.program_id(0)

    @pl.when(step < steps)
    def _():
        rows = media_ref[...].astype(F32) + time_ref[pl.ds(step // per_item, 1), :]
        out_ref[...] = layer_norm(rows, gain_ref[...], bias_ref[...]).astype(BF16)

    @pl.when(step == steps)
    def _():
        out_ref[...] = lat_ref[...]


def forward_kernel(
    flag_ref, row_ref, weight_ref, query_ref, both_ref, top_ref, *refs,
    items, patches, scale, head_size, heads,
):
    message_refs, (part_ref, mark_ref) = refs[:-2], refs[-2:]
    lats, width = query_ref.shape
    frames = len(message_refs)
    own = message_refs[0].shape[0]
    row_total = own // items
    masks = head_masks(lats, width, head_size)
    queries = spread_heads(query_ref[...].astype(F32), masks).astype(BF16)
    both_ref[...] = matmul(row_ref[...], weight_ref[...]).astype(BF16)
    base = items * patches
    lat_both = both_ref[base : base + lats, :]
    group = pl.program_id(0)
    term, lane = iota((16, GROUP * LANES), 0), iota((16, GROUP * LANES), 1)
    place = jnp.logical_and(
        lane % LANES == term * heads + group * GROUP + lane // LANES, term < 9
    ).astype(BF16)
    for i in range(items):
        both = jnp.concatenate([both_ref[i * patches : (i + 1) * patches, :], lat_both], 0)
        live = live_rows(flag_ref, i, items, patches, lats, queries.shape[0])
        scores = scale * transposed_right(both[:, :width], queries)
        masked = jnp.where(live, scores, MASKED)
        top = jnp.max(masked, axis=0, keepdims=True)
        block_exp = jnp.where(live, jnp.exp(masked - top), 0.0)
        total = jnp.sum(block_exp, axis=0, keepdims=True)
        moment = jnp.sum(block_exp * scores, axis=0, keepdims=True)
        part = transposed_left(block_exp.astype(BF16), both[:, width:])
        part_ref[i] = collect_heads(part, masks)
        top_ref[0, i] = jnp.broadcast_to(top, top_ref.shape[2:])
        terms = jnp.concatenate(
            [t.astype(F32) for x in (top, total, moment) for t in split_terms(x)]
            + [jnp.zeros((7, top.shape[1]), F32)],
            0,
        ).astype(BF16)
        wide = transposed_left(terms, place)
        mark = wide[:lats, :LANES]
        for h in range(1, GROUP):
            mark = mark + wide[h * lats : (h + 1) * lats, h * LANES : (h + 1) * LANES]
        mark_ref[i] = mark

    end = message_refs[0].shape[1] - LANES
    for s, message_ref in enumerate(message_refs):
        start = pl.multiple_of(lax.rem(flag_ref[items + 1] + s, frames) * row_total, row_total)
        rows = pl.ds(start, row_total)
        block = jnp.concatenate([part_ref[i, rows, :] for i in range(items)], 0).astype(BF16)
        mark = jnp.concatenate([mark_ref[i, rows, :] for i in range(items)], 0).astype(BF16)
        for g in range(end // width):

            @pl.when(group == g)
            def _():
                message_ref[:, g * width : (g + 1) * width] = block
                if g == 0:
                    message_ref[:, end:] = mark
                else:
                    message_ref[:, end:] = message_ref[:, end:] + mark


def merge_kernel(*refs, chunks, frames, items, head_size, heads):
    message_refs = refs[: chunks * frames]
    base_ref, weight_ref, gain_ref, bias_ref = refs[chunks * frames : chunks * frames + 4]
    merged_ref, attended_ref, mid_ref, ffn_ref, log_ref, entropy_ref = refs[chunks * frames + 4 :]
    own, columns = message_refs[0].shape
    half = columns - LANES
    lane, column = iota((LANES, 3 * LANES), 0), iota((LANES, 3 * LANES), 1)
    gather = jnp.logical_and(
        jnp.logical_and(lane // heads // 3 == column // LANES, lane % heads == column % LANES),
        lane < 9 * heads,
    ).astype(BF16)
    expand = head_expand(half, head_size)
    live = iota((own, LANES), 1) < heads
    spread = jnp.zeros((own, LANES), F32)
    for c in range(chunks):
        sources = message_refs[c * frames : (c + 1) * frames]
        stats = [matmul(x[:, half:], gather) for x in sources]
        tops = [x[:, :LANES] for x in stats]
        peak = functools.reduce(jnp.maximum, tops)
        factors = [jnp.exp(t - peak) for t in tops]
        whole = sum(f * x[:, LANES : 2 * LANES] for f, x in zip(factors, stats))
        moment = sum(f * x[:, 2 * LANES :] for f, x in zip(factors, stats))
        whole = jnp.where(live, whole, 1.0)
        log_total = jnp.where(live, peak + jnp.log(whole), 0.0)
        log_ref[c] = log_total
        spread = spread + jnp.where(live, log_total - moment / whole, 0.0)
        merged = jnp.zeros((own, half), F32)
        for x, factor in zip(sources, factors):
            share = jnp.where(live, factor / whole, 0.0)
            wide = jnp.dot(share, expand, precision=HIGHEST, preferred_element_type=F32)
            merged = merged + x[:, :half].astype(F32) * wide
        merged_ref[:, c * half : (c + 1) * half] = merged
        attended_ref[:, c * half : (c + 1) * half] = merged.astype(BF16)
    entropy_ref[...] = jnp.broadcast_to(
        jnp.sum(spread, axis=1, keepdims=True) * (1.0 / HEADS), entropy_ref.shape
    )
    base = jnp.concatenate([base_ref[...]] * items, 0)
    mid = base + matmul(attended_ref[...], weight_ref[...])
    mid_ref[...] = mid
    ffn_ref[...] = layer_norm(mid, gain_ref[...], bias_ref[...]).astype(BF16)


def gelu_parts(x):
    share = 0.5 * (1.0 + lax.erf(x * (0.5**0.5)))
    slope = share + x * jnp.exp(-0.5 * x * x) * ((2.0 * jnp.pi) ** -0.5)
    return x * share, slope


def feed_kernel(*refs, devices):
    row_refs, low_refs = refs[:devices], refs[devices : 2 * devices]
    up_ref, down_ref = refs[2 * devices : 2 * devices + 2]
    plane_ref, plane_low_ref = refs[2 * devices + 2 : 2 * devices + 4]
    grad_refs = refs[2 * devices + 4 : 3 * devices + 4]
    result_refs = refs[3 * devices + 4 :]
    own = row_refs[0].shape[0]
    for d in range(devices):
        plane_ref[d * own : (d + 1) * own, :] = row_refs[d][...]
        plane_low_ref[d * own : (d + 1) * own, :] = low_refs[d][...]
    upward = matmul(plane_ref[...], up_ref[...])
    hidden, slope = gelu_parts(upward)
    grad_up = (slope * transposed_right(plane_low_ref[...], down_ref[...])).astype(BF16)
    grad = transposed_right(grad_up, up_ref[...]).astype(BF16)
    result = matmul(hidden.astype(BF16), down_ref[...]).astype(BF16)
    for d in range(devices):
        grad_refs[d][...] = grad[d * own : (d + 1) * own, :]
        result_refs[d][...] = result[d * own : (d + 1) * own, :]


def feed_grad_kernel(
    plane_ref, plane_low_ref, other_ref, other_low_ref, up_ref, down_ref, down_grad_ref, up_grad_ref,
    total_ref, *, plane_blocks,
):
    step = pl.program_id(0)
    near = step < plane_blocks
    rows = jnp.where(near, plane_ref[...], other_ref[...])
    low = jnp.where(near, plane_low_ref[...], other_low_ref[...])
    hidden, slope = gelu_parts(matmul(rows, up_ref[...]))
    grad_up = (slope * transposed_right(low, down_ref[...])).astype(BF16)
    down_part = transposed_left(hidden.astype(BF16), low)
    up_part = transposed_left(rows, grad_up)

    @pl.when(step == 0)
    def _():
        down_grad_ref[...] = down_part
        total_ref[...] = up_part

    @pl.when(step > 0)
    def _():
        down_grad_ref[...] += down_part
        total_ref[...] += up_part

    @pl.when(step == pl.num_programs(0) - 1)
    def _():
        up_grad_ref[...] = total_ref[...].astype(BF16)


def norm_backward(rows, gain, gradient):
    center = rows - jnp.mean(rows, axis=1, keepdims=True)
    rate = lax.rsqrt(jnp.mean(center * center, axis=1, keepdims=True) + EPSILON)
    unit = center * rate
    scaled = gradient * gain
    inner = scaled - jnp.mean(scaled, axis=1, keepdims=True)
    back = rate * (inner - unit * jnp.mean(scaled * unit, axis=1, keepdims=True))
    return (
        back,
        jnp.sum(gradient * unit, axis=0, keepdims=True),
        jnp.sum(gradient, axis=0, keepdims=True),
    )


def turn_kernel(*refs, devices, items, chunks, head_size, heads):
    part_refs = refs[:devices]
    mid_ref, cotangent_ref, gain_ref, merged_ref, log_ref, weight_ref = refs[
        devices : devices + 6
    ]
    message_ref, branch_ref, base_ref, sums_ref = refs[devices + 6 :]
    own, width = mid_ref.shape
    half = width // chunks
    gradient = total_of([x[...] for x in part_refs])
    back, gain_sum, bias_sum = norm_backward(mid_ref[...], gain_ref[...], gradient)
    grad_mid = cotangent_ref[...] + back
    sums_ref[...] = jnp.zeros(sums_ref.shape, F32)
    sums_ref[0:1, :] = gain_sum
    sums_ref[1:2, :] = bias_sum
    row_total = own // items
    base_ref[...] = total_of(
        [grad_mid[i * row_total : (i + 1) * row_total] for i in range(items)]
    )
    branch = grad_mid.astype(BF16)
    branch_ref[...] = branch
    grad_att = transposed_right(branch, weight_ref[...]).astype(BF16)
    expand = head_expand(half, head_size)
    lane, column = iota((6 * LANES, LANES), 0), iota((6 * LANES, LANES), 1)
    place = jnp.logical_and(
        lane % LANES < heads, column == (lane // LANES) * heads + lane % LANES
    ).astype(BF16)
    message_ref[:, :width] = grad_att
    for c in range(chunks):
        columns = slice(c * half, (c + 1) * half)
        delta = lax.dot_general(
            merged_ref[:, columns] * grad_att[:, columns].astype(F32),
            expand,
            (((1,), (1,)), ((), ())),
            precision=HIGHEST,
            preferred_element_type=F32,
        )
        terms = jnp.concatenate([t for x in (log_ref[c], delta) for t in split_terms(x)], 1)
        message_ref[:, width + c * LANES : width + (c + 1) * LANES] = matmul(
            terms, place
        ).astype(BF16)


def backward_kernel(
    *refs, frames, items, patches, scale, head_size, heads,
):
    flag_ref, both_ref, query_ref, top_ref = refs[:4]
    grad_refs = refs[4 : 4 + frames]
    mark_refs = refs[4 + frames : 4 + 2 * frames]
    out_ref, sum_ref, held_ref, note_ref = refs[4 + 2 * frames :]
    lats, width = query_ref.shape
    own = grad_refs[0].shape[0]
    row_total = own // items
    base = items * patches
    for s in range(frames):
        source = lax.rem(flag_ref[items + 1] + (frames - s), frames)
        rows = pl.ds(pl.multiple_of(source * row_total, row_total), row_total)
        block = grad_refs[s][...].astype(F32)
        mark = mark_refs[s][...].astype(F32)
        for i in range(items):
            held_ref[i, rows, :] = block[i * row_total : (i + 1) * row_total]
            note_ref[i, rows, :] = mark[i * row_total : (i + 1) * row_total]
    masks = head_masks(lats, width, head_size)
    queries = spread_heads(query_ref[...].astype(F32), masks).astype(BF16)
    lat_both = both_ref[base : base + lats, :]
    row, lane = iota((GROUP * 8, LANES), 0), iota((GROUP * 8, LANES), 1)
    pick = jnp.logical_and(
        jnp.logical_and(
            lane // heads // 3 == row % 8,
            lane % heads == pl.program_id(0) * GROUP + row // 8,
        ),
        lane < 6 * heads,
    ).astype(BF16)
    grad_query = jnp.zeros((queries.shape[0], width), F32)
    lat_grad_key = jnp.zeros((lats, width), F32)
    lat_grad_value = jnp.zeros((lats, width), F32)
    for i in range(items):
        rows = slice(i * patches, (i + 1) * patches)
        stats = transposed_right(pick, note_ref[i].astype(BF16))
        stats = jnp.concatenate([stats[h * 8 : (h + 1) * 8] for h in range(GROUP)], 1)
        log_total = stats[0:1]
        delta = stats[1:2]
        top = top_ref[0, i, 0:1, :]
        rescale = jnp.exp(top - log_total)
        both = jnp.concatenate([both_ref[rows, :], lat_both], 0)
        keys, values = both[:, :width], both[:, width:]
        grads = spread_heads(held_ref[i], masks).astype(BF16)
        live = live_rows(flag_ref, i, items, patches, lats, queries.shape[0])
        masked = jnp.where(live, scale * transposed_right(keys, queries), MASKED)
        probs = jnp.where(live, jnp.exp(masked - log_total), 0.0)
        block_exp = jnp.where(live, jnp.exp(masked - top), 0.0)
        weights = (block_exp.astype(BF16).astype(F32) * rescale).astype(BF16)
        grad_scores = (probs * (transposed_right(values, grads) - delta)).astype(BF16)
        grad_key = scale * matmul(grad_scores, queries)
        grad_value = matmul(weights, grads)
        out_ref[rows, :width] = grad_key[:patches].astype(BF16)
        out_ref[rows, width:] = grad_value[:patches].astype(BF16)
        grad_query = grad_query + transposed_left(grad_scores, keys)
        lat_grad_key = lat_grad_key + grad_key[patches:]
        lat_grad_value = lat_grad_value + grad_value[patches:]
    out_ref[base : base + lats, :width] = lat_grad_key.astype(BF16)
    out_ref[base : base + lats, width:] = lat_grad_value.astype(BF16)
    sum_ref[...] = scale * collect_heads(grad_query, masks)


def media_kernel(flag_ref, *refs, chunks, items, frames, together):
    grad_refs = refs[:chunks]
    weight_ref, media_ref, time_ref, gain_ref, out_ref, sums_ref = refs[chunks:]
    step = pl.program_id(0)
    span = weight_ref.shape[1] // chunks
    patches = media_ref.shape[0] // together
    gradient = transposed_right(grad_refs[0][...], weight_ref[:, :span])
    for c in range(1, chunks):
        gradient = gradient + transposed_right(
            grad_refs[c][...], weight_ref[:, c * span : (c + 1) * span]
        )

    @pl.when(step == 0)
    def _():
        sums_ref[...] = jnp.zeros(sums_ref.shape, F32)

    for k in range(together):
        item = step * together + k
        rows = slice(k * patches, (k + 1) * patches)
        inputs = media_ref[rows, :].astype(F32) + time_ref[pl.ds(item, 1), :]
        back, gain_sum, bias_sum = norm_backward(inputs, gain_ref[...], gradient[rows])
        out_ref[rows, :] = back.astype(BF16)
        place = iota((frames, 1), 0) == flag_ref[items + 2 + item]
        sums_ref[0:frames, :] += jnp.where(place, jnp.sum(back, axis=0, keepdims=True), 0.0)
        sums_ref[8:9, :] += gain_sum
        sums_ref[9:10, :] += bias_sum


def latent_kernel(
    flag_ref, *refs, chunks, items,
):
    grad_refs = refs[:chunks]
    query_refs = refs[chunks : 2 * chunks]
    (
        weight_ref, query_weight_ref, latent_ref, gain_ref, base_ref, ffn_ref, media_ref, out_ref,
    ) = refs[2 * chunks :]
    lats, width = latent_ref.shape
    span = weight_ref.shape[1] // chunks
    half = width // chunks
    gradient = jnp.zeros((lats, width), F32)
    for c in range(chunks):
        gradient = gradient + transposed_right(
            grad_refs[c][...], weight_ref[:, c * span : (c + 1) * span]
        )
        gradient = gradient + transposed_right(
            query_refs[c][...].astype(BF16), query_weight_ref[:, c * half : (c + 1) * half]
        )
        out_ref[lats : 2 * lats, c * half : (c + 1) * half] = query_refs[c][...]
    back, gain_sum, bias_sum = norm_backward(latent_ref[...], gain_ref[...], gradient)
    out_ref[:lats, :] = back
    row_total = base_ref.shape[0]
    start = pl.multiple_of(flag_ref[items + 1] * row_total, row_total)
    out_ref[pl.ds(start, row_total), :] += base_ref[...]
    at = 2 * lats
    out_ref[at : at + 16, :] = media_ref[...]
    out_ref[at + 16 : at + 24, :] = ffn_ref[...]
    out_ref[at + 18 : at + 19, :] = gain_sum
    out_ref[at + 19 : at + 20, :] = bias_sum
    out_ref[at + 24 :, :] = jnp.zeros((out_ref.shape[0] - at - 24, width), F32)


def place_kernel(flag_ref, *refs, chunks, frames, items, groups):
    chunk_refs = refs[: chunks * frames]
    more_refs = refs[chunks * frames : (chunks + 1) * frames]
    key_ref, value_ref, out_ref = refs[(chunks + 1) * frames :]
    width = key_ref.shape[2] // (chunks * groups)
    for s in range(frames):
        source = lax.rem(flag_ref[items + 1] + (frames - s), frames)
        out_ref[source] = more_refs[s][...].astype(F32)
        for c in range(chunks):
            for g in range(groups):
                at = (c * groups + g) * width
                block = chunk_refs[c * frames + s][:, 2 * g * width : 2 * (g + 1) * width]
                block = block.astype(F32)
                key_ref[source, :, at : at + width] = block[:, :width]
                value_ref[source, :, at : at + width] = block[:, width:]


def body(
    media,
    cotangent,
    frame_count,
    frame_start,
    latents,
    time_embed,
    media_gain,
    media_bias,
    latent_gain,
    latent_bias,
    ffn_gain,
    ffn_bias,
    query_weight,
    key_weight,
    value_weight,
    out_weight,
    up_weight,
    down_weight,
):
    items = media.shape[0]
    patches = media.shape[2]
    width = media.shape[3]
    lats = latents.shape[0]
    frame_total = time_embed.shape[0]
    row_total = cotangent.shape[1]
    own = items * row_total
    head_size = width // HEADS
    half = width // CHUNKS
    chunk_heads = HEADS // CHUNKS
    group_width = GROUP * head_size
    groups = chunk_heads // GROUP
    stack = GROUP * lats
    tokens = items * patches
    all_tokens = tokens + lats
    shard = query_weight.shape[0]
    hidden_shard = down_weight.shape[0]
    item_size = lax.axis_size("items")
    frame_size = lax.axis_size("frames")
    plane = item_size * own
    item_index = lax.axis_index("items")
    slot = lax.axis_index("frames")
    row_base = slot * row_total
    params = pltpu.CompilerParams(vmem_limit_bytes=56 * 2**20)
    smem = pl.BlockSpec(memory_space=pltpu.SMEM)
    whole = pl.BlockSpec(memory_space=pltpu.VMEM)
    sizes = dict(items=items, head_size=head_size, heads=chunk_heads)

    def struct(shape, kind):
        return jax.ShapeDtypeStruct(shape, kind)

    short = pl.CostEstimate(flops=1000, bytes_accessed=1000, transcendentals=0)

    kv_full = lax.all_gather(
        jnp.concatenate(
            [
                w[:, g * group_width : (g + 1) * group_width]
                for g in range(HEADS // GROUP)
                for w in (key_weight, value_weight)
            ],
            1,
        ),
        "items",
        axis=0,
        tiled=True,
    )

    lat_norm = layer_norm(latents, latent_gain, latent_bias).astype(BF16)
    lat_cols = lax.dynamic_slice_in_dim(lat_norm, item_index * shard, shard, 1)
    query_part = matmul(lat_cols, query_weight)
    distance = 1
    while distance < item_size:
        query_part = query_part + send_across(query_part, "items", distance)
        distance *= 2
    queries = query_part.astype(BF16)

    counts = lax.dynamic_slice_in_dim(frame_count, item_index * items, items)
    starts = lax.dynamic_slice_in_dim(frame_start, item_index * items, items)
    offset = (slot - starts) % frame_total
    flags = jnp.concatenate(
        [
            (offset < counts).astype(jnp.int32),
            (slot == 0).astype(jnp.int32)[None],
            slot.astype(jnp.int32)[None],
            offset.astype(jnp.int32),
        ]
    )
    picker = (offset[:, None] == jnp.arange(frame_total, dtype=jnp.int32)[None, :]).astype(F32)
    time_rows = jnp.dot(picker, time_embed, precision=HIGHEST, preferred_element_type=F32)
    flat_media = media.reshape(tokens, width)
    steps = tokens // lats
    all_rows = pl.pallas_call(
        functools.partial(norm_kernel, steps=steps, per_item=patches // lats),
        grid=(steps + 1,),
        in_specs=[
            pl.BlockSpec((lats, width), lambda i: (jnp.minimum(i, steps - 1), 0)),
            whole,
            whole,
            whole,
            whole,
        ],
        out_specs=pl.BlockSpec((lats, width), lambda i: (i, 0)),
        out_shape=struct((all_tokens, width), BF16),
        cost_estimate=short,
        compiler_params=params,
    )(flat_media, time_rows, media_gain[None], media_bias[None], lat_norm)

    grad_out = cotangent.reshape(own, width)
    grad_low = grad_out.astype(BF16)
    low_shift = jnp.stack(spread_on(grad_low, "frames")[1:])
    out_full = lax.all_gather(after(out_weight, all_rows), "items", axis=0, tiled=True)

    boths, tops, messages = [], [], []
    for c in range(CHUNKS):

        def block_of(g, c=c):
            return (0, c * groups + g)

        both, top, *parts = pl.pallas_call(
            functools.partial(
                forward_kernel, patches=patches, scale=head_size**-0.5, **sizes
            ),
            grid=(groups,),
            in_specs=[
                smem,
                pl.BlockSpec((all_tokens, width), lambda g: (0, 0)),
                pl.BlockSpec((width, 2 * group_width), block_of),
                pl.BlockSpec((lats, group_width), block_of),
            ],
            out_specs=[
                pl.BlockSpec((all_tokens, 2 * group_width), lambda g: (0, g)),
                pl.BlockSpec((1, items, 8, stack), lambda g: (g, 0, 0, 0)),
            ]
            + [pl.BlockSpec((own, half + LANES), lambda g: (0, 0))] * frame_size,
            out_shape=[
                struct((all_tokens, 2 * half), BF16),
                struct((groups, items, 8, stack), F32),
            ]
            + [struct((own, half + LANES), BF16)] * frame_size,
            scratch_shapes=[
                pltpu.VMEM((items, lats, group_width), F32),
                pltpu.VMEM((items, lats, LANES), F32),
            ],
            cost_estimate=short,
            compiler_params=params,
        )(flags, all_rows, kv_full, queries)
        boths.append(both)
        tops.append(top)
        messages += [p if s == 0 else send_on(p, "frames", s) for s, p in enumerate(parts)]
    up_slice = lax.all_to_all(after(up_weight, boths[0]), "items", 1, 0, tiled=True)
    low_other = lax.all_gather(after(low_shift, boths[0]), "items", axis=0).reshape(-1, width)
    low_blocks = spread_across(after(grad_low, boths[0]), "items")

    base_rows = lax.dynamic_slice_in_dim(latents, row_base, row_total, 0)
    merged, attended, mid_rows, ffn_in, logs, entropy_wide = pl.pallas_call(
        functools.partial(merge_kernel, chunks=CHUNKS, frames=frame_size, **sizes),
        out_shape=[
            struct((own, width), F32),
            struct((own, width), BF16),
            struct((own, width), F32),
            struct((own, width), BF16),
            struct((CHUNKS, own, LANES), F32),
            struct((own, LANES), F32),
        ],
        cost_estimate=short,
        compiler_params=params,
    )(*messages, base_rows, out_full, ffn_gain[None], ffn_bias[None])
    entropy = entropy_wide[:, 0].reshape(items, row_total)

    ffn_blocks = spread_across(ffn_in, "items")
    ffn_plane, low_plane, *parts = pl.pallas_call(
        functools.partial(feed_kernel, devices=item_size),
        out_shape=[struct((plane, width), BF16)] * 2 + [struct((own, width), BF16)] * (2 * item_size),
        cost_estimate=short,
        compiler_params=params,
    )(*ffn_blocks, *low_blocks, up_slice, down_weight)
    ffn_shift = jnp.stack(spread_on(after(ffn_in, parts[0]), "frames")[1:])
    ffn_other = lax.all_gather(ffn_shift, "items", axis=0)
    query_full = lax.all_gather(after(query_weight, ffn_shift), "items", axis=0, tiled=True)
    grad_blocks = collect_across(parts[:item_size], "items")

    turn, grad_branch, grad_base, ffn_sums = pl.pallas_call(
        functools.partial(turn_kernel, devices=item_size, chunks=CHUNKS, **sizes),
        out_shape=[
            struct((own, width + CHUNKS * LANES), BF16),
            struct((own, width), BF16),
            struct((row_total, width), F32),
            struct((8, width), F32),
        ],
        cost_estimate=short,
        compiler_params=params,
    )(*grad_blocks, mid_rows, grad_out, ffn_gain[None], merged, logs, out_full)
    turns = spread_on(turn, "frames")

    chip, core = item_index // 2, item_index % 2
    chunk_grads, chunk_queries, terms, swapped, kv_chunks = [], [], [], [], []
    for c in range(CHUNKS):

        def block_of(g, c=c):
            return (0, c * groups + g)

        chunk_grad, chunk_query = pl.pallas_call(
            functools.partial(
                backward_kernel, frames=frame_size, patches=patches, scale=head_size**-0.5, **sizes
            ),
            grid=(groups,),
            in_specs=[
                smem,
                pl.BlockSpec((all_tokens, 2 * group_width), lambda g: (0, g)),
                pl.BlockSpec((lats, group_width), block_of),
                pl.BlockSpec((1, items, 8, stack), lambda g: (g, 0, 0, 0)),
            ]
            + [pl.BlockSpec((own, group_width), block_of)] * frame_size
            + [pl.BlockSpec((own, LANES), lambda g, c=c: (0, width // LANES + c))] * frame_size,
            out_specs=[
                pl.BlockSpec((all_tokens, 2 * group_width), lambda g: (0, g)),
                pl.BlockSpec((lats, group_width), lambda g: (0, g)),
            ],
            out_shape=[
                struct((all_tokens, 2 * half), BF16),
                struct((lats, half), F32),
            ],
            scratch_shapes=[
                pltpu.VMEM((items, lats, group_width), F32),
                pltpu.VMEM((items, lats, LANES), F32),
            ],
            cost_estimate=short,
            compiler_params=params,
        )(flags, after(boths[c], *terms), queries, tops[c], *turns, *turns)
        term = transposed_left(all_rows, chunk_grad).astype(BF16)
        blocks = term.reshape(item_size // 2, 2, shard, 2 * half)

        def block(k, which):
            return lax.dynamic_slice(
                blocks, (chip ^ k, which, 0, 0), (1, 1, shard, 2 * half)
            ).reshape(shard, 2 * half)

        received = send_across(
            jnp.stack([block(k, 1 - core) for k in range(item_size // 2)]), "items", 1
        )
        swapped.append(received)
        pieces = []
        for k in range(item_size // 2):
            piece = block(k, core).astype(F32) + received[k].astype(F32)
            pieces.append(send_across(piece.astype(BF16), "items", 2 * k) if k else piece)
        kv_chunks.append(total_of(pieces))
        chunk_grads.append(chunk_grad)
        chunk_queries.append(chunk_query)
        terms.append(term)

    together = 2
    media_grad, media_sums = pl.pallas_call(
        functools.partial(
            media_kernel, chunks=CHUNKS, items=items, frames=frame_total, together=together
        ),
        grid=(items // together,),
        in_specs=[smem]
        + [pl.BlockSpec((together * patches, 2 * half), lambda i: (i, 0))] * CHUNKS
        + [
            whole,
            pl.BlockSpec((together * patches, width), lambda i: (i, 0)),
            whole,
            whole,
        ],
        out_specs=[
            pl.BlockSpec((together * patches, width), lambda i: (i, 0)),
            pl.BlockSpec((16, width), lambda i: (0, 0)),
        ],
        out_shape=[struct((tokens, width), BF16), struct((16, width), F32)],
        cost_estimate=short,
        compiler_params=params,
    )(
        flags,
        *[after(g, terms[-1], swapped[0]) for g in chunk_grads],
        kv_full,
        flat_media,
        time_rows,
        media_gain[None],
    )

    sum_rows = 2 * lats + 24
    sum_rows += -sum_rows % (8 * item_size)
    last_block = pl.BlockSpec((lats, 2 * half), lambda i: (tokens // lats, 0))
    payload = pl.pallas_call(
        functools.partial(latent_kernel, chunks=CHUNKS, items=items),
        grid=(1,),
        in_specs=[smem] + [last_block] * CHUNKS + [whole] * (CHUNKS + 7),
        out_specs=whole,
        out_shape=struct((sum_rows, width), F32),
        cost_estimate=short,
        compiler_params=params,
    )(
        flags,
        *chunk_grads,
        *chunk_queries,
        kv_full,
        query_full,
        latents,
        latent_gain[None],
        grad_base,
        ffn_sums,
        media_sums,
    )
    payload_part = lax.psum_scatter(payload, "items", scatter_dimension=0, tiled=True)
    sums = lax.all_gather(
        total_of(spread_on(payload_part, "frames")), "items", axis=0, tiled=True
    )
    latents_grad = sums[:lats]
    query_grad = transposed_left(lat_cols, sums[lats : 2 * lats].astype(BF16))
    at = 2 * lats
    column_sums = lax.dynamic_slice_in_dim(sums[at : at + 16], item_index * shard, shard, 1)

    result = mid_rows + total_of(
        collect_across([after(p, terms[-1]) for p in parts[item_size:]], "items")
    )

    branch_plane = lax.all_gather(grad_branch, "items", axis=0, tiled=True)
    ffn_other = after(ffn_other.reshape(-1, width), payload, swapped[-1])
    block_rows = min(512, plane)
    plane_blocks = plane // block_rows
    near = pl.BlockSpec((block_rows, width), lambda i: (jnp.minimum(i, plane_blocks - 1), 0))
    far = pl.BlockSpec((block_rows, width), lambda i: (jnp.maximum(i - plane_blocks, 0), 0))
    down_grad, up_part = pl.pallas_call(
        functools.partial(feed_grad_kernel, plane_blocks=plane_blocks),
        grid=(plane_blocks * frame_size,),
        in_specs=[near, near, far, far, whole, whole],
        out_specs=[
            pl.BlockSpec((hidden_shard, width), lambda i: (0, 0)),
            pl.BlockSpec((width, hidden_shard), lambda i: (0, 0)),
        ],
        out_shape=[struct((hidden_shard, width), F32), struct((width, hidden_shard), BF16)],
        scratch_shapes=[pltpu.VMEM((width, hidden_shard), F32)],
        cost_estimate=short,
        compiler_params=params,
    )(ffn_plane, low_plane, ffn_other, low_other, up_slice, down_weight)
    up_grad = lax.all_to_all(up_part, "items", 0, 1, tiled=True).astype(F32)

    att_plane = lax.all_to_all(after(attended, terms[0]), "items", 1, 0, tiled=True)
    out_part = transposed_left(att_plane, branch_plane)

    placed = []
    for k in kv_chunks + [out_part]:
        placed += reduce_rows(k, "frames")
    key_grad, value_grad, out_grad = pl.pallas_call(
        functools.partial(
            place_kernel, chunks=CHUNKS, frames=frame_size, items=items, groups=groups
        ),
        in_specs=[smem] + [whole] * len(placed),
        out_specs=[whole] * 3,
        out_shape=[struct((frame_size, shard // frame_size, width), F32)] * 3,
        cost_estimate=short,
        compiler_params=params,
    )(flags, *placed)
    return (
        result.reshape(items, row_total, width),
        entropy,
        media_grad.reshape(media.shape),
        latents_grad,
        column_sums[:frame_total],
        column_sums[8],
        column_sums[9],
        sums[at + 18],
        sums[at + 19],
        sums[at + 16],
        sums[at + 17],
        query_grad,
        key_grad.reshape(shard, width),
        value_grad.reshape(shard, width),
        out_grad.reshape(shard, width),
        up_grad,
        down_grad,
    )


def solution(mesh):
    return jax.shard_map(
        body,
        mesh=mesh,
        in_specs=(
            P("items", "frames", None, None),
            P("items", "frames", None),
            P(),
            P(),
            P(),
            P(),
            P(),
            P(),
            P(),
            P(),
            P(),
            P(),
            P("items", None),
            P("items", None),
            P("items", None),
            P("items", None),
            P("items", None),
            P("items", None),
        ),
        out_specs=(
            P("items", "frames", None),
            P("items", "frames"),
            P("items", "frames", None, None),
            P(),
            P(None, "items"),
            P("items"),
            P("items"),
            P(),
            P(),
            P(),
            P(),
            P("items", None),
            P("items", None),
            P("items", None),
            P("items", None),
            P("items", None),
            P("items", None),
        ),
        check_vma=False,
    )
```

```python
import functools

import jax
import jax.numpy as jnp
from jax import lax
from jax.experimental import pallas as pl
from jax.experimental.pallas import tpu as pltpu
from jax.sharding import PartitionSpec as P

HEADS = 16
GROUP = 4
CHUNKS = 2
LANES = 128
EPSILON = 1e-05
MASKED = -1e30
F32 = jnp.float32
BF16 = jnp.bfloat16
HIGHEST = lax.Precision.HIGHEST


def layer_norm(inputs, norm_gain, norm_bias):
    center = inputs - jnp.mean(inputs, axis=-1, keepdims=True)
    spread = jnp.mean(center * center, axis=-1, keepdims=True)
    return center * lax.rsqrt(spread + EPSILON) * norm_gain + norm_bias


def matmul(left_side, right_side):
    return jnp.dot(left_side, right_side, preferred_element_type=F32)


def transposed_left(left_side, right_side):
    return lax.dot_general(
        left_side, right_side, (((0,), (0,)), ((), ())), preferred_element_type=F32
    )


def transposed_right(left_side, right_side):
    return lax.dot_general(
        left_side, right_side, (((1,), (1,)), ((), ())), preferred_element_type=F32
    )


def send_on(x, axis, step):
    size = lax.axis_size(axis)
    return lax.ppermute(x, axis, [(i, (i + step) % size) for i in range(size)])


def send_across(x, axis, distance):
    return lax.ppermute(x, axis, [(i, i ^ distance) for i in range(lax.axis_size(axis))])


def spread_on(x, axis):
    return [x] + [send_on(x, axis, s) for s in range(1, lax.axis_size(axis))]


def spread_across(x, axis):
    return [x] + [send_across(x, axis, d) for d in range(1, lax.axis_size(axis))]


def collect_across(pieces, axis):
    return [pieces[0]] + [send_across(p, axis, d) for d, p in enumerate(pieces) if d]


def total_of(pieces):
    return functools.reduce(jnp.add, [p.astype(F32) for p in pieces])


def scatter_rows(x, axis):
    size = lax.axis_size(axis)
    me = lax.axis_index(axis)
    rows = x.shape[0] // size
    out = []
    for s in range(size):
        piece = lax.dynamic_slice_in_dim(x, ((me + s) % size) * rows, rows, 0)
        out.append(send_on(piece.astype(BF16), axis, s) if s else piece)
    return out


def after(x, *earlier):
    return lax.optimization_barrier((x,) + earlier)[0]


def split_terms(x):
    high = x.astype(BF16)
    rest = x - high.astype(F32)
    middle = rest.astype(BF16)
    return high, middle, (rest - middle.astype(F32)).astype(BF16)


def iota(shape, dim):
    return lax.broadcasted_iota(jnp.int32, shape, dim)


def head_masks(rows, width, head_size):
    lane = iota((rows, width), 1)
    return [
        jnp.logical_and(lane >= h * head_size, lane < (h + 1) * head_size)
        for h in range(width // head_size)
    ]


def spread_heads(block, masks):
    return jnp.concatenate([jnp.where(m, block, jnp.zeros_like(block)) for m in masks], 0)


def collect_heads(block, masks):
    rows = block.shape[0] // len(masks)
    total = jnp.where(masks[0], block[:rows], 0.0)
    for h in range(1, len(masks)):
        total = total + jnp.where(masks[h], block[h * rows : (h + 1) * rows], 0.0)
    return total


def head_expand(width, head_size):
    row, column = iota((LANES, width), 0), iota((LANES, width), 1)
    return jnp.logical_and(column >= row * head_size, column < (row + 1) * head_size).astype(F32)


def live_rows(flag_ref, item, items, patches, lats, columns):
    row = iota((patches + lats, columns), 0)
    media = jnp.logical_and(row < patches, flag_ref[item] > 0)
    return jnp.logical_or(media, jnp.logical_and(row >= patches, flag_ref[items] > 0))


def norm_kernel(media_ref, time_ref, gain_ref, bias_ref, lat_ref, out_ref, *, steps, per_item):
    step = pl.program_id(0)

    @pl.when(step < steps)
    def _():
        rows = media_ref[...].astype(F32) + time_ref[pl.ds(step // per_item, 1), :]
        out_ref[...] = layer_norm(rows, gain_ref[...], bias_ref[...]).astype(BF16)

    @pl.when(step == steps)
    def _():
        out_ref[...] = lat_ref[...]


def forward_kernel(
    flag_ref, both_ref, query_ref, top_ref, *refs, items, patches, scale, head_size, heads,
):
    message_refs, (part_ref, mark_ref) = refs[:-2], refs[-2:]
    lats, width = query_ref.shape
    frames = len(message_refs)
    own = message_refs[0].shape[0]
    row_total = own // items
    masks = head_masks(lats, width, head_size)
    queries = spread_heads(query_ref[...].astype(F32), masks).astype(BF16)
    base = items * patches
    lat_both = both_ref[base : base + lats, :]
    group = pl.program_id(0)
    term, lane = iota((16, GROUP * LANES), 0), iota((16, GROUP * LANES), 1)
    place = jnp.logical_and(
        lane % LANES == term * heads + group * GROUP + lane // LANES, term < 9
    ).astype(BF16)
    for i in range(items):
        both = jnp.concatenate([both_ref[i * patches : (i + 1) * patches, :], lat_both], 0)
        live = live_rows(flag_ref, i, items, patches, lats, queries.shape[0])
        scores = scale * transposed_right(both[:, :width], queries)
        masked = jnp.where(live, scores, MASKED)
        top = jnp.max(masked, axis=0, keepdims=True)
        block_exp = jnp.where(live, jnp.exp(masked - top), 0.0)
        total = jnp.sum(block_exp, axis=0, keepdims=True)
        moment = jnp.sum(block_exp * scores, axis=0, keepdims=True)
        part = transposed_left(block_exp.astype(BF16), both[:, width:])
        part_ref[i] = collect_heads(part, masks)
        top_ref[0, i] = jnp.broadcast_to(top, top_ref.shape[2:])
        terms = jnp.concatenate(
            [t.astype(F32) for x in (top, total, moment) for t in split_terms(x)]
            + [jnp.zeros((7, top.shape[1]), F32)],
            0,
        ).astype(BF16)
        wide = transposed_left(terms, place)
        mark = wide[:lats, :LANES]
        for h in range(1, GROUP):
            mark = mark + wide[h * lats : (h + 1) * lats, h * LANES : (h + 1) * LANES]
        mark_ref[i] = mark

    end = message_refs[0].shape[1] - LANES
    for s, message_ref in enumerate(message_refs):
        start = pl.multiple_of(lax.rem(flag_ref[items + 1] + s, frames) * row_total, row_total)
        rows = pl.ds(start, row_total)
        block = jnp.concatenate([part_ref[i, rows, :] for i in range(items)], 0).astype(BF16)
        mark = jnp.concatenate([mark_ref[i, rows, :] for i in range(items)], 0).astype(BF16)
        for g in range(end // width):

            @pl.when(group == g)
            def _():
                message_ref[:, g * width : (g + 1) * width] = block
                if g == 0:
                    message_ref[:, end:] = mark
                else:
                    message_ref[:, end:] = message_ref[:, end:] + mark


def merge_kernel(*refs, chunks, frames, items, head_size, heads):
    message_refs = refs[: chunks * frames]
    base_ref, weight_ref, gain_ref, bias_ref = refs[chunks * frames : chunks * frames + 4]
    merged_ref, attended_ref, mid_ref, ffn_ref, log_ref, entropy_ref = refs[chunks * frames + 4 :]
    own, columns = message_refs[0].shape
    half = columns - LANES
    lane, column = iota((LANES, 3 * LANES), 0), iota((LANES, 3 * LANES), 1)
    gather = jnp.logical_and(
        jnp.logical_and(lane // heads // 3 == column // LANES, lane % heads == column % LANES),
        lane < 9 * heads,
    ).astype(BF16)
    expand = head_expand(half, head_size)
    live = iota((own, LANES), 1) < heads
    spread = jnp.zeros((own, LANES), F32)
    for c in range(chunks):
        sources = message_refs[c * frames : (c + 1) * frames]
        stats = [matmul(x[:, half:], gather) for x in sources]
        tops = [x[:, :LANES] for x in stats]
        peak = functools.reduce(jnp.maximum, tops)
        factors = [jnp.exp(t - peak) for t in tops]
        whole = sum(f * x[:, LANES : 2 * LANES] for f, x in zip(factors, stats))
        moment = sum(f * x[:, 2 * LANES :] for f, x in zip(factors, stats))
        whole = jnp.where(live, whole, 1.0)
        log_total = jnp.where(live, peak + jnp.log(whole), 0.0)
        log_ref[c] = log_total
        spread = spread + jnp.where(live, log_total - moment / whole, 0.0)
        merged = jnp.zeros((own, half), F32)
        for x, factor in zip(sources, factors):
            share = jnp.where(live, factor / whole, 0.0)
            wide = jnp.dot(share, expand, precision=HIGHEST, preferred_element_type=F32)
            merged = merged + x[:, :half].astype(F32) * wide
        merged_ref[:, c * half : (c + 1) * half] = merged
        attended_ref[:, c * half : (c + 1) * half] = merged.astype(BF16)
    entropy_ref[...] = jnp.broadcast_to(
        jnp.sum(spread, axis=1, keepdims=True) * (1.0 / HEADS), entropy_ref.shape
    )
    base = jnp.concatenate([base_ref[...]] * items, 0)
    mid = base + matmul(attended_ref[...], weight_ref[...])
    mid_ref[...] = mid
    ffn_ref[...] = layer_norm(mid, gain_ref[...], bias_ref[...]).astype(BF16)


def gelu_parts(x):
    share = 0.5 * (1.0 + lax.erf(x * (0.5**0.5)))
    slope = share + x * jnp.exp(-0.5 * x * x) * ((2.0 * jnp.pi) ** -0.5)
    return x * share, slope


def feed_kernel(flag_ref, *refs, devices, items):
    row_refs = refs[:devices]
    low_ref, up_ref, down_ref, plane_ref, plane_low_ref, result_ref = refs[devices : devices + 6]
    grad_refs = refs[devices + 6 :]
    own = row_refs[0].shape[0]
    me = flag_ref[2 * items + 2]
    for d in range(devices):
        plane_ref[d * own : (d + 1) * own, :] = row_refs[d][...]
        plane_low_ref[d * own : (d + 1) * own, :] = low_ref[jnp.bitwise_xor(me, d)]
    upward = matmul(plane_ref[...], up_ref[...])
    hidden, slope = gelu_parts(upward)
    grad_up = (slope * transposed_right(plane_low_ref[...], down_ref[...])).astype(BF16)
    grad = transposed_right(grad_up, up_ref[...]).astype(BF16)
    result = matmul(hidden.astype(BF16), down_ref[...]).astype(BF16)
    for d in range(devices):
        grad_refs[d][...] = grad[d * own : (d + 1) * own, :]
        result_ref[jnp.bitwise_xor(me, d)] = result[d * own : (d + 1) * own, :]


def feed_grad_kernel(
    plane_ref, plane_low_ref, other_ref, other_low_ref, up_ref, down_ref, hidden_ref, up_grad_ref,
    total_ref, *, plane_blocks,
):
    step = pl.program_id(0)
    near = step < plane_blocks
    rows = jnp.where(near, plane_ref[...], other_ref[...])
    low = jnp.where(near, plane_low_ref[...], other_low_ref[...])
    hidden, slope = gelu_parts(matmul(rows, up_ref[...]))
    hidden_ref[...] = hidden.astype(BF16)
    grad_up = (slope * transposed_right(low, down_ref[...])).astype(BF16)
    up_part = transposed_left(rows, grad_up)

    @pl.when(step == 0)
    def _():
        total_ref[...] = up_part

    @pl.when(step > 0)
    def _():
        total_ref[...] += up_part

    @pl.when(step == pl.num_programs(0) - 1)
    def _():
        up_grad_ref[...] = total_ref[...].astype(BF16)


def norm_backward(rows, gain, gradient):
    center = rows - jnp.mean(rows, axis=1, keepdims=True)
    rate = lax.rsqrt(jnp.mean(center * center, axis=1, keepdims=True) + EPSILON)
    unit = center * rate
    scaled = gradient * gain
    inner = scaled - jnp.mean(scaled, axis=1, keepdims=True)
    back = rate * (inner - unit * jnp.mean(scaled * unit, axis=1, keepdims=True))
    return (
        back,
        jnp.sum(gradient * unit, axis=0, keepdims=True),
        jnp.sum(gradient, axis=0, keepdims=True),
    )


def turn_kernel(*refs, devices, items, chunks, head_size, heads):
    part_refs = refs[:devices]
    mid_ref, cotangent_ref, gain_ref, merged_ref, log_ref, weight_ref = refs[
        devices : devices + 6
    ]
    message_ref, branch_ref, base_ref, sums_ref = refs[devices + 6 :]
    own, width = mid_ref.shape
    half = width // chunks
    gradient = total_of([x[...] for x in part_refs])
    back, gain_sum, bias_sum = norm_backward(mid_ref[...], gain_ref[...], gradient)
    grad_mid = cotangent_ref[...] + back
    sums_ref[...] = jnp.zeros(sums_ref.shape, F32)
    sums_ref[0:1, :] = gain_sum
    sums_ref[1:2, :] = bias_sum
    row_total = own // items
    base_ref[...] = total_of(
        [grad_mid[i * row_total : (i + 1) * row_total] for i in range(items)]
    )
    branch = grad_mid.astype(BF16)
    branch_ref[...] = branch
    grad_att = transposed_right(branch, weight_ref[...]).astype(BF16)
    expand = head_expand(half, head_size)
    lane, column = iota((6 * LANES, LANES), 0), iota((6 * LANES, LANES), 1)
    place = jnp.logical_and(
        lane % LANES < heads, column == (lane // LANES) * heads + lane % LANES
    ).astype(BF16)
    message_ref[:, :width] = grad_att
    for c in range(chunks):
        columns = slice(c * half, (c + 1) * half)
        delta = lax.dot_general(
            merged_ref[:, columns] * grad_att[:, columns].astype(F32),
            expand,
            (((1,), (1,)), ((), ())),
            precision=HIGHEST,
            preferred_element_type=F32,
        )
        terms = jnp.concatenate([t for x in (log_ref[c], delta) for t in split_terms(x)], 1)
        message_ref[:, width + c * LANES : width + (c + 1) * LANES] = matmul(
            terms, place
        ).astype(BF16)


def backward_kernel(
    *refs, frames, items, patches, scale, head_size, heads,
):
    flag_ref, both_ref, query_ref, top_ref = refs[:4]
    grad_refs = refs[4 : 4 + frames]
    mark_refs = refs[4 + frames : 4 + 2 * frames]
    out_ref, sum_ref, held_ref, note_ref = refs[4 + 2 * frames :]
    lats, width = query_ref.shape
    own = grad_refs[0].shape[0]
    row_total = own // items
    base = items * patches
    for s in range(frames):
        source = lax.rem(flag_ref[items + 1] + (frames - s), frames)
        rows = pl.ds(pl.multiple_of(source * row_total, row_total), row_total)
        block = grad_refs[s][...].astype(F32)
        mark = mark_refs[s][...].astype(F32)
        for i in range(items):
            held_ref[i, rows, :] = block[i * row_total : (i + 1) * row_total]
            note_ref[i, rows, :] = mark[i * row_total : (i + 1) * row_total]
    masks = head_masks(lats, width, head_size)
    queries = spread_heads(query_ref[...].astype(F32), masks).astype(BF16)
    lat_both = both_ref[base : base + lats, :]
    row, lane = iota((GROUP * 8, LANES), 0), iota((GROUP * 8, LANES), 1)
    pick = jnp.logical_and(
        jnp.logical_and(
            lane // heads // 3 == row % 8,
            lane % heads == pl.program_id(0) * GROUP + row // 8,
        ),
        lane < 6 * heads,
    ).astype(BF16)
    grad_query = jnp.zeros((queries.shape[0], width), F32)
    lat_grad_key = jnp.zeros((lats, width), F32)
    lat_grad_value = jnp.zeros((lats, width), F32)
    for i in range(items):
        rows = slice(i * patches, (i + 1) * patches)
        stats = transposed_right(pick, note_ref[i].astype(BF16))
        stats = jnp.concatenate([stats[h * 8 : (h + 1) * 8] for h in range(GROUP)], 1)
        log_total = stats[0:1]
        delta = stats[1:2]
        top = top_ref[0, i, 0:1, :]
        rescale = jnp.exp(top - log_total)
        both = jnp.concatenate([both_ref[rows, :], lat_both], 0)
        keys, values = both[:, :width], both[:, width:]
        grads = spread_heads(held_ref[i], masks).astype(BF16)
        live = live_rows(flag_ref, i, items, patches, lats, queries.shape[0])
        masked = jnp.where(live, scale * transposed_right(keys, queries), MASKED)
        probs = jnp.where(live, jnp.exp(masked - log_total), 0.0)
        block_exp = jnp.where(live, jnp.exp(masked - top), 0.0)
        weights = (block_exp.astype(BF16).astype(F32) * rescale).astype(BF16)
        grad_scores = (probs * (transposed_right(values, grads) - delta)).astype(BF16)
        grad_key = scale * matmul(grad_scores, queries)
        grad_value = matmul(weights, grads)
        out_ref[rows, :width] = grad_key[:patches].astype(BF16)
        out_ref[rows, width:] = grad_value[:patches].astype(BF16)
        grad_query = grad_query + transposed_left(grad_scores, keys)
        lat_grad_key = lat_grad_key + grad_key[patches:]
        lat_grad_value = lat_grad_value + grad_value[patches:]
    out_ref[base : base + lats, :width] = lat_grad_key.astype(BF16)
    out_ref[base : base + lats, width:] = lat_grad_value.astype(BF16)
    sum_ref[...] = scale * collect_heads(grad_query, masks)


def media_kernel(flag_ref, *refs, chunks, items, frames, together):
    grad_refs = refs[:chunks]
    weight_ref, media_ref, time_ref, gain_ref, out_ref, sums_ref = refs[chunks:]
    step = pl.program_id(0)
    span = weight_ref.shape[1] // chunks
    patches = media_ref.shape[0] // together
    gradient = transposed_right(grad_refs[0][...], weight_ref[:, :span])
    for c in range(1, chunks):
        gradient = gradient + transposed_right(
            grad_refs[c][...], weight_ref[:, c * span : (c + 1) * span]
        )

    @pl.when(step == 0)
    def _():
        sums_ref[...] = jnp.zeros(sums_ref.shape, F32)

    for k in range(together):
        item = step * together + k
        rows = slice(k * patches, (k + 1) * patches)
        inputs = media_ref[rows, :].astype(F32) + time_ref[pl.ds(item, 1), :]
        back, gain_sum, bias_sum = norm_backward(inputs, gain_ref[...], gradient[rows])
        out_ref[rows, :] = back.astype(BF16)
        place = iota((frames, 1), 0) == flag_ref[items + 2 + item]
        sums_ref[0:frames, :] += jnp.where(place, jnp.sum(back, axis=0, keepdims=True), 0.0)
        sums_ref[8:9, :] += gain_sum
        sums_ref[9:10, :] += bias_sum


def latent_kernel(
    flag_ref, *refs, chunks, items,
):
    grad_refs = refs[:chunks]
    query_refs = refs[chunks : 2 * chunks]
    (
        weight_ref, query_weight_ref, latent_ref, gain_ref, base_ref, ffn_ref, out_ref,
    ) = refs[2 * chunks :]
    lats, width = latent_ref.shape
    span = weight_ref.shape[1] // chunks
    half = width // chunks
    gradient = jnp.zeros((lats, width), F32)
    for c in range(chunks):
        gradient = gradient + transposed_right(
            grad_refs[c][...], weight_ref[:, c * span : (c + 1) * span]
        )
        gradient = gradient + transposed_right(
            query_refs[c][...].astype(BF16), query_weight_ref[:, c * half : (c + 1) * half]
        )
        out_ref[lats : 2 * lats, c * half : (c + 1) * half] = query_refs[c][...]
    back, gain_sum, bias_sum = norm_backward(latent_ref[...], gain_ref[...], gradient)
    out_ref[:lats, :] = back
    row_total = base_ref.shape[0]
    start = pl.multiple_of(flag_ref[items + 1] * row_total, row_total)
    out_ref[pl.ds(start, row_total), :] += base_ref[...]
    at = 2 * lats
    out_ref[at : at + 8, :] = ffn_ref[...]
    out_ref[at + 2 : at + 3, :] = gain_sum
    out_ref[at + 3 : at + 4, :] = bias_sum
    out_ref[at + 8 :, :] = jnp.zeros((out_ref.shape[0] - at - 8, width), F32)


def place_kernel(flag_ref, *refs, chunks, frames, items, groups):
    chunk_refs = refs[: chunks * frames]
    key_ref, value_ref, out_ref = refs[chunks * frames :]
    width = key_ref.shape[2] // (chunks * groups)
    for s in range(frames):
        source = lax.rem(flag_ref[items + 1] + (frames - s), frames)
        last = chunk_refs[(chunks - 1) * frames + s]
        out_ref[source] = last[:, 2 * groups * width :].astype(F32)
        for c in range(chunks):
            for g in range(groups):
                at = (c * groups + g) * width
                block = chunk_refs[c * frames + s][:, 2 * g * width : 2 * (g + 1) * width]
                block = block.astype(F32)
                key_ref[source, :, at : at + width] = block[:, :width]
                value_ref[source, :, at : at + width] = block[:, width:]


def body(
    media,
    cotangent,
    frame_count,
    frame_start,
    latents,
    time_embed,
    media_gain,
    media_bias,
    latent_gain,
    latent_bias,
    ffn_gain,
    ffn_bias,
    query_weight,
    key_weight,
    value_weight,
    out_weight,
    up_weight,
    down_weight,
):
    items = media.shape[0]
    patches = media.shape[2]
    width = media.shape[3]
    lats = latents.shape[0]
    frame_total = time_embed.shape[0]
    row_total = cotangent.shape[1]
    own = items * row_total
    head_size = width // HEADS
    half = width // CHUNKS
    chunk_heads = HEADS // CHUNKS
    group_width = GROUP * head_size
    groups = chunk_heads // GROUP
    stack = GROUP * lats
    tokens = items * patches
    all_tokens = tokens + lats
    shard = query_weight.shape[0]
    hidden_shard = down_weight.shape[0]
    item_size = lax.axis_size("items")
    frame_size = lax.axis_size("frames")
    plane = item_size * own
    item_index = lax.axis_index("items")
    slot = lax.axis_index("frames")
    row_base = slot * row_total
    params = pltpu.CompilerParams(vmem_limit_bytes=56 * 2**20)
    smem = pl.BlockSpec(memory_space=pltpu.SMEM)
    whole = pl.BlockSpec(memory_space=pltpu.VMEM)
    sizes = dict(items=items, head_size=head_size, heads=chunk_heads)

    def struct(shape, kind):
        return jax.ShapeDtypeStruct(shape, kind)

    short = pl.CostEstimate(flops=1000, bytes_accessed=1000, transcendentals=0)

    kv_full = lax.all_gather(
        jnp.concatenate(
            [
                w[:, g * group_width : (g + 1) * group_width]
                for g in range(HEADS // GROUP)
                for w in (key_weight, value_weight)
            ],
            1,
        ),
        "items",
        axis=0,
        tiled=True,
    )

    lat_norm = layer_norm(latents, latent_gain, latent_bias).astype(BF16)
    lat_cols = lax.dynamic_slice_in_dim(lat_norm, item_index * shard, shard, 1)

    def column_blocks(x):
        return jnp.transpose(x.reshape(-1, item_size, shard), (1, 0, 2))

    def scatter_exchange(x, axis):
        return jnp.sum(lax.all_to_all(x, axis, 0, 0).astype(F32), axis=0)

    query_cols = scatter_exchange(column_blocks(matmul(lat_cols, query_weight)), "items")
    query_cols = jnp.broadcast_to(query_cols.astype(BF16)[None], (item_size, lats, shard))
    queries = jnp.transpose(lax.all_to_all(query_cols, "items", 0, 0), (1, 0, 2)).reshape(
        lats, width
    )

    counts = lax.dynamic_slice_in_dim(frame_count, item_index * items, items)
    starts = lax.dynamic_slice_in_dim(frame_start, item_index * items, items)
    offset = (slot - starts) % frame_total
    flags = jnp.concatenate(
        [
            (offset < counts).astype(jnp.int32),
            (slot == 0).astype(jnp.int32)[None],
            slot.astype(jnp.int32)[None],
            offset.astype(jnp.int32),
            item_index.astype(jnp.int32)[None],
        ]
    )
    picker = (offset[:, None] == jnp.arange(frame_total, dtype=jnp.int32)[None, :]).astype(F32)
    time_rows = jnp.dot(picker, time_embed, precision=HIGHEST, preferred_element_type=F32)
    flat_media = media.reshape(tokens, width)
    steps = tokens // lats
    all_rows = pl.pallas_call(
        functools.partial(norm_kernel, steps=steps, per_item=patches // lats),
        grid=(steps + 1,),
        in_specs=[
            pl.BlockSpec((lats, width), lambda i: (jnp.minimum(i, steps - 1), 0)),
            whole,
            whole,
            whole,
            whole,
        ],
        out_specs=pl.BlockSpec((lats, width), lambda i: (i, 0)),
        out_shape=struct((all_tokens, width), BF16),
        cost_estimate=short,
        compiler_params=params,
    )(flat_media, time_rows, media_gain[None], media_bias[None], lat_norm)

    grad_out = cotangent.reshape(own, width)
    grad_low = grad_out.astype(BF16)
    low_shift = spread_on(grad_low, "frames")[1:]
    out_full = lax.all_gather(after(out_weight, all_rows), "items", axis=0, tiled=True)

    boths, tops, messages = [], [], []
    for c in range(CHUNKS):

        def block_of(g, c=c):
            return (0, c * groups + g)

        rows = after(all_rows, *low_shift) if c == 0 else all_rows
        both = matmul(rows, kv_full[:, 2 * c * half : 2 * (c + 1) * half]).astype(BF16)
        top, *parts = pl.pallas_call(
            functools.partial(
                forward_kernel, patches=patches, scale=head_size**-0.5, **sizes
            ),
            grid=(groups,),
            in_specs=[
                smem,
                pl.BlockSpec((all_tokens, 2 * group_width), lambda g: (0, g)),
                pl.BlockSpec((lats, group_width), block_of),
            ],
            out_specs=[pl.BlockSpec((1, items, 8, stack), lambda g: (g, 0, 0, 0))]
            + [pl.BlockSpec((own, half + LANES), lambda g: (0, 0))] * frame_size,
            out_shape=[struct((groups, items, 8, stack), F32)]
            + [struct((own, half + LANES), BF16)] * frame_size,
            scratch_shapes=[
                pltpu.VMEM((items, lats, group_width), F32),
                pltpu.VMEM((items, lats, LANES), F32),
            ],
            cost_estimate=short,
            compiler_params=params,
        )(flags, both, queries)
        boths.append(both)
        tops.append(top)
        messages += [p if s == 0 else send_on(p, "frames", s) for s, p in enumerate(parts)]
    up_slice = lax.all_to_all(after(up_weight, tops[1]), "items", 1, 0, tiled=True)
    low_every = lax.all_gather(after(grad_low, boths[0]), "items", axis=0)
    low_other = lax.all_gather(
        after(jnp.stack(low_shift), boths[1]), "items", axis=0
    ).reshape(-1, width)

    base_rows = lax.dynamic_slice_in_dim(latents, row_base, row_total, 0)
    merged, attended, mid_rows, ffn_in, logs, entropy_wide = pl.pallas_call(
        functools.partial(merge_kernel, chunks=CHUNKS, frames=frame_size, **sizes),
        out_shape=[
            struct((own, width), F32),
            struct((own, width), BF16),
            struct((own, width), F32),
            struct((own, width), BF16),
            struct((CHUNKS, own, LANES), F32),
            struct((own, LANES), F32),
        ],
        cost_estimate=short,
        compiler_params=params,
    )(*messages, base_rows, out_full, ffn_gain[None], ffn_bias[None])
    entropy = entropy_wide[:, 0].reshape(items, row_total)

    ffn_blocks = spread_across(ffn_in, "items")
    ffn_shift = spread_on(ffn_in, "frames")[1:]
    ffn_plane, low_plane, result_part, *parts = pl.pallas_call(
        functools.partial(feed_kernel, devices=item_size, items=items),
        in_specs=[smem] + [whole] * (item_size + 3),
        out_shape=[struct((plane, width), BF16)] * 2
        + [struct((item_size, own, width), BF16)]
        + [struct((own, width), BF16)] * item_size,
        cost_estimate=short,
        compiler_params=params,
    )(flags, after(ffn_blocks[0], *ffn_shift), *ffn_blocks[1:], low_every, up_slice, down_weight)
    ffn_other = lax.all_gather(jnp.stack(ffn_shift), "items", axis=0).reshape(-1, width)
    query_full = lax.all_gather(after(query_weight, ffn_plane), "items", axis=0, tiled=True)
    grad_blocks = collect_across(parts, "items")
    grad_blocks[0] = after(grad_blocks[0], low_other)

    turn, grad_branch, grad_base, ffn_sums = pl.pallas_call(
        functools.partial(turn_kernel, devices=item_size, chunks=CHUNKS, **sizes),
        out_shape=[
            struct((own, width + CHUNKS * LANES), BF16),
            struct((own, width), BF16),
            struct((row_total, width), F32),
            struct((8, width), F32),
        ],
        cost_estimate=short,
        compiler_params=params,
    )(*grad_blocks, mid_rows, grad_out, ffn_gain[None], merged, logs, out_full)
    turns = spread_on(turn, "frames")

    chip, core = item_index // 2, item_index % 2
    chunk_grads, chunk_queries, blocks, swapped = [], [], [], []

    def block(c, k, which):
        return lax.dynamic_slice(
            blocks[c], (chip ^ k, which, 0, 0), (1, 1, shard, 2 * half)
        ).reshape(shard, 2 * half)

    for c in range(CHUNKS):

        def block_of(g, c=c):
            return (0, c * groups + g)

        chunk_grad, chunk_query = pl.pallas_call(
            functools.partial(
                backward_kernel, frames=frame_size, patches=patches, scale=head_size**-0.5, **sizes
            ),
            grid=(groups,),
            in_specs=[
                smem,
                pl.BlockSpec((all_tokens, 2 * group_width), lambda g: (0, g)),
                pl.BlockSpec((lats, group_width), block_of),
                pl.BlockSpec((1, items, 8, stack), lambda g: (g, 0, 0, 0)),
            ]
            + [pl.BlockSpec((own, group_width), block_of)] * frame_size
            + [pl.BlockSpec((own, LANES), lambda g, c=c: (0, width // LANES + c))] * frame_size,
            out_specs=[
                pl.BlockSpec((all_tokens, 2 * group_width), lambda g: (0, g)),
                pl.BlockSpec((lats, group_width), lambda g: (0, g)),
            ],
            out_shape=[
                struct((all_tokens, 2 * half), BF16),
                struct((lats, half), F32),
            ],
            scratch_shapes=[
                pltpu.VMEM((items, lats, group_width), F32),
                pltpu.VMEM((items, lats, LANES), F32),
            ],
            cost_estimate=short,
            compiler_params=params,
        )(flags, after(boths[c], *sends[-1:]) if c else boths[c], queries, tops[c], *turns, *turns)
        term = transposed_left(all_rows, chunk_grad).astype(BF16)
        blocks.append(term.reshape(item_size // 2, 2, shard, 2 * half))
        sends = [jnp.stack([block(c, k, 1 - core) for k in range(item_size // 2)])]
        swapped.append(send_across(sends[0], "items", 1))
        chunk_grads.append(chunk_grad)
        chunk_queries.append(chunk_query)

    sum_rows = 2 * lats + 8
    sum_rows += -sum_rows % (8 * item_size)
    last_block = pl.BlockSpec((lats, 2 * half), lambda i: (tokens // lats, 0))
    payload = pl.pallas_call(
        functools.partial(latent_kernel, chunks=CHUNKS, items=items),
        grid=(1,),
        in_specs=[smem] + [last_block] * CHUNKS + [whole] * (CHUNKS + 6),
        out_specs=whole,
        out_shape=struct((sum_rows, width), F32),
        cost_estimate=short,
        compiler_params=params,
    )(
        flags,
        *chunk_grads[:-1],
        after(chunk_grads[-1], sends[0], swapped[0]),
        *chunk_queries,
        kv_full,
        query_full,
        latents,
        latent_gain[None],
        grad_base,
        ffn_sums,
    )
    payload_part = lax.psum_scatter(payload, "items", scatter_dimension=0, tiled=True)

    def chip_pieces(c):
        pieces = [
            block(c, k, core).astype(F32) + swapped[c][k].astype(F32)
            for k in range(item_size // 2)
        ]
        return pieces[:1] + [
            send_across(p.astype(BF16), "items", 2 * k) for k, p in enumerate(pieces) if k
        ]

    pieces = [chip_pieces(c) for c in range(CHUNKS)]

    together = 2
    media_grad, media_sums = pl.pallas_call(
        functools.partial(
            media_kernel, chunks=CHUNKS, items=items, frames=frame_total, together=together
        ),
        grid=(items // together,),
        in_specs=[smem]
        + [pl.BlockSpec((together * patches, 2 * half), lambda i: (i, 0))] * CHUNKS
        + [
            whole,
            pl.BlockSpec((together * patches, width), lambda i: (i, 0)),
            whole,
            whole,
        ],
        out_specs=[
            pl.BlockSpec((together * patches, width), lambda i: (i, 0)),
            pl.BlockSpec((16, width), lambda i: (0, 0)),
        ],
        out_shape=[struct((tokens, width), BF16), struct((16, width), F32)],
        cost_estimate=short,
        compiler_params=params,
    )(
        flags,
        *chunk_grads[:-1],
        after(chunk_grads[-1], payload, swapped[-1], pieces[0][0], ffn_other),
        kv_full,
        flat_media,
        time_rows,
        media_gain[None],
    )

    block_rows = min(512, plane)
    plane_blocks = plane // block_rows
    near = pl.BlockSpec((block_rows, width), lambda i: (jnp.minimum(i, plane_blocks - 1), 0))
    far = pl.BlockSpec((block_rows, width), lambda i: (jnp.maximum(i - plane_blocks, 0), 0))
    first_total = total_of(pieces[0])
    hidden, up_part = pl.pallas_call(
        functools.partial(feed_grad_kernel, plane_blocks=plane_blocks),
        grid=(plane_blocks * frame_size,),
        in_specs=[near, near, far, far, whole, whole],
        out_specs=[
            pl.BlockSpec((block_rows, hidden_shard), lambda i: (i, 0)),
            pl.BlockSpec((width, hidden_shard), lambda i: (0, 0)),
        ],
        out_shape=[
            struct((plane * frame_size, hidden_shard), BF16),
            struct((width, hidden_shard), BF16),
        ],
        scratch_shapes=[pltpu.VMEM((width, hidden_shard), F32)],
        cost_estimate=short,
        compiler_params=params,
    )(
        ffn_plane,
        low_plane,
        after(ffn_other, media_sums, first_total),
        low_other,
        up_slice,
        down_weight,
    )
    up_grad = lax.all_to_all(up_part, "items", 0, 1, tiled=True).astype(F32)

    first_rows = scatter_rows(first_total, "frames")
    branch_plane = lax.all_gather(grad_branch, "items", axis=0, tiled=True)
    att_plane = lax.all_to_all(after(attended, blocks[0]), "items", 1, 0, tiled=True)
    out_part = transposed_left(att_plane, branch_plane)
    last_rows = scatter_rows(
        jnp.concatenate([total_of(pieces[-1]), after(out_part, up_part)], 1), "frames"
    )
    hidden = after(hidden, first_rows[-1], pieces[-1][-1])
    down_grad = transposed_left(hidden[:plane], low_plane) + transposed_left(
        hidden[plane:], low_other
    )
    placed = []
    for part in (first_rows, last_rows):
        placed += spread_on(total_of(part).astype(BF16), "frames")
    key_grad, value_grad, out_grad = pl.pallas_call(
        functools.partial(
            place_kernel, chunks=CHUNKS, frames=frame_size, items=items, groups=groups
        ),
        in_specs=[smem] + [whole] * len(placed),
        out_specs=[whole] * 3,
        out_shape=[struct((frame_size, shard // frame_size, width), F32)] * 3,
        cost_estimate=short,
        compiler_params=params,
    )(flags, *placed)

    sums = lax.all_gather(
        total_of(spread_on(payload_part, "frames")), "items", axis=0, tiled=True
    )
    latents_grad = sums[:lats]
    query_grad = transposed_left(lat_cols, sums[lats : 2 * lats].astype(BF16))
    at = 2 * lats
    column_sums = total_of(
        spread_on(scatter_exchange(column_blocks(media_sums), "items"), "frames")
    )

    result = mid_rows + scatter_exchange(after(result_part, blocks[0]), "items")
    return (
        result.reshape(items, row_total, width),
        entropy,
        media_grad.reshape(media.shape),
        latents_grad,
        column_sums[:frame_total],
        column_sums[8],
        column_sums[9],
        sums[at + 2],
        sums[at + 3],
        sums[at],
        sums[at + 1],
        query_grad,
        key_grad.reshape(shard, width),
        value_grad.reshape(shard, width),
        out_grad.reshape(shard, width),
        up_grad,
        down_grad,
    )


def solution(mesh):
    return jax.shard_map(
        body,
        mesh=mesh,
        in_specs=(
            P("items", "frames", None, None),
            P("items", "frames", None),
            P(),
            P(),
            P(),
            P(),
            P(),
            P(),
            P(),
            P(),
            P(),
            P(),
            P("items", None),
            P("items", None),
            P("items", None),
            P("items", None),
            P("items", None),
            P("items", None),
        ),
        out_specs=(
            P("items", "frames", None),
            P("items", "frames"),
            P("items", "frames", None, None),
            P(),
            P(None, "items"),
            P("items"),
            P("items"),
            P(),
            P(),
            P(),
            P(),
            P("items", None),
            P("items", None),
            P("items", None),
            P("items", None),
            P("items", None),
            P("items", None),
        ),
        check_vma=False,
    )
```

```python
import functools

import jax
import jax.numpy as jnp
from jax import lax
from jax.experimental import pallas as pl
from jax.experimental.pallas import tpu as pltpu
from jax.sharding import PartitionSpec as P

HEADS = 16
GROUP = 4
CHUNKS = 2
LANES = 128
EPSILON = 1e-05
MASKED = -1e30
F32 = jnp.float32
BF16 = jnp.bfloat16
HIGHEST = lax.Precision.HIGHEST


def layer_norm(inputs, norm_gain, norm_bias):
    center = inputs - jnp.mean(inputs, axis=-1, keepdims=True)
    spread = jnp.mean(center * center, axis=-1, keepdims=True)
    return center * lax.rsqrt(spread + EPSILON) * norm_gain + norm_bias


def matmul(left_side, right_side):
    return jnp.dot(left_side, right_side, preferred_element_type=F32)


def transposed_left(left_side, right_side):
    return lax.dot_general(
        left_side, right_side, (((0,), (0,)), ((), ())), preferred_element_type=F32
    )


def transposed_right(left_side, right_side):
    return lax.dot_general(
        left_side, right_side, (((1,), (1,)), ((), ())), preferred_element_type=F32
    )


def send_on(x, axis, step):
    size = lax.axis_size(axis)
    return lax.ppermute(x, axis, [(i, (i + step) % size) for i in range(size)])


def send_across(x, axis, distance):
    return lax.ppermute(x, axis, [(i, i ^ distance) for i in range(lax.axis_size(axis))])


def spread_on(x, axis):
    return [x] + [send_on(x, axis, s) for s in range(1, lax.axis_size(axis))]


def spread_across(x, axis):
    return [x] + [send_across(x, axis, d) for d in range(1, lax.axis_size(axis))]


def collect_across(pieces, axis):
    return [pieces[0]] + [send_across(p, axis, d) for d, p in enumerate(pieces) if d]


def total_of(pieces):
    return functools.reduce(jnp.add, [p.astype(F32) for p in pieces])


def scatter_rows(x, axis):
    size = lax.axis_size(axis)
    me = lax.axis_index(axis)
    rows = x.shape[0] // size
    out = []
    for s in range(size):
        piece = lax.dynamic_slice_in_dim(x, ((me + s) % size) * rows, rows, 0)
        out.append(send_on(piece.astype(BF16), axis, s) if s else piece)
    return out


def after(x, *earlier):
    return lax.optimization_barrier((x,) + earlier)[0]


def split_terms(x):
    high = x.astype(BF16)
    rest = x - high.astype(F32)
    middle = rest.astype(BF16)
    return high, middle, (rest - middle.astype(F32)).astype(BF16)


def iota(shape, dim):
    return lax.broadcasted_iota(jnp.int32, shape, dim)


def head_masks(rows, width, head_size):
    lane = iota((rows, width), 1)
    return [
        jnp.logical_and(lane >= h * head_size, lane < (h + 1) * head_size)
        for h in range(width // head_size)
    ]


def spread_heads(block, masks):
    return jnp.concatenate([jnp.where(m, block, jnp.zeros_like(block)) for m in masks], 0)


def collect_heads(block, masks):
    rows = block.shape[0] // len(masks)
    total = jnp.where(masks[0], block[:rows], 0.0)
    for h in range(1, len(masks)):
        total = total + jnp.where(masks[h], block[h * rows : (h + 1) * rows], 0.0)
    return total


def head_expand(width, head_size):
    row, column = iota((LANES, width), 0), iota((LANES, width), 1)
    return jnp.logical_and(column >= row * head_size, column < (row + 1) * head_size).astype(F32)


def live_rows(flag_ref, item, items, patches, lats, columns):
    row = iota((patches + lats, columns), 0)
    media = jnp.logical_and(row < patches, flag_ref[item] > 0)
    return jnp.logical_or(media, jnp.logical_and(row >= patches, flag_ref[items] > 0))


def join_kernel(key_ref, value_ref, out_ref, *, width):
    for g in range(key_ref.shape[1] // width):
        columns = slice(g * width, (g + 1) * width)
        out_ref[:, 2 * g * width : (2 * g + 1) * width] = key_ref[:, columns]
        out_ref[:, (2 * g + 1) * width : (2 * g + 2) * width] = value_ref[:, columns]


def norm_kernel(media_ref, time_ref, gain_ref, bias_ref, lat_ref, out_ref, *, steps, per_item):
    step = pl.program_id(0)

    @pl.when(step < steps)
    def _():
        rows = media_ref[...].astype(F32) + time_ref[pl.ds(step // per_item, 1), :]
        out_ref[...] = layer_norm(rows, gain_ref[...], bias_ref[...]).astype(BF16)

    @pl.when(step == steps)
    def _():
        out_ref[...] = lat_ref[...]


def forward_kernel(
    flag_ref, both_ref, query_ref, top_ref, *refs, items, patches, scale, head_size, heads,
):
    message_refs, (part_ref, mark_ref) = refs[:-2], refs[-2:]
    lats, width = query_ref.shape
    frames = len(message_refs)
    own = message_refs[0].shape[0]
    row_total = own // items
    masks = head_masks(lats, width, head_size)
    queries = spread_heads(query_ref[...].astype(F32), masks).astype(BF16)
    base = items * patches
    lat_both = both_ref[base : base + lats, :]
    group = pl.program_id(0)
    term, lane = iota((16, GROUP * LANES), 0), iota((16, GROUP * LANES), 1)
    place = jnp.logical_and(
        lane % LANES == term * heads + group * GROUP + lane // LANES, term < 9
    ).astype(BF16)
    for i in range(items):
        both = jnp.concatenate([both_ref[i * patches : (i + 1) * patches, :], lat_both], 0)
        live = live_rows(flag_ref, i, items, patches, lats, queries.shape[0])
        scores = scale * transposed_right(both[:, :width], queries)
        masked = jnp.where(live, scores, MASKED)
        top = jnp.max(masked, axis=0, keepdims=True)
        block_exp = jnp.where(live, jnp.exp(masked - top), 0.0)
        total = jnp.sum(block_exp, axis=0, keepdims=True)
        moment = jnp.sum(block_exp * scores, axis=0, keepdims=True)
        part = transposed_left(block_exp.astype(BF16), both[:, width:])
        part_ref[i] = collect_heads(part, masks)
        top_ref[0, i] = jnp.broadcast_to(top, top_ref.shape[2:])
        terms = jnp.concatenate(
            [t.astype(F32) for x in (top, total, moment) for t in split_terms(x)]
            + [jnp.zeros((7, top.shape[1]), F32)],
            0,
        ).astype(BF16)
        wide = transposed_left(terms, place)
        mark = wide[:lats, :LANES]
        for h in range(1, GROUP):
            mark = mark + wide[h * lats : (h + 1) * lats, h * LANES : (h + 1) * LANES]
        mark_ref[i] = mark

    end = message_refs[0].shape[1] - LANES
    for s, message_ref in enumerate(message_refs):
        start = pl.multiple_of(lax.rem(flag_ref[items + 1] + s, frames) * row_total, row_total)
        rows = pl.ds(start, row_total)
        block = jnp.concatenate([part_ref[i, rows, :] for i in range(items)], 0).astype(BF16)
        mark = jnp.concatenate([mark_ref[i, rows, :] for i in range(items)], 0).astype(BF16)
        for g in range(end // width):

            @pl.when(group == g)
            def _():
                message_ref[:, g * width : (g + 1) * width] = block
                if g == 0:
                    message_ref[:, end:] = mark
                else:
                    message_ref[:, end:] = message_ref[:, end:] + mark


def merge_kernel(*refs, chunks, frames, items, head_size, heads):
    message_refs = refs[: chunks * frames]
    base_ref, weight_ref, gain_ref, bias_ref = refs[chunks * frames : chunks * frames + 4]
    merged_ref, attended_ref, mid_ref, ffn_ref, log_ref, entropy_ref = refs[chunks * frames + 4 :]
    own, columns = message_refs[0].shape
    half = columns - LANES
    lane, column = iota((LANES, 3 * LANES), 0), iota((LANES, 3 * LANES), 1)
    gather = jnp.logical_and(
        jnp.logical_and(lane // heads // 3 == column // LANES, lane % heads == column % LANES),
        lane < 9 * heads,
    ).astype(BF16)
    expand = head_expand(half, head_size)
    live = iota((own, LANES), 1) < heads
    spread = jnp.zeros((own, LANES), F32)
    for c in range(chunks):
        sources = message_refs[c * frames : (c + 1) * frames]
        stats = [matmul(x[:, half:], gather) for x in sources]
        tops = [x[:, :LANES] for x in stats]
        peak = functools.reduce(jnp.maximum, tops)
        factors = [jnp.exp(t - peak) for t in tops]
        whole = sum(f * x[:, LANES : 2 * LANES] for f, x in zip(factors, stats))
        moment = sum(f * x[:, 2 * LANES :] for f, x in zip(factors, stats))
        whole = jnp.where(live, whole, 1.0)
        log_total = jnp.where(live, peak + jnp.log(whole), 0.0)
        log_ref[c] = log_total
        spread = spread + jnp.where(live, log_total - moment / whole, 0.0)
        merged = jnp.zeros((own, half), F32)
        for x, factor in zip(sources, factors):
            share = jnp.where(live, factor / whole, 0.0)
            wide = jnp.dot(share, expand, precision=HIGHEST, preferred_element_type=F32)
            merged = merged + x[:, :half].astype(F32) * wide
        merged_ref[:, c * half : (c + 1) * half] = merged
        attended_ref[:, c * half : (c + 1) * half] = merged.astype(BF16)
    entropy_ref[...] = jnp.broadcast_to(
        jnp.sum(spread, axis=1, keepdims=True) * (1.0 / HEADS), entropy_ref.shape
    )
    base = jnp.concatenate([base_ref[...]] * items, 0)
    mid = base + matmul(attended_ref[...], weight_ref[...])
    mid_ref[...] = mid
    ffn_ref[...] = layer_norm(mid, gain_ref[...], bias_ref[...]).astype(BF16)


def gelu_parts(x):
    share = 0.5 * (1.0 + lax.erf(x * (0.5**0.5)))
    slope = share + x * jnp.exp(-0.5 * x * x) * ((2.0 * jnp.pi) ** -0.5)
    return x * share, slope


def feed_kernel(flag_ref, *refs, devices, items):
    row_refs = refs[:devices]
    low_ref, up_ref, down_ref, plane_ref, plane_low_ref, result_ref = refs[devices : devices + 6]
    grad_refs = refs[devices + 6 :]
    own = row_refs[0].shape[0]
    me = flag_ref[2 * items + 2]
    for d in range(devices):
        plane_ref[d * own : (d + 1) * own, :] = row_refs[d][...]
        plane_low_ref[d * own : (d + 1) * own, :] = low_ref[jnp.bitwise_xor(me, d)]
    upward = matmul(plane_ref[...], up_ref[...])
    hidden, slope = gelu_parts(upward)
    grad_up = (slope * transposed_right(plane_low_ref[...], down_ref[...])).astype(BF16)
    grad = transposed_right(grad_up, up_ref[...]).astype(BF16)
    result = matmul(hidden.astype(BF16), down_ref[...]).astype(BF16)
    for d in range(devices):
        grad_refs[d][...] = grad[d * own : (d + 1) * own, :]
        result_ref[jnp.bitwise_xor(me, d)] = result[d * own : (d + 1) * own, :]


def feed_grad_kernel(
    plane_ref, plane_low_ref, other_ref, other_low_ref, up_ref, down_ref, hidden_ref, up_grad_ref,
    total_ref, *, plane_blocks,
):
    step = pl.program_id(0)
    near = step < plane_blocks
    rows = jnp.where(near, plane_ref[...], other_ref[...])
    low = jnp.where(near, plane_low_ref[...], other_low_ref[...])
    hidden, slope = gelu_parts(matmul(rows, up_ref[...]))
    hidden_ref[...] = hidden.astype(BF16)
    grad_up = (slope * transposed_right(low, down_ref[...])).astype(BF16)
    up_part = transposed_left(rows, grad_up)

    @pl.when(step == 0)
    def _():
        total_ref[...] = up_part

    @pl.when(step > 0)
    def _():
        total_ref[...] += up_part

    @pl.when(step == pl.num_programs(0) - 1)
    def _():
        up_grad_ref[...] = total_ref[...].astype(BF16)


def norm_backward(rows, gain, gradient):
    center = rows - jnp.mean(rows, axis=1, keepdims=True)
    rate = lax.rsqrt(jnp.mean(center * center, axis=1, keepdims=True) + EPSILON)
    unit = center * rate
    scaled = gradient * gain
    inner = scaled - jnp.mean(scaled, axis=1, keepdims=True)
    back = rate * (inner - unit * jnp.mean(scaled * unit, axis=1, keepdims=True))
    return (
        back,
        jnp.sum(gradient * unit, axis=0, keepdims=True),
        jnp.sum(gradient, axis=0, keepdims=True),
    )


def turn_kernel(*refs, devices, items, chunks, head_size, heads):
    part_refs = refs[:devices]
    mid_ref, cotangent_ref, gain_ref, merged_ref, log_ref, weight_ref = refs[
        devices : devices + 6
    ]
    message_ref, branch_ref, base_ref, sums_ref = refs[devices + 6 :]
    own, width = mid_ref.shape
    half = width // chunks
    gradient = total_of([x[...] for x in part_refs])
    back, gain_sum, bias_sum = norm_backward(mid_ref[...], gain_ref[...], gradient)
    grad_mid = cotangent_ref[...] + back
    sums_ref[...] = jnp.zeros(sums_ref.shape, F32)
    sums_ref[0:1, :] = gain_sum
    sums_ref[1:2, :] = bias_sum
    row_total = own // items
    base_ref[...] = total_of(
        [grad_mid[i * row_total : (i + 1) * row_total] for i in range(items)]
    )
    branch = grad_mid.astype(BF16)
    branch_ref[...] = branch
    grad_att = transposed_right(branch, weight_ref[...]).astype(BF16)
    expand = head_expand(half, head_size)
    lane, column = iota((6 * LANES, LANES), 0), iota((6 * LANES, LANES), 1)
    place = jnp.logical_and(
        lane % LANES < heads, column == (lane // LANES) * heads + lane % LANES
    ).astype(BF16)
    message_ref[:, :width] = grad_att
    for c in range(chunks):
        columns = slice(c * half, (c + 1) * half)
        delta = lax.dot_general(
            merged_ref[:, columns] * grad_att[:, columns].astype(F32),
            expand,
            (((1,), (1,)), ((), ())),
            precision=HIGHEST,
            preferred_element_type=F32,
        )
        terms = jnp.concatenate([t for x in (log_ref[c], delta) for t in split_terms(x)], 1)
        message_ref[:, width + c * LANES : width + (c + 1) * LANES] = matmul(
            terms, place
        ).astype(BF16)


def backward_kernel(
    *refs, frames, items, patches, scale, head_size, heads,
):
    flag_ref, both_ref, query_ref, top_ref = refs[:4]
    grad_refs = refs[4 : 4 + frames]
    mark_refs = refs[4 + frames : 4 + 2 * frames]
    out_ref, sum_ref, held_ref, note_ref = refs[4 + 2 * frames :]
    lats, width = query_ref.shape
    own = grad_refs[0].shape[0]
    row_total = own // items
    base = items * patches
    for s in range(frames):
        source = lax.rem(flag_ref[items + 1] + (frames - s), frames)
        rows = pl.ds(pl.multiple_of(source * row_total, row_total), row_total)
        block = grad_refs[s][...].astype(F32)
        mark = mark_refs[s][...].astype(F32)
        for i in range(items):
            held_ref[i, rows, :] = block[i * row_total : (i + 1) * row_total]
            note_ref[i, rows, :] = mark[i * row_total : (i + 1) * row_total]
    masks = head_masks(lats, width, head_size)
    queries = spread_heads(query_ref[...].astype(F32), masks).astype(BF16)
    lat_both = both_ref[base : base + lats, :]
    row, lane = iota((GROUP * 8, LANES), 0), iota((GROUP * 8, LANES), 1)
    pick = jnp.logical_and(
        jnp.logical_and(
            lane // heads // 3 == row % 8,
            lane % heads == pl.program_id(0) * GROUP + row // 8,
        ),
        lane < 6 * heads,
    ).astype(BF16)
    grad_query = jnp.zeros((queries.shape[0], width), F32)
    lat_grad_key = jnp.zeros((lats, width), F32)
    lat_grad_value = jnp.zeros((lats, width), F32)
    for i in range(items):
        rows = slice(i * patches, (i + 1) * patches)
        stats = transposed_right(pick, note_ref[i].astype(BF16))
        stats = jnp.concatenate([stats[h * 8 : (h + 1) * 8] for h in range(GROUP)], 1)
        log_total = stats[0:1]
        delta = stats[1:2]
        top = top_ref[0, i, 0:1, :]
        rescale = jnp.exp(top - log_total)
        both = jnp.concatenate([both_ref[rows, :], lat_both], 0)
        keys, values = both[:, :width], both[:, width:]
        grads = spread_heads(held_ref[i], masks).astype(BF16)
        live = live_rows(flag_ref, i, items, patches, lats, queries.shape[0])
        masked = jnp.where(live, scale * transposed_right(keys, queries), MASKED)
        probs = jnp.where(live, jnp.exp(masked - log_total), 0.0)
        block_exp = jnp.where(live, jnp.exp(masked - top), 0.0)
        weights = (block_exp.astype(BF16).astype(F32) * rescale).astype(BF16)
        grad_scores = (probs * (transposed_right(values, grads) - delta)).astype(BF16)
        grad_key = scale * matmul(grad_scores, queries)
        grad_value = matmul(weights, grads)
        out_ref[rows, :width] = grad_key[:patches].astype(BF16)
        out_ref[rows, width:] = grad_value[:patches].astype(BF16)
        grad_query = grad_query + transposed_left(grad_scores, keys)
        lat_grad_key = lat_grad_key + grad_key[patches:]
        lat_grad_value = lat_grad_value + grad_value[patches:]
    out_ref[base : base + lats, :width] = lat_grad_key.astype(BF16)
    out_ref[base : base + lats, width:] = lat_grad_value.astype(BF16)
    sum_ref[...] = scale * collect_heads(grad_query, masks)


def media_kernel(flag_ref, *refs, chunks, items, frames, together):
    grad_refs = refs[:chunks]
    weight_ref, media_ref, time_ref, gain_ref, out_ref, sums_ref = refs[chunks:]
    step = pl.program_id(0)
    span = weight_ref.shape[1] // chunks
    patches = media_ref.shape[0] // together
    gradient = transposed_right(grad_refs[0][...], weight_ref[:, :span])
    for c in range(1, chunks):
        gradient = gradient + transposed_right(
            grad_refs[c][...], weight_ref[:, c * span : (c + 1) * span]
        )

    @pl.when(step == 0)
    def _():
        sums_ref[...] = jnp.zeros(sums_ref.shape, F32)

    for k in range(together):
        item = step * together + k
        rows = slice(k * patches, (k + 1) * patches)
        inputs = media_ref[rows, :].astype(F32) + time_ref[pl.ds(item, 1), :]
        back, gain_sum, bias_sum = norm_backward(inputs, gain_ref[...], gradient[rows])
        out_ref[rows, :] = back.astype(BF16)
        place = iota((frames, 1), 0) == flag_ref[items + 2 + item]
        sums_ref[0:frames, :] += jnp.where(place, jnp.sum(back, axis=0, keepdims=True), 0.0)
        sums_ref[8:9, :] += gain_sum
        sums_ref[9:10, :] += bias_sum


def latent_kernel(
    flag_ref, *refs, chunks, items,
):
    grad_refs = refs[:chunks]
    query_refs = refs[chunks : 2 * chunks]
    (
        weight_ref, query_weight_ref, latent_ref, gain_ref, base_ref, ffn_ref, out_ref,
    ) = refs[2 * chunks :]
    lats, width = latent_ref.shape
    span = weight_ref.shape[1] // chunks
    half = width // chunks
    gradient = jnp.zeros((lats, width), F32)
    for c in range(chunks):
        gradient = gradient + transposed_right(
            grad_refs[c][...], weight_ref[:, c * span : (c + 1) * span]
        )
        gradient = gradient + transposed_right(
            query_refs[c][...].astype(BF16), query_weight_ref[:, c * half : (c + 1) * half]
        )
        out_ref[lats : 2 * lats, c * half : (c + 1) * half] = query_refs[c][...]
    back, gain_sum, bias_sum = norm_backward(latent_ref[...], gain_ref[...], gradient)
    out_ref[:lats, :] = back
    row_total = base_ref.shape[0]
    start = pl.multiple_of(flag_ref[items + 1] * row_total, row_total)
    out_ref[pl.ds(start, row_total), :] += base_ref[...]
    at = 2 * lats
    out_ref[at : at + 8, :] = ffn_ref[...]
    out_ref[at + 2 : at + 3, :] = gain_sum
    out_ref[at + 3 : at + 4, :] = bias_sum
    out_ref[at + 8 :, :] = jnp.zeros((out_ref.shape[0] - at - 8, width), F32)


def place_kernel(flag_ref, *refs, chunks, frames, items, groups):
    chunk_refs = refs[: chunks * frames]
    more_refs = refs[chunks * frames : (chunks + 1) * frames]
    key_ref, value_ref, out_ref = refs[(chunks + 1) * frames :]
    width = key_ref.shape[2] // (chunks * groups)
    for s in range(frames):
        source = lax.rem(flag_ref[items + 1] + (frames - s), frames)
        out_ref[source] = more_refs[s][...].astype(F32)
        for c in range(chunks):
            for g in range(groups):
                at = (c * groups + g) * width
                block = chunk_refs[c * frames + s][:, 2 * g * width : 2 * (g + 1) * width]
                block = block.astype(F32)
                key_ref[source, :, at : at + width] = block[:, :width]
                value_ref[source, :, at : at + width] = block[:, width:]


def body(
    media,
    cotangent,
    frame_count,
    frame_start,
    latents,
    time_embed,
    media_gain,
    media_bias,
    latent_gain,
    latent_bias,
    ffn_gain,
    ffn_bias,
    query_weight,
    key_weight,
    value_weight,
    out_weight,
    up_weight,
    down_weight,
):
    items = media.shape[0]
    patches = media.shape[2]
    width = media.shape[3]
    lats = latents.shape[0]
    frame_total = time_embed.shape[0]
    row_total = cotangent.shape[1]
    own = items * row_total
    head_size = width // HEADS
    half = width // CHUNKS
    chunk_heads = HEADS // CHUNKS
    group_width = GROUP * head_size
    groups = chunk_heads // GROUP
    stack = GROUP * lats
    tokens = items * patches
    all_tokens = tokens + lats
    shard = query_weight.shape[0]
    hidden_shard = down_weight.shape[0]
    item_size = lax.axis_size("items")
    frame_size = lax.axis_size("frames")
    plane = item_size * own
    item_index = lax.axis_index("items")
    slot = lax.axis_index("frames")
    row_base = slot * row_total
    params = pltpu.CompilerParams(vmem_limit_bytes=56 * 2**20)
    smem = pl.BlockSpec(memory_space=pltpu.SMEM)
    whole = pl.BlockSpec(memory_space=pltpu.VMEM)
    sizes = dict(items=items, head_size=head_size, heads=chunk_heads)

    def struct(shape, kind):
        return jax.ShapeDtypeStruct(shape, kind)

    short = pl.CostEstimate(flops=1000, bytes_accessed=1000, transcendentals=0)

    joined = pl.pallas_call(
        functools.partial(join_kernel, width=group_width),
        out_shape=struct((shard, 2 * width), BF16),
        cost_estimate=short,
        compiler_params=params,
    )(key_weight, value_weight)
    kv_full = lax.all_gather(joined, "items", axis=0, tiled=True)

    lat_norm = layer_norm(latents, latent_gain, latent_bias).astype(BF16)
    lat_cols = lax.dynamic_slice_in_dim(lat_norm, item_index * shard, shard, 1)

    def column_blocks(x):
        return jnp.transpose(x.reshape(-1, item_size, shard), (1, 0, 2))

    def scatter_exchange(x, axis):
        return jnp.sum(lax.all_to_all(x, axis, 0, 0).astype(F32), axis=0)

    query_cols = scatter_exchange(column_blocks(matmul(lat_cols, query_weight)), "items")
    query_cols = jnp.broadcast_to(query_cols.astype(BF16)[None], (item_size, lats, shard))
    queries = jnp.transpose(lax.all_to_all(query_cols, "items", 0, 0), (1, 0, 2)).reshape(
        lats, width
    )

    counts = lax.dynamic_slice_in_dim(frame_count, item_index * items, items)
    starts = lax.dynamic_slice_in_dim(frame_start, item_index * items, items)
    offset = (slot - starts) % frame_total
    flags = jnp.concatenate(
        [
            (offset < counts).astype(jnp.int32),
            (slot == 0).astype(jnp.int32)[None],
            slot.astype(jnp.int32)[None],
            offset.astype(jnp.int32),
            item_index.astype(jnp.int32)[None],
        ]
    )
    picker = (offset[:, None] == jnp.arange(frame_total, dtype=jnp.int32)[None, :]).astype(F32)
    time_rows = jnp.dot(picker, time_embed, precision=HIGHEST, preferred_element_type=F32)
    flat_media = media.reshape(tokens, width)
    steps = tokens // lats
    all_rows = pl.pallas_call(
        functools.partial(norm_kernel, steps=steps, per_item=patches // lats),
        grid=(steps + 1,),
        in_specs=[
            pl.BlockSpec((lats, width), lambda i: (jnp.minimum(i, steps - 1), 0)),
            whole,
            whole,
            whole,
            whole,
        ],
        out_specs=pl.BlockSpec((lats, width), lambda i: (i, 0)),
        out_shape=struct((all_tokens, width), BF16),
        cost_estimate=short,
        compiler_params=params,
    )(flat_media, time_rows, media_gain[None], media_bias[None], lat_norm)

    grad_out = cotangent.reshape(own, width)
    grad_low = grad_out.astype(BF16)
    low_shift = spread_on(grad_low, "frames")[1:]
    out_full = lax.all_gather(after(out_weight, all_rows), "items", axis=0, tiled=True)

    boths, tops, messages = [], [], []
    for c in range(CHUNKS):

        def block_of(g, c=c):
            return (0, c * groups + g)

        rows = after(all_rows, tops[-1]) if c else after(all_rows, queries, *low_shift)
        both = matmul(rows, kv_full[:, 2 * c * half : 2 * (c + 1) * half]).astype(BF16)
        top, *parts = pl.pallas_call(
            functools.partial(
                forward_kernel, patches=patches, scale=head_size**-0.5, **sizes
            ),
            grid=(groups,),
            in_specs=[
                smem,
                pl.BlockSpec((all_tokens, 2 * group_width), lambda g: (0, g)),
                pl.BlockSpec((lats, group_width), block_of),
            ],
            out_specs=[pl.BlockSpec((1, items, 8, stack), lambda g: (g, 0, 0, 0))]
            + [pl.BlockSpec((own, half + LANES), lambda g: (0, 0))] * frame_size,
            out_shape=[struct((groups, items, 8, stack), F32)]
            + [struct((own, half + LANES), BF16)] * frame_size,
            scratch_shapes=[
                pltpu.VMEM((items, lats, group_width), F32),
                pltpu.VMEM((items, lats, LANES), F32),
            ],
            cost_estimate=short,
            compiler_params=params,
        )(flags, both, queries)
        boths.append(both)
        tops.append(top)
        messages += [p if s == 0 else send_on(p, "frames", s) for s, p in enumerate(parts)]
    up_slice = lax.all_to_all(after(up_weight, *messages[1:2]), "items", 1, 0, tiled=True)
    low_every = lax.all_gather(after(grad_low, boths[0]), "items", axis=0)
    low_other = lax.all_gather(
        after(jnp.stack(low_shift), boths[1]), "items", axis=0
    ).reshape(-1, width)

    base_rows = lax.dynamic_slice_in_dim(latents, row_base, row_total, 0)
    merged, attended, mid_rows, ffn_in, logs, entropy_wide = pl.pallas_call(
        functools.partial(merge_kernel, chunks=CHUNKS, frames=frame_size, **sizes),
        out_shape=[
            struct((own, width), F32),
            struct((own, width), BF16),
            struct((own, width), F32),
            struct((own, width), BF16),
            struct((CHUNKS, own, LANES), F32),
            struct((own, LANES), F32),
        ],
        cost_estimate=short,
        compiler_params=params,
    )(*messages, base_rows, out_full, ffn_gain[None], ffn_bias[None])
    entropy = entropy_wide[:, 0].reshape(items, row_total)

    ffn_blocks = spread_across(ffn_in, "items")
    ffn_plane, low_plane, result_part, *parts = pl.pallas_call(
        functools.partial(feed_kernel, devices=item_size, items=items),
        in_specs=[smem] + [whole] * (item_size + 3),
        out_shape=[struct((plane, width), BF16)] * 2
        + [struct((item_size, own, width), BF16)]
        + [struct((own, width), BF16)] * item_size,
        cost_estimate=short,
        compiler_params=params,
    )(flags, *ffn_blocks, low_every, up_slice, down_weight)
    query_full = lax.all_gather(after(query_weight, ffn_plane), "items", axis=0, tiled=True)
    grad_blocks = collect_across(parts, "items")
    grad_blocks[0] = after(grad_blocks[0], low_other)

    turn, grad_branch, grad_base, ffn_sums = pl.pallas_call(
        functools.partial(turn_kernel, devices=item_size, chunks=CHUNKS, **sizes),
        out_shape=[
            struct((own, width + CHUNKS * LANES), BF16),
            struct((own, width), BF16),
            struct((row_total, width), F32),
            struct((8, width), F32),
        ],
        cost_estimate=short,
        compiler_params=params,
    )(*grad_blocks, mid_rows, grad_out, ffn_gain[None], merged, logs, out_full)
    turns = spread_on(turn, "frames")
    branch_plane = lax.all_gather(grad_branch, "items", axis=0, tiled=True)
    att_plane = lax.all_to_all(after(attended, turn), "items", 1, 0, tiled=True)
    result_pieces = lax.all_to_all(after(result_part, att_plane), "items", 0, 0)
    turns[0] = after(turns[0], att_plane)
    ffn_shift = spread_on(after(ffn_in, turns[-1]), "frames")[1:]
    ffn_other = lax.all_gather(jnp.stack(ffn_shift), "items", axis=0).reshape(-1, width)

    chip, core = item_index // 2, item_index % 2
    chunk_grads, chunk_queries, blocks, pieces = [], [], [], []

    def block(c, k, which):
        return lax.dynamic_slice(
            blocks[c], (chip ^ k, which, 0, 0), (1, 1, shard, 2 * half)
        ).reshape(shard, 2 * half)

    def chip_pieces(c, received):
        sums = [
            block(c, k, core).astype(F32) + received[k].astype(F32)
            for k in range(item_size // 2)
        ]
        return sums[:1] + [p.astype(BF16) for p in sums[1:]]

    def send_pieces(sums):
        return sums[:1] + [
            send_across(p, "items", 2 * k) for k, p in enumerate(sums) if k
        ]

    for c in range(CHUNKS):

        def block_of(g, c=c):
            return (0, c * groups + g)

        chunk_grad, chunk_query = pl.pallas_call(
            functools.partial(
                backward_kernel, frames=frame_size, patches=patches, scale=head_size**-0.5, **sizes
            ),
            grid=(groups,),
            in_specs=[
                smem,
                pl.BlockSpec((all_tokens, 2 * group_width), lambda g: (0, g)),
                pl.BlockSpec((lats, group_width), block_of),
                pl.BlockSpec((1, items, 8, stack), lambda g: (g, 0, 0, 0)),
            ]
            + [pl.BlockSpec((own, group_width), block_of)] * frame_size
            + [pl.BlockSpec((own, LANES), lambda g, c=c: (0, width // LANES + c))] * frame_size,
            out_specs=[
                pl.BlockSpec((all_tokens, 2 * group_width), lambda g: (0, g)),
                pl.BlockSpec((lats, group_width), lambda g: (0, g)),
            ],
            out_shape=[
                struct((all_tokens, 2 * half), BF16),
                struct((lats, half), F32),
            ],
            scratch_shapes=[
                pltpu.VMEM((items, lats, group_width), F32),
                pltpu.VMEM((items, lats, LANES), F32),
            ],
            cost_estimate=short,
            compiler_params=params,
        )(flags, after(boths[c], send) if c else boths[c], queries, tops[c], *turns, *turns)
        if c:
            pieces.append(chip_pieces(c - 1, received))
            term_rows = after(all_rows, *pieces[-1])
        else:
            term_rows = all_rows
        term = transposed_left(term_rows, chunk_grad).astype(BF16)
        blocks.append(term.reshape(item_size // 2, 2, shard, 2 * half))
        send = jnp.stack([block(c, k, 1 - core) for k in range(item_size // 2)])
        received = send_across(send, "items", 1)
        chunk_grads.append(chunk_grad)
        chunk_queries.append(chunk_query)
    first_total = total_of(send_pieces(pieces[0]))

    sum_rows = 2 * lats + 8
    sum_rows += -sum_rows % (8 * item_size)
    last_block = pl.BlockSpec((lats, 2 * half), lambda i: (tokens // lats, 0))
    payload = pl.pallas_call(
        functools.partial(latent_kernel, chunks=CHUNKS, items=items),
        grid=(1,),
        in_specs=[smem] + [last_block] * CHUNKS + [whole] * (CHUNKS + 6),
        out_specs=whole,
        out_shape=struct((sum_rows, width), F32),
        cost_estimate=short,
        compiler_params=params,
    )(
        flags,
        *chunk_grads[:-1],
        after(chunk_grads[-1], send, result_pieces),
        *chunk_queries,
        kv_full,
        query_full,
        latents,
        latent_gain[None],
        grad_base,
        ffn_sums,
    )
    payload_part = lax.psum_scatter(payload, "items", scatter_dimension=0, tiled=True)

    pieces.append(chip_pieces(CHUNKS - 1, received))
    last_total = total_of(send_pieces(pieces[-1]))
    first_rows = scatter_rows(first_total, "frames")
    out_part = transposed_left(att_plane, branch_plane)
    out_rows = scatter_rows(after(out_part, payload), "frames")

    block_rows = min(512, plane)
    plane_blocks = plane // block_rows
    near = pl.BlockSpec((block_rows, width), lambda i: (jnp.minimum(i, plane_blocks - 1), 0))
    far = pl.BlockSpec((block_rows, width), lambda i: (jnp.maximum(i - plane_blocks, 0), 0))
    hidden, up_part = pl.pallas_call(
        functools.partial(feed_grad_kernel, plane_blocks=plane_blocks),
        grid=(plane_blocks * frame_size,),
        in_specs=[near, near, far, far, whole, whole],
        out_specs=[
            pl.BlockSpec((block_rows, hidden_shard), lambda i: (i, 0)),
            pl.BlockSpec((width, hidden_shard), lambda i: (0, 0)),
        ],
        out_shape=[
            struct((plane * frame_size, hidden_shard), BF16),
            struct((width, hidden_shard), BF16),
        ],
        scratch_shapes=[pltpu.VMEM((width, hidden_shard), F32)],
        cost_estimate=short,
        compiler_params=params,
    )(
        ffn_plane,
        low_plane,
        after(ffn_other, payload, *pieces[-1], *first_rows[:1]),
        low_other,
        up_slice,
        down_weight,
    )
    up_grad = lax.all_to_all(up_part, "items", 0, 1, tiled=True).astype(F32)

    together = 2
    media_grad, media_sums = pl.pallas_call(
        functools.partial(
            media_kernel, chunks=CHUNKS, items=items, frames=frame_total, together=together
        ),
        grid=(items // together,),
        in_specs=[smem]
        + [pl.BlockSpec((together * patches, 2 * half), lambda i: (i, 0))] * CHUNKS
        + [
            whole,
            pl.BlockSpec((together * patches, width), lambda i: (i, 0)),
            whole,
            whole,
        ],
        out_specs=[
            pl.BlockSpec((together * patches, width), lambda i: (i, 0)),
            pl.BlockSpec((16, width), lambda i: (0, 0)),
        ],
        out_shape=[struct((tokens, width), BF16), struct((16, width), F32)],
        cost_estimate=short,
        compiler_params=params,
    )(
        flags,
        *chunk_grads[:-1],
        after(chunk_grads[-1], up_part, last_total, *first_rows, *out_rows),
        kv_full,
        flat_media,
        time_rows,
        media_gain[None],
    )

    first_placed = spread_on(total_of(first_rows).astype(BF16), "frames")
    out_placed = spread_on(total_of(out_rows).astype(BF16), "frames")
    last_rows = scatter_rows(last_total, "frames")
    hidden = after(hidden, media_sums, *last_rows)
    down_grad = transposed_left(hidden[:plane], low_plane) + transposed_left(
        hidden[plane:], low_other
    )
    last_placed = spread_on(total_of(last_rows).astype(BF16), "frames")
    placed = first_placed + last_placed + out_placed
    key_grad, value_grad, out_grad = pl.pallas_call(
        functools.partial(
            place_kernel, chunks=CHUNKS, frames=frame_size, items=items, groups=groups
        ),
        in_specs=[smem] + [whole] * len(placed),
        out_specs=[whole] * 3,
        out_shape=[struct((frame_size, shard // frame_size, width), F32)] * 3,
        cost_estimate=short,
        compiler_params=params,
    )(flags, *placed)

    payload_others = spread_on(payload_part.astype(BF16), "frames")[1:]
    sums = lax.all_gather(
        total_of([payload_part] + payload_others), "items", axis=0, tiled=True
    )
    latents_grad = sums[:lats]
    query_grad = transposed_left(lat_cols, sums[lats : 2 * lats].astype(BF16))
    at = 2 * lats
    column_sums = total_of(
        spread_on(scatter_exchange(column_blocks(media_sums), "items"), "frames")
    )

    result = mid_rows + total_of([result_pieces[d] for d in range(item_size)])
    return (
        result.reshape(items, row_total, width),
        entropy,
        media_grad.reshape(media.shape),
        latents_grad,
        column_sums[:frame_total],
        column_sums[8],
        column_sums[9],
        sums[at + 2],
        sums[at + 3],
        sums[at],
        sums[at + 1],
        query_grad,
        key_grad.reshape(shard, width),
        value_grad.reshape(shard, width),
        out_grad.reshape(shard, width),
        up_grad,
        down_grad,
    )


def solution(mesh):
    return jax.shard_map(
        body,
        mesh=mesh,
        in_specs=(
            P("items", "frames", None, None),
            P("items", "frames", None),
            P(),
            P(),
            P(),
            P(),
            P(),
            P(),
            P(),
            P(),
            P(),
            P(),
            P("items", None),
            P("items", None),
            P("items", None),
            P("items", None),
            P("items", None),
            P("items", None),
        ),
        out_specs=(
            P("items", "frames", None),
            P("items", "frames"),
            P("items", "frames", None, None),
            P(),
            P(None, "items"),
            P("items"),
            P("items"),
            P(),
            P(),
            P(),
            P(),
            P("items", None),
            P("items", None),
            P("items", None),
            P("items", None),
            P("items", None),
            P("items", None),
        ),
        check_vma=False,
    )
```

```python
import functools

import jax
import jax.numpy as jnp
from jax import lax
from jax.experimental import pallas as pl
from jax.experimental.pallas import tpu as pltpu
from jax.sharding import PartitionSpec as P

HEADS = 16
GROUP = 4
CHUNKS = 2
LANES = 128
EPSILON = 1e-05
MASKED = -1e30
F32 = jnp.float32
BF16 = jnp.bfloat16
HIGHEST = lax.Precision.HIGHEST


def layer_norm(inputs, norm_gain, norm_bias):
    center = inputs - jnp.mean(inputs, axis=-1, keepdims=True)
    spread = jnp.mean(center * center, axis=-1, keepdims=True)
    return center * lax.rsqrt(spread + EPSILON) * norm_gain + norm_bias


def matmul(left_side, right_side):
    return jnp.dot(left_side, right_side, preferred_element_type=F32)


def transposed_left(left_side, right_side):
    return lax.dot_general(
        left_side, right_side, (((0,), (0,)), ((), ())), preferred_element_type=F32
    )


def transposed_right(left_side, right_side):
    return lax.dot_general(
        left_side, right_side, (((1,), (1,)), ((), ())), preferred_element_type=F32
    )


def send_on(x, axis, step):
    size = lax.axis_size(axis)
    return lax.ppermute(x, axis, [(i, (i + step) % size) for i in range(size)])


def send_across(x, axis, distance):
    return lax.ppermute(x, axis, [(i, i ^ distance) for i in range(lax.axis_size(axis))])


def spread_on(x, axis):
    return [x] + [send_on(x, axis, s) for s in range(1, lax.axis_size(axis))]


def spread_across(x, axis):
    return [x] + [send_across(x, axis, d) for d in range(1, lax.axis_size(axis))]


def collect_across(pieces, axis):
    return [pieces[0]] + [send_across(p, axis, d) for d, p in enumerate(pieces) if d]


def total_of(pieces):
    return functools.reduce(jnp.add, [p.astype(F32) for p in pieces])


def scatter_rows(x, axis):
    size = lax.axis_size(axis)
    me = lax.axis_index(axis)
    rows = x.shape[0] // size
    out = []
    for s in range(size):
        piece = lax.dynamic_slice_in_dim(x, ((me + s) % size) * rows, rows, 0)
        out.append(send_on(piece.astype(BF16), axis, s) if s else piece)
    return out


def after(x, *earlier):
    return lax.optimization_barrier((x,) + earlier)[0]


def split_terms(x):
    high = x.astype(BF16)
    rest = x - high.astype(F32)
    middle = rest.astype(BF16)
    return high, middle, (rest - middle.astype(F32)).astype(BF16)


def iota(shape, dim):
    return lax.broadcasted_iota(jnp.int32, shape, dim)


def head_masks(rows, width, head_size):
    lane = iota((rows, width), 1)
    return [
        jnp.logical_and(lane >= h * head_size, lane < (h + 1) * head_size)
        for h in range(width // head_size)
    ]


def spread_heads(block, masks):
    return jnp.concatenate([jnp.where(m, block, jnp.zeros_like(block)) for m in masks], 0)


def collect_heads(block, masks):
    rows = block.shape[0] // len(masks)
    total = jnp.where(masks[0], block[:rows], 0.0)
    for h in range(1, len(masks)):
        total = total + jnp.where(masks[h], block[h * rows : (h + 1) * rows], 0.0)
    return total


def head_expand(width, head_size):
    row, column = iota((LANES, width), 0), iota((LANES, width), 1)
    return jnp.logical_and(column >= row * head_size, column < (row + 1) * head_size).astype(F32)


def live_rows(flag_ref, item, items, patches, lats, columns):
    row = iota((patches + lats, columns), 0)
    media = jnp.logical_and(row < patches, flag_ref[item] > 0)
    return jnp.logical_or(media, jnp.logical_and(row >= patches, flag_ref[items] > 0))


def join_kernel(key_ref, value_ref, *out_refs, width):
    groups = key_ref.shape[1] // width // len(out_refs)
    for c, out_ref in enumerate(out_refs):
        for g in range(groups):
            columns = slice((c * groups + g) * width, (c * groups + g + 1) * width)
            out_ref[:, 2 * g * width : (2 * g + 1) * width] = key_ref[:, columns]
            out_ref[:, (2 * g + 1) * width : (2 * g + 2) * width] = value_ref[:, columns]


def norm_kernel(media_ref, time_ref, gain_ref, bias_ref, lat_ref, out_ref, *, steps, per_item):
    step = pl.program_id(0)

    @pl.when(step < steps)
    def _():
        rows = media_ref[...].astype(F32) + time_ref[pl.ds(step // per_item, 1), :]
        out_ref[...] = layer_norm(rows, gain_ref[...], bias_ref[...]).astype(BF16)

    @pl.when(step == steps)
    def _():
        out_ref[...] = lat_ref[...]


def forward_kernel(
    flag_ref, both_ref, query_ref, top_ref, *refs, items, patches, scale, head_size, heads,
):
    message_refs, (part_ref, mark_ref) = refs[:-2], refs[-2:]
    lats, width = query_ref.shape
    frames = len(message_refs)
    own = message_refs[0].shape[0]
    row_total = own // items
    masks = head_masks(lats, width, head_size)
    queries = spread_heads(query_ref[...].astype(F32), masks).astype(BF16)
    base = items * patches
    lat_both = both_ref[base : base + lats, :]
    group = pl.program_id(0)
    term, lane = iota((16, GROUP * LANES), 0), iota((16, GROUP * LANES), 1)
    place = jnp.logical_and(
        lane % LANES == term * heads + group * GROUP + lane // LANES, term < 9
    ).astype(BF16)
    for i in range(items):
        both = jnp.concatenate([both_ref[i * patches : (i + 1) * patches, :], lat_both], 0)
        live = live_rows(flag_ref, i, items, patches, lats, queries.shape[0])
        scores = scale * transposed_right(both[:, :width], queries)
        masked = jnp.where(live, scores, MASKED)
        top = jnp.max(masked, axis=0, keepdims=True)
        block_exp = jnp.where(live, jnp.exp(masked - top), 0.0)
        total = jnp.sum(block_exp, axis=0, keepdims=True)
        moment = jnp.sum(block_exp * scores, axis=0, keepdims=True)
        part = transposed_left(block_exp.astype(BF16), both[:, width:])
        part_ref[i] = collect_heads(part, masks)
        top_ref[0, i] = jnp.broadcast_to(top, top_ref.shape[2:])
        terms = jnp.concatenate(
            [t.astype(F32) for x in (top, total, moment) for t in split_terms(x)]
            + [jnp.zeros((7, top.shape[1]), F32)],
            0,
        ).astype(BF16)
        wide = transposed_left(terms, place)
        mark = wide[:lats, :LANES]
        for h in range(1, GROUP):
            mark = mark + wide[h * lats : (h + 1) * lats, h * LANES : (h + 1) * LANES]
        mark_ref[i] = mark

    end = message_refs[0].shape[1] - LANES
    for s, message_ref in enumerate(message_refs):
        start = pl.multiple_of(lax.rem(flag_ref[items + 1] + s, frames) * row_total, row_total)
        rows = pl.ds(start, row_total)
        block = jnp.concatenate([part_ref[i, rows, :] for i in range(items)], 0).astype(BF16)
        mark = jnp.concatenate([mark_ref[i, rows, :] for i in range(items)], 0).astype(BF16)
        for g in range(end // width):

            @pl.when(group == g)
            def _():
                message_ref[:, g * width : (g + 1) * width] = block
                if g == 0:
                    message_ref[:, end:] = mark
                else:
                    message_ref[:, end:] = message_ref[:, end:] + mark


def merge_kernel(*refs, chunks, frames, items, head_size, heads):
    message_refs = refs[: chunks * frames]
    base_ref, weight_ref, gain_ref, bias_ref = refs[chunks * frames : chunks * frames + 4]
    merged_ref, attended_ref, mid_ref, ffn_ref, log_ref, entropy_ref = refs[chunks * frames + 4 :]
    own, columns = message_refs[0].shape
    half = columns - LANES
    lane, column = iota((LANES, 3 * LANES), 0), iota((LANES, 3 * LANES), 1)
    gather = jnp.logical_and(
        jnp.logical_and(lane // heads // 3 == column // LANES, lane % heads == column % LANES),
        lane < 9 * heads,
    ).astype(BF16)
    expand = head_expand(half, head_size)
    live = iota((own, LANES), 1) < heads
    spread = jnp.zeros((own, LANES), F32)
    for c in range(chunks):
        sources = message_refs[c * frames : (c + 1) * frames]
        stats = [matmul(x[:, half:], gather) for x in sources]
        tops = [x[:, :LANES] for x in stats]
        peak = functools.reduce(jnp.maximum, tops)
        factors = [jnp.exp(t - peak) for t in tops]
        whole = sum(f * x[:, LANES : 2 * LANES] for f, x in zip(factors, stats))
        moment = sum(f * x[:, 2 * LANES :] for f, x in zip(factors, stats))
        whole = jnp.where(live, whole, 1.0)
        log_total = jnp.where(live, peak + jnp.log(whole), 0.0)
        log_ref[c] = log_total
        spread = spread + jnp.where(live, log_total - moment / whole, 0.0)
        merged = jnp.zeros((own, half), F32)
        for x, factor in zip(sources, factors):
            share = jnp.where(live, factor / whole, 0.0)
            wide = jnp.dot(share, expand, precision=HIGHEST, preferred_element_type=F32)
            merged = merged + x[:, :half].astype(F32) * wide
        merged_ref[:, c * half : (c + 1) * half] = merged
        attended_ref[:, c * half : (c + 1) * half] = merged.astype(BF16)
    entropy_ref[...] = jnp.broadcast_to(
        jnp.sum(spread, axis=1, keepdims=True) * (1.0 / HEADS), entropy_ref.shape
    )
    base = jnp.concatenate([base_ref[...]] * items, 0)
    mid = base + matmul(attended_ref[...], weight_ref[...])
    mid_ref[...] = mid
    ffn_ref[...] = layer_norm(mid, gain_ref[...], bias_ref[...]).astype(BF16)


def gelu_parts(x):
    share = 0.5 * (1.0 + lax.erf(x * (0.5**0.5)))
    slope = share + x * jnp.exp(-0.5 * x * x) * ((2.0 * jnp.pi) ** -0.5)
    return x * share, slope


def feed_kernel(flag_ref, *refs, devices, items):
    row_refs = refs[:devices]
    low_ref, up_ref, down_ref, plane_ref, plane_low_ref, result_ref = refs[devices : devices + 6]
    grad_refs = refs[devices + 6 :]
    own = row_refs[0].shape[0]
    me = flag_ref[2 * items + 2]
    for d in range(devices):
        plane_ref[d * own : (d + 1) * own, :] = row_refs[d][...]
        plane_low_ref[d * own : (d + 1) * own, :] = low_ref[jnp.bitwise_xor(me, d)]
    upward = matmul(plane_ref[...], up_ref[...])
    hidden, slope = gelu_parts(upward)
    grad_up = (slope * transposed_right(plane_low_ref[...], down_ref[...])).astype(BF16)
    grad = transposed_right(grad_up, up_ref[...]).astype(BF16)
    result = matmul(hidden.astype(BF16), down_ref[...]).astype(BF16)
    for d in range(devices):
        grad_refs[d][...] = grad[d * own : (d + 1) * own, :]
        result_ref[jnp.bitwise_xor(me, d)] = result[d * own : (d + 1) * own, :]


def feed_grad_kernel(
    plane_ref, plane_low_ref, other_ref, other_low_ref, up_ref, down_ref, down_grad_ref, up_grad_ref,
    total_ref, *, plane_blocks,
):
    step = pl.program_id(0)
    near = step < plane_blocks
    rows = jnp.where(near, plane_ref[...], other_ref[...])
    low = jnp.where(near, plane_low_ref[...], other_low_ref[...])
    hidden, slope = gelu_parts(matmul(rows, up_ref[...]))
    grad_up = (slope * transposed_right(low, down_ref[...])).astype(BF16)
    down_part = transposed_left(hidden.astype(BF16), low)
    up_part = transposed_left(rows, grad_up)

    @pl.when(step == 0)
    def _():
        down_grad_ref[...] = down_part
        total_ref[...] = up_part

    @pl.when(step > 0)
    def _():
        down_grad_ref[...] += down_part
        total_ref[...] += up_part

    @pl.when(step == pl.num_programs(0) - 1)
    def _():
        up_grad_ref[...] = total_ref[...].astype(BF16)


def norm_backward(rows, gain, gradient):
    center = rows - jnp.mean(rows, axis=1, keepdims=True)
    rate = lax.rsqrt(jnp.mean(center * center, axis=1, keepdims=True) + EPSILON)
    unit = center * rate
    scaled = gradient * gain
    inner = scaled - jnp.mean(scaled, axis=1, keepdims=True)
    back = rate * (inner - unit * jnp.mean(scaled * unit, axis=1, keepdims=True))
    return (
        back,
        jnp.sum(gradient * unit, axis=0, keepdims=True),
        jnp.sum(gradient, axis=0, keepdims=True),
    )


def turn_kernel(*refs, devices, items, chunks, head_size, heads):
    part_refs = refs[:devices]
    mid_ref, cotangent_ref, gain_ref, merged_ref, log_ref, weight_ref = refs[
        devices : devices + 6
    ]
    message_ref, branch_ref, base_ref, sums_ref = refs[devices + 6 :]
    own, width = mid_ref.shape
    half = width // chunks
    gradient = total_of([x[...] for x in part_refs])
    back, gain_sum, bias_sum = norm_backward(mid_ref[...], gain_ref[...], gradient)
    grad_mid = cotangent_ref[...] + back
    sums_ref[...] = jnp.zeros(sums_ref.shape, F32)
    sums_ref[0:1, :] = gain_sum
    sums_ref[1:2, :] = bias_sum
    row_total = own // items
    base_ref[...] = total_of(
        [grad_mid[i * row_total : (i + 1) * row_total] for i in range(items)]
    )
    branch = grad_mid.astype(BF16)
    branch_ref[...] = branch
    grad_att = transposed_right(branch, weight_ref[...]).astype(BF16)
    expand = head_expand(half, head_size)
    lane, column = iota((6 * LANES, LANES), 0), iota((6 * LANES, LANES), 1)
    place = jnp.logical_and(
        lane % LANES < heads, column == (lane // LANES) * heads + lane % LANES
    ).astype(BF16)
    message_ref[:, :width] = grad_att
    for c in range(chunks):
        columns = slice(c * half, (c + 1) * half)
        delta = lax.dot_general(
            merged_ref[:, columns] * grad_att[:, columns].astype(F32),
            expand,
            (((1,), (1,)), ((), ())),
            precision=HIGHEST,
            preferred_element_type=F32,
        )
        terms = jnp.concatenate([t for x in (log_ref[c], delta) for t in split_terms(x)], 1)
        message_ref[:, width + c * LANES : width + (c + 1) * LANES] = matmul(
            terms, place
        ).astype(BF16)


def backward_kernel(
    *refs, frames, items, patches, scale, head_size, heads,
):
    flag_ref, both_ref, query_ref, top_ref = refs[:4]
    grad_refs = refs[4 : 4 + frames]
    mark_refs = refs[4 + frames : 4 + 2 * frames]
    out_ref, sum_ref, held_ref, note_ref = refs[4 + 2 * frames :]
    lats, width = query_ref.shape
    own = grad_refs[0].shape[0]
    row_total = own // items
    base = items * patches
    for s in range(frames):
        source = lax.rem(flag_ref[items + 1] + (frames - s), frames)
        rows = pl.ds(pl.multiple_of(source * row_total, row_total), row_total)
        block = grad_refs[s][...].astype(F32)
        mark = mark_refs[s][...].astype(F32)
        for i in range(items):
            held_ref[i, rows, :] = block[i * row_total : (i + 1) * row_total]
            note_ref[i, rows, :] = mark[i * row_total : (i + 1) * row_total]
    masks = head_masks(lats, width, head_size)
    queries = spread_heads(query_ref[...].astype(F32), masks).astype(BF16)
    lat_both = both_ref[base : base + lats, :]
    row, lane = iota((GROUP * 8, LANES), 0), iota((GROUP * 8, LANES), 1)
    pick = jnp.logical_and(
        jnp.logical_and(
            lane // heads // 3 == row % 8,
            lane % heads == pl.program_id(0) * GROUP + row // 8,
        ),
        lane < 6 * heads,
    ).astype(BF16)
    grad_query = jnp.zeros((queries.shape[0], width), F32)
    lat_grad_key = jnp.zeros((lats, width), F32)
    lat_grad_value = jnp.zeros((lats, width), F32)
    for i in range(items):
        rows = slice(i * patches, (i + 1) * patches)
        stats = transposed_right(pick, note_ref[i].astype(BF16))
        stats = jnp.concatenate([stats[h * 8 : (h + 1) * 8] for h in range(GROUP)], 1)
        log_total = stats[0:1]
        delta = stats[1:2]
        top = top_ref[0, i, 0:1, :]
        rescale = jnp.exp(top - log_total)
        both = jnp.concatenate([both_ref[rows, :], lat_both], 0)
        keys, values = both[:, :width], both[:, width:]
        grads = spread_heads(held_ref[i], masks).astype(BF16)
        live = live_rows(flag_ref, i, items, patches, lats, queries.shape[0])
        masked = jnp.where(live, scale * transposed_right(keys, queries), MASKED)
        probs = jnp.where(live, jnp.exp(masked - log_total), 0.0)
        block_exp = jnp.where(live, jnp.exp(masked - top), 0.0)
        weights = (block_exp.astype(BF16).astype(F32) * rescale).astype(BF16)
        grad_scores = (probs * (transposed_right(values, grads) - delta)).astype(BF16)
        grad_key = scale * matmul(grad_scores, queries)
        grad_value = matmul(weights, grads)
        out_ref[rows, :width] = grad_key[:patches].astype(BF16)
        out_ref[rows, width:] = grad_value[:patches].astype(BF16)
        grad_query = grad_query + transposed_left(grad_scores, keys)
        lat_grad_key = lat_grad_key + grad_key[patches:]
        lat_grad_value = lat_grad_value + grad_value[patches:]
    out_ref[base : base + lats, :width] = lat_grad_key.astype(BF16)
    out_ref[base : base + lats, width:] = lat_grad_value.astype(BF16)
    sum_ref[...] = scale * collect_heads(grad_query, masks)


def media_kernel(flag_ref, *refs, chunks, items, frames, first, latent):
    grad_refs, lat_refs, weight_refs = [
        refs[k * chunks : (k + 1) * chunks] for k in range(3)
    ]
    media_ref, time_ref, gain_ref = refs[3 * chunks : 3 * chunks + 3]
    out_ref, sums_ref = refs[3 * chunks + 3 + latent : 3 * chunks + 5 + latent]
    step = pl.program_id(0)
    item = first + step

    @pl.when(step == 0)
    def _():
        sums_ref[...] = jnp.zeros(sums_ref.shape, F32)
        if latent:
            refs[-1][...] = functools.reduce(
                jnp.add,
                [transposed_right(g[...], w[...]) for g, w in zip(lat_refs, weight_refs)],
            )

    gradient = functools.reduce(
        jnp.add, [transposed_right(g[...], w[...]) for g, w in zip(grad_refs, weight_refs)]
    )
    inputs = media_ref[...].astype(F32) + time_ref[pl.ds(item, 1), :]
    back, gain_sum, bias_sum = norm_backward(inputs, gain_ref[...], gradient)
    out_ref[...] = back.astype(BF16)
    place = iota((frames, 1), 0) == flag_ref[items + 2 + item]
    sums_ref[0:frames, :] += jnp.where(place, jnp.sum(back, axis=0, keepdims=True), 0.0)
    sums_ref[8:9, :] += gain_sum
    sums_ref[9:10, :] += bias_sum


def latent_kernel(flag_ref, *refs, chunks, items):
    query_refs = refs[:chunks]
    (
        product_ref, query_weight_ref, latent_ref, gain_ref, base_ref, ffn_ref, media_ref, more_ref,
        out_ref,
    ) = refs[chunks:]
    lats, width = latent_ref.shape
    half = width // chunks
    gradient = product_ref[...]
    for c in range(chunks):
        gradient = gradient + transposed_right(
            query_refs[c][...].astype(BF16), query_weight_ref[:, c * half : (c + 1) * half]
        )
        out_ref[lats : 2 * lats, c * half : (c + 1) * half] = query_refs[c][...]
    back, gain_sum, bias_sum = norm_backward(latent_ref[...], gain_ref[...], gradient)
    out_ref[:lats, :] = back
    row_total = base_ref.shape[0]
    start = pl.multiple_of(flag_ref[items + 1] * row_total, row_total)
    out_ref[pl.ds(start, row_total), :] += base_ref[...]
    at = 2 * lats
    out_ref[at : at + 8, :] = ffn_ref[...]
    out_ref[at + 2 : at + 3, :] = gain_sum
    out_ref[at + 3 : at + 4, :] = bias_sum
    out_ref[at + 8 : at + 24, :] = media_ref[...] + more_ref[...]
    out_ref[at + 24 :, :] = jnp.zeros((out_ref.shape[0] - at - 24, width), F32)


def place_kernel(flag_ref, *refs, chunks, frames, items, groups):
    chunk_refs = refs[: chunks * frames]
    key_ref, value_ref, out_ref = refs[chunks * frames :]
    width = key_ref.shape[2] // (chunks * groups)
    for s in range(frames):
        source = lax.rem(flag_ref[items + 1] + (frames - s), frames)
        out_ref[source] = chunk_refs[s][:, 2 * groups * width :].astype(F32)
        for c in range(chunks):
            for g in range(groups):
                at = (c * groups + g) * width
                block = chunk_refs[c * frames + s][:, 2 * g * width : 2 * (g + 1) * width]
                block = block.astype(F32)
                key_ref[source, :, at : at + width] = block[:, :width]
                value_ref[source, :, at : at + width] = block[:, width:]


def body(
    media,
    cotangent,
    frame_count,
    frame_start,
    latents,
    time_embed,
    media_gain,
    media_bias,
    latent_gain,
    latent_bias,
    ffn_gain,
    ffn_bias,
    query_weight,
    key_weight,
    value_weight,
    out_weight,
    up_weight,
    down_weight,
):
    items = media.shape[0]
    patches = media.shape[2]
    width = media.shape[3]
    lats = latents.shape[0]
    frame_total = time_embed.shape[0]
    row_total = cotangent.shape[1]
    own = items * row_total
    head_size = width // HEADS
    half = width // CHUNKS
    chunk_heads = HEADS // CHUNKS
    group_width = GROUP * head_size
    groups = chunk_heads // GROUP
    stack = GROUP * lats
    tokens = items * patches
    all_tokens = tokens + lats
    shard = query_weight.shape[0]
    hidden_shard = down_weight.shape[0]
    item_size = lax.axis_size("items")
    frame_size = lax.axis_size("frames")
    plane = item_size * own
    item_index = lax.axis_index("items")
    slot = lax.axis_index("frames")
    row_base = slot * row_total
    params = pltpu.CompilerParams(vmem_limit_bytes=56 * 2**20)
    smem = pl.BlockSpec(memory_space=pltpu.SMEM)
    whole = pl.BlockSpec(memory_space=pltpu.VMEM)
    sizes = dict(items=items, head_size=head_size, heads=chunk_heads)

    def struct(shape, kind):
        return jax.ShapeDtypeStruct(shape, kind)

    short = pl.CostEstimate(flops=1000, bytes_accessed=1000, transcendentals=0)

    joined = pl.pallas_call(
        functools.partial(join_kernel, width=group_width),
        out_shape=[struct((shard, 2 * half), BF16)] * CHUNKS,
        cost_estimate=short,
        compiler_params=params,
    )(key_weight, value_weight)
    kv_parts = [lax.all_gather(joined[0], "items", axis=0, tiled=True)]

    lat_norm = layer_norm(latents, latent_gain, latent_bias).astype(BF16)
    lat_cols = lax.dynamic_slice_in_dim(lat_norm, item_index * shard, shard, 1)

    def column_blocks(x):
        return jnp.transpose(x.reshape(-1, item_size, shard), (1, 0, 2))

    def scatter_exchange(x, axis):
        return jnp.sum(lax.all_to_all(x, axis, 0, 0).astype(F32), axis=0)

    query_cols = scatter_exchange(column_blocks(matmul(lat_cols, query_weight)), "items")
    query_cols = jnp.broadcast_to(query_cols.astype(BF16)[None], (item_size, lats, shard))
    queries = jnp.transpose(lax.all_to_all(query_cols, "items", 0, 0), (1, 0, 2)).reshape(
        lats, width
    )

    counts = lax.dynamic_slice_in_dim(frame_count, item_index * items, items)
    starts = lax.dynamic_slice_in_dim(frame_start, item_index * items, items)
    offset = (slot - starts) % frame_total
    flags = jnp.concatenate(
        [
            (offset < counts).astype(jnp.int32),
            (slot == 0).astype(jnp.int32)[None],
            slot.astype(jnp.int32)[None],
            offset.astype(jnp.int32),
            item_index.astype(jnp.int32)[None],
        ]
    )
    picker = (offset[:, None] == jnp.arange(frame_total, dtype=jnp.int32)[None, :]).astype(F32)
    time_rows = jnp.dot(picker, time_embed, precision=HIGHEST, preferred_element_type=F32)
    flat_media = media.reshape(tokens, width)
    steps = tokens // lats
    all_rows = pl.pallas_call(
        functools.partial(norm_kernel, steps=steps, per_item=patches // lats),
        grid=(steps + 1,),
        in_specs=[
            pl.BlockSpec((lats, width), lambda i: (jnp.minimum(i, steps - 1), 0)),
            whole,
            whole,
            whole,
            whole,
        ],
        out_specs=pl.BlockSpec((lats, width), lambda i: (i, 0)),
        out_shape=struct((all_tokens, width), BF16),
        cost_estimate=short,
        compiler_params=params,
    )(flat_media, time_rows, media_gain[None], media_bias[None], lat_norm)

    grad_out = cotangent.reshape(own, width)
    grad_low = grad_out.astype(BF16)
    low_shift = spread_on(grad_low, "frames")[1:]
    kv_parts.append(
        lax.all_gather(after(joined[1], lat_norm), "items", axis=0, tiled=True)
    )
    out_full = lax.all_gather(after(out_weight, all_rows), "items", axis=0, tiled=True)

    chip, core = item_index // 2, item_index % 2
    rows_across = all_rows.T.reshape(item_size // 2, 2, shard, all_tokens)
    send_rows, keep_rows = [
        jnp.concatenate(
            [
                lax.dynamic_slice(
                    rows_across, (chip ^ k, which, 0, 0), (1, 1, shard, all_tokens)
                ).reshape(shard, all_tokens)
                for k in range(item_size // 2)
            ],
            0,
        )
        for which in (1 - core, core)
    ]

    boths, tops, messages = [], [], []
    for c in range(CHUNKS):

        def block_of(g, c=c):
            return (0, c * groups + g)

        if c:
            rows = after(all_rows, tops[-1])
        else:
            rows = after(all_rows, queries, send_rows, keep_rows, *low_shift)
        both = matmul(rows, kv_parts[c]).astype(BF16)
        top, *parts = pl.pallas_call(
            functools.partial(
                forward_kernel, patches=patches, scale=head_size**-0.5, **sizes
            ),
            grid=(groups,),
            in_specs=[
                smem,
                pl.BlockSpec((all_tokens, 2 * group_width), lambda g: (0, g)),
                pl.BlockSpec((lats, group_width), block_of),
            ],
            out_specs=[pl.BlockSpec((1, items, 8, stack), lambda g: (g, 0, 0, 0))]
            + [pl.BlockSpec((own, half + LANES), lambda g: (0, 0))] * frame_size,
            out_shape=[struct((groups, items, 8, stack), F32)]
            + [struct((own, half + LANES), BF16)] * frame_size,
            scratch_shapes=[
                pltpu.VMEM((items, lats, group_width), F32),
                pltpu.VMEM((items, lats, LANES), F32),
            ],
            cost_estimate=short,
            compiler_params=params,
        )(flags, both, queries)
        boths.append(both)
        tops.append(top)
        messages += [p if s == 0 else send_on(p, "frames", s) for s, p in enumerate(parts)]
    up_slice = lax.all_to_all(after(up_weight, messages[frame_size + 1]), "items", 1, 0, tiled=True)
    low_every = lax.all_gather(after(grad_low, boths[0]), "items", axis=0)
    low_other = lax.all_gather(
        after(jnp.stack(low_shift), boths[1]), "items", axis=0
    ).reshape(-1, width)

    base_rows = lax.dynamic_slice_in_dim(latents, row_base, row_total, 0)
    merged, attended, mid_rows, ffn_in, logs, entropy_wide = pl.pallas_call(
        functools.partial(merge_kernel, chunks=CHUNKS, frames=frame_size, **sizes),
        out_shape=[
            struct((own, width), F32),
            struct((own, width), BF16),
            struct((own, width), F32),
            struct((own, width), BF16),
            struct((CHUNKS, own, LANES), F32),
            struct((own, LANES), F32),
        ],
        cost_estimate=short,
        compiler_params=params,
    )(*messages, base_rows, out_full, ffn_gain[None], ffn_bias[None])
    entropy = entropy_wide[:, 0].reshape(items, row_total)

    ffn_blocks = spread_across(ffn_in, "items")
    ffn_plane, low_plane, result_part, *parts = pl.pallas_call(
        functools.partial(feed_kernel, devices=item_size, items=items),
        in_specs=[smem] + [whole] * (item_size + 3),
        out_shape=[struct((plane, width), BF16)] * 2
        + [struct((item_size, own, width), BF16)]
        + [struct((own, width), BF16)] * item_size,
        cost_estimate=short,
        compiler_params=params,
    )(flags, *ffn_blocks, low_every, up_slice, down_weight)
    grad_blocks = collect_across(parts, "items")
    ffn_shift = spread_on(after(ffn_in, grad_blocks[1]), "frames")[1:]
    grad_blocks[0] = after(grad_blocks[0], *ffn_shift)

    turn, grad_branch, grad_base, ffn_sums = pl.pallas_call(
        functools.partial(turn_kernel, devices=item_size, chunks=CHUNKS, **sizes),
        out_shape=[
            struct((own, width + CHUNKS * LANES), BF16),
            struct((own, width), BF16),
            struct((row_total, width), F32),
            struct((8, width), F32),
        ],
        cost_estimate=short,
        compiler_params=params,
    )(*grad_blocks, mid_rows, grad_out, ffn_gain[None], merged, logs, out_full)
    turns = spread_on(turn, "frames")
    branch_plane = lax.all_gather(grad_branch, "items", axis=0, tiled=True)
    ffn_other = lax.all_gather(
        after(jnp.stack(ffn_shift), grad_branch), "items", axis=0
    ).reshape(-1, width)
    query_full = lax.all_gather(after(query_weight, ffn_plane), "items", axis=0, tiled=True)
    att_plane = lax.all_to_all(after(attended, turns[1]), "items", 1, 0, tiled=True)
    turns[0] = after(turns[0], att_plane, low_other)

    chunk_grads, chunk_queries, pieces = [], [], []

    def chip_pieces(keep, received):
        sums = [keep[k].astype(F32) + received[k].astype(F32) for k in range(item_size // 2)]
        return sums[:1] + [p.astype(BF16) for p in sums[1:]]

    def send_pieces(sums):
        return sums[:1] + [
            send_across(p, "items", 2 * k) for k, p in enumerate(sums) if k
        ]

    for c in range(CHUNKS):

        def block_of(g, c=c):
            return (0, c * groups + g)

        chunk_grad, chunk_query = pl.pallas_call(
            functools.partial(
                backward_kernel, frames=frame_size, patches=patches, scale=head_size**-0.5, **sizes
            ),
            grid=(groups,),
            in_specs=[
                smem,
                pl.BlockSpec((all_tokens, 2 * group_width), lambda g: (0, g)),
                pl.BlockSpec((lats, group_width), block_of),
                pl.BlockSpec((1, items, 8, stack), lambda g: (g, 0, 0, 0)),
            ]
            + [pl.BlockSpec((own, group_width), block_of)] * frame_size
            + [pl.BlockSpec((own, LANES), lambda g, c=c: (0, width // LANES + c))] * frame_size,
            out_specs=[
                pl.BlockSpec((all_tokens, 2 * group_width), lambda g: (0, g)),
                pl.BlockSpec((lats, group_width), lambda g: (0, g)),
            ],
            out_shape=[
                struct((all_tokens, 2 * half), BF16),
                struct((lats, half), F32),
            ],
            scratch_shapes=[
                pltpu.VMEM((items, lats, group_width), F32),
                pltpu.VMEM((items, lats, LANES), F32),
            ],
            cost_estimate=short,
            compiler_params=params,
        )(flags, after(boths[c], keep) if c else boths[c], queries, tops[c], *turns, *turns)
        if c:
            pieces.append(chip_pieces(keep, received))
            term_grad = after(chunk_grad, *pieces[-1])
        else:
            term_grad = chunk_grad
        send = matmul(send_rows, term_grad).astype(BF16)
        received = send_across(send, "items", 1).reshape(-1, shard, 2 * half)
        keep = matmul(after(keep_rows, send), term_grad).astype(BF16)
        keep = keep.reshape(-1, shard, 2 * half)
        chunk_grads.append(chunk_grad)
        chunk_queries.append(chunk_query)
    first_total = total_of(send_pieces(pieces[0]))
    result_pieces = lax.all_to_all(after(result_part, keep), "items", 0, 0)

    media_parts = items // 2
    media_grads, media_sums = [], []
    ready = (keep,)
    for m in range(2):
        lat = m == 1

        def part_block(i, m=m):
            return (m * media_parts + i, 0)

        last_block = pl.BlockSpec((lats, 2 * half), lambda i: (tokens // lats, 0))
        parts = pl.pallas_call(
            functools.partial(
                media_kernel, chunks=CHUNKS, items=items, frames=frame_total,
                first=m * media_parts, latent=lat,
            ),
            grid=(media_parts,),
            in_specs=[smem]
            + [pl.BlockSpec((patches, 2 * half), part_block)] * CHUNKS
            + [last_block] * CHUNKS
            + [whole] * CHUNKS
            + [pl.BlockSpec((patches, width), part_block), whole, whole]
            + [pl.BlockSpec(memory_space=pl.ANY)] * lat,
            out_specs=[
                pl.BlockSpec((patches, width), part_block),
                pl.BlockSpec((16, width), lambda i: (0, 0)),
            ]
            + [pl.BlockSpec((lats, width), lambda i: (0, 0))] * lat,
            out_shape=[
                struct((tokens, width), BF16),
                struct((16, width), F32),
            ]
            + [struct((lats, width), F32)] * lat,
            input_output_aliases={3 * CHUNKS + 4: 0} if lat else {},
            cost_estimate=short,
            compiler_params=params,
        )(
            flags,
            *chunk_grads[:-1],
            after(chunk_grads[-1], *ready),
            *chunk_grads,
            *kv_parts,
            flat_media,
            time_rows,
            media_gain[None],
            *media_grads,
        )
        media_grads.append(parts[0])
        media_sums.append(parts[1])
        if m == 0:
            pieces.append(chip_pieces(keep, received))
            out_part = transposed_left(att_plane, branch_plane)
            first_rows = scatter_rows(
                jnp.concatenate([first_total, after(out_part, parts[1])], 1), "frames"
            )
            ready = (first_rows[0], *pieces[-1])
    media_grad = media_grads[-1]

    sum_rows = 2 * lats + 24
    sum_rows += -sum_rows % (8 * item_size)
    payload = pl.pallas_call(
        functools.partial(latent_kernel, chunks=CHUNKS, items=items),
        in_specs=[smem] + [whole] * (CHUNKS + 8),
        out_specs=whole,
        out_shape=struct((sum_rows, width), F32),
        cost_estimate=short,
        compiler_params=params,
    )(
        flags,
        *chunk_queries,
        parts[2],
        query_full,
        latents,
        latent_gain[None],
        grad_base,
        ffn_sums,
        *media_sums,
    )
    payload_part = lax.psum_scatter(payload, "items", scatter_dimension=0, tiled=True)
    last_total = total_of(send_pieces(pieces[-1]))

    block_rows = min(512, plane)
    plane_blocks = plane // block_rows
    near = pl.BlockSpec((block_rows, width), lambda i: (jnp.minimum(i, plane_blocks - 1), 0))
    far = pl.BlockSpec((block_rows, width), lambda i: (jnp.maximum(i - plane_blocks, 0), 0))
    down_grad, up_part = pl.pallas_call(
        functools.partial(feed_grad_kernel, plane_blocks=plane_blocks),
        grid=(plane_blocks * frame_size,),
        in_specs=[near, near, far, far, whole, whole],
        out_specs=[
            pl.BlockSpec((hidden_shard, width), lambda i: (0, 0)),
            pl.BlockSpec((width, hidden_shard), lambda i: (0, 0)),
        ],
        out_shape=[struct((hidden_shard, width), F32), struct((width, hidden_shard), BF16)],
        scratch_shapes=[pltpu.VMEM((width, hidden_shard), F32)],
        cost_estimate=short,
        compiler_params=params,
    )(
        ffn_plane,
        low_plane,
        after(ffn_other, payload, *first_rows[:1]),
        low_other,
        up_slice,
        down_weight,
    )
    up_grad = lax.all_to_all(up_part, "items", 0, 1, tiled=True).astype(F32)

    first_rows[0] = after(first_rows[0], up_part)
    first_placed = spread_on(total_of(first_rows).astype(BF16), "frames")
    last_rows = scatter_rows(last_total, "frames")
    last_placed = spread_on(total_of(last_rows).astype(BF16), "frames")
    placed = first_placed + last_placed
    key_grad, value_grad, out_grad = pl.pallas_call(
        functools.partial(
            place_kernel, chunks=CHUNKS, frames=frame_size, items=items, groups=groups
        ),
        in_specs=[smem] + [whole] * len(placed),
        out_specs=[whole] * 3,
        out_shape=[struct((frame_size, shard // frame_size, width), F32)] * 3,
        cost_estimate=short,
        compiler_params=params,
    )(flags, *placed)

    payload_others = spread_on(payload_part.astype(BF16), "frames")[1:]
    sums = lax.all_gather(
        total_of([payload_part] + payload_others), "items", axis=0, tiled=True
    )
    latents_grad = sums[:lats]
    query_grad = transposed_left(lat_cols, sums[lats : 2 * lats].astype(BF16))
    at = 2 * lats
    column_sums = lax.dynamic_slice_in_dim(
        sums[at + 8 : at + 24], item_index * shard, shard, 1
    )

    result = mid_rows + total_of([result_pieces[d] for d in range(item_size)])
    return (
        result.reshape(items, row_total, width),
        entropy,
        media_grad.reshape(media.shape),
        latents_grad,
        column_sums[:frame_total],
        column_sums[8],
        column_sums[9],
        sums[at + 2],
        sums[at + 3],
        sums[at],
        sums[at + 1],
        query_grad,
        key_grad.reshape(shard, width),
        value_grad.reshape(shard, width),
        out_grad.reshape(shard, width),
        up_grad,
        down_grad,
    )


def solution(mesh):
    return jax.shard_map(
        body,
        mesh=mesh,
        in_specs=(
            P("items", "frames", None, None),
            P("items", "frames", None),
            P(),
            P(),
            P(),
            P(),
            P(),
            P(),
            P(),
            P(),
            P(),
            P(),
            P("items", None),
            P("items", None),
            P("items", None),
            P("items", None),
            P("items", None),
            P("items", None),
        ),
        out_specs=(
            P("items", "frames", None),
            P("items", "frames"),
            P("items", "frames", None, None),
            P(),
            P(None, "items"),
            P("items"),
            P("items"),
            P(),
            P(),
            P(),
            P(),
            P("items", None),
            P("items", None),
            P("items", None),
            P("items", None),
            P("items", None),
            P("items", None),
        ),
        check_vma=False,
    )
```

```python
import functools
import math

import jax
import jax.numpy as jnp
from jax import lax
from jax.experimental import pallas as pl
from jax.experimental.pallas import tpu as pltpu
from jax.sharding import PartitionSpec as P

HEADS = 16
GROUP = 4
CHUNKS = 2
LANES = 128
EPSILON = 1e-05
MASKED = -1e30
F32 = jnp.float32
BF16 = jnp.bfloat16
HIGHEST = lax.Precision.HIGHEST


def layer_norm(inputs, norm_gain, norm_bias):
    center = inputs - jnp.mean(inputs, axis=-1, keepdims=True)
    spread = jnp.mean(center * center, axis=-1, keepdims=True)
    return center * lax.rsqrt(spread + EPSILON) * norm_gain + norm_bias


def matmul(left_side, right_side):
    return jnp.dot(left_side, right_side, preferred_element_type=F32)


def transposed_left(left_side, right_side):
    return lax.dot_general(
        left_side, right_side, (((0,), (0,)), ((), ())), preferred_element_type=F32
    )


def transposed_right(left_side, right_side):
    return lax.dot_general(
        left_side, right_side, (((1,), (1,)), ((), ())), preferred_element_type=F32
    )


def send_on(x, axis, step):
    size = lax.axis_size(axis)
    return lax.ppermute(x, axis, [(i, (i + step) % size) for i in range(size)])


def send_across(x, axis, distance):
    return lax.ppermute(x, axis, [(i, i ^ distance) for i in range(lax.axis_size(axis))])


def spread_on(x, axis):
    return [x] + [send_on(x, axis, s) for s in range(1, lax.axis_size(axis))]


def spread_across(x, axis):
    return [x] + [send_across(x, axis, d) for d in range(1, lax.axis_size(axis))]


def collect_across(pieces, axis):
    return [pieces[0]] + [send_across(p, axis, d) for d, p in enumerate(pieces) if d]


def total_of(pieces):
    return functools.reduce(jnp.add, [p.astype(F32) for p in pieces])


def after(x, *earlier):
    return lax.optimization_barrier((x,) + earlier)[0]


def split_terms(x):
    high = x.astype(BF16)
    rest = x - high.astype(F32)
    middle = rest.astype(BF16)
    return high, middle, (rest - middle.astype(F32)).astype(BF16)


def iota(shape, dim):
    return lax.broadcasted_iota(jnp.int32, shape, dim)


def head_masks(rows, width, head_size):
    lane = iota((rows, width), 1)
    return [
        jnp.logical_and(lane >= h * head_size, lane < (h + 1) * head_size)
        for h in range(width // head_size)
    ]


def spread_heads(block, masks):
    return jnp.concatenate([jnp.where(m, block, jnp.zeros_like(block)) for m in masks], 0)


def collect_heads(block, masks):
    rows = block.shape[0] // len(masks)
    total = jnp.where(masks[0], block[:rows], 0.0)
    for h in range(1, len(masks)):
        total = total + jnp.where(masks[h], block[h * rows : (h + 1) * rows], 0.0)
    return total


def head_expand(width, head_size):
    row, column = iota((LANES, width), 0), iota((LANES, width), 1)
    return jnp.logical_and(column >= row * head_size, column < (row + 1) * head_size).astype(F32)


def live_rows(flag_ref, item, items, patches, lats, columns):
    row = iota((patches + lats, columns), 0)
    media = jnp.logical_and(row < patches, flag_ref[item] > 0)
    return jnp.logical_or(media, jnp.logical_and(row >= patches, flag_ref[items] > 0))


def pack_shape(own, shard, width):
    unit = math.gcd(own, shard)
    return unit, width * unit // shard


def join_kernel(key_ref, value_ref, cotangent_ref, out_ref, low_ref, *, width):
    for g in range(key_ref.shape[1] // width):
        columns = slice(g * width, (g + 1) * width)
        out_ref[:, 2 * g * width : (2 * g + 1) * width] = key_ref[:, columns]
        out_ref[:, (2 * g + 1) * width : (2 * g + 2) * width] = value_ref[:, columns]
    low = cotangent_ref[...].astype(BF16)
    low_ref[...] = low
    own, span = low.shape
    unit, piece = pack_shape(own, out_ref.shape[0], span)
    for a in range(own // unit):
        for b in range(span // piece):
            at = 2 * span + a * piece
            out_ref[b * unit : (b + 1) * unit, at : at + piece] = low[
                a * unit : (a + 1) * unit, b * piece : (b + 1) * piece
            ]


def norm_kernel(media_ref, time_ref, gain_ref, bias_ref, lat_ref, out_ref, *, steps, per_item):
    step = pl.program_id(0)

    @pl.when(step < steps)
    def _():
        rows = media_ref[...].astype(F32) + time_ref[pl.ds(step // per_item, 1), :]
        out_ref[...] = layer_norm(rows, gain_ref[...], bias_ref[...]).astype(BF16)

    @pl.when(step == steps)
    def _():
        out_ref[...] = lat_ref[...]


def forward_kernel(
    flag_ref, both_ref, query_ref, top_ref, *refs, items, patches, scale, head_size, heads,
):
    message_refs, (part_ref, mark_ref) = refs[:-2], refs[-2:]
    lats, width = query_ref.shape
    frames = len(message_refs)
    own = message_refs[0].shape[0]
    row_total = own // items
    masks = head_masks(lats, width, head_size)
    queries = spread_heads(query_ref[...].astype(F32), masks).astype(BF16)
    base = items * patches
    lat_both = both_ref[base : base + lats, :]
    group = pl.program_id(0)
    term, lane = iota((16, GROUP * LANES), 0), iota((16, GROUP * LANES), 1)
    place = jnp.logical_and(
        lane % LANES == term * heads + group * GROUP + lane // LANES, term < 9
    ).astype(BF16)
    for i in range(items):
        both = jnp.concatenate([both_ref[i * patches : (i + 1) * patches, :], lat_both], 0)
        live = live_rows(flag_ref, i, items, patches, lats, queries.shape[0])
        scores = scale * transposed_right(both[:, :width], queries)
        masked = jnp.where(live, scores, MASKED)
        top = jnp.max(masked, axis=0, keepdims=True)
        block_exp = jnp.where(live, jnp.exp(masked - top), 0.0)
        total = jnp.sum(block_exp, axis=0, keepdims=True)
        moment = jnp.sum(block_exp * scores, axis=0, keepdims=True)
        part = transposed_left(block_exp.astype(BF16), both[:, width:])
        part_ref[i] = collect_heads(part, masks)
        top_ref[0, i] = jnp.broadcast_to(top, top_ref.shape[2:])
        terms = jnp.concatenate(
            [t.astype(F32) for x in (top, total, moment) for t in split_terms(x)]
            + [jnp.zeros((7, top.shape[1]), F32)],
            0,
        ).astype(BF16)
        wide = transposed_left(terms, place)
        mark = wide[:lats, :LANES]
        for h in range(1, GROUP):
            mark = mark + wide[h * lats : (h + 1) * lats, h * LANES : (h + 1) * LANES]
        mark_ref[i] = mark

    end = message_refs[0].shape[1] - LANES
    for s, message_ref in enumerate(message_refs):
        start = pl.multiple_of(lax.rem(flag_ref[items + 1] + s, frames) * row_total, row_total)
        rows = pl.ds(start, row_total)
        block = jnp.concatenate([part_ref[i, rows, :] for i in range(items)], 0).astype(BF16)
        mark = jnp.concatenate([mark_ref[i, rows, :] for i in range(items)], 0).astype(BF16)
        for g in range(end // width):

            @pl.when(group == g)
            def _():
                message_ref[:, g * width : (g + 1) * width] = block
                if g == 0:
                    message_ref[:, end:] = mark
                else:
                    message_ref[:, end:] = message_ref[:, end:] + mark


def merge_kernel(*refs, chunks, frames, items, head_size, heads):
    message_refs = refs[: chunks * frames]
    base_ref, weight_ref, gain_ref, bias_ref = refs[chunks * frames : chunks * frames + 4]
    merged_ref, attended_ref, mid_ref, ffn_ref, log_ref, entropy_ref = refs[chunks * frames + 4 :]
    own, columns = message_refs[0].shape
    half = columns - LANES
    lane, column = iota((LANES, 3 * LANES), 0), iota((LANES, 3 * LANES), 1)
    gather = jnp.logical_and(
        jnp.logical_and(lane // heads // 3 == column // LANES, lane % heads == column % LANES),
        lane < 9 * heads,
    ).astype(BF16)
    expand = head_expand(half, head_size)
    live = iota((own, LANES), 1) < heads
    spread = jnp.zeros((own, LANES), F32)
    for c in range(chunks):
        sources = message_refs[c * frames : (c + 1) * frames]
        stats = [matmul(x[:, half:], gather) for x in sources]
        tops = [x[:, :LANES] for x in stats]
        peak = functools.reduce(jnp.maximum, tops)
        factors = [jnp.exp(t - peak) for t in tops]
        whole = sum(f * x[:, LANES : 2 * LANES] for f, x in zip(factors, stats))
        moment = sum(f * x[:, 2 * LANES :] for f, x in zip(factors, stats))
        whole = jnp.where(live, whole, 1.0)
        log_total = jnp.where(live, peak + jnp.log(whole), 0.0)
        log_ref[c] = log_total
        spread = spread + jnp.where(live, log_total - moment / whole, 0.0)
        merged = jnp.zeros((own, half), F32)
        for x, factor in zip(sources, factors):
            share = jnp.where(live, factor / whole, 0.0)
            wide = jnp.dot(share, expand, precision=HIGHEST, preferred_element_type=F32)
            merged = merged + x[:, :half].astype(F32) * wide
        merged_ref[:, c * half : (c + 1) * half] = merged
        attended_ref[:, c * half : (c + 1) * half] = merged.astype(BF16)
    entropy_ref[...] = jnp.broadcast_to(
        jnp.sum(spread, axis=1, keepdims=True) * (1.0 / HEADS), entropy_ref.shape
    )
    base = jnp.concatenate([base_ref[...]] * items, 0)
    mid = base + matmul(attended_ref[...], weight_ref[...])
    mid_ref[...] = mid
    ffn_ref[...] = layer_norm(mid, gain_ref[...], bias_ref[...]).astype(BF16)


def gelu_parts(x):
    share = 0.5 * (1.0 + lax.erf(x * (0.5**0.5)))
    slope = share + x * jnp.exp(-0.5 * x * x) * ((2.0 * jnp.pi) ** -0.5)
    return x * share, slope


def feed_kernel(flag_ref, *refs, devices, items):
    row_refs = refs[:devices]
    low_ref, up_ref, down_ref, plane_ref, plane_low_ref, result_ref = refs[devices : devices + 6]
    grad_refs = refs[devices + 6 :]
    own, width = row_refs[0].shape
    shard = low_ref.shape[0] // devices
    unit, piece = pack_shape(own, shard, width)
    me = flag_ref[2 * items + 2]
    for d in range(devices):
        plane_ref[d * own : (d + 1) * own, :] = row_refs[d][...]
        source = jnp.bitwise_xor(me, d) * shard
        for a in range(own // unit):
            rows = slice(d * own + a * unit, d * own + (a + 1) * unit)
            for b in range(shard // unit):
                start = pl.multiple_of(source + b * unit, unit)
                plane_low_ref[rows, b * piece : (b + 1) * piece] = low_ref[
                    pl.ds(start, unit), a * piece : (a + 1) * piece
                ]
    upward = matmul(plane_ref[...], up_ref[...])
    hidden, slope = gelu_parts(upward)
    grad_up = (slope * transposed_right(plane_low_ref[...], down_ref[...])).astype(BF16)
    grad = transposed_right(grad_up, up_ref[...]).astype(BF16)
    result = matmul(hidden.astype(BF16), down_ref[...]).astype(BF16)
    for d in range(devices):
        grad_refs[d][...] = grad[d * own : (d + 1) * own, :]
        result_ref[jnp.bitwise_xor(me, d)] = result[d * own : (d + 1) * own, :]


def feed_grad_kernel(
    plane_ref, plane_low_ref, other_ref, other_low_ref, up_ref, down_ref, down_grad_ref, up_grad_ref,
    total_ref, *, plane_blocks,
):
    step = pl.program_id(0)
    near = step < plane_blocks
    rows = jnp.where(near, plane_ref[...], other_ref[...])
    low = jnp.where(near, plane_low_ref[...], other_low_ref[...])
    hidden, slope = gelu_parts(matmul(rows, up_ref[...]))
    grad_up = (slope * transposed_right(low, down_ref[...])).astype(BF16)
    down_part = transposed_left(hidden.astype(BF16), low)
    up_part = transposed_left(rows, grad_up)

    @pl.when(step == 0)
    def _():
        down_grad_ref[...] = down_part
        total_ref[...] = up_part

    @pl.when(step > 0)
    def _():
        down_grad_ref[...] += down_part
        total_ref[...] += up_part

    @pl.when(step == pl.num_programs(0) - 1)
    def _():
        up_grad_ref[...] = total_ref[...].astype(BF16)


def norm_backward(rows, gain, gradient):
    center = rows - jnp.mean(rows, axis=1, keepdims=True)
    rate = lax.rsqrt(jnp.mean(center * center, axis=1, keepdims=True) + EPSILON)
    unit = center * rate
    scaled = gradient * gain
    inner = scaled - jnp.mean(scaled, axis=1, keepdims=True)
    back = rate * (inner - unit * jnp.mean(scaled * unit, axis=1, keepdims=True))
    return (
        back,
        jnp.sum(gradient * unit, axis=0, keepdims=True),
        jnp.sum(gradient, axis=0, keepdims=True),
    )


def turn_kernel(*refs, devices, items, chunks, head_size, heads):
    part_refs = refs[:devices]
    mid_ref, cotangent_ref, gain_ref, merged_ref, log_ref, weight_ref = refs[
        devices : devices + 6
    ]
    message_ref, branch_ref, base_ref, sums_ref = refs[devices + 6 :]
    own, width = mid_ref.shape
    half = width // chunks
    gradient = total_of([x[...] for x in part_refs])
    back, gain_sum, bias_sum = norm_backward(mid_ref[...], gain_ref[...], gradient)
    grad_mid = cotangent_ref[...] + back
    sums_ref[...] = jnp.zeros(sums_ref.shape, F32)
    sums_ref[0:1, :] = gain_sum
    sums_ref[1:2, :] = bias_sum
    row_total = own // items
    base_ref[...] = total_of(
        [grad_mid[i * row_total : (i + 1) * row_total] for i in range(items)]
    )
    branch = grad_mid.astype(BF16)
    branch_ref[...] = branch
    grad_att = transposed_right(branch, weight_ref[...]).astype(BF16)
    expand = head_expand(half, head_size)
    lane, column = iota((6 * LANES, LANES), 0), iota((6 * LANES, LANES), 1)
    place = jnp.logical_and(
        lane % LANES < heads, column == (lane // LANES) * heads + lane % LANES
    ).astype(BF16)
    message_ref[:, :width] = grad_att
    for c in range(chunks):
        columns = slice(c * half, (c + 1) * half)
        delta = lax.dot_general(
            merged_ref[:, columns] * grad_att[:, columns].astype(F32),
            expand,
            (((1,), (1,)), ((), ())),
            precision=HIGHEST,
            preferred_element_type=F32,
        )
        terms = jnp.concatenate([t for x in (log_ref[c], delta) for t in split_terms(x)], 1)
        message_ref[:, width + c * LANES : width + (c + 1) * LANES] = matmul(
            terms, place
        ).astype(BF16)


def backward_kernel(
    *refs, frames, items, patches, scale, head_size, heads,
):
    flag_ref, both_ref, query_ref, top_ref = refs[:4]
    grad_refs = refs[4 : 4 + frames]
    mark_refs = refs[4 + frames : 4 + 2 * frames]
    out_ref, sum_ref, held_ref, note_ref = refs[4 + 2 * frames :]
    lats, width = query_ref.shape
    own = grad_refs[0].shape[0]
    row_total = own // items
    base = items * patches
    for s in range(frames):
        source = lax.rem(flag_ref[items + 1] + (frames - s), frames)
        rows = pl.ds(pl.multiple_of(source * row_total, row_total), row_total)
        block = grad_refs[s][...].astype(F32)
        mark = mark_refs[s][...].astype(F32)
        for i in range(items):
            held_ref[i, rows, :] = block[i * row_total : (i + 1) * row_total]
            note_ref[i, rows, :] = mark[i * row_total : (i + 1) * row_total]
    masks = head_masks(lats, width, head_size)
    queries = spread_heads(query_ref[...].astype(F32), masks).astype(BF16)
    lat_both = both_ref[base : base + lats, :]
    row, lane = iota((GROUP * 8, LANES), 0), iota((GROUP * 8, LANES), 1)
    pick = jnp.logical_and(
        jnp.logical_and(
            lane // heads // 3 == row % 8,
            lane % heads == pl.program_id(0) * GROUP + row // 8,
        ),
        lane < 6 * heads,
    ).astype(BF16)
    grad_query = jnp.zeros((queries.shape[0], width), F32)
    lat_grad_key = jnp.zeros((lats, width), F32)
    lat_grad_value = jnp.zeros((lats, width), F32)
    for i in range(items):
        rows = slice(i * patches, (i + 1) * patches)
        stats = transposed_right(pick, note_ref[i].astype(BF16))
        stats = jnp.concatenate([stats[h * 8 : (h + 1) * 8] for h in range(GROUP)], 1)
        log_total = stats[0:1]
        delta = stats[1:2]
        top = top_ref[0, i, 0:1, :]
        rescale = jnp.exp(top - log_total)
        both = jnp.concatenate([both_ref[rows, :], lat_both], 0)
        keys, values = both[:, :width], both[:, width:]
        grads = spread_heads(held_ref[i], masks).astype(BF16)
        live = live_rows(flag_ref, i, items, patches, lats, queries.shape[0])
        masked = jnp.where(live, scale * transposed_right(keys, queries), MASKED)
        probs = jnp.where(live, jnp.exp(masked - log_total), 0.0)
        block_exp = jnp.where(live, jnp.exp(masked - top), 0.0)
        weights = (block_exp.astype(BF16).astype(F32) * rescale).astype(BF16)
        grad_scores = (probs * (transposed_right(values, grads) - delta)).astype(BF16)
        grad_key = scale * matmul(grad_scores, queries)
        grad_value = matmul(weights, grads)
        out_ref[rows, :width] = grad_key[:patches].astype(BF16)
        out_ref[rows, width:] = grad_value[:patches].astype(BF16)
        grad_query = grad_query + transposed_left(grad_scores, keys)
        lat_grad_key = lat_grad_key + grad_key[patches:]
        lat_grad_value = lat_grad_value + grad_value[patches:]
    out_ref[base : base + lats, :width] = lat_grad_key.astype(BF16)
    out_ref[base : base + lats, width:] = lat_grad_value.astype(BF16)
    sum_ref[...] = scale * collect_heads(grad_query, masks)


def media_kernel(flag_ref, *refs, chunks, items, frames):
    grad_refs, lat_refs, weight_refs = [
        refs[k * chunks : (k + 1) * chunks] for k in range(3)
    ]
    media_ref, time_ref, gain_ref, out_ref, sums_ref, product_ref = refs[3 * chunks :]
    item = pl.program_id(0)

    @pl.when(item == 0)
    def _():
        sums_ref[...] = jnp.zeros(sums_ref.shape, F32)
        product_ref[...] = functools.reduce(
            jnp.add, [transposed_right(g[...], w[...]) for g, w in zip(lat_refs, weight_refs)]
        )

    gradient = functools.reduce(
        jnp.add, [transposed_right(g[...], w[...]) for g, w in zip(grad_refs, weight_refs)]
    )
    inputs = media_ref[...].astype(F32) + time_ref[pl.ds(item, 1), :]
    back, gain_sum, bias_sum = norm_backward(inputs, gain_ref[...], gradient)
    out_ref[...] = back.astype(BF16)
    place = iota((frames, 1), 0) == flag_ref[items + 2 + item]
    sums_ref[0:frames, :] += jnp.where(place, jnp.sum(back, axis=0, keepdims=True), 0.0)
    sums_ref[8:9, :] += gain_sum
    sums_ref[9:10, :] += bias_sum


def latent_kernel(flag_ref, *refs, chunks, items):
    query_refs = refs[:chunks]
    (
        product_ref, query_weight_ref, latent_ref, gain_ref, base_ref, ffn_ref, media_ref, out_ref,
    ) = refs[chunks:]
    lats, width = latent_ref.shape
    half = width // chunks
    gradient = product_ref[...]
    for c in range(chunks):
        gradient = gradient + transposed_right(
            query_refs[c][...].astype(BF16), query_weight_ref[:, c * half : (c + 1) * half]
        )
        out_ref[lats : 2 * lats, c * half : (c + 1) * half] = query_refs[c][...]
    back, gain_sum, bias_sum = norm_backward(latent_ref[...], gain_ref[...], gradient)
    out_ref[:lats, :] = back
    row_total = base_ref.shape[0]
    start = pl.multiple_of(flag_ref[items + 1] * row_total, row_total)
    out_ref[pl.ds(start, row_total), :] += base_ref[...]
    at = 2 * lats
    out_ref[at : at + 8, :] = ffn_ref[...]
    out_ref[at + 2 : at + 3, :] = gain_sum
    out_ref[at + 3 : at + 4, :] = bias_sum
    out_ref[at + 8 : at + 24, :] = media_ref[...]
    out_ref[at + 24 :, :] = jnp.zeros((out_ref.shape[0] - at - 24, width), F32)


def rows_kernel(flag_ref, *refs, count, frames, items):
    total = total_of([x[...] for x in refs[:count]])
    out_refs, held_ref = refs[count:-1], refs[-1]
    rows = total.shape[0] // frames
    for f in range(frames):
        held_ref[f] = total[f * rows : (f + 1) * rows]
    for s, out_ref in enumerate(out_refs):
        block = held_ref[lax.rem(flag_ref[items + 1] + s, frames)]
        out_ref[...] = block.astype(out_ref.dtype)


def place_kernel(flag_ref, *refs, chunks, frames, items, groups):
    chunk_refs = refs[: chunks * frames]
    more_refs = refs[chunks * frames : (chunks + 1) * frames]
    key_ref, value_ref, out_ref = refs[(chunks + 1) * frames :]
    width = key_ref.shape[2] // (chunks * groups)
    for s in range(frames):
        source = lax.rem(flag_ref[items + 1] + (frames - s), frames)
        out_ref[source] = more_refs[s][...].astype(F32)
        for c in range(chunks):
            for g in range(groups):
                at = (c * groups + g) * width
                block = chunk_refs[c * frames + s][:, 2 * g * width : 2 * (g + 1) * width]
                block = block.astype(F32)
                key_ref[source, :, at : at + width] = block[:, :width]
                value_ref[source, :, at : at + width] = block[:, width:]


def body(
    media,
    cotangent,
    frame_count,
    frame_start,
    latents,
    time_embed,
    media_gain,
    media_bias,
    latent_gain,
    latent_bias,
    ffn_gain,
    ffn_bias,
    query_weight,
    key_weight,
    value_weight,
    out_weight,
    up_weight,
    down_weight,
):
    items = media.shape[0]
    patches = media.shape[2]
    width = media.shape[3]
    lats = latents.shape[0]
    frame_total = time_embed.shape[0]
    row_total = cotangent.shape[1]
    own = items * row_total
    head_size = width // HEADS
    half = width // CHUNKS
    chunk_heads = HEADS // CHUNKS
    group_width = GROUP * head_size
    groups = chunk_heads // GROUP
    stack = GROUP * lats
    tokens = items * patches
    all_tokens = tokens + lats
    shard = query_weight.shape[0]
    hidden_shard = down_weight.shape[0]
    item_size = lax.axis_size("items")
    frame_size = lax.axis_size("frames")
    plane = item_size * own
    item_index = lax.axis_index("items")
    slot = lax.axis_index("frames")
    row_base = slot * row_total
    params = pltpu.CompilerParams(vmem_limit_bytes=56 * 2**20)
    smem = pl.BlockSpec(memory_space=pltpu.SMEM)
    whole = pl.BlockSpec(memory_space=pltpu.VMEM)
    sizes = dict(items=items, head_size=head_size, heads=chunk_heads)

    def struct(shape, kind):
        return jax.ShapeDtypeStruct(shape, kind)

    short = pl.CostEstimate(flops=1000, bytes_accessed=1000, transcendentals=0)

    def column_blocks(x):
        return jnp.transpose(x.reshape(-1, item_size, shard), (1, 0, 2))

    def scatter_exchange(x, axis):
        return jnp.sum(lax.all_to_all(x, axis, 0, 0).astype(F32), axis=0)

    grad_out = cotangent.reshape(own, width)
    low_columns = own * width // shard
    joined, grad_low = pl.pallas_call(
        functools.partial(join_kernel, width=group_width),
        out_shape=[struct((shard, 2 * width + low_columns), BF16), struct((own, width), BF16)],
        cost_estimate=short,
        compiler_params=params,
    )(key_weight, value_weight, grad_out)
    kv_full = lax.all_gather(joined, "items", axis=0, tiled=True)

    lat_norm = layer_norm(latents, latent_gain, latent_bias).astype(BF16)
    lat_cols = lax.dynamic_slice_in_dim(lat_norm, item_index * shard, shard, 1)
    query_blocks = column_blocks(matmul(lat_cols, query_weight))
    query_cols = scatter_exchange(query_blocks, "items").astype(BF16)
    query_spread = jnp.broadcast_to(query_cols[None], (item_size, lats, shard))
    queries = jnp.transpose(lax.all_to_all(query_spread, "items", 0, 0), (1, 0, 2)).reshape(
        lats, width
    )

    counts = lax.dynamic_slice_in_dim(frame_count, item_index * items, items)
    starts = lax.dynamic_slice_in_dim(frame_start, item_index * items, items)
    offset = (slot - starts) % frame_total
    flags = jnp.concatenate(
        [
            (offset < counts).astype(jnp.int32),
            (slot == 0).astype(jnp.int32)[None],
            slot.astype(jnp.int32)[None],
            offset.astype(jnp.int32),
            item_index.astype(jnp.int32)[None],
        ]
    )
    picker = (offset[:, None] == jnp.arange(frame_total, dtype=jnp.int32)[None, :]).astype(F32)
    time_rows = jnp.dot(picker, time_embed, precision=HIGHEST, preferred_element_type=F32)
    flat_media = media.reshape(tokens, width)
    steps = tokens // lats
    all_rows = pl.pallas_call(
        functools.partial(norm_kernel, steps=steps, per_item=patches // lats),
        grid=(steps + 1,),
        in_specs=[
            pl.BlockSpec((lats, width), lambda i: (jnp.minimum(i, steps - 1), 0)),
            whole,
            whole,
            whole,
            whole,
        ],
        out_specs=pl.BlockSpec((lats, width), lambda i: (i, 0)),
        out_shape=struct((all_tokens, width), BF16),
        cost_estimate=short,
        compiler_params=params,
    )(
        after(flat_media, query_blocks),
        time_rows,
        media_gain[None],
        media_bias[None],
        lat_norm,
    )
    out_full = lax.all_gather(after(out_weight, all_rows), "items", axis=0, tiled=True)

    chip, core = item_index // 2, item_index % 2
    rows_across = after(all_rows, query_cols).T.reshape(item_size // 2, 2, shard, all_tokens)
    send_rows, keep_rows = [
        jnp.concatenate(
            [
                lax.dynamic_slice(
                    rows_across, (chip ^ k, which, 0, 0), (1, 1, shard, all_tokens)
                ).reshape(shard, all_tokens)
                for k in range(item_size // 2)
            ],
            0,
        )
        for which in (1 - core, core)
    ]
    low_shift = spread_on(after(grad_low, all_rows), "frames")[1:]

    boths, tops, messages = [], [], []
    for c in range(CHUNKS):

        def block_of(g, c=c):
            return (0, c * groups + g)

        if c:
            rows = after(all_rows, tops[-1])
        else:
            rows = after(all_rows, queries, send_rows, keep_rows, *low_shift)
        both = matmul(rows, kv_full[:, 2 * c * half : 2 * (c + 1) * half]).astype(BF16)
        top, *parts = pl.pallas_call(
            functools.partial(
                forward_kernel, patches=patches, scale=head_size**-0.5, **sizes
            ),
            grid=(groups,),
            in_specs=[
                smem,
                pl.BlockSpec((all_tokens, 2 * group_width), lambda g: (0, g)),
                pl.BlockSpec((lats, group_width), block_of),
            ],
            out_specs=[pl.BlockSpec((1, items, 8, stack), lambda g: (g, 0, 0, 0))]
            + [pl.BlockSpec((own, half + LANES), lambda g: (0, 0))] * frame_size,
            out_shape=[struct((groups, items, 8, stack), F32)]
            + [struct((own, half + LANES), BF16)] * frame_size,
            scratch_shapes=[
                pltpu.VMEM((items, lats, group_width), F32),
                pltpu.VMEM((items, lats, LANES), F32),
            ],
            cost_estimate=short,
            compiler_params=params,
        )(flags, both, queries)
        boths.append(both)
        tops.append(top)
        messages += [p if s == 0 else send_on(p, "frames", s) for s, p in enumerate(parts)]
    up_slice = lax.all_to_all(after(up_weight, boths[0]), "items", 1, 0, tiled=True)
    low_other = lax.all_gather(
        after(jnp.stack(low_shift), tops[1]), "items", axis=0
    ).reshape(-1, width)

    base_rows = lax.dynamic_slice_in_dim(latents, row_base, row_total, 0)
    merged, attended, mid_rows, ffn_in, logs, entropy_wide = pl.pallas_call(
        functools.partial(merge_kernel, chunks=CHUNKS, frames=frame_size, **sizes),
        out_shape=[
            struct((own, width), F32),
            struct((own, width), BF16),
            struct((own, width), F32),
            struct((own, width), BF16),
            struct((CHUNKS, own, LANES), F32),
            struct((own, LANES), F32),
        ],
        cost_estimate=short,
        compiler_params=params,
    )(*messages, base_rows, out_full, ffn_gain[None], ffn_bias[None])
    entropy = entropy_wide[:, 0].reshape(items, row_total)

    ffn_blocks = spread_across(ffn_in, "items")
    ffn_plane, low_plane, result_part, *parts = pl.pallas_call(
        functools.partial(feed_kernel, devices=item_size, items=items),
        grid=(1,),
        in_specs=[smem]
        + [whole] * item_size
        + [
            pl.BlockSpec((width, low_columns), lambda i: (0, 2 * width // low_columns)),
            whole,
            whole,
        ],
        out_specs=[whole] * (3 + item_size),
        out_shape=[struct((plane, width), BF16)] * 2
        + [struct((item_size, own, width), BF16)]
        + [struct((own, width), BF16)] * item_size,
        cost_estimate=short,
        compiler_params=params,
    )(flags, *ffn_blocks, kv_full, up_slice, down_weight)
    grad_blocks = collect_across(parts, "items")
    query_full = lax.all_gather(after(query_weight, ffn_plane), "items", axis=0, tiled=True)

    turn, grad_branch, grad_base, ffn_sums = pl.pallas_call(
        functools.partial(turn_kernel, devices=item_size, chunks=CHUNKS, **sizes),
        out_shape=[
            struct((own, width + CHUNKS * LANES), BF16),
            struct((own, width), BF16),
            struct((row_total, width), F32),
            struct((8, width), F32),
        ],
        cost_estimate=short,
        compiler_params=params,
    )(*grad_blocks, mid_rows, grad_out, ffn_gain[None], merged, logs, out_full)
    turns = spread_on(turn, "frames")
    branch_plane = lax.all_gather(grad_branch, "items", axis=0, tiled=True)
    att_plane = lax.all_to_all(after(attended, turn), "items", 1, 0, tiled=True)
    result_pieces = lax.all_to_all(after(result_part, att_plane), "items", 0, 0)
    turns[0] = after(turns[0], att_plane)

    chunk_grads, chunk_queries = [], []

    def weight_terms(c):
        send = matmul(send_rows, chunk_grads[c]).astype(BF16)
        received = send_across(send, "items", 1).reshape(-1, shard, 2 * half)
        keep = matmul(after(keep_rows, send), chunk_grads[c]).astype(BF16)
        return send, keep.reshape(-1, shard, 2 * half), received

    def chip_pieces(keep, received):
        sums = [keep[k].astype(F32) + received[k].astype(F32) for k in range(item_size // 2)]
        return sums[:1] + [p.astype(BF16) for p in sums[1:]]

    def send_pieces(sums):
        return sums[:1] + [
            send_across(p, "items", 2 * k) for k, p in enumerate(sums) if k
        ]

    def frame_rows(parts):
        rows, columns = parts[0].shape
        rows //= frame_size
        return pl.pallas_call(
            functools.partial(
                rows_kernel, count=len(parts), frames=frame_size, items=items
            ),
            in_specs=[smem] + [whole] * len(parts),
            out_specs=[whole] * frame_size,
            out_shape=[struct((rows, columns), F32)]
            + [struct((rows, columns), BF16)] * (frame_size - 1),
            scratch_shapes=[pltpu.VMEM((frame_size, rows, columns), F32)],
            cost_estimate=short,
            compiler_params=params,
        )(flags, *parts)

    def send_rows_on(rows):
        return [rows[0]] + [send_on(p, "frames", s) for s, p in enumerate(rows) if s]

    for c in range(CHUNKS):

        def block_of(g, c=c):
            return (0, c * groups + g)

        chunk_grad, chunk_query = pl.pallas_call(
            functools.partial(
                backward_kernel, frames=frame_size, patches=patches, scale=head_size**-0.5, **sizes
            ),
            grid=(groups,),
            in_specs=[
                smem,
                pl.BlockSpec((all_tokens, 2 * group_width), lambda g: (0, g)),
                pl.BlockSpec((lats, group_width), block_of),
                pl.BlockSpec((1, items, 8, stack), lambda g: (g, 0, 0, 0)),
            ]
            + [pl.BlockSpec((own, group_width), block_of)] * frame_size
            + [pl.BlockSpec((own, LANES), lambda g, c=c: (0, width // LANES + c))] * frame_size,
            out_specs=[
                pl.BlockSpec((all_tokens, 2 * group_width), lambda g: (0, g)),
                pl.BlockSpec((lats, group_width), lambda g: (0, g)),
            ],
            out_shape=[
                struct((all_tokens, 2 * half), BF16),
                struct((lats, half), F32),
            ],
            scratch_shapes=[
                pltpu.VMEM((items, lats, group_width), F32),
                pltpu.VMEM((items, lats, LANES), F32),
            ],
            cost_estimate=short,
            compiler_params=params,
        )(flags, after(boths[c], *held) if c else boths[c], queries, tops[c], *turns, *turns)
        chunk_grads.append(chunk_grad)
        chunk_queries.append(chunk_query)
        if c == 0:
            ffn_shift = spread_on(after(ffn_in, chunk_grad), "frames")[1:]
            first_send, first_keep, first_received = weight_terms(0)
            held = (first_send, *ffn_shift)
    ffn_other = lax.all_gather(
        after(jnp.stack(ffn_shift), branch_plane), "items", axis=0
    ).reshape(-1, width)
    first_pieces = chip_pieces(after(first_keep, chunk_grads[-1]), first_received)
    first_sums = send_pieces(first_pieces)
    out_part = transposed_left(att_plane, after(branch_plane, chunk_grads[-1]))
    out_rows = frame_rows([out_part])
    out_moved = send_rows_on(out_rows)

    last_block = pl.BlockSpec((lats, 2 * half), lambda i: (tokens // lats, 0))
    media_grad, media_sums, lat_product = pl.pallas_call(
        functools.partial(media_kernel, chunks=CHUNKS, items=items, frames=frame_total),
        grid=(items,),
        in_specs=[smem]
        + [pl.BlockSpec((patches, 2 * half), lambda i: (i, 0))] * CHUNKS
        + [last_block] * CHUNKS
        + [pl.BlockSpec((width, 2 * half), lambda i, c=c: (0, c)) for c in range(CHUNKS)]
        + [pl.BlockSpec((patches, width), lambda i: (i, 0)), whole, whole],
        out_specs=[
            pl.BlockSpec((patches, width), lambda i: (i, 0)),
            pl.BlockSpec((16, width), lambda i: (0, 0)),
            pl.BlockSpec((lats, width), lambda i: (0, 0)),
        ],
        out_shape=[
            struct((tokens, width), BF16),
            struct((16, width), F32),
            struct((lats, width), F32),
        ],
        cost_estimate=short,
        compiler_params=params,
    )(
        flags,
        *chunk_grads[:-1],
        after(chunk_grads[-1], *first_pieces, *out_rows, result_pieces),
        *chunk_grads,
        *[kv_full] * CHUNKS,
        flat_media,
        time_rows,
        media_gain[None],
    )

    sum_rows = 2 * lats + 24
    sum_rows += -sum_rows % (8 * item_size)
    payload = pl.pallas_call(
        functools.partial(latent_kernel, chunks=CHUNKS, items=items),
        in_specs=[smem] + [whole] * (CHUNKS + 7),
        out_specs=whole,
        out_shape=struct((sum_rows, width), F32),
        cost_estimate=short,
        compiler_params=params,
    )(
        flags,
        *chunk_queries,
        lat_product,
        query_full,
        latents,
        latent_gain[None],
        grad_base,
        ffn_sums,
        media_sums,
    )
    payload_part = lax.psum_scatter(payload, "items", scatter_dimension=0, tiled=True)

    chunk_grads[-1] = after(chunk_grads[-1], payload)
    last_send, last_keep, last_received = weight_terms(CHUNKS - 1)
    first_rows = frame_rows([after(first_sums[0], last_send), *first_sums[1:]])
    first_moved = send_rows_on(first_rows)
    out_placed = spread_on(total_of(out_moved).astype(BF16), "frames")
    last_pieces = chip_pieces(last_keep, last_received)
    last_sums = send_pieces(last_pieces)

    block_rows = min(512, plane)
    plane_blocks = plane // block_rows
    near = pl.BlockSpec((block_rows, width), lambda i: (jnp.minimum(i, plane_blocks - 1), 0))
    far = pl.BlockSpec((block_rows, width), lambda i: (jnp.maximum(i - plane_blocks, 0), 0))
    down_grad, up_part = pl.pallas_call(
        functools.partial(feed_grad_kernel, plane_blocks=plane_blocks),
        grid=(plane_blocks * frame_size,),
        in_specs=[near, near, far, far, whole, whole],
        out_specs=[
            pl.BlockSpec((hidden_shard, width), lambda i: (0, 0)),
            pl.BlockSpec((width, hidden_shard), lambda i: (0, 0)),
        ],
        out_shape=[struct((hidden_shard, width), F32), struct((width, hidden_shard), BF16)],
        scratch_shapes=[pltpu.VMEM((width, hidden_shard), F32)],
        cost_estimate=short,
        compiler_params=params,
    )(
        ffn_plane,
        low_plane,
        after(ffn_other, payload, *first_rows, *last_pieces, out_placed[0]),
        low_other,
        up_slice,
        down_weight,
    )
    up_grad = lax.all_to_all(up_part, "items", 0, 1, tiled=True).astype(F32)

    first_moved[0] = after(first_moved[0], up_part)
    first_placed = spread_on(total_of(first_moved).astype(BF16), "frames")
    last_moved = send_rows_on(frame_rows([after(last_sums[0], up_part), *last_sums[1:]]))
    last_placed = spread_on(total_of(last_moved).astype(BF16), "frames")
    placed = first_placed + last_placed + out_placed
    key_grad, value_grad, out_grad = pl.pallas_call(
        functools.partial(
            place_kernel, chunks=CHUNKS, frames=frame_size, items=items, groups=groups
        ),
        in_specs=[smem] + [whole] * len(placed),
        out_specs=[whole] * 3,
        out_shape=[struct((frame_size, shard // frame_size, width), F32)] * 3,
        cost_estimate=short,
        compiler_params=params,
    )(flags, *placed)

    payload_others = spread_on(payload_part.astype(BF16), "frames")[1:]
    sums = lax.all_gather(
        total_of([payload_part] + payload_others), "items", axis=0, tiled=True
    )
    latents_grad = sums[:lats]
    query_grad = transposed_left(lat_cols, sums[lats : 2 * lats].astype(BF16))
    at = 2 * lats
    column_sums = lax.dynamic_slice_in_dim(
        sums[at + 8 : at + 24], item_index * shard, shard, 1
    )

    result = mid_rows + total_of([result_pieces[d] for d in range(item_size)])
    return (
        result.reshape(items, row_total, width),
        entropy,
        media_grad.reshape(media.shape),
        latents_grad,
        column_sums[:frame_total],
        column_sums[8],
        column_sums[9],
        sums[at + 2],
        sums[at + 3],
        sums[at],
        sums[at + 1],
        query_grad,
        key_grad.reshape(shard, width),
        value_grad.reshape(shard, width),
        out_grad.reshape(shard, width),
        up_grad,
        down_grad,
    )


def solution(mesh):
    return jax.shard_map(
        body,
        mesh=mesh,
        in_specs=(
            P("items", "frames", None, None),
            P("items", "frames", None),
            P(),
            P(),
            P(),
            P(),
            P(),
            P(),
            P(),
            P(),
            P(),
            P(),
            P("items", None),
            P("items", None),
            P("items", None),
            P("items", None),
            P("items", None),
            P("items", None),
        ),
        out_specs=(
            P("items", "frames", None),
            P("items", "frames"),
            P("items", "frames", None, None),
            P(),
            P(None, "items"),
            P("items"),
            P("items"),
            P(),
            P(),
            P(),
            P(),
            P("items", None),
            P("items", None),
            P("items", None),
            P("items", None),
            P("items", None),
            P("items", None),
        ),
        check_vma=False,
    )
```

```python
import functools
import math

import jax
import jax.numpy as jnp
from jax import lax
from jax.experimental import pallas as pl
from jax.experimental.pallas import tpu as pltpu
from jax.sharding import PartitionSpec as P

HEADS = 16
GROUP = 4
CHUNKS = 2
LANES = 128
EPSILON = 1e-05
MASKED = -1e30
F32 = jnp.float32
BF16 = jnp.bfloat16
HIGHEST = lax.Precision.HIGHEST


def layer_norm(inputs, norm_gain, norm_bias):
    center = inputs - jnp.mean(inputs, axis=-1, keepdims=True)
    spread = jnp.mean(center * center, axis=-1, keepdims=True)
    return center * lax.rsqrt(spread + EPSILON) * norm_gain + norm_bias


def matmul(left_side, right_side):
    return jnp.dot(left_side, right_side, preferred_element_type=F32)


def transposed_left(left_side, right_side):
    return lax.dot_general(
        left_side, right_side, (((0,), (0,)), ((), ())), preferred_element_type=F32
    )


def transposed_right(left_side, right_side):
    return lax.dot_general(
        left_side, right_side, (((1,), (1,)), ((), ())), preferred_element_type=F32
    )


def send_on(x, axis, step):
    size = lax.axis_size(axis)
    return lax.ppermute(x, axis, [(i, (i + step) % size) for i in range(size)])


def send_across(x, axis, distance):
    return lax.ppermute(x, axis, [(i, i ^ distance) for i in range(lax.axis_size(axis))])


def spread_on(x, axis):
    return [x] + [send_on(x, axis, s) for s in range(1, lax.axis_size(axis))]


def spread_across(x, axis):
    return [x] + [send_across(x, axis, d) for d in range(1, lax.axis_size(axis))]


def collect_across(pieces, axis):
    return [pieces[0]] + [send_across(p, axis, d) for d, p in enumerate(pieces) if d]


def total_of(pieces):
    return functools.reduce(jnp.add, [p.astype(F32) for p in pieces])


def after(x, *earlier):
    return lax.optimization_barrier((x,) + earlier)[0]


def split_terms(x):
    high = x.astype(BF16)
    rest = x - high.astype(F32)
    middle = rest.astype(BF16)
    return high, middle, (rest - middle.astype(F32)).astype(BF16)


def iota(shape, dim):
    return lax.broadcasted_iota(jnp.int32, shape, dim)


def head_masks(rows, width, head_size):
    lane = iota((rows, width), 1)
    return [
        jnp.logical_and(lane >= h * head_size, lane < (h + 1) * head_size)
        for h in range(width // head_size)
    ]


def spread_heads(block, masks):
    return jnp.concatenate([jnp.where(m, block, jnp.zeros_like(block)) for m in masks], 0)


def collect_heads(block, masks):
    rows = block.shape[0] // len(masks)
    total = jnp.where(masks[0], block[:rows], 0.0)
    for h in range(1, len(masks)):
        total = total + jnp.where(masks[h], block[h * rows : (h + 1) * rows], 0.0)
    return total


def head_expand(width, head_size):
    row, column = iota((LANES, width), 0), iota((LANES, width), 1)
    return jnp.logical_and(column >= row * head_size, column < (row + 1) * head_size).astype(F32)


def live_rows(flag_ref, item, items, patches, lats, columns):
    row = iota((patches + lats, columns), 0)
    media = jnp.logical_and(row < patches, flag_ref[item] > 0)
    return jnp.logical_or(media, jnp.logical_and(row >= patches, flag_ref[items] > 0))


def pack_shape(own, shard, width):
    unit = math.gcd(own, shard)
    return unit, width * unit // shard


def join_kernel(key_ref, value_ref, cotangent_ref, out_ref, low_ref, *, width):
    for g in range(key_ref.shape[1] // width):
        columns = slice(g * width, (g + 1) * width)
        out_ref[:, 2 * g * width : (2 * g + 1) * width] = key_ref[:, columns]
        out_ref[:, (2 * g + 1) * width : (2 * g + 2) * width] = value_ref[:, columns]
    low = cotangent_ref[...].astype(BF16)
    low_ref[...] = low
    own, span = low.shape
    unit, piece = pack_shape(own, out_ref.shape[0], span)
    for a in range(own // unit):
        for b in range(span // piece):
            at = 2 * span + a * piece
            out_ref[b * unit : (b + 1) * unit, at : at + piece] = low[
                a * unit : (a + 1) * unit, b * piece : (b + 1) * piece
            ]


def norm_kernel(media_ref, time_ref, gain_ref, bias_ref, lat_ref, out_ref, *, steps, per_item):
    step = pl.program_id(0)

    @pl.when(step < steps)
    def _():
        rows = media_ref[...].astype(F32) + time_ref[pl.ds(step // per_item, 1), :]
        out_ref[...] = layer_norm(rows, gain_ref[...], bias_ref[...]).astype(BF16)

    @pl.when(step == steps)
    def _():
        out_ref[...] = lat_ref[...]


def forward_kernel(
    flag_ref, both_ref, query_ref, top_ref, *refs, items, patches, scale, head_size, heads,
):
    message_refs, (part_ref, mark_ref) = refs[:-2], refs[-2:]
    lats, width = query_ref.shape
    frames = len(message_refs)
    own = message_refs[0].shape[0]
    row_total = own // items
    masks = head_masks(lats, width, head_size)
    queries = spread_heads(query_ref[...].astype(F32), masks).astype(BF16)
    base = items * patches
    lat_both = both_ref[base : base + lats, :]
    group = pl.program_id(0)
    term, lane = iota((16, GROUP * LANES), 0), iota((16, GROUP * LANES), 1)
    place = jnp.logical_and(
        lane % LANES == term * heads + group * GROUP + lane // LANES, term < 9
    ).astype(BF16)
    for i in range(items):
        both = jnp.concatenate([both_ref[i * patches : (i + 1) * patches, :], lat_both], 0)
        live = live_rows(flag_ref, i, items, patches, lats, queries.shape[0])
        scores = scale * transposed_right(both[:, :width], queries)
        masked = jnp.where(live, scores, MASKED)
        top = jnp.max(masked, axis=0, keepdims=True)
        block_exp = jnp.where(live, jnp.exp(masked - top), 0.0)
        total = jnp.sum(block_exp, axis=0, keepdims=True)
        moment = jnp.sum(block_exp * scores, axis=0, keepdims=True)
        part = transposed_left(block_exp.astype(BF16), both[:, width:])
        part_ref[i] = collect_heads(part, masks)
        top_ref[0, i] = jnp.broadcast_to(top, top_ref.shape[2:])
        terms = jnp.concatenate(
            [t.astype(F32) for x in (top, total, moment) for t in split_terms(x)]
            + [jnp.zeros((7, top.shape[1]), F32)],
            0,
        ).astype(BF16)
        wide = transposed_left(terms, place)
        mark = wide[:lats, :LANES]
        for h in range(1, GROUP):
            mark = mark + wide[h * lats : (h + 1) * lats, h * LANES : (h + 1) * LANES]
        mark_ref[i] = mark

    end = message_refs[0].shape[1] - LANES
    for s, message_ref in enumerate(message_refs):
        start = pl.multiple_of(lax.rem(flag_ref[items + 1] + s, frames) * row_total, row_total)
        rows = pl.ds(start, row_total)
        block = jnp.concatenate([part_ref[i, rows, :] for i in range(items)], 0).astype(BF16)
        mark = jnp.concatenate([mark_ref[i, rows, :] for i in range(items)], 0).astype(BF16)
        for g in range(end // width):

            @pl.when(group == g)
            def _():
                message_ref[:, g * width : (g + 1) * width] = block
                if g == 0:
                    message_ref[:, end:] = mark
                else:
                    message_ref[:, end:] = message_ref[:, end:] + mark


def merge_kernel(*refs, chunks, frames, items, head_size, heads):
    message_refs = refs[: chunks * frames]
    base_ref, weight_ref, gain_ref, bias_ref = refs[chunks * frames : chunks * frames + 4]
    merged_ref, attended_ref, mid_ref, ffn_ref, log_ref, entropy_ref = refs[chunks * frames + 4 :]
    own, columns = message_refs[0].shape
    half = columns - LANES
    lane, column = iota((LANES, 3 * LANES), 0), iota((LANES, 3 * LANES), 1)
    gather = jnp.logical_and(
        jnp.logical_and(lane // heads // 3 == column // LANES, lane % heads == column % LANES),
        lane < 9 * heads,
    ).astype(BF16)
    expand = head_expand(half, head_size)
    live = iota((own, LANES), 1) < heads
    spread = jnp.zeros((own, LANES), F32)
    for c in range(chunks):
        sources = message_refs[c * frames : (c + 1) * frames]
        stats = [matmul(x[:, half:], gather) for x in sources]
        tops = [x[:, :LANES] for x in stats]
        peak = functools.reduce(jnp.maximum, tops)
        factors = [jnp.exp(t - peak) for t in tops]
        whole = sum(f * x[:, LANES : 2 * LANES] for f, x in zip(factors, stats))
        moment = sum(f * x[:, 2 * LANES :] for f, x in zip(factors, stats))
        whole = jnp.where(live, whole, 1.0)
        log_total = jnp.where(live, peak + jnp.log(whole), 0.0)
        log_ref[c] = log_total
        spread = spread + jnp.where(live, log_total - moment / whole, 0.0)
        merged = jnp.zeros((own, half), F32)
        for x, factor in zip(sources, factors):
            share = jnp.where(live, factor / whole, 0.0)
            wide = jnp.dot(share, expand, precision=HIGHEST, preferred_element_type=F32)
            merged = merged + x[:, :half].astype(F32) * wide
        merged_ref[:, c * half : (c + 1) * half] = merged
        attended_ref[:, c * half : (c + 1) * half] = merged.astype(BF16)
    entropy_ref[...] = jnp.broadcast_to(
        jnp.sum(spread, axis=1, keepdims=True) * (1.0 / HEADS), entropy_ref.shape
    )
    base = jnp.concatenate([base_ref[...]] * items, 0)
    mid = base + matmul(attended_ref[...], weight_ref[...])
    mid_ref[...] = mid
    ffn_ref[...] = layer_norm(mid, gain_ref[...], bias_ref[...]).astype(BF16)


def gelu_parts(x):
    share = 0.5 * (1.0 + lax.erf(x * (0.5**0.5)))
    slope = share + x * jnp.exp(-0.5 * x * x) * ((2.0 * jnp.pi) ** -0.5)
    return x * share, slope


def feed_kernel(flag_ref, *refs, devices, items):
    row_refs = refs[:devices]
    low_ref, up_ref, down_ref, plane_ref, plane_low_ref, result_ref = refs[devices : devices + 6]
    grad_refs = refs[devices + 6 :]
    own, width = row_refs[0].shape
    shard = low_ref.shape[0] // devices
    unit, piece = pack_shape(own, shard, width)
    me = flag_ref[2 * items + 2]
    for d in range(devices):
        plane_ref[d * own : (d + 1) * own, :] = row_refs[d][...]
        source = jnp.bitwise_xor(me, d) * shard
        for a in range(own // unit):
            rows = slice(d * own + a * unit, d * own + (a + 1) * unit)
            for b in range(shard // unit):
                start = pl.multiple_of(source + b * unit, unit)
                plane_low_ref[rows, b * piece : (b + 1) * piece] = low_ref[
                    pl.ds(start, unit), a * piece : (a + 1) * piece
                ]
    upward = matmul(plane_ref[...], up_ref[...])
    hidden, slope = gelu_parts(upward)
    grad_up = (slope * transposed_right(plane_low_ref[...], down_ref[...])).astype(BF16)
    grad = transposed_right(grad_up, up_ref[...]).astype(BF16)
    result = matmul(hidden.astype(BF16), down_ref[...]).astype(BF16)
    for d in range(devices):
        grad_refs[d][...] = grad[d * own : (d + 1) * own, :]
        result_ref[jnp.bitwise_xor(me, d)] = result[d * own : (d + 1) * own, :]


def feed_grad_kernel(
    plane_ref, plane_low_ref, other_ref, other_low_ref, up_ref, down_ref, down_grad_ref, up_grad_ref,
    total_ref, *, plane_blocks,
):
    step = pl.program_id(0)
    near = step < plane_blocks
    rows = jnp.where(near, plane_ref[...], other_ref[...])
    low = jnp.where(near, plane_low_ref[...], other_low_ref[...])
    hidden, slope = gelu_parts(matmul(rows, up_ref[...]))
    grad_up = (slope * transposed_right(low, down_ref[...])).astype(BF16)
    down_part = transposed_left(hidden.astype(BF16), low)
    up_part = transposed_left(rows, grad_up)

    @pl.when(step == 0)
    def _():
        down_grad_ref[...] = down_part
        total_ref[...] = up_part

    @pl.when(step > 0)
    def _():
        down_grad_ref[...] += down_part
        total_ref[...] += up_part

    @pl.when(step == pl.num_programs(0) - 1)
    def _():
        up_grad_ref[...] = total_ref[...].astype(BF16)


def norm_backward(rows, gain, gradient):
    center = rows - jnp.mean(rows, axis=1, keepdims=True)
    rate = lax.rsqrt(jnp.mean(center * center, axis=1, keepdims=True) + EPSILON)
    unit = center * rate
    scaled = gradient * gain
    inner = scaled - jnp.mean(scaled, axis=1, keepdims=True)
    back = rate * (inner - unit * jnp.mean(scaled * unit, axis=1, keepdims=True))
    return (
        back,
        jnp.sum(gradient * unit, axis=0, keepdims=True),
        jnp.sum(gradient, axis=0, keepdims=True),
    )


def turn_kernel(*refs, devices, items, chunks, head_size, heads):
    part_refs = refs[:devices]
    mid_ref, cotangent_ref, gain_ref, merged_ref, log_ref, weight_ref = refs[
        devices : devices + 6
    ]
    message_ref, branch_ref, base_ref, sums_ref = refs[devices + 6 :]
    own, width = mid_ref.shape
    half = width // chunks
    gradient = total_of([x[...] for x in part_refs])
    back, gain_sum, bias_sum = norm_backward(mid_ref[...], gain_ref[...], gradient)
    grad_mid = cotangent_ref[...] + back
    sums_ref[...] = jnp.zeros(sums_ref.shape, F32)
    sums_ref[0:1, :] = gain_sum
    sums_ref[1:2, :] = bias_sum
    row_total = own // items
    base_ref[...] = total_of(
        [grad_mid[i * row_total : (i + 1) * row_total] for i in range(items)]
    )
    branch = grad_mid.astype(BF16)
    branch_ref[...] = branch
    grad_att = transposed_right(branch, weight_ref[...]).astype(BF16)
    expand = head_expand(half, head_size)
    lane, column = iota((6 * LANES, LANES), 0), iota((6 * LANES, LANES), 1)
    place = jnp.logical_and(
        lane % LANES < heads, column == (lane // LANES) * heads + lane % LANES
    ).astype(BF16)
    message_ref[:, :width] = grad_att
    for c in range(chunks):
        columns = slice(c * half, (c + 1) * half)
        delta = lax.dot_general(
            merged_ref[:, columns] * grad_att[:, columns].astype(F32),
            expand,
            (((1,), (1,)), ((), ())),
            precision=HIGHEST,
            preferred_element_type=F32,
        )
        terms = jnp.concatenate([t for x in (log_ref[c], delta) for t in split_terms(x)], 1)
        message_ref[:, width + c * LANES : width + (c + 1) * LANES] = matmul(
            terms, place
        ).astype(BF16)


def backward_kernel(
    *refs, frames, items, patches, scale, head_size, heads,
):
    flag_ref, both_ref, query_ref, top_ref = refs[:4]
    grad_refs = refs[4 : 4 + frames]
    mark_refs = refs[4 + frames : 4 + 2 * frames]
    out_ref, sum_ref, held_ref, note_ref = refs[4 + 2 * frames :]
    lats, width = query_ref.shape
    own = grad_refs[0].shape[0]
    row_total = own // items
    base = items * patches
    for s in range(frames):
        source = lax.rem(flag_ref[items + 1] + (frames - s), frames)
        rows = pl.ds(pl.multiple_of(source * row_total, row_total), row_total)
        block = grad_refs[s][...].astype(F32)
        mark = mark_refs[s][...].astype(F32)
        for i in range(items):
            held_ref[i, rows, :] = block[i * row_total : (i + 1) * row_total]
            note_ref[i, rows, :] = mark[i * row_total : (i + 1) * row_total]
    masks = head_masks(lats, width, head_size)
    queries = spread_heads(query_ref[...].astype(F32), masks).astype(BF16)
    lat_both = both_ref[base : base + lats, :]
    row, lane = iota((GROUP * 8, LANES), 0), iota((GROUP * 8, LANES), 1)
    pick = jnp.logical_and(
        jnp.logical_and(
            lane // heads // 3 == row % 8,
            lane % heads == pl.program_id(0) * GROUP + row // 8,
        ),
        lane < 6 * heads,
    ).astype(BF16)
    grad_query = jnp.zeros((queries.shape[0], width), F32)
    lat_grad_key = jnp.zeros((lats, width), F32)
    lat_grad_value = jnp.zeros((lats, width), F32)
    for i in range(items):
        rows = slice(i * patches, (i + 1) * patches)
        stats = transposed_right(pick, note_ref[i].astype(BF16))
        stats = jnp.concatenate([stats[h * 8 : (h + 1) * 8] for h in range(GROUP)], 1)
        log_total = stats[0:1]
        delta = stats[1:2]
        top = top_ref[0, i, 0:1, :]
        rescale = jnp.exp(top - log_total)
        both = jnp.concatenate([both_ref[rows, :], lat_both], 0)
        keys, values = both[:, :width], both[:, width:]
        grads = spread_heads(held_ref[i], masks).astype(BF16)
        live = live_rows(flag_ref, i, items, patches, lats, queries.shape[0])
        masked = jnp.where(live, scale * transposed_right(keys, queries), MASKED)
        probs = jnp.where(live, jnp.exp(masked - log_total), 0.0)
        block_exp = jnp.where(live, jnp.exp(masked - top), 0.0)
        weights = (block_exp.astype(BF16).astype(F32) * rescale).astype(BF16)
        grad_scores = (probs * (transposed_right(values, grads) - delta)).astype(BF16)
        grad_key = scale * matmul(grad_scores, queries)
        grad_value = matmul(weights, grads)
        out_ref[rows, :width] = grad_key[:patches].astype(BF16)
        out_ref[rows, width:] = grad_value[:patches].astype(BF16)
        grad_query = grad_query + transposed_left(grad_scores, keys)
        lat_grad_key = lat_grad_key + grad_key[patches:]
        lat_grad_value = lat_grad_value + grad_value[patches:]
    out_ref[base : base + lats, :width] = lat_grad_key.astype(BF16)
    out_ref[base : base + lats, width:] = lat_grad_value.astype(BF16)
    sum_ref[...] = scale * collect_heads(grad_query, masks)


def media_kernel(flag_ref, *refs, chunks, items, frames):
    grad_refs, lat_refs, weight_refs = [
        refs[k * chunks : (k + 1) * chunks] for k in range(3)
    ]
    media_ref, time_ref, gain_ref, out_ref, sums_ref, product_ref = refs[3 * chunks :]
    item = pl.program_id(0)

    @pl.when(item == 0)
    def _():
        sums_ref[...] = jnp.zeros(sums_ref.shape, F32)
        product_ref[...] = functools.reduce(
            jnp.add, [transposed_right(g[...], w[...]) for g, w in zip(lat_refs, weight_refs)]
        )

    gradient = functools.reduce(
        jnp.add, [transposed_right(g[...], w[...]) for g, w in zip(grad_refs, weight_refs)]
    )
    inputs = media_ref[...].astype(F32) + time_ref[pl.ds(item, 1), :]
    back, gain_sum, bias_sum = norm_backward(inputs, gain_ref[...], gradient)
    out_ref[...] = back.astype(BF16)
    place = iota((frames, 1), 0) == flag_ref[items + 2 + item]
    sums_ref[0:frames, :] += jnp.where(place, jnp.sum(back, axis=0, keepdims=True), 0.0)
    sums_ref[8:9, :] += gain_sum
    sums_ref[9:10, :] += bias_sum


def latent_kernel(flag_ref, *refs, chunks, items):
    query_refs = refs[:chunks]
    (
        product_ref, query_weight_ref, latent_ref, gain_ref, base_ref, ffn_ref, media_ref, out_ref,
    ) = refs[chunks:]
    lats, width = latent_ref.shape
    half = width // chunks
    gradient = product_ref[...]
    for c in range(chunks):
        gradient = gradient + transposed_right(
            query_refs[c][...].astype(BF16), query_weight_ref[:, c * half : (c + 1) * half]
        )
        out_ref[lats : 2 * lats, c * half : (c + 1) * half] = query_refs[c][...]
    back, gain_sum, bias_sum = norm_backward(latent_ref[...], gain_ref[...], gradient)
    out_ref[:lats, :] = back
    row_total = base_ref.shape[0]
    start = pl.multiple_of(flag_ref[items + 1] * row_total, row_total)
    out_ref[pl.ds(start, row_total), :] += base_ref[...]
    at = 2 * lats
    out_ref[at : at + 8, :] = ffn_ref[...]
    out_ref[at + 2 : at + 3, :] = gain_sum
    out_ref[at + 3 : at + 4, :] = bias_sum
    out_ref[at + 8 : at + 24, :] = media_ref[...]
    out_ref[at + 24 :, :] = jnp.zeros((out_ref.shape[0] - at - 24, width), F32)


def rows_kernel(flag_ref, *refs, count, frames, items):
    total = total_of([x[...] for x in refs[:count]])
    out_refs, held_ref = refs[count:-1], refs[-1]
    rows = total.shape[0] // frames
    for f in range(frames):
        held_ref[f] = total[f * rows : (f + 1) * rows]
    for s, out_ref in enumerate(out_refs):
        block = held_ref[lax.rem(flag_ref[items + 1] + s, frames)]
        out_ref[...] = block.astype(out_ref.dtype)


def place_kernel(flag_ref, *refs, chunks, frames, items, groups):
    chunk_refs = refs[: chunks * frames]
    more_refs = refs[chunks * frames : (chunks + 1) * frames]
    key_ref, value_ref, out_ref = refs[(chunks + 1) * frames :]
    width = key_ref.shape[2] // (chunks * groups)
    for s in range(frames):
        source = lax.rem(flag_ref[items + 1] + (frames - s), frames)
        out_ref[source] = more_refs[s][...].astype(F32)
        for c in range(chunks):
            for g in range(groups):
                at = (c * groups + g) * width
                block = chunk_refs[c * frames + s][:, 2 * g * width : 2 * (g + 1) * width]
                block = block.astype(F32)
                key_ref[source, :, at : at + width] = block[:, :width]
                value_ref[source, :, at : at + width] = block[:, width:]


def body(
    media,
    cotangent,
    frame_count,
    frame_start,
    latents,
    time_embed,
    media_gain,
    media_bias,
    latent_gain,
    latent_bias,
    ffn_gain,
    ffn_bias,
    query_weight,
    key_weight,
    value_weight,
    out_weight,
    up_weight,
    down_weight,
):
    items = media.shape[0]
    patches = media.shape[2]
    width = media.shape[3]
    lats = latents.shape[0]
    frame_total = time_embed.shape[0]
    row_total = cotangent.shape[1]
    own = items * row_total
    head_size = width // HEADS
    half = width // CHUNKS
    chunk_heads = HEADS // CHUNKS
    group_width = GROUP * head_size
    groups = chunk_heads // GROUP
    stack = GROUP * lats
    tokens = items * patches
    all_tokens = tokens + lats
    shard = query_weight.shape[0]
    hidden_shard = down_weight.shape[0]
    item_size = lax.axis_size("items")
    frame_size = lax.axis_size("frames")
    plane = item_size * own
    item_index = lax.axis_index("items")
    slot = lax.axis_index("frames")
    row_base = slot * row_total
    params = pltpu.CompilerParams(vmem_limit_bytes=56 * 2**20)
    smem = pl.BlockSpec(memory_space=pltpu.SMEM)
    whole = pl.BlockSpec(memory_space=pltpu.VMEM)
    sizes = dict(items=items, head_size=head_size, heads=chunk_heads)

    def struct(shape, kind):
        return jax.ShapeDtypeStruct(shape, kind)

    short = pl.CostEstimate(flops=1000, bytes_accessed=1000, transcendentals=0)

    def column_blocks(x):
        return jnp.transpose(x.reshape(-1, item_size, shard), (1, 0, 2))

    def scatter_exchange(x, axis):
        return jnp.sum(lax.all_to_all(x, axis, 0, 0).astype(F32), axis=0)

    grad_out = cotangent.reshape(own, width)
    low_columns = own * width // shard
    joined, grad_low = pl.pallas_call(
        functools.partial(join_kernel, width=group_width),
        out_shape=[struct((shard, 2 * width + low_columns), BF16), struct((own, width), BF16)],
        cost_estimate=short,
        compiler_params=params,
    )(key_weight, value_weight, grad_out)
    kv_full = lax.all_gather(joined, "items", axis=0, tiled=True)

    lat_norm = layer_norm(latents, latent_gain, latent_bias).astype(BF16)
    lat_cols = lax.dynamic_slice_in_dim(lat_norm, item_index * shard, shard, 1)
    query_blocks = column_blocks(matmul(lat_cols, query_weight))
    query_cols = scatter_exchange(query_blocks, "items").astype(BF16)
    query_spread = jnp.broadcast_to(query_cols[None], (item_size, lats, shard))
    queries = jnp.transpose(lax.all_to_all(query_spread, "items", 0, 0), (1, 0, 2)).reshape(
        lats, width
    )

    counts = lax.dynamic_slice_in_dim(frame_count, item_index * items, items)
    starts = lax.dynamic_slice_in_dim(frame_start, item_index * items, items)
    offset = (slot - starts) % frame_total
    flags = jnp.concatenate(
        [
            (offset < counts).astype(jnp.int32),
            (slot == 0).astype(jnp.int32)[None],
            slot.astype(jnp.int32)[None],
            offset.astype(jnp.int32),
            item_index.astype(jnp.int32)[None],
        ]
    )
    picker = (offset[:, None] == jnp.arange(frame_total, dtype=jnp.int32)[None, :]).astype(F32)
    time_rows = jnp.dot(picker, time_embed, precision=HIGHEST, preferred_element_type=F32)
    flat_media = media.reshape(tokens, width)
    steps = tokens // lats
    all_rows = pl.pallas_call(
        functools.partial(norm_kernel, steps=steps, per_item=patches // lats),
        grid=(steps + 1,),
        in_specs=[
            pl.BlockSpec((lats, width), lambda i: (jnp.minimum(i, steps - 1), 0)),
            whole,
            whole,
            whole,
            whole,
        ],
        out_specs=pl.BlockSpec((lats, width), lambda i: (i, 0)),
        out_shape=struct((all_tokens, width), BF16),
        cost_estimate=short,
        compiler_params=params,
    )(
        after(flat_media, query_blocks),
        time_rows,
        media_gain[None],
        media_bias[None],
        lat_norm,
    )
    out_full = lax.all_gather(after(out_weight, all_rows), "items", axis=0, tiled=True)

    chip, core = item_index // 2, item_index % 2
    rows_across = after(all_rows, query_cols).T.reshape(item_size // 2, 2, shard, all_tokens)
    send_rows, keep_rows = [
        jnp.concatenate(
            [
                lax.dynamic_slice(
                    rows_across, (chip ^ k, which, 0, 0), (1, 1, shard, all_tokens)
                ).reshape(shard, all_tokens)
                for k in range(item_size // 2)
            ],
            0,
        )
        for which in (1 - core, core)
    ]
    low_shift = spread_on(after(grad_low, all_rows), "frames")[1:]

    boths, tops, messages = [], [], []
    for c in range(CHUNKS):

        def block_of(g, c=c):
            return (0, c * groups + g)

        if c:
            rows = after(all_rows, tops[-1])
        else:
            rows = after(all_rows, queries, send_rows, keep_rows, *low_shift)
        both = matmul(rows, kv_full[:, 2 * c * half : 2 * (c + 1) * half]).astype(BF16)
        top, *parts = pl.pallas_call(
            functools.partial(
                forward_kernel, patches=patches, scale=head_size**-0.5, **sizes
            ),
            grid=(groups,),
            in_specs=[
                smem,
                pl.BlockSpec((all_tokens, 2 * group_width), lambda g: (0, g)),
                pl.BlockSpec((lats, group_width), block_of),
            ],
            out_specs=[pl.BlockSpec((1, items, 8, stack), lambda g: (g, 0, 0, 0))]
            + [pl.BlockSpec((own, half + LANES), lambda g: (0, 0))] * frame_size,
            out_shape=[struct((groups, items, 8, stack), F32)]
            + [struct((own, half + LANES), BF16)] * frame_size,
            scratch_shapes=[
                pltpu.VMEM((items, lats, group_width), F32),
                pltpu.VMEM((items, lats, LANES), F32),
            ],
            cost_estimate=short,
            compiler_params=params,
        )(flags, both, queries)
        boths.append(both)
        tops.append(top)
        messages += [p if s == 0 else send_on(p, "frames", s) for s, p in enumerate(parts)]
    up_slice = lax.all_to_all(after(up_weight, boths[0]), "items", 1, 0, tiled=True)
    low_other = lax.all_gather(
        after(jnp.stack(low_shift), tops[1]), "items", axis=0
    ).reshape(-1, width)

    base_rows = lax.dynamic_slice_in_dim(latents, row_base, row_total, 0)
    merged, attended, mid_rows, ffn_in, logs, entropy_wide = pl.pallas_call(
        functools.partial(merge_kernel, chunks=CHUNKS, frames=frame_size, **sizes),
        out_shape=[
            struct((own, width), F32),
            struct((own, width), BF16),
            struct((own, width), F32),
            struct((own, width), BF16),
            struct((CHUNKS, own, LANES), F32),
            struct((own, LANES), F32),
        ],
        cost_estimate=short,
        compiler_params=params,
    )(*messages, base_rows, out_full, ffn_gain[None], ffn_bias[None])
    entropy = entropy_wide[:, 0].reshape(items, row_total)

    ffn_blocks = spread_across(ffn_in, "items")
    ffn_plane, low_plane, result_part, *parts = pl.pallas_call(
        functools.partial(feed_kernel, devices=item_size, items=items),
        grid=(1,),
        in_specs=[smem]
        + [whole] * item_size
        + [
            pl.BlockSpec((width, low_columns), lambda i: (0, 2 * width // low_columns)),
            whole,
            whole,
        ],
        out_specs=[whole] * (3 + item_size),
        out_shape=[struct((plane, width), BF16)] * 2
        + [struct((item_size, own, width), BF16)]
        + [struct((own, width), BF16)] * item_size,
        cost_estimate=short,
        compiler_params=params,
    )(flags, *ffn_blocks, kv_full, up_slice, down_weight)
    grad_blocks = collect_across(parts, "items")
    query_full = lax.all_gather(after(query_weight, ffn_plane), "items", axis=0, tiled=True)

    turn, grad_branch, grad_base, ffn_sums = pl.pallas_call(
        functools.partial(turn_kernel, devices=item_size, chunks=CHUNKS, **sizes),
        out_shape=[
            struct((own, width + CHUNKS * LANES), BF16),
            struct((own, width), BF16),
            struct((row_total, width), F32),
            struct((8, width), F32),
        ],
        cost_estimate=short,
        compiler_params=params,
    )(*grad_blocks, mid_rows, grad_out, ffn_gain[None], merged, logs, out_full)
    turns = spread_on(turn, "frames")
    branch_plane = lax.all_gather(grad_branch, "items", axis=0, tiled=True)
    att_plane = lax.all_to_all(after(attended, turn), "items", 1, 0, tiled=True)
    result_pieces = lax.all_to_all(after(result_part, att_plane), "items", 0, 0)
    turns[0] = after(turns[0], low_other)

    chunk_grads, chunk_queries = [], []

    def weight_terms(c):
        send = matmul(send_rows, chunk_grads[c]).astype(BF16)
        received = send_across(send, "items", 1).reshape(-1, shard, 2 * half)
        keep = matmul(after(keep_rows, send), chunk_grads[c]).astype(BF16)
        return send, keep.reshape(-1, shard, 2 * half), received

    def chip_pieces(keep, received):
        sums = [keep[k].astype(F32) + received[k].astype(F32) for k in range(item_size // 2)]
        return sums[:1] + [p.astype(BF16) for p in sums[1:]]

    def send_pieces(sums):
        return sums[:1] + [
            send_across(p, "items", 2 * k) for k, p in enumerate(sums) if k
        ]

    def frame_rows(parts):
        rows, columns = parts[0].shape
        rows //= frame_size
        return pl.pallas_call(
            functools.partial(
                rows_kernel, count=len(parts), frames=frame_size, items=items
            ),
            in_specs=[smem] + [whole] * len(parts),
            out_specs=[whole] * frame_size,
            out_shape=[struct((rows, columns), F32)]
            + [struct((rows, columns), BF16)] * (frame_size - 1),
            scratch_shapes=[pltpu.VMEM((frame_size, rows, columns), F32)],
            cost_estimate=short,
            compiler_params=params,
        )(flags, *parts)

    def send_rows_on(rows):
        return [rows[0]] + [send_on(p, "frames", s) for s, p in enumerate(rows) if s]

    for c in range(CHUNKS):

        def block_of(g, c=c):
            return (0, c * groups + g)

        chunk_grad, chunk_query = pl.pallas_call(
            functools.partial(
                backward_kernel, frames=frame_size, patches=patches, scale=head_size**-0.5, **sizes
            ),
            grid=(groups,),
            in_specs=[
                smem,
                pl.BlockSpec((all_tokens, 2 * group_width), lambda g: (0, g)),
                pl.BlockSpec((lats, group_width), block_of),
                pl.BlockSpec((1, items, 8, stack), lambda g: (g, 0, 0, 0)),
            ]
            + [pl.BlockSpec((own, group_width), block_of)] * frame_size
            + [pl.BlockSpec((own, LANES), lambda g, c=c: (0, width // LANES + c))] * frame_size,
            out_specs=[
                pl.BlockSpec((all_tokens, 2 * group_width), lambda g: (0, g)),
                pl.BlockSpec((lats, group_width), lambda g: (0, g)),
            ],
            out_shape=[
                struct((all_tokens, 2 * half), BF16),
                struct((lats, half), F32),
            ],
            scratch_shapes=[
                pltpu.VMEM((items, lats, group_width), F32),
                pltpu.VMEM((items, lats, LANES), F32),
            ],
            cost_estimate=short,
            compiler_params=params,
        )(flags, after(boths[c], *held) if c else boths[c], queries, tops[c], *turns, *turns)
        chunk_grads.append(chunk_grad)
        chunk_queries.append(chunk_query)
        if c == 0:
            ffn_shift = spread_on(after(ffn_in, chunk_grad), "frames")[1:]
            first_send, first_keep, first_received = weight_terms(0)
            held = (first_send, att_plane)
    ffn_other = lax.all_gather(
        after(jnp.stack(ffn_shift), branch_plane), "items", axis=0
    ).reshape(-1, width)
    first_pieces = chip_pieces(after(first_keep, chunk_grads[-1]), first_received)
    first_sums = send_pieces(first_pieces)
    out_part = transposed_left(att_plane, after(branch_plane, chunk_grads[-1]))
    out_rows = frame_rows([out_part])
    out_moved = send_rows_on(out_rows)

    last_block = pl.BlockSpec((lats, 2 * half), lambda i: (tokens // lats, 0))
    media_grad, media_sums, lat_product = pl.pallas_call(
        functools.partial(media_kernel, chunks=CHUNKS, items=items, frames=frame_total),
        grid=(items,),
        in_specs=[smem]
        + [pl.BlockSpec((patches, 2 * half), lambda i: (i, 0))] * CHUNKS
        + [last_block] * CHUNKS
        + [pl.BlockSpec((width, 2 * half), lambda i, c=c: (0, c)) for c in range(CHUNKS)]
        + [pl.BlockSpec((patches, width), lambda i: (i, 0)), whole, whole],
        out_specs=[
            pl.BlockSpec((patches, width), lambda i: (i, 0)),
            pl.BlockSpec((16, width), lambda i: (0, 0)),
            pl.BlockSpec((lats, width), lambda i: (0, 0)),
        ],
        out_shape=[
            struct((tokens, width), BF16),
            struct((16, width), F32),
            struct((lats, width), F32),
        ],
        cost_estimate=short,
        compiler_params=params,
    )(
        flags,
        *chunk_grads[:-1],
        after(chunk_grads[-1], *first_pieces, *out_rows, *ffn_shift, result_pieces),
        *chunk_grads,
        *[kv_full] * CHUNKS,
        flat_media,
        time_rows,
        media_gain[None],
    )

    sum_rows = 2 * lats + 24
    sum_rows += -sum_rows % (8 * item_size)
    payload = pl.pallas_call(
        functools.partial(latent_kernel, chunks=CHUNKS, items=items),
        in_specs=[smem] + [whole] * (CHUNKS + 7),
        out_specs=whole,
        out_shape=struct((sum_rows, width), F32),
        cost_estimate=short,
        compiler_params=params,
    )(
        flags,
        *chunk_queries,
        after(lat_product, *first_sums, *out_moved),
        query_full,
        latents,
        latent_gain[None],
        grad_base,
        ffn_sums,
        media_sums,
    )
    payload_part = lax.psum_scatter(payload, "items", scatter_dimension=0, tiled=True)

    first_rows = frame_rows([after(first_sums[0], payload), *first_sums[1:]])
    first_moved = send_rows_on(first_rows)
    out_total = total_of(out_moved).astype(BF16)
    chunk_grads[-1] = after(chunk_grads[-1], payload, out_total, *first_rows)
    last_send, last_keep, last_received = weight_terms(CHUNKS - 1)
    out_placed = spread_on(out_total, "frames")
    last_pieces = chip_pieces(last_keep, last_received)
    last_sums = send_pieces(last_pieces)

    block_rows = min(512, plane)
    plane_blocks = plane // block_rows
    near = pl.BlockSpec((block_rows, width), lambda i: (jnp.minimum(i, plane_blocks - 1), 0))
    far = pl.BlockSpec((block_rows, width), lambda i: (jnp.maximum(i - plane_blocks, 0), 0))
    down_grad, up_part = pl.pallas_call(
        functools.partial(feed_grad_kernel, plane_blocks=plane_blocks),
        grid=(plane_blocks * frame_size,),
        in_specs=[near, near, far, far, whole, whole],
        out_specs=[
            pl.BlockSpec((hidden_shard, width), lambda i: (0, 0)),
            pl.BlockSpec((width, hidden_shard), lambda i: (0, 0)),
        ],
        out_shape=[struct((hidden_shard, width), F32), struct((width, hidden_shard), BF16)],
        scratch_shapes=[pltpu.VMEM((width, hidden_shard), F32)],
        cost_estimate=short,
        compiler_params=params,
    )(
        ffn_plane,
        low_plane,
        after(ffn_other, *first_moved, *last_pieces),
        low_other,
        up_slice,
        down_weight,
    )
    up_grad = lax.all_to_all(up_part, "items", 0, 1, tiled=True).astype(F32)

    first_placed = spread_on(total_of(first_moved).astype(BF16), "frames")
    last_moved = send_rows_on(frame_rows([after(last_sums[0], up_part), *last_sums[1:]]))
    last_placed = spread_on(total_of(last_moved).astype(BF16), "frames")
    placed = first_placed + last_placed + out_placed
    key_grad, value_grad, out_grad = pl.pallas_call(
        functools.partial(
            place_kernel, chunks=CHUNKS, frames=frame_size, items=items, groups=groups
        ),
        in_specs=[smem] + [whole] * len(placed),
        out_specs=[whole] * 3,
        out_shape=[struct((frame_size, shard // frame_size, width), F32)] * 3,
        cost_estimate=short,
        compiler_params=params,
    )(flags, *placed)

    payload_part = after(payload_part, up_part)
    payload_others = spread_on(payload_part.astype(BF16), "frames")[1:]
    sums = lax.all_gather(
        total_of([payload_part] + payload_others), "items", axis=0, tiled=True
    )
    latents_grad = sums[:lats]
    query_grad = transposed_left(lat_cols, sums[lats : 2 * lats].astype(BF16))
    at = 2 * lats
    column_sums = lax.dynamic_slice_in_dim(
        sums[at + 8 : at + 24], item_index * shard, shard, 1
    )

    result = mid_rows + total_of([result_pieces[d] for d in range(item_size)])
    return (
        result.reshape(items, row_total, width),
        entropy,
        media_grad.reshape(media.shape),
        latents_grad,
        column_sums[:frame_total],
        column_sums[8],
        column_sums[9],
        sums[at + 2],
        sums[at + 3],
        sums[at],
        sums[at + 1],
        query_grad,
        key_grad.reshape(shard, width),
        value_grad.reshape(shard, width),
        out_grad.reshape(shard, width),
        up_grad,
        down_grad,
    )


def solution(mesh):
    return jax.shard_map(
        body,
        mesh=mesh,
        in_specs=(
            P("items", "frames", None, None),
            P("items", "frames", None),
            P(),
            P(),
            P(),
            P(),
            P(),
            P(),
            P(),
            P(),
            P(),
            P(),
            P("items", None),
            P("items", None),
            P("items", None),
            P("items", None),
            P("items", None),
            P("items", None),
        ),
        out_specs=(
            P("items", "frames", None),
            P("items", "frames"),
            P("items", "frames", None, None),
            P(),
            P(None, "items"),
            P("items"),
            P("items"),
            P(),
            P(),
            P(),
            P(),
            P("items", None),
            P("items", None),
            P("items", None),
            P("items", None),
            P("items", None),
            P("items", None),
        ),
        check_vma=False,
    )
```

```python
import functools
import math

import jax
import jax.numpy as jnp
from jax import lax
from jax.experimental import pallas as pl
from jax.experimental.pallas import tpu as pltpu
from jax.sharding import PartitionSpec as P

HEADS = 16
GROUP = 4
CHUNKS = 2
LANES = 128
EPSILON = 1e-05
MASKED = -1e30
F32 = jnp.float32
BF16 = jnp.bfloat16
HIGHEST = lax.Precision.HIGHEST


def layer_norm(inputs, norm_gain, norm_bias):
    center = inputs - jnp.mean(inputs, axis=-1, keepdims=True)
    spread = jnp.mean(center * center, axis=-1, keepdims=True)
    return center * lax.rsqrt(spread + EPSILON) * norm_gain + norm_bias


def matmul(left_side, right_side):
    return jnp.dot(left_side, right_side, preferred_element_type=F32)


def transposed_left(left_side, right_side):
    return lax.dot_general(
        left_side, right_side, (((0,), (0,)), ((), ())), preferred_element_type=F32
    )


def transposed_right(left_side, right_side):
    return lax.dot_general(
        left_side, right_side, (((1,), (1,)), ((), ())), preferred_element_type=F32
    )


def send_on(x, axis, step):
    size = lax.axis_size(axis)
    return lax.ppermute(x, axis, [(i, (i + step) % size) for i in range(size)])


def send_across(x, axis, distance):
    return lax.ppermute(x, axis, [(i, i ^ distance) for i in range(lax.axis_size(axis))])


def spread_on(x, axis):
    return [x] + [send_on(x, axis, s) for s in range(1, lax.axis_size(axis))]


def spread_across(x, axis):
    chips = [x] + [send_across(x, axis, d) for d in range(2, lax.axis_size(axis), 2)]
    return [b for block in chips for b in (block, send_across(block, axis, 1))]


def collect_across(pieces, axis):
    return [pieces[0]] + [send_across(p, axis, d) for d, p in enumerate(pieces) if d]


def total_of(pieces):
    return functools.reduce(jnp.add, [p.astype(F32) for p in pieces])


def after(x, *earlier):
    return lax.optimization_barrier((x,) + earlier)[0]


def split_terms(x):
    high = x.astype(BF16)
    rest = x - high.astype(F32)
    middle = rest.astype(BF16)
    return high, middle, (rest - middle.astype(F32)).astype(BF16)


def iota(shape, dim):
    return lax.broadcasted_iota(jnp.int32, shape, dim)


def head_masks(rows, width, head_size):
    lane = iota((rows, width), 1)
    return [
        jnp.logical_and(lane >= h * head_size, lane < (h + 1) * head_size)
        for h in range(width // head_size)
    ]


def spread_heads(block, masks):
    return jnp.concatenate([jnp.where(m, block, jnp.zeros_like(block)) for m in masks], 0)


def collect_heads(block, masks):
    rows = block.shape[0] // len(masks)
    total = jnp.where(masks[0], block[:rows], 0.0)
    for h in range(1, len(masks)):
        total = total + jnp.where(masks[h], block[h * rows : (h + 1) * rows], 0.0)
    return total


def head_expand(width, head_size):
    row, column = iota((LANES, width), 0), iota((LANES, width), 1)
    return jnp.logical_and(column >= row * head_size, column < (row + 1) * head_size).astype(F32)


def live_rows(flag_ref, item, items, patches, lats, columns):
    row = iota((patches + lats, columns), 0)
    media = jnp.logical_and(row < patches, flag_ref[item] > 0)
    return jnp.logical_or(media, jnp.logical_and(row >= patches, flag_ref[items] > 0))


def pack_shape(own, shard, width):
    unit = math.gcd(own, shard)
    return unit, width * unit // shard


def join_kernel(key_ref, value_ref, cotangent_ref, out_ref, low_ref, *, width):
    for g in range(key_ref.shape[1] // width):
        columns = slice(g * width, (g + 1) * width)
        out_ref[:, 2 * g * width : (2 * g + 1) * width] = key_ref[:, columns]
        out_ref[:, (2 * g + 1) * width : (2 * g + 2) * width] = value_ref[:, columns]
    low = cotangent_ref[...].astype(BF16)
    low_ref[...] = low
    own, span = low.shape
    unit, piece = pack_shape(own, out_ref.shape[0], span)
    for a in range(own // unit):
        for b in range(span // piece):
            at = 2 * span + a * piece
            out_ref[b * unit : (b + 1) * unit, at : at + piece] = low[
                a * unit : (a + 1) * unit, b * piece : (b + 1) * piece
            ]


def norm_kernel(media_ref, time_ref, gain_ref, bias_ref, lat_ref, out_ref, *, steps, per_item):
    step = pl.program_id(0)

    @pl.when(step < steps)
    def _():
        rows = media_ref[...].astype(F32) + time_ref[pl.ds(step // per_item, 1), :]
        out_ref[...] = layer_norm(rows, gain_ref[...], bias_ref[...]).astype(BF16)

    @pl.when(step == steps)
    def _():
        out_ref[...] = lat_ref[...]


def forward_kernel(
    flag_ref, both_ref, query_ref, top_ref, *refs, items, patches, scale, head_size, heads,
):
    message_refs, (part_ref, mark_ref) = refs[:-2], refs[-2:]
    lats, width = query_ref.shape
    frames = len(message_refs)
    own = message_refs[0].shape[0]
    row_total = own // items
    masks = head_masks(lats, width, head_size)
    queries = spread_heads(query_ref[...].astype(F32), masks).astype(BF16)
    base = items * patches
    lat_both = both_ref[base : base + lats, :]
    group = pl.program_id(0)
    term, lane = iota((16, GROUP * LANES), 0), iota((16, GROUP * LANES), 1)
    place = jnp.logical_and(
        lane % LANES == term * heads + group * GROUP + lane // LANES, term < 9
    ).astype(BF16)
    for i in range(items):
        both = jnp.concatenate([both_ref[i * patches : (i + 1) * patches, :], lat_both], 0)
        live = live_rows(flag_ref, i, items, patches, lats, queries.shape[0])
        scores = scale * transposed_right(both[:, :width], queries)
        masked = jnp.where(live, scores, MASKED)
        top = jnp.max(masked, axis=0, keepdims=True)
        block_exp = jnp.where(live, jnp.exp(masked - top), 0.0)
        total = jnp.sum(block_exp, axis=0, keepdims=True)
        moment = jnp.sum(block_exp * scores, axis=0, keepdims=True)
        part = transposed_left(block_exp.astype(BF16), both[:, width:])
        part_ref[i] = collect_heads(part, masks)
        top_ref[0, i] = jnp.broadcast_to(top, top_ref.shape[2:])
        terms = jnp.concatenate(
            [t.astype(F32) for x in (top, total, moment) for t in split_terms(x)]
            + [jnp.zeros((7, top.shape[1]), F32)],
            0,
        ).astype(BF16)
        wide = transposed_left(terms, place)
        mark = wide[:lats, :LANES]
        for h in range(1, GROUP):
            mark = mark + wide[h * lats : (h + 1) * lats, h * LANES : (h + 1) * LANES]
        mark_ref[i] = mark

    end = message_refs[0].shape[1] - LANES
    for s, message_ref in enumerate(message_refs):
        start = pl.multiple_of(lax.rem(flag_ref[items + 1] + s, frames) * row_total, row_total)
        rows = pl.ds(start, row_total)
        block = jnp.concatenate([part_ref[i, rows, :] for i in range(items)], 0).astype(BF16)
        mark = jnp.concatenate([mark_ref[i, rows, :] for i in range(items)], 0).astype(BF16)
        for g in range(end // width):

            @pl.when(group == g)
            def _():
                message_ref[:, g * width : (g + 1) * width] = block
                if g == 0:
                    message_ref[:, end:] = mark
                else:
                    message_ref[:, end:] = message_ref[:, end:] + mark


def merge_kernel(*refs, chunks, frames, items, head_size, heads):
    message_refs = refs[: chunks * frames]
    base_ref, weight_ref, gain_ref, bias_ref = refs[chunks * frames : chunks * frames + 4]
    merged_ref, attended_ref, mid_ref, ffn_ref, log_ref, entropy_ref = refs[chunks * frames + 4 :]
    own, columns = message_refs[0].shape
    half = columns - LANES
    lane, column = iota((LANES, 3 * LANES), 0), iota((LANES, 3 * LANES), 1)
    gather = jnp.logical_and(
        jnp.logical_and(lane // heads // 3 == column // LANES, lane % heads == column % LANES),
        lane < 9 * heads,
    ).astype(BF16)
    expand = head_expand(half, head_size)
    live = iota((own, LANES), 1) < heads
    spread = jnp.zeros((own, LANES), F32)
    for c in range(chunks):
        sources = message_refs[c * frames : (c + 1) * frames]
        stats = [matmul(x[:, half:], gather) for x in sources]
        tops = [x[:, :LANES] for x in stats]
        peak = functools.reduce(jnp.maximum, tops)
        factors = [jnp.exp(t - peak) for t in tops]
        whole = sum(f * x[:, LANES : 2 * LANES] for f, x in zip(factors, stats))
        moment = sum(f * x[:, 2 * LANES :] for f, x in zip(factors, stats))
        whole = jnp.where(live, whole, 1.0)
        log_total = jnp.where(live, peak + jnp.log(whole), 0.0)
        log_ref[c] = log_total
        spread = spread + jnp.where(live, log_total - moment / whole, 0.0)
        merged = jnp.zeros((own, half), F32)
        for x, factor in zip(sources, factors):
            share = jnp.where(live, factor / whole, 0.0)
            wide = jnp.dot(share, expand, precision=HIGHEST, preferred_element_type=F32)
            merged = merged + x[:, :half].astype(F32) * wide
        merged_ref[:, c * half : (c + 1) * half] = merged
        attended_ref[:, c * half : (c + 1) * half] = merged.astype(BF16)
    entropy_ref[...] = jnp.broadcast_to(
        jnp.sum(spread, axis=1, keepdims=True) * (1.0 / HEADS), entropy_ref.shape
    )
    base = jnp.concatenate([base_ref[...]] * items, 0)
    mid = base + matmul(attended_ref[...], weight_ref[...])
    mid_ref[...] = mid
    ffn_ref[...] = layer_norm(mid, gain_ref[...], bias_ref[...]).astype(BF16)


def gelu_parts(x):
    share = 0.5 * (1.0 + lax.erf(x * (0.5**0.5)))
    slope = share + x * jnp.exp(-0.5 * x * x) * ((2.0 * jnp.pi) ** -0.5)
    return x * share, slope


def feed_kernel(flag_ref, *refs, devices, items):
    row_refs = refs[:devices]
    low_ref, up_ref, down_ref, plane_ref, plane_low_ref, result_ref = refs[devices : devices + 6]
    grad_refs = refs[devices + 6 :]
    own, width = row_refs[0].shape
    shard = low_ref.shape[0] // devices
    unit, piece = pack_shape(own, shard, width)
    me = flag_ref[2 * items + 2]
    for d in range(devices):
        plane_ref[d * own : (d + 1) * own, :] = row_refs[d][...]
        source = jnp.bitwise_xor(me, d) * shard
        for a in range(own // unit):
            rows = slice(d * own + a * unit, d * own + (a + 1) * unit)
            for b in range(shard // unit):
                start = pl.multiple_of(source + b * unit, unit)
                plane_low_ref[rows, b * piece : (b + 1) * piece] = low_ref[
                    pl.ds(start, unit), a * piece : (a + 1) * piece
                ]
    upward = matmul(plane_ref[...], up_ref[...])
    hidden, slope = gelu_parts(upward)
    grad_up = (slope * transposed_right(plane_low_ref[...], down_ref[...])).astype(BF16)
    grad = transposed_right(grad_up, up_ref[...]).astype(BF16)
    result = matmul(hidden.astype(BF16), down_ref[...]).astype(BF16)
    for d in range(devices):
        grad_refs[d][...] = grad[d * own : (d + 1) * own, :]
        result_ref[jnp.bitwise_xor(me, d)] = result[d * own : (d + 1) * own, :]


def feed_back_kernel(
    plane_ref, plane_low_ref, other_ref, other_low_ref, up_ref, down_ref, hidden_ref, grad_ref, *,
    plane_blocks,
):
    near = pl.program_id(0) < plane_blocks
    rows = jnp.where(near, plane_ref[...], other_ref[...])
    low = jnp.where(near, plane_low_ref[...], other_low_ref[...])
    hidden, slope = gelu_parts(matmul(rows, up_ref[...]))
    hidden_ref[...] = hidden.astype(BF16)
    grad_ref[...] = (slope * transposed_right(low, down_ref[...])).astype(BF16)


def outer_kernel(plane_ref, other_ref, stacked_ref, out_ref, total_ref, *, plane_blocks, flip):
    step = pl.program_id(0)
    rows = jnp.where(step < plane_blocks, plane_ref[...], other_ref[...])
    pair = (stacked_ref[...], rows) if flip else (rows, stacked_ref[...])
    part = transposed_left(*pair)

    @pl.when(step == 0)
    def _():
        total_ref[...] = part

    @pl.when(step > 0)
    def _():
        total_ref[...] += part

    @pl.when(step == pl.num_programs(0) - 1)
    def _():
        out_ref[...] = total_ref[...].astype(out_ref.dtype)


def norm_backward(rows, gain, gradient):
    center = rows - jnp.mean(rows, axis=1, keepdims=True)
    rate = lax.rsqrt(jnp.mean(center * center, axis=1, keepdims=True) + EPSILON)
    unit = center * rate
    scaled = gradient * gain
    inner = scaled - jnp.mean(scaled, axis=1, keepdims=True)
    back = rate * (inner - unit * jnp.mean(scaled * unit, axis=1, keepdims=True))
    return (
        back,
        jnp.sum(gradient * unit, axis=0, keepdims=True),
        jnp.sum(gradient, axis=0, keepdims=True),
    )


def turn_kernel(*refs, devices, items, chunks, head_size, heads):
    part_refs = refs[:devices]
    mid_ref, cotangent_ref, gain_ref, merged_ref, log_ref, weight_ref = refs[
        devices : devices + 6
    ]
    message_ref, branch_ref, base_ref, sums_ref = refs[devices + 6 :]
    own, width = mid_ref.shape
    half = width // chunks
    gradient = total_of([x[...] for x in part_refs])
    back, gain_sum, bias_sum = norm_backward(mid_ref[...], gain_ref[...], gradient)
    grad_mid = cotangent_ref[...] + back
    sums_ref[...] = jnp.zeros(sums_ref.shape, F32)
    sums_ref[0:1, :] = gain_sum
    sums_ref[1:2, :] = bias_sum
    row_total = own // items
    base_ref[...] = total_of(
        [grad_mid[i * row_total : (i + 1) * row_total] for i in range(items)]
    )
    branch = grad_mid.astype(BF16)
    branch_ref[...] = branch
    grad_att = transposed_right(branch, weight_ref[...]).astype(BF16)
    expand = head_expand(half, head_size)
    lane, column = iota((6 * LANES, LANES), 0), iota((6 * LANES, LANES), 1)
    place = jnp.logical_and(
        lane % LANES < heads, column == (lane // LANES) * heads + lane % LANES
    ).astype(BF16)
    message_ref[:, :width] = grad_att
    for c in range(chunks):
        columns = slice(c * half, (c + 1) * half)
        delta = lax.dot_general(
            merged_ref[:, columns] * grad_att[:, columns].astype(F32),
            expand,
            (((1,), (1,)), ((), ())),
            precision=HIGHEST,
            preferred_element_type=F32,
        )
        terms = jnp.concatenate([t for x in (log_ref[c], delta) for t in split_terms(x)], 1)
        message_ref[:, width + c * LANES : width + (c + 1) * LANES] = matmul(
            terms, place
        ).astype(BF16)


def backward_kernel(
    *refs, frames, items, patches, scale, head_size, heads,
):
    flag_ref, both_ref, query_ref, top_ref = refs[:4]
    grad_refs = refs[4 : 4 + frames]
    mark_refs = refs[4 + frames : 4 + 2 * frames]
    out_ref, sum_ref, held_ref, note_ref = refs[4 + 2 * frames :]
    lats, width = query_ref.shape
    own = grad_refs[0].shape[0]
    row_total = own // items
    base = items * patches
    for s in range(frames):
        source = lax.rem(flag_ref[items + 1] + (frames - s), frames)
        rows = pl.ds(pl.multiple_of(source * row_total, row_total), row_total)
        block = grad_refs[s][...].astype(F32)
        mark = mark_refs[s][...].astype(F32)
        for i in range(items):
            held_ref[i, rows, :] = block[i * row_total : (i + 1) * row_total]
            note_ref[i, rows, :] = mark[i * row_total : (i + 1) * row_total]
    masks = head_masks(lats, width, head_size)
    queries = spread_heads(query_ref[...].astype(F32), masks).astype(BF16)
    lat_both = both_ref[base : base + lats, :]
    row, lane = iota((GROUP * 8, LANES), 0), iota((GROUP * 8, LANES), 1)
    pick = jnp.logical_and(
        jnp.logical_and(
            lane // heads // 3 == row % 8,
            lane % heads == pl.program_id(0) * GROUP + row // 8,
        ),
        lane < 6 * heads,
    ).astype(BF16)
    grad_query = jnp.zeros((queries.shape[0], width), F32)
    lat_grad_key = jnp.zeros((lats, width), F32)
    lat_grad_value = jnp.zeros((lats, width), F32)
    for i in range(items):
        rows = slice(i * patches, (i + 1) * patches)
        stats = transposed_right(pick, note_ref[i].astype(BF16))
        stats = jnp.concatenate([stats[h * 8 : (h + 1) * 8] for h in range(GROUP)], 1)
        log_total = stats[0:1]
        delta = stats[1:2]
        top = top_ref[0, i, 0:1, :]
        rescale = jnp.exp(top - log_total)
        both = jnp.concatenate([both_ref[rows, :], lat_both], 0)
        keys, values = both[:, :width], both[:, width:]
        grads = spread_heads(held_ref[i], masks).astype(BF16)
        live = live_rows(flag_ref, i, items, patches, lats, queries.shape[0])
        masked = jnp.where(live, scale * transposed_right(keys, queries), MASKED)
        probs = jnp.where(live, jnp.exp(masked - log_total), 0.0)
        block_exp = jnp.where(live, jnp.exp(masked - top), 0.0)
        weights = (block_exp.astype(BF16).astype(F32) * rescale).astype(BF16)
        grad_scores = (probs * (transposed_right(values, grads) - delta)).astype(BF16)
        grad_key = scale * matmul(grad_scores, queries)
        grad_value = matmul(weights, grads)
        out_ref[rows, :width] = grad_key[:patches].astype(BF16)
        out_ref[rows, width:] = grad_value[:patches].astype(BF16)
        grad_query = grad_query + transposed_left(grad_scores, keys)
        lat_grad_key = lat_grad_key + grad_key[patches:]
        lat_grad_value = lat_grad_value + grad_value[patches:]
    out_ref[base : base + lats, :width] = lat_grad_key.astype(BF16)
    out_ref[base : base + lats, width:] = lat_grad_value.astype(BF16)
    sum_ref[...] = scale * collect_heads(grad_query, masks)


def media_kernel(flag_ref, *refs, chunks, items, frames):
    grad_refs, lat_refs, weight_refs = [
        refs[k * chunks : (k + 1) * chunks] for k in range(3)
    ]
    media_ref, time_ref, gain_ref, out_ref, sums_ref, product_ref = refs[3 * chunks :]
    item = pl.program_id(0)

    @pl.when(item == 0)
    def _():
        sums_ref[...] = jnp.zeros(sums_ref.shape, F32)
        product_ref[...] = functools.reduce(
            jnp.add, [transposed_right(g[...], w[...]) for g, w in zip(lat_refs, weight_refs)]
        )

    gradient = functools.reduce(
        jnp.add, [transposed_right(g[...], w[...]) for g, w in zip(grad_refs, weight_refs)]
    )
    inputs = media_ref[...].astype(F32) + time_ref[pl.ds(item, 1), :]
    back, gain_sum, bias_sum = norm_backward(inputs, gain_ref[...], gradient)
    out_ref[...] = back.astype(BF16)
    place = iota((frames, 1), 0) == flag_ref[items + 2 + item]
    sums_ref[0:frames, :] += jnp.where(place, jnp.sum(back, axis=0, keepdims=True), 0.0)
    sums_ref[8:9, :] += gain_sum
    sums_ref[9:10, :] += bias_sum


def latent_kernel(flag_ref, *refs, chunks, items):
    query_refs = refs[:chunks]
    (
        product_ref, query_weight_ref, latent_ref, gain_ref, base_ref, ffn_ref, media_ref, out_ref,
    ) = refs[chunks:]
    lats, width = latent_ref.shape
    half = width // chunks
    gradient = product_ref[...]
    for c in range(chunks):
        gradient = gradient + transposed_right(
            query_refs[c][...].astype(BF16), query_weight_ref[:, c * half : (c + 1) * half]
        )
        out_ref[lats : 2 * lats, c * half : (c + 1) * half] = query_refs[c][...]
    back, gain_sum, bias_sum = norm_backward(latent_ref[...], gain_ref[...], gradient)
    out_ref[:lats, :] = back
    row_total = base_ref.shape[0]
    start = pl.multiple_of(flag_ref[items + 1] * row_total, row_total)
    out_ref[pl.ds(start, row_total), :] += base_ref[...]
    at = 2 * lats
    out_ref[at : at + 8, :] = ffn_ref[...]
    out_ref[at + 2 : at + 3, :] = gain_sum
    out_ref[at + 3 : at + 4, :] = bias_sum
    out_ref[at + 8 : at + 24, :] = media_ref[...]
    out_ref[at + 24 :, :] = jnp.zeros((out_ref.shape[0] - at - 24, width), F32)


def rows_kernel(flag_ref, *refs, count, frames, items):
    total = total_of([x[...] for x in refs[:count]])
    out_refs, held_ref = refs[count:-1], refs[-1]
    rows = total.shape[0] // frames
    for f in range(frames):
        held_ref[f] = total[f * rows : (f + 1) * rows]
    for s, out_ref in enumerate(out_refs):
        block = held_ref[lax.rem(flag_ref[items + 1] + s, frames)]
        out_ref[...] = block.astype(out_ref.dtype)


def place_kernel(flag_ref, *refs, chunks, frames, items, groups):
    chunk_refs = refs[: chunks * frames]
    more_refs = refs[chunks * frames : (chunks + 1) * frames]
    key_ref, value_ref, out_ref = refs[(chunks + 1) * frames :]
    width = key_ref.shape[2] // (chunks * groups)
    for s in range(frames):
        source = lax.rem(flag_ref[items + 1] + (frames - s), frames)
        out_ref[source] = more_refs[s][...].astype(F32)
        for c in range(chunks):
            for g in range(groups):
                at = (c * groups + g) * width
                block = chunk_refs[c * frames + s][:, 2 * g * width : 2 * (g + 1) * width]
                block = block.astype(F32)
                key_ref[source, :, at : at + width] = block[:, :width]
                value_ref[source, :, at : at + width] = block[:, width:]


def body(
    media,
    cotangent,
    frame_count,
    frame_start,
    latents,
    time_embed,
    media_gain,
    media_bias,
    latent_gain,
    latent_bias,
    ffn_gain,
    ffn_bias,
    query_weight,
    key_weight,
    value_weight,
    out_weight,
    up_weight,
    down_weight,
):
    items = media.shape[0]
    patches = media.shape[2]
    width = media.shape[3]
    lats = latents.shape[0]
    frame_total = time_embed.shape[0]
    row_total = cotangent.shape[1]
    own = items * row_total
    head_size = width // HEADS
    half = width // CHUNKS
    chunk_heads = HEADS // CHUNKS
    group_width = GROUP * head_size
    groups = chunk_heads // GROUP
    stack = GROUP * lats
    tokens = items * patches
    all_tokens = tokens + lats
    shard = query_weight.shape[0]
    hidden_shard = down_weight.shape[0]
    item_size = lax.axis_size("items")
    frame_size = lax.axis_size("frames")
    plane = item_size * own
    item_index = lax.axis_index("items")
    slot = lax.axis_index("frames")
    row_base = slot * row_total
    params = pltpu.CompilerParams(vmem_limit_bytes=56 * 2**20)
    smem = pl.BlockSpec(memory_space=pltpu.SMEM)
    whole = pl.BlockSpec(memory_space=pltpu.VMEM)
    sizes = dict(items=items, head_size=head_size, heads=chunk_heads)

    def struct(shape, kind):
        return jax.ShapeDtypeStruct(shape, kind)

    short = pl.CostEstimate(flops=1000, bytes_accessed=1000, transcendentals=0)

    def column_blocks(x):
        return jnp.transpose(x.reshape(-1, item_size, shard), (1, 0, 2))

    def scatter_exchange(x, axis):
        return jnp.sum(lax.all_to_all(x, axis, 0, 0).astype(F32), axis=0)

    grad_out = cotangent.reshape(own, width)
    low_columns = own * width // shard
    joined, grad_low = pl.pallas_call(
        functools.partial(join_kernel, width=group_width),
        out_shape=[struct((shard, 2 * width + low_columns), BF16), struct((own, width), BF16)],
        cost_estimate=short,
        compiler_params=params,
    )(key_weight, value_weight, grad_out)
    kv_full = lax.all_gather(joined, "items", axis=0, tiled=True)

    lat_norm = layer_norm(latents, latent_gain, latent_bias).astype(BF16)
    lat_cols = lax.dynamic_slice_in_dim(lat_norm, item_index * shard, shard, 1)
    query_blocks = column_blocks(matmul(lat_cols, query_weight))
    query_cols = scatter_exchange(query_blocks, "items").astype(BF16)
    query_spread = jnp.broadcast_to(query_cols[None], (item_size, lats, shard))
    queries = jnp.transpose(lax.all_to_all(query_spread, "items", 0, 0), (1, 0, 2)).reshape(
        lats, width
    )

    counts = lax.dynamic_slice_in_dim(frame_count, item_index * items, items)
    starts = lax.dynamic_slice_in_dim(frame_start, item_index * items, items)
    offset = (slot - starts) % frame_total
    flags = jnp.concatenate(
        [
            (offset < counts).astype(jnp.int32),
            (slot == 0).astype(jnp.int32)[None],
            slot.astype(jnp.int32)[None],
            offset.astype(jnp.int32),
            item_index.astype(jnp.int32)[None],
        ]
    )
    picker = (offset[:, None] == jnp.arange(frame_total, dtype=jnp.int32)[None, :]).astype(F32)
    time_rows = jnp.dot(picker, time_embed, precision=HIGHEST, preferred_element_type=F32)
    flat_media = media.reshape(tokens, width)
    steps = tokens // lats
    all_rows = pl.pallas_call(
        functools.partial(norm_kernel, steps=steps, per_item=patches // lats),
        grid=(steps + 1,),
        in_specs=[
            pl.BlockSpec((lats, width), lambda i: (jnp.minimum(i, steps - 1), 0)),
            whole,
            whole,
            whole,
            whole,
        ],
        out_specs=pl.BlockSpec((lats, width), lambda i: (i, 0)),
        out_shape=struct((all_tokens, width), BF16),
        cost_estimate=short,
        compiler_params=params,
    )(
        after(flat_media, query_blocks),
        time_rows,
        media_gain[None],
        media_bias[None],
        lat_norm,
    )
    out_full = lax.all_gather(after(out_weight, all_rows), "items", axis=0, tiled=True)

    chip, core = item_index // 2, item_index % 2
    rows_across = after(all_rows, query_cols).T.reshape(item_size // 2, 2, shard, all_tokens)
    send_rows, keep_rows = [
        jnp.concatenate(
            [
                lax.dynamic_slice(
                    rows_across, (chip ^ k, which, 0, 0), (1, 1, shard, all_tokens)
                ).reshape(shard, all_tokens)
                for k in range(item_size // 2)
            ],
            0,
        )
        for which in (1 - core, core)
    ]
    low_shift = spread_on(after(grad_low, all_rows), "frames")[1:]

    boths, tops, messages = [], [], []
    for c in range(CHUNKS):

        def block_of(g, c=c):
            return (0, c * groups + g)

        if c:
            rows = after(all_rows, tops[-1])
        else:
            rows = after(all_rows, queries, send_rows, keep_rows, *low_shift)
        both = matmul(rows, kv_full[:, 2 * c * half : 2 * (c + 1) * half]).astype(BF16)
        top, *parts = pl.pallas_call(
            functools.partial(
                forward_kernel, patches=patches, scale=head_size**-0.5, **sizes
            ),
            grid=(groups,),
            in_specs=[
                smem,
                pl.BlockSpec((all_tokens, 2 * group_width), lambda g: (0, g)),
                pl.BlockSpec((lats, group_width), block_of),
            ],
            out_specs=[pl.BlockSpec((1, items, 8, stack), lambda g: (g, 0, 0, 0))]
            + [pl.BlockSpec((own, half + LANES), lambda g: (0, 0))] * frame_size,
            out_shape=[struct((groups, items, 8, stack), F32)]
            + [struct((own, half + LANES), BF16)] * frame_size,
            scratch_shapes=[
                pltpu.VMEM((items, lats, group_width), F32),
                pltpu.VMEM((items, lats, LANES), F32),
            ],
            cost_estimate=short,
            compiler_params=params,
        )(flags, both, queries)
        boths.append(both)
        tops.append(top)
        messages += [p if s == 0 else send_on(p, "frames", s) for s, p in enumerate(parts)]
    up_slice = lax.all_to_all(after(up_weight, boths[0]), "items", 1, 0, tiled=True)
    low_other = lax.all_gather(
        after(jnp.stack(low_shift), tops[1]), "items", axis=0
    ).reshape(-1, width)

    base_rows = lax.dynamic_slice_in_dim(latents, row_base, row_total, 0)
    merged, attended, mid_rows, ffn_in, logs, entropy_wide = pl.pallas_call(
        functools.partial(merge_kernel, chunks=CHUNKS, frames=frame_size, **sizes),
        out_shape=[
            struct((own, width), F32),
            struct((own, width), BF16),
            struct((own, width), F32),
            struct((own, width), BF16),
            struct((CHUNKS, own, LANES), F32),
            struct((own, LANES), F32),
        ],
        cost_estimate=short,
        compiler_params=params,
    )(*messages, base_rows, out_full, ffn_gain[None], ffn_bias[None])
    entropy = entropy_wide[:, 0].reshape(items, row_total)

    query_full = lax.all_gather(after(query_weight, ffn_in), "items", axis=0, tiled=True)
    ffn_blocks = spread_across(ffn_in, "items")
    ffn_plane, low_plane, result_part, *parts = pl.pallas_call(
        functools.partial(feed_kernel, devices=item_size, items=items),
        grid=(1,),
        in_specs=[smem]
        + [whole] * item_size
        + [
            pl.BlockSpec((width, low_columns), lambda i: (0, 2 * width // low_columns)),
            whole,
            whole,
        ],
        out_specs=[whole] * (3 + item_size),
        out_shape=[struct((plane, width), BF16)] * 2
        + [struct((item_size, own, width), BF16)]
        + [struct((own, width), BF16)] * item_size,
        cost_estimate=short,
        compiler_params=params,
    )(flags, *ffn_blocks, kv_full, up_slice, down_weight)
    grad_blocks = collect_across(parts, "items")
    ffn_shift = spread_on(after(ffn_in, *ffn_blocks), "frames")[1:]
    ffn_other = lax.all_gather(jnp.stack(ffn_shift), "items", axis=0).reshape(-1, width)
    grad_blocks[0] = after(grad_blocks[0], *ffn_shift)

    turn, grad_branch, grad_base, ffn_sums = pl.pallas_call(
        functools.partial(turn_kernel, devices=item_size, chunks=CHUNKS, **sizes),
        out_shape=[
            struct((own, width + CHUNKS * LANES), BF16),
            struct((own, width), BF16),
            struct((row_total, width), F32),
            struct((8, width), F32),
        ],
        cost_estimate=short,
        compiler_params=params,
    )(*grad_blocks, mid_rows, grad_out, ffn_gain[None], merged, logs, out_full)
    turns = spread_on(turn, "frames")
    branch_plane = lax.all_gather(grad_branch, "items", axis=0, tiled=True)
    att_plane = lax.all_to_all(after(attended, turn), "items", 1, 0, tiled=True)
    result_pieces = lax.all_to_all(after(result_part, att_plane), "items", 0, 0)
    turns[0] = after(turns[0], low_other, query_full)

    chunk_grads, chunk_queries = [], []

    def weight_terms(c):
        send = matmul(send_rows, chunk_grads[c]).astype(BF16)
        received = send_across(send, "items", 1).reshape(-1, shard, 2 * half)
        keep = matmul(after(keep_rows, send), chunk_grads[c]).astype(BF16)
        return send, keep.reshape(-1, shard, 2 * half), received

    def chip_pieces(keep, received):
        sums = [keep[k].astype(F32) + received[k].astype(F32) for k in range(item_size // 2)]
        return sums[:1] + [p.astype(BF16) for p in sums[1:]]

    def send_pieces(sums):
        return sums[:1] + [
            send_across(p, "items", 2 * k) for k, p in enumerate(sums) if k
        ]

    def frame_rows(parts):
        rows, columns = parts[0].shape
        rows //= frame_size
        return pl.pallas_call(
            functools.partial(
                rows_kernel, count=len(parts), frames=frame_size, items=items
            ),
            in_specs=[smem] + [whole] * len(parts),
            out_specs=[whole] * frame_size,
            out_shape=[struct((rows, columns), F32)]
            + [struct((rows, columns), BF16)] * (frame_size - 1),
            scratch_shapes=[pltpu.VMEM((frame_size, rows, columns), F32)],
            cost_estimate=short,
            compiler_params=params,
        )(flags, *parts)

    def send_rows_on(rows):
        return [rows[0]] + [send_on(p, "frames", s) for s, p in enumerate(rows) if s]

    for c in range(CHUNKS):

        def block_of(g, c=c):
            return (0, c * groups + g)

        chunk_grad, chunk_query = pl.pallas_call(
            functools.partial(
                backward_kernel, frames=frame_size, patches=patches, scale=head_size**-0.5, **sizes
            ),
            grid=(groups,),
            in_specs=[
                smem,
                pl.BlockSpec((all_tokens, 2 * group_width), lambda g: (0, g)),
                pl.BlockSpec((lats, group_width), block_of),
                pl.BlockSpec((1, items, 8, stack), lambda g: (g, 0, 0, 0)),
            ]
            + [pl.BlockSpec((own, group_width), block_of)] * frame_size
            + [pl.BlockSpec((own, LANES), lambda g, c=c: (0, width // LANES + c))] * frame_size,
            out_specs=[
                pl.BlockSpec((all_tokens, 2 * group_width), lambda g: (0, g)),
                pl.BlockSpec((lats, group_width), lambda g: (0, g)),
            ],
            out_shape=[
                struct((all_tokens, 2 * half), BF16),
                struct((lats, half), F32),
            ],
            scratch_shapes=[
                pltpu.VMEM((items, lats, group_width), F32),
                pltpu.VMEM((items, lats, LANES), F32),
            ],
            cost_estimate=short,
            compiler_params=params,
        )(flags, after(boths[c], *held) if c else boths[c], queries, tops[c], *turns, *turns)
        chunk_grads.append(chunk_grad)
        chunk_queries.append(chunk_query)
        if c == 0:
            first_send, first_keep, first_received = weight_terms(0)
            held = (first_send,)
    first_pieces = chip_pieces(after(first_keep, chunk_grads[-1]), first_received)
    first_sums = send_pieces(first_pieces)
    out_part = transposed_left(att_plane, after(branch_plane, chunk_grads[-1]))
    out_rows = frame_rows([out_part])
    out_moved = send_rows_on(out_rows)

    last_block = pl.BlockSpec((lats, 2 * half), lambda i: (tokens // lats, 0))
    media_grad, media_sums, lat_product = pl.pallas_call(
        functools.partial(media_kernel, chunks=CHUNKS, items=items, frames=frame_total),
        grid=(items,),
        in_specs=[smem]
        + [pl.BlockSpec((patches, 2 * half), lambda i: (i, 0))] * CHUNKS
        + [last_block] * CHUNKS
        + [pl.BlockSpec((width, 2 * half), lambda i, c=c: (0, c)) for c in range(CHUNKS)]
        + [pl.BlockSpec((patches, width), lambda i: (i, 0)), whole, whole],
        out_specs=[
            pl.BlockSpec((patches, width), lambda i: (i, 0)),
            pl.BlockSpec((16, width), lambda i: (0, 0)),
            pl.BlockSpec((lats, width), lambda i: (0, 0)),
        ],
        out_shape=[
            struct((tokens, width), BF16),
            struct((16, width), F32),
            struct((lats, width), F32),
        ],
        cost_estimate=short,
        compiler_params=params,
    )(
        flags,
        *chunk_grads[:-1],
        after(chunk_grads[-1], *first_pieces, *out_rows, ffn_other),
        *chunk_grads,
        *[kv_full] * CHUNKS,
        flat_media,
        time_rows,
        media_gain[None],
    )

    sum_rows = 2 * lats + 24
    sum_rows += -sum_rows % (8 * item_size)
    payload = pl.pallas_call(
        functools.partial(latent_kernel, chunks=CHUNKS, items=items),
        in_specs=[smem] + [whole] * (CHUNKS + 7),
        out_specs=whole,
        out_shape=struct((sum_rows, width), F32),
        cost_estimate=short,
        compiler_params=params,
    )(
        flags,
        *chunk_queries,
        after(lat_product, *first_sums, *out_moved, result_pieces),
        query_full,
        latents,
        latent_gain[None],
        grad_base,
        ffn_sums,
        media_sums,
    )
    payload_part = lax.psum_scatter(payload, "items", scatter_dimension=0, tiled=True)

    first_rows = frame_rows([after(first_sums[0], payload), *first_sums[1:]])
    first_moved = send_rows_on(first_rows)
    out_total = total_of(out_moved).astype(BF16)
    chunk_grads[-1] = after(chunk_grads[-1], payload, out_total, *first_rows)
    last_send, last_keep, last_received = weight_terms(CHUNKS - 1)
    out_placed = spread_on(out_total, "frames")
    last_pieces = chip_pieces(last_keep, last_received)
    last_sums = send_pieces(last_pieces)

    block_rows = min(512, plane)
    plane_blocks = plane // block_rows
    near = pl.BlockSpec((block_rows, width), lambda i: (jnp.minimum(i, plane_blocks - 1), 0))
    far = pl.BlockSpec((block_rows, width), lambda i: (jnp.maximum(i - plane_blocks, 0), 0))
    stacked = pl.BlockSpec((block_rows, hidden_shard), lambda i: (i, 0))
    steps = plane_blocks * frame_size
    hidden, grad_up = pl.pallas_call(
        functools.partial(feed_back_kernel, plane_blocks=plane_blocks),
        grid=(steps,),
        in_specs=[near, near, far, far, whole, whole],
        out_specs=[stacked, stacked],
        out_shape=[struct((plane * frame_size, hidden_shard), BF16)] * 2,
        cost_estimate=short,
        compiler_params=params,
    )(
        ffn_plane,
        low_plane,
        after(ffn_other, *first_moved, *last_pieces),
        low_other,
        up_slice,
        down_weight,
    )

    def outer(near_rows, far_rows, stacked_rows, shape, kind, flip):
        return pl.pallas_call(
            functools.partial(outer_kernel, plane_blocks=plane_blocks, flip=flip),
            grid=(steps,),
            in_specs=[near, far, stacked],
            out_specs=pl.BlockSpec(shape, lambda i: (0, 0)),
            out_shape=struct(shape, kind),
            scratch_shapes=[pltpu.VMEM(shape, F32)],
            cost_estimate=short,
            compiler_params=params,
        )(near_rows, far_rows, stacked_rows)

    up_part = outer(
        ffn_plane, ffn_other, after(grad_up, *last_sums), (width, hidden_shard), BF16, False
    )
    up_grad = lax.all_to_all(up_part, "items", 0, 1, tiled=True).astype(F32)

    first_placed = spread_on(total_of(first_moved).astype(BF16), "frames")
    last_rows = frame_rows([after(last_sums[0], up_part), *last_sums[1:]])
    last_moved = send_rows_on(last_rows)
    down_grad = outer(
        low_plane,
        low_other,
        after(hidden, *last_rows, *first_placed, *out_placed),
        (hidden_shard, width),
        F32,
        True,
    )
    last_placed = spread_on(total_of(last_moved).astype(BF16), "frames")
    placed = first_placed + last_placed + out_placed
    key_grad, value_grad, out_grad = pl.pallas_call(
        functools.partial(
            place_kernel, chunks=CHUNKS, frames=frame_size, items=items, groups=groups
        ),
        in_specs=[smem] + [whole] * len(placed),
        out_specs=[whole] * 3,
        out_shape=[struct((frame_size, shard // frame_size, width), F32)] * 3,
        cost_estimate=short,
        compiler_params=params,
    )(flags, *placed)

    payload_part = after(payload_part, up_part)
    payload_others = spread_on(payload_part.astype(BF16), "frames")[1:]
    sums = lax.all_gather(
        total_of([payload_part] + payload_others), "items", axis=0, tiled=True
    )
    latents_grad = sums[:lats]
    query_grad = transposed_left(lat_cols, sums[lats : 2 * lats].astype(BF16))
    at = 2 * lats
    column_sums = lax.dynamic_slice_in_dim(
        sums[at + 8 : at + 24], item_index * shard, shard, 1
    )

    result = mid_rows + total_of([result_pieces[d] for d in range(item_size)])
    return (
        result.reshape(items, row_total, width),
        entropy,
        media_grad.reshape(media.shape),
        latents_grad,
        column_sums[:frame_total],
        column_sums[8],
        column_sums[9],
        sums[at + 2],
        sums[at + 3],
        sums[at],
        sums[at + 1],
        query_grad,
        key_grad.reshape(shard, width),
        value_grad.reshape(shard, width),
        out_grad.reshape(shard, width),
        up_grad,
        down_grad,
    )


def solution(mesh):
    return jax.shard_map(
        body,
        mesh=mesh,
        in_specs=(
            P("items", "frames", None, None),
            P("items", "frames", None),
            P(),
            P(),
            P(),
            P(),
            P(),
            P(),
            P(),
            P(),
            P(),
            P(),
            P("items", None),
            P("items", None),
            P("items", None),
            P("items", None),
            P("items", None),
            P("items", None),
        ),
        out_specs=(
            P("items", "frames", None),
            P("items", "frames"),
            P("items", "frames", None, None),
            P(),
            P(None, "items"),
            P("items"),
            P("items"),
            P(),
            P(),
            P(),
            P(),
            P("items", None),
            P("items", None),
            P("items", None),
            P("items", None),
            P("items", None),
            P("items", None),
        ),
        check_vma=False,
    )
```

```python
import functools
import math

import jax
import jax.numpy as jnp
from jax import lax
from jax.experimental import pallas as pl
from jax.experimental.pallas import tpu as pltpu
from jax.sharding import PartitionSpec as P

HEADS = 16
GROUP = 4
CHUNKS = 2
LANES = 128
EPSILON = 1e-05
MASKED = -1e30
F32 = jnp.float32
BF16 = jnp.bfloat16
HIGHEST = lax.Precision.HIGHEST


def layer_norm(inputs, norm_gain, norm_bias):
    center = inputs - jnp.mean(inputs, axis=-1, keepdims=True)
    spread = jnp.mean(center * center, axis=-1, keepdims=True)
    return center * lax.rsqrt(spread + EPSILON) * norm_gain + norm_bias


def matmul(left_side, right_side):
    return jnp.dot(left_side, right_side, preferred_element_type=F32)


def transposed_left(left_side, right_side):
    return lax.dot_general(
        left_side, right_side, (((0,), (0,)), ((), ())), preferred_element_type=F32
    )


def transposed_right(left_side, right_side):
    return lax.dot_general(
        left_side, right_side, (((1,), (1,)), ((), ())), preferred_element_type=F32
    )


def send_on(x, axis, step):
    size = lax.axis_size(axis)
    return lax.ppermute(x, axis, [(i, (i + step) % size) for i in range(size)])


def send_across(x, axis, distance):
    return lax.ppermute(x, axis, [(i, i ^ distance) for i in range(lax.axis_size(axis))])


def spread_on(x, axis):
    return [x] + [send_on(x, axis, s) for s in range(1, lax.axis_size(axis))]


def spread_across(x, axis):
    chips = [x] + [send_across(x, axis, d) for d in range(2, lax.axis_size(axis), 2)]
    return [b for block in chips for b in (block, send_across(block, axis, 1))]


def collect_across(pieces, axis):
    return [pieces[0]] + [send_across(p, axis, d) for d, p in enumerate(pieces) if d]


def total_of(pieces):
    return functools.reduce(jnp.add, [p.astype(F32) for p in pieces])


class Rows:
    def __init__(self, array):
        self.array = array
        self.rows, self.columns = array.shape

    def tiles(self, tile):
        return pl.BlockSpec((self.rows, tile), lambda i: (0, i))

    def whole(self):
        return pl.BlockSpec(memory_space=pltpu.VMEM)


def after(x, *earlier):
    return lax.optimization_barrier((x,) + earlier)[0]


def split_terms(x):
    high = x.astype(BF16)
    rest = x - high.astype(F32)
    middle = rest.astype(BF16)
    return high, middle, (rest - middle.astype(F32)).astype(BF16)


def iota(shape, dim):
    return lax.broadcasted_iota(jnp.int32, shape, dim)


def head_masks(rows, width, head_size):
    lane = iota((rows, width), 1)
    return [
        jnp.logical_and(lane >= h * head_size, lane < (h + 1) * head_size)
        for h in range(width // head_size)
    ]


def spread_heads(block, masks):
    return jnp.concatenate([jnp.where(m, block, jnp.zeros_like(block)) for m in masks], 0)


def collect_heads(block, masks):
    rows = block.shape[0] // len(masks)
    total = jnp.where(masks[0], block[:rows], 0.0)
    for h in range(1, len(masks)):
        total = total + jnp.where(masks[h], block[h * rows : (h + 1) * rows], 0.0)
    return total


def head_expand(width, head_size):
    row, column = iota((LANES, width), 0), iota((LANES, width), 1)
    return jnp.logical_and(column >= row * head_size, column < (row + 1) * head_size).astype(F32)


def live_rows(flag_ref, item, items, patches, lats, columns):
    row = iota((patches + lats, columns), 0)
    media = jnp.logical_and(row < patches, flag_ref[item] > 0)
    return jnp.logical_or(media, jnp.logical_and(row >= patches, flag_ref[items] > 0))


def pack_shape(own, shard, width):
    unit = math.gcd(own, shard)
    return unit, width * unit // shard


def join_kernel(key_ref, value_ref, cotangent_ref, out_ref, low_ref, *, width):
    for g in range(key_ref.shape[1] // width):
        columns = slice(g * width, (g + 1) * width)
        out_ref[:, 2 * g * width : (2 * g + 1) * width] = key_ref[:, columns]
        out_ref[:, (2 * g + 1) * width : (2 * g + 2) * width] = value_ref[:, columns]
    low = cotangent_ref[...].astype(BF16)
    low_ref[...] = low
    own, span = low.shape
    unit, piece = pack_shape(own, out_ref.shape[0], span)
    for a in range(own // unit):
        for b in range(span // piece):
            at = 2 * span + a * piece
            out_ref[b * unit : (b + 1) * unit, at : at + piece] = low[
                a * unit : (a + 1) * unit, b * piece : (b + 1) * piece
            ]


def norm_kernel(media_ref, time_ref, gain_ref, bias_ref, lat_ref, out_ref, *, steps, per_item):
    step = pl.program_id(0)

    @pl.when(step < steps)
    def _():
        rows = media_ref[...].astype(F32) + time_ref[pl.ds(step // per_item, 1), :]
        out_ref[...] = layer_norm(rows, gain_ref[...], bias_ref[...]).astype(BF16)

    @pl.when(step == steps)
    def _():
        out_ref[...] = lat_ref[...]


def forward_kernel(
    flag_ref, both_ref, query_ref, top_ref, *refs, items, patches, scale, head_size, heads,
):
    message_refs, (part_ref, mark_ref) = refs[:-2], refs[-2:]
    lats, width = query_ref.shape
    frames = len(message_refs)
    own = message_refs[0].shape[0]
    row_total = own // items
    masks = head_masks(lats, width, head_size)
    queries = spread_heads(query_ref[...].astype(F32), masks).astype(BF16)
    base = items * patches
    lat_both = both_ref[base : base + lats, :]
    group = pl.program_id(0)
    term, lane = iota((16, GROUP * LANES), 0), iota((16, GROUP * LANES), 1)
    place = jnp.logical_and(
        lane % LANES == term * heads + group * GROUP + lane // LANES, term < 9
    ).astype(BF16)
    for i in range(items):
        both = jnp.concatenate([both_ref[i * patches : (i + 1) * patches, :], lat_both], 0)
        live = live_rows(flag_ref, i, items, patches, lats, queries.shape[0])
        scores = scale * transposed_right(both[:, :width], queries)
        masked = jnp.where(live, scores, MASKED)
        top = jnp.max(masked, axis=0, keepdims=True)
        block_exp = jnp.where(live, jnp.exp(masked - top), 0.0)
        total = jnp.sum(block_exp, axis=0, keepdims=True)
        moment = jnp.sum(block_exp * scores, axis=0, keepdims=True)
        part = transposed_left(block_exp.astype(BF16), both[:, width:])
        part_ref[i] = collect_heads(part, masks)
        top_ref[0, i] = jnp.broadcast_to(top, top_ref.shape[2:])
        terms = jnp.concatenate(
            [t.astype(F32) for x in (top, total, moment) for t in split_terms(x)]
            + [jnp.zeros((7, top.shape[1]), F32)],
            0,
        ).astype(BF16)
        wide = transposed_left(terms, place)
        mark = wide[:lats, :LANES]
        for h in range(1, GROUP):
            mark = mark + wide[h * lats : (h + 1) * lats, h * LANES : (h + 1) * LANES]
        mark_ref[i] = mark

    end = message_refs[0].shape[1] - LANES
    for s, message_ref in enumerate(message_refs):
        start = pl.multiple_of(lax.rem(flag_ref[items + 1] + s, frames) * row_total, row_total)
        rows = pl.ds(start, row_total)
        block = jnp.concatenate([part_ref[i, rows, :] for i in range(items)], 0).astype(BF16)
        mark = jnp.concatenate([mark_ref[i, rows, :] for i in range(items)], 0).astype(BF16)
        for g in range(end // width):

            @pl.when(group == g)
            def _():
                message_ref[:, g * width : (g + 1) * width] = block
                if g == 0:
                    message_ref[:, end:] = mark
                else:
                    message_ref[:, end:] = message_ref[:, end:] + mark


def merge_kernel(*refs, chunks, frames, items, head_size, heads):
    message_refs = refs[: chunks * frames]
    base_ref, weight_ref, gain_ref, bias_ref = refs[chunks * frames : chunks * frames + 4]
    merged_ref, mid_ref, ffn_ref, log_ref, entropy_ref = refs[chunks * frames + 4 :]
    own, columns = message_refs[0].shape
    half = columns - LANES
    lane, column = iota((LANES, 3 * LANES), 0), iota((LANES, 3 * LANES), 1)
    gather = jnp.logical_and(
        jnp.logical_and(lane // heads // 3 == column // LANES, lane % heads == column % LANES),
        lane < 9 * heads,
    ).astype(BF16)
    expand = head_expand(half, head_size)
    live = iota((own, LANES), 1) < heads
    spread = jnp.zeros((own, LANES), F32)
    for c in range(chunks):
        sources = message_refs[c * frames : (c + 1) * frames]
        stats = [matmul(x[:, half:], gather) for x in sources]
        tops = [x[:, :LANES] for x in stats]
        peak = functools.reduce(jnp.maximum, tops)
        factors = [jnp.exp(t - peak) for t in tops]
        whole = sum(f * x[:, LANES : 2 * LANES] for f, x in zip(factors, stats))
        moment = sum(f * x[:, 2 * LANES :] for f, x in zip(factors, stats))
        whole = jnp.where(live, whole, 1.0)
        log_total = jnp.where(live, peak + jnp.log(whole), 0.0)
        log_ref[c] = log_total
        spread = spread + jnp.where(live, log_total - moment / whole, 0.0)
        merged = jnp.zeros((own, half), F32)
        for x, factor in zip(sources, factors):
            share = jnp.where(live, factor / whole, 0.0)
            wide = jnp.dot(share, expand, precision=HIGHEST, preferred_element_type=F32)
            merged = merged + x[:, :half].astype(F32) * wide
        merged_ref[:, c * half : (c + 1) * half] = merged
    entropy_ref[...] = jnp.broadcast_to(
        jnp.sum(spread, axis=1, keepdims=True) * (1.0 / HEADS), entropy_ref.shape
    )
    base = jnp.concatenate([base_ref[...]] * items, 0)
    mid = base + matmul(merged_ref[...].astype(BF16), weight_ref[...])
    mid_ref[...] = mid
    ffn_ref[...] = layer_norm(mid, gain_ref[...], bias_ref[...]).astype(BF16)


def gelu_parts(x):
    share = 0.5 * (1.0 + lax.erf(x * (0.5**0.5)))
    slope = share + x * jnp.exp(-0.5 * x * x) * ((2.0 * jnp.pi) ** -0.5)
    return x * share, slope


def feed_kernel(flag_ref, *refs, devices, items):
    row_refs = refs[:devices]
    low_ref, up_ref, down_ref, plane_ref, plane_low_ref, result_ref = refs[devices : devices + 6]
    grad_refs = refs[devices + 6 :]
    own, width = row_refs[0].shape
    shard = low_ref.shape[0] // devices
    unit, piece = pack_shape(own, shard, width)
    me = flag_ref[2 * items + 2]
    for d in range(devices):
        plane_ref[d * own : (d + 1) * own, :] = row_refs[d][...]
        source = jnp.bitwise_xor(me, d) * shard
        for a in range(own // unit):
            rows = slice(d * own + a * unit, d * own + (a + 1) * unit)
            for b in range(shard // unit):
                start = pl.multiple_of(source + b * unit, unit)
                plane_low_ref[rows, b * piece : (b + 1) * piece] = low_ref[
                    pl.ds(start, unit), a * piece : (a + 1) * piece
                ]
    upward = matmul(plane_ref[...], up_ref[...])
    hidden, slope = gelu_parts(upward)
    grad_up = (slope * transposed_right(plane_low_ref[...], down_ref[...])).astype(BF16)
    grad = transposed_right(grad_up, up_ref[...]).astype(BF16)
    result = matmul(hidden.astype(BF16), down_ref[...]).astype(BF16)
    for d in range(devices):
        grad_refs[d][...] = grad[d * own : (d + 1) * own, :]
        result_ref[jnp.bitwise_xor(me, d)] = result[d * own : (d + 1) * own, :]


def feed_back_kernel(
    plane_ref, plane_low_ref, other_ref, other_low_ref, up_ref, down_ref, near_hidden_ref,
    near_grad_ref, far_hidden_ref, far_grad_ref, *, plane_blocks,
):
    near = pl.program_id(0) < plane_blocks
    rows = jnp.where(near, plane_ref[...], other_ref[...])
    low = jnp.where(near, plane_low_ref[...], other_low_ref[...])
    hidden, slope = gelu_parts(matmul(rows, up_ref[...]))
    hidden = hidden.astype(BF16)
    grad_up = (slope * transposed_right(low, down_ref[...])).astype(BF16)

    @pl.when(near)
    def _():
        near_hidden_ref[...] = hidden
        near_grad_ref[...] = grad_up

    @pl.when(jnp.logical_not(near))
    def _():
        far_hidden_ref[...] = hidden
        far_grad_ref[...] = grad_up


def outer_kernel(near_ref, far_ref, near_more_ref, far_more_ref, out_ref):
    total = transposed_left(near_ref[...], near_more_ref[...]) + transposed_left(
        far_ref[...], far_more_ref[...]
    )
    out_ref[...] = total.astype(out_ref.dtype)


def norm_backward(rows, gain, gradient):
    center = rows - jnp.mean(rows, axis=1, keepdims=True)
    rate = lax.rsqrt(jnp.mean(center * center, axis=1, keepdims=True) + EPSILON)
    unit = center * rate
    scaled = gradient * gain
    inner = scaled - jnp.mean(scaled, axis=1, keepdims=True)
    back = rate * (inner - unit * jnp.mean(scaled * unit, axis=1, keepdims=True))
    return (
        back,
        jnp.sum(gradient * unit, axis=0, keepdims=True),
        jnp.sum(gradient, axis=0, keepdims=True),
    )


def turn_kernel(*refs, devices, items, chunks, head_size, heads):
    part_refs = refs[:devices]
    mid_ref, cotangent_ref, gain_ref, merged_ref, log_ref, weight_ref = refs[
        devices : devices + 6
    ]
    message_ref, branch_ref, base_ref, sums_ref = refs[devices + 6 :]
    own, width = mid_ref.shape
    half = width // chunks
    gradient = total_of([x[...] for x in part_refs])
    back, gain_sum, bias_sum = norm_backward(mid_ref[...], gain_ref[...], gradient)
    grad_mid = cotangent_ref[...] + back
    sums_ref[...] = jnp.zeros(sums_ref.shape, F32)
    sums_ref[0:1, :] = gain_sum
    sums_ref[1:2, :] = bias_sum
    row_total = own // items
    base_ref[...] = total_of(
        [grad_mid[i * row_total : (i + 1) * row_total] for i in range(items)]
    )
    branch = grad_mid.astype(BF16)
    branch_ref[:, :width] = branch
    branch_ref[:, width:] = merged_ref[...].astype(BF16)
    grad_att = transposed_right(branch, weight_ref[...]).astype(BF16)
    expand = head_expand(half, head_size)
    lane, column = iota((6 * LANES, LANES), 0), iota((6 * LANES, LANES), 1)
    place = jnp.logical_and(
        lane % LANES < heads, column == (lane // LANES) * heads + lane % LANES
    ).astype(BF16)
    message_ref[:, :width] = grad_att
    for c in range(chunks):
        columns = slice(c * half, (c + 1) * half)
        delta = lax.dot_general(
            merged_ref[:, columns] * grad_att[:, columns].astype(F32),
            expand,
            (((1,), (1,)), ((), ())),
            precision=HIGHEST,
            preferred_element_type=F32,
        )
        terms = jnp.concatenate([t for x in (log_ref[c], delta) for t in split_terms(x)], 1)
        message_ref[:, width + c * LANES : width + (c + 1) * LANES] = matmul(
            terms, place
        ).astype(BF16)


def backward_kernel(
    *refs, frames, items, patches, scale, head_size, heads,
):
    flag_ref, both_ref, query_ref, top_ref = refs[:4]
    grad_refs = refs[4 : 4 + frames]
    mark_refs = refs[4 + frames : 4 + 2 * frames]
    out_ref, sum_ref, held_ref, note_ref = refs[4 + 2 * frames :]
    lats, width = query_ref.shape
    own = grad_refs[0].shape[0]
    row_total = own // items
    base = items * patches
    for s in range(frames):
        source = lax.rem(flag_ref[items + 1] + (frames - s), frames)
        rows = pl.ds(pl.multiple_of(source * row_total, row_total), row_total)
        block = grad_refs[s][...].astype(F32)
        mark = mark_refs[s][...].astype(F32)
        for i in range(items):
            held_ref[i, rows, :] = block[i * row_total : (i + 1) * row_total]
            note_ref[i, rows, :] = mark[i * row_total : (i + 1) * row_total]
    masks = head_masks(lats, width, head_size)
    queries = spread_heads(query_ref[...].astype(F32), masks).astype(BF16)
    lat_both = both_ref[base : base + lats, :]
    row, lane = iota((GROUP * 8, LANES), 0), iota((GROUP * 8, LANES), 1)
    pick = jnp.logical_and(
        jnp.logical_and(
            lane // heads // 3 == row % 8,
            lane % heads == pl.program_id(0) * GROUP + row // 8,
        ),
        lane < 6 * heads,
    ).astype(BF16)
    grad_query = jnp.zeros((queries.shape[0], width), F32)
    lat_grad_key = jnp.zeros((lats, width), F32)
    lat_grad_value = jnp.zeros((lats, width), F32)
    for i in range(items):
        rows = slice(i * patches, (i + 1) * patches)
        stats = transposed_right(pick, note_ref[i].astype(BF16))
        stats = jnp.concatenate([stats[h * 8 : (h + 1) * 8] for h in range(GROUP)], 1)
        log_total = stats[0:1]
        delta = stats[1:2]
        top = top_ref[0, i, 0:1, :]
        rescale = jnp.exp(top - log_total)
        both = jnp.concatenate([both_ref[rows, :], lat_both], 0)
        keys, values = both[:, :width], both[:, width:]
        grads = spread_heads(held_ref[i], masks).astype(BF16)
        live = live_rows(flag_ref, i, items, patches, lats, queries.shape[0])
        masked = jnp.where(live, scale * transposed_right(keys, queries), MASKED)
        probs = jnp.where(live, jnp.exp(masked - log_total), 0.0)
        block_exp = jnp.where(live, jnp.exp(masked - top), 0.0)
        weights = (block_exp.astype(BF16).astype(F32) * rescale).astype(BF16)
        grad_scores = (probs * (transposed_right(values, grads) - delta)).astype(BF16)
        grad_key = scale * matmul(grad_scores, queries)
        grad_value = matmul(weights, grads)
        out_ref[rows, :width] = grad_key[:patches].astype(BF16)
        out_ref[rows, width:] = grad_value[:patches].astype(BF16)
        grad_query = grad_query + transposed_left(grad_scores, keys)
        lat_grad_key = lat_grad_key + grad_key[patches:]
        lat_grad_value = lat_grad_value + grad_value[patches:]
    out_ref[base : base + lats, :width] = lat_grad_key.astype(BF16)
    out_ref[base : base + lats, width:] = lat_grad_value.astype(BF16)
    sum_ref[...] = scale * collect_heads(grad_query, masks)


def media_kernel(flag_ref, *refs, chunks, items, frames):
    grad_refs, lat_refs, weight_refs = [
        refs[k * chunks : (k + 1) * chunks] for k in range(3)
    ]
    media_ref, time_ref, gain_ref, out_ref, sums_ref, product_ref = refs[3 * chunks :]
    item = pl.program_id(0)

    @pl.when(item == 0)
    def _():
        sums_ref[...] = jnp.zeros(sums_ref.shape, F32)
        product_ref[...] = functools.reduce(
            jnp.add, [matmul(g[...], w[...]) for g, w in zip(lat_refs, weight_refs)]
        )

    gradient = functools.reduce(
        jnp.add, [matmul(g[...], w[...]) for g, w in zip(grad_refs, weight_refs)]
    )
    inputs = media_ref[...].astype(F32) + time_ref[pl.ds(item, 1), :]
    back, gain_sum, bias_sum = norm_backward(inputs, gain_ref[...], gradient)
    out_ref[...] = back.astype(BF16)
    place = iota((frames, 1), 0) == flag_ref[items + 2 + item]
    sums_ref[0:frames, :] += jnp.where(place, jnp.sum(back, axis=0, keepdims=True), 0.0)
    sums_ref[8:9, :] += gain_sum
    sums_ref[9:10, :] += bias_sum


def latent_kernel(flag_ref, *refs, chunks, items):
    query_refs = refs[:chunks]
    (
        product_ref, query_weight_ref, latent_ref, gain_ref, base_ref, ffn_ref, media_ref, out_ref,
    ) = refs[chunks:]
    lats, width = latent_ref.shape
    half = width // chunks
    gradient = product_ref[...]
    for c in range(chunks):
        gradient = gradient + transposed_right(
            query_refs[c][...].astype(BF16), query_weight_ref[:, c * half : (c + 1) * half]
        )
        out_ref[lats : 2 * lats, c * half : (c + 1) * half] = query_refs[c][...]
    back, gain_sum, bias_sum = norm_backward(latent_ref[...], gain_ref[...], gradient)
    out_ref[:lats, :] = back
    row_total = base_ref.shape[0]
    start = pl.multiple_of(flag_ref[items + 1] * row_total, row_total)
    out_ref[pl.ds(start, row_total), :] += base_ref[...]
    at = 2 * lats
    out_ref[at : at + 8, :] = ffn_ref[...]
    out_ref[at + 2 : at + 3, :] = gain_sum
    out_ref[at + 3 : at + 4, :] = bias_sum
    out_ref[at + 8 : at + 24, :] = media_ref[...]
    out_ref[at + 24 :, :] = jnp.zeros((out_ref.shape[0] - at - 24, width), F32)


def rows_kernel(flag_ref, *refs, count, frames, items):
    total = total_of([x[...] for x in refs[:count]])
    out_refs, held_ref = refs[count:-1], refs[-1]
    rows = total.shape[0] // frames
    for f in range(frames):
        held_ref[f] = total[f * rows : (f + 1) * rows]
    for s, out_ref in enumerate(out_refs):
        block = held_ref[lax.rem(flag_ref[items + 1] + s, frames)]
        out_ref[...] = block.astype(out_ref.dtype)


def place_kernel(flag_ref, *refs, chunks, frames, items, groups):
    chunk_refs = refs[: chunks * frames]
    more_refs = refs[chunks * frames : (chunks + 1) * frames]
    key_ref, value_ref, out_ref = refs[(chunks + 1) * frames :]
    width = key_ref.shape[2] // (chunks * groups)
    for s in range(frames):
        source = lax.rem(flag_ref[items + 1] + (frames - s), frames)
        out_ref[source] = more_refs[s][...].astype(F32)
        for c in range(chunks):
            for g in range(groups):
                at = (c * groups + g) * width
                block = chunk_refs[c * frames + s][:, 2 * g * width : 2 * (g + 1) * width]
                block = block.astype(F32)
                key_ref[source, :, at : at + width] = block[:, :width]
                value_ref[source, :, at : at + width] = block[:, width:]


def body(
    media,
    cotangent,
    frame_count,
    frame_start,
    latents,
    time_embed,
    media_gain,
    media_bias,
    latent_gain,
    latent_bias,
    ffn_gain,
    ffn_bias,
    query_weight,
    key_weight,
    value_weight,
    out_weight,
    up_weight,
    down_weight,
):
    items = media.shape[0]
    patches = media.shape[2]
    width = media.shape[3]
    lats = latents.shape[0]
    frame_total = time_embed.shape[0]
    row_total = cotangent.shape[1]
    own = items * row_total
    head_size = width // HEADS
    half = width // CHUNKS
    chunk_heads = HEADS // CHUNKS
    group_width = GROUP * head_size
    groups = chunk_heads // GROUP
    stack = GROUP * lats
    tokens = items * patches
    all_tokens = tokens + lats
    shard = query_weight.shape[0]
    hidden_shard = down_weight.shape[0]
    item_size = lax.axis_size("items")
    frame_size = lax.axis_size("frames")
    plane = item_size * own
    item_index = lax.axis_index("items")
    slot = lax.axis_index("frames")
    row_base = slot * row_total
    params = pltpu.CompilerParams(vmem_limit_bytes=56 * 2**20)
    smem = pl.BlockSpec(memory_space=pltpu.SMEM)
    whole = pl.BlockSpec(memory_space=pltpu.VMEM)
    sizes = dict(items=items, head_size=head_size, heads=chunk_heads)

    def struct(shape, kind):
        return jax.ShapeDtypeStruct(shape, kind)

    short = pl.CostEstimate(flops=1000, bytes_accessed=1000, transcendentals=0)

    def column_blocks(x):
        return jnp.transpose(x.reshape(-1, item_size, shard), (1, 0, 2))

    def scatter_exchange(x, axis):
        return jnp.sum(lax.all_to_all(x, axis, 0, 0).astype(F32), axis=0)

    grad_out = cotangent.reshape(own, width)
    low_columns = own * width // shard
    joined, grad_low = pl.pallas_call(
        functools.partial(join_kernel, width=group_width),
        out_shape=[struct((shard, 2 * width + low_columns), BF16), struct((own, width), BF16)],
        cost_estimate=short,
        compiler_params=params,
    )(key_weight, value_weight, grad_out)
    kv_full = lax.all_gather(joined, "items", axis=0, tiled=True)

    lat_norm = layer_norm(latents, latent_gain, latent_bias).astype(BF16)
    lat_cols = lax.dynamic_slice_in_dim(lat_norm, item_index * shard, shard, 1)
    query_blocks = column_blocks(matmul(lat_cols, query_weight))
    query_cols = scatter_exchange(query_blocks, "items").astype(BF16)
    query_spread = jnp.broadcast_to(query_cols[None], (item_size, lats, shard))
    queries = jnp.transpose(lax.all_to_all(query_spread, "items", 0, 0), (1, 0, 2)).reshape(
        lats, width
    )

    counts = lax.dynamic_slice_in_dim(frame_count, item_index * items, items)
    starts = lax.dynamic_slice_in_dim(frame_start, item_index * items, items)
    offset = (slot - starts) % frame_total
    flags = jnp.concatenate(
        [
            (offset < counts).astype(jnp.int32),
            (slot == 0).astype(jnp.int32)[None],
            slot.astype(jnp.int32)[None],
            offset.astype(jnp.int32),
            item_index.astype(jnp.int32)[None],
        ]
    )
    picker = (offset[:, None] == jnp.arange(frame_total, dtype=jnp.int32)[None, :]).astype(F32)
    time_rows = jnp.dot(picker, time_embed, precision=HIGHEST, preferred_element_type=F32)
    flat_media = media.reshape(tokens, width)
    steps = tokens // lats
    all_rows = pl.pallas_call(
        functools.partial(norm_kernel, steps=steps, per_item=patches // lats),
        grid=(steps + 1,),
        in_specs=[
            pl.BlockSpec((lats, width), lambda i: (jnp.minimum(i, steps - 1), 0)),
            whole,
            whole,
            whole,
            whole,
        ],
        out_specs=pl.BlockSpec((lats, width), lambda i: (i, 0)),
        out_shape=struct((all_tokens, width), BF16),
        cost_estimate=short,
        compiler_params=params,
    )(
        after(flat_media, query_blocks),
        time_rows,
        media_gain[None],
        media_bias[None],
        lat_norm,
    )
    out_full = lax.all_gather(after(out_weight, all_rows), "items", axis=0, tiled=True)

    chip, core = item_index // 2, item_index % 2
    rows_across = after(all_rows, query_cols).T.reshape(item_size // 2, 2, shard, all_tokens)
    send_rows, keep_rows = [
        jnp.concatenate(
            [
                lax.dynamic_slice(
                    rows_across, (chip ^ k, which, 0, 0), (1, 1, shard, all_tokens)
                ).reshape(shard, all_tokens)
                for k in range(item_size // 2)
            ],
            0,
        )
        for which in (1 - core, core)
    ]
    low_shift = spread_on(after(grad_low, all_rows), "frames")[1:]

    boths, tops, messages = [], [], []
    for c in range(CHUNKS):

        def block_of(g, c=c):
            return (0, c * groups + g)

        if c:
            rows = after(all_rows, tops[-1])
        else:
            rows = after(all_rows, queries, send_rows, keep_rows, *low_shift)
        both = matmul(rows, kv_full[:, 2 * c * half : 2 * (c + 1) * half]).astype(BF16)
        top, *parts = pl.pallas_call(
            functools.partial(
                forward_kernel, patches=patches, scale=head_size**-0.5, **sizes
            ),
            grid=(groups,),
            in_specs=[
                smem,
                pl.BlockSpec((all_tokens, 2 * group_width), lambda g: (0, g)),
                pl.BlockSpec((lats, group_width), block_of),
            ],
            out_specs=[pl.BlockSpec((1, items, 8, stack), lambda g: (g, 0, 0, 0))]
            + [pl.BlockSpec((own, half + LANES), lambda g: (0, 0))] * frame_size,
            out_shape=[struct((groups, items, 8, stack), F32)]
            + [struct((own, half + LANES), BF16)] * frame_size,
            scratch_shapes=[
                pltpu.VMEM((items, lats, group_width), F32),
                pltpu.VMEM((items, lats, LANES), F32),
            ],
            cost_estimate=short,
            compiler_params=params,
        )(flags, both, queries)
        boths.append(both)
        tops.append(top)
        messages += [p if s == 0 else send_on(p, "frames", s) for s, p in enumerate(parts)]
    up_slice = lax.all_to_all(after(up_weight, boths[0]), "items", 1, 0, tiled=True)
    low_other = lax.all_gather(
        after(jnp.stack(low_shift), tops[1]), "items", axis=0
    ).reshape(-1, width)

    base_rows = lax.dynamic_slice_in_dim(latents, row_base, row_total, 0)
    merged, mid_rows, ffn_in, logs, entropy_wide = pl.pallas_call(
        functools.partial(merge_kernel, chunks=CHUNKS, frames=frame_size, **sizes),
        out_shape=[
            struct((own, width), F32),
            struct((own, width), F32),
            struct((own, width), BF16),
            struct((CHUNKS, own, LANES), F32),
            struct((own, LANES), F32),
        ],
        cost_estimate=short,
        compiler_params=params,
    )(after(messages[0], up_slice), *messages[1:], base_rows, out_full, ffn_gain[None], ffn_bias[None])
    entropy = entropy_wide[:, 0].reshape(items, row_total)

    query_full = lax.all_gather(after(query_weight, ffn_in), "items", axis=0, tiled=True)
    ffn_blocks = spread_across(ffn_in, "items")
    ffn_plane, low_plane, result_part, *parts = pl.pallas_call(
        functools.partial(feed_kernel, devices=item_size, items=items),
        grid=(1,),
        in_specs=[smem]
        + [whole] * item_size
        + [
            pl.BlockSpec((width, low_columns), lambda i: (0, 2 * width // low_columns)),
            whole,
            whole,
        ],
        out_specs=[whole] * (3 + item_size),
        out_shape=[struct((plane, width), BF16)] * 2
        + [struct((item_size, own, width), BF16)]
        + [struct((own, width), BF16)] * item_size,
        cost_estimate=short,
        compiler_params=params,
    )(flags, *ffn_blocks, kv_full, up_slice, down_weight)
    grad_blocks = collect_across(parts, "items")
    ffn_shift = spread_on(after(ffn_in, *ffn_blocks), "frames")[1:]
    kv_back = after(kv_full, ffn_plane)[:, : 2 * width].T
    ffn_other = lax.all_gather(jnp.stack(ffn_shift), "items", axis=0).reshape(-1, width)
    grad_blocks[0] = after(grad_blocks[0], *ffn_shift)
    grad_out = after(grad_out, kv_back)

    turn, grad_branch, grad_base, ffn_sums = pl.pallas_call(
        functools.partial(turn_kernel, devices=item_size, chunks=CHUNKS, **sizes),
        out_shape=[
            struct((own, width + CHUNKS * LANES), BF16),
            struct((own, 2 * width), BF16),
            struct((row_total, width), F32),
            struct((8, width), F32),
        ],
        cost_estimate=short,
        compiler_params=params,
    )(*grad_blocks, mid_rows, grad_out, ffn_gain[None], merged, logs, out_full)
    turns = spread_on(turn, "frames")
    branch_plane = lax.all_gather(grad_branch, "items", axis=0, tiled=True)
    att_plane = lax.dynamic_slice_in_dim(
        branch_plane, width + item_index * shard, shard, 1
    )
    result_pieces = lax.all_to_all(after(result_part, turns[-1]), "items", 0, 0)
    turns[0] = after(turns[0], low_other, query_full)

    chunk_grads, chunk_queries = [], []

    def weight_terms(c):
        send = matmul(send_rows, chunk_grads[c]).astype(BF16)
        received = send_across(send, "items", 1).reshape(-1, shard, 2 * half)
        keep = matmul(after(keep_rows, send), chunk_grads[c]).astype(BF16)
        return send, keep.reshape(-1, shard, 2 * half), received

    def chip_pieces(keep, received):
        sums = [keep[k].astype(F32) + received[k].astype(F32) for k in range(item_size // 2)]
        return sums[:1] + [p.astype(BF16) for p in sums[1:]]

    def send_pieces(sums):
        return sums[:1] + [
            send_across(p, "items", 2 * k) for k, p in enumerate(sums) if k
        ]

    def frame_rows(parts):
        rows, columns = parts[0].shape
        rows //= frame_size
        return pl.pallas_call(
            functools.partial(
                rows_kernel, count=len(parts), frames=frame_size, items=items
            ),
            in_specs=[smem] + [whole] * len(parts),
            out_specs=[whole] * frame_size,
            out_shape=[struct((rows, columns), F32)]
            + [struct((rows, columns), BF16)] * (frame_size - 1),
            scratch_shapes=[pltpu.VMEM((frame_size, rows, columns), F32)],
            cost_estimate=short,
            compiler_params=params,
        )(flags, *parts)

    def send_rows_on(rows):
        return [rows[0]] + [send_on(p, "frames", s) for s, p in enumerate(rows) if s]

    for c in range(CHUNKS):

        def block_of(g, c=c):
            return (0, c * groups + g)

        chunk_grad, chunk_query = pl.pallas_call(
            functools.partial(
                backward_kernel, frames=frame_size, patches=patches, scale=head_size**-0.5, **sizes
            ),
            grid=(groups,),
            in_specs=[
                smem,
                pl.BlockSpec((all_tokens, 2 * group_width), lambda g: (0, g)),
                pl.BlockSpec((lats, group_width), block_of),
                pl.BlockSpec((1, items, 8, stack), lambda g: (g, 0, 0, 0)),
            ]
            + [pl.BlockSpec((own, group_width), block_of)] * frame_size
            + [pl.BlockSpec((own, LANES), lambda g, c=c: (0, width // LANES + c))] * frame_size,
            out_specs=[
                pl.BlockSpec((all_tokens, 2 * group_width), lambda g: (0, g)),
                pl.BlockSpec((lats, group_width), lambda g: (0, g)),
            ],
            out_shape=[
                struct((all_tokens, 2 * half), BF16),
                struct((lats, half), F32),
            ],
            scratch_shapes=[
                pltpu.VMEM((items, lats, group_width), F32),
                pltpu.VMEM((items, lats, LANES), F32),
            ],
            cost_estimate=short,
            compiler_params=params,
        )(flags, after(boths[c], *held) if c else boths[c], queries, tops[c], *turns, *turns)
        chunk_grads.append(chunk_grad)
        chunk_queries.append(chunk_query)
        if c == 0:
            first_send, first_keep, first_received = weight_terms(0)
            held = (first_send,)
    first_pieces = chip_pieces(after(first_keep, chunk_grads[-1]), first_received)
    first_sums = send_pieces(first_pieces)
    out_part = transposed_left(att_plane, after(branch_plane, chunk_grads[-1])[:, :width])
    out_rows = frame_rows([out_part])
    out_moved = send_rows_on(out_rows)

    last_block = pl.BlockSpec((lats, 2 * half), lambda i: (tokens // lats, 0))
    media_grad, media_sums, lat_product = pl.pallas_call(
        functools.partial(media_kernel, chunks=CHUNKS, items=items, frames=frame_total),
        grid=(items,),
        in_specs=[smem]
        + [pl.BlockSpec((patches, 2 * half), lambda i: (i, 0))] * CHUNKS
        + [last_block] * CHUNKS
        + [pl.BlockSpec((2 * half, width), lambda i, c=c: (c, 0)) for c in range(CHUNKS)]
        + [pl.BlockSpec((patches, width), lambda i: (i, 0)), whole, whole],
        out_specs=[
            pl.BlockSpec((patches, width), lambda i: (i, 0)),
            pl.BlockSpec((16, width), lambda i: (0, 0)),
            pl.BlockSpec((lats, width), lambda i: (0, 0)),
        ],
        out_shape=[
            struct((tokens, width), BF16),
            struct((16, width), F32),
            struct((lats, width), F32),
        ],
        cost_estimate=short,
        compiler_params=params,
    )(
        flags,
        *chunk_grads[:-1],
        after(chunk_grads[-1], *first_pieces, *out_rows, ffn_other),
        *chunk_grads,
        *[kv_back] * CHUNKS,
        flat_media,
        time_rows,
        media_gain[None],
    )

    sum_rows = 2 * lats + 24
    sum_rows += -sum_rows % (8 * item_size)
    payload = pl.pallas_call(
        functools.partial(latent_kernel, chunks=CHUNKS, items=items),
        in_specs=[smem] + [whole] * (CHUNKS + 7),
        out_specs=whole,
        out_shape=struct((sum_rows, width), F32),
        cost_estimate=short,
        compiler_params=params,
    )(
        flags,
        *chunk_queries,
        after(lat_product, *first_sums, *out_moved, result_pieces),
        query_full,
        latents,
        latent_gain[None],
        grad_base,
        ffn_sums,
        media_sums,
    )
    payload_part = lax.psum_scatter(payload, "items", scatter_dimension=0, tiled=True)

    first_rows = frame_rows([after(first_sums[0], payload), *first_sums[1:]])
    first_moved = send_rows_on(first_rows)
    out_total = total_of(out_moved).astype(BF16)
    chunk_grads[-1] = after(chunk_grads[-1], payload, out_total, *first_rows)
    last_send, last_keep, last_received = weight_terms(CHUNKS - 1)
    out_placed = spread_on(out_total, "frames")
    last_pieces = chip_pieces(after(last_keep, *first_moved), last_received)
    first_total = total_of(first_moved).astype(BF16)
    first_placed = spread_on(first_total, "frames")
    last_sums = send_pieces(last_pieces)

    block_rows = min(512, plane)
    plane_blocks = plane // block_rows
    near = pl.BlockSpec((block_rows, width), lambda i: (jnp.minimum(i, plane_blocks - 1), 0))
    far = pl.BlockSpec((block_rows, width), lambda i: (jnp.maximum(i - plane_blocks, 0), 0))
    near_hidden = pl.BlockSpec(
        (block_rows, hidden_shard), lambda i: (jnp.minimum(i, plane_blocks - 1), 0)
    )
    far_hidden = pl.BlockSpec(
        (block_rows, hidden_shard), lambda i: (jnp.maximum(i - plane_blocks, 0), 0)
    )
    hidden_near, grad_near, hidden_far, grad_far = pl.pallas_call(
        functools.partial(feed_back_kernel, plane_blocks=plane_blocks),
        grid=(plane_blocks * frame_size,),
        in_specs=[near, near, far, far, whole, whole],
        out_specs=[near_hidden, near_hidden, far_hidden, far_hidden],
        out_shape=[struct((plane, hidden_shard), BF16)] * 2
        + [struct((plane * (frame_size - 1), hidden_shard), BF16)] * 2,
        cost_estimate=short,
        compiler_params=params,
    )(
        ffn_plane,
        low_plane,
        after(ffn_other, *out_placed, *last_pieces),
        low_other,
        up_slice,
        down_weight,
    )

    def outer(left_near, left_far, right_near, right_far, tile, kind):
        rows = left_near.columns, right_near.columns
        return pl.pallas_call(
            outer_kernel,
            grid=(rows[0] // tile,),
            in_specs=[
                left_near.tiles(tile),
                left_far.tiles(tile),
                right_near.whole(),
                right_far.whole(),
            ],
            out_specs=pl.BlockSpec((tile, rows[1]), lambda i: (i, 0)),
            out_shape=struct(rows, kind),
            cost_estimate=short,
            compiler_params=params,
        )(left_near.array, left_far.array, right_near.array, right_far.array)

    up_part = outer(
        Rows(ffn_plane),
        Rows(ffn_other),
        Rows(after(grad_near, *last_sums, *first_placed)),
        Rows(grad_far),
        width // 4,
        BF16,
    )
    up_grad = lax.all_to_all(up_part, "items", 0, 1, tiled=True).astype(F32)

    last_rows = frame_rows([after(last_sums[0], up_part), *last_sums[1:]])
    last_moved = send_rows_on(last_rows)
    down_grad = outer(
        Rows(after(hidden_near, *last_rows)),
        Rows(hidden_far),
        Rows(low_plane),
        Rows(low_other),
        256 if hidden_shard % 256 == 0 else hidden_shard,
        F32,
    )
    last_placed = spread_on(total_of(last_moved).astype(BF16), "frames")
    placed = first_placed + last_placed + out_placed
    key_grad, value_grad, out_grad = pl.pallas_call(
        functools.partial(
            place_kernel, chunks=CHUNKS, frames=frame_size, items=items, groups=groups
        ),
        in_specs=[smem] + [whole] * len(placed),
        out_specs=[whole] * 3,
        out_shape=[struct((frame_size, shard // frame_size, width), F32)] * 3,
        cost_estimate=short,
        compiler_params=params,
    )(flags, *placed)

    payload_part = after(payload_part, up_part)
    payload_others = spread_on(payload_part.astype(BF16), "frames")[1:]
    sums = lax.all_gather(
        total_of([payload_part] + payload_others), "items", axis=0, tiled=True
    )
    latents_grad = sums[:lats]
    query_grad = transposed_left(lat_cols, sums[lats : 2 * lats].astype(BF16))
    at = 2 * lats
    column_sums = lax.dynamic_slice_in_dim(
        sums[at + 8 : at + 24], item_index * shard, shard, 1
    )

    result = mid_rows + total_of([result_pieces[d] for d in range(item_size)])
    return (
        result.reshape(items, row_total, width),
        entropy,
        media_grad.reshape(media.shape),
        latents_grad,
        column_sums[:frame_total],
        column_sums[8],
        column_sums[9],
        sums[at + 2],
        sums[at + 3],
        sums[at],
        sums[at + 1],
        query_grad,
        key_grad.reshape(shard, width),
        value_grad.reshape(shard, width),
        out_grad.reshape(shard, width),
        up_grad,
        down_grad,
    )


def solution(mesh):
    return jax.shard_map(
        body,
        mesh=mesh,
        in_specs=(
            P("items", "frames", None, None),
            P("items", "frames", None),
            P(),
            P(),
            P(),
            P(),
            P(),
            P(),
            P(),
            P(),
            P(),
            P(),
            P("items", None),
            P("items", None),
            P("items", None),
            P("items", None),
            P("items", None),
            P("items", None),
        ),
        out_specs=(
            P("items", "frames", None),
            P("items", "frames"),
            P("items", "frames", None, None),
            P(),
            P(None, "items"),
            P("items"),
            P("items"),
            P(),
            P(),
            P(),
            P(),
            P("items", None),
            P("items", None),
            P("items", None),
            P("items", None),
            P("items", None),
            P("items", None),
        ),
        check_vma=False,
    )
```

```python
import functools
import math

import jax
import jax.numpy as jnp
from jax import lax
from jax.experimental import pallas as pl
from jax.experimental.pallas import tpu as pltpu
from jax.sharding import PartitionSpec as P

HEADS = 16
GROUP = 4
CHUNKS = 2
LANES = 128
EPSILON = 1e-05
MASKED = -1e30
F32 = jnp.float32
BF16 = jnp.bfloat16
HIGHEST = lax.Precision.HIGHEST


def layer_norm(inputs, norm_gain, norm_bias):
    center = inputs - jnp.mean(inputs, axis=-1, keepdims=True)
    spread = jnp.mean(center * center, axis=-1, keepdims=True)
    return center * lax.rsqrt(spread + EPSILON) * norm_gain + norm_bias


def matmul(left_side, right_side):
    return jnp.dot(left_side, right_side, preferred_element_type=F32)


def transposed_left(left_side, right_side):
    return lax.dot_general(
        left_side, right_side, (((0,), (0,)), ((), ())), preferred_element_type=F32
    )


def transposed_right(left_side, right_side):
    return lax.dot_general(
        left_side, right_side, (((1,), (1,)), ((), ())), preferred_element_type=F32
    )


def send_on(x, axis, step):
    size = lax.axis_size(axis)
    return lax.ppermute(x, axis, [(i, (i + step) % size) for i in range(size)])


def send_across(x, axis, distance):
    return lax.ppermute(x, axis, [(i, i ^ distance) for i in range(lax.axis_size(axis))])


def spread_on(x, axis):
    return [x] + [send_on(x, axis, s) for s in range(1, lax.axis_size(axis))]


def spread_across(x, axis):
    chips = [x] + [send_across(x, axis, d) for d in range(2, lax.axis_size(axis), 2)]
    return [b for block in chips for b in (block, send_across(block, axis, 1))]


def collect_across(pieces, axis):
    return [pieces[0]] + [send_across(p, axis, d) for d, p in enumerate(pieces) if d]


def total_of(pieces):
    return functools.reduce(jnp.add, [p.astype(F32) for p in pieces])


class Rows:
    def __init__(self, array):
        self.array = array
        self.rows, self.columns = array.shape

    def tiles(self, tile):
        return pl.BlockSpec((self.rows, tile), lambda i: (0, i))

    def whole(self):
        return pl.BlockSpec(memory_space=pltpu.VMEM)


def after(x, *earlier):
    return lax.optimization_barrier((x,) + earlier)[0]


def split_terms(x):
    high = x.astype(BF16)
    rest = x - high.astype(F32)
    middle = rest.astype(BF16)
    return high, middle, (rest - middle.astype(F32)).astype(BF16)


def iota(shape, dim):
    return lax.broadcasted_iota(jnp.int32, shape, dim)


def head_masks(rows, width, head_size):
    lane = iota((rows, width), 1)
    return [
        jnp.logical_and(lane >= h * head_size, lane < (h + 1) * head_size)
        for h in range(width // head_size)
    ]


def spread_heads(block, masks):
    return jnp.concatenate([jnp.where(m, block, jnp.zeros_like(block)) for m in masks], 0)


def collect_heads(block, masks):
    rows = block.shape[0] // len(masks)
    total = jnp.where(masks[0], block[:rows], 0.0)
    for h in range(1, len(masks)):
        total = total + jnp.where(masks[h], block[h * rows : (h + 1) * rows], 0.0)
    return total


def head_expand(width, head_size):
    row, column = iota((LANES, width), 0), iota((LANES, width), 1)
    return jnp.logical_and(column >= row * head_size, column < (row + 1) * head_size).astype(F32)


def live_rows(flag_ref, item, items, patches, lats, columns):
    row = iota((patches + lats, columns), 0)
    media = jnp.logical_and(row < patches, flag_ref[item] > 0)
    return jnp.logical_or(media, jnp.logical_and(row >= patches, flag_ref[items] > 0))


def pack_shape(own, shard, width):
    unit = math.gcd(own, shard)
    return unit, width * unit // shard


def join_kernel(key_ref, value_ref, cotangent_ref, out_ref, low_ref, *, width):
    for g in range(key_ref.shape[1] // width):
        columns = slice(g * width, (g + 1) * width)
        out_ref[:, 2 * g * width : (2 * g + 1) * width] = key_ref[:, columns]
        out_ref[:, (2 * g + 1) * width : (2 * g + 2) * width] = value_ref[:, columns]
    low = cotangent_ref[...].astype(BF16)
    low_ref[...] = low
    own, span = low.shape
    unit, piece = pack_shape(own, out_ref.shape[0], span)
    for a in range(own // unit):
        for b in range(span // piece):
            at = 2 * span + a * piece
            out_ref[b * unit : (b + 1) * unit, at : at + piece] = low[
                a * unit : (a + 1) * unit, b * piece : (b + 1) * piece
            ]


def norm_kernel(media_ref, time_ref, gain_ref, bias_ref, lat_ref, out_ref, *, steps, per_item):
    step = pl.program_id(0)

    @pl.when(step < steps)
    def _():
        rows = media_ref[...].astype(F32) + time_ref[pl.ds(step // per_item, 1), :]
        out_ref[...] = layer_norm(rows, gain_ref[...], bias_ref[...]).astype(BF16)

    @pl.when(step == steps)
    def _():
        out_ref[...] = lat_ref[...]


def forward_kernel(
    flag_ref, both_ref, query_ref, top_ref, *refs, items, patches, scale, head_size, heads,
):
    message_refs, (part_ref, mark_ref) = refs[:-2], refs[-2:]
    lats, width = query_ref.shape
    frames = len(message_refs)
    own = message_refs[0].shape[0]
    row_total = own // items
    masks = head_masks(lats, width, head_size)
    queries = spread_heads(query_ref[...].astype(F32), masks).astype(BF16)
    base = items * patches
    lat_both = both_ref[base : base + lats, :]
    group = pl.program_id(0)
    term, lane = iota((16, GROUP * LANES), 0), iota((16, GROUP * LANES), 1)
    place = jnp.logical_and(
        lane % LANES == term * heads + group * GROUP + lane // LANES, term < 9
    ).astype(BF16)
    for i in range(items):
        both = jnp.concatenate([both_ref[i * patches : (i + 1) * patches, :], lat_both], 0)
        live = live_rows(flag_ref, i, items, patches, lats, queries.shape[0])
        scores = scale * transposed_right(both[:, :width], queries)
        masked = jnp.where(live, scores, MASKED)
        top = jnp.max(masked, axis=0, keepdims=True)
        block_exp = jnp.where(live, jnp.exp(masked - top), 0.0)
        total = jnp.sum(block_exp, axis=0, keepdims=True)
        moment = jnp.sum(block_exp * scores, axis=0, keepdims=True)
        part = transposed_left(block_exp.astype(BF16), both[:, width:])
        part_ref[i] = collect_heads(part, masks)
        top_ref[0, i] = jnp.broadcast_to(top, top_ref.shape[2:])
        terms = jnp.concatenate(
            [t.astype(F32) for x in (top, total, moment) for t in split_terms(x)]
            + [jnp.zeros((7, top.shape[1]), F32)],
            0,
        ).astype(BF16)
        wide = transposed_left(terms, place)
        mark = wide[:lats, :LANES]
        for h in range(1, GROUP):
            mark = mark + wide[h * lats : (h + 1) * lats, h * LANES : (h + 1) * LANES]
        mark_ref[i] = mark

    end = message_refs[0].shape[1] - LANES
    for s, message_ref in enumerate(message_refs):
        start = pl.multiple_of(lax.rem(flag_ref[items + 1] + s, frames) * row_total, row_total)
        rows = pl.ds(start, row_total)
        block = jnp.concatenate([part_ref[i, rows, :] for i in range(items)], 0).astype(BF16)
        mark = jnp.concatenate([mark_ref[i, rows, :] for i in range(items)], 0).astype(BF16)
        for g in range(end // width):

            @pl.when(group == g)
            def _():
                message_ref[:, g * width : (g + 1) * width] = block
                if g == 0:
                    message_ref[:, end:] = mark
                else:
                    message_ref[:, end:] = message_ref[:, end:] + mark


def merge_kernel(*refs, chunks, frames, items, head_size, heads):
    message_refs = refs[: chunks * frames]
    base_ref, weight_ref, gain_ref, bias_ref = refs[chunks * frames : chunks * frames + 4]
    merged_ref, mid_ref, ffn_ref, log_ref, entropy_ref = refs[chunks * frames + 4 :]
    own, columns = message_refs[0].shape
    half = columns - LANES
    lane, column = iota((LANES, 3 * LANES), 0), iota((LANES, 3 * LANES), 1)
    gather = jnp.logical_and(
        jnp.logical_and(lane // heads // 3 == column // LANES, lane % heads == column % LANES),
        lane < 9 * heads,
    ).astype(BF16)
    expand = head_expand(half, head_size)
    live = iota((own, LANES), 1) < heads
    spread = jnp.zeros((own, LANES), F32)
    for c in range(chunks):
        sources = message_refs[c * frames : (c + 1) * frames]
        stats = [matmul(x[:, half:], gather) for x in sources]
        tops = [x[:, :LANES] for x in stats]
        peak = functools.reduce(jnp.maximum, tops)
        factors = [jnp.exp(t - peak) for t in tops]
        whole = sum(f * x[:, LANES : 2 * LANES] for f, x in zip(factors, stats))
        moment = sum(f * x[:, 2 * LANES :] for f, x in zip(factors, stats))
        whole = jnp.where(live, whole, 1.0)
        log_total = jnp.where(live, peak + jnp.log(whole), 0.0)
        log_ref[c] = log_total
        spread = spread + jnp.where(live, log_total - moment / whole, 0.0)
        merged = jnp.zeros((own, half), F32)
        for x, factor in zip(sources, factors):
            share = jnp.where(live, factor / whole, 0.0)
            wide = jnp.dot(share, expand, precision=HIGHEST, preferred_element_type=F32)
            merged = merged + x[:, :half].astype(F32) * wide
        merged_ref[:, c * half : (c + 1) * half] = merged
    entropy_ref[...] = jnp.broadcast_to(
        jnp.sum(spread, axis=1, keepdims=True) * (1.0 / HEADS), entropy_ref.shape
    )
    base = jnp.concatenate([base_ref[...]] * items, 0)
    mid = base + matmul(merged_ref[...].astype(BF16), weight_ref[...])
    mid_ref[...] = mid
    ffn_ref[...] = layer_norm(mid, gain_ref[...], bias_ref[...]).astype(BF16)


def gelu_parts(x):
    share = 0.5 * (1.0 + lax.erf(x * (0.5**0.5)))
    slope = share + x * jnp.exp(-0.5 * x * x) * ((2.0 * jnp.pi) ** -0.5)
    return x * share, slope


def feed_kernel(flag_ref, *refs, devices, items):
    row_refs = refs[:devices]
    low_ref, up_ref, down_ref, plane_ref, plane_low_ref, result_ref = refs[devices : devices + 6]
    grad_refs = refs[devices + 6 :]
    own, width = row_refs[0].shape
    shard = low_ref.shape[0] // devices
    unit, piece = pack_shape(own, shard, width)
    me = flag_ref[2 * items + 2]
    for d in range(devices):
        plane_ref[d * own : (d + 1) * own, :] = row_refs[d][...]
        source = jnp.bitwise_xor(me, d) * shard
        for a in range(own // unit):
            rows = slice(d * own + a * unit, d * own + (a + 1) * unit)
            for b in range(shard // unit):
                start = pl.multiple_of(source + b * unit, unit)
                plane_low_ref[rows, b * piece : (b + 1) * piece] = low_ref[
                    pl.ds(start, unit), a * piece : (a + 1) * piece
                ]
    upward = matmul(plane_ref[...], up_ref[...])
    hidden, slope = gelu_parts(upward)
    grad_up = (slope * transposed_right(plane_low_ref[...], down_ref[...])).astype(BF16)
    grad = transposed_right(grad_up, up_ref[...]).astype(BF16)
    result = matmul(hidden.astype(BF16), down_ref[...]).astype(BF16)
    for d in range(devices):
        grad_refs[d][...] = grad[d * own : (d + 1) * own, :]
        result_ref[jnp.bitwise_xor(me, d)] = result[d * own : (d + 1) * own, :]


def feed_back_kernel(
    plane_ref, plane_low_ref, other_ref, other_low_ref, up_ref, down_ref, near_hidden_ref,
    near_grad_ref, far_hidden_ref, far_grad_ref, *, plane_blocks,
):
    near = pl.program_id(0) < plane_blocks
    rows = jnp.where(near, plane_ref[...], other_ref[...])
    low = jnp.where(near, plane_low_ref[...], other_low_ref[...])
    hidden, slope = gelu_parts(matmul(rows, up_ref[...]))
    hidden = hidden.astype(BF16)
    grad_up = (slope * transposed_right(low, down_ref[...])).astype(BF16)

    @pl.when(near)
    def _():
        near_hidden_ref[...] = hidden
        near_grad_ref[...] = grad_up

    @pl.when(jnp.logical_not(near))
    def _():
        far_hidden_ref[...] = hidden
        far_grad_ref[...] = grad_up


def outer_kernel(near_ref, far_ref, near_more_ref, far_more_ref, out_ref):
    total = transposed_left(near_ref[...], near_more_ref[...]) + transposed_left(
        far_ref[...], far_more_ref[...]
    )
    out_ref[...] = total.astype(out_ref.dtype)


def norm_backward(rows, gain, gradient):
    center = rows - jnp.mean(rows, axis=1, keepdims=True)
    rate = lax.rsqrt(jnp.mean(center * center, axis=1, keepdims=True) + EPSILON)
    unit = center * rate
    scaled = gradient * gain
    inner = scaled - jnp.mean(scaled, axis=1, keepdims=True)
    back = rate * (inner - unit * jnp.mean(scaled * unit, axis=1, keepdims=True))
    return (
        back,
        jnp.sum(gradient * unit, axis=0, keepdims=True),
        jnp.sum(gradient, axis=0, keepdims=True),
    )


def turn_kernel(*refs, devices, items, chunks, head_size, heads):
    part_refs = refs[:devices]
    mid_ref, cotangent_ref, gain_ref, merged_ref, log_ref, weight_ref = refs[
        devices : devices + 6
    ]
    message_ref, branch_ref, base_ref, sums_ref = refs[devices + 6 :]
    own, width = mid_ref.shape
    half = width // chunks
    gradient = total_of([x[...] for x in part_refs])
    back, gain_sum, bias_sum = norm_backward(mid_ref[...], gain_ref[...], gradient)
    grad_mid = cotangent_ref[...] + back
    sums_ref[...] = jnp.zeros(sums_ref.shape, F32)
    sums_ref[0:1, :] = gain_sum
    sums_ref[1:2, :] = bias_sum
    row_total = own // items
    base_ref[...] = total_of(
        [grad_mid[i * row_total : (i + 1) * row_total] for i in range(items)]
    )
    branch = grad_mid.astype(BF16)
    branch_ref[:, :width] = branch
    branch_ref[:, width:] = merged_ref[...].astype(BF16)
    grad_att = transposed_right(branch, weight_ref[...]).astype(BF16)
    expand = head_expand(half, head_size)
    lane, column = iota((6 * LANES, LANES), 0), iota((6 * LANES, LANES), 1)
    place = jnp.logical_and(
        lane % LANES < heads, column == (lane // LANES) * heads + lane % LANES
    ).astype(BF16)
    message_ref[:, :width] = grad_att
    for c in range(chunks):
        columns = slice(c * half, (c + 1) * half)
        delta = lax.dot_general(
            merged_ref[:, columns] * grad_att[:, columns].astype(F32),
            expand,
            (((1,), (1,)), ((), ())),
            precision=HIGHEST,
            preferred_element_type=F32,
        )
        terms = jnp.concatenate([t for x in (log_ref[c], delta) for t in split_terms(x)], 1)
        message_ref[:, width + c * LANES : width + (c + 1) * LANES] = matmul(
            terms, place
        ).astype(BF16)


def backward_kernel(
    *refs, frames, items, patches, scale, head_size, heads,
):
    flag_ref, both_ref, query_ref, top_ref = refs[:4]
    grad_refs = refs[4 : 4 + frames]
    mark_refs = refs[4 + frames : 4 + 2 * frames]
    out_ref, sum_ref, held_ref, note_ref = refs[4 + 2 * frames :]
    lats, width = query_ref.shape
    own = grad_refs[0].shape[0]
    row_total = own // items
    base = items * patches
    for s in range(frames):
        source = lax.rem(flag_ref[items + 1] + (frames - s), frames)
        rows = pl.ds(pl.multiple_of(source * row_total, row_total), row_total)
        block = grad_refs[s][...].astype(F32)
        mark = mark_refs[s][...].astype(F32)
        for i in range(items):
            held_ref[i, rows, :] = block[i * row_total : (i + 1) * row_total]
            note_ref[i, rows, :] = mark[i * row_total : (i + 1) * row_total]
    masks = head_masks(lats, width, head_size)
    queries = spread_heads(query_ref[...].astype(F32), masks).astype(BF16)
    lat_both = both_ref[base : base + lats, :]
    row, lane = iota((GROUP * 8, LANES), 0), iota((GROUP * 8, LANES), 1)
    pick = jnp.logical_and(
        jnp.logical_and(
            lane // heads // 3 == row % 8,
            lane % heads == pl.program_id(0) * GROUP + row // 8,
        ),
        lane < 6 * heads,
    ).astype(BF16)
    grad_query = jnp.zeros((queries.shape[0], width), F32)
    lat_grad_key = jnp.zeros((lats, width), F32)
    lat_grad_value = jnp.zeros((lats, width), F32)
    for i in range(items):
        rows = slice(i * patches, (i + 1) * patches)
        stats = transposed_right(pick, note_ref[i].astype(BF16))
        stats = jnp.concatenate([stats[h * 8 : (h + 1) * 8] for h in range(GROUP)], 1)
        log_total = stats[0:1]
        delta = stats[1:2]
        top = top_ref[0, i, 0:1, :]
        rescale = jnp.exp(top - log_total)
        both = jnp.concatenate([both_ref[rows, :], lat_both], 0)
        keys, values = both[:, :width], both[:, width:]
        grads = spread_heads(held_ref[i], masks).astype(BF16)
        live = live_rows(flag_ref, i, items, patches, lats, queries.shape[0])
        masked = jnp.where(live, scale * transposed_right(keys, queries), MASKED)
        probs = jnp.where(live, jnp.exp(masked - log_total), 0.0)
        block_exp = jnp.where(live, jnp.exp(masked - top), 0.0)
        weights = (block_exp.astype(BF16).astype(F32) * rescale).astype(BF16)
        grad_scores = (probs * (transposed_right(values, grads) - delta)).astype(BF16)
        grad_key = scale * matmul(grad_scores, queries)
        grad_value = matmul(weights, grads)
        out_ref[rows, :width] = grad_key[:patches].astype(BF16)
        out_ref[rows, width:] = grad_value[:patches].astype(BF16)
        grad_query = grad_query + transposed_left(grad_scores, keys)
        lat_grad_key = lat_grad_key + grad_key[patches:]
        lat_grad_value = lat_grad_value + grad_value[patches:]
    out_ref[base : base + lats, :width] = lat_grad_key.astype(BF16)
    out_ref[base : base + lats, width:] = lat_grad_value.astype(BF16)
    sum_ref[...] = scale * collect_heads(grad_query, masks)


def media_kernel(flag_ref, *refs, chunks, items, frames):
    grad_refs, lat_refs, weight_refs = [
        refs[k * chunks : (k + 1) * chunks] for k in range(3)
    ]
    media_ref, time_ref, gain_ref, out_ref, sums_ref, product_ref = refs[3 * chunks :]
    item = pl.program_id(0)

    @pl.when(item == 0)
    def _():
        sums_ref[...] = jnp.zeros(sums_ref.shape, F32)
        product_ref[...] = functools.reduce(
            jnp.add, [transposed_right(g[...], w[...]) for g, w in zip(lat_refs, weight_refs)]
        )

    gradient = functools.reduce(
        jnp.add, [transposed_right(g[...], w[...]) for g, w in zip(grad_refs, weight_refs)]
    )
    inputs = media_ref[...].astype(F32) + time_ref[pl.ds(item, 1), :]
    back, gain_sum, bias_sum = norm_backward(inputs, gain_ref[...], gradient)
    out_ref[...] = back.astype(BF16)
    place = iota((frames, 1), 0) == flag_ref[items + 2 + item]
    sums_ref[0:frames, :] += jnp.where(place, jnp.sum(back, axis=0, keepdims=True), 0.0)
    sums_ref[8:9, :] += gain_sum
    sums_ref[9:10, :] += bias_sum


def latent_kernel(flag_ref, *refs, chunks, items):
    query_refs = refs[:chunks]
    (
        product_ref, query_weight_ref, latent_ref, gain_ref, base_ref, ffn_ref, media_ref, out_ref,
    ) = refs[chunks:]
    lats, width = latent_ref.shape
    half = width // chunks
    gradient = product_ref[...]
    for c in range(chunks):
        gradient = gradient + transposed_right(
            query_refs[c][...].astype(BF16), query_weight_ref[:, c * half : (c + 1) * half]
        )
        out_ref[lats : 2 * lats, c * half : (c + 1) * half] = query_refs[c][...]
    back, gain_sum, bias_sum = norm_backward(latent_ref[...], gain_ref[...], gradient)
    out_ref[:lats, :] = back
    row_total = base_ref.shape[0]
    start = pl.multiple_of(flag_ref[items + 1] * row_total, row_total)
    out_ref[pl.ds(start, row_total), :] += base_ref[...]
    at = 2 * lats
    out_ref[at : at + 8, :] = ffn_ref[...]
    out_ref[at + 2 : at + 3, :] = gain_sum
    out_ref[at + 3 : at + 4, :] = bias_sum
    out_ref[at + 8 : at + 24, :] = media_ref[...]
    out_ref[at + 24 :, :] = jnp.zeros((out_ref.shape[0] - at - 24, width), F32)


def rows_kernel(flag_ref, *refs, counts, frames, items):
    part_refs, out_refs, held_ref = refs[: sum(counts)], refs[sum(counts) : -1], refs[-1]
    rows = held_ref.shape[1]
    first = column = 0
    for count in counts:
        total = total_of([x[...] for x in part_refs[first : first + count]])
        for f in range(frames):
            held_ref[f, :, column : column + total.shape[1]] = total[f * rows : (f + 1) * rows]
        first += count
        column += total.shape[1]
    for s, out_ref in enumerate(out_refs):
        block = held_ref[lax.rem(flag_ref[items + 1] + s, frames)]
        out_ref[...] = block.astype(out_ref.dtype)


def place_kernel(flag_ref, *refs, chunks, frames, items, groups):
    block_refs = refs[:frames]
    key_ref, value_ref, out_ref = refs[frames:]
    width = key_ref.shape[2] // (chunks * groups)
    for s in range(frames):
        source = lax.rem(flag_ref[items + 1] + (frames - s), frames)
        for g in range(chunks * groups):
            block = block_refs[s][:, 2 * g * width : 2 * (g + 1) * width].astype(F32)
            key_ref[source, :, g * width : (g + 1) * width] = block[:, :width]
            value_ref[source, :, g * width : (g + 1) * width] = block[:, width:]
        out_ref[source] = block_refs[s][:, 2 * chunks * groups * width :].astype(F32)


def body(
    media,
    cotangent,
    frame_count,
    frame_start,
    latents,
    time_embed,
    media_gain,
    media_bias,
    latent_gain,
    latent_bias,
    ffn_gain,
    ffn_bias,
    query_weight,
    key_weight,
    value_weight,
    out_weight,
    up_weight,
    down_weight,
):
    items = media.shape[0]
    patches = media.shape[2]
    width = media.shape[3]
    lats = latents.shape[0]
    frame_total = time_embed.shape[0]
    row_total = cotangent.shape[1]
    own = items * row_total
    head_size = width // HEADS
    half = width // CHUNKS
    chunk_heads = HEADS // CHUNKS
    group_width = GROUP * head_size
    groups = chunk_heads // GROUP
    stack = GROUP * lats
    tokens = items * patches
    all_tokens = tokens + lats
    shard = query_weight.shape[0]
    hidden_shard = down_weight.shape[0]
    item_size = lax.axis_size("items")
    frame_size = lax.axis_size("frames")
    plane = item_size * own
    item_index = lax.axis_index("items")
    slot = lax.axis_index("frames")
    row_base = slot * row_total
    params = pltpu.CompilerParams(vmem_limit_bytes=56 * 2**20)
    smem = pl.BlockSpec(memory_space=pltpu.SMEM)
    whole = pl.BlockSpec(memory_space=pltpu.VMEM)
    sizes = dict(items=items, head_size=head_size, heads=chunk_heads)

    def struct(shape, kind):
        return jax.ShapeDtypeStruct(shape, kind)

    short = pl.CostEstimate(flops=1000, bytes_accessed=1000, transcendentals=0)

    def column_blocks(x):
        return jnp.transpose(x.reshape(-1, item_size, shard), (1, 0, 2))

    def scatter_exchange(x, axis):
        return jnp.sum(lax.all_to_all(x, axis, 0, 0).astype(F32), axis=0)

    grad_out = cotangent.reshape(own, width)
    low_columns = own * width // shard
    joined, grad_low = pl.pallas_call(
        functools.partial(join_kernel, width=group_width),
        out_shape=[struct((shard, 2 * width + low_columns), BF16), struct((own, width), BF16)],
        cost_estimate=short,
        compiler_params=params,
    )(key_weight, value_weight, grad_out)
    kv_full = lax.all_gather(joined, "items", axis=0, tiled=True)

    lat_norm = layer_norm(latents, latent_gain, latent_bias).astype(BF16)
    lat_cols = lax.dynamic_slice_in_dim(lat_norm, item_index * shard, shard, 1)
    query_blocks = column_blocks(matmul(lat_cols, query_weight))
    query_cols = scatter_exchange(query_blocks, "items").astype(BF16)
    query_spread = jnp.broadcast_to(query_cols[None], (item_size, lats, shard))
    queries = jnp.transpose(lax.all_to_all(query_spread, "items", 0, 0), (1, 0, 2)).reshape(
        lats, width
    )

    counts = lax.dynamic_slice_in_dim(frame_count, item_index * items, items)
    starts = lax.dynamic_slice_in_dim(frame_start, item_index * items, items)
    offset = (slot - starts) % frame_total
    flags = jnp.concatenate(
        [
            (offset < counts).astype(jnp.int32),
            (slot == 0).astype(jnp.int32)[None],
            slot.astype(jnp.int32)[None],
            offset.astype(jnp.int32),
            item_index.astype(jnp.int32)[None],
        ]
    )
    picker = (offset[:, None] == jnp.arange(frame_total, dtype=jnp.int32)[None, :]).astype(F32)
    time_rows = jnp.dot(picker, time_embed, precision=HIGHEST, preferred_element_type=F32)
    flat_media = media.reshape(tokens, width)
    steps = tokens // lats
    all_rows = pl.pallas_call(
        functools.partial(norm_kernel, steps=steps, per_item=patches // lats),
        grid=(steps + 1,),
        in_specs=[
            pl.BlockSpec((lats, width), lambda i: (jnp.minimum(i, steps - 1), 0)),
            whole,
            whole,
            whole,
            whole,
        ],
        out_specs=pl.BlockSpec((lats, width), lambda i: (i, 0)),
        out_shape=struct((all_tokens, width), BF16),
        cost_estimate=short,
        compiler_params=params,
    )(
        after(flat_media, query_blocks),
        time_rows,
        media_gain[None],
        media_bias[None],
        lat_norm,
    )
    out_full = lax.all_gather(after(out_weight, all_rows), "items", axis=0, tiled=True)

    chip, core = item_index // 2, item_index % 2
    rows_across = after(all_rows, query_cols).T.reshape(item_size // 2, 2, shard, all_tokens)
    send_rows, keep_rows = [
        jnp.concatenate(
            [
                lax.dynamic_slice(
                    rows_across, (chip ^ k, which, 0, 0), (1, 1, shard, all_tokens)
                ).reshape(shard, all_tokens)
                for k in range(item_size // 2)
            ],
            0,
        )
        for which in (1 - core, core)
    ]
    low_shift = spread_on(after(grad_low, all_rows), "frames")[1:]

    up_slice = lax.all_to_all(after(up_weight, queries), "items", 1, 0, tiled=True)

    boths, tops, messages = [], [], []
    for c in range(CHUNKS):

        def block_of(g, c=c):
            return (0, c * groups + g)

        if c:
            rows = after(all_rows, tops[-1])
        else:
            rows = after(all_rows, queries, send_rows, keep_rows, *low_shift)
        both = matmul(rows, kv_full[:, 2 * c * half : 2 * (c + 1) * half]).astype(BF16)
        top, *parts = pl.pallas_call(
            functools.partial(
                forward_kernel, patches=patches, scale=head_size**-0.5, **sizes
            ),
            grid=(groups,),
            in_specs=[
                smem,
                pl.BlockSpec((all_tokens, 2 * group_width), lambda g: (0, g)),
                pl.BlockSpec((lats, group_width), block_of),
            ],
            out_specs=[pl.BlockSpec((1, items, 8, stack), lambda g: (g, 0, 0, 0))]
            + [pl.BlockSpec((own, half + LANES), lambda g: (0, 0))] * frame_size,
            out_shape=[struct((groups, items, 8, stack), F32)]
            + [struct((own, half + LANES), BF16)] * frame_size,
            scratch_shapes=[
                pltpu.VMEM((items, lats, group_width), F32),
                pltpu.VMEM((items, lats, LANES), F32),
            ],
            cost_estimate=short,
            compiler_params=params,
        )(flags, after(both, up_slice) if c else both, queries)
        boths.append(both)
        tops.append(top)
        messages += [p if s == 0 else send_on(p, "frames", s) for s, p in enumerate(parts)]
    low_other = lax.all_gather(
        after(jnp.stack(low_shift), tops[1]), "items", axis=0
    ).reshape(-1, width)

    base_rows = lax.dynamic_slice_in_dim(latents, row_base, row_total, 0)
    merged, mid_rows, ffn_in, logs, entropy_wide = pl.pallas_call(
        functools.partial(merge_kernel, chunks=CHUNKS, frames=frame_size, **sizes),
        out_shape=[
            struct((own, width), F32),
            struct((own, width), F32),
            struct((own, width), BF16),
            struct((CHUNKS, own, LANES), F32),
            struct((own, LANES), F32),
        ],
        cost_estimate=short,
        compiler_params=params,
    )(*messages, base_rows, out_full, ffn_gain[None], ffn_bias[None])
    entropy = entropy_wide[:, 0].reshape(items, row_total)

    query_full = lax.all_gather(after(query_weight, ffn_in), "items", axis=0, tiled=True)
    ffn_blocks = spread_across(ffn_in, "items")
    ffn_plane, low_plane, result_part, *parts = pl.pallas_call(
        functools.partial(feed_kernel, devices=item_size, items=items),
        grid=(1,),
        in_specs=[smem]
        + [whole] * item_size
        + [
            pl.BlockSpec((width, low_columns), lambda i: (0, 2 * width // low_columns)),
            whole,
            whole,
        ],
        out_specs=[whole] * (3 + item_size),
        out_shape=[struct((plane, width), BF16)] * 2
        + [struct((item_size, own, width), BF16)]
        + [struct((own, width), BF16)] * item_size,
        cost_estimate=short,
        compiler_params=params,
    )(flags, *ffn_blocks, kv_full, up_slice, down_weight)
    grad_blocks = collect_across(parts, "items")
    ffn_shift = spread_on(after(ffn_in, *ffn_blocks), "frames")[1:]
    ffn_other = lax.all_gather(jnp.stack(ffn_shift), "items", axis=0).reshape(-1, width)
    grad_blocks[0] = after(grad_blocks[0], *ffn_shift)

    turn, grad_branch, grad_base, ffn_sums = pl.pallas_call(
        functools.partial(turn_kernel, devices=item_size, chunks=CHUNKS, **sizes),
        out_shape=[
            struct((own, width + CHUNKS * LANES), BF16),
            struct((own, 2 * width), BF16),
            struct((row_total, width), F32),
            struct((8, width), F32),
        ],
        cost_estimate=short,
        compiler_params=params,
    )(*grad_blocks, mid_rows, grad_out, ffn_gain[None], merged, logs, out_full)
    turns = spread_on(turn, "frames")
    branch_plane = lax.all_gather(grad_branch, "items", axis=0, tiled=True)
    att_plane = lax.dynamic_slice_in_dim(
        branch_plane, width + item_index * shard, shard, 1
    )
    result_pieces = lax.all_to_all(after(result_part, turns[-1]), "items", 0, 0)
    turns[0] = after(turns[0], low_other, query_full)

    chunk_grads, chunk_queries = [], []

    def weight_terms(c):
        send = matmul(send_rows, chunk_grads[c]).astype(BF16)
        received = send_across(send, "items", 1).reshape(-1, shard, 2 * half)
        keep = matmul(after(keep_rows, send), chunk_grads[c]).astype(BF16)
        return send, keep.reshape(-1, shard, 2 * half), received

    def chip_pieces(keep, received):
        sums = [keep[k].astype(F32) + received[k].astype(F32) for k in range(item_size // 2)]
        return sums[:1] + [p.astype(BF16) for p in sums[1:]]

    def send_pieces(sums):
        return sums[:1] + [
            send_across(p, "items", 2 * k) for k, p in enumerate(sums) if k
        ]

    def frame_rows(ranges):
        rows = shard // frame_size
        columns = sum(parts[0].shape[1] for parts in ranges)
        return pl.pallas_call(
            functools.partial(
                rows_kernel,
                counts=tuple(len(parts) for parts in ranges),
                frames=frame_size,
                items=items,
            ),
            in_specs=[smem] + [whole] * sum(len(parts) for parts in ranges),
            out_specs=[whole] * frame_size,
            out_shape=[struct((rows, columns), F32)]
            + [struct((rows, columns), BF16)] * (frame_size - 1),
            scratch_shapes=[pltpu.VMEM((frame_size, rows, columns), F32)],
            cost_estimate=short,
            compiler_params=params,
        )(flags, *[part for parts in ranges for part in parts])

    def send_rows_on(rows):
        return [rows[0]] + [send_on(p, "frames", s) for s, p in enumerate(rows) if s]

    for c in range(CHUNKS):

        def block_of(g, c=c):
            return (0, c * groups + g)

        chunk_grad, chunk_query = pl.pallas_call(
            functools.partial(
                backward_kernel, frames=frame_size, patches=patches, scale=head_size**-0.5, **sizes
            ),
            grid=(groups,),
            in_specs=[
                smem,
                pl.BlockSpec((all_tokens, 2 * group_width), lambda g: (0, g)),
                pl.BlockSpec((lats, group_width), block_of),
                pl.BlockSpec((1, items, 8, stack), lambda g: (g, 0, 0, 0)),
            ]
            + [pl.BlockSpec((own, group_width), block_of)] * frame_size
            + [pl.BlockSpec((own, LANES), lambda g, c=c: (0, width // LANES + c))] * frame_size,
            out_specs=[
                pl.BlockSpec((all_tokens, 2 * group_width), lambda g: (0, g)),
                pl.BlockSpec((lats, group_width), lambda g: (0, g)),
            ],
            out_shape=[
                struct((all_tokens, 2 * half), BF16),
                struct((lats, half), F32),
            ],
            scratch_shapes=[
                pltpu.VMEM((items, lats, group_width), F32),
                pltpu.VMEM((items, lats, LANES), F32),
            ],
            cost_estimate=short,
            compiler_params=params,
        )(flags, after(boths[c], *held) if c else boths[c], queries, tops[c], *turns, *turns)
        chunk_grads.append(chunk_grad)
        chunk_queries.append(chunk_query)
        if c == 0:
            first_send, first_keep, first_received = weight_terms(0)
            held = (first_send, ffn_other)
    pieces = [chip_pieces(after(first_keep, chunk_grads[-1]), first_received)]
    kv_sums = [send_pieces(pieces[0])]
    last_grad = chunk_grads[-1]
    chunk_grads[-1] = after(last_grad, *pieces[0])
    last_send, last_keep, last_received = weight_terms(CHUNKS - 1)
    pieces.append(chip_pieces(last_keep, last_received))
    kv_sums.append(send_pieces(pieces[-1]))
    chunk_grads[-1] = last_grad
    out_part = transposed_left(att_plane, after(branch_plane, last_send)[:, :width])

    last_block = pl.BlockSpec((lats, 2 * half), lambda i: (tokens // lats, 0))
    media_grad, media_sums, lat_product = pl.pallas_call(
        functools.partial(media_kernel, chunks=CHUNKS, items=items, frames=frame_total),
        grid=(items,),
        in_specs=[smem]
        + [pl.BlockSpec((patches, 2 * half), lambda i: (i, 0))] * CHUNKS
        + [last_block] * CHUNKS
        + [pl.BlockSpec((width, 2 * half), lambda i, c=c: (0, c)) for c in range(CHUNKS)]
        + [pl.BlockSpec((patches, width), lambda i: (i, 0)), whole, whole],
        out_specs=[
            pl.BlockSpec((patches, width), lambda i: (i, 0)),
            pl.BlockSpec((16, width), lambda i: (0, 0)),
            pl.BlockSpec((lats, width), lambda i: (0, 0)),
        ],
        out_shape=[
            struct((tokens, width), BF16),
            struct((16, width), F32),
            struct((lats, width), F32),
        ],
        cost_estimate=short,
        compiler_params=params,
    )(
        flags,
        *chunk_grads[:-1],
        after(chunk_grads[-1], *pieces[-1], out_part),
        *chunk_grads,
        *[kv_full] * CHUNKS,
        flat_media,
        time_rows,
        media_gain[None],
    )

    sum_rows = 2 * lats + 24
    sum_rows += -sum_rows % (8 * item_size)
    payload = pl.pallas_call(
        functools.partial(latent_kernel, chunks=CHUNKS, items=items),
        in_specs=[smem] + [whole] * (CHUNKS + 7),
        out_specs=whole,
        out_shape=struct((sum_rows, width), F32),
        cost_estimate=short,
        compiler_params=params,
    )(
        flags,
        *chunk_queries,
        after(lat_product, result_pieces, *kv_sums[0]),
        query_full,
        latents,
        latent_gain[None],
        grad_base,
        ffn_sums,
        media_sums,
    )
    payload_part = lax.psum_scatter(payload, "items", scatter_dimension=0, tiled=True)

    block_rows = min(512, plane)
    plane_blocks = plane // block_rows
    near = pl.BlockSpec((block_rows, width), lambda i: (jnp.minimum(i, plane_blocks - 1), 0))
    far = pl.BlockSpec((block_rows, width), lambda i: (jnp.maximum(i - plane_blocks, 0), 0))
    near_hidden = pl.BlockSpec(
        (block_rows, hidden_shard), lambda i: (jnp.minimum(i, plane_blocks - 1), 0)
    )
    far_hidden = pl.BlockSpec(
        (block_rows, hidden_shard), lambda i: (jnp.maximum(i - plane_blocks, 0), 0)
    )
    hidden_near, grad_near, hidden_far, grad_far = pl.pallas_call(
        functools.partial(feed_back_kernel, plane_blocks=plane_blocks),
        grid=(plane_blocks * frame_size,),
        in_specs=[near, near, far, far, whole, whole],
        out_specs=[near_hidden, near_hidden, far_hidden, far_hidden],
        out_shape=[struct((plane, hidden_shard), BF16)] * 2
        + [struct((plane * (frame_size - 1), hidden_shard), BF16)] * 2,
        cost_estimate=short,
        compiler_params=params,
    )(
        ffn_plane,
        low_plane,
        after(ffn_other, payload),
        low_other,
        up_slice,
        down_weight,
    )

    def outer(left_near, left_far, right_near, right_far, tile, kind):
        rows = left_near.columns, right_near.columns
        return pl.pallas_call(
            outer_kernel,
            grid=(rows[0] // tile,),
            in_specs=[
                left_near.tiles(tile),
                left_far.tiles(tile),
                right_near.whole(),
                right_far.whole(),
            ],
            out_specs=pl.BlockSpec((tile, rows[1]), lambda i: (i, 0)),
            out_shape=struct(rows, kind),
            cost_estimate=short,
            compiler_params=params,
        )(left_near.array, left_far.array, right_near.array, right_far.array)

    shared_rows = frame_rows(
        [[after(kv[0], grad_near), *kv[1:]] for kv in kv_sums] + [[out_part]]
    )
    shared_moved = send_rows_on(shared_rows)
    up_part = outer(
        Rows(ffn_plane),
        Rows(ffn_other),
        Rows(after(grad_near, *shared_rows)),
        Rows(grad_far),
        width // 4,
        BF16,
    )
    up_grad = lax.all_to_all(up_part, "items", 0, 1, tiled=True).astype(F32)

    down_grad = outer(
        Rows(after(hidden_near, up_part)),
        Rows(hidden_far),
        Rows(low_plane),
        Rows(low_other),
        256 if hidden_shard % 256 == 0 else hidden_shard,
        F32,
    )
    placed = spread_on(total_of(shared_moved).astype(BF16), "frames")
    key_grad, value_grad, out_grad = pl.pallas_call(
        functools.partial(
            place_kernel, chunks=CHUNKS, frames=frame_size, items=items, groups=groups
        ),
        in_specs=[smem] + [whole] * len(placed),
        out_specs=[whole] * 3,
        out_shape=[struct((frame_size, shard // frame_size, width), F32)] * 3,
        cost_estimate=short,
        compiler_params=params,
    )(flags, *placed)

    payload_part = after(payload_part, up_part)
    payload_others = spread_on(payload_part.astype(BF16), "frames")[1:]
    sums = lax.all_gather(
        total_of([payload_part] + payload_others), "items", axis=0, tiled=True
    )
    latents_grad = sums[:lats]
    query_grad = transposed_left(lat_cols, sums[lats : 2 * lats].astype(BF16))
    at = 2 * lats
    column_sums = lax.dynamic_slice_in_dim(
        sums[at + 8 : at + 24], item_index * shard, shard, 1
    )

    result = mid_rows + total_of([result_pieces[d] for d in range(item_size)])
    return (
        result.reshape(items, row_total, width),
        entropy,
        media_grad.reshape(media.shape),
        latents_grad,
        column_sums[:frame_total],
        column_sums[8],
        column_sums[9],
        sums[at + 2],
        sums[at + 3],
        sums[at],
        sums[at + 1],
        query_grad,
        key_grad.reshape(shard, width),
        value_grad.reshape(shard, width),
        out_grad.reshape(shard, width),
        up_grad,
        down_grad,
    )


def solution(mesh):
    return jax.shard_map(
        body,
        mesh=mesh,
        in_specs=(
            P("items", "frames", None, None),
            P("items", "frames", None),
            P(),
            P(),
            P(),
            P(),
            P(),
            P(),
            P(),
            P(),
            P(),
            P(),
            P("items", None),
            P("items", None),
            P("items", None),
            P("items", None),
            P("items", None),
            P("items", None),
        ),
        out_specs=(
            P("items", "frames", None),
            P("items", "frames"),
            P("items", "frames", None, None),
            P(),
            P(None, "items"),
            P("items"),
            P("items"),
            P(),
            P(),
            P(),
            P(),
            P("items", None),
            P("items", None),
            P("items", None),
            P("items", None),
            P("items", None),
            P("items", None),
        ),
        check_vma=False,
    )
```

```python
import functools
import math

import jax
import jax.numpy as jnp
from jax import lax
from jax.experimental import pallas as pl
from jax.experimental.pallas import tpu as pltpu
from jax.sharding import PartitionSpec as P

HEADS = 16
GROUP = 4
CHUNKS = 2
LANES = 128
EPSILON = 1e-05
MASKED = -1e30
F32 = jnp.float32
BF16 = jnp.bfloat16
HIGHEST = lax.Precision.HIGHEST


def layer_norm(inputs, norm_gain, norm_bias):
    center = inputs - jnp.mean(inputs, axis=-1, keepdims=True)
    spread = jnp.mean(center * center, axis=-1, keepdims=True)
    return center * lax.rsqrt(spread + EPSILON) * norm_gain + norm_bias


def matmul(left_side, right_side):
    return jnp.dot(left_side, right_side, preferred_element_type=F32)


def transposed_left(left_side, right_side):
    return lax.dot_general(
        left_side, right_side, (((0,), (0,)), ((), ())), preferred_element_type=F32
    )


def transposed_right(left_side, right_side):
    return lax.dot_general(
        left_side, right_side, (((1,), (1,)), ((), ())), preferred_element_type=F32
    )


def send_on(x, axis, step):
    size = lax.axis_size(axis)
    return lax.ppermute(x, axis, [(i, (i + step) % size) for i in range(size)])


def send_across(x, axis, distance):
    return lax.ppermute(x, axis, [(i, i ^ distance) for i in range(lax.axis_size(axis))])


def spread_on(x, axis):
    return [x] + [send_on(x, axis, s) for s in range(1, lax.axis_size(axis))]


def spread_across(x, axis):
    chips = [x] + [send_across(x, axis, d) for d in range(2, lax.axis_size(axis), 2)]
    return [b for block in chips for b in (block, send_across(block, axis, 1))]


def collect_across(pieces, axis):
    return [pieces[0]] + [send_across(p, axis, d) for d, p in enumerate(pieces) if d]


def total_of(pieces):
    return functools.reduce(jnp.add, [p.astype(F32) for p in pieces])


def after(x, *earlier):
    return lax.optimization_barrier((x,) + earlier)[0]


def split_terms(x):
    high = x.astype(BF16)
    rest = x - high.astype(F32)
    middle = rest.astype(BF16)
    return high, middle, (rest - middle.astype(F32)).astype(BF16)


def iota(shape, dim):
    return lax.broadcasted_iota(jnp.int32, shape, dim)


def head_masks(rows, width, head_size):
    lane = iota((rows, width), 1)
    return [
        jnp.logical_and(lane >= h * head_size, lane < (h + 1) * head_size)
        for h in range(width // head_size)
    ]


def spread_heads(block, masks):
    return jnp.concatenate([jnp.where(m, block, jnp.zeros_like(block)) for m in masks], 0)


def collect_heads(block, masks):
    rows = block.shape[0] // len(masks)
    total = jnp.where(masks[0], block[:rows], 0.0)
    for h in range(1, len(masks)):
        total = total + jnp.where(masks[h], block[h * rows : (h + 1) * rows], 0.0)
    return total


def head_expand(width, head_size):
    row, column = iota((LANES, width), 0), iota((LANES, width), 1)
    return jnp.logical_and(column >= row * head_size, column < (row + 1) * head_size).astype(F32)


def live_rows(flag_ref, item, items, patches, lats, columns):
    row = iota((patches + lats, columns), 0)
    media = jnp.logical_and(row < patches, flag_ref[item] > 0)
    return jnp.logical_or(media, jnp.logical_and(row >= patches, flag_ref[items] > 0))


def pack_shape(own, shard, width):
    unit = math.gcd(own, shard)
    return unit, width * unit // shard


def join_kernel(key_ref, value_ref, cotangent_ref, out_ref, low_ref, *, width):
    for g in range(key_ref.shape[1] // width):
        columns = slice(g * width, (g + 1) * width)
        out_ref[:, 2 * g * width : (2 * g + 1) * width] = key_ref[:, columns]
        out_ref[:, (2 * g + 1) * width : (2 * g + 2) * width] = value_ref[:, columns]
    low = cotangent_ref[...].astype(BF16)
    low_ref[...] = low
    own, span = low.shape
    unit, piece = pack_shape(own, out_ref.shape[0], span)
    for a in range(own // unit):
        for b in range(span // piece):
            at = 2 * span + a * piece
            out_ref[b * unit : (b + 1) * unit, at : at + piece] = low[
                a * unit : (a + 1) * unit, b * piece : (b + 1) * piece
            ]


def norm_kernel(media_ref, time_ref, gain_ref, bias_ref, lat_ref, out_ref, *, steps, per_item):
    step = pl.program_id(0)

    @pl.when(step < steps)
    def _():
        rows = media_ref[...].astype(F32) + time_ref[pl.ds(step // per_item, 1), :]
        out_ref[...] = layer_norm(rows, gain_ref[...], bias_ref[...]).astype(BF16)

    @pl.when(step == steps)
    def _():
        out_ref[...] = lat_ref[...]


def forward_kernel(
    flag_ref, both_ref, query_ref, top_ref, *refs, items, patches, scale, head_size, heads,
):
    message_refs, (part_ref, mark_ref) = refs[:-2], refs[-2:]
    lats, width = query_ref.shape
    frames = len(message_refs)
    own = message_refs[0].shape[0]
    row_total = own // items
    masks = head_masks(lats, width, head_size)
    queries = spread_heads(query_ref[...].astype(F32), masks).astype(BF16)
    base = items * patches
    lat_both = both_ref[base : base + lats, :]
    group = pl.program_id(0)
    term, lane = iota((16, GROUP * LANES), 0), iota((16, GROUP * LANES), 1)
    place = jnp.logical_and(
        lane % LANES == term * heads + group * GROUP + lane // LANES, term < 9
    ).astype(BF16)
    for i in range(items):
        both = jnp.concatenate([both_ref[i * patches : (i + 1) * patches, :], lat_both], 0)
        live = live_rows(flag_ref, i, items, patches, lats, queries.shape[0])
        scores = scale * transposed_right(both[:, :width], queries)
        masked = jnp.where(live, scores, MASKED)
        top = jnp.max(masked, axis=0, keepdims=True)
        block_exp = jnp.where(live, jnp.exp(masked - top), 0.0)
        total = jnp.sum(block_exp, axis=0, keepdims=True)
        moment = jnp.sum(block_exp * scores, axis=0, keepdims=True)
        part = transposed_left(block_exp.astype(BF16), both[:, width:])
        part_ref[i] = collect_heads(part, masks)
        top_ref[0, i] = jnp.broadcast_to(top, top_ref.shape[2:])
        terms = jnp.concatenate(
            [t.astype(F32) for x in (top, total, moment) for t in split_terms(x)]
            + [jnp.zeros((7, top.shape[1]), F32)],
            0,
        ).astype(BF16)
        wide = transposed_left(terms, place)
        mark = wide[:lats, :LANES]
        for h in range(1, GROUP):
            mark = mark + wide[h * lats : (h + 1) * lats, h * LANES : (h + 1) * LANES]
        mark_ref[i] = mark

    end = message_refs[0].shape[1] - LANES
    for s, message_ref in enumerate(message_refs):
        start = pl.multiple_of(lax.rem(flag_ref[items + 1] + s, frames) * row_total, row_total)
        rows = pl.ds(start, row_total)
        block = jnp.concatenate([part_ref[i, rows, :] for i in range(items)], 0).astype(BF16)
        mark = jnp.concatenate([mark_ref[i, rows, :] for i in range(items)], 0).astype(BF16)
        for g in range(end // width):

            @pl.when(group == g)
            def _():
                message_ref[:, g * width : (g + 1) * width] = block
                if g == 0:
                    message_ref[:, end:] = mark
                else:
                    message_ref[:, end:] = message_ref[:, end:] + mark


def merge_kernel(*refs, chunks, frames, items, head_size, heads):
    message_refs = refs[: chunks * frames]
    base_ref, weight_ref, gain_ref, bias_ref = refs[chunks * frames : chunks * frames + 4]
    merged_ref, mid_ref, ffn_ref, log_ref, entropy_ref = refs[chunks * frames + 4 :]
    own, columns = message_refs[0].shape
    half = columns - LANES
    lane, column = iota((LANES, 3 * LANES), 0), iota((LANES, 3 * LANES), 1)
    gather = jnp.logical_and(
        jnp.logical_and(lane // heads // 3 == column // LANES, lane % heads == column % LANES),
        lane < 9 * heads,
    ).astype(BF16)
    expand = head_expand(half, head_size)
    live = iota((own, LANES), 1) < heads
    spread = jnp.zeros((own, LANES), F32)
    for c in range(chunks):
        sources = message_refs[c * frames : (c + 1) * frames]
        stats = [matmul(x[:, half:], gather) for x in sources]
        tops = [x[:, :LANES] for x in stats]
        peak = functools.reduce(jnp.maximum, tops)
        factors = [jnp.exp(t - peak) for t in tops]
        whole = sum(f * x[:, LANES : 2 * LANES] for f, x in zip(factors, stats))
        moment = sum(f * x[:, 2 * LANES :] for f, x in zip(factors, stats))
        whole = jnp.where(live, whole, 1.0)
        log_total = jnp.where(live, peak + jnp.log(whole), 0.0)
        log_ref[c] = log_total
        spread = spread + jnp.where(live, log_total - moment / whole, 0.0)
        merged = jnp.zeros((own, half), F32)
        for x, factor in zip(sources, factors):
            share = jnp.where(live, factor / whole, 0.0)
            wide = jnp.dot(share, expand, precision=HIGHEST, preferred_element_type=F32)
            merged = merged + x[:, :half].astype(F32) * wide
        merged_ref[:, c * half : (c + 1) * half] = merged
    entropy_ref[...] = jnp.broadcast_to(
        jnp.sum(spread, axis=1, keepdims=True) * (1.0 / HEADS), entropy_ref.shape
    )
    base = jnp.concatenate([base_ref[...]] * items, 0)
    mid = base + matmul(merged_ref[...].astype(BF16), weight_ref[...])
    mid_ref[...] = mid
    ffn_ref[...] = layer_norm(mid, gain_ref[...], bias_ref[...]).astype(BF16)


def gelu_parts(x):
    share = 0.5 * (1.0 + lax.erf(x * (0.5**0.5)))
    slope = share + x * jnp.exp(-0.5 * x * x) * ((2.0 * jnp.pi) ** -0.5)
    return x * share, slope


def feed_kernel(flag_ref, *refs, devices, items):
    row_refs = refs[:devices]
    low_ref, up_ref, down_ref, result_ref = refs[devices : devices + 4]
    grad_refs, (plane_ref, plane_low_ref) = refs[devices + 4 : -2], refs[-2:]
    own, width = row_refs[0].shape
    shard = low_ref.shape[0] // devices
    unit, piece = pack_shape(own, shard, width)
    me = flag_ref[2 * items + 2]
    for d in range(devices):
        plane_ref[d * own : (d + 1) * own, :] = row_refs[d][...]
        source = jnp.bitwise_xor(me, d) * shard
        for a in range(own // unit):
            rows = slice(d * own + a * unit, d * own + (a + 1) * unit)
            for b in range(shard // unit):
                start = pl.multiple_of(source + b * unit, unit)
                plane_low_ref[rows, b * piece : (b + 1) * piece] = low_ref[
                    pl.ds(start, unit), a * piece : (a + 1) * piece
                ]
    upward = matmul(plane_ref[...], up_ref[...])
    hidden, slope = gelu_parts(upward)
    grad_up = (slope * transposed_right(plane_low_ref[...], down_ref[...])).astype(BF16)
    grad = transposed_right(grad_up, up_ref[...]).astype(BF16)
    result = matmul(hidden.astype(BF16), down_ref[...]).astype(BF16)
    for d in range(devices):
        grad_refs[d][...] = grad[d * own : (d + 1) * own, :]
        result_ref[jnp.bitwise_xor(me, d)] = result[d * own : (d + 1) * own, :]


def feed_back_kernel(row_ref, low_ref, up_ref, down_ref, hidden_ref, grad_ref):
    hidden, slope = gelu_parts(matmul(row_ref[...], up_ref[...]))
    hidden_ref[...] = hidden.astype(BF16)
    grad_ref[...] = (slope * transposed_right(low_ref[...], down_ref[...])).astype(BF16)


def outer_kernel(left_ref, right_ref, out_ref):
    out_ref[...] = transposed_left(left_ref[...], right_ref[...]).astype(out_ref.dtype)


def norm_backward(rows, gain, gradient):
    center = rows - jnp.mean(rows, axis=1, keepdims=True)
    rate = lax.rsqrt(jnp.mean(center * center, axis=1, keepdims=True) + EPSILON)
    unit = center * rate
    scaled = gradient * gain
    inner = scaled - jnp.mean(scaled, axis=1, keepdims=True)
    back = rate * (inner - unit * jnp.mean(scaled * unit, axis=1, keepdims=True))
    return (
        back,
        jnp.sum(gradient * unit, axis=0, keepdims=True),
        jnp.sum(gradient, axis=0, keepdims=True),
    )


def turn_kernel(*refs, devices, items, chunks, head_size, heads):
    part_refs = refs[:devices]
    mid_ref, cotangent_ref, gain_ref, merged_ref, log_ref, weight_ref = refs[
        devices : devices + 6
    ]
    message_ref, branch_ref, base_ref, sums_ref = refs[devices + 6 :]
    own, width = mid_ref.shape
    half = width // chunks
    gradient = total_of([x[...] for x in part_refs])
    back, gain_sum, bias_sum = norm_backward(mid_ref[...], gain_ref[...], gradient)
    grad_mid = cotangent_ref[...] + back
    sums_ref[...] = jnp.zeros(sums_ref.shape, F32)
    sums_ref[0:1, :] = gain_sum
    sums_ref[1:2, :] = bias_sum
    row_total = own // items
    base_ref[...] = total_of(
        [grad_mid[i * row_total : (i + 1) * row_total] for i in range(items)]
    )
    branch = grad_mid.astype(BF16)
    branch_ref[:, :width] = branch
    branch_ref[:, width:] = merged_ref[...].astype(BF16)
    grad_att = transposed_right(branch, weight_ref[...]).astype(BF16)
    expand = head_expand(half, head_size)
    lane, column = iota((6 * LANES, LANES), 0), iota((6 * LANES, LANES), 1)
    place = jnp.logical_and(
        lane % LANES < heads, column == (lane // LANES) * heads + lane % LANES
    ).astype(BF16)
    message_ref[:, :width] = grad_att
    for c in range(chunks):
        columns = slice(c * half, (c + 1) * half)
        delta = lax.dot_general(
            merged_ref[:, columns] * grad_att[:, columns].astype(F32),
            expand,
            (((1,), (1,)), ((), ())),
            precision=HIGHEST,
            preferred_element_type=F32,
        )
        terms = jnp.concatenate([t for x in (log_ref[c], delta) for t in split_terms(x)], 1)
        message_ref[:, width + c * LANES : width + (c + 1) * LANES] = matmul(
            terms, place
        ).astype(BF16)


def backward_kernel(
    *refs, frames, items, patches, scale, head_size, heads,
):
    flag_ref, both_ref, query_ref, top_ref = refs[:4]
    grad_refs = refs[4 : 4 + frames]
    mark_refs = refs[4 + frames : 4 + 2 * frames]
    out_ref, sum_ref, held_ref, note_ref = refs[4 + 2 * frames :]
    lats, width = query_ref.shape
    own = grad_refs[0].shape[0]
    row_total = own // items
    base = items * patches
    for s in range(frames):
        source = lax.rem(flag_ref[items + 1] + (frames - s), frames)
        rows = pl.ds(pl.multiple_of(source * row_total, row_total), row_total)
        block = grad_refs[s][...].astype(F32)
        mark = mark_refs[s][...].astype(F32)
        for i in range(items):
            held_ref[i, rows, :] = block[i * row_total : (i + 1) * row_total]
            note_ref[i, rows, :] = mark[i * row_total : (i + 1) * row_total]
    masks = head_masks(lats, width, head_size)
    queries = spread_heads(query_ref[...].astype(F32), masks).astype(BF16)
    lat_both = both_ref[base : base + lats, :]
    row, lane = iota((GROUP * 8, LANES), 0), iota((GROUP * 8, LANES), 1)
    pick = jnp.logical_and(
        jnp.logical_and(
            lane // heads // 3 == row % 8,
            lane % heads == pl.program_id(0) * GROUP + row // 8,
        ),
        lane < 6 * heads,
    ).astype(BF16)
    grad_query = jnp.zeros((queries.shape[0], width), F32)
    lat_grad_key = jnp.zeros((lats, width), F32)
    lat_grad_value = jnp.zeros((lats, width), F32)
    for i in range(items):
        rows = slice(i * patches, (i + 1) * patches)
        stats = transposed_right(pick, note_ref[i].astype(BF16))
        stats = jnp.concatenate([stats[h * 8 : (h + 1) * 8] for h in range(GROUP)], 1)
        log_total = stats[0:1]
        delta = stats[1:2]
        top = top_ref[0, i, 0:1, :]
        rescale = jnp.exp(top - log_total)
        both = jnp.concatenate([both_ref[rows, :], lat_both], 0)
        keys, values = both[:, :width], both[:, width:]
        grads = spread_heads(held_ref[i], masks).astype(BF16)
        live = live_rows(flag_ref, i, items, patches, lats, queries.shape[0])
        masked = jnp.where(live, scale * transposed_right(keys, queries), MASKED)
        probs = jnp.where(live, jnp.exp(masked - log_total), 0.0)
        block_exp = jnp.where(live, jnp.exp(masked - top), 0.0)
        weights = (block_exp.astype(BF16).astype(F32) * rescale).astype(BF16)
        grad_scores = (probs * (transposed_right(values, grads) - delta)).astype(BF16)
        grad_key = scale * matmul(grad_scores, queries)
        grad_value = matmul(weights, grads)
        out_ref[rows, :width] = grad_key[:patches].astype(BF16)
        out_ref[rows, width:] = grad_value[:patches].astype(BF16)
        grad_query = grad_query + transposed_left(grad_scores, keys)
        lat_grad_key = lat_grad_key + grad_key[patches:]
        lat_grad_value = lat_grad_value + grad_value[patches:]
    out_ref[base : base + lats, :width] = lat_grad_key.astype(BF16)
    out_ref[base : base + lats, width:] = lat_grad_value.astype(BF16)
    sum_ref[...] = scale * collect_heads(grad_query, masks)


def media_kernel(flag_ref, *refs, chunks, items, frames):
    grad_refs, lat_refs, weight_refs = [
        refs[k * chunks : (k + 1) * chunks] for k in range(3)
    ]
    media_ref, time_ref, gain_ref, out_ref, sums_ref, product_ref = refs[3 * chunks :]
    item = pl.program_id(0)

    @pl.when(item == 0)
    def _():
        sums_ref[...] = jnp.zeros(sums_ref.shape, F32)
        product_ref[...] = functools.reduce(
            jnp.add, [transposed_right(g[...], w[...]) for g, w in zip(lat_refs, weight_refs)]
        )

    gradient = functools.reduce(
        jnp.add, [transposed_right(g[...], w[...]) for g, w in zip(grad_refs, weight_refs)]
    )
    inputs = media_ref[...].astype(F32) + time_ref[pl.ds(item, 1), :]
    back, gain_sum, bias_sum = norm_backward(inputs, gain_ref[...], gradient)
    out_ref[...] = back.astype(BF16)
    place = iota((frames, 1), 0) == flag_ref[items + 2 + item]
    sums_ref[0:frames, :] += jnp.where(place, jnp.sum(back, axis=0, keepdims=True), 0.0)
    sums_ref[8:9, :] += gain_sum
    sums_ref[9:10, :] += bias_sum


def latent_kernel(flag_ref, *refs, chunks, items):
    query_refs = refs[:chunks]
    (
        product_ref, query_weight_ref, latent_ref, gain_ref, base_ref, ffn_ref, media_ref, out_ref,
    ) = refs[chunks:]
    lats, width = latent_ref.shape
    half = width // chunks
    gradient = product_ref[...]
    for c in range(chunks):
        gradient = gradient + transposed_right(
            query_refs[c][...].astype(BF16), query_weight_ref[:, c * half : (c + 1) * half]
        )
        out_ref[lats : 2 * lats, c * half : (c + 1) * half] = query_refs[c][...]
    back, gain_sum, bias_sum = norm_backward(latent_ref[...], gain_ref[...], gradient)
    out_ref[:lats, :] = back
    row_total = base_ref.shape[0]
    start = pl.multiple_of(flag_ref[items + 1] * row_total, row_total)
    out_ref[pl.ds(start, row_total), :] += base_ref[...]
    at = 2 * lats
    out_ref[at : at + 8, :] = ffn_ref[...]
    out_ref[at + 2 : at + 3, :] = gain_sum
    out_ref[at + 3 : at + 4, :] = bias_sum
    out_ref[at + 8 : at + 24, :] = media_ref[...]
    out_ref[at + 24 :, :] = jnp.zeros((out_ref.shape[0] - at - 24, width), F32)


def rows_kernel(flag_ref, *refs, counts, frames, items):
    part_refs, out_refs, held_ref = refs[: sum(counts)], refs[sum(counts) : -1], refs[-1]
    rows = held_ref.shape[1]
    first = column = 0
    for count in counts:
        total = total_of([x[...] for x in part_refs[first : first + count]])
        for f in range(frames):
            held_ref[f, :, column : column + total.shape[1]] = total[f * rows : (f + 1) * rows]
        first += count
        column += total.shape[1]
    for s, out_ref in enumerate(out_refs):
        block = held_ref[lax.rem(flag_ref[items + 1] + s, frames)]
        out_ref[...] = block.astype(out_ref.dtype)


def place_kernel(flag_ref, *refs, chunks, frames, items, groups):
    chunk_refs = refs[: chunks * frames]
    key_ref, value_ref, out_ref = refs[chunks * frames :]
    width = key_ref.shape[2] // (chunks * groups)
    for s in range(frames):
        source = lax.rem(flag_ref[items + 1] + (frames - s), frames)
        out_ref[source] = chunk_refs[s][:, 2 * groups * width :].astype(F32)
        for c in range(chunks):
            for g in range(groups):
                at = (c * groups + g) * width
                block = chunk_refs[c * frames + s][:, 2 * g * width : 2 * (g + 1) * width]
                block = block.astype(F32)
                key_ref[source, :, at : at + width] = block[:, :width]
                value_ref[source, :, at : at + width] = block[:, width:]


def body(
    media,
    cotangent,
    frame_count,
    frame_start,
    latents,
    time_embed,
    media_gain,
    media_bias,
    latent_gain,
    latent_bias,
    ffn_gain,
    ffn_bias,
    query_weight,
    key_weight,
    value_weight,
    out_weight,
    up_weight,
    down_weight,
):
    items = media.shape[0]
    patches = media.shape[2]
    width = media.shape[3]
    lats = latents.shape[0]
    frame_total = time_embed.shape[0]
    row_total = cotangent.shape[1]
    own = items * row_total
    head_size = width // HEADS
    half = width // CHUNKS
    chunk_heads = HEADS // CHUNKS
    group_width = GROUP * head_size
    groups = chunk_heads // GROUP
    stack = GROUP * lats
    tokens = items * patches
    all_tokens = tokens + lats
    shard = query_weight.shape[0]
    hidden_shard = down_weight.shape[0]
    item_size = lax.axis_size("items")
    frame_size = lax.axis_size("frames")
    plane = item_size * own
    item_index = lax.axis_index("items")
    slot = lax.axis_index("frames")
    row_base = slot * row_total
    params = pltpu.CompilerParams(vmem_limit_bytes=56 * 2**20)
    smem = pl.BlockSpec(memory_space=pltpu.SMEM)
    whole = pl.BlockSpec(memory_space=pltpu.VMEM)
    sizes = dict(items=items, head_size=head_size, heads=chunk_heads)

    def struct(shape, kind):
        return jax.ShapeDtypeStruct(shape, kind)

    short = pl.CostEstimate(flops=1000, bytes_accessed=1000, transcendentals=0)

    def column_blocks(x):
        return jnp.transpose(x.reshape(-1, item_size, shard), (1, 0, 2))

    def scatter_exchange(x, axis):
        return jnp.sum(lax.all_to_all(x, axis, 0, 0).astype(F32), axis=0)

    grad_out = cotangent.reshape(own, width)
    low_columns = own * width // shard
    joined, grad_low = pl.pallas_call(
        functools.partial(join_kernel, width=group_width),
        out_shape=[struct((shard, 2 * width + low_columns), BF16), struct((own, width), BF16)],
        cost_estimate=short,
        compiler_params=params,
    )(key_weight, value_weight, grad_out)
    kv_full = lax.all_gather(joined, "items", axis=0, tiled=True)
    up_slice = lax.all_to_all(after(up_weight, joined), "items", 1, 0, tiled=True)

    lat_norm = layer_norm(latents, latent_gain, latent_bias).astype(BF16)
    lat_cols = lax.dynamic_slice_in_dim(lat_norm, item_index * shard, shard, 1)
    query_blocks = column_blocks(matmul(lat_cols, query_weight))
    query_cols = scatter_exchange(after(query_blocks, up_slice), "items").astype(BF16)
    query_spread = jnp.broadcast_to(query_cols[None], (item_size, lats, shard))
    queries = jnp.transpose(lax.all_to_all(query_spread, "items", 0, 0), (1, 0, 2)).reshape(
        lats, width
    )

    counts = lax.dynamic_slice_in_dim(frame_count, item_index * items, items)
    starts = lax.dynamic_slice_in_dim(frame_start, item_index * items, items)
    offset = (slot - starts) % frame_total
    flags = jnp.concatenate(
        [
            (offset < counts).astype(jnp.int32),
            (slot == 0).astype(jnp.int32)[None],
            slot.astype(jnp.int32)[None],
            offset.astype(jnp.int32),
            item_index.astype(jnp.int32)[None],
        ]
    )
    picker = (offset[:, None] == jnp.arange(frame_total, dtype=jnp.int32)[None, :]).astype(F32)
    time_rows = jnp.dot(picker, time_embed, precision=HIGHEST, preferred_element_type=F32)
    flat_media = media.reshape(tokens, width)
    steps = tokens // lats
    all_rows = pl.pallas_call(
        functools.partial(norm_kernel, steps=steps, per_item=patches // lats),
        grid=(steps + 1,),
        in_specs=[
            pl.BlockSpec((lats, width), lambda i: (jnp.minimum(i, steps - 1), 0)),
            whole,
            whole,
            whole,
            whole,
        ],
        out_specs=pl.BlockSpec((lats, width), lambda i: (i, 0)),
        out_shape=struct((all_tokens, width), BF16),
        cost_estimate=short,
        compiler_params=params,
    )(
        after(flat_media, query_blocks),
        time_rows,
        media_gain[None],
        media_bias[None],
        lat_norm,
    )
    out_full = lax.all_gather(after(out_weight, all_rows), "items", axis=0, tiled=True)

    chip, core = item_index // 2, item_index % 2
    rows_across = after(all_rows, query_cols).T.reshape(item_size // 2, 2, shard, all_tokens)
    send_rows, keep_rows = [
        jnp.concatenate(
            [
                lax.dynamic_slice(
                    rows_across, (chip ^ k, which, 0, 0), (1, 1, shard, all_tokens)
                ).reshape(shard, all_tokens)
                for k in range(item_size // 2)
            ],
            0,
        )
        for which in (1 - core, core)
    ]
    low_shift = jnp.stack(spread_on(after(grad_low, all_rows), "frames"))
    low_frames = jnp.stack(
        [
            lax.dynamic_index_in_dim(low_shift, (slot + frame_size - f) % frame_size, 0, False)
            for f in range(frame_size)
        ]
    )

    boths, tops, messages = [], [], []
    for c in range(CHUNKS):

        def block_of(g, c=c):
            return (0, c * groups + g)

        if c:
            rows = after(all_rows, tops[-1])
        else:
            rows = after(all_rows, queries, send_rows, keep_rows, low_frames)
        both = matmul(rows, kv_full[:, 2 * c * half : 2 * (c + 1) * half]).astype(BF16)
        top, *parts = pl.pallas_call(
            functools.partial(
                forward_kernel, patches=patches, scale=head_size**-0.5, **sizes
            ),
            grid=(groups,),
            in_specs=[
                smem,
                pl.BlockSpec((all_tokens, 2 * group_width), lambda g: (0, g)),
                pl.BlockSpec((lats, group_width), block_of),
            ],
            out_specs=[pl.BlockSpec((1, items, 8, stack), lambda g: (g, 0, 0, 0))]
            + [pl.BlockSpec((own, half + LANES), lambda g: (0, 0))] * frame_size,
            out_shape=[struct((groups, items, 8, stack), F32)]
            + [struct((own, half + LANES), BF16)] * frame_size,
            scratch_shapes=[
                pltpu.VMEM((items, lats, group_width), F32),
                pltpu.VMEM((items, lats, LANES), F32),
            ],
            cost_estimate=short,
            compiler_params=params,
        )(flags, both, queries)
        boths.append(both)
        tops.append(top)
        messages += [p if s == 0 else send_on(p, "frames", s) for s, p in enumerate(parts)]
    low_all = lax.all_gather(after(low_frames, tops[1]), "items", axis=0).reshape(-1, width)

    base_rows = lax.dynamic_slice_in_dim(latents, row_base, row_total, 0)
    merged, mid_rows, ffn_in, logs, entropy_wide = pl.pallas_call(
        functools.partial(merge_kernel, chunks=CHUNKS, frames=frame_size, **sizes),
        out_shape=[
            struct((own, width), F32),
            struct((own, width), F32),
            struct((own, width), BF16),
            struct((CHUNKS, own, LANES), F32),
            struct((own, LANES), F32),
        ],
        cost_estimate=short,
        compiler_params=params,
    )(*messages, base_rows, out_full, ffn_gain[None], ffn_bias[None])
    entropy = entropy_wide[:, 0].reshape(items, row_total)

    ffn_frames = lax.all_gather(after(ffn_in, low_all), "frames", axis=0)
    ffn_blocks = spread_across(ffn_in, "items")
    result_part, *parts = pl.pallas_call(
        functools.partial(feed_kernel, devices=item_size, items=items),
        grid=(1,),
        in_specs=[smem]
        + [whole] * item_size
        + [
            pl.BlockSpec((width, low_columns), lambda i: (0, 2 * width // low_columns)),
            whole,
            whole,
        ],
        out_specs=[whole] * (1 + item_size),
        out_shape=[struct((item_size, own, width), BF16)]
        + [struct((own, width), BF16)] * item_size,
        scratch_shapes=[pltpu.VMEM((plane, width), BF16)] * 2,
        cost_estimate=short,
        compiler_params=params,
    )(flags, *ffn_blocks, kv_full, up_slice, down_weight)
    grad_blocks = collect_across(parts, "items")

    turn, grad_branch, grad_base, ffn_sums = pl.pallas_call(
        functools.partial(turn_kernel, devices=item_size, chunks=CHUNKS, **sizes),
        out_shape=[
            struct((own, width + CHUNKS * LANES), BF16),
            struct((own, 2 * width), BF16),
            struct((row_total, width), F32),
            struct((8, width), F32),
        ],
        cost_estimate=short,
        compiler_params=params,
    )(*grad_blocks, mid_rows, grad_out, ffn_gain[None], merged, logs, out_full)
    turns = spread_on(turn, "frames")
    ffn_all = lax.all_gather(after(ffn_frames, turn), "items", axis=0).reshape(-1, width)
    branch_plane = lax.all_gather(after(grad_branch, ffn_frames), "items", axis=0, tiled=True)
    query_full = lax.all_gather(after(query_weight, grad_branch), "items", axis=0, tiled=True)
    att_plane = lax.dynamic_slice_in_dim(
        branch_plane, width + item_index * shard, shard, 1
    )
    result_pieces = lax.all_to_all(after(result_part, turns[-1]), "items", 0, 0)
    turns[0] = after(turns[0], low_all, ffn_frames)

    chunk_grads, chunk_queries = [], []

    def weight_terms(c):
        send = matmul(send_rows, chunk_grads[c]).astype(BF16)
        received = send_across(send, "items", 1).reshape(-1, shard, 2 * half)
        keep = matmul(after(keep_rows, send), chunk_grads[c]).astype(BF16)
        return send, keep.reshape(-1, shard, 2 * half), received

    def chip_pieces(keep, received):
        sums = [keep[k].astype(F32) + received[k].astype(F32) for k in range(item_size // 2)]
        return sums[:1] + [p.astype(BF16) for p in sums[1:]]

    def send_pieces(sums):
        return sums[:1] + [
            send_across(p, "items", 2 * k) for k, p in enumerate(sums) if k
        ]

    def frame_rows(ranges):
        rows = shard // frame_size
        columns = sum(parts[0].shape[1] for parts in ranges)
        return pl.pallas_call(
            functools.partial(
                rows_kernel,
                counts=tuple(len(parts) for parts in ranges),
                frames=frame_size,
                items=items,
            ),
            in_specs=[smem] + [whole] * sum(len(parts) for parts in ranges),
            out_specs=[whole] * frame_size,
            out_shape=[struct((rows, columns), F32)]
            + [struct((rows, columns), BF16)] * (frame_size - 1),
            scratch_shapes=[pltpu.VMEM((frame_size, rows, columns), F32)],
            cost_estimate=short,
            compiler_params=params,
        )(flags, *[part for parts in ranges for part in parts])

    def send_rows_on(rows):
        return [rows[0]] + [send_on(p, "frames", s) for s, p in enumerate(rows) if s]

    for c in range(CHUNKS):

        def block_of(g, c=c):
            return (0, c * groups + g)

        chunk_grad, chunk_query = pl.pallas_call(
            functools.partial(
                backward_kernel, frames=frame_size, patches=patches, scale=head_size**-0.5, **sizes
            ),
            grid=(groups,),
            in_specs=[
                smem,
                pl.BlockSpec((all_tokens, 2 * group_width), lambda g: (0, g)),
                pl.BlockSpec((lats, group_width), block_of),
                pl.BlockSpec((1, items, 8, stack), lambda g: (g, 0, 0, 0)),
            ]
            + [pl.BlockSpec((own, group_width), block_of)] * frame_size
            + [pl.BlockSpec((own, LANES), lambda g, c=c: (0, width // LANES + c))] * frame_size,
            out_specs=[
                pl.BlockSpec((all_tokens, 2 * group_width), lambda g: (0, g)),
                pl.BlockSpec((lats, group_width), lambda g: (0, g)),
            ],
            out_shape=[
                struct((all_tokens, 2 * half), BF16),
                struct((lats, half), F32),
            ],
            scratch_shapes=[
                pltpu.VMEM((items, lats, group_width), F32),
                pltpu.VMEM((items, lats, LANES), F32),
            ],
            cost_estimate=short,
            compiler_params=params,
        )(flags, after(boths[c], *held) if c else boths[c], queries, tops[c], *turns, *turns)
        chunk_grads.append(chunk_grad)
        chunk_queries.append(chunk_query)
        if c == 0:
            first_send, first_keep, first_received = weight_terms(0)
            held = (first_send,)
    pieces = [chip_pieces(after(first_keep, chunk_grads[-1]), first_received)]
    kv_sums = [send_pieces(pieces[0])]
    last_grad = chunk_grads[-1]
    chunk_grads[-1] = after(last_grad, *pieces[0])
    last_send, last_keep, last_received = weight_terms(CHUNKS - 1)
    pieces.append(chip_pieces(last_keep, last_received))
    kv_sums.append(send_pieces(pieces[-1]))
    chunk_grads[-1] = last_grad
    out_part = transposed_left(att_plane, after(branch_plane, last_send)[:, :width])

    last_block = pl.BlockSpec((lats, 2 * half), lambda i: (tokens // lats, 0))
    media_grad, media_sums, lat_product = pl.pallas_call(
        functools.partial(media_kernel, chunks=CHUNKS, items=items, frames=frame_total),
        grid=(items,),
        in_specs=[smem]
        + [pl.BlockSpec((patches, 2 * half), lambda i: (i, 0))] * CHUNKS
        + [last_block] * CHUNKS
        + [pl.BlockSpec((width, 2 * half), lambda i, c=c: (0, c)) for c in range(CHUNKS)]
        + [pl.BlockSpec((patches, width), lambda i: (i, 0)), whole, whole],
        out_specs=[
            pl.BlockSpec((patches, width), lambda i: (i, 0)),
            pl.BlockSpec((16, width), lambda i: (0, 0)),
            pl.BlockSpec((lats, width), lambda i: (0, 0)),
        ],
        out_shape=[
            struct((tokens, width), BF16),
            struct((16, width), F32),
            struct((lats, width), F32),
        ],
        cost_estimate=short,
        compiler_params=params,
    )(
        flags,
        *chunk_grads[:-1],
        after(chunk_grads[-1], *pieces[-1], out_part),
        *chunk_grads,
        *[kv_full] * CHUNKS,
        flat_media,
        time_rows,
        media_gain[None],
    )

    sum_rows = 2 * lats + 24
    sum_rows += -sum_rows % (8 * item_size)
    payload = pl.pallas_call(
        functools.partial(latent_kernel, chunks=CHUNKS, items=items),
        in_specs=[smem] + [whole] * (CHUNKS + 7),
        out_specs=whole,
        out_shape=struct((sum_rows, width), F32),
        cost_estimate=short,
        compiler_params=params,
    )(
        flags,
        *chunk_queries,
        after(lat_product, result_pieces, *kv_sums[0]),
        query_full,
        latents,
        latent_gain[None],
        grad_base,
        ffn_sums,
        media_sums,
    )
    payload_part = lax.psum_scatter(payload, "items", scatter_dimension=0, tiled=True)

    first_rows = frame_rows([[after(kv_sums[0][0], payload), *kv_sums[0][1:]], [out_part]])
    first_moved = send_rows_on(first_rows)
    all_plane = plane * frame_size
    block_rows = min(512, all_plane)
    row_block = pl.BlockSpec((block_rows, width), lambda i: (i, 0))
    hidden_block = pl.BlockSpec((block_rows, hidden_shard), lambda i: (i, 0))
    hidden, grad_up = pl.pallas_call(
        feed_back_kernel,
        grid=(all_plane // block_rows,),
        in_specs=[row_block, row_block, whole, whole],
        out_specs=[hidden_block, hidden_block],
        out_shape=[struct((all_plane, hidden_shard), BF16)] * 2,
        cost_estimate=short,
        compiler_params=params,
    )(after(ffn_all, *first_rows, *kv_sums[-1]), low_all, up_slice, down_weight)

    def outer(left, right, tile, kind):
        rows, columns = left.shape
        shape = (columns, right.shape[1])
        return pl.pallas_call(
            outer_kernel,
            grid=(columns // tile,),
            in_specs=[pl.BlockSpec((rows, tile), lambda i: (0, i)), whole],
            out_specs=pl.BlockSpec((tile, shape[1]), lambda i: (i, 0)),
            out_shape=struct(shape, kind),
            cost_estimate=short,
            compiler_params=params,
        )(left, right)

    last_rows = frame_rows([[after(kv_sums[-1][0], hidden), *kv_sums[-1][1:]]])
    last_moved = send_rows_on(last_rows)
    first_total = total_of(first_moved).astype(BF16)
    first_placed = spread_on(first_total, "frames")
    up_part = outer(ffn_all, after(grad_up, first_total, *last_rows), width // 4, BF16)
    up_grad = lax.all_to_all(up_part, "items", 0, 1, tiled=True).astype(F32)
    last_total = total_of(last_moved).astype(BF16)
    last_placed = spread_on(last_total, "frames")
    down_grad = outer(
        after(hidden, up_part, last_total),
        low_all,
        256 if hidden_shard % 256 == 0 else hidden_shard,
        F32,
    )
    placed = first_placed + last_placed
    key_grad, value_grad, out_grad = pl.pallas_call(
        functools.partial(
            place_kernel, chunks=CHUNKS, frames=frame_size, items=items, groups=groups
        ),
        in_specs=[smem] + [whole] * len(placed),
        out_specs=[whole] * 3,
        out_shape=[struct((frame_size, shard // frame_size, width), F32)] * 3,
        cost_estimate=short,
        compiler_params=params,
    )(flags, *placed)

    payload_part = after(payload_part, up_part)
    payload_others = spread_on(payload_part.astype(BF16), "frames")[1:]
    sums = lax.all_gather(
        total_of([payload_part] + payload_others), "items", axis=0, tiled=True
    )
    latents_grad = sums[:lats]
    query_grad = transposed_left(lat_cols, sums[lats : 2 * lats].astype(BF16))
    at = 2 * lats
    column_sums = lax.dynamic_slice_in_dim(
        sums[at + 8 : at + 24], item_index * shard, shard, 1
    )

    result = mid_rows + total_of([result_pieces[d] for d in range(item_size)])
    return (
        result.reshape(items, row_total, width),
        entropy,
        media_grad.reshape(media.shape),
        latents_grad,
        column_sums[:frame_total],
        column_sums[8],
        column_sums[9],
        sums[at + 2],
        sums[at + 3],
        sums[at],
        sums[at + 1],
        query_grad,
        key_grad.reshape(shard, width),
        value_grad.reshape(shard, width),
        out_grad.reshape(shard, width),
        up_grad,
        down_grad,
    )


def solution(mesh):
    return jax.shard_map(
        body,
        mesh=mesh,
        in_specs=(
            P("items", "frames", None, None),
            P("items", "frames", None),
            P(),
            P(),
            P(),
            P(),
            P(),
            P(),
            P(),
            P(),
            P(),
            P(),
            P("items", None),
            P("items", None),
            P("items", None),
            P("items", None),
            P("items", None),
            P("items", None),
        ),
        out_specs=(
            P("items", "frames", None),
            P("items", "frames"),
            P("items", "frames", None, None),
            P(),
            P(None, "items"),
            P("items"),
            P("items"),
            P(),
            P(),
            P(),
            P(),
            P("items", None),
            P("items", None),
            P("items", None),
            P("items", None),
            P("items", None),
            P("items", None),
        ),
        check_vma=False,
    )
```

```python
import functools
import math

import jax
import jax.numpy as jnp
from jax import lax
from jax.experimental import pallas as pl
from jax.experimental.pallas import tpu as pltpu
from jax.sharding import PartitionSpec as P

HEADS = 16
GROUP = 4
CHUNKS = 2
LANES = 128
EPSILON = 1e-05
MASKED = -1e30
F32 = jnp.float32
BF16 = jnp.bfloat16
HIGHEST = lax.Precision.HIGHEST


def layer_norm(inputs, norm_gain, norm_bias):
    center = inputs - jnp.mean(inputs, axis=-1, keepdims=True)
    spread = jnp.mean(center * center, axis=-1, keepdims=True)
    return center * lax.rsqrt(spread + EPSILON) * norm_gain + norm_bias


def matmul(left_side, right_side):
    return jnp.dot(left_side, right_side, preferred_element_type=F32)


def transposed_left(left_side, right_side):
    return lax.dot_general(
        left_side, right_side, (((0,), (0,)), ((), ())), preferred_element_type=F32
    )


def transposed_right(left_side, right_side):
    return lax.dot_general(
        left_side, right_side, (((1,), (1,)), ((), ())), preferred_element_type=F32
    )


def send_on(x, axis, step):
    size = lax.axis_size(axis)
    return lax.ppermute(x, axis, [(i, (i + step) % size) for i in range(size)])


def send_across(x, axis, distance):
    return lax.ppermute(x, axis, [(i, i ^ distance) for i in range(lax.axis_size(axis))])


def spread_on(x, axis):
    return [x] + [send_on(x, axis, s) for s in range(1, lax.axis_size(axis))]


def spread_across(x, axis):
    chips = [x] + [send_across(x, axis, d) for d in range(2, lax.axis_size(axis), 2)]
    return [b for block in chips for b in (block, send_across(block, axis, 1))]


def collect_across(pieces, axis):
    return [pieces[0]] + [send_across(p, axis, d) for d, p in enumerate(pieces) if d]


def total_of(pieces):
    return functools.reduce(jnp.add, [p.astype(F32) for p in pieces])


def after(x, *earlier):
    return lax.optimization_barrier((x,) + earlier)[0]


def split_terms(x):
    high = x.astype(BF16)
    rest = x - high.astype(F32)
    middle = rest.astype(BF16)
    return high, middle, (rest - middle.astype(F32)).astype(BF16)


def iota(shape, dim):
    return lax.broadcasted_iota(jnp.int32, shape, dim)


def head_masks(rows, width, head_size):
    lane = iota((rows, width), 1)
    return [
        jnp.logical_and(lane >= h * head_size, lane < (h + 1) * head_size)
        for h in range(width // head_size)
    ]


def spread_heads(block, masks):
    return jnp.concatenate([jnp.where(m, block, jnp.zeros_like(block)) for m in masks], 0)


def collect_heads(block, masks):
    rows = block.shape[0] // len(masks)
    total = jnp.where(masks[0], block[:rows], 0.0)
    for h in range(1, len(masks)):
        total = total + jnp.where(masks[h], block[h * rows : (h + 1) * rows], 0.0)
    return total


def head_expand(width, head_size):
    row, column = iota((LANES, width), 0), iota((LANES, width), 1)
    return jnp.logical_and(column >= row * head_size, column < (row + 1) * head_size).astype(F32)


def live_rows(flag_ref, item, items, patches, lats, columns):
    row = iota((patches + lats, columns), 0)
    media = jnp.logical_and(row < patches, flag_ref[item] > 0)
    return jnp.logical_or(media, jnp.logical_and(row >= patches, flag_ref[items] > 0))


def pack_shape(own, shard, width):
    unit = math.gcd(own, shard)
    return unit, width * unit // shard


def join_kernel(key_ref, value_ref, cotangent_ref, out_ref, low_ref, *, width):
    for g in range(key_ref.shape[1] // width):
        columns = slice(g * width, (g + 1) * width)
        out_ref[:, 2 * g * width : (2 * g + 1) * width] = key_ref[:, columns]
        out_ref[:, (2 * g + 1) * width : (2 * g + 2) * width] = value_ref[:, columns]
    low = cotangent_ref[...].astype(BF16)
    low_ref[...] = low
    own, span = low.shape
    unit, piece = pack_shape(own, out_ref.shape[0], span)
    for a in range(own // unit):
        for b in range(span // piece):
            at = 2 * span + a * piece
            out_ref[b * unit : (b + 1) * unit, at : at + piece] = low[
                a * unit : (a + 1) * unit, b * piece : (b + 1) * piece
            ]


def norm_kernel(media_ref, time_ref, gain_ref, bias_ref, lat_ref, out_ref, *, steps, per_item):
    step = pl.program_id(0)

    @pl.when(step < steps)
    def _():
        rows = media_ref[...].astype(F32) + time_ref[pl.ds(step // per_item, 1), :]
        out_ref[...] = layer_norm(rows, gain_ref[...], bias_ref[...]).astype(BF16)

    @pl.when(step == steps)
    def _():
        out_ref[...] = lat_ref[...]


def forward_kernel(
    flag_ref, both_ref, query_ref, top_ref, *refs, items, patches, scale, head_size, heads,
):
    message_refs, (part_ref, mark_ref) = refs[:-2], refs[-2:]
    lats, width = query_ref.shape
    frames = len(message_refs)
    own = message_refs[0].shape[0]
    row_total = own // items
    masks = head_masks(lats, width, head_size)
    queries = spread_heads(query_ref[...].astype(F32), masks).astype(BF16)
    base = items * patches
    lat_both = both_ref[base : base + lats, :]
    group = pl.program_id(0)
    term, lane = iota((16, GROUP * LANES), 0), iota((16, GROUP * LANES), 1)
    place = jnp.logical_and(
        lane % LANES == term * heads + group * GROUP + lane // LANES, term < 9
    ).astype(BF16)
    for i in range(items):
        both = jnp.concatenate([both_ref[i * patches : (i + 1) * patches, :], lat_both], 0)
        live = live_rows(flag_ref, i, items, patches, lats, queries.shape[0])
        scores = scale * transposed_right(both[:, :width], queries)
        masked = jnp.where(live, scores, MASKED)
        top = jnp.max(masked, axis=0, keepdims=True)
        block_exp = jnp.where(live, jnp.exp(masked - top), 0.0)
        total = jnp.sum(block_exp, axis=0, keepdims=True)
        moment = jnp.sum(block_exp * scores, axis=0, keepdims=True)
        part = transposed_left(block_exp.astype(BF16), both[:, width:])
        part_ref[i] = collect_heads(part, masks)
        top_ref[0, i] = jnp.broadcast_to(top, top_ref.shape[2:])
        terms = jnp.concatenate(
            [t.astype(F32) for x in (top, total, moment) for t in split_terms(x)]
            + [jnp.zeros((7, top.shape[1]), F32)],
            0,
        ).astype(BF16)
        wide = transposed_left(terms, place)
        mark = wide[:lats, :LANES]
        for h in range(1, GROUP):
            mark = mark + wide[h * lats : (h + 1) * lats, h * LANES : (h + 1) * LANES]
        mark_ref[i] = mark

    end = message_refs[0].shape[1] - LANES
    for s, message_ref in enumerate(message_refs):
        start = pl.multiple_of(lax.rem(flag_ref[items + 1] + s, frames) * row_total, row_total)
        rows = pl.ds(start, row_total)
        block = jnp.concatenate([part_ref[i, rows, :] for i in range(items)], 0).astype(BF16)
        mark = jnp.concatenate([mark_ref[i, rows, :] for i in range(items)], 0).astype(BF16)
        for g in range(end // width):

            @pl.when(group == g)
            def _():
                message_ref[:, g * width : (g + 1) * width] = block
                if g == 0:
                    message_ref[:, end:] = mark
                else:
                    message_ref[:, end:] = message_ref[:, end:] + mark


def merge_kernel(*refs, chunks, frames, items, head_size, heads):
    message_refs = refs[: chunks * frames]
    base_ref, weight_ref, gain_ref, bias_ref = refs[chunks * frames : chunks * frames + 4]
    merged_ref, mid_ref, ffn_ref, log_ref, entropy_ref = refs[chunks * frames + 4 :]
    own, columns = message_refs[0].shape
    half = columns - LANES
    lane, column = iota((LANES, 3 * LANES), 0), iota((LANES, 3 * LANES), 1)
    gather = jnp.logical_and(
        jnp.logical_and(lane // heads // 3 == column // LANES, lane % heads == column % LANES),
        lane < 9 * heads,
    ).astype(BF16)
    expand = head_expand(half, head_size)
    live = iota((own, LANES), 1) < heads
    spread = jnp.zeros((own, LANES), F32)
    for c in range(chunks):
        sources = message_refs[c * frames : (c + 1) * frames]
        stats = [matmul(x[:, half:], gather) for x in sources]
        tops = [x[:, :LANES] for x in stats]
        peak = functools.reduce(jnp.maximum, tops)
        factors = [jnp.exp(t - peak) for t in tops]
        whole = sum(f * x[:, LANES : 2 * LANES] for f, x in zip(factors, stats))
        moment = sum(f * x[:, 2 * LANES :] for f, x in zip(factors, stats))
        whole = jnp.where(live, whole, 1.0)
        log_total = jnp.where(live, peak + jnp.log(whole), 0.0)
        log_ref[c] = log_total
        spread = spread + jnp.where(live, log_total - moment / whole, 0.0)
        merged = jnp.zeros((own, half), F32)
        for x, factor in zip(sources, factors):
            share = jnp.where(live, factor / whole, 0.0)
            wide = jnp.dot(share, expand, precision=HIGHEST, preferred_element_type=F32)
            merged = merged + x[:, :half].astype(F32) * wide
        merged_ref[:, c * half : (c + 1) * half] = merged
    entropy_ref[...] = jnp.broadcast_to(
        jnp.sum(spread, axis=1, keepdims=True) * (1.0 / HEADS), entropy_ref.shape
    )
    base = jnp.concatenate([base_ref[...]] * items, 0)
    mid = base + matmul(merged_ref[...].astype(BF16), weight_ref[...])
    mid_ref[...] = mid
    ffn_ref[...] = layer_norm(mid, gain_ref[...], bias_ref[...]).astype(BF16)


def gelu_parts(x):
    share = 0.5 * (1.0 + lax.erf(x * (0.5**0.5)))
    slope = share + x * jnp.exp(-0.5 * x * x) * ((2.0 * jnp.pi) ** -0.5)
    return x * share, slope


def feed_kernel(flag_ref, *refs, devices, items):
    row_refs = refs[:devices]
    low_ref, up_ref, down_ref, result_ref = refs[devices : devices + 4]
    grad_refs, (plane_ref, plane_low_ref) = refs[devices + 4 : -2], refs[-2:]
    own, width = row_refs[0].shape
    shard = low_ref.shape[0] // devices
    unit, piece = pack_shape(own, shard, width)
    me = flag_ref[2 * items + 2]
    for d in range(devices):
        plane_ref[d * own : (d + 1) * own, :] = row_refs[d][...]
        source = jnp.bitwise_xor(me, d) * shard
        for a in range(own // unit):
            rows = slice(d * own + a * unit, d * own + (a + 1) * unit)
            for b in range(shard // unit):
                start = pl.multiple_of(source + b * unit, unit)
                plane_low_ref[rows, b * piece : (b + 1) * piece] = low_ref[
                    pl.ds(start, unit), a * piece : (a + 1) * piece
                ]
    upward = transposed_right(plane_ref[...], up_ref[...])
    hidden, slope = gelu_parts(upward)
    grad_up = (slope * transposed_right(plane_low_ref[...], down_ref[...])).astype(BF16)
    grad = matmul(grad_up, up_ref[...]).astype(BF16)
    result = matmul(hidden.astype(BF16), down_ref[...]).astype(BF16)
    for d in range(devices):
        grad_refs[d][...] = grad[d * own : (d + 1) * own, :]
        result_ref[jnp.bitwise_xor(me, d)] = result[d * own : (d + 1) * own, :]


def feed_back_kernel(row_ref, low_ref, up_ref, down_ref, hidden_ref, grad_ref):
    hidden, slope = gelu_parts(transposed_right(row_ref[...], up_ref[...]))
    hidden_ref[...] = hidden.astype(BF16)
    grad_ref[...] = (slope * transposed_right(low_ref[...], down_ref[...])).astype(BF16)


def outer_kernel(left_ref, right_ref, out_ref):
    out_ref[...] = transposed_left(left_ref[...], right_ref[...]).astype(out_ref.dtype)


def norm_backward(rows, gain, gradient):
    center = rows - jnp.mean(rows, axis=1, keepdims=True)
    rate = lax.rsqrt(jnp.mean(center * center, axis=1, keepdims=True) + EPSILON)
    unit = center * rate
    scaled = gradient * gain
    inner = scaled - jnp.mean(scaled, axis=1, keepdims=True)
    back = rate * (inner - unit * jnp.mean(scaled * unit, axis=1, keepdims=True))
    return (
        back,
        jnp.sum(gradient * unit, axis=0, keepdims=True),
        jnp.sum(gradient, axis=0, keepdims=True),
    )


def turn_kernel(*refs, devices, items, chunks, head_size, heads):
    part_refs = refs[:devices]
    mid_ref, cotangent_ref, gain_ref, merged_ref, log_ref, weight_ref = refs[
        devices : devices + 6
    ]
    message_ref, branch_ref, base_ref, sums_ref = refs[devices + 6 :]
    own, width = mid_ref.shape
    half = width // chunks
    gradient = total_of([x[...] for x in part_refs])
    back, gain_sum, bias_sum = norm_backward(mid_ref[...], gain_ref[...], gradient)
    grad_mid = cotangent_ref[...] + back
    sums_ref[...] = jnp.zeros(sums_ref.shape, F32)
    sums_ref[0:1, :] = gain_sum
    sums_ref[1:2, :] = bias_sum
    row_total = own // items
    base_ref[...] = total_of(
        [grad_mid[i * row_total : (i + 1) * row_total] for i in range(items)]
    )
    branch = grad_mid.astype(BF16)
    branch_ref[:, :width] = branch
    branch_ref[:, width:] = merged_ref[...].astype(BF16)
    grad_att = transposed_right(branch, weight_ref[...]).astype(BF16)
    expand = head_expand(half, head_size)
    lane, column = iota((6 * LANES, LANES), 0), iota((6 * LANES, LANES), 1)
    place = jnp.logical_and(
        lane % LANES < heads, column == (lane // LANES) * heads + lane % LANES
    ).astype(BF16)
    message_ref[:, :width] = grad_att
    for c in range(chunks):
        columns = slice(c * half, (c + 1) * half)
        delta = lax.dot_general(
            merged_ref[:, columns] * grad_att[:, columns].astype(F32),
            expand,
            (((1,), (1,)), ((), ())),
            precision=HIGHEST,
            preferred_element_type=F32,
        )
        terms = jnp.concatenate([t for x in (log_ref[c], delta) for t in split_terms(x)], 1)
        message_ref[:, width + c * LANES : width + (c + 1) * LANES] = matmul(
            terms, place
        ).astype(BF16)


def backward_kernel(
    *refs, frames, items, patches, scale, head_size, heads,
):
    flag_ref, both_ref, query_ref, top_ref = refs[:4]
    grad_refs = refs[4 : 4 + frames]
    mark_refs = refs[4 + frames : 4 + 2 * frames]
    out_ref, sum_ref, held_ref, note_ref = refs[4 + 2 * frames :]
    lats, width = query_ref.shape
    own = grad_refs[0].shape[0]
    row_total = own // items
    base = items * patches
    for s in range(frames):
        source = lax.rem(flag_ref[items + 1] + (frames - s), frames)
        rows = pl.ds(pl.multiple_of(source * row_total, row_total), row_total)
        block = grad_refs[s][...].astype(F32)
        mark = mark_refs[s][...].astype(F32)
        for i in range(items):
            held_ref[i, rows, :] = block[i * row_total : (i + 1) * row_total]
            note_ref[i, rows, :] = mark[i * row_total : (i + 1) * row_total]
    masks = head_masks(lats, width, head_size)
    queries = spread_heads(query_ref[...].astype(F32), masks).astype(BF16)
    lat_both = both_ref[base : base + lats, :]
    row, lane = iota((GROUP * 8, LANES), 0), iota((GROUP * 8, LANES), 1)
    pick = jnp.logical_and(
        jnp.logical_and(
            lane // heads // 3 == row % 8,
            lane % heads == pl.program_id(0) * GROUP + row // 8,
        ),
        lane < 6 * heads,
    ).astype(BF16)
    grad_query = jnp.zeros((queries.shape[0], width), F32)
    lat_grad_key = jnp.zeros((lats, width), F32)
    lat_grad_value = jnp.zeros((lats, width), F32)
    for i in range(items):
        rows = slice(i * patches, (i + 1) * patches)
        stats = transposed_right(pick, note_ref[i].astype(BF16))
        stats = jnp.concatenate([stats[h * 8 : (h + 1) * 8] for h in range(GROUP)], 1)
        log_total = stats[0:1]
        delta = stats[1:2]
        top = top_ref[0, i, 0:1, :]
        rescale = jnp.exp(top - log_total)
        both = jnp.concatenate([both_ref[rows, :], lat_both], 0)
        keys, values = both[:, :width], both[:, width:]
        grads = spread_heads(held_ref[i], masks).astype(BF16)
        live = live_rows(flag_ref, i, items, patches, lats, queries.shape[0])
        masked = jnp.where(live, scale * transposed_right(keys, queries), MASKED)
        probs = jnp.where(live, jnp.exp(masked - log_total), 0.0)
        block_exp = jnp.where(live, jnp.exp(masked - top), 0.0)
        weights = (block_exp.astype(BF16).astype(F32) * rescale).astype(BF16)
        grad_scores = (probs * (transposed_right(values, grads) - delta)).astype(BF16)
        grad_key = scale * matmul(grad_scores, queries)
        grad_value = matmul(weights, grads)
        out_ref[rows, :width] = grad_key[:patches].astype(BF16)
        out_ref[rows, width:] = grad_value[:patches].astype(BF16)
        grad_query = grad_query + transposed_left(grad_scores, keys)
        lat_grad_key = lat_grad_key + grad_key[patches:]
        lat_grad_value = lat_grad_value + grad_value[patches:]
    out_ref[base : base + lats, :width] = lat_grad_key.astype(BF16)
    out_ref[base : base + lats, width:] = lat_grad_value.astype(BF16)
    sum_ref[...] = scale * collect_heads(grad_query, masks)


def media_kernel(flag_ref, *refs, chunks, items, frames):
    grad_refs, lat_refs, weight_refs = [
        refs[k * chunks : (k + 1) * chunks] for k in range(3)
    ]
    media_ref, time_ref, gain_ref, out_ref, sums_ref, product_ref = refs[3 * chunks :]
    item = pl.program_id(0)

    @pl.when(item == 0)
    def _():
        sums_ref[...] = jnp.zeros(sums_ref.shape, F32)
        product_ref[...] = functools.reduce(
            jnp.add, [transposed_right(g[...], w[...]) for g, w in zip(lat_refs, weight_refs)]
        )

    gradient = functools.reduce(
        jnp.add, [transposed_right(g[...], w[...]) for g, w in zip(grad_refs, weight_refs)]
    )
    inputs = media_ref[...].astype(F32) + time_ref[pl.ds(item, 1), :]
    back, gain_sum, bias_sum = norm_backward(inputs, gain_ref[...], gradient)
    out_ref[...] = back.astype(BF16)
    place = iota((frames, 1), 0) == flag_ref[items + 2 + item]
    sums_ref[0:frames, :] += jnp.where(place, jnp.sum(back, axis=0, keepdims=True), 0.0)
    sums_ref[8:9, :] += gain_sum
    sums_ref[9:10, :] += bias_sum


def latent_kernel(flag_ref, *refs, chunks, items):
    query_refs = refs[:chunks]
    (
        product_ref, latent_ref, gain_ref, base_ref, ffn_ref, media_ref, out_ref,
    ) = refs[chunks:]
    lats, width = latent_ref.shape
    half = width // chunks
    gradient = product_ref[...]
    for c in range(chunks):
        out_ref[lats : 2 * lats, c * half : (c + 1) * half] = query_refs[c][...]
    back, gain_sum, bias_sum = norm_backward(latent_ref[...], gain_ref[...], gradient)
    out_ref[:lats, :] = back
    row_total = base_ref.shape[0]
    start = pl.multiple_of(flag_ref[items + 1] * row_total, row_total)
    out_ref[pl.ds(start, row_total), :] += base_ref[...]
    at = 2 * lats
    out_ref[at : at + 8, :] = ffn_ref[...]
    out_ref[at + 2 : at + 3, :] = gain_sum
    out_ref[at + 3 : at + 4, :] = bias_sum
    out_ref[at + 8 : at + 24, :] = media_ref[...]
    out_ref[at + 24 :, :] = jnp.zeros((out_ref.shape[0] - at - 24, width), F32)


def query_norm_kernel(norm_ref, latent_ref, gain_ref, sum_ref, out_ref, out_gain_ref, out_bias_ref):
    back, gain_sum, bias_sum = norm_backward(latent_ref[...], gain_ref[...], norm_ref[...])
    lats = latent_ref.shape[0]
    out_ref[...] = sum_ref[:lats, :] + back
    out_gain_ref[...] = sum_ref[2 * lats + 2 : 2 * lats + 3, :] + gain_sum
    out_bias_ref[...] = sum_ref[2 * lats + 3 : 2 * lats + 4, :] + bias_sum


def rows_kernel(flag_ref, *refs, counts, frames, items):
    part_refs, out_refs, held_ref = refs[: sum(counts)], refs[sum(counts) : -1], refs[-1]
    rows = held_ref.shape[1]
    first = column = 0
    for count in counts:
        total = total_of([x[...] for x in part_refs[first : first + count]])
        for f in range(frames):
            held_ref[f, :, column : column + total.shape[1]] = total[f * rows : (f + 1) * rows]
        first += count
        column += total.shape[1]
    for s, out_ref in enumerate(out_refs):
        block = held_ref[lax.rem(flag_ref[items + 1] + s, frames)]
        out_ref[...] = block.astype(out_ref.dtype)


def place_kernel(flag_ref, *refs, chunks, frames, items, groups):
    chunk_refs = refs[: chunks * frames]
    key_ref, value_ref, out_ref = refs[chunks * frames :]
    width = key_ref.shape[2] // (chunks * groups)
    for s in range(frames):
        source = lax.rem(flag_ref[items + 1] + (frames - s), frames)
        out_ref[source] = chunk_refs[s][:, 2 * groups * width :].astype(F32)
        for c in range(chunks):
            for g in range(groups):
                at = (c * groups + g) * width
                block = chunk_refs[c * frames + s][:, 2 * g * width : 2 * (g + 1) * width]
                block = block.astype(F32)
                key_ref[source, :, at : at + width] = block[:, :width]
                value_ref[source, :, at : at + width] = block[:, width:]


def body(
    media,
    cotangent,
    frame_count,
    frame_start,
    latents,
    time_embed,
    media_gain,
    media_bias,
    latent_gain,
    latent_bias,
    ffn_gain,
    ffn_bias,
    query_weight,
    key_weight,
    value_weight,
    out_weight,
    up_weight,
    down_weight,
):
    items = media.shape[0]
    patches = media.shape[2]
    width = media.shape[3]
    lats = latents.shape[0]
    frame_total = time_embed.shape[0]
    row_total = cotangent.shape[1]
    own = items * row_total
    head_size = width // HEADS
    half = width // CHUNKS
    chunk_heads = HEADS // CHUNKS
    group_width = GROUP * head_size
    groups = chunk_heads // GROUP
    stack = GROUP * lats
    tokens = items * patches
    all_tokens = tokens + lats
    shard = query_weight.shape[0]
    hidden_shard = down_weight.shape[0]
    item_size = lax.axis_size("items")
    frame_size = lax.axis_size("frames")
    plane = item_size * own
    item_index = lax.axis_index("items")
    slot = lax.axis_index("frames")
    row_base = slot * row_total
    params = pltpu.CompilerParams(vmem_limit_bytes=56 * 2**20)
    smem = pl.BlockSpec(memory_space=pltpu.SMEM)
    whole = pl.BlockSpec(memory_space=pltpu.VMEM)
    sizes = dict(items=items, head_size=head_size, heads=chunk_heads)

    def struct(shape, kind):
        return jax.ShapeDtypeStruct(shape, kind)

    short = pl.CostEstimate(flops=1000, bytes_accessed=1000, transcendentals=0)

    def frame_order(x):
        return jnp.stack(
            [
                lax.dynamic_index_in_dim(x, (slot + frame_size - f) % frame_size, 0, False)
                for f in range(frame_size)
            ]
        )

    def column_blocks(x):
        return jnp.transpose(x.reshape(-1, item_size, shard), (1, 0, 2))

    def scatter_exchange(x, axis):
        return jnp.sum(lax.all_to_all(x, axis, 0, 0).astype(F32), axis=0)

    grad_out = cotangent.reshape(own, width)
    low_columns = own * width // shard
    joined, grad_low = pl.pallas_call(
        functools.partial(join_kernel, width=group_width),
        out_shape=[struct((shard, 2 * width + low_columns), BF16), struct((own, width), BF16)],
        cost_estimate=short,
        compiler_params=params,
    )(key_weight, value_weight, grad_out)
    kv_full = lax.all_gather(joined, "items", axis=0, tiled=True)
    hidden_part = hidden_shard // frame_size
    up_mine = lax.dynamic_index_in_dim(
        up_weight.reshape(shard, item_size, frame_size, hidden_part), slot, 2, False
    )
    up_mine = lax.all_to_all(jnp.transpose(up_mine, (1, 2, 0)), "items", 0, 0)
    up_mine = jnp.transpose(up_mine, (1, 0, 2)).reshape(hidden_part, width)
    up_parts = jnp.stack(spread_on(up_mine, "frames"))
    up_rows = frame_order(up_parts).reshape(hidden_shard, width)

    lat_norm = layer_norm(latents, latent_gain, latent_bias).astype(BF16)
    lat_cols = lax.dynamic_slice_in_dim(lat_norm, item_index * shard, shard, 1)
    query_blocks = column_blocks(matmul(lat_cols, query_weight))
    query_cols = scatter_exchange(after(query_blocks, up_mine), "items").astype(BF16)
    query_spread = jnp.broadcast_to(query_cols[None], (item_size, lats, shard))
    queries = jnp.transpose(lax.all_to_all(query_spread, "items", 0, 0), (1, 0, 2)).reshape(
        lats, width
    )

    counts = lax.dynamic_slice_in_dim(frame_count, item_index * items, items)
    starts = lax.dynamic_slice_in_dim(frame_start, item_index * items, items)
    offset = (slot - starts) % frame_total
    flags = jnp.concatenate(
        [
            (offset < counts).astype(jnp.int32),
            (slot == 0).astype(jnp.int32)[None],
            slot.astype(jnp.int32)[None],
            offset.astype(jnp.int32),
            item_index.astype(jnp.int32)[None],
        ]
    )
    picker = (offset[:, None] == jnp.arange(frame_total, dtype=jnp.int32)[None, :]).astype(F32)
    time_rows = jnp.dot(picker, time_embed, precision=HIGHEST, preferred_element_type=F32)
    flat_media = media.reshape(tokens, width)
    steps = tokens // lats
    all_rows = pl.pallas_call(
        functools.partial(norm_kernel, steps=steps, per_item=patches // lats),
        grid=(steps + 1,),
        in_specs=[
            pl.BlockSpec((lats, width), lambda i: (jnp.minimum(i, steps - 1), 0)),
            whole,
            whole,
            whole,
            whole,
        ],
        out_specs=pl.BlockSpec((lats, width), lambda i: (i, 0)),
        out_shape=struct((all_tokens, width), BF16),
        cost_estimate=short,
        compiler_params=params,
    )(
        after(flat_media, query_blocks),
        time_rows,
        media_gain[None],
        media_bias[None],
        lat_norm,
    )
    out_full = lax.all_gather(after(out_weight, all_rows), "items", axis=0, tiled=True)

    chip, core = item_index // 2, item_index % 2
    rows_across = after(all_rows, query_cols).T.reshape(item_size // 2, 2, shard, all_tokens)
    send_rows, keep_rows = [
        jnp.concatenate(
            [
                lax.dynamic_slice(
                    rows_across, (chip ^ k, which, 0, 0), (1, 1, shard, all_tokens)
                ).reshape(shard, all_tokens)
                for k in range(item_size // 2)
            ],
            0,
        )
        for which in (1 - core, core)
    ]
    low_frames = jnp.stack(spread_on(after(grad_low, all_rows), "frames"))

    boths, tops, messages = [], [], []
    for c in range(CHUNKS):

        def block_of(g, c=c):
            return (0, c * groups + g)

        if c:
            rows = after(all_rows, tops[-1])
        else:
            rows = after(all_rows, queries, send_rows, keep_rows, low_frames, up_rows)
        both = matmul(rows, kv_full[:, 2 * c * half : 2 * (c + 1) * half]).astype(BF16)
        top, *parts = pl.pallas_call(
            functools.partial(
                forward_kernel, patches=patches, scale=head_size**-0.5, **sizes
            ),
            grid=(groups,),
            in_specs=[
                smem,
                pl.BlockSpec((all_tokens, 2 * group_width), lambda g: (0, g)),
                pl.BlockSpec((lats, group_width), block_of),
            ],
            out_specs=[pl.BlockSpec((1, items, 8, stack), lambda g: (g, 0, 0, 0))]
            + [pl.BlockSpec((own, half + LANES), lambda g: (0, 0))] * frame_size,
            out_shape=[struct((groups, items, 8, stack), F32)]
            + [struct((own, half + LANES), BF16)] * frame_size,
            scratch_shapes=[
                pltpu.VMEM((items, lats, group_width), F32),
                pltpu.VMEM((items, lats, LANES), F32),
            ],
            cost_estimate=short,
            compiler_params=params,
        )(flags, both, queries)
        boths.append(both)
        tops.append(top)
        messages += [p if s == 0 else send_on(p, "frames", s) for s, p in enumerate(parts)]
    low_all = lax.all_gather(after(low_frames, tops[1]), "items", axis=0).reshape(-1, width)

    base_rows = lax.dynamic_slice_in_dim(latents, row_base, row_total, 0)
    merged, mid_rows, ffn_in, logs, entropy_wide = pl.pallas_call(
        functools.partial(merge_kernel, chunks=CHUNKS, frames=frame_size, **sizes),
        out_shape=[
            struct((own, width), F32),
            struct((own, width), F32),
            struct((own, width), BF16),
            struct((CHUNKS, own, LANES), F32),
            struct((own, LANES), F32),
        ],
        cost_estimate=short,
        compiler_params=params,
    )(*messages, base_rows, out_full, ffn_gain[None], ffn_bias[None])
    entropy = entropy_wide[:, 0].reshape(items, row_total)

    ffn_blocks = spread_across(ffn_in, "items")
    ffn_frames = spread_on(after(ffn_in, *ffn_blocks), "frames")
    result_part, *parts = pl.pallas_call(
        functools.partial(feed_kernel, devices=item_size, items=items),
        grid=(1,),
        in_specs=[smem]
        + [whole] * item_size
        + [
            pl.BlockSpec((width, low_columns), lambda i: (0, 2 * width // low_columns)),
            whole,
            whole,
        ],
        out_specs=[whole] * (1 + item_size),
        out_shape=[struct((item_size, own, width), BF16)]
        + [struct((own, width), BF16)] * item_size,
        scratch_shapes=[pltpu.VMEM((plane, width), BF16)] * 2,
        cost_estimate=short,
        compiler_params=params,
    )(flags, *ffn_blocks, kv_full, up_rows, down_weight)
    grad_blocks = collect_across(parts, "items")
    grad_blocks[0] = after(grad_blocks[0], *ffn_frames)

    turn, grad_branch, grad_base, ffn_sums = pl.pallas_call(
        functools.partial(turn_kernel, devices=item_size, chunks=CHUNKS, **sizes),
        out_shape=[
            struct((own, width + CHUNKS * LANES), BF16),
            struct((own, 2 * width), BF16),
            struct((row_total, width), F32),
            struct((8, width), F32),
        ],
        cost_estimate=short,
        compiler_params=params,
    )(*grad_blocks, mid_rows, grad_out, ffn_gain[None], merged, logs, out_full)
    turns = spread_on(turn, "frames")
    branch_plane = lax.all_gather(grad_branch, "items", axis=0, tiled=True)
    ffn_all = lax.all_gather(
        after(jnp.stack(ffn_frames), grad_branch), "items", axis=0
    ).reshape(-1, width)
    att_plane = lax.dynamic_slice_in_dim(
        branch_plane, width + item_index * shard, shard, 1
    )
    result_pieces = lax.all_to_all(after(result_part, turn), "items", 0, 0)
    turns[0] = after(turns[0], low_all, result_pieces)

    chunk_grads, chunk_queries = [], []

    def weight_terms(c):
        send = matmul(send_rows, chunk_grads[c]).astype(BF16)
        received = send_across(send, "items", 1).reshape(-1, shard, 2 * half)
        keep = matmul(after(keep_rows, send), chunk_grads[c]).astype(BF16)
        return send, keep.reshape(-1, shard, 2 * half), received

    def chip_pieces(keep, received):
        sums = [keep[k].astype(F32) + received[k].astype(F32) for k in range(item_size // 2)]
        return sums[:1] + [p.astype(BF16) for p in sums[1:]]

    def send_pieces(sums):
        return sums[:1] + [
            send_across(p, "items", 2 * k) for k, p in enumerate(sums) if k
        ]

    def frame_rows(ranges):
        rows = shard // frame_size
        columns = sum(parts[0].shape[1] for parts in ranges)
        return pl.pallas_call(
            functools.partial(
                rows_kernel,
                counts=tuple(len(parts) for parts in ranges),
                frames=frame_size,
                items=items,
            ),
            in_specs=[smem] + [whole] * sum(len(parts) for parts in ranges),
            out_specs=[whole] * frame_size,
            out_shape=[struct((rows, columns), F32)]
            + [struct((rows, columns), BF16)] * (frame_size - 1),
            scratch_shapes=[pltpu.VMEM((frame_size, rows, columns), F32)],
            cost_estimate=short,
            compiler_params=params,
        )(flags, *[part for parts in ranges for part in parts])

    def send_rows_on(rows):
        return [rows[0]] + [send_on(p, "frames", s) for s, p in enumerate(rows) if s]

    for c in range(CHUNKS):

        def block_of(g, c=c):
            return (0, c * groups + g)

        chunk_grad, chunk_query = pl.pallas_call(
            functools.partial(
                backward_kernel, frames=frame_size, patches=patches, scale=head_size**-0.5, **sizes
            ),
            grid=(groups,),
            in_specs=[
                smem,
                pl.BlockSpec((all_tokens, 2 * group_width), lambda g: (0, g)),
                pl.BlockSpec((lats, group_width), block_of),
                pl.BlockSpec((1, items, 8, stack), lambda g: (g, 0, 0, 0)),
            ]
            + [pl.BlockSpec((own, group_width), block_of)] * frame_size
            + [pl.BlockSpec((own, LANES), lambda g, c=c: (0, width // LANES + c))] * frame_size,
            out_specs=[
                pl.BlockSpec((all_tokens, 2 * group_width), lambda g: (0, g)),
                pl.BlockSpec((lats, group_width), lambda g: (0, g)),
            ],
            out_shape=[
                struct((all_tokens, 2 * half), BF16),
                struct((lats, half), F32),
            ],
            scratch_shapes=[
                pltpu.VMEM((items, lats, group_width), F32),
                pltpu.VMEM((items, lats, LANES), F32),
            ],
            cost_estimate=short,
            compiler_params=params,
        )(flags, after(boths[c], *held) if c else boths[c], queries, tops[c], *turns, *turns)
        chunk_grads.append(chunk_grad)
        chunk_queries.append(chunk_query)
        if c == 0:
            first_send, first_keep, first_received = weight_terms(0)
            held = (first_send,)
    pieces = [chip_pieces(after(first_keep, chunk_grads[-1]), first_received)]
    kv_sums = [send_pieces(pieces[0])]
    last_grad = chunk_grads[-1]
    chunk_grads[-1] = after(last_grad, *pieces[0])
    last_send, last_keep, last_received = weight_terms(CHUNKS - 1)
    pieces.append(chip_pieces(last_keep, last_received))
    kv_sums.append(send_pieces(pieces[-1]))
    chunk_grads[-1] = last_grad
    out_part = transposed_left(att_plane, after(branch_plane, last_send)[:, :width])

    last_block = pl.BlockSpec((lats, 2 * half), lambda i: (tokens // lats, 0))
    media_grad, media_sums, lat_product = pl.pallas_call(
        functools.partial(media_kernel, chunks=CHUNKS, items=items, frames=frame_total),
        grid=(items,),
        in_specs=[smem]
        + [pl.BlockSpec((patches, 2 * half), lambda i: (i, 0))] * CHUNKS
        + [last_block] * CHUNKS
        + [pl.BlockSpec((width, 2 * half), lambda i, c=c: (0, c)) for c in range(CHUNKS)]
        + [pl.BlockSpec((patches, width), lambda i: (i, 0)), whole, whole],
        out_specs=[
            pl.BlockSpec((patches, width), lambda i: (i, 0)),
            pl.BlockSpec((16, width), lambda i: (0, 0)),
            pl.BlockSpec((lats, width), lambda i: (0, 0)),
        ],
        out_shape=[
            struct((tokens, width), BF16),
            struct((16, width), F32),
            struct((lats, width), F32),
        ],
        cost_estimate=short,
        compiler_params=params,
    )(
        flags,
        *chunk_grads[:-1],
        after(chunk_grads[-1], *pieces[-1], out_part),
        *chunk_grads,
        *[kv_full] * CHUNKS,
        flat_media,
        time_rows,
        media_gain[None],
    )

    sum_rows = 2 * lats + 24
    sum_rows += -sum_rows % (8 * item_size)
    payload = pl.pallas_call(
        functools.partial(latent_kernel, chunks=CHUNKS, items=items),
        in_specs=[smem] + [whole] * (CHUNKS + 6),
        out_specs=whole,
        out_shape=struct((sum_rows, width), F32),
        cost_estimate=short,
        compiler_params=params,
    )(
        flags,
        *chunk_queries,
        after(lat_product, *kv_sums[0], *kv_sums[-1]),
        latents,
        latent_gain[None],
        grad_base,
        ffn_sums,
        media_sums,
    )
    payload_part = lax.psum_scatter(payload, "items", scatter_dimension=0, tiled=True)

    first_rows = frame_rows([[after(kv_sums[0][0], payload), *kv_sums[0][1:]], [out_part]])
    first_moved = send_rows_on(first_rows)
    all_plane = plane * frame_size
    block_rows = min(512, all_plane)
    row_block = pl.BlockSpec((block_rows, width), lambda i: (i, 0))
    hidden_block = pl.BlockSpec((block_rows, hidden_shard), lambda i: (i, 0))
    hidden, grad_up = pl.pallas_call(
        feed_back_kernel,
        grid=(all_plane // block_rows,),
        in_specs=[row_block, row_block, whole, whole],
        out_specs=[hidden_block, hidden_block],
        out_shape=[struct((all_plane, hidden_shard), BF16)] * 2,
        cost_estimate=short,
        compiler_params=params,
    )(after(ffn_all, *first_rows, *kv_sums[-1]), low_all, up_rows, down_weight)

    def outer(left, right, tile, kind):
        rows, columns = left.shape
        shape = (columns, right.shape[1])
        return pl.pallas_call(
            outer_kernel,
            grid=(columns // tile,),
            in_specs=[pl.BlockSpec((rows, tile), lambda i: (0, i)), whole],
            out_specs=pl.BlockSpec((tile, shape[1]), lambda i: (i, 0)),
            out_shape=struct(shape, kind),
            cost_estimate=short,
            compiler_params=params,
        )(left, right)

    last_rows = frame_rows([[after(kv_sums[-1][0], hidden), *kv_sums[-1][1:]]])
    last_moved = send_rows_on(last_rows)
    first_total = total_of(first_moved).astype(BF16)
    first_placed = spread_on(first_total, "frames")
    up_part = outer(ffn_all, after(grad_up, *first_placed, *last_rows), width // 4, BF16)
    up_grad = lax.all_to_all(up_part, "items", 0, 1, tiled=True).astype(F32)
    last_total = total_of(last_moved).astype(BF16)
    last_placed = spread_on(last_total, "frames")
    down_grad = outer(
        after(hidden, up_part, last_total),
        low_all,
        256 if hidden_shard % 256 == 0 else hidden_shard,
        F32,
    )
    placed = first_placed + last_placed
    key_grad, value_grad, out_grad = pl.pallas_call(
        functools.partial(
            place_kernel, chunks=CHUNKS, frames=frame_size, items=items, groups=groups
        ),
        in_specs=[smem] + [whole] * len(placed),
        out_specs=[whole] * 3,
        out_shape=[struct((frame_size, shard // frame_size, width), F32)] * 3,
        cost_estimate=short,
        compiler_params=params,
    )(flags, *placed)

    payload_part = after(payload_part, up_part)
    payload_others = spread_on(payload_part.astype(BF16), "frames")[1:]
    sums = lax.all_gather(
        total_of([payload_part] + payload_others), "items", axis=0, tiled=True
    )
    query_low = sums[lats : 2 * lats].astype(BF16)
    query_grad = transposed_left(lat_cols, query_low)
    norm_cols = transposed_right(query_low, query_weight)
    norm_cols = jnp.broadcast_to(norm_cols[None], (item_size, lats, shard))
    norm_grad = jnp.transpose(lax.all_to_all(norm_cols, "items", 0, 0), (1, 0, 2))
    latents_grad, lat_gain, lat_bias = pl.pallas_call(
        query_norm_kernel,
        out_shape=[struct((lats, width), F32), struct((1, width), F32), struct((1, width), F32)],
        cost_estimate=short,
        compiler_params=params,
    )(norm_grad.reshape(lats, width), latents, latent_gain[None], sums)
    at = 2 * lats
    column_sums = lax.dynamic_slice_in_dim(
        sums[at + 8 : at + 24], item_index * shard, shard, 1
    )

    result = mid_rows + total_of([result_pieces[d] for d in range(item_size)])
    return (
        result.reshape(items, row_total, width),
        entropy,
        media_grad.reshape(media.shape),
        latents_grad,
        column_sums[:frame_total],
        column_sums[8],
        column_sums[9],
        lat_gain[0],
        lat_bias[0],
        sums[at],
        sums[at + 1],
        query_grad,
        key_grad.reshape(shard, width),
        value_grad.reshape(shard, width),
        out_grad.reshape(shard, width),
        up_grad,
        down_grad,
    )


def solution(mesh):
    return jax.shard_map(
        body,
        mesh=mesh,
        in_specs=(
            P("items", "frames", None, None),
            P("items", "frames", None),
            P(),
            P(),
            P(),
            P(),
            P(),
            P(),
            P(),
            P(),
            P(),
            P(),
            P("items", None),
            P("items", None),
            P("items", None),
            P("items", None),
            P("items", None),
            P("items", None),
        ),
        out_specs=(
            P("items", "frames", None),
            P("items", "frames"),
            P("items", "frames", None, None),
            P(),
            P(None, "items"),
            P("items"),
            P("items"),
            P(),
            P(),
            P(),
            P(),
            P("items", None),
            P("items", None),
            P("items", None),
            P("items", None),
            P("items", None),
            P("items", None),
        ),
        check_vma=False,
    )
```

```python
import functools
import math

import jax
import jax.numpy as jnp
from jax import lax
from jax.experimental import pallas as pl
from jax.experimental.pallas import tpu as pltpu
from jax.sharding import PartitionSpec as P

HEADS = 16
GROUP = 4
CHUNKS = 2
LANES = 128
EPSILON = 1e-05
MASKED = -1e30
F32 = jnp.float32
BF16 = jnp.bfloat16
HIGHEST = lax.Precision.HIGHEST


def layer_norm(inputs, norm_gain, norm_bias):
    center = inputs - jnp.mean(inputs, axis=-1, keepdims=True)
    spread = jnp.mean(center * center, axis=-1, keepdims=True)
    return center * lax.rsqrt(spread + EPSILON) * norm_gain + norm_bias


def matmul(left_side, right_side):
    return jnp.dot(left_side, right_side, preferred_element_type=F32)


def transposed_left(left_side, right_side):
    return lax.dot_general(
        left_side, right_side, (((0,), (0,)), ((), ())), preferred_element_type=F32
    )


def transposed_right(left_side, right_side):
    return lax.dot_general(
        left_side, right_side, (((1,), (1,)), ((), ())), preferred_element_type=F32
    )


def send_on(x, axis, step):
    size = lax.axis_size(axis)
    return lax.ppermute(x, axis, [(i, (i + step) % size) for i in range(size)])


def send_across(x, axis, distance):
    return lax.ppermute(x, axis, [(i, i ^ distance) for i in range(lax.axis_size(axis))])


def spread_on(x, axis):
    return [x] + [send_on(x, axis, s) for s in range(1, lax.axis_size(axis))]


def spread_across(x, axis):
    chips = [x] + [send_across(x, axis, d) for d in range(2, lax.axis_size(axis), 2)]
    return [b for block in chips for b in (block, send_across(block, axis, 1))]


def collect_across(pieces, axis):
    return [pieces[0]] + [send_across(p, axis, d) for d, p in enumerate(pieces) if d]


def total_of(pieces):
    return functools.reduce(jnp.add, [p.astype(F32) for p in pieces])


def after(x, *earlier):
    return lax.optimization_barrier((x,) + earlier)[0]


def split_terms(x):
    high = x.astype(BF16)
    rest = x - high.astype(F32)
    middle = rest.astype(BF16)
    return high, middle, (rest - middle.astype(F32)).astype(BF16)


def iota(shape, dim):
    return lax.broadcasted_iota(jnp.int32, shape, dim)


def head_masks(rows, width, head_size):
    lane = iota((rows, width), 1)
    return [
        jnp.logical_and(lane >= h * head_size, lane < (h + 1) * head_size)
        for h in range(width // head_size)
    ]


def spread_heads(block, masks):
    return jnp.concatenate([jnp.where(m, block, jnp.zeros_like(block)) for m in masks], 0)


def collect_heads(block, masks):
    rows = block.shape[0] // len(masks)
    total = jnp.where(masks[0], block[:rows], 0.0)
    for h in range(1, len(masks)):
        total = total + jnp.where(masks[h], block[h * rows : (h + 1) * rows], 0.0)
    return total


def head_expand(width, head_size):
    row, column = iota((LANES, width), 0), iota((LANES, width), 1)
    return jnp.logical_and(column >= row * head_size, column < (row + 1) * head_size).astype(F32)


def live_rows(flag_ref, item, items, patches, lats, columns):
    row = iota((patches + lats, columns), 0)
    media = jnp.logical_and(row < patches, flag_ref[item] > 0)
    return jnp.logical_or(media, jnp.logical_and(row >= patches, flag_ref[items] > 0))


def pack_shape(own, shard, width):
    unit = math.gcd(own, shard)
    return unit, width * unit // shard


def join_kernel(key_ref, value_ref, cotangent_ref, out_ref, low_ref, *, width):
    for g in range(key_ref.shape[1] // width):
        columns = slice(g * width, (g + 1) * width)
        out_ref[:, 2 * g * width : (2 * g + 1) * width] = key_ref[:, columns]
        out_ref[:, (2 * g + 1) * width : (2 * g + 2) * width] = value_ref[:, columns]
    low = cotangent_ref[...].astype(BF16)
    low_ref[...] = low
    own, span = low.shape
    unit, piece = pack_shape(own, out_ref.shape[0], span)
    for a in range(own // unit):
        for b in range(span // piece):
            at = 2 * span + a * piece
            out_ref[b * unit : (b + 1) * unit, at : at + piece] = low[
                a * unit : (a + 1) * unit, b * piece : (b + 1) * piece
            ]


def norm_kernel(media_ref, time_ref, gain_ref, bias_ref, lat_ref, out_ref, *, steps, per_item):
    step = pl.program_id(0)

    @pl.when(step < steps)
    def _():
        rows = media_ref[...].astype(F32) + time_ref[pl.ds(step // per_item, 1), :]
        out_ref[...] = layer_norm(rows, gain_ref[...], bias_ref[...]).astype(BF16)

    @pl.when(step == steps)
    def _():
        out_ref[...] = lat_ref[...]


def forward_kernel(
    flag_ref, both_ref, query_ref, top_ref, *refs, items, patches, scale, head_size, heads,
):
    message_refs, (part_ref, mark_ref) = refs[:-2], refs[-2:]
    lats, width = query_ref.shape
    frames = len(message_refs)
    own = message_refs[0].shape[0]
    row_total = own // items
    masks = head_masks(lats, width, head_size)
    queries = spread_heads(query_ref[...].astype(F32), masks).astype(BF16)
    base = items * patches
    lat_both = both_ref[base : base + lats, :]
    group = pl.program_id(0)
    term, lane = iota((16, GROUP * LANES), 0), iota((16, GROUP * LANES), 1)
    place = jnp.logical_and(
        lane % LANES == term * heads + group * GROUP + lane // LANES, term < 9
    ).astype(BF16)
    for i in range(items):
        both = jnp.concatenate([both_ref[i * patches : (i + 1) * patches, :], lat_both], 0)
        live = live_rows(flag_ref, i, items, patches, lats, queries.shape[0])
        scores = scale * transposed_right(both[:, :width], queries)
        masked = jnp.where(live, scores, MASKED)
        top = jnp.max(masked, axis=0, keepdims=True)
        block_exp = jnp.where(live, jnp.exp(masked - top), 0.0)
        total = jnp.sum(block_exp, axis=0, keepdims=True)
        moment = jnp.sum(block_exp * scores, axis=0, keepdims=True)
        part = transposed_left(block_exp.astype(BF16), both[:, width:])
        part_ref[i] = collect_heads(part, masks)
        top_ref[0, i] = jnp.broadcast_to(top, top_ref.shape[2:])
        terms = jnp.concatenate(
            [t.astype(F32) for x in (top, total, moment) for t in split_terms(x)]
            + [jnp.zeros((7, top.shape[1]), F32)],
            0,
        ).astype(BF16)
        wide = transposed_left(terms, place)
        mark = wide[:lats, :LANES]
        for h in range(1, GROUP):
            mark = mark + wide[h * lats : (h + 1) * lats, h * LANES : (h + 1) * LANES]
        mark_ref[i] = mark

    end = message_refs[0].shape[1] - LANES
    for s, message_ref in enumerate(message_refs):
        start = pl.multiple_of(lax.rem(flag_ref[items + 1] + s, frames) * row_total, row_total)
        rows = pl.ds(start, row_total)
        block = jnp.concatenate([part_ref[i, rows, :] for i in range(items)], 0).astype(BF16)
        mark = jnp.concatenate([mark_ref[i, rows, :] for i in range(items)], 0).astype(BF16)
        for g in range(end // width):

            @pl.when(group == g)
            def _():
                message_ref[:, g * width : (g + 1) * width] = block
                if g == 0:
                    message_ref[:, end:] = mark
                else:
                    message_ref[:, end:] = message_ref[:, end:] + mark


def merge_kernel(*refs, chunks, frames, items, head_size, heads):
    message_refs = refs[: chunks * frames]
    base_ref, weight_ref, gain_ref, bias_ref = refs[chunks * frames : chunks * frames + 4]
    merged_ref, mid_ref, ffn_ref, log_ref, entropy_ref = refs[chunks * frames + 4 :]
    own, columns = message_refs[0].shape
    half = columns - LANES
    lane, column = iota((LANES, 3 * LANES), 0), iota((LANES, 3 * LANES), 1)
    gather = jnp.logical_and(
        jnp.logical_and(lane // heads // 3 == column // LANES, lane % heads == column % LANES),
        lane < 9 * heads,
    ).astype(BF16)
    expand = head_expand(half, head_size)
    live = iota((own, LANES), 1) < heads
    spread = jnp.zeros((own, LANES), F32)
    for c in range(chunks):
        sources = message_refs[c * frames : (c + 1) * frames]
        stats = [matmul(x[:, half:], gather) for x in sources]
        tops = [x[:, :LANES] for x in stats]
        peak = functools.reduce(jnp.maximum, tops)
        factors = [jnp.exp(t - peak) for t in tops]
        whole = sum(f * x[:, LANES : 2 * LANES] for f, x in zip(factors, stats))
        moment = sum(f * x[:, 2 * LANES :] for f, x in zip(factors, stats))
        whole = jnp.where(live, whole, 1.0)
        log_total = jnp.where(live, peak + jnp.log(whole), 0.0)
        log_ref[c] = log_total
        spread = spread + jnp.where(live, log_total - moment / whole, 0.0)
        merged = jnp.zeros((own, half), F32)
        for x, factor in zip(sources, factors):
            share = jnp.where(live, factor / whole, 0.0)
            wide = jnp.dot(share, expand, precision=HIGHEST, preferred_element_type=F32)
            merged = merged + x[:, :half].astype(F32) * wide
        merged_ref[:, c * half : (c + 1) * half] = merged
    entropy_ref[...] = jnp.broadcast_to(
        jnp.sum(spread, axis=1, keepdims=True) * (1.0 / HEADS), entropy_ref.shape
    )
    base = jnp.concatenate([base_ref[...]] * items, 0)
    mid = base + matmul(merged_ref[...].astype(BF16), weight_ref[...])
    mid_ref[...] = mid
    ffn_ref[...] = layer_norm(mid, gain_ref[...], bias_ref[...]).astype(BF16)


def gelu_parts(x):
    share = 0.5 * (1.0 + lax.erf(x * (0.5**0.5)))
    slope = share + x * jnp.exp(-0.5 * x * x) * ((2.0 * jnp.pi) ** -0.5)
    return x * share, slope


def feed_kernel(flag_ref, *refs, devices, items):
    row_refs = refs[:devices]
    low_ref, up_ref, down_ref, result_ref = refs[devices : devices + 4]
    grad_refs, (plane_ref, plane_low_ref) = refs[devices + 4 : -2], refs[-2:]
    own, width = row_refs[0].shape
    shard = low_ref.shape[0] // devices
    unit, piece = pack_shape(own, shard, width)
    me = flag_ref[2 * items + 2]
    for d in range(devices):
        plane_ref[d * own : (d + 1) * own, :] = row_refs[d][...]
        source = jnp.bitwise_xor(me, d) * shard
        for a in range(own // unit):
            rows = slice(d * own + a * unit, d * own + (a + 1) * unit)
            for b in range(shard // unit):
                start = pl.multiple_of(source + b * unit, unit)
                plane_low_ref[rows, b * piece : (b + 1) * piece] = low_ref[
                    pl.ds(start, unit), a * piece : (a + 1) * piece
                ]
    upward = transposed_right(plane_ref[...], up_ref[...])
    hidden, slope = gelu_parts(upward)
    grad_up = (slope * transposed_right(plane_low_ref[...], down_ref[...])).astype(BF16)
    grad = matmul(grad_up, up_ref[...]).astype(BF16)
    result = matmul(hidden.astype(BF16), down_ref[...]).astype(BF16)
    for d in range(devices):
        grad_refs[d][...] = grad[d * own : (d + 1) * own, :]
        result_ref[jnp.bitwise_xor(me, d)] = result[d * own : (d + 1) * own, :]


def feed_back_kernel(row_ref, low_ref, up_ref, down_ref, hidden_ref, grad_ref):
    hidden, slope = gelu_parts(transposed_right(row_ref[...], up_ref[...]))
    hidden_ref[...] = hidden.astype(BF16)
    grad_ref[...] = (slope * transposed_right(low_ref[...], down_ref[...])).astype(BF16)


def outer_kernel(left_ref, right_ref, out_ref):
    out_ref[...] = transposed_left(left_ref[...], right_ref[...]).astype(out_ref.dtype)


def norm_backward(rows, gain, gradient):
    center = rows - jnp.mean(rows, axis=1, keepdims=True)
    rate = lax.rsqrt(jnp.mean(center * center, axis=1, keepdims=True) + EPSILON)
    unit = center * rate
    scaled = gradient * gain
    inner = scaled - jnp.mean(scaled, axis=1, keepdims=True)
    back = rate * (inner - unit * jnp.mean(scaled * unit, axis=1, keepdims=True))
    return (
        back,
        jnp.sum(gradient * unit, axis=0, keepdims=True),
        jnp.sum(gradient, axis=0, keepdims=True),
    )


def turn_kernel(*refs, devices, items, chunks, head_size, heads):
    part_refs = refs[:devices]
    mid_ref, cotangent_ref, gain_ref, merged_ref, log_ref, weight_ref = refs[
        devices : devices + 6
    ]
    message_ref, branch_ref, base_ref, sums_ref = refs[devices + 6 :]
    own, width = mid_ref.shape
    half = width // chunks
    gradient = total_of([x[...] for x in part_refs])
    back, gain_sum, bias_sum = norm_backward(mid_ref[...], gain_ref[...], gradient)
    grad_mid = cotangent_ref[...] + back
    sums_ref[...] = jnp.zeros(sums_ref.shape, F32)
    sums_ref[0:1, :] = gain_sum
    sums_ref[1:2, :] = bias_sum
    row_total = own // items
    base_ref[...] = total_of(
        [grad_mid[i * row_total : (i + 1) * row_total] for i in range(items)]
    )
    branch = grad_mid.astype(BF16)
    branch_ref[:, :width] = branch
    branch_ref[:, width:] = merged_ref[...].astype(BF16)
    grad_att = transposed_right(branch, weight_ref[...]).astype(BF16)
    expand = head_expand(half, head_size)
    lane, column = iota((6 * LANES, LANES), 0), iota((6 * LANES, LANES), 1)
    place = jnp.logical_and(
        lane % LANES < heads, column == (lane // LANES) * heads + lane % LANES
    ).astype(BF16)
    message_ref[:, :width] = grad_att
    for c in range(chunks):
        columns = slice(c * half, (c + 1) * half)
        delta = lax.dot_general(
            merged_ref[:, columns] * grad_att[:, columns].astype(F32),
            expand,
            (((1,), (1,)), ((), ())),
            precision=HIGHEST,
            preferred_element_type=F32,
        )
        terms = jnp.concatenate([t for x in (log_ref[c], delta) for t in split_terms(x)], 1)
        message_ref[:, width + c * LANES : width + (c + 1) * LANES] = matmul(
            terms, place
        ).astype(BF16)


def backward_kernel(
    *refs, frames, items, patches, scale, head_size, heads,
):
    flag_ref, both_ref, query_ref, top_ref = refs[:4]
    grad_refs = refs[4 : 4 + frames]
    mark_refs = refs[4 + frames : 4 + 2 * frames]
    out_ref, sum_ref, held_ref, note_ref = refs[4 + 2 * frames :]
    lats, width = query_ref.shape
    own = grad_refs[0].shape[0]
    row_total = own // items
    base = items * patches
    for s in range(frames):
        source = lax.rem(flag_ref[items + 1] + (frames - s), frames)
        rows = pl.ds(pl.multiple_of(source * row_total, row_total), row_total)
        block = grad_refs[s][...].astype(F32)
        mark = mark_refs[s][...].astype(F32)
        for i in range(items):
            held_ref[i, rows, :] = block[i * row_total : (i + 1) * row_total]
            note_ref[i, rows, :] = mark[i * row_total : (i + 1) * row_total]
    masks = head_masks(lats, width, head_size)
    queries = spread_heads(query_ref[...].astype(F32), masks).astype(BF16)
    lat_both = both_ref[base : base + lats, :]
    row, lane = iota((GROUP * 8, LANES), 0), iota((GROUP * 8, LANES), 1)
    pick = jnp.logical_and(
        jnp.logical_and(
            lane // heads // 3 == row % 8,
            lane % heads == pl.program_id(0) * GROUP + row // 8,
        ),
        lane < 6 * heads,
    ).astype(BF16)
    grad_query = jnp.zeros((queries.shape[0], width), F32)
    lat_grad_key = jnp.zeros((lats, width), F32)
    lat_grad_value = jnp.zeros((lats, width), F32)
    for i in range(items):
        rows = slice(i * patches, (i + 1) * patches)
        stats = transposed_right(pick, note_ref[i].astype(BF16))
        stats = jnp.concatenate([stats[h * 8 : (h + 1) * 8] for h in range(GROUP)], 1)
        log_total = stats[0:1]
        delta = stats[1:2]
        top = top_ref[0, i, 0:1, :]
        rescale = jnp.exp(top - log_total)
        both = jnp.concatenate([both_ref[rows, :], lat_both], 0)
        keys, values = both[:, :width], both[:, width:]
        grads = spread_heads(held_ref[i], masks).astype(BF16)
        live = live_rows(flag_ref, i, items, patches, lats, queries.shape[0])
        masked = jnp.where(live, scale * transposed_right(keys, queries), MASKED)
        probs = jnp.where(live, jnp.exp(masked - log_total), 0.0)
        block_exp = jnp.where(live, jnp.exp(masked - top), 0.0)
        weights = (block_exp.astype(BF16).astype(F32) * rescale).astype(BF16)
        grad_scores = (probs * (transposed_right(values, grads) - delta)).astype(BF16)
        grad_key = scale * matmul(grad_scores, queries)
        grad_value = matmul(weights, grads)
        out_ref[rows, :width] = grad_key[:patches].astype(BF16)
        out_ref[rows, width:] = grad_value[:patches].astype(BF16)
        grad_query = grad_query + transposed_left(grad_scores, keys)
        lat_grad_key = lat_grad_key + grad_key[patches:]
        lat_grad_value = lat_grad_value + grad_value[patches:]
    out_ref[base : base + lats, :width] = lat_grad_key.astype(BF16)
    out_ref[base : base + lats, width:] = lat_grad_value.astype(BF16)
    sum_ref[...] = scale * collect_heads(grad_query, masks)


def media_kernel(flag_ref, *refs, chunks, items, frames):
    grad_refs, lat_refs, weight_refs = [
        refs[k * chunks : (k + 1) * chunks] for k in range(3)
    ]
    media_ref, time_ref, gain_ref, out_ref, sums_ref, product_ref = refs[3 * chunks :]
    item = pl.program_id(0)

    @pl.when(item == 0)
    def _():
        sums_ref[...] = jnp.zeros(sums_ref.shape, F32)
        product_ref[...] = functools.reduce(
            jnp.add, [transposed_right(g[...], w[...]) for g, w in zip(lat_refs, weight_refs)]
        )

    gradient = functools.reduce(
        jnp.add, [transposed_right(g[...], w[...]) for g, w in zip(grad_refs, weight_refs)]
    )
    inputs = media_ref[...].astype(F32) + time_ref[pl.ds(item, 1), :]
    back, gain_sum, bias_sum = norm_backward(inputs, gain_ref[...], gradient)
    out_ref[...] = back.astype(BF16)
    place = iota((frames, 1), 0) == flag_ref[items + 2 + item]
    sums_ref[0:frames, :] += jnp.where(place, jnp.sum(back, axis=0, keepdims=True), 0.0)
    sums_ref[8:9, :] += gain_sum
    sums_ref[9:10, :] += bias_sum


def latent_kernel(flag_ref, *refs, chunks, items):
    query_refs = refs[:chunks]
    (
        product_ref, latent_ref, gain_ref, base_ref, ffn_ref, media_ref, out_ref,
    ) = refs[chunks:]
    lats, width = latent_ref.shape
    half = width // chunks
    gradient = product_ref[...]
    for c in range(chunks):
        out_ref[lats : 2 * lats, c * half : (c + 1) * half] = query_refs[c][...]
    back, gain_sum, bias_sum = norm_backward(latent_ref[...], gain_ref[...], gradient)
    out_ref[:lats, :] = back
    row_total = base_ref.shape[0]
    start = pl.multiple_of(flag_ref[items + 1] * row_total, row_total)
    out_ref[pl.ds(start, row_total), :] += base_ref[...]
    at = 2 * lats
    out_ref[at : at + 8, :] = ffn_ref[...]
    out_ref[at + 2 : at + 3, :] = gain_sum
    out_ref[at + 3 : at + 4, :] = bias_sum
    out_ref[at + 8 : at + 24, :] = media_ref[...]
    out_ref[at + 24 :, :] = jnp.zeros((out_ref.shape[0] - at - 24, width), F32)


def query_norm_kernel(flag_ref, *refs, devices, items):
    column_refs = refs[:devices]
    latent_ref, gain_ref, sum_ref, out_ref, out_gain_ref, out_bias_ref, held_ref = refs[devices:]
    for d in range(devices):
        held_ref[jnp.bitwise_xor(flag_ref[2 * items + 2], d)] = column_refs[d][...]
    gradient = jnp.concatenate([held_ref[k] for k in range(devices)], 1)
    back, gain_sum, bias_sum = norm_backward(latent_ref[...], gain_ref[...], gradient)
    lats = latent_ref.shape[0]
    out_ref[...] = sum_ref[:lats, :] + back
    out_gain_ref[...] = sum_ref[2 * lats + 2 : 2 * lats + 3, :] + gain_sum
    out_bias_ref[...] = sum_ref[2 * lats + 3 : 2 * lats + 4, :] + bias_sum


def rows_kernel(flag_ref, *refs, count, frames, items):
    part_refs, out_refs, held_ref = refs[:count], refs[count:-1], refs[-1]
    rows = held_ref.shape[1]
    column = 0
    for part_ref in part_refs:
        total = total_of([part_ref[k] for k in range(part_ref.shape[0])])
        for f in range(frames):
            held_ref[f, :, column : column + total.shape[1]] = total[f * rows : (f + 1) * rows]
        column += total.shape[1]
    for s, out_ref in enumerate(out_refs):
        block = held_ref[lax.rem(flag_ref[items + 1] + s, frames)]
        out_ref[...] = block.astype(out_ref.dtype)


def place_kernel(flag_ref, *refs, chunks, frames, items, groups):
    chunk_refs = refs[: chunks * frames]
    key_ref, value_ref, out_ref = refs[chunks * frames :]
    width = key_ref.shape[2] // (chunks * groups)
    for s in range(frames):
        source = lax.rem(flag_ref[items + 1] + (frames - s), frames)
        out_ref[source] = chunk_refs[s][:, 2 * groups * width :].astype(F32)
        for c in range(chunks):
            for g in range(groups):
                at = (c * groups + g) * width
                block = chunk_refs[c * frames + s][:, 2 * g * width : 2 * (g + 1) * width]
                block = block.astype(F32)
                key_ref[source, :, at : at + width] = block[:, :width]
                value_ref[source, :, at : at + width] = block[:, width:]


def body(
    media,
    cotangent,
    frame_count,
    frame_start,
    latents,
    time_embed,
    media_gain,
    media_bias,
    latent_gain,
    latent_bias,
    ffn_gain,
    ffn_bias,
    query_weight,
    key_weight,
    value_weight,
    out_weight,
    up_weight,
    down_weight,
):
    items = media.shape[0]
    patches = media.shape[2]
    width = media.shape[3]
    lats = latents.shape[0]
    frame_total = time_embed.shape[0]
    row_total = cotangent.shape[1]
    own = items * row_total
    head_size = width // HEADS
    half = width // CHUNKS
    chunk_heads = HEADS // CHUNKS
    group_width = GROUP * head_size
    groups = chunk_heads // GROUP
    stack = GROUP * lats
    tokens = items * patches
    all_tokens = tokens + lats
    shard = query_weight.shape[0]
    hidden_shard = down_weight.shape[0]
    item_size = lax.axis_size("items")
    frame_size = lax.axis_size("frames")
    plane = item_size * own
    item_index = lax.axis_index("items")
    slot = lax.axis_index("frames")
    row_base = slot * row_total
    params = pltpu.CompilerParams(vmem_limit_bytes=56 * 2**20)
    smem = pl.BlockSpec(memory_space=pltpu.SMEM)
    whole = pl.BlockSpec(memory_space=pltpu.VMEM)
    sizes = dict(items=items, head_size=head_size, heads=chunk_heads)

    def struct(shape, kind):
        return jax.ShapeDtypeStruct(shape, kind)

    short = pl.CostEstimate(flops=1000, bytes_accessed=1000, transcendentals=0)

    def frame_order(x):
        return jnp.stack(
            [
                lax.dynamic_index_in_dim(x, (slot + frame_size - f) % frame_size, 0, False)
                for f in range(frame_size)
            ]
        )

    def column_blocks(x):
        return jnp.transpose(x.reshape(-1, item_size, shard), (1, 0, 2))

    def scatter_exchange(x, axis):
        return jnp.sum(lax.all_to_all(x, axis, 0, 0).astype(F32), axis=0)

    grad_out = cotangent.reshape(own, width)
    low_columns = own * width // shard
    joined, grad_low = pl.pallas_call(
        functools.partial(join_kernel, width=group_width),
        out_shape=[struct((shard, 2 * width + low_columns), BF16), struct((own, width), BF16)],
        cost_estimate=short,
        compiler_params=params,
    )(key_weight, value_weight, grad_out)
    kv_full = lax.all_gather(joined, "items", axis=0, tiled=True)
    low_frames = jnp.stack(spread_on(grad_low, "frames"))

    hidden_part = hidden_shard // frame_size
    up_mine = lax.dynamic_index_in_dim(
        after(up_weight, low_frames).reshape(shard, item_size, frame_size, hidden_part),
        slot,
        2,
        False,
    )
    up_mine = lax.all_to_all(jnp.transpose(up_mine, (1, 2, 0)), "items", 0, 0)
    up_mine = jnp.transpose(up_mine, (1, 0, 2)).reshape(hidden_part, width)
    up_parts = jnp.stack(spread_on(up_mine, "frames"))
    up_rows = frame_order(up_parts).reshape(hidden_shard, width)

    lat_norm = layer_norm(latents, latent_gain, latent_bias).astype(BF16)
    lat_cols = lax.dynamic_slice_in_dim(lat_norm, item_index * shard, shard, 1)
    query_blocks = column_blocks(matmul(lat_cols, query_weight))
    query_cols = scatter_exchange(after(query_blocks, up_mine), "items").astype(BF16)
    query_spread = jnp.broadcast_to(query_cols[None], (item_size, lats, shard))
    queries = jnp.transpose(lax.all_to_all(query_spread, "items", 0, 0), (1, 0, 2)).reshape(
        lats, width
    )

    counts = lax.dynamic_slice_in_dim(frame_count, item_index * items, items)
    starts = lax.dynamic_slice_in_dim(frame_start, item_index * items, items)
    offset = (slot - starts) % frame_total
    flags = jnp.concatenate(
        [
            (offset < counts).astype(jnp.int32),
            (slot == 0).astype(jnp.int32)[None],
            slot.astype(jnp.int32)[None],
            offset.astype(jnp.int32),
            item_index.astype(jnp.int32)[None],
        ]
    )
    picker = (offset[:, None] == jnp.arange(frame_total, dtype=jnp.int32)[None, :]).astype(F32)
    time_rows = jnp.dot(picker, time_embed, precision=HIGHEST, preferred_element_type=F32)
    flat_media = media.reshape(tokens, width)
    steps = tokens // lats
    all_rows = pl.pallas_call(
        functools.partial(norm_kernel, steps=steps, per_item=patches // lats),
        grid=(steps + 1,),
        in_specs=[
            pl.BlockSpec((lats, width), lambda i: (jnp.minimum(i, steps - 1), 0)),
            whole,
            whole,
            whole,
            whole,
        ],
        out_specs=pl.BlockSpec((lats, width), lambda i: (i, 0)),
        out_shape=struct((all_tokens, width), BF16),
        cost_estimate=short,
        compiler_params=params,
    )(
        after(flat_media, query_blocks),
        time_rows,
        media_gain[None],
        media_bias[None],
        lat_norm,
    )
    out_full = lax.all_gather(after(out_weight, all_rows), "items", axis=0, tiled=True)

    core = item_index % 2
    rows_across = after(all_rows, query_cols).T.reshape(item_size // 2, 2, shard, all_tokens)
    send_rows, keep_rows = [
        jnp.concatenate(
            [
                lax.dynamic_slice(
                    rows_across, (k, which, 0, 0), (1, 1, shard, all_tokens)
                ).reshape(shard, all_tokens)
                for k in range(item_size // 2)
            ],
            0,
        )
        for which in (1 - core, core)
    ]
    boths, tops, messages = [], [], []
    for c in range(CHUNKS):

        def block_of(g, c=c):
            return (0, c * groups + g)

        if c:
            rows = after(all_rows, tops[-1])
        else:
            rows = after(all_rows, queries, send_rows, keep_rows)
        both = matmul(rows, kv_full[:, 2 * c * half : 2 * (c + 1) * half]).astype(BF16)
        top, *parts = pl.pallas_call(
            functools.partial(
                forward_kernel, patches=patches, scale=head_size**-0.5, **sizes
            ),
            grid=(groups,),
            in_specs=[
                smem,
                pl.BlockSpec((all_tokens, 2 * group_width), lambda g: (0, g)),
                pl.BlockSpec((lats, group_width), block_of),
            ],
            out_specs=[pl.BlockSpec((1, items, 8, stack), lambda g: (g, 0, 0, 0))]
            + [pl.BlockSpec((own, half + LANES), lambda g: (0, 0))] * frame_size,
            out_shape=[struct((groups, items, 8, stack), F32)]
            + [struct((own, half + LANES), BF16)] * frame_size,
            scratch_shapes=[
                pltpu.VMEM((items, lats, group_width), F32),
                pltpu.VMEM((items, lats, LANES), F32),
            ],
            cost_estimate=short,
            compiler_params=params,
        )(flags, after(both, up_rows) if c else both, queries)
        boths.append(both)
        tops.append(top)
        messages += [p if s == 0 else send_on(p, "frames", s) for s, p in enumerate(parts)]
    low_all = lax.all_gather(after(low_frames, tops[1]), "items", axis=0).reshape(-1, width)

    base_rows = lax.dynamic_slice_in_dim(latents, row_base, row_total, 0)
    merged, mid_rows, ffn_in, logs, entropy_wide = pl.pallas_call(
        functools.partial(merge_kernel, chunks=CHUNKS, frames=frame_size, **sizes),
        out_shape=[
            struct((own, width), F32),
            struct((own, width), F32),
            struct((own, width), BF16),
            struct((CHUNKS, own, LANES), F32),
            struct((own, LANES), F32),
        ],
        cost_estimate=short,
        compiler_params=params,
    )(*messages, base_rows, out_full, ffn_gain[None], ffn_bias[None])
    entropy = entropy_wide[:, 0].reshape(items, row_total)

    ffn_blocks = spread_across(ffn_in, "items")
    ffn_frames = spread_on(after(ffn_in, *ffn_blocks), "frames")
    result_part, *parts = pl.pallas_call(
        functools.partial(feed_kernel, devices=item_size, items=items),
        grid=(1,),
        in_specs=[smem]
        + [whole] * item_size
        + [
            pl.BlockSpec((width, low_columns), lambda i: (0, 2 * width // low_columns)),
            whole,
            whole,
        ],
        out_specs=[whole] * (1 + item_size),
        out_shape=[struct((item_size, own, width), BF16)]
        + [struct((own, width), BF16)] * item_size,
        scratch_shapes=[pltpu.VMEM((plane, width), BF16)] * 2,
        cost_estimate=short,
        compiler_params=params,
    )(flags, *ffn_blocks, kv_full, up_rows, down_weight)
    grad_blocks = collect_across(parts, "items")
    grad_blocks[0] = after(grad_blocks[0], *ffn_frames)

    turn, grad_branch, grad_base, ffn_sums = pl.pallas_call(
        functools.partial(turn_kernel, devices=item_size, chunks=CHUNKS, **sizes),
        out_shape=[
            struct((own, width + CHUNKS * LANES), BF16),
            struct((own, 2 * width), BF16),
            struct((row_total, width), F32),
            struct((8, width), F32),
        ],
        cost_estimate=short,
        compiler_params=params,
    )(*grad_blocks, mid_rows, grad_out, ffn_gain[None], merged, logs, out_full)
    turns = spread_on(turn, "frames")
    branch_plane = lax.all_gather(grad_branch, "items", axis=0, tiled=True)
    ffn_all = lax.all_gather(
        after(jnp.stack(ffn_frames), grad_branch), "items", axis=0
    ).reshape(-1, width)
    att_plane = lax.dynamic_slice_in_dim(
        branch_plane, width + item_index * shard, shard, 1
    )
    turns[0] = after(turns[0], low_all)

    chunk_grads, chunk_queries = [], []

    def weight_terms(c):
        send = matmul(send_rows, chunk_grads[c]).astype(BF16)
        received = send_across(send, "items", 1).reshape(-1, shard, 2 * half)
        keep = matmul(after(keep_rows, send), chunk_grads[c]).astype(BF16)
        return send, keep.reshape(-1, shard, 2 * half), received

    def chip_terms(keep, received):
        return (keep.astype(F32) + received.astype(F32)).astype(BF16)

    def exchange_chips(x):
        groups_of = [list(range(k, item_size, 2)) for k in range(2)]
        return lax.all_to_all(x, "items", 0, 0, axis_index_groups=groups_of)

    def frame_rows(ranges):
        rows = shard // frame_size
        columns = sum(x.shape[-1] for x in ranges)
        return pl.pallas_call(
            functools.partial(rows_kernel, count=len(ranges), frames=frame_size, items=items),
            in_specs=[smem] + [whole] * len(ranges),
            out_specs=[whole] * frame_size,
            out_shape=[struct((rows, columns), F32)]
            + [struct((rows, columns), BF16)] * (frame_size - 1),
            scratch_shapes=[pltpu.VMEM((frame_size, rows, columns), F32)],
            cost_estimate=short,
            compiler_params=params,
        )(flags, *ranges)

    def send_rows_on(rows):
        return [rows[0]] + [send_on(p, "frames", s) for s, p in enumerate(rows) if s]

    for c in range(CHUNKS):

        def block_of(g, c=c):
            return (0, c * groups + g)

        chunk_grad, chunk_query = pl.pallas_call(
            functools.partial(
                backward_kernel, frames=frame_size, patches=patches, scale=head_size**-0.5, **sizes
            ),
            grid=(groups,),
            in_specs=[
                smem,
                pl.BlockSpec((all_tokens, 2 * group_width), lambda g: (0, g)),
                pl.BlockSpec((lats, group_width), block_of),
                pl.BlockSpec((1, items, 8, stack), lambda g: (g, 0, 0, 0)),
            ]
            + [pl.BlockSpec((own, group_width), block_of)] * frame_size
            + [pl.BlockSpec((own, LANES), lambda g, c=c: (0, width // LANES + c))] * frame_size,
            out_specs=[
                pl.BlockSpec((all_tokens, 2 * group_width), lambda g: (0, g)),
                pl.BlockSpec((lats, group_width), lambda g: (0, g)),
            ],
            out_shape=[
                struct((all_tokens, 2 * half), BF16),
                struct((lats, half), F32),
            ],
            scratch_shapes=[
                pltpu.VMEM((items, lats, group_width), F32),
                pltpu.VMEM((items, lats, LANES), F32),
            ],
            cost_estimate=short,
            compiler_params=params,
        )(flags, after(boths[c], *held) if c else boths[c], queries, tops[c], *turns, *turns)
        chunk_grads.append(chunk_grad)
        chunk_queries.append(chunk_query)
        if c == 0:
            first_send, first_keep, first_received = weight_terms(0)
            result_pieces = lax.all_to_all(after(result_part, chunk_grad), "items", 0, 0)
            held = (first_send,)
    first_terms = chip_terms(after(first_keep, chunk_grads[-1]), first_received)
    first_moved = exchange_chips(after(first_terms, result_pieces))

    last_block = pl.BlockSpec((lats, 2 * half), lambda i: (tokens // lats, 0))
    media_grad, media_sums, lat_product = pl.pallas_call(
        functools.partial(media_kernel, chunks=CHUNKS, items=items, frames=frame_total),
        grid=(items,),
        in_specs=[smem]
        + [pl.BlockSpec((patches, 2 * half), lambda i: (i, 0))] * CHUNKS
        + [last_block] * CHUNKS
        + [pl.BlockSpec((width, 2 * half), lambda i, c=c: (0, c)) for c in range(CHUNKS)]
        + [pl.BlockSpec((patches, width), lambda i: (i, 0)), whole, whole],
        out_specs=[
            pl.BlockSpec((patches, width), lambda i: (i, 0)),
            pl.BlockSpec((16, width), lambda i: (0, 0)),
            pl.BlockSpec((lats, width), lambda i: (0, 0)),
        ],
        out_shape=[
            struct((tokens, width), BF16),
            struct((16, width), F32),
            struct((lats, width), F32),
        ],
        cost_estimate=short,
        compiler_params=params,
    )(
        flags,
        *chunk_grads[:-1],
        after(chunk_grads[-1], first_terms, result_pieces),
        *chunk_grads,
        *[kv_full] * CHUNKS,
        flat_media,
        time_rows,
        media_gain[None],
    )

    sum_rows = 2 * lats + 24
    sum_rows += -sum_rows % (8 * item_size)
    payload = pl.pallas_call(
        functools.partial(latent_kernel, chunks=CHUNKS, items=items),
        in_specs=[smem] + [whole] * (CHUNKS + 6),
        out_specs=whole,
        out_shape=struct((sum_rows, width), F32),
        cost_estimate=short,
        compiler_params=params,
    )(
        flags,
        *chunk_queries,
        lat_product,
        latents,
        latent_gain[None],
        grad_base,
        ffn_sums,
        media_sums,
    )
    payload_part = lax.psum_scatter(payload, "items", scatter_dimension=0, tiled=True)

    chunk_grads[-1] = after(chunk_grads[-1], payload)
    last_send, last_keep, last_received = weight_terms(CHUNKS - 1)
    last_terms = chip_terms(after(last_keep, first_moved), last_received)
    last_moved = exchange_chips(last_terms)
    out_part = transposed_left(att_plane, after(branch_plane, last_send)[:, :width])
    first_rows = frame_rows([after(first_moved, last_terms), out_part[None]])
    first_frames = send_rows_on(first_rows)
    all_plane = plane * frame_size
    block_rows = min(512, all_plane)
    row_block = pl.BlockSpec((block_rows, width), lambda i: (i, 0))
    hidden_block = pl.BlockSpec((block_rows, hidden_shard), lambda i: (i, 0))
    hidden, grad_up = pl.pallas_call(
        feed_back_kernel,
        grid=(all_plane // block_rows,),
        in_specs=[row_block, row_block, whole, whole],
        out_specs=[hidden_block, hidden_block],
        out_shape=[struct((all_plane, hidden_shard), BF16)] * 2,
        cost_estimate=short,
        compiler_params=params,
    )(after(ffn_all, *first_rows), low_all, up_rows, down_weight)

    def outer(left, right, tile, kind):
        rows, columns = left.shape
        shape = (columns, right.shape[1])
        return pl.pallas_call(
            outer_kernel,
            grid=(columns // tile,),
            in_specs=[pl.BlockSpec((rows, tile), lambda i: (0, i)), whole],
            out_specs=pl.BlockSpec((tile, shape[1]), lambda i: (i, 0)),
            out_shape=struct(shape, kind),
            cost_estimate=short,
            compiler_params=params,
        )(left, right)

    first_total = total_of(first_frames).astype(BF16)
    first_placed = spread_on(first_total, "frames")
    last_rows = frame_rows([after(last_moved, hidden)])
    last_frames = send_rows_on(last_rows)
    up_part = outer(ffn_all, after(grad_up, first_total, *last_rows), width // 4, BF16)
    up_grad = lax.all_to_all(up_part, "items", 0, 1, tiled=True).astype(F32)
    last_total = total_of(last_frames).astype(BF16)
    last_placed = spread_on(last_total, "frames")
    down_grad = outer(
        after(hidden, up_part, last_total),
        low_all,
        256 if hidden_shard % 256 == 0 else hidden_shard,
        F32,
    )
    placed = first_placed + last_placed
    key_grad, value_grad, out_grad = pl.pallas_call(
        functools.partial(
            place_kernel, chunks=CHUNKS, frames=frame_size, items=items, groups=groups
        ),
        in_specs=[smem] + [whole] * len(placed),
        out_specs=[whole] * 3,
        out_shape=[struct((frame_size, shard // frame_size, width), F32)] * 3,
        cost_estimate=short,
        compiler_params=params,
    )(flags, *placed)

    payload_part = after(payload_part, hidden)
    payload_others = spread_on(payload_part.astype(BF16), "frames")[1:]
    sums = lax.all_gather(
        total_of([payload_part] + payload_others), "items", axis=0, tiled=True
    )
    query_low = sums[lats : 2 * lats].astype(BF16)
    query_grad = transposed_left(lat_cols, query_low)
    norm_cols = transposed_right(query_low, query_weight)
    latents_grad, lat_gain, lat_bias = pl.pallas_call(
        functools.partial(query_norm_kernel, devices=item_size, items=items),
        in_specs=[smem] + [whole] * (item_size + 3),
        out_specs=[whole] * 3,
        out_shape=[struct((lats, width), F32), struct((1, width), F32), struct((1, width), F32)],
        scratch_shapes=[pltpu.VMEM((item_size, lats, shard), F32)],
        cost_estimate=short,
        compiler_params=params,
    )(flags, *spread_across(norm_cols, "items"), latents, latent_gain[None], sums)
    at = 2 * lats
    column_sums = lax.dynamic_slice_in_dim(
        sums[at + 8 : at + 24], item_index * shard, shard, 1
    )

    result = mid_rows + total_of([result_pieces[d] for d in range(item_size)])
    return (
        result.reshape(items, row_total, width),
        entropy,
        media_grad.reshape(media.shape),
        latents_grad,
        column_sums[:frame_total],
        column_sums[8],
        column_sums[9],
        lat_gain[0],
        lat_bias[0],
        sums[at],
        sums[at + 1],
        query_grad,
        key_grad.reshape(shard, width),
        value_grad.reshape(shard, width),
        out_grad.reshape(shard, width),
        up_grad,
        down_grad,
    )


def solution(mesh):
    return jax.shard_map(
        body,
        mesh=mesh,
        in_specs=(
            P("items", "frames", None, None),
            P("items", "frames", None),
            P(),
            P(),
            P(),
            P(),
            P(),
            P(),
            P(),
            P(),
            P(),
            P(),
            P("items", None),
            P("items", None),
            P("items", None),
            P("items", None),
            P("items", None),
            P("items", None),
        ),
        out_specs=(
            P("items", "frames", None),
            P("items", "frames"),
            P("items", "frames", None, None),
            P(),
            P(None, "items"),
            P("items"),
            P("items"),
            P(),
            P(),
            P(),
            P(),
            P("items", None),
            P("items", None),
            P("items", None),
            P("items", None),
            P("items", None),
            P("items", None),
        ),
        check_vma=False,
    )
```

```python
import functools
import math

import jax
import jax.numpy as jnp
from jax import lax
from jax.experimental import pallas as pl
from jax.experimental.pallas import tpu as pltpu
from jax.sharding import PartitionSpec as P

HEADS = 16
GROUP = 4
CHUNKS = 2
LANES = 128
EPSILON = 1e-05
MASKED = -1e30
F32 = jnp.float32
BF16 = jnp.bfloat16
HIGHEST = lax.Precision.HIGHEST


def layer_norm(inputs, norm_gain, norm_bias):
    center = inputs - jnp.mean(inputs, axis=-1, keepdims=True)
    spread = jnp.mean(center * center, axis=-1, keepdims=True)
    return center * lax.rsqrt(spread + EPSILON) * norm_gain + norm_bias


def matmul(left_side, right_side):
    return jnp.dot(left_side, right_side, preferred_element_type=F32)


def transposed_left(left_side, right_side):
    return lax.dot_general(
        left_side, right_side, (((0,), (0,)), ((), ())), preferred_element_type=F32
    )


def transposed_right(left_side, right_side):
    return lax.dot_general(
        left_side, right_side, (((1,), (1,)), ((), ())), preferred_element_type=F32
    )


def send_on(x, axis, step):
    size = lax.axis_size(axis)
    return lax.ppermute(x, axis, [(i, (i + step) % size) for i in range(size)])


def send_across(x, axis, distance):
    return lax.ppermute(x, axis, [(i, i ^ distance) for i in range(lax.axis_size(axis))])


def spread_on(x, axis):
    return [x] + [send_on(x, axis, s) for s in range(1, lax.axis_size(axis))]


def spread_across(x, axis):
    chips = [x] + [send_across(x, axis, d) for d in range(2, lax.axis_size(axis), 2)]
    return [b for block in chips for b in (block, send_across(block, axis, 1))]


def collect_across(pieces, axis):
    return [pieces[0]] + [send_across(p, axis, d) for d, p in enumerate(pieces) if d]


def total_of(pieces):
    return functools.reduce(jnp.add, [p.astype(F32) for p in pieces])


def after(x, *earlier):
    return lax.optimization_barrier((x,) + earlier)[0]


def split_terms(x):
    high = x.astype(BF16)
    rest = x - high.astype(F32)
    middle = rest.astype(BF16)
    return high, middle, (rest - middle.astype(F32)).astype(BF16)


def iota(shape, dim):
    return lax.broadcasted_iota(jnp.int32, shape, dim)


def head_masks(rows, width, head_size):
    lane = iota((rows, width), 1)
    return [
        jnp.logical_and(lane >= h * head_size, lane < (h + 1) * head_size)
        for h in range(width // head_size)
    ]


def spread_heads(block, masks):
    return jnp.concatenate([jnp.where(m, block, jnp.zeros_like(block)) for m in masks], 0)


def collect_heads(block, masks):
    rows = block.shape[0] // len(masks)
    total = jnp.where(masks[0], block[:rows], 0.0)
    for h in range(1, len(masks)):
        total = total + jnp.where(masks[h], block[h * rows : (h + 1) * rows], 0.0)
    return total


def head_expand(width, head_size):
    row, column = iota((LANES, width), 0), iota((LANES, width), 1)
    return jnp.logical_and(column >= row * head_size, column < (row + 1) * head_size).astype(F32)


def live_rows(flag_ref, item, items, patches, lats, columns):
    row = iota((patches + lats, columns), 0)
    media = jnp.logical_and(row < patches, flag_ref[item] > 0)
    return jnp.logical_or(media, jnp.logical_and(row >= patches, flag_ref[items] > 0))


def pack_shape(own, shard, width):
    unit = math.gcd(own, shard)
    return unit, width * unit // shard


def join_kernel(key_ref, value_ref, cotangent_ref, out_ref, low_ref, *, width):
    for g in range(key_ref.shape[1] // width):
        columns = slice(g * width, (g + 1) * width)
        out_ref[:, 2 * g * width : (2 * g + 1) * width] = key_ref[:, columns]
        out_ref[:, (2 * g + 1) * width : (2 * g + 2) * width] = value_ref[:, columns]
    low = cotangent_ref[...].astype(BF16)
    low_ref[...] = low
    own, span = low.shape
    unit, piece = pack_shape(own, out_ref.shape[0], span)
    for a in range(own // unit):
        for b in range(span // piece):
            at = 2 * span + a * piece
            out_ref[b * unit : (b + 1) * unit, at : at + piece] = low[
                a * unit : (a + 1) * unit, b * piece : (b + 1) * piece
            ]


def norm_kernel(media_ref, time_ref, gain_ref, bias_ref, lat_ref, out_ref, *, steps, per_item):
    step = pl.program_id(0)

    @pl.when(step < steps)
    def _():
        rows = media_ref[...].astype(F32) + time_ref[pl.ds(step // per_item, 1), :]
        out_ref[...] = layer_norm(rows, gain_ref[...], bias_ref[...]).astype(BF16)

    @pl.when(step == steps)
    def _():
        out_ref[...] = lat_ref[...]


def forward_kernel(
    flag_ref, both_ref, query_ref, top_ref, *refs, items, patches, scale, head_size, heads,
):
    message_refs, (part_ref, mark_ref) = refs[:-2], refs[-2:]
    lats, width = query_ref.shape
    frames = len(message_refs)
    own = message_refs[0].shape[0]
    row_total = own // items
    masks = head_masks(lats, width, head_size)
    queries = spread_heads(query_ref[...].astype(F32), masks).astype(BF16)
    base = items * patches
    lat_both = both_ref[base : base + lats, :]
    group = pl.program_id(0)
    term, lane = iota((16, GROUP * LANES), 0), iota((16, GROUP * LANES), 1)
    place = jnp.logical_and(
        lane % LANES == term * heads + group * GROUP + lane // LANES, term < 9
    ).astype(BF16)
    for i in range(items):
        both = jnp.concatenate([both_ref[i * patches : (i + 1) * patches, :], lat_both], 0)
        live = live_rows(flag_ref, i, items, patches, lats, queries.shape[0])
        scores = scale * transposed_right(both[:, :width], queries)
        masked = jnp.where(live, scores, MASKED)
        top = jnp.max(masked, axis=0, keepdims=True)
        block_exp = jnp.where(live, jnp.exp(masked - top), 0.0)
        total = jnp.sum(block_exp, axis=0, keepdims=True)
        moment = jnp.sum(block_exp * scores, axis=0, keepdims=True)
        part = transposed_left(block_exp.astype(BF16), both[:, width:])
        part_ref[i] = collect_heads(part, masks)
        top_ref[0, i] = jnp.broadcast_to(top, top_ref.shape[2:])
        terms = jnp.concatenate(
            [t.astype(F32) for x in (top, total, moment) for t in split_terms(x)]
            + [jnp.zeros((7, top.shape[1]), F32)],
            0,
        ).astype(BF16)
        wide = transposed_left(terms, place)
        mark = wide[:lats, :LANES]
        for h in range(1, GROUP):
            mark = mark + wide[h * lats : (h + 1) * lats, h * LANES : (h + 1) * LANES]
        mark_ref[i] = mark

    end = message_refs[0].shape[1] - LANES
    for s, message_ref in enumerate(message_refs):
        start = pl.multiple_of(lax.rem(flag_ref[items + 1] + s, frames) * row_total, row_total)
        rows = pl.ds(start, row_total)
        block = jnp.concatenate([part_ref[i, rows, :] for i in range(items)], 0).astype(BF16)
        mark = jnp.concatenate([mark_ref[i, rows, :] for i in range(items)], 0).astype(BF16)
        for g in range(end // width):

            @pl.when(group == g)
            def _():
                message_ref[:, g * width : (g + 1) * width] = block
                if g == 0:
                    message_ref[:, end:] = mark
                else:
                    message_ref[:, end:] = message_ref[:, end:] + mark


def merge_kernel(*refs, chunks, frames, items, head_size, heads):
    message_refs = refs[: chunks * frames]
    base_ref, weight_ref, gain_ref, bias_ref = refs[chunks * frames : chunks * frames + 4]
    merged_ref, mid_ref, ffn_ref, log_ref, entropy_ref = refs[chunks * frames + 4 :]
    own, columns = message_refs[0].shape
    half = columns - LANES
    lane, column = iota((LANES, 3 * LANES), 0), iota((LANES, 3 * LANES), 1)
    gather = jnp.logical_and(
        jnp.logical_and(lane // heads // 3 == column // LANES, lane % heads == column % LANES),
        lane < 9 * heads,
    ).astype(BF16)
    expand = head_expand(half, head_size)
    live = iota((own, LANES), 1) < heads
    spread = jnp.zeros((own, LANES), F32)
    for c in range(chunks):
        sources = message_refs[c * frames : (c + 1) * frames]
        stats = [matmul(x[:, half:], gather) for x in sources]
        tops = [x[:, :LANES] for x in stats]
        peak = functools.reduce(jnp.maximum, tops)
        factors = [jnp.exp(t - peak) for t in tops]
        whole = sum(f * x[:, LANES : 2 * LANES] for f, x in zip(factors, stats))
        moment = sum(f * x[:, 2 * LANES :] for f, x in zip(factors, stats))
        whole = jnp.where(live, whole, 1.0)
        log_total = jnp.where(live, peak + jnp.log(whole), 0.0)
        log_ref[c] = log_total
        spread = spread + jnp.where(live, log_total - moment / whole, 0.0)
        merged = jnp.zeros((own, half), F32)
        for x, factor in zip(sources, factors):
            share = jnp.where(live, factor / whole, 0.0)
            wide = jnp.dot(share, expand, precision=HIGHEST, preferred_element_type=F32)
            merged = merged + x[:, :half].astype(F32) * wide
        merged_ref[:, c * half : (c + 1) * half] = merged
    entropy_ref[...] = jnp.broadcast_to(
        jnp.sum(spread, axis=1, keepdims=True) * (1.0 / HEADS), entropy_ref.shape
    )
    base = jnp.concatenate([base_ref[...]] * items, 0)
    mid = base + matmul(merged_ref[...].astype(BF16), weight_ref[...])
    mid_ref[...] = mid
    ffn_ref[...] = layer_norm(mid, gain_ref[...], bias_ref[...]).astype(BF16)


def gelu_parts(x):
    share = 0.5 * (1.0 + lax.erf(x * (0.5**0.5)))
    slope = share + x * jnp.exp(-0.5 * x * x) * ((2.0 * jnp.pi) ** -0.5)
    return x * share, slope


def feed_kernel(flag_ref, *refs, devices, items):
    row_refs = refs[:devices]
    low_ref, up_ref, down_ref, result_ref = refs[devices : devices + 4]
    grad_refs, (plane_ref, plane_low_ref) = refs[devices + 4 : -2], refs[-2:]
    own, width = row_refs[0].shape
    shard = low_ref.shape[0] // devices
    unit, piece = pack_shape(own, shard, width)
    me = flag_ref[2 * items + 2]
    for d in range(devices):
        plane_ref[d * own : (d + 1) * own, :] = row_refs[d][...]
        source = jnp.bitwise_xor(me, d) * shard
        for a in range(own // unit):
            rows = slice(d * own + a * unit, d * own + (a + 1) * unit)
            for b in range(shard // unit):
                start = pl.multiple_of(source + b * unit, unit)
                plane_low_ref[rows, b * piece : (b + 1) * piece] = low_ref[
                    pl.ds(start, unit), a * piece : (a + 1) * piece
                ]
    upward = matmul(plane_ref[...], up_ref[...])
    hidden, slope = gelu_parts(upward)
    grad_up = (slope * transposed_right(plane_low_ref[...], down_ref[...])).astype(BF16)
    grad = transposed_right(grad_up, up_ref[...]).astype(BF16)
    result = matmul(hidden.astype(BF16), down_ref[...]).astype(BF16)
    for d in range(devices):
        grad_refs[d][...] = grad[d * own : (d + 1) * own, :]
        result_ref[jnp.bitwise_xor(me, d)] = result[d * own : (d + 1) * own, :]


def feed_back_kernel(row_ref, low_ref, up_ref, down_ref, hidden_ref, grad_ref):
    hidden, slope = gelu_parts(matmul(row_ref[...], up_ref[...]))
    hidden_ref[...] = hidden.astype(BF16)
    grad_ref[...] = (slope * transposed_right(low_ref[...], down_ref[...])).astype(BF16)


def outer_kernel(left_ref, right_ref, out_ref):
    out_ref[...] = transposed_left(left_ref[...], right_ref[...]).astype(out_ref.dtype)


def norm_backward(rows, gain, gradient):
    center = rows - jnp.mean(rows, axis=1, keepdims=True)
    rate = lax.rsqrt(jnp.mean(center * center, axis=1, keepdims=True) + EPSILON)
    unit = center * rate
    scaled = gradient * gain
    inner = scaled - jnp.mean(scaled, axis=1, keepdims=True)
    back = rate * (inner - unit * jnp.mean(scaled * unit, axis=1, keepdims=True))
    return (
        back,
        jnp.sum(gradient * unit, axis=0, keepdims=True),
        jnp.sum(gradient, axis=0, keepdims=True),
    )


def turn_kernel(*refs, devices, items, chunks, head_size, heads):
    part_refs = refs[:devices]
    mid_ref, cotangent_ref, gain_ref, merged_ref, log_ref, weight_ref = refs[
        devices : devices + 6
    ]
    message_ref, branch_ref, base_ref, sums_ref = refs[devices + 6 :]
    own, width = mid_ref.shape
    half = width // chunks
    gradient = total_of([x[...] for x in part_refs])
    back, gain_sum, bias_sum = norm_backward(mid_ref[...], gain_ref[...], gradient)
    grad_mid = cotangent_ref[...] + back
    sums_ref[...] = jnp.zeros(sums_ref.shape, F32)
    sums_ref[0:1, :] = gain_sum
    sums_ref[1:2, :] = bias_sum
    row_total = own // items
    base_ref[...] = total_of(
        [grad_mid[i * row_total : (i + 1) * row_total] for i in range(items)]
    )
    branch = grad_mid.astype(BF16)
    branch_ref[:, :width] = branch
    branch_ref[:, width:] = merged_ref[...].astype(BF16)
    grad_att = transposed_right(branch, weight_ref[...]).astype(BF16)
    expand = head_expand(half, head_size)
    lane, column = iota((6 * LANES, LANES), 0), iota((6 * LANES, LANES), 1)
    place = jnp.logical_and(
        lane % LANES < heads, column == (lane // LANES) * heads + lane % LANES
    ).astype(BF16)
    message_ref[:, :width] = grad_att
    for c in range(chunks):
        columns = slice(c * half, (c + 1) * half)
        delta = lax.dot_general(
            merged_ref[:, columns] * grad_att[:, columns].astype(F32),
            expand,
            (((1,), (1,)), ((), ())),
            precision=HIGHEST,
            preferred_element_type=F32,
        )
        terms = jnp.concatenate([t for x in (log_ref[c], delta) for t in split_terms(x)], 1)
        message_ref[:, width + c * LANES : width + (c + 1) * LANES] = matmul(
            terms, place
        ).astype(BF16)


def backward_kernel(
    *refs, frames, items, patches, scale, head_size, heads,
):
    flag_ref, both_ref, query_ref, top_ref = refs[:4]
    grad_refs = refs[4 : 4 + frames]
    mark_refs = refs[4 + frames : 4 + 2 * frames]
    out_ref, sum_ref, held_ref, note_ref = refs[4 + 2 * frames :]
    lats, width = query_ref.shape
    own = grad_refs[0].shape[0]
    row_total = own // items
    base = items * patches
    for s in range(frames):
        source = lax.rem(flag_ref[items + 1] + (frames - s), frames)
        rows = pl.ds(pl.multiple_of(source * row_total, row_total), row_total)
        block = grad_refs[s][...].astype(F32)
        mark = mark_refs[s][...].astype(F32)
        for i in range(items):
            held_ref[i, rows, :] = block[i * row_total : (i + 1) * row_total]
            note_ref[i, rows, :] = mark[i * row_total : (i + 1) * row_total]
    masks = head_masks(lats, width, head_size)
    queries = spread_heads(query_ref[...].astype(F32), masks).astype(BF16)
    lat_both = both_ref[base : base + lats, :]
    row, lane = iota((GROUP * 8, LANES), 0), iota((GROUP * 8, LANES), 1)
    pick = jnp.logical_and(
        jnp.logical_and(
            lane // heads // 3 == row % 8,
            lane % heads == pl.program_id(0) * GROUP + row // 8,
        ),
        lane < 6 * heads,
    ).astype(BF16)
    grad_query = jnp.zeros((queries.shape[0], width), F32)
    lat_grad_key = jnp.zeros((lats, width), F32)
    lat_grad_value = jnp.zeros((lats, width), F32)
    for i in range(items):
        rows = slice(i * patches, (i + 1) * patches)
        stats = transposed_right(pick, note_ref[i].astype(BF16))
        stats = jnp.concatenate([stats[h * 8 : (h + 1) * 8] for h in range(GROUP)], 1)
        log_total = stats[0:1]
        delta = stats[1:2]
        top = top_ref[0, i, 0:1, :]
        rescale = jnp.exp(top - log_total)
        both = jnp.concatenate([both_ref[rows, :], lat_both], 0)
        keys, values = both[:, :width], both[:, width:]
        grads = spread_heads(held_ref[i], masks).astype(BF16)
        live = live_rows(flag_ref, i, items, patches, lats, queries.shape[0])
        masked = jnp.where(live, scale * transposed_right(keys, queries), MASKED)
        probs = jnp.where(live, jnp.exp(masked - log_total), 0.0)
        block_exp = jnp.where(live, jnp.exp(masked - top), 0.0)
        weights = (block_exp.astype(BF16).astype(F32) * rescale).astype(BF16)
        grad_scores = (probs * (transposed_right(values, grads) - delta)).astype(BF16)
        grad_key = scale * matmul(grad_scores, queries)
        grad_value = matmul(weights, grads)
        out_ref[rows, :width] = grad_key[:patches].astype(BF16)
        out_ref[rows, width:] = grad_value[:patches].astype(BF16)
        grad_query = grad_query + transposed_left(grad_scores, keys)
        lat_grad_key = lat_grad_key + grad_key[patches:]
        lat_grad_value = lat_grad_value + grad_value[patches:]
    out_ref[base : base + lats, :width] = lat_grad_key.astype(BF16)
    out_ref[base : base + lats, width:] = lat_grad_value.astype(BF16)
    sum_ref[...] = scale * collect_heads(grad_query, masks)


def media_kernel(flag_ref, *refs, chunks, items, frames):
    grad_refs, lat_refs, weight_refs = [
        refs[k * chunks : (k + 1) * chunks] for k in range(3)
    ]
    media_ref, time_ref, gain_ref, out_ref, sums_ref, product_ref = refs[3 * chunks :]
    item = pl.program_id(0)

    @pl.when(item == 0)
    def _():
        sums_ref[...] = jnp.zeros(sums_ref.shape, F32)
        product_ref[...] = functools.reduce(
            jnp.add, [transposed_right(g[...], w[...]) for g, w in zip(lat_refs, weight_refs)]
        )

    gradient = functools.reduce(
        jnp.add, [transposed_right(g[...], w[...]) for g, w in zip(grad_refs, weight_refs)]
    )
    inputs = media_ref[...].astype(F32) + time_ref[pl.ds(item, 1), :]
    back, gain_sum, bias_sum = norm_backward(inputs, gain_ref[...], gradient)
    out_ref[...] = back.astype(BF16)
    place = iota((frames, 1), 0) == flag_ref[items + 2 + item]
    sums_ref[0:frames, :] += jnp.where(place, jnp.sum(back, axis=0, keepdims=True), 0.0)
    sums_ref[8:9, :] += gain_sum
    sums_ref[9:10, :] += bias_sum


def latent_kernel(flag_ref, *refs, chunks, items):
    query_refs = refs[:chunks]
    (
        product_ref, latent_ref, gain_ref, base_ref, ffn_ref, media_ref, out_ref,
    ) = refs[chunks:]
    lats, width = latent_ref.shape
    half = width // chunks
    gradient = product_ref[...]
    for c in range(chunks):
        out_ref[lats : 2 * lats, c * half : (c + 1) * half] = query_refs[c][...]
    back, gain_sum, bias_sum = norm_backward(latent_ref[...], gain_ref[...], gradient)
    out_ref[:lats, :] = back
    row_total = base_ref.shape[0]
    start = pl.multiple_of(flag_ref[items + 1] * row_total, row_total)
    out_ref[pl.ds(start, row_total), :] += base_ref[...]
    at = 2 * lats
    out_ref[at : at + 8, :] = ffn_ref[...]
    out_ref[at + 2 : at + 3, :] = gain_sum
    out_ref[at + 3 : at + 4, :] = bias_sum
    out_ref[at + 8 : at + 24, :] = media_ref[...]
    out_ref[at + 24 :, :] = jnp.zeros((out_ref.shape[0] - at - 24, width), F32)


def query_norm_kernel(flag_ref, *refs, devices, items):
    column_refs = refs[:devices]
    latent_ref, gain_ref, sum_ref, out_ref, out_gain_ref, out_bias_ref, held_ref = refs[devices:]
    for d in range(devices):
        held_ref[jnp.bitwise_xor(flag_ref[2 * items + 2], d)] = column_refs[d][...]
    gradient = jnp.concatenate([held_ref[k] for k in range(devices)], 1)
    back, gain_sum, bias_sum = norm_backward(latent_ref[...], gain_ref[...], gradient)
    lats = latent_ref.shape[0]
    out_ref[...] = sum_ref[:lats, :] + back
    out_gain_ref[...] = sum_ref[2 * lats + 2 : 2 * lats + 3, :] + gain_sum
    out_bias_ref[...] = sum_ref[2 * lats + 3 : 2 * lats + 4, :] + bias_sum


def rows_kernel(flag_ref, *refs, count, frames, items):
    part_refs, out_refs, held_ref = refs[:count], refs[count:-1], refs[-1]
    rows = held_ref.shape[1]
    column = 0
    for part_ref in part_refs:
        total = total_of([part_ref[k] for k in range(part_ref.shape[0])])
        for f in range(frames):
            held_ref[f, :, column : column + total.shape[1]] = total[f * rows : (f + 1) * rows]
        column += total.shape[1]
    for s, out_ref in enumerate(out_refs):
        block = held_ref[lax.rem(flag_ref[items + 1] + s, frames)]
        out_ref[...] = block.astype(out_ref.dtype)


def place_kernel(flag_ref, *refs, chunks, frames, items, groups):
    chunk_refs = refs[: chunks * frames]
    key_ref, value_ref, out_ref = refs[chunks * frames :]
    width = key_ref.shape[2] // (chunks * groups)
    for s in range(frames):
        source = lax.rem(flag_ref[items + 1] + (frames - s), frames)
        out_ref[source] = chunk_refs[s][:, 2 * groups * width :].astype(F32)
        for c in range(chunks):
            for g in range(groups):
                at = (c * groups + g) * width
                block = chunk_refs[c * frames + s][:, 2 * g * width : 2 * (g + 1) * width]
                block = block.astype(F32)
                key_ref[source, :, at : at + width] = block[:, :width]
                value_ref[source, :, at : at + width] = block[:, width:]


def body(
    media,
    cotangent,
    frame_count,
    frame_start,
    latents,
    time_embed,
    media_gain,
    media_bias,
    latent_gain,
    latent_bias,
    ffn_gain,
    ffn_bias,
    query_weight,
    key_weight,
    value_weight,
    out_weight,
    up_weight,
    down_weight,
):
    items = media.shape[0]
    patches = media.shape[2]
    width = media.shape[3]
    lats = latents.shape[0]
    frame_total = time_embed.shape[0]
    row_total = cotangent.shape[1]
    own = items * row_total
    head_size = width // HEADS
    half = width // CHUNKS
    chunk_heads = HEADS // CHUNKS
    group_width = GROUP * head_size
    groups = chunk_heads // GROUP
    stack = GROUP * lats
    tokens = items * patches
    all_tokens = tokens + lats
    shard = query_weight.shape[0]
    hidden_shard = down_weight.shape[0]
    item_size = lax.axis_size("items")
    frame_size = lax.axis_size("frames")
    plane = item_size * own
    item_index = lax.axis_index("items")
    slot = lax.axis_index("frames")
    row_base = slot * row_total
    params = pltpu.CompilerParams(vmem_limit_bytes=56 * 2**20)
    smem = pl.BlockSpec(memory_space=pltpu.SMEM)
    whole = pl.BlockSpec(memory_space=pltpu.VMEM)
    sizes = dict(items=items, head_size=head_size, heads=chunk_heads)

    def struct(shape, kind):
        return jax.ShapeDtypeStruct(shape, kind)

    def cost(micros):
        return pl.CostEstimate(
            flops=int(micros * 1.15e9), bytes_accessed=int(micros * 3.6e6), transcendentals=0
        )

    def column_blocks(x):
        return jnp.transpose(x.reshape(-1, item_size, shard), (1, 0, 2))

    def scatter_exchange(x, axis):
        return jnp.sum(lax.all_to_all(x, axis, 0, 0).astype(F32), axis=0)

    grad_out = cotangent.reshape(own, width)
    low_columns = own * width // shard
    joined, grad_low = pl.pallas_call(
        functools.partial(join_kernel, width=group_width),
        out_shape=[struct((shard, 2 * width + low_columns), BF16), struct((own, width), BF16)],
        cost_estimate=cost(2.5),
        compiler_params=params,
    )(key_weight, value_weight, grad_out)
    kv_full = lax.all_gather(joined, "items", axis=0, tiled=True)
    low_frames = jnp.stack(spread_on(grad_low, "frames"))

    lat_norm = layer_norm(latents, latent_gain, latent_bias).astype(BF16)
    lat_cols = lax.dynamic_slice_in_dim(lat_norm, item_index * shard, shard, 1)
    query_blocks = column_blocks(matmul(lat_cols, query_weight))
    query_cols = scatter_exchange(query_blocks, "items").astype(BF16)
    query_spread = jnp.broadcast_to(query_cols[None], (item_size, lats, shard))
    queries = jnp.transpose(lax.all_to_all(query_spread, "items", 0, 0), (1, 0, 2)).reshape(
        lats, width
    )

    counts = lax.dynamic_slice_in_dim(frame_count, item_index * items, items)
    starts = lax.dynamic_slice_in_dim(frame_start, item_index * items, items)
    offset = (slot - starts) % frame_total
    flags = jnp.concatenate(
        [
            (offset < counts).astype(jnp.int32),
            (slot == 0).astype(jnp.int32)[None],
            slot.astype(jnp.int32)[None],
            offset.astype(jnp.int32),
            item_index.astype(jnp.int32)[None],
        ]
    )
    picker = (offset[:, None] == jnp.arange(frame_total, dtype=jnp.int32)[None, :]).astype(F32)
    time_rows = jnp.dot(picker, time_embed, precision=HIGHEST, preferred_element_type=F32)
    flat_media = media.reshape(tokens, width)
    steps = tokens // lats
    all_rows = pl.pallas_call(
        functools.partial(norm_kernel, steps=steps, per_item=patches // lats),
        grid=(steps + 1,),
        in_specs=[
            pl.BlockSpec((lats, width), lambda i: (jnp.minimum(i, steps - 1), 0)),
            whole,
            whole,
            whole,
            whole,
        ],
        out_specs=pl.BlockSpec((lats, width), lambda i: (i, 0)),
        out_shape=struct((all_tokens, width), BF16),
        cost_estimate=cost(12),
        compiler_params=params,
    )(
        after(flat_media, query_blocks),
        time_rows,
        media_gain[None],
        media_bias[None],
        lat_norm,
    )
    out_full = lax.all_gather(after(out_weight, all_rows), "items", axis=0, tiled=True)

    core = item_index % 2
    rows_across = after(all_rows, query_cols).T.reshape(item_size // 2, 2, shard, all_tokens)
    send_rows, keep_rows = [
        jnp.concatenate(
            [
                lax.dynamic_slice(
                    rows_across, (k, which, 0, 0), (1, 1, shard, all_tokens)
                ).reshape(shard, all_tokens)
                for k in range(item_size // 2)
            ],
            0,
        )
        for which in (1 - core, core)
    ]
    boths, tops, messages = [], [], []
    for c in range(CHUNKS):

        def block_of(g, c=c):
            return (0, c * groups + g)

        if c:
            rows = after(all_rows, tops[-1])
        else:
            rows = after(all_rows, queries, send_rows, keep_rows)
        both = matmul(rows, kv_full[:, 2 * c * half : 2 * (c + 1) * half]).astype(BF16)
        top, *parts = pl.pallas_call(
            functools.partial(
                forward_kernel, patches=patches, scale=head_size**-0.5, **sizes
            ),
            grid=(groups,),
            in_specs=[
                smem,
                pl.BlockSpec((all_tokens, 2 * group_width), lambda g: (0, g)),
                pl.BlockSpec((lats, group_width), block_of),
            ],
            out_specs=[pl.BlockSpec((1, items, 8, stack), lambda g: (g, 0, 0, 0))]
            + [pl.BlockSpec((own, half + LANES), lambda g: (0, 0))] * frame_size,
            out_shape=[struct((groups, items, 8, stack), F32)]
            + [struct((own, half + LANES), BF16)] * frame_size,
            scratch_shapes=[
                pltpu.VMEM((items, lats, group_width), F32),
                pltpu.VMEM((items, lats, LANES), F32),
            ],
            cost_estimate=cost(7.8),
            compiler_params=params,
        )(flags, both, queries)
        boths.append(both)
        tops.append(top)
        messages += [p if s == 0 else send_on(p, "frames", s) for s, p in enumerate(parts)]
    up_slice = lax.all_to_all(after(up_weight, boths[0]), "items", 1, 0, tiled=True)
    low_all = lax.all_gather(after(low_frames, tops[1]), "items", axis=0).reshape(-1, width)

    base_rows = lax.dynamic_slice_in_dim(latents, row_base, row_total, 0)
    merged, mid_rows, ffn_in, logs, entropy_wide = pl.pallas_call(
        functools.partial(merge_kernel, chunks=CHUNKS, frames=frame_size, **sizes),
        out_shape=[
            struct((own, width), F32),
            struct((own, width), F32),
            struct((own, width), BF16),
            struct((CHUNKS, own, LANES), F32),
            struct((own, LANES), F32),
        ],
        cost_estimate=cost(6.3),
        compiler_params=params,
    )(*messages, base_rows, out_full, ffn_gain[None], ffn_bias[None])
    entropy = entropy_wide[:, 0].reshape(items, row_total)

    ffn_blocks = spread_across(ffn_in, "items")
    ffn_frames = spread_on(after(ffn_in, *ffn_blocks), "frames")
    result_part, *parts = pl.pallas_call(
        functools.partial(feed_kernel, devices=item_size, items=items),
        grid=(1,),
        in_specs=[smem]
        + [whole] * item_size
        + [
            pl.BlockSpec((width, low_columns), lambda i: (0, 2 * width // low_columns)),
            whole,
            whole,
        ],
        out_specs=[whole] * (1 + item_size),
        out_shape=[struct((item_size, own, width), BF16)]
        + [struct((own, width), BF16)] * item_size,
        scratch_shapes=[pltpu.VMEM((plane, width), BF16)] * 2,
        cost_estimate=cost(10),
        compiler_params=params,
    )(flags, *ffn_blocks, kv_full, up_slice, down_weight)
    grad_blocks = collect_across(parts, "items")
    grad_blocks[0] = after(grad_blocks[0], *ffn_frames)

    turn, grad_branch, grad_base, ffn_sums = pl.pallas_call(
        functools.partial(turn_kernel, devices=item_size, chunks=CHUNKS, **sizes),
        out_shape=[
            struct((own, width + CHUNKS * LANES), BF16),
            struct((own, 2 * width), BF16),
            struct((row_total, width), F32),
            struct((8, width), F32),
        ],
        cost_estimate=cost(7.6),
        compiler_params=params,
    )(*grad_blocks, mid_rows, grad_out, ffn_gain[None], merged, logs, out_full)
    turns = spread_on(turn, "frames")
    branch_plane = lax.all_gather(grad_branch, "items", axis=0, tiled=True)
    ffn_all = lax.all_gather(
        after(jnp.stack(ffn_frames), grad_branch), "items", axis=0
    ).reshape(-1, width)
    att_plane = lax.dynamic_slice_in_dim(
        branch_plane, width + item_index * shard, shard, 1
    )
    turns[0] = after(turns[0], low_all)

    chunk_grads, chunk_queries = [], []

    def weight_terms(c):
        send = matmul(send_rows, chunk_grads[c]).astype(BF16)
        received = send_across(send, "items", 1).reshape(-1, shard, 2 * half)
        keep = matmul(after(keep_rows, send), chunk_grads[c]).astype(BF16)
        return send, keep.reshape(-1, shard, 2 * half), received

    def chip_terms(keep, received):
        return (keep.astype(F32) + received.astype(F32)).astype(BF16)

    def exchange_chips(x):
        groups_of = [list(range(k, item_size, 2)) for k in range(2)]
        return lax.all_to_all(x, "items", 0, 0, axis_index_groups=groups_of)

    def frame_rows(ranges):
        rows = shard // frame_size
        columns = sum(x.shape[-1] for x in ranges)
        return pl.pallas_call(
            functools.partial(rows_kernel, count=len(ranges), frames=frame_size, items=items),
            in_specs=[smem] + [whole] * len(ranges),
            out_specs=[whole] * frame_size,
            out_shape=[struct((rows, columns), F32)]
            + [struct((rows, columns), BF16)] * (frame_size - 1),
            scratch_shapes=[pltpu.VMEM((frame_size, rows, columns), F32)],
            cost_estimate=cost(3.5),
            compiler_params=params,
        )(flags, *ranges)

    def send_rows_on(rows):
        return [rows[0]] + [send_on(p, "frames", s) for s, p in enumerate(rows) if s]

    for c in range(CHUNKS):

        def block_of(g, c=c):
            return (0, c * groups + g)

        chunk_grad, chunk_query = pl.pallas_call(
            functools.partial(
                backward_kernel, frames=frame_size, patches=patches, scale=head_size**-0.5, **sizes
            ),
            grid=(groups,),
            in_specs=[
                smem,
                pl.BlockSpec((all_tokens, 2 * group_width), lambda g: (0, g)),
                pl.BlockSpec((lats, group_width), block_of),
                pl.BlockSpec((1, items, 8, stack), lambda g: (g, 0, 0, 0)),
            ]
            + [pl.BlockSpec((own, group_width), block_of)] * frame_size
            + [pl.BlockSpec((own, LANES), lambda g, c=c: (0, width // LANES + c))] * frame_size,
            out_specs=[
                pl.BlockSpec((all_tokens, 2 * group_width), lambda g: (0, g)),
                pl.BlockSpec((lats, group_width), lambda g: (0, g)),
            ],
            out_shape=[
                struct((all_tokens, 2 * half), BF16),
                struct((lats, half), F32),
            ],
            scratch_shapes=[
                pltpu.VMEM((items, lats, group_width), F32),
                pltpu.VMEM((items, lats, LANES), F32),
            ],
            cost_estimate=cost(8),
            compiler_params=params,
        )(flags, after(boths[c], *held) if c else boths[c], queries, tops[c], *turns, *turns)
        chunk_grads.append(chunk_grad)
        chunk_queries.append(chunk_query)
        if c == 0:
            first_send, first_keep, first_received = weight_terms(0)
            result_pieces = lax.all_to_all(after(result_part, chunk_grad), "items", 0, 0)
            held = (first_send,)
    first_terms = chip_terms(after(first_keep, chunk_grads[-1]), first_received)
    first_moved = exchange_chips(after(first_terms, result_pieces))

    last_block = pl.BlockSpec((lats, 2 * half), lambda i: (tokens // lats, 0))
    media_grad, media_sums, lat_product = pl.pallas_call(
        functools.partial(media_kernel, chunks=CHUNKS, items=items, frames=frame_total),
        grid=(items,),
        in_specs=[smem]
        + [pl.BlockSpec((patches, 2 * half), lambda i: (i, 0))] * CHUNKS
        + [last_block] * CHUNKS
        + [pl.BlockSpec((width, 2 * half), lambda i, c=c: (0, c)) for c in range(CHUNKS)]
        + [pl.BlockSpec((patches, width), lambda i: (i, 0)), whole, whole],
        out_specs=[
            pl.BlockSpec((patches, width), lambda i: (i, 0)),
            pl.BlockSpec((16, width), lambda i: (0, 0)),
            pl.BlockSpec((lats, width), lambda i: (0, 0)),
        ],
        out_shape=[
            struct((tokens, width), BF16),
            struct((16, width), F32),
            struct((lats, width), F32),
        ],
        cost_estimate=cost(21),
        compiler_params=params,
    )(
        flags,
        *chunk_grads[:-1],
        after(chunk_grads[-1], first_terms, result_pieces),
        *chunk_grads,
        *[kv_full] * CHUNKS,
        flat_media,
        time_rows,
        media_gain[None],
    )

    sum_rows = 2 * lats + 24
    sum_rows += -sum_rows % (8 * item_size)
    payload = pl.pallas_call(
        functools.partial(latent_kernel, chunks=CHUNKS, items=items),
        in_specs=[smem] + [whole] * (CHUNKS + 6),
        out_specs=whole,
        out_shape=struct((sum_rows, width), F32),
        cost_estimate=cost(3),
        compiler_params=params,
    )(
        flags,
        *chunk_queries,
        after(lat_product, first_moved),
        latents,
        latent_gain[None],
        grad_base,
        ffn_sums,
        media_sums,
    )
    payload_part = lax.psum_scatter(payload, "items", scatter_dimension=0, tiled=True)

    chunk_grads[-1] = after(chunk_grads[-1], payload)
    last_send, last_keep, last_received = weight_terms(CHUNKS - 1)
    last_terms = chip_terms(after(last_keep, first_moved), last_received)
    last_moved = exchange_chips(last_terms)
    out_part = transposed_left(att_plane, after(branch_plane, last_send)[:, :width])
    first_rows = frame_rows([after(first_moved, last_terms), out_part[None]])
    first_frames = send_rows_on(first_rows)
    all_plane = plane * frame_size
    block_rows = min(512, all_plane)
    row_block = pl.BlockSpec((block_rows, width), lambda i: (i, 0))
    hidden_block = pl.BlockSpec((block_rows, hidden_shard), lambda i: (i, 0))
    hidden, grad_up = pl.pallas_call(
        feed_back_kernel,
        grid=(all_plane // block_rows,),
        in_specs=[row_block, row_block, whole, whole],
        out_specs=[hidden_block, hidden_block],
        out_shape=[struct((all_plane, hidden_shard), BF16)] * 2,
        cost_estimate=cost(15),
        compiler_params=params,
    )(after(ffn_all, *first_rows), low_all, up_slice, down_weight)

    def outer(left, right, tile, kind):
        rows, columns = left.shape
        shape = (columns, right.shape[1])
        return pl.pallas_call(
            outer_kernel,
            grid=(columns // tile,),
            in_specs=[pl.BlockSpec((rows, tile), lambda i: (0, i)), whole],
            out_specs=pl.BlockSpec((tile, shape[1]), lambda i: (i, 0)),
            out_shape=struct(shape, kind),
            cost_estimate=cost(9.5),
            compiler_params=params,
        )(left, right)

    first_total = total_of(first_frames).astype(BF16)
    first_placed = spread_on(first_total, "frames")
    last_rows = frame_rows([after(last_moved, hidden)])
    last_frames = send_rows_on(last_rows)
    up_part = outer(ffn_all, after(grad_up, first_total, *last_rows), width // 4, BF16)
    up_grad = lax.all_to_all(up_part, "items", 0, 1, tiled=True).astype(F32)
    last_total = total_of(last_frames).astype(BF16)
    last_placed = spread_on(last_total, "frames")
    down_grad = outer(
        after(hidden, up_part, last_total),
        low_all,
        256 if hidden_shard % 256 == 0 else hidden_shard,
        F32,
    )
    placed = first_placed + last_placed
    key_grad, value_grad, out_grad = pl.pallas_call(
        functools.partial(
            place_kernel, chunks=CHUNKS, frames=frame_size, items=items, groups=groups
        ),
        in_specs=[smem] + [whole] * len(placed),
        out_specs=[whole] * 3,
        out_shape=[struct((frame_size, shard // frame_size, width), F32)] * 3,
        cost_estimate=cost(3.4),
        compiler_params=params,
    )(flags, *placed)

    payload_part = after(payload_part, hidden)
    payload_others = spread_on(payload_part.astype(BF16), "frames")[1:]
    sums = lax.all_gather(
        total_of([payload_part] + payload_others), "items", axis=0, tiled=True
    )
    query_low = sums[lats : 2 * lats].astype(BF16)
    query_grad = transposed_left(lat_cols, query_low)
    norm_cols = transposed_right(query_low, query_weight)
    latents_grad, lat_gain, lat_bias = pl.pallas_call(
        functools.partial(query_norm_kernel, devices=item_size, items=items),
        in_specs=[smem] + [whole] * (item_size + 3),
        out_specs=[whole] * 3,
        out_shape=[struct((lats, width), F32), struct((1, width), F32), struct((1, width), F32)],
        scratch_shapes=[pltpu.VMEM((item_size, lats, shard), F32)],
        cost_estimate=cost(3),
        compiler_params=params,
    )(flags, *spread_across(norm_cols, "items"), latents, latent_gain[None], sums)
    at = 2 * lats
    column_sums = lax.dynamic_slice_in_dim(
        sums[at + 8 : at + 24], item_index * shard, shard, 1
    )

    result = mid_rows + total_of([result_pieces[d] for d in range(item_size)])
    return (
        result.reshape(items, row_total, width),
        entropy,
        media_grad.reshape(media.shape),
        latents_grad,
        column_sums[:frame_total],
        column_sums[8],
        column_sums[9],
        lat_gain[0],
        lat_bias[0],
        sums[at],
        sums[at + 1],
        query_grad,
        key_grad.reshape(shard, width),
        value_grad.reshape(shard, width),
        out_grad.reshape(shard, width),
        up_grad,
        down_grad,
    )


def solution(mesh):
    return jax.shard_map(
        body,
        mesh=mesh,
        in_specs=(
            P("items", "frames", None, None),
            P("items", "frames", None),
            P(),
            P(),
            P(),
            P(),
            P(),
            P(),
            P(),
            P(),
            P(),
            P(),
            P("items", None),
            P("items", None),
            P("items", None),
            P("items", None),
            P("items", None),
            P("items", None),
        ),
        out_specs=(
            P("items", "frames", None),
            P("items", "frames"),
            P("items", "frames", None, None),
            P(),
            P(None, "items"),
            P("items"),
            P("items"),
            P(),
            P(),
            P(),
            P(),
            P("items", None),
            P("items", None),
            P("items", None),
            P("items", None),
            P("items", None),
            P("items", None),
        ),
        check_vma=False,
    )
```

```python
import functools
import math

import jax
import jax.numpy as jnp
from jax import lax
from jax.experimental import pallas as pl
from jax.experimental.pallas import tpu as pltpu
from jax.sharding import PartitionSpec as P

HEADS = 16
GROUP = 4
CHUNKS = 2
LANES = 128
EPSILON = 1e-05
MASKED = -1e30
F32 = jnp.float32
BF16 = jnp.bfloat16
HIGHEST = lax.Precision.HIGHEST


def layer_norm(inputs, norm_gain, norm_bias):
    center = inputs - jnp.mean(inputs, axis=-1, keepdims=True)
    spread = jnp.mean(center * center, axis=-1, keepdims=True)
    return center * lax.rsqrt(spread + EPSILON) * norm_gain + norm_bias


def matmul(left_side, right_side):
    return jnp.dot(left_side, right_side, preferred_element_type=F32)


def transposed_left(left_side, right_side):
    return lax.dot_general(
        left_side, right_side, (((0,), (0,)), ((), ())), preferred_element_type=F32
    )


def transposed_right(left_side, right_side):
    return lax.dot_general(
        left_side, right_side, (((1,), (1,)), ((), ())), preferred_element_type=F32
    )


def send_on(x, axis, step):
    size = lax.axis_size(axis)
    return lax.ppermute(x, axis, [(i, (i + step) % size) for i in range(size)])


def send_across(x, axis, distance):
    return lax.ppermute(x, axis, [(i, i ^ distance) for i in range(lax.axis_size(axis))])


def spread_on(x, axis):
    return [x] + [send_on(x, axis, s) for s in range(1, lax.axis_size(axis))]


def spread_across(x, axis):
    chips = [x] + [send_across(x, axis, d) for d in range(2, lax.axis_size(axis), 2)]
    return [b for block in chips for b in (block, send_across(block, axis, 1))]


def collect_across(pieces, axis):
    return [pieces[0]] + [send_across(p, axis, d) for d, p in enumerate(pieces) if d]


def total_of(pieces):
    return functools.reduce(jnp.add, [p.astype(F32) for p in pieces])


def after(x, *earlier):
    return lax.optimization_barrier((x,) + earlier)[0]


def split_terms(x):
    high = x.astype(BF16)
    rest = x - high.astype(F32)
    middle = rest.astype(BF16)
    return high, middle, (rest - middle.astype(F32)).astype(BF16)


def iota(shape, dim):
    return lax.broadcasted_iota(jnp.int32, shape, dim)


def head_masks(rows, width, head_size):
    lane = iota((rows, width), 1)
    return [
        jnp.logical_and(lane >= h * head_size, lane < (h + 1) * head_size)
        for h in range(width // head_size)
    ]


def spread_heads(block, masks):
    return jnp.concatenate([jnp.where(m, block, jnp.zeros_like(block)) for m in masks], 0)


def collect_heads(block, masks):
    rows = block.shape[0] // len(masks)
    total = jnp.where(masks[0], block[:rows], 0.0)
    for h in range(1, len(masks)):
        total = total + jnp.where(masks[h], block[h * rows : (h + 1) * rows], 0.0)
    return total


def head_expand(width, head_size):
    row, column = iota((LANES, width), 0), iota((LANES, width), 1)
    return jnp.logical_and(column >= row * head_size, column < (row + 1) * head_size).astype(F32)


def live_rows(flag_ref, item, items, patches, lats, columns):
    row = iota((patches + lats, columns), 0)
    media = jnp.logical_and(row < patches, flag_ref[item] > 0)
    return jnp.logical_or(media, jnp.logical_and(row >= patches, flag_ref[items] > 0))


def pack_shape(own, shard, width):
    unit = math.gcd(own, shard)
    return unit, width * unit // shard


def join_kernel(key_ref, value_ref, cotangent_ref, out_ref, low_ref, *, width):
    for g in range(key_ref.shape[1] // width):
        columns = slice(g * width, (g + 1) * width)
        out_ref[:, 2 * g * width : (2 * g + 1) * width] = key_ref[:, columns]
        out_ref[:, (2 * g + 1) * width : (2 * g + 2) * width] = value_ref[:, columns]
    low = cotangent_ref[...].astype(BF16)
    low_ref[...] = low
    own, span = low.shape
    unit, piece = pack_shape(own, out_ref.shape[0], span)
    for a in range(own // unit):
        for b in range(span // piece):
            at = 2 * span + a * piece
            out_ref[b * unit : (b + 1) * unit, at : at + piece] = low[
                a * unit : (a + 1) * unit, b * piece : (b + 1) * piece
            ]


def norm_kernel(media_ref, time_ref, gain_ref, bias_ref, lat_ref, out_ref, *, steps, per_item):
    step = pl.program_id(0)

    @pl.when(step < steps)
    def _():
        rows = media_ref[...].astype(F32) + time_ref[pl.ds(step // per_item, 1), :]
        out_ref[...] = layer_norm(rows, gain_ref[...], bias_ref[...]).astype(BF16)

    @pl.when(step == steps)
    def _():
        out_ref[...] = lat_ref[...]


def forward_kernel(
    flag_ref, both_ref, query_ref, top_ref, *refs, items, patches, scale, head_size, heads,
):
    message_refs, (part_ref, mark_ref) = refs[:-2], refs[-2:]
    lats, width = query_ref.shape
    frames = len(message_refs)
    own = message_refs[0].shape[0]
    row_total = own // items
    masks = head_masks(lats, width, head_size)
    queries = spread_heads(query_ref[...].astype(F32), masks).astype(BF16)
    base = items * patches
    lat_both = both_ref[base : base + lats, :]
    group = pl.program_id(0)
    term, lane = iota((16, GROUP * LANES), 0), iota((16, GROUP * LANES), 1)
    place = jnp.logical_and(
        lane % LANES == term * heads + group * GROUP + lane // LANES, term < 9
    ).astype(BF16)
    for i in range(items):
        both = jnp.concatenate([both_ref[i * patches : (i + 1) * patches, :], lat_both], 0)
        live = live_rows(flag_ref, i, items, patches, lats, queries.shape[0])
        scores = scale * transposed_right(both[:, :width], queries)
        masked = jnp.where(live, scores, MASKED)
        top = jnp.max(masked, axis=0, keepdims=True)
        block_exp = jnp.where(live, jnp.exp(masked - top), 0.0)
        total = jnp.sum(block_exp, axis=0, keepdims=True)
        moment = jnp.sum(block_exp * scores, axis=0, keepdims=True)
        part = transposed_left(block_exp.astype(BF16), both[:, width:])
        part_ref[i] = collect_heads(part, masks)
        top_ref[0, i] = jnp.broadcast_to(top, top_ref.shape[2:])
        terms = jnp.concatenate(
            [t.astype(F32) for x in (top, total, moment) for t in split_terms(x)]
            + [jnp.zeros((7, top.shape[1]), F32)],
            0,
        ).astype(BF16)
        wide = transposed_left(terms, place)
        mark = wide[:lats, :LANES]
        for h in range(1, GROUP):
            mark = mark + wide[h * lats : (h + 1) * lats, h * LANES : (h + 1) * LANES]
        mark_ref[i] = mark

    end = message_refs[0].shape[1] - LANES
    for s, message_ref in enumerate(message_refs):
        start = pl.multiple_of(lax.rem(flag_ref[items + 1] + s, frames) * row_total, row_total)
        rows = pl.ds(start, row_total)
        block = jnp.concatenate([part_ref[i, rows, :] for i in range(items)], 0).astype(BF16)
        mark = jnp.concatenate([mark_ref[i, rows, :] for i in range(items)], 0).astype(BF16)
        for g in range(end // width):

            @pl.when(group == g)
            def _():
                message_ref[:, g * width : (g + 1) * width] = block
                if g == 0:
                    message_ref[:, end:] = mark
                else:
                    message_ref[:, end:] = message_ref[:, end:] + mark


def merge_kernel(*refs, chunks, frames, items, head_size, heads):
    message_refs = refs[: chunks * frames]
    base_ref, weight_ref, gain_ref, bias_ref = refs[chunks * frames : chunks * frames + 4]
    merged_ref, mid_ref, ffn_ref, log_ref, entropy_ref = refs[chunks * frames + 4 :]
    own, columns = message_refs[0].shape
    half = columns - LANES
    lane, column = iota((LANES, 3 * LANES), 0), iota((LANES, 3 * LANES), 1)
    gather = jnp.logical_and(
        jnp.logical_and(lane // heads // 3 == column // LANES, lane % heads == column % LANES),
        lane < 9 * heads,
    ).astype(BF16)
    expand = head_expand(half, head_size)
    live = iota((own, LANES), 1) < heads
    spread = jnp.zeros((own, LANES), F32)
    for c in range(chunks):
        sources = message_refs[c * frames : (c + 1) * frames]
        stats = [matmul(x[:, half:], gather) for x in sources]
        tops = [x[:, :LANES] for x in stats]
        peak = functools.reduce(jnp.maximum, tops)
        factors = [jnp.exp(t - peak) for t in tops]
        whole = sum(f * x[:, LANES : 2 * LANES] for f, x in zip(factors, stats))
        moment = sum(f * x[:, 2 * LANES :] for f, x in zip(factors, stats))
        whole = jnp.where(live, whole, 1.0)
        log_total = jnp.where(live, peak + jnp.log(whole), 0.0)
        log_ref[c] = log_total
        spread = spread + jnp.where(live, log_total - moment / whole, 0.0)
        merged = jnp.zeros((own, half), F32)
        for x, factor in zip(sources, factors):
            share = jnp.where(live, factor / whole, 0.0)
            wide = jnp.dot(share, expand, precision=HIGHEST, preferred_element_type=F32)
            merged = merged + x[:, :half].astype(F32) * wide
        merged_ref[:, c * half : (c + 1) * half] = merged
    entropy_ref[...] = jnp.broadcast_to(
        jnp.sum(spread, axis=1, keepdims=True) * (1.0 / HEADS), entropy_ref.shape
    )
    base = jnp.concatenate([base_ref[...]] * items, 0)
    mid = base + matmul(merged_ref[...].astype(BF16), weight_ref[...])
    mid_ref[...] = mid
    ffn_ref[...] = layer_norm(mid, gain_ref[...], bias_ref[...]).astype(BF16)


def gelu_parts(x):
    share = 0.5 * (1.0 + lax.erf(x * (0.5**0.5)))
    slope = share + x * jnp.exp(-0.5 * x * x) * ((2.0 * jnp.pi) ** -0.5)
    return x * share, slope


def feed_kernel(flag_ref, *refs, devices, items):
    row_refs = refs[:devices]
    low_ref, up_ref, down_ref, result_ref = refs[devices : devices + 4]
    grad_refs, (plane_ref, plane_low_ref) = refs[devices + 4 : -2], refs[-2:]
    own, width = row_refs[0].shape
    shard = low_ref.shape[0] // devices
    unit, piece = pack_shape(own, shard, width)
    me = flag_ref[2 * items + 2]
    for d in range(devices):
        plane_ref[d * own : (d + 1) * own, :] = row_refs[d][...]
        source = jnp.bitwise_xor(me, d) * shard
        for a in range(own // unit):
            rows = slice(d * own + a * unit, d * own + (a + 1) * unit)
            for b in range(shard // unit):
                start = pl.multiple_of(source + b * unit, unit)
                plane_low_ref[rows, b * piece : (b + 1) * piece] = low_ref[
                    pl.ds(start, unit), a * piece : (a + 1) * piece
                ]
    upward = matmul(plane_ref[...], up_ref[...])
    hidden, slope = gelu_parts(upward)
    grad_up = (slope * transposed_right(plane_low_ref[...], down_ref[...])).astype(BF16)
    grad = transposed_right(grad_up, up_ref[...]).astype(BF16)
    result = matmul(hidden.astype(BF16), down_ref[...]).astype(BF16)
    for d in range(devices):
        grad_refs[d][...] = grad[d * own : (d + 1) * own, :]
        result_ref[jnp.bitwise_xor(me, d)] = result[d * own : (d + 1) * own, :]


def feed_back_kernel(row_ref, low_ref, up_ref, down_ref, hidden_ref, grad_ref):
    hidden, slope = gelu_parts(matmul(row_ref[...], up_ref[...]))
    hidden_ref[...] = hidden.astype(BF16)
    grad_ref[...] = (slope * transposed_right(low_ref[...], down_ref[...])).astype(BF16)


def outer_kernel(left_ref, right_ref, out_ref):
    out_ref[...] = transposed_left(left_ref[...], right_ref[...]).astype(out_ref.dtype)


def norm_backward(rows, gain, gradient):
    center = rows - jnp.mean(rows, axis=1, keepdims=True)
    rate = lax.rsqrt(jnp.mean(center * center, axis=1, keepdims=True) + EPSILON)
    unit = center * rate
    scaled = gradient * gain
    inner = scaled - jnp.mean(scaled, axis=1, keepdims=True)
    back = rate * (inner - unit * jnp.mean(scaled * unit, axis=1, keepdims=True))
    return (
        back,
        jnp.sum(gradient * unit, axis=0, keepdims=True),
        jnp.sum(gradient, axis=0, keepdims=True),
    )


def turn_kernel(*refs, devices, items, chunks, head_size, heads):
    part_refs = refs[:devices]
    mid_ref, cotangent_ref, gain_ref, merged_ref, log_ref, weight_ref = refs[
        devices : devices + 6
    ]
    message_ref, branch_ref, base_ref, sums_ref = refs[devices + 6 :]
    own, width = mid_ref.shape
    half = width // chunks
    gradient = total_of([x[...] for x in part_refs])
    back, gain_sum, bias_sum = norm_backward(mid_ref[...], gain_ref[...], gradient)
    grad_mid = cotangent_ref[...] + back
    sums_ref[...] = jnp.zeros(sums_ref.shape, F32)
    sums_ref[0:1, :] = gain_sum
    sums_ref[1:2, :] = bias_sum
    row_total = own // items
    base_ref[...] = total_of(
        [grad_mid[i * row_total : (i + 1) * row_total] for i in range(items)]
    )
    branch = grad_mid.astype(BF16)
    branch_ref[:, :width] = branch
    branch_ref[:, width:] = merged_ref[...].astype(BF16)
    grad_att = transposed_right(branch, weight_ref[...]).astype(BF16)
    expand = head_expand(half, head_size)
    lane, column = iota((6 * LANES, LANES), 0), iota((6 * LANES, LANES), 1)
    place = jnp.logical_and(
        lane % LANES < heads, column == (lane // LANES) * heads + lane % LANES
    ).astype(BF16)
    message_ref[:, :width] = grad_att
    for c in range(chunks):
        columns = slice(c * half, (c + 1) * half)
        delta = lax.dot_general(
            merged_ref[:, columns] * grad_att[:, columns].astype(F32),
            expand,
            (((1,), (1,)), ((), ())),
            precision=HIGHEST,
            preferred_element_type=F32,
        )
        terms = jnp.concatenate([t for x in (log_ref[c], delta) for t in split_terms(x)], 1)
        message_ref[:, width + c * LANES : width + (c + 1) * LANES] = matmul(
            terms, place
        ).astype(BF16)


def backward_kernel(
    *refs, frames, items, patches, scale, head_size, heads,
):
    flag_ref, both_ref, query_ref, top_ref = refs[:4]
    grad_refs = refs[4 : 4 + frames]
    mark_refs = refs[4 + frames : 4 + 2 * frames]
    out_ref, sum_ref, held_ref, note_ref = refs[4 + 2 * frames :]
    lats, width = query_ref.shape
    own = grad_refs[0].shape[0]
    row_total = own // items
    base = items * patches
    for s in range(frames):
        source = lax.rem(flag_ref[items + 1] + (frames - s), frames)
        rows = pl.ds(pl.multiple_of(source * row_total, row_total), row_total)
        block = grad_refs[s][...].astype(F32)
        mark = mark_refs[s][...].astype(F32)
        for i in range(items):
            held_ref[i, rows, :] = block[i * row_total : (i + 1) * row_total]
            note_ref[i, rows, :] = mark[i * row_total : (i + 1) * row_total]
    masks = head_masks(lats, width, head_size)
    queries = spread_heads(query_ref[...].astype(F32), masks).astype(BF16)
    lat_both = both_ref[base : base + lats, :]
    row, lane = iota((GROUP * 8, LANES), 0), iota((GROUP * 8, LANES), 1)
    pick = jnp.logical_and(
        jnp.logical_and(
            lane // heads // 3 == row % 8,
            lane % heads == pl.program_id(0) * GROUP + row // 8,
        ),
        lane < 6 * heads,
    ).astype(BF16)
    grad_query = jnp.zeros((queries.shape[0], width), F32)
    lat_grad_key = jnp.zeros((lats, width), F32)
    lat_grad_value = jnp.zeros((lats, width), F32)
    for i in range(items):
        rows = slice(i * patches, (i + 1) * patches)
        stats = transposed_right(pick, note_ref[i].astype(BF16))
        stats = jnp.concatenate([stats[h * 8 : (h + 1) * 8] for h in range(GROUP)], 1)
        log_total = stats[0:1]
        delta = stats[1:2]
        top = top_ref[0, i, 0:1, :]
        rescale = jnp.exp(top - log_total)
        both = jnp.concatenate([both_ref[rows, :], lat_both], 0)
        keys, values = both[:, :width], both[:, width:]
        grads = spread_heads(held_ref[i], masks).astype(BF16)
        live = live_rows(flag_ref, i, items, patches, lats, queries.shape[0])
        masked = jnp.where(live, scale * transposed_right(keys, queries), MASKED)
        probs = jnp.where(live, jnp.exp(masked - log_total), 0.0)
        block_exp = jnp.where(live, jnp.exp(masked - top), 0.0)
        weights = (block_exp.astype(BF16).astype(F32) * rescale).astype(BF16)
        grad_scores = (probs * (transposed_right(values, grads) - delta)).astype(BF16)
        grad_key = scale * matmul(grad_scores, queries)
        grad_value = matmul(weights, grads)
        out_ref[rows, :width] = grad_key[:patches].astype(BF16)
        out_ref[rows, width:] = grad_value[:patches].astype(BF16)
        grad_query = grad_query + transposed_left(grad_scores, keys)
        lat_grad_key = lat_grad_key + grad_key[patches:]
        lat_grad_value = lat_grad_value + grad_value[patches:]
    out_ref[base : base + lats, :width] = lat_grad_key.astype(BF16)
    out_ref[base : base + lats, width:] = lat_grad_value.astype(BF16)
    sum_ref[...] = scale * collect_heads(grad_query, masks)


def media_kernel(flag_ref, *refs, chunks, items, frames):
    grad_refs, lat_refs, weight_refs = [
        refs[k * chunks : (k + 1) * chunks] for k in range(3)
    ]
    media_ref, time_ref, gain_ref, out_ref, sums_ref, product_ref = refs[3 * chunks :]
    item = pl.program_id(0)

    @pl.when(item == 0)
    def _():
        sums_ref[...] = jnp.zeros(sums_ref.shape, F32)
        product_ref[...] = functools.reduce(
            jnp.add, [transposed_right(g[...], w[...]) for g, w in zip(lat_refs, weight_refs)]
        )

    gradient = functools.reduce(
        jnp.add, [transposed_right(g[...], w[...]) for g, w in zip(grad_refs, weight_refs)]
    )
    inputs = media_ref[...].astype(F32) + time_ref[pl.ds(item, 1), :]
    back, gain_sum, bias_sum = norm_backward(inputs, gain_ref[...], gradient)
    out_ref[...] = back.astype(BF16)
    place = iota((frames, 1), 0) == flag_ref[items + 2 + item]
    sums_ref[0:frames, :] += jnp.where(place, jnp.sum(back, axis=0, keepdims=True), 0.0)
    sums_ref[8:9, :] += gain_sum
    sums_ref[9:10, :] += bias_sum


def latent_kernel(flag_ref, *refs, chunks, items):
    query_refs = refs[:chunks]
    (
        product_ref, latent_ref, gain_ref, base_ref, ffn_ref, media_ref, out_ref,
    ) = refs[chunks:]
    lats, width = latent_ref.shape
    half = width // chunks
    gradient = product_ref[...]
    for c in range(chunks):
        out_ref[lats : 2 * lats, c * half : (c + 1) * half] = query_refs[c][...]
    back, gain_sum, bias_sum = norm_backward(latent_ref[...], gain_ref[...], gradient)
    out_ref[:lats, :] = back
    row_total = base_ref.shape[0]
    start = pl.multiple_of(flag_ref[items + 1] * row_total, row_total)
    out_ref[pl.ds(start, row_total), :] += base_ref[...]
    at = 2 * lats
    out_ref[at : at + 8, :] = ffn_ref[...]
    out_ref[at + 2 : at + 3, :] = gain_sum
    out_ref[at + 3 : at + 4, :] = bias_sum
    out_ref[at + 8 : at + 24, :] = media_ref[...]
    out_ref[at + 24 :, :] = jnp.zeros((out_ref.shape[0] - at - 24, width), F32)


def query_norm_kernel(flag_ref, *refs, devices, items):
    column_refs = refs[:devices]
    latent_ref, gain_ref, sum_ref, out_ref, out_gain_ref, out_bias_ref, held_ref = refs[devices:]
    for d in range(devices):
        held_ref[jnp.bitwise_xor(flag_ref[2 * items + 2], d)] = column_refs[d][...]
    gradient = jnp.concatenate([held_ref[k] for k in range(devices)], 1)
    back, gain_sum, bias_sum = norm_backward(latent_ref[...], gain_ref[...], gradient)
    lats = latent_ref.shape[0]
    out_ref[...] = sum_ref[:lats, :] + back
    out_gain_ref[...] = sum_ref[2 * lats + 2 : 2 * lats + 3, :] + gain_sum
    out_bias_ref[...] = sum_ref[2 * lats + 3 : 2 * lats + 4, :] + bias_sum


def rows_kernel(flag_ref, *refs, count, frames, items):
    part_refs, out_refs, held_ref = refs[:count], refs[count:-1], refs[-1]
    rows = held_ref.shape[1]
    column = 0
    for part_ref in part_refs:
        total = total_of([part_ref[k] for k in range(part_ref.shape[0])])
        for f in range(frames):
            held_ref[f, :, column : column + total.shape[1]] = total[f * rows : (f + 1) * rows]
        column += total.shape[1]
    for s, out_ref in enumerate(out_refs):
        block = held_ref[lax.rem(flag_ref[items + 1] + s, frames)]
        out_ref[...] = block.astype(out_ref.dtype)


def place_kernel(flag_ref, *refs, chunks, frames, items, groups):
    chunk_refs = refs[: chunks * frames]
    key_ref, value_ref, out_ref = refs[chunks * frames :]
    width = key_ref.shape[2] // (chunks * groups)
    for s in range(frames):
        source = lax.rem(flag_ref[items + 1] + (frames - s), frames)
        out_ref[source] = chunk_refs[s][:, 2 * groups * width :].astype(F32)
        for c in range(chunks):
            for g in range(groups):
                at = (c * groups + g) * width
                block = chunk_refs[c * frames + s][:, 2 * g * width : 2 * (g + 1) * width]
                block = block.astype(F32)
                key_ref[source, :, at : at + width] = block[:, :width]
                value_ref[source, :, at : at + width] = block[:, width:]


def body(
    media,
    cotangent,
    frame_count,
    frame_start,
    latents,
    time_embed,
    media_gain,
    media_bias,
    latent_gain,
    latent_bias,
    ffn_gain,
    ffn_bias,
    query_weight,
    key_weight,
    value_weight,
    out_weight,
    up_weight,
    down_weight,
):
    items = media.shape[0]
    patches = media.shape[2]
    width = media.shape[3]
    lats = latents.shape[0]
    frame_total = time_embed.shape[0]
    row_total = cotangent.shape[1]
    own = items * row_total
    head_size = width // HEADS
    half = width // CHUNKS
    chunk_heads = HEADS // CHUNKS
    group_width = GROUP * head_size
    groups = chunk_heads // GROUP
    stack = GROUP * lats
    tokens = items * patches
    all_tokens = tokens + lats
    shard = query_weight.shape[0]
    hidden_shard = down_weight.shape[0]
    item_size = lax.axis_size("items")
    frame_size = lax.axis_size("frames")
    plane = item_size * own
    item_index = lax.axis_index("items")
    slot = lax.axis_index("frames")
    row_base = slot * row_total
    params = pltpu.CompilerParams(vmem_limit_bytes=56 * 2**20)
    smem = pl.BlockSpec(memory_space=pltpu.SMEM)
    whole = pl.BlockSpec(memory_space=pltpu.VMEM)
    sizes = dict(items=items, head_size=head_size, heads=chunk_heads)

    def struct(shape, kind):
        return jax.ShapeDtypeStruct(shape, kind)

    def cost(micros):
        return pl.CostEstimate(
            flops=int(micros * 1.15e9), bytes_accessed=int(micros * 3.6e6), transcendentals=0
        )

    def column_blocks(x):
        return jnp.transpose(x.reshape(-1, item_size, shard), (1, 0, 2))

    def scatter_exchange(x, axis):
        return jnp.sum(lax.all_to_all(x, axis, 0, 0).astype(F32), axis=0)

    grad_out = cotangent.reshape(own, width)
    low_columns = own * width // shard
    joined, grad_low = pl.pallas_call(
        functools.partial(join_kernel, width=group_width),
        out_shape=[struct((shard, 2 * width + low_columns), BF16), struct((own, width), BF16)],
        cost_estimate=cost(2.5),
        compiler_params=params,
    )(key_weight, value_weight, grad_out)
    kv_full = lax.all_gather(joined, "items", axis=0, tiled=True)
    low_frames = jnp.stack(spread_on(grad_low, "frames"))

    lat_norm = layer_norm(latents, latent_gain, latent_bias).astype(BF16)
    lat_cols = lax.dynamic_slice_in_dim(lat_norm, item_index * shard, shard, 1)
    query_blocks = column_blocks(matmul(lat_cols, query_weight))
    query_cols = scatter_exchange(query_blocks, "items").astype(BF16)
    query_spread = jnp.broadcast_to(query_cols[None], (item_size, lats, shard))
    queries = jnp.transpose(lax.all_to_all(query_spread, "items", 0, 0), (1, 0, 2)).reshape(
        lats, width
    )

    counts = lax.dynamic_slice_in_dim(frame_count, item_index * items, items)
    starts = lax.dynamic_slice_in_dim(frame_start, item_index * items, items)
    offset = (slot - starts) % frame_total
    flags = jnp.concatenate(
        [
            (offset < counts).astype(jnp.int32),
            (slot == 0).astype(jnp.int32)[None],
            slot.astype(jnp.int32)[None],
            offset.astype(jnp.int32),
            item_index.astype(jnp.int32)[None],
        ]
    )
    picker = (offset[:, None] == jnp.arange(frame_total, dtype=jnp.int32)[None, :]).astype(F32)
    time_rows = jnp.dot(picker, time_embed, precision=HIGHEST, preferred_element_type=F32)
    flat_media = media.reshape(tokens, width)
    steps = tokens // lats
    all_rows = pl.pallas_call(
        functools.partial(norm_kernel, steps=steps, per_item=patches // lats),
        grid=(steps + 1,),
        in_specs=[
            pl.BlockSpec((lats, width), lambda i: (jnp.minimum(i, steps - 1), 0)),
            whole,
            whole,
            whole,
            whole,
        ],
        out_specs=pl.BlockSpec((lats, width), lambda i: (i, 0)),
        out_shape=struct((all_tokens, width), BF16),
        cost_estimate=cost(12),
        compiler_params=params,
    )(
        after(flat_media, query_blocks),
        time_rows,
        media_gain[None],
        media_bias[None],
        lat_norm,
    )
    out_full = lax.all_gather(after(out_weight, all_rows), "items", axis=0, tiled=True)

    core = item_index % 2
    rows_across = after(all_rows, query_cols).T.reshape(item_size // 2, 2, shard, all_tokens)
    send_rows, keep_rows = [
        jnp.concatenate(
            [
                lax.dynamic_slice(
                    rows_across, (k, which, 0, 0), (1, 1, shard, all_tokens)
                ).reshape(shard, all_tokens)
                for k in range(item_size // 2)
            ],
            0,
        )
        for which in (1 - core, core)
    ]
    boths, tops, messages = [], [], []
    for c in range(CHUNKS):

        def block_of(g, c=c):
            return (0, c * groups + g)

        if c:
            rows = after(all_rows, tops[-1])
        else:
            rows = after(all_rows, queries, send_rows, keep_rows)
        both = matmul(rows, kv_full[:, 2 * c * half : 2 * (c + 1) * half]).astype(BF16)
        top, *parts = pl.pallas_call(
            functools.partial(
                forward_kernel, patches=patches, scale=head_size**-0.5, **sizes
            ),
            grid=(groups,),
            in_specs=[
                smem,
                pl.BlockSpec((all_tokens, 2 * group_width), lambda g: (0, g)),
                pl.BlockSpec((lats, group_width), block_of),
            ],
            out_specs=[pl.BlockSpec((1, items, 8, stack), lambda g: (g, 0, 0, 0))]
            + [pl.BlockSpec((own, half + LANES), lambda g: (0, 0))] * frame_size,
            out_shape=[struct((groups, items, 8, stack), F32)]
            + [struct((own, half + LANES), BF16)] * frame_size,
            scratch_shapes=[
                pltpu.VMEM((items, lats, group_width), F32),
                pltpu.VMEM((items, lats, LANES), F32),
            ],
            cost_estimate=cost(7.8),
            compiler_params=params,
        )(flags, after(both, *messages) if c else both, queries)
        boths.append(both)
        tops.append(top)
        messages += [p if s == 0 else send_on(p, "frames", s) for s, p in enumerate(parts)]
    up_slice = lax.all_to_all(after(up_weight, boths[0]), "items", 1, 0, tiled=True)
    low_all = lax.all_gather(after(low_frames, tops[1]), "items", axis=0).reshape(-1, width)

    base_rows = lax.dynamic_slice_in_dim(latents, row_base, row_total, 0)
    merged, mid_rows, ffn_in, logs, entropy_wide = pl.pallas_call(
        functools.partial(merge_kernel, chunks=CHUNKS, frames=frame_size, **sizes),
        out_shape=[
            struct((own, width), F32),
            struct((own, width), F32),
            struct((own, width), BF16),
            struct((CHUNKS, own, LANES), F32),
            struct((own, LANES), F32),
        ],
        cost_estimate=cost(6.3),
        compiler_params=params,
    )(*messages, base_rows, out_full, ffn_gain[None], ffn_bias[None])
    entropy = entropy_wide[:, 0].reshape(items, row_total)

    ffn_blocks = spread_across(ffn_in, "items")
    ffn_frames = spread_on(after(ffn_in, *ffn_blocks), "frames")
    result_part, *parts = pl.pallas_call(
        functools.partial(feed_kernel, devices=item_size, items=items),
        grid=(1,),
        in_specs=[smem]
        + [whole] * item_size
        + [
            pl.BlockSpec((width, low_columns), lambda i: (0, 2 * width // low_columns)),
            whole,
            whole,
        ],
        out_specs=[whole] * (1 + item_size),
        out_shape=[struct((item_size, own, width), BF16)]
        + [struct((own, width), BF16)] * item_size,
        scratch_shapes=[pltpu.VMEM((plane, width), BF16)] * 2,
        cost_estimate=cost(10),
        compiler_params=params,
    )(flags, *ffn_blocks, kv_full, up_slice, down_weight)
    grad_blocks = collect_across(parts, "items")
    grad_blocks[0] = after(grad_blocks[0], *ffn_frames)
    ffn_all = lax.all_gather(jnp.stack(ffn_frames), "items", axis=0).reshape(-1, width)

    turn, grad_branch, grad_base, ffn_sums = pl.pallas_call(
        functools.partial(turn_kernel, devices=item_size, chunks=CHUNKS, **sizes),
        out_shape=[
            struct((own, width + CHUNKS * LANES), BF16),
            struct((own, 2 * width), BF16),
            struct((row_total, width), F32),
            struct((8, width), F32),
        ],
        cost_estimate=cost(7.6),
        compiler_params=params,
    )(*grad_blocks, mid_rows, grad_out, ffn_gain[None], merged, logs, out_full)
    turns = spread_on(turn, "frames")
    branch_plane = lax.all_gather(grad_branch, "items", axis=0, tiled=True)
    att_plane = lax.dynamic_slice_in_dim(
        branch_plane, width + item_index * shard, shard, 1
    )
    turns[0] = after(turns[0], low_all)

    chunk_grads, chunk_queries = [], []

    def weight_terms(c):
        send = matmul(send_rows, chunk_grads[c]).astype(BF16)
        received = send_across(send, "items", 1).reshape(-1, shard, 2 * half)
        keep = matmul(after(keep_rows, send), chunk_grads[c]).astype(BF16)
        return send, keep.reshape(-1, shard, 2 * half), received

    def chip_terms(keep, received):
        return (keep.astype(F32) + received.astype(F32)).astype(BF16)

    def exchange_chips(x):
        groups_of = [list(range(k, item_size, 2)) for k in range(2)]
        return lax.all_to_all(x, "items", 0, 0, axis_index_groups=groups_of)

    def frame_rows(ranges):
        rows = shard // frame_size
        columns = sum(x.shape[-1] for x in ranges)
        return pl.pallas_call(
            functools.partial(rows_kernel, count=len(ranges), frames=frame_size, items=items),
            in_specs=[smem] + [whole] * len(ranges),
            out_specs=[whole] * frame_size,
            out_shape=[struct((rows, columns), F32)]
            + [struct((rows, columns), BF16)] * (frame_size - 1),
            scratch_shapes=[pltpu.VMEM((frame_size, rows, columns), F32)],
            cost_estimate=cost(3.5),
            compiler_params=params,
        )(flags, *ranges)

    def send_rows_on(rows):
        return [rows[0]] + [send_on(p, "frames", s) for s, p in enumerate(rows) if s]

    for c in range(CHUNKS):

        def block_of(g, c=c):
            return (0, c * groups + g)

        chunk_grad, chunk_query = pl.pallas_call(
            functools.partial(
                backward_kernel, frames=frame_size, patches=patches, scale=head_size**-0.5, **sizes
            ),
            grid=(groups,),
            in_specs=[
                smem,
                pl.BlockSpec((all_tokens, 2 * group_width), lambda g: (0, g)),
                pl.BlockSpec((lats, group_width), block_of),
                pl.BlockSpec((1, items, 8, stack), lambda g: (g, 0, 0, 0)),
            ]
            + [pl.BlockSpec((own, group_width), block_of)] * frame_size
            + [pl.BlockSpec((own, LANES), lambda g, c=c: (0, width // LANES + c))] * frame_size,
            out_specs=[
                pl.BlockSpec((all_tokens, 2 * group_width), lambda g: (0, g)),
                pl.BlockSpec((lats, group_width), lambda g: (0, g)),
            ],
            out_shape=[
                struct((all_tokens, 2 * half), BF16),
                struct((lats, half), F32),
            ],
            scratch_shapes=[
                pltpu.VMEM((items, lats, group_width), F32),
                pltpu.VMEM((items, lats, LANES), F32),
            ],
            cost_estimate=cost(8),
            compiler_params=params,
        )(flags, after(boths[c], *held) if c else boths[c], queries, tops[c], *turns, *turns)
        chunk_grads.append(chunk_grad)
        chunk_queries.append(chunk_query)
        if c == 0:
            first_send, first_keep, first_received = weight_terms(0)
            held = (first_send, ffn_all)
    first_terms = chip_terms(after(first_keep, chunk_grads[-1]), first_received)
    first_moved = exchange_chips(first_terms)

    last_block = pl.BlockSpec((lats, 2 * half), lambda i: (tokens // lats, 0))
    media_grad, media_sums, lat_product = pl.pallas_call(
        functools.partial(media_kernel, chunks=CHUNKS, items=items, frames=frame_total),
        grid=(items,),
        in_specs=[smem]
        + [pl.BlockSpec((patches, 2 * half), lambda i: (i, 0))] * CHUNKS
        + [last_block] * CHUNKS
        + [pl.BlockSpec((width, 2 * half), lambda i, c=c: (0, c)) for c in range(CHUNKS)]
        + [pl.BlockSpec((patches, width), lambda i: (i, 0)), whole, whole],
        out_specs=[
            pl.BlockSpec((patches, width), lambda i: (i, 0)),
            pl.BlockSpec((16, width), lambda i: (0, 0)),
            pl.BlockSpec((lats, width), lambda i: (0, 0)),
        ],
        out_shape=[
            struct((tokens, width), BF16),
            struct((16, width), F32),
            struct((lats, width), F32),
        ],
        cost_estimate=cost(21),
        compiler_params=params,
    )(
        flags,
        *chunk_grads[:-1],
        after(chunk_grads[-1], first_terms),
        *chunk_grads,
        *[kv_full] * CHUNKS,
        flat_media,
        time_rows,
        media_gain[None],
    )

    sum_rows = 2 * lats + 24
    sum_rows += -sum_rows % (8 * item_size)
    payload = pl.pallas_call(
        functools.partial(latent_kernel, chunks=CHUNKS, items=items),
        in_specs=[smem] + [whole] * (CHUNKS + 6),
        out_specs=whole,
        out_shape=struct((sum_rows, width), F32),
        cost_estimate=cost(3),
        compiler_params=params,
    )(
        flags,
        *chunk_queries,
        after(lat_product, first_moved),
        latents,
        latent_gain[None],
        grad_base,
        ffn_sums,
        media_sums,
    )
    payload_part = lax.psum_scatter(payload, "items", scatter_dimension=0, tiled=True)

    chunk_grads[-1] = after(chunk_grads[-1], payload)
    last_send, last_keep, last_received = weight_terms(CHUNKS - 1)
    last_terms = chip_terms(after(last_keep, first_moved), last_received)
    last_moved = exchange_chips(last_terms)
    out_part = transposed_left(att_plane, after(branch_plane, last_send)[:, :width])
    first_rows = frame_rows([after(first_moved, last_terms), out_part[None]])
    first_frames = send_rows_on(first_rows)
    all_plane = plane * frame_size
    block_rows = min(512, all_plane)
    row_block = pl.BlockSpec((block_rows, width), lambda i: (i, 0))
    hidden_block = pl.BlockSpec((block_rows, hidden_shard), lambda i: (i, 0))
    hidden, grad_up = pl.pallas_call(
        feed_back_kernel,
        grid=(all_plane // block_rows,),
        in_specs=[row_block, row_block, whole, whole],
        out_specs=[hidden_block, hidden_block],
        out_shape=[struct((all_plane, hidden_shard), BF16)] * 2,
        cost_estimate=cost(15),
        compiler_params=params,
    )(after(ffn_all, *first_rows), low_all, up_slice, down_weight)

    def outer(left, right, tile, kind):
        rows, columns = left.shape
        shape = (columns, right.shape[1])
        return pl.pallas_call(
            outer_kernel,
            grid=(columns // tile,),
            in_specs=[pl.BlockSpec((rows, tile), lambda i: (0, i)), whole],
            out_specs=pl.BlockSpec((tile, shape[1]), lambda i: (i, 0)),
            out_shape=struct(shape, kind),
            cost_estimate=cost(9.5),
            compiler_params=params,
        )(left, right)

    first_total = total_of(first_frames).astype(BF16)
    first_placed = spread_on(first_total, "frames")
    last_rows = frame_rows([after(last_moved, hidden)])
    last_frames = send_rows_on(last_rows)
    up_part = outer(ffn_all, after(grad_up, first_total, *last_rows), width // 4, BF16)
    result_pieces = lax.all_to_all(after(result_part, last_moved), "items", 0, 0)
    up_grad = lax.all_to_all(
        after(up_part, result_pieces), "items", 0, 1, tiled=True
    ).astype(F32)
    last_total = total_of(last_frames).astype(BF16)
    last_placed = spread_on(last_total, "frames")
    down_grad = outer(
        after(hidden, up_part, last_total),
        low_all,
        256 if hidden_shard % 256 == 0 else hidden_shard,
        F32,
    )
    placed = first_placed + last_placed
    payload_part = after(payload_part, up_part)
    payload_others = spread_on(payload_part.astype(BF16), "frames")[1:]
    sums = lax.all_gather(
        total_of([payload_part] + payload_others), "items", axis=0, tiled=True
    )
    query_low = sums[lats : 2 * lats].astype(BF16)
    query_grad = transposed_left(lat_cols, query_low)
    norm_cols = transposed_right(query_low, query_weight)
    latents_grad, lat_gain, lat_bias = pl.pallas_call(
        functools.partial(query_norm_kernel, devices=item_size, items=items),
        in_specs=[smem] + [whole] * (item_size + 3),
        out_specs=[whole] * 3,
        out_shape=[struct((lats, width), F32), struct((1, width), F32), struct((1, width), F32)],
        scratch_shapes=[pltpu.VMEM((item_size, lats, shard), F32)],
        cost_estimate=cost(3),
        compiler_params=params,
    )(flags, *spread_across(norm_cols, "items"), latents, latent_gain[None], sums)
    at = 2 * lats
    column_sums = lax.dynamic_slice_in_dim(
        sums[at + 8 : at + 24], item_index * shard, shard, 1
    )

    key_grad, value_grad, out_grad = pl.pallas_call(
        functools.partial(
            place_kernel, chunks=CHUNKS, frames=frame_size, items=items, groups=groups
        ),
        in_specs=[smem] + [whole] * len(placed),
        out_specs=[whole] * 3,
        out_shape=[struct((frame_size, shard // frame_size, width), F32)] * 3,
        cost_estimate=cost(3.4),
        compiler_params=params,
    )(flags, after(placed[0], latents_grad, up_grad), *placed[1:])

    result = mid_rows + total_of([result_pieces[d] for d in range(item_size)])
    return (
        result.reshape(items, row_total, width),
        entropy,
        media_grad.reshape(media.shape),
        latents_grad,
        column_sums[:frame_total],
        column_sums[8],
        column_sums[9],
        lat_gain[0],
        lat_bias[0],
        sums[at],
        sums[at + 1],
        query_grad,
        key_grad.reshape(shard, width),
        value_grad.reshape(shard, width),
        out_grad.reshape(shard, width),
        up_grad,
        down_grad,
    )


def solution(mesh):
    return jax.shard_map(
        body,
        mesh=mesh,
        in_specs=(
            P("items", "frames", None, None),
            P("items", "frames", None),
            P(),
            P(),
            P(),
            P(),
            P(),
            P(),
            P(),
            P(),
            P(),
            P(),
            P("items", None),
            P("items", None),
            P("items", None),
            P("items", None),
            P("items", None),
            P("items", None),
        ),
        out_specs=(
            P("items", "frames", None),
            P("items", "frames"),
            P("items", "frames", None, None),
            P(),
            P(None, "items"),
            P("items"),
            P("items"),
            P(),
            P(),
            P(),
            P(),
            P("items", None),
            P("items", None),
            P("items", None),
            P("items", None),
            P("items", None),
            P("items", None),
        ),
        check_vma=False,
    )
```

```python
import functools
import math

import jax
import jax.numpy as jnp
from jax import lax
from jax.experimental import pallas as pl
from jax.experimental.pallas import tpu as pltpu
from jax.sharding import PartitionSpec as P

HEADS = 16
GROUP = 4
CHUNKS = 2
LANES = 128
EPSILON = 1e-05
MASKED = -1e30
F32 = jnp.float32
BF16 = jnp.bfloat16
HIGHEST = lax.Precision.HIGHEST


def layer_norm(inputs, norm_gain, norm_bias):
    center = inputs - jnp.mean(inputs, axis=-1, keepdims=True)
    spread = jnp.mean(center * center, axis=-1, keepdims=True)
    return center * lax.rsqrt(spread + EPSILON) * norm_gain + norm_bias


def matmul(left_side, right_side):
    return jnp.dot(left_side, right_side, preferred_element_type=F32)


def transposed_left(left_side, right_side):
    return lax.dot_general(
        left_side, right_side, (((0,), (0,)), ((), ())), preferred_element_type=F32
    )


def transposed_right(left_side, right_side):
    return lax.dot_general(
        left_side, right_side, (((1,), (1,)), ((), ())), preferred_element_type=F32
    )


def send_on(x, axis, step):
    size = lax.axis_size(axis)
    return lax.ppermute(x, axis, [(i, (i + step) % size) for i in range(size)])


def send_across(x, axis, distance):
    return lax.ppermute(x, axis, [(i, i ^ distance) for i in range(lax.axis_size(axis))])


def spread_on(x, axis):
    return [x] + [send_on(x, axis, s) for s in range(1, lax.axis_size(axis))]


def spread_across(x, axis):
    chips = [x] + [send_across(x, axis, d) for d in range(2, lax.axis_size(axis), 2)]
    return [b for block in chips for b in (block, send_across(block, axis, 1))]


def collect_across(pieces, axis):
    return [pieces[0]] + [send_across(p, axis, d) for d, p in enumerate(pieces) if d]


def total_of(pieces):
    return functools.reduce(jnp.add, [p.astype(F32) for p in pieces])


def after(x, *earlier):
    return lax.optimization_barrier((x,) + earlier)[0]


def split_terms(x):
    high = x.astype(BF16)
    rest = x - high.astype(F32)
    middle = rest.astype(BF16)
    return high, middle, (rest - middle.astype(F32)).astype(BF16)


def iota(shape, dim):
    return lax.broadcasted_iota(jnp.int32, shape, dim)


def head_masks(rows, width, head_size):
    lane = iota((rows, width), 1)
    return [
        jnp.logical_and(lane >= h * head_size, lane < (h + 1) * head_size)
        for h in range(width // head_size)
    ]


def spread_heads(block, masks):
    return jnp.concatenate([jnp.where(m, block, jnp.zeros_like(block)) for m in masks], 0)


def collect_heads(block, masks):
    rows = block.shape[0] // len(masks)
    total = jnp.where(masks[0], block[:rows], 0.0)
    for h in range(1, len(masks)):
        total = total + jnp.where(masks[h], block[h * rows : (h + 1) * rows], 0.0)
    return total


def head_expand(width, head_size):
    row, column = iota((LANES, width), 0), iota((LANES, width), 1)
    return jnp.logical_and(column >= row * head_size, column < (row + 1) * head_size).astype(F32)


def live_rows(flag_ref, item, items, patches, lats, columns):
    row = iota((patches + lats, columns), 0)
    media = jnp.logical_and(row < patches, flag_ref[item] > 0)
    return jnp.logical_or(media, jnp.logical_and(row >= patches, flag_ref[items] > 0))


def pack_shape(own, shard, width):
    unit = math.gcd(own, shard)
    return unit, width * unit // shard


def join_kernel(key_ref, value_ref, cotangent_ref, out_ref, low_ref, *, width):
    for g in range(key_ref.shape[1] // width):
        columns = slice(g * width, (g + 1) * width)
        out_ref[:, 2 * g * width : (2 * g + 1) * width] = key_ref[:, columns]
        out_ref[:, (2 * g + 1) * width : (2 * g + 2) * width] = value_ref[:, columns]
    low = cotangent_ref[...].astype(BF16)
    low_ref[...] = low
    own, span = low.shape
    unit, piece = pack_shape(own, out_ref.shape[0], span)
    for a in range(own // unit):
        for b in range(span // piece):
            at = 2 * span + a * piece
            out_ref[b * unit : (b + 1) * unit, at : at + piece] = low[
                a * unit : (a + 1) * unit, b * piece : (b + 1) * piece
            ]


def norm_kernel(media_ref, time_ref, gain_ref, bias_ref, lat_ref, out_ref, *, steps, per_item):
    step = pl.program_id(0)

    @pl.when(step < steps)
    def _():
        rows = media_ref[...].astype(F32) + time_ref[pl.ds(step // per_item, 1), :]
        out_ref[...] = layer_norm(rows, gain_ref[...], bias_ref[...]).astype(BF16)

    @pl.when(step == steps)
    def _():
        out_ref[...] = lat_ref[...]


def forward_kernel(
    flag_ref, both_ref, query_ref, top_ref, *refs, items, patches, scale, head_size, heads,
):
    message_refs, (part_ref, mark_ref) = refs[:-2], refs[-2:]
    lats, width = query_ref.shape
    frames = len(message_refs)
    own = message_refs[0].shape[0]
    row_total = own // items
    masks = head_masks(lats, width, head_size)
    queries = spread_heads(query_ref[...].astype(F32), masks).astype(BF16)
    base = items * patches
    lat_both = both_ref[base : base + lats, :]
    group = pl.program_id(0)
    term, lane = iota((16, GROUP * LANES), 0), iota((16, GROUP * LANES), 1)
    place = jnp.logical_and(
        lane % LANES == term * heads + group * GROUP + lane // LANES, term < 9
    ).astype(BF16)
    for i in range(items):
        both = jnp.concatenate([both_ref[i * patches : (i + 1) * patches, :], lat_both], 0)
        live = live_rows(flag_ref, i, items, patches, lats, queries.shape[0])
        scores = scale * transposed_right(both[:, :width], queries)
        masked = jnp.where(live, scores, MASKED)
        top = jnp.max(masked, axis=0, keepdims=True)
        block_exp = jnp.where(live, jnp.exp(masked - top), 0.0)
        total = jnp.sum(block_exp, axis=0, keepdims=True)
        moment = jnp.sum(block_exp * scores, axis=0, keepdims=True)
        part = transposed_left(block_exp.astype(BF16), both[:, width:])
        part_ref[i] = collect_heads(part, masks)
        top_ref[0, i] = jnp.broadcast_to(top, top_ref.shape[2:])
        terms = jnp.concatenate(
            [t.astype(F32) for x in (top, total, moment) for t in split_terms(x)]
            + [jnp.zeros((7, top.shape[1]), F32)],
            0,
        ).astype(BF16)
        wide = transposed_left(terms, place)
        mark = wide[:lats, :LANES]
        for h in range(1, GROUP):
            mark = mark + wide[h * lats : (h + 1) * lats, h * LANES : (h + 1) * LANES]
        mark_ref[i] = mark

    end = message_refs[0].shape[1] - LANES
    for s, message_ref in enumerate(message_refs):
        start = pl.multiple_of(lax.rem(flag_ref[items + 1] + s, frames) * row_total, row_total)
        rows = pl.ds(start, row_total)
        block = jnp.concatenate([part_ref[i, rows, :] for i in range(items)], 0).astype(BF16)
        mark = jnp.concatenate([mark_ref[i, rows, :] for i in range(items)], 0).astype(BF16)
        for g in range(end // width):

            @pl.when(group == g)
            def _():
                message_ref[:, g * width : (g + 1) * width] = block
                if g == 0:
                    message_ref[:, end:] = mark
                else:
                    message_ref[:, end:] = message_ref[:, end:] + mark


def merge_kernel(*refs, chunks, frames, items, head_size, heads):
    message_refs = refs[: chunks * frames]
    base_ref, weight_ref, gain_ref, bias_ref = refs[chunks * frames : chunks * frames + 4]
    merged_ref, mid_ref, ffn_ref, log_ref, entropy_ref = refs[chunks * frames + 4 :]
    own, columns = message_refs[0].shape
    half = columns - LANES
    lane, column = iota((LANES, 3 * LANES), 0), iota((LANES, 3 * LANES), 1)
    gather = jnp.logical_and(
        jnp.logical_and(lane // heads // 3 == column // LANES, lane % heads == column % LANES),
        lane < 9 * heads,
    ).astype(BF16)
    expand = head_expand(half, head_size)
    live = iota((own, LANES), 1) < heads
    spread = jnp.zeros((own, LANES), F32)
    for c in range(chunks):
        sources = message_refs[c * frames : (c + 1) * frames]
        stats = [matmul(x[:, half:], gather) for x in sources]
        tops = [x[:, :LANES] for x in stats]
        peak = functools.reduce(jnp.maximum, tops)
        factors = [jnp.exp(t - peak) for t in tops]
        whole = sum(f * x[:, LANES : 2 * LANES] for f, x in zip(factors, stats))
        moment = sum(f * x[:, 2 * LANES :] for f, x in zip(factors, stats))
        whole = jnp.where(live, whole, 1.0)
        log_total = jnp.where(live, peak + jnp.log(whole), 0.0)
        log_ref[c] = log_total
        spread = spread + jnp.where(live, log_total - moment / whole, 0.0)
        merged = jnp.zeros((own, half), F32)
        for x, factor in zip(sources, factors):
            share = jnp.where(live, factor / whole, 0.0)
            wide = jnp.dot(share, expand, precision=HIGHEST, preferred_element_type=F32)
            merged = merged + x[:, :half].astype(F32) * wide
        merged_ref[:, c * half : (c + 1) * half] = merged
    entropy_ref[...] = jnp.broadcast_to(
        jnp.sum(spread, axis=1, keepdims=True) * (1.0 / HEADS), entropy_ref.shape
    )
    base = jnp.concatenate([base_ref[...]] * items, 0)
    mid = base + matmul(merged_ref[...].astype(BF16), weight_ref[...])
    mid_ref[...] = mid
    ffn_ref[...] = layer_norm(mid, gain_ref[...], bias_ref[...]).astype(BF16)


def gelu_parts(x):
    share = 0.5 * (1.0 + lax.erf(x * (0.5**0.5)))
    slope = share + x * jnp.exp(-0.5 * x * x) * ((2.0 * jnp.pi) ** -0.5)
    return x * share, slope


def feed_kernel(flag_ref, *refs, devices, items):
    row_refs = refs[:devices]
    low_ref, up_ref, down_ref, result_ref = refs[devices : devices + 4]
    grad_refs, (plane_ref, plane_low_ref) = refs[devices + 4 : -2], refs[-2:]
    own, width = row_refs[0].shape
    shard = low_ref.shape[0] // devices
    unit, piece = pack_shape(own, shard, width)
    me = flag_ref[2 * items + 2]
    for d in range(devices):
        plane_ref[d * own : (d + 1) * own, :] = row_refs[d][...]
        source = jnp.bitwise_xor(me, d) * shard
        for a in range(own // unit):
            rows = slice(d * own + a * unit, d * own + (a + 1) * unit)
            for b in range(shard // unit):
                start = pl.multiple_of(source + b * unit, unit)
                plane_low_ref[rows, b * piece : (b + 1) * piece] = low_ref[
                    pl.ds(start, unit), a * piece : (a + 1) * piece
                ]
    upward = matmul(plane_ref[...], up_ref[...])
    hidden, slope = gelu_parts(upward)
    grad_up = (slope * transposed_right(plane_low_ref[...], down_ref[...])).astype(BF16)
    grad = transposed_right(grad_up, up_ref[...]).astype(BF16)
    result = matmul(hidden.astype(BF16), down_ref[...]).astype(BF16)
    for d in range(devices):
        grad_refs[d][...] = grad[d * own : (d + 1) * own, :]
        result_ref[jnp.bitwise_xor(me, d)] = result[d * own : (d + 1) * own, :]


def feed_back_kernel(row_ref, low_ref, up_ref, down_ref, hidden_ref, grad_ref):
    hidden, slope = gelu_parts(matmul(row_ref[...], up_ref[...]))
    hidden_ref[...] = hidden.astype(BF16)
    grad_ref[...] = (slope * transposed_right(low_ref[...], down_ref[...])).astype(BF16)


def outer_kernel(left_ref, right_ref, out_ref):
    out_ref[...] = transposed_left(left_ref[...], right_ref[...]).astype(out_ref.dtype)


def norm_backward(rows, gain, gradient):
    center = rows - jnp.mean(rows, axis=1, keepdims=True)
    rate = lax.rsqrt(jnp.mean(center * center, axis=1, keepdims=True) + EPSILON)
    unit = center * rate
    scaled = gradient * gain
    inner = scaled - jnp.mean(scaled, axis=1, keepdims=True)
    back = rate * (inner - unit * jnp.mean(scaled * unit, axis=1, keepdims=True))
    return (
        back,
        jnp.sum(gradient * unit, axis=0, keepdims=True),
        jnp.sum(gradient, axis=0, keepdims=True),
    )


def turn_kernel(*refs, devices, items, chunks, head_size, heads):
    part_refs = refs[:devices]
    mid_ref, cotangent_ref, gain_ref, merged_ref, log_ref, weight_ref = refs[
        devices : devices + 6
    ]
    message_ref, branch_ref, base_ref, sums_ref = refs[devices + 6 :]
    own, width = mid_ref.shape
    half = width // chunks
    gradient = total_of([x[...] for x in part_refs])
    back, gain_sum, bias_sum = norm_backward(mid_ref[...], gain_ref[...], gradient)
    grad_mid = cotangent_ref[...] + back
    sums_ref[...] = jnp.zeros(sums_ref.shape, F32)
    sums_ref[0:1, :] = gain_sum
    sums_ref[1:2, :] = bias_sum
    row_total = own // items
    base_ref[...] = total_of(
        [grad_mid[i * row_total : (i + 1) * row_total] for i in range(items)]
    )
    branch = grad_mid.astype(BF16)
    branch_ref[:, :width] = branch
    branch_ref[:, width:] = merged_ref[...].astype(BF16)
    grad_att = transposed_right(branch, weight_ref[...]).astype(BF16)
    expand = head_expand(half, head_size)
    lane, column = iota((6 * LANES, LANES), 0), iota((6 * LANES, LANES), 1)
    place = jnp.logical_and(
        lane % LANES < heads, column == (lane // LANES) * heads + lane % LANES
    ).astype(BF16)
    message_ref[:, :width] = grad_att
    for c in range(chunks):
        columns = slice(c * half, (c + 1) * half)
        delta = lax.dot_general(
            merged_ref[:, columns] * grad_att[:, columns].astype(F32),
            expand,
            (((1,), (1,)), ((), ())),
            precision=HIGHEST,
            preferred_element_type=F32,
        )
        terms = jnp.concatenate([t for x in (log_ref[c], delta) for t in split_terms(x)], 1)
        message_ref[:, width + c * LANES : width + (c + 1) * LANES] = matmul(
            terms, place
        ).astype(BF16)


def backward_kernel(
    *refs, frames, items, patches, scale, head_size, heads,
):
    flag_ref, both_ref, query_ref, top_ref = refs[:4]
    grad_refs = refs[4 : 4 + frames]
    mark_refs = refs[4 + frames : 4 + 2 * frames]
    out_ref, sum_ref, held_ref, note_ref = refs[4 + 2 * frames :]
    lats, width = query_ref.shape
    own = grad_refs[0].shape[0]
    row_total = own // items
    base = items * patches
    for s in range(frames):
        source = lax.rem(flag_ref[items + 1] + (frames - s), frames)
        rows = pl.ds(pl.multiple_of(source * row_total, row_total), row_total)
        block = grad_refs[s][...].astype(F32)
        mark = mark_refs[s][...].astype(F32)
        for i in range(items):
            held_ref[i, rows, :] = block[i * row_total : (i + 1) * row_total]
            note_ref[i, rows, :] = mark[i * row_total : (i + 1) * row_total]
    masks = head_masks(lats, width, head_size)
    queries = spread_heads(query_ref[...].astype(F32), masks).astype(BF16)
    lat_both = both_ref[base : base + lats, :]
    row, lane = iota((GROUP * 8, LANES), 0), iota((GROUP * 8, LANES), 1)
    pick = jnp.logical_and(
        jnp.logical_and(
            lane // heads // 3 == row % 8,
            lane % heads == pl.program_id(0) * GROUP + row // 8,
        ),
        lane < 6 * heads,
    ).astype(BF16)
    grad_query = jnp.zeros((queries.shape[0], width), F32)
    lat_grad_key = jnp.zeros((lats, width), F32)
    lat_grad_value = jnp.zeros((lats, width), F32)
    for i in range(items):
        rows = slice(i * patches, (i + 1) * patches)
        stats = transposed_right(pick, note_ref[i].astype(BF16))
        stats = jnp.concatenate([stats[h * 8 : (h + 1) * 8] for h in range(GROUP)], 1)
        log_total = stats[0:1]
        delta = stats[1:2]
        top = top_ref[0, i, 0:1, :]
        rescale = jnp.exp(top - log_total)
        both = jnp.concatenate([both_ref[rows, :], lat_both], 0)
        keys, values = both[:, :width], both[:, width:]
        grads = spread_heads(held_ref[i], masks).astype(BF16)
        live = live_rows(flag_ref, i, items, patches, lats, queries.shape[0])
        masked = jnp.where(live, scale * transposed_right(keys, queries), MASKED)
        probs = jnp.where(live, jnp.exp(masked - log_total), 0.0)
        block_exp = jnp.where(live, jnp.exp(masked - top), 0.0)
        weights = (block_exp.astype(BF16).astype(F32) * rescale).astype(BF16)
        grad_scores = (probs * (transposed_right(values, grads) - delta)).astype(BF16)
        grad_key = scale * matmul(grad_scores, queries)
        grad_value = matmul(weights, grads)
        out_ref[rows, :width] = grad_key[:patches].astype(BF16)
        out_ref[rows, width:] = grad_value[:patches].astype(BF16)
        grad_query = grad_query + transposed_left(grad_scores, keys)
        lat_grad_key = lat_grad_key + grad_key[patches:]
        lat_grad_value = lat_grad_value + grad_value[patches:]
    out_ref[base : base + lats, :width] = lat_grad_key.astype(BF16)
    out_ref[base : base + lats, width:] = lat_grad_value.astype(BF16)
    sum_ref[...] = scale * collect_heads(grad_query, masks)


def media_kernel(flag_ref, *refs, chunks, items, frames):
    grad_refs, lat_refs, weight_refs = [
        refs[k * chunks : (k + 1) * chunks] for k in range(3)
    ]
    media_ref, time_ref, gain_ref, out_ref, sums_ref, product_ref = refs[3 * chunks :]
    item = pl.program_id(0)

    @pl.when(item == 0)
    def _():
        sums_ref[...] = jnp.zeros(sums_ref.shape, F32)
        product_ref[...] = functools.reduce(
            jnp.add, [transposed_right(g[...], w[...]) for g, w in zip(lat_refs, weight_refs)]
        )

    gradient = functools.reduce(
        jnp.add, [transposed_right(g[...], w[...]) for g, w in zip(grad_refs, weight_refs)]
    )
    inputs = media_ref[...].astype(F32) + time_ref[pl.ds(item, 1), :]
    back, gain_sum, bias_sum = norm_backward(inputs, gain_ref[...], gradient)
    out_ref[...] = back.astype(BF16)
    place = iota((frames, 1), 0) == flag_ref[items + 2 + item]
    sums_ref[0:frames, :] += jnp.where(place, jnp.sum(back, axis=0, keepdims=True), 0.0)
    sums_ref[8:9, :] += gain_sum
    sums_ref[9:10, :] += bias_sum


def latent_kernel(flag_ref, *refs, chunks, items):
    query_refs = refs[:chunks]
    (
        product_ref, latent_ref, gain_ref, base_ref, ffn_ref, media_ref, out_ref,
    ) = refs[chunks:]
    lats, width = latent_ref.shape
    half = width // chunks
    gradient = product_ref[...]
    for c in range(chunks):
        out_ref[lats : 2 * lats, c * half : (c + 1) * half] = query_refs[c][...]
    back, gain_sum, bias_sum = norm_backward(latent_ref[...], gain_ref[...], gradient)
    out_ref[:lats, :] = back
    row_total = base_ref.shape[0]
    start = pl.multiple_of(flag_ref[items + 1] * row_total, row_total)
    out_ref[pl.ds(start, row_total), :] += base_ref[...]
    at = 2 * lats
    out_ref[at : at + 8, :] = ffn_ref[...]
    out_ref[at + 2 : at + 3, :] = gain_sum
    out_ref[at + 3 : at + 4, :] = bias_sum
    out_ref[at + 8 : at + 24, :] = media_ref[...]
    out_ref[at + 24 :, :] = jnp.zeros((out_ref.shape[0] - at - 24, width), F32)


def query_norm_kernel(flag_ref, *refs, devices, items):
    column_refs = refs[:devices]
    latent_ref, gain_ref, sum_ref, out_ref, out_gain_ref, out_bias_ref, held_ref = refs[devices:]
    for d in range(devices):
        held_ref[jnp.bitwise_xor(flag_ref[2 * items + 2], d)] = column_refs[d][...]
    gradient = jnp.concatenate([held_ref[k] for k in range(devices)], 1)
    back, gain_sum, bias_sum = norm_backward(latent_ref[...], gain_ref[...], gradient)
    lats = latent_ref.shape[0]
    out_ref[...] = sum_ref[:lats, :] + back
    out_gain_ref[...] = sum_ref[2 * lats + 2 : 2 * lats + 3, :] + gain_sum
    out_bias_ref[...] = sum_ref[2 * lats + 3 : 2 * lats + 4, :] + bias_sum


def rows_kernel(flag_ref, *refs, count, frames, items):
    part_refs, out_refs, held_ref = refs[:count], refs[count:-1], refs[-1]
    rows = held_ref.shape[1]
    column = 0
    for part_ref in part_refs:
        total = total_of([part_ref[k] for k in range(part_ref.shape[0])])
        for f in range(frames):
            held_ref[f, :, column : column + total.shape[1]] = total[f * rows : (f + 1) * rows]
        column += total.shape[1]
    for s, out_ref in enumerate(out_refs):
        block = held_ref[lax.rem(flag_ref[items + 1] + s, frames)]
        out_ref[...] = block.astype(out_ref.dtype)


def place_kernel(flag_ref, *refs, chunks, frames, items, groups):
    chunk_refs = refs[: chunks * frames]
    key_ref, value_ref, out_ref = refs[chunks * frames :]
    width = key_ref.shape[2] // (chunks * groups)
    for s in range(frames):
        source = lax.rem(flag_ref[items + 1] + (frames - s), frames)
        out_ref[source] = chunk_refs[s][:, 2 * groups * width :].astype(F32)
        for c in range(chunks):
            for g in range(groups):
                at = (c * groups + g) * width
                block = chunk_refs[c * frames + s][:, 2 * g * width : 2 * (g + 1) * width]
                block = block.astype(F32)
                key_ref[source, :, at : at + width] = block[:, :width]
                value_ref[source, :, at : at + width] = block[:, width:]


def body(
    media,
    cotangent,
    frame_count,
    frame_start,
    latents,
    time_embed,
    media_gain,
    media_bias,
    latent_gain,
    latent_bias,
    ffn_gain,
    ffn_bias,
    query_weight,
    key_weight,
    value_weight,
    out_weight,
    up_weight,
    down_weight,
):
    items = media.shape[0]
    patches = media.shape[2]
    width = media.shape[3]
    lats = latents.shape[0]
    frame_total = time_embed.shape[0]
    row_total = cotangent.shape[1]
    own = items * row_total
    head_size = width // HEADS
    half = width // CHUNKS
    chunk_heads = HEADS // CHUNKS
    group_width = GROUP * head_size
    groups = chunk_heads // GROUP
    stack = GROUP * lats
    tokens = items * patches
    all_tokens = tokens + lats
    shard = query_weight.shape[0]
    hidden_shard = down_weight.shape[0]
    item_size = lax.axis_size("items")
    frame_size = lax.axis_size("frames")
    plane = item_size * own
    item_index = lax.axis_index("items")
    slot = lax.axis_index("frames")
    row_base = slot * row_total
    params = pltpu.CompilerParams(vmem_limit_bytes=56 * 2**20)
    smem = pl.BlockSpec(memory_space=pltpu.SMEM)
    whole = pl.BlockSpec(memory_space=pltpu.VMEM)
    sizes = dict(items=items, head_size=head_size, heads=chunk_heads)

    def struct(shape, kind):
        return jax.ShapeDtypeStruct(shape, kind)

    def cost(micros):
        return pl.CostEstimate(
            flops=int(micros * 1.15e9), bytes_accessed=int(micros * 3.6e6), transcendentals=0
        )

    def column_blocks(x):
        return jnp.transpose(x.reshape(-1, item_size, shard), (1, 0, 2))

    def scatter_exchange(x, axis):
        return jnp.sum(lax.all_to_all(x, axis, 0, 0).astype(F32), axis=0)

    grad_out = cotangent.reshape(own, width)
    low_columns = own * width // shard
    joined, grad_low = pl.pallas_call(
        functools.partial(join_kernel, width=group_width),
        out_shape=[struct((shard, 2 * width + low_columns), BF16), struct((own, width), BF16)],
        cost_estimate=cost(2.5),
        compiler_params=params,
    )(key_weight, value_weight, grad_out)
    kv_full = lax.all_gather(joined, "items", axis=0, tiled=True)
    low_frames = jnp.stack(spread_on(grad_low, "frames"))

    lat_norm = layer_norm(latents, latent_gain, latent_bias).astype(BF16)
    lat_cols = lax.dynamic_slice_in_dim(lat_norm, item_index * shard, shard, 1)
    query_blocks = column_blocks(matmul(lat_cols, query_weight))
    query_cols = scatter_exchange(query_blocks, "items").astype(BF16)
    query_spread = jnp.broadcast_to(query_cols[None], (item_size, lats, shard))
    queries = jnp.transpose(lax.all_to_all(query_spread, "items", 0, 0), (1, 0, 2)).reshape(
        lats, width
    )

    counts = lax.dynamic_slice_in_dim(frame_count, item_index * items, items)
    starts = lax.dynamic_slice_in_dim(frame_start, item_index * items, items)
    offset = (slot - starts) % frame_total
    flags = jnp.concatenate(
        [
            (offset < counts).astype(jnp.int32),
            (slot == 0).astype(jnp.int32)[None],
            slot.astype(jnp.int32)[None],
            offset.astype(jnp.int32),
            item_index.astype(jnp.int32)[None],
        ]
    )
    picker = (offset[:, None] == jnp.arange(frame_total, dtype=jnp.int32)[None, :]).astype(F32)
    time_rows = jnp.dot(picker, time_embed, precision=HIGHEST, preferred_element_type=F32)
    flat_media = media.reshape(tokens, width)
    steps = tokens // lats
    all_rows = pl.pallas_call(
        functools.partial(norm_kernel, steps=steps, per_item=patches // lats),
        grid=(steps + 1,),
        in_specs=[
            pl.BlockSpec((lats, width), lambda i: (jnp.minimum(i, steps - 1), 0)),
            whole,
            whole,
            whole,
            whole,
        ],
        out_specs=pl.BlockSpec((lats, width), lambda i: (i, 0)),
        out_shape=struct((all_tokens, width), BF16),
        cost_estimate=cost(12),
        compiler_params=params,
    )(
        after(flat_media, query_blocks),
        time_rows,
        media_gain[None],
        media_bias[None],
        lat_norm,
    )
    out_full = lax.all_gather(after(out_weight, all_rows), "items", axis=0, tiled=True)

    core = item_index % 2
    rows_across = after(all_rows, query_cols).T.reshape(item_size // 2, 2, shard, all_tokens)
    send_rows, keep_rows = [
        jnp.concatenate(
            [
                lax.dynamic_slice(
                    rows_across, (k, which, 0, 0), (1, 1, shard, all_tokens)
                ).reshape(shard, all_tokens)
                for k in range(item_size // 2)
            ],
            0,
        )
        for which in (1 - core, core)
    ]
    boths, tops, messages = [], [], []
    for c in range(CHUNKS):

        def block_of(g, c=c):
            return (0, c * groups + g)

        if c:
            rows = after(all_rows, tops[-1])
        else:
            rows = after(all_rows, queries, send_rows, keep_rows)
        both = matmul(rows, kv_full[:, 2 * c * half : 2 * (c + 1) * half]).astype(BF16)
        top, *parts = pl.pallas_call(
            functools.partial(
                forward_kernel, patches=patches, scale=head_size**-0.5, **sizes
            ),
            grid=(groups,),
            in_specs=[
                smem,
                pl.BlockSpec((all_tokens, 2 * group_width), lambda g: (0, g)),
                pl.BlockSpec((lats, group_width), block_of),
            ],
            out_specs=[pl.BlockSpec((1, items, 8, stack), lambda g: (g, 0, 0, 0))]
            + [pl.BlockSpec((own, half + LANES), lambda g: (0, 0))] * frame_size,
            out_shape=[struct((groups, items, 8, stack), F32)]
            + [struct((own, half + LANES), BF16)] * frame_size,
            scratch_shapes=[
                pltpu.VMEM((items, lats, group_width), F32),
                pltpu.VMEM((items, lats, LANES), F32),
            ],
            cost_estimate=cost(7.8),
            compiler_params=params,
        )(flags, after(both, *messages) if c else both, queries)
        boths.append(both)
        tops.append(top)
        messages += [p if s == 0 else send_on(p, "frames", s) for s, p in enumerate(parts)]
    up_slice = lax.all_to_all(after(up_weight, boths[0]), "items", 1, 0, tiled=True)
    low_all = lax.all_gather(after(low_frames, tops[1]), "items", axis=0).reshape(-1, width)

    base_rows = lax.dynamic_slice_in_dim(latents, row_base, row_total, 0)
    merged, mid_rows, ffn_in, logs, entropy_wide = pl.pallas_call(
        functools.partial(merge_kernel, chunks=CHUNKS, frames=frame_size, **sizes),
        out_shape=[
            struct((own, width), F32),
            struct((own, width), F32),
            struct((own, width), BF16),
            struct((CHUNKS, own, LANES), F32),
            struct((own, LANES), F32),
        ],
        cost_estimate=cost(6.3),
        compiler_params=params,
    )(*messages, base_rows, out_full, ffn_gain[None], ffn_bias[None])
    entropy = entropy_wide[:, 0].reshape(items, row_total)

    ffn_blocks = spread_across(ffn_in, "items")
    ffn_frames = spread_on(after(ffn_in, *ffn_blocks), "frames")
    result_part, *parts = pl.pallas_call(
        functools.partial(feed_kernel, devices=item_size, items=items),
        grid=(1,),
        in_specs=[smem]
        + [whole] * item_size
        + [
            pl.BlockSpec((width, low_columns), lambda i: (0, 2 * width // low_columns)),
            whole,
            whole,
        ],
        out_specs=[whole] * (1 + item_size),
        out_shape=[struct((item_size, own, width), BF16)]
        + [struct((own, width), BF16)] * item_size,
        scratch_shapes=[pltpu.VMEM((plane, width), BF16)] * 2,
        cost_estimate=cost(10),
        compiler_params=params,
    )(flags, *ffn_blocks, kv_full, up_slice, down_weight)
    grad_blocks = collect_across(parts, "items")
    grad_blocks[0] = after(grad_blocks[0], *ffn_frames)
    ffn_all = lax.all_gather(
        after(jnp.stack(ffn_frames), parts[0]), "items", axis=0
    ).reshape(-1, width)

    turn, grad_branch, grad_base, ffn_sums = pl.pallas_call(
        functools.partial(turn_kernel, devices=item_size, chunks=CHUNKS, **sizes),
        out_shape=[
            struct((own, width + CHUNKS * LANES), BF16),
            struct((own, 2 * width), BF16),
            struct((row_total, width), F32),
            struct((8, width), F32),
        ],
        cost_estimate=cost(7.6),
        compiler_params=params,
    )(*grad_blocks, mid_rows, grad_out, ffn_gain[None], merged, logs, out_full)
    turns = spread_on(turn, "frames")
    branch_plane = lax.all_gather(grad_branch, "items", axis=0, tiled=True)
    result_sum = lax.psum_scatter(
        after(result_part, grad_branch).reshape(-1, width), "items", scatter_dimension=0, tiled=True
    )
    att_plane = lax.dynamic_slice_in_dim(
        branch_plane, width + item_index * shard, shard, 1
    )
    turns[0] = after(turns[0], low_all)

    chunk_grads, chunk_queries = [], []

    def weight_terms(c):
        send = matmul(send_rows, chunk_grads[c]).astype(BF16)
        received = send_across(send, "items", 1).reshape(-1, shard, 2 * half)
        keep = matmul(after(keep_rows, send), chunk_grads[c]).astype(BF16)
        return send, keep.reshape(-1, shard, 2 * half), received

    def chip_terms(keep, received):
        return (keep.astype(F32) + received.astype(F32)).astype(BF16)

    def exchange_chips(x):
        groups_of = [list(range(k, item_size, 2)) for k in range(2)]
        return lax.all_to_all(x, "items", 0, 0, axis_index_groups=groups_of)

    def permute_chips(x):
        chip = item_index // 2
        out = []
        for k in range(item_size // 2):
            piece = lax.dynamic_index_in_dim(x, chip ^ k, 0, False)
            out.append(send_across(piece, "items", 2 * k) if k else piece)
        return out

    def frame_rows(ranges):
        rows = shard // frame_size
        columns = sum(x.shape[-1] for x in ranges)
        return pl.pallas_call(
            functools.partial(rows_kernel, count=len(ranges), frames=frame_size, items=items),
            in_specs=[smem] + [whole] * len(ranges),
            out_specs=[whole] * frame_size,
            out_shape=[struct((rows, columns), F32)]
            + [struct((rows, columns), BF16)] * (frame_size - 1),
            scratch_shapes=[pltpu.VMEM((frame_size, rows, columns), F32)],
            cost_estimate=cost(3.5),
            compiler_params=params,
        )(flags, *ranges)

    def send_rows_on(rows):
        return [rows[0]] + [send_on(p, "frames", s) for s, p in enumerate(rows) if s]

    for c in range(CHUNKS):

        def block_of(g, c=c):
            return (0, c * groups + g)

        chunk_grad, chunk_query = pl.pallas_call(
            functools.partial(
                backward_kernel, frames=frame_size, patches=patches, scale=head_size**-0.5, **sizes
            ),
            grid=(groups,),
            in_specs=[
                smem,
                pl.BlockSpec((all_tokens, 2 * group_width), lambda g: (0, g)),
                pl.BlockSpec((lats, group_width), block_of),
                pl.BlockSpec((1, items, 8, stack), lambda g: (g, 0, 0, 0)),
            ]
            + [pl.BlockSpec((own, group_width), block_of)] * frame_size
            + [pl.BlockSpec((own, LANES), lambda g, c=c: (0, width // LANES + c))] * frame_size,
            out_specs=[
                pl.BlockSpec((all_tokens, 2 * group_width), lambda g: (0, g)),
                pl.BlockSpec((lats, group_width), lambda g: (0, g)),
            ],
            out_shape=[
                struct((all_tokens, 2 * half), BF16),
                struct((lats, half), F32),
            ],
            scratch_shapes=[
                pltpu.VMEM((items, lats, group_width), F32),
                pltpu.VMEM((items, lats, LANES), F32),
            ],
            cost_estimate=cost(8),
            compiler_params=params,
        )(flags, after(boths[c], *held) if c else boths[c], queries, tops[c], *turns, *turns)
        chunk_grads.append(chunk_grad)
        chunk_queries.append(chunk_query)
        if c == 0:
            first_send, first_keep, first_received = weight_terms(0)
            held = (first_send, ffn_all)
    first_terms = chip_terms(after(first_keep, chunk_grads[-1]), first_received)
    first_moved = exchange_chips(first_terms)
    last_grad = chunk_grads[-1]
    chunk_grads[-1] = after(last_grad, first_terms)
    last_send, last_keep, last_received = weight_terms(CHUNKS - 1)
    last_terms = chip_terms(last_keep, last_received)
    last_moved = permute_chips(last_terms)
    chunk_grads[-1] = last_grad
    out_part = transposed_left(att_plane, after(branch_plane, last_send)[:, :width])

    last_block = pl.BlockSpec((lats, 2 * half), lambda i: (tokens // lats, 0))
    media_grad, media_sums, lat_product = pl.pallas_call(
        functools.partial(media_kernel, chunks=CHUNKS, items=items, frames=frame_total),
        grid=(items,),
        in_specs=[smem]
        + [pl.BlockSpec((patches, 2 * half), lambda i: (i, 0))] * CHUNKS
        + [last_block] * CHUNKS
        + [pl.BlockSpec((width, 2 * half), lambda i, c=c: (0, c)) for c in range(CHUNKS)]
        + [pl.BlockSpec((patches, width), lambda i: (i, 0)), whole, whole],
        out_specs=[
            pl.BlockSpec((patches, width), lambda i: (i, 0)),
            pl.BlockSpec((16, width), lambda i: (0, 0)),
            pl.BlockSpec((lats, width), lambda i: (0, 0)),
        ],
        out_shape=[
            struct((tokens, width), BF16),
            struct((16, width), F32),
            struct((lats, width), F32),
        ],
        cost_estimate=cost(21),
        compiler_params=params,
    )(
        flags,
        *chunk_grads[:-1],
        after(chunk_grads[-1], last_moved[0], out_part),
        *chunk_grads,
        *[kv_full] * CHUNKS,
        flat_media,
        time_rows,
        media_gain[None],
    )

    sum_rows = 2 * lats + 24
    sum_rows += -sum_rows % (8 * item_size)
    payload = pl.pallas_call(
        functools.partial(latent_kernel, chunks=CHUNKS, items=items),
        in_specs=[smem] + [whole] * (CHUNKS + 6),
        out_specs=whole,
        out_shape=struct((sum_rows, width), F32),
        cost_estimate=cost(3),
        compiler_params=params,
    )(
        flags,
        *chunk_queries,
        after(lat_product, first_moved),
        latents,
        latent_gain[None],
        grad_base,
        ffn_sums,
        media_sums,
    )
    payload_part = lax.psum_scatter(payload, "items", scatter_dimension=0, tiled=True)

    first_rows = frame_rows([after(first_moved, payload), out_part[None]])
    first_frames = send_rows_on(first_rows)
    all_plane = plane * frame_size
    block_rows = min(512, all_plane)
    row_block = pl.BlockSpec((block_rows, width), lambda i: (i, 0))
    hidden_block = pl.BlockSpec((block_rows, hidden_shard), lambda i: (i, 0))
    hidden, grad_up = pl.pallas_call(
        feed_back_kernel,
        grid=(all_plane // block_rows,),
        in_specs=[row_block, row_block, whole, whole],
        out_specs=[hidden_block, hidden_block],
        out_shape=[struct((all_plane, hidden_shard), BF16)] * 2,
        cost_estimate=cost(15),
        compiler_params=params,
    )(after(ffn_all, *first_rows, *last_moved), low_all, up_slice, down_weight)

    def outer(left, right, tile, kind):
        rows, columns = left.shape
        shape = (columns, right.shape[1])
        return pl.pallas_call(
            outer_kernel,
            grid=(columns // tile,),
            in_specs=[pl.BlockSpec((rows, tile), lambda i: (0, i)), whole],
            out_specs=pl.BlockSpec((tile, shape[1]), lambda i: (i, 0)),
            out_shape=struct(shape, kind),
            cost_estimate=cost(9.5),
            compiler_params=params,
        )(left, right)

    first_total = total_of(first_frames).astype(BF16)
    first_placed = spread_on(first_total, "frames")
    last_rows = frame_rows([after(jnp.stack(last_moved), hidden)])
    last_frames = send_rows_on(last_rows)
    up_part = outer(ffn_all, after(grad_up, first_total, *last_rows), width // 4, BF16)
    up_grad = lax.all_to_all(up_part, "items", 0, 1, tiled=True).astype(F32)
    last_total = total_of(last_frames).astype(BF16)
    last_placed = spread_on(last_total, "frames")
    down_grad = outer(
        after(hidden, up_part, last_total, *first_placed),
        low_all,
        256 if hidden_shard % 256 == 0 else hidden_shard,
        F32,
    )
    placed = first_placed + last_placed
    payload_part = after(payload_part, up_part)
    payload_others = spread_on(payload_part.astype(BF16), "frames")[1:]
    sums = lax.all_gather(
        total_of([payload_part] + payload_others), "items", axis=0, tiled=True
    )
    query_low = sums[lats : 2 * lats].astype(BF16)
    query_grad = transposed_left(lat_cols, query_low)
    norm_cols = transposed_right(query_low, query_weight)
    latents_grad, lat_gain, lat_bias = pl.pallas_call(
        functools.partial(query_norm_kernel, devices=item_size, items=items),
        in_specs=[smem] + [whole] * (item_size + 3),
        out_specs=[whole] * 3,
        out_shape=[struct((lats, width), F32), struct((1, width), F32), struct((1, width), F32)],
        scratch_shapes=[pltpu.VMEM((item_size, lats, shard), F32)],
        cost_estimate=cost(3),
        compiler_params=params,
    )(flags, *spread_across(norm_cols, "items"), latents, latent_gain[None], sums)
    at = 2 * lats
    column_sums = lax.dynamic_slice_in_dim(
        sums[at + 8 : at + 24], item_index * shard, shard, 1
    )

    key_grad, value_grad, out_grad = pl.pallas_call(
        functools.partial(
            place_kernel, chunks=CHUNKS, frames=frame_size, items=items, groups=groups
        ),
        in_specs=[smem] + [whole] * len(placed),
        out_specs=[whole] * 3,
        out_shape=[struct((frame_size, shard // frame_size, width), F32)] * 3,
        cost_estimate=cost(3.4),
        compiler_params=params,
    )(flags, *placed)

    result = mid_rows + result_sum.astype(F32)
    return (
        result.reshape(items, row_total, width),
        entropy,
        media_grad.reshape(media.shape),
        latents_grad,
        column_sums[:frame_total],
        column_sums[8],
        column_sums[9],
        lat_gain[0],
        lat_bias[0],
        sums[at],
        sums[at + 1],
        query_grad,
        key_grad.reshape(shard, width),
        value_grad.reshape(shard, width),
        out_grad.reshape(shard, width),
        up_grad,
        down_grad,
    )


def solution(mesh):
    return jax.shard_map(
        body,
        mesh=mesh,
        in_specs=(
            P("items", "frames", None, None),
            P("items", "frames", None),
            P(),
            P(),
            P(),
            P(),
            P(),
            P(),
            P(),
            P(),
            P(),
            P(),
            P("items", None),
            P("items", None),
            P("items", None),
            P("items", None),
            P("items", None),
            P("items", None),
        ),
        out_specs=(
            P("items", "frames", None),
            P("items", "frames"),
            P("items", "frames", None, None),
            P(),
            P(None, "items"),
            P("items"),
            P("items"),
            P(),
            P(),
            P(),
            P(),
            P("items", None),
            P("items", None),
            P("items", None),
            P("items", None),
            P("items", None),
            P("items", None),
        ),
        check_vma=False,
    )
```

```python
import functools
import math

import jax
import jax.numpy as jnp
from jax import lax
from jax.experimental import pallas as pl
from jax.experimental.pallas import tpu as pltpu
from jax.sharding import PartitionSpec as P

HEADS = 16
GROUP = 4
CHUNKS = 2
LANES = 128
EPSILON = 1e-05
MASKED = -1e30
F32 = jnp.float32
BF16 = jnp.bfloat16
HIGHEST = lax.Precision.HIGHEST


def layer_norm(inputs, norm_gain, norm_bias):
    center = inputs - jnp.mean(inputs, axis=-1, keepdims=True)
    spread = jnp.mean(center * center, axis=-1, keepdims=True)
    return center * lax.rsqrt(spread + EPSILON) * norm_gain + norm_bias


def matmul(left_side, right_side):
    return jnp.dot(left_side, right_side, preferred_element_type=F32)


def transposed_left(left_side, right_side):
    return lax.dot_general(
        left_side, right_side, (((0,), (0,)), ((), ())), preferred_element_type=F32
    )


def transposed_right(left_side, right_side):
    return lax.dot_general(
        left_side, right_side, (((1,), (1,)), ((), ())), preferred_element_type=F32
    )


def send_on(x, axis, step):
    size = lax.axis_size(axis)
    return lax.ppermute(x, axis, [(i, (i + step) % size) for i in range(size)])


def send_across(x, axis, distance):
    return lax.ppermute(x, axis, [(i, i ^ distance) for i in range(lax.axis_size(axis))])


def spread_on(x, axis):
    return [x] + [send_on(x, axis, s) for s in range(1, lax.axis_size(axis))]


def spread_across(x, axis):
    chips = [x] + [send_across(x, axis, d) for d in range(2, lax.axis_size(axis), 2)]
    return [b for block in chips for b in (block, send_across(block, axis, 1))]


def collect_across(pieces, axis):
    return [pieces[0]] + [send_across(p, axis, d) for d, p in enumerate(pieces) if d]


def total_of(pieces):
    return functools.reduce(jnp.add, [p.astype(F32) for p in pieces])


def after(x, *earlier):
    return lax.optimization_barrier((x,) + earlier)[0]


def split_terms(x):
    high = x.astype(BF16)
    rest = x - high.astype(F32)
    middle = rest.astype(BF16)
    return high, middle, (rest - middle.astype(F32)).astype(BF16)


def iota(shape, dim):
    return lax.broadcasted_iota(jnp.int32, shape, dim)


def head_masks(rows, width, head_size):
    lane = iota((rows, width), 1)
    return [
        jnp.logical_and(lane >= h * head_size, lane < (h + 1) * head_size)
        for h in range(width // head_size)
    ]


def spread_heads(block, masks):
    return jnp.concatenate([jnp.where(m, block, jnp.zeros_like(block)) for m in masks], 0)


def collect_heads(block, masks):
    rows = block.shape[0] // len(masks)
    total = jnp.where(masks[0], block[:rows], 0.0)
    for h in range(1, len(masks)):
        total = total + jnp.where(masks[h], block[h * rows : (h + 1) * rows], 0.0)
    return total


def head_expand(width, head_size):
    row, column = iota((LANES, width), 0), iota((LANES, width), 1)
    return jnp.logical_and(column >= row * head_size, column < (row + 1) * head_size).astype(F32)


def live_rows(flag_ref, item, items, patches, lats, columns):
    row = iota((patches + lats, columns), 0)
    media = jnp.logical_and(row < patches, flag_ref[item] > 0)
    return jnp.logical_or(media, jnp.logical_and(row >= patches, flag_ref[items] > 0))


def pack_shape(own, shard, width):
    unit = math.gcd(own, shard)
    return unit, width * unit // shard


def join_kernel(key_ref, value_ref, cotangent_ref, out_ref, low_ref, *, width):
    for g in range(key_ref.shape[1] // width):
        columns = slice(g * width, (g + 1) * width)
        out_ref[:, 2 * g * width : (2 * g + 1) * width] = key_ref[:, columns]
        out_ref[:, (2 * g + 1) * width : (2 * g + 2) * width] = value_ref[:, columns]
    low = cotangent_ref[...].astype(BF16)
    low_ref[...] = low
    own, span = low.shape
    unit, piece = pack_shape(own, out_ref.shape[0], span)
    for a in range(own // unit):
        for b in range(span // piece):
            at = 2 * span + a * piece
            out_ref[b * unit : (b + 1) * unit, at : at + piece] = low[
                a * unit : (a + 1) * unit, b * piece : (b + 1) * piece
            ]


def norm_kernel(media_ref, time_ref, gain_ref, bias_ref, lat_ref, out_ref, *, steps, per_item):
    step = pl.program_id(0)

    @pl.when(step < steps)
    def _():
        rows = media_ref[...].astype(F32) + time_ref[pl.ds(step // per_item, 1), :]
        out_ref[...] = layer_norm(rows, gain_ref[...], bias_ref[...]).astype(BF16)

    @pl.when(step == steps)
    def _():
        out_ref[...] = lat_ref[...]


def forward_kernel(
    flag_ref, both_ref, query_ref, top_ref, *refs, items, patches, scale, head_size, heads,
):
    message_refs, (part_ref, mark_ref) = refs[:-2], refs[-2:]
    lats, width = query_ref.shape
    frames = len(message_refs)
    own = message_refs[0].shape[0]
    row_total = own // items
    masks = head_masks(lats, width, head_size)
    queries = spread_heads(query_ref[...].astype(F32), masks).astype(BF16)
    base = items * patches
    lat_both = both_ref[base : base + lats, :]
    group = pl.program_id(0)
    term, lane = iota((16, GROUP * LANES), 0), iota((16, GROUP * LANES), 1)
    place = jnp.logical_and(
        lane % LANES == term * heads + group * GROUP + lane // LANES, term < 9
    ).astype(BF16)
    for i in range(items):
        both = jnp.concatenate([both_ref[i * patches : (i + 1) * patches, :], lat_both], 0)
        live = live_rows(flag_ref, i, items, patches, lats, queries.shape[0])
        scores = scale * transposed_right(both[:, :width], queries)
        masked = jnp.where(live, scores, MASKED)
        top = jnp.max(masked, axis=0, keepdims=True)
        block_exp = jnp.where(live, jnp.exp(masked - top), 0.0)
        total = jnp.sum(block_exp, axis=0, keepdims=True)
        moment = jnp.sum(block_exp * scores, axis=0, keepdims=True)
        part = transposed_left(block_exp.astype(BF16), both[:, width:])
        part_ref[i] = collect_heads(part, masks)
        top_ref[0, i] = jnp.broadcast_to(top, top_ref.shape[2:])
        terms = jnp.concatenate(
            [t.astype(F32) for x in (top, total, moment) for t in split_terms(x)]
            + [jnp.zeros((7, top.shape[1]), F32)],
            0,
        ).astype(BF16)
        wide = transposed_left(terms, place)
        mark = wide[:lats, :LANES]
        for h in range(1, GROUP):
            mark = mark + wide[h * lats : (h + 1) * lats, h * LANES : (h + 1) * LANES]
        mark_ref[i] = mark

    end = message_refs[0].shape[1] - LANES
    for s, message_ref in enumerate(message_refs):
        start = pl.multiple_of(lax.rem(flag_ref[items + 1] + s, frames) * row_total, row_total)
        rows = pl.ds(start, row_total)
        block = jnp.concatenate([part_ref[i, rows, :] for i in range(items)], 0).astype(BF16)
        mark = jnp.concatenate([mark_ref[i, rows, :] for i in range(items)], 0).astype(BF16)
        for g in range(end // width):

            @pl.when(group == g)
            def _():
                message_ref[:, g * width : (g + 1) * width] = block
                if g == 0:
                    message_ref[:, end:] = mark
                else:
                    message_ref[:, end:] = message_ref[:, end:] + mark


def merge_kernel(*refs, chunks, frames, items, head_size, heads):
    message_refs = refs[: chunks * frames]
    base_ref, weight_ref, gain_ref, bias_ref = refs[chunks * frames : chunks * frames + 4]
    merged_ref, mid_ref, ffn_ref, log_ref, entropy_ref = refs[chunks * frames + 4 :]
    own, columns = message_refs[0].shape
    half = columns - LANES
    lane, column = iota((LANES, 3 * LANES), 0), iota((LANES, 3 * LANES), 1)
    gather = jnp.logical_and(
        jnp.logical_and(lane // heads // 3 == column // LANES, lane % heads == column % LANES),
        lane < 9 * heads,
    ).astype(BF16)
    expand = head_expand(half, head_size)
    live = iota((own, LANES), 1) < heads
    spread = jnp.zeros((own, LANES), F32)
    for c in range(chunks):
        sources = message_refs[c * frames : (c + 1) * frames]
        stats = [matmul(x[:, half:], gather) for x in sources]
        tops = [x[:, :LANES] for x in stats]
        peak = functools.reduce(jnp.maximum, tops)
        factors = [jnp.exp(t - peak) for t in tops]
        whole = sum(f * x[:, LANES : 2 * LANES] for f, x in zip(factors, stats))
        moment = sum(f * x[:, 2 * LANES :] for f, x in zip(factors, stats))
        whole = jnp.where(live, whole, 1.0)
        log_total = jnp.where(live, peak + jnp.log(whole), 0.0)
        log_ref[c] = log_total
        spread = spread + jnp.where(live, log_total - moment / whole, 0.0)
        merged = jnp.zeros((own, half), F32)
        for x, factor in zip(sources, factors):
            share = jnp.where(live, factor / whole, 0.0)
            wide = jnp.dot(share, expand, precision=HIGHEST, preferred_element_type=F32)
            merged = merged + x[:, :half].astype(F32) * wide
        merged_ref[:, c * half : (c + 1) * half] = merged
    entropy_ref[...] = jnp.broadcast_to(
        jnp.sum(spread, axis=1, keepdims=True) * (1.0 / HEADS), entropy_ref.shape
    )
    base = jnp.concatenate([base_ref[...]] * items, 0)
    mid = base + matmul(merged_ref[...].astype(BF16), weight_ref[...])
    mid_ref[...] = mid
    ffn_ref[...] = layer_norm(mid, gain_ref[...], bias_ref[...]).astype(BF16)


def gelu_parts(x):
    share = 0.5 * (1.0 + lax.erf(x * (0.5**0.5)))
    slope = share + x * jnp.exp(-0.5 * x * x) * ((2.0 * jnp.pi) ** -0.5)
    return x * share, slope


def feed_kernel(flag_ref, *refs, devices, items):
    row_refs = refs[:devices]
    low_ref, up_ref, down_ref, result_ref = refs[devices : devices + 4]
    grad_refs, (plane_ref, plane_low_ref) = refs[devices + 4 : -2], refs[-2:]
    own, width = row_refs[0].shape
    shard = low_ref.shape[0] // devices
    unit, piece = pack_shape(own, shard, width)
    me = flag_ref[2 * items + 2]
    for d in range(devices):
        plane_ref[d * own : (d + 1) * own, :] = row_refs[d][...]
        source = jnp.bitwise_xor(me, d) * shard
        for a in range(own // unit):
            rows = slice(d * own + a * unit, d * own + (a + 1) * unit)
            for b in range(shard // unit):
                start = pl.multiple_of(source + b * unit, unit)
                plane_low_ref[rows, b * piece : (b + 1) * piece] = low_ref[
                    pl.ds(start, unit), a * piece : (a + 1) * piece
                ]
    upward = matmul(plane_ref[...], up_ref[...])
    hidden, slope = gelu_parts(upward)
    grad_up = (slope * transposed_right(plane_low_ref[...], down_ref[...])).astype(BF16)
    grad = transposed_right(grad_up, up_ref[...]).astype(BF16)
    result = matmul(hidden.astype(BF16), down_ref[...]).astype(BF16)
    for d in range(devices):
        grad_refs[d][...] = grad[d * own : (d + 1) * own, :]
        result_ref[jnp.bitwise_xor(me, d)] = result[d * own : (d + 1) * own, :]


def feed_back_kernel(row_ref, low_ref, up_ref, down_ref, hidden_ref, grad_ref):
    hidden, slope = gelu_parts(matmul(row_ref[...], up_ref[...]))
    hidden_ref[...] = hidden.astype(BF16)
    grad_ref[...] = (slope * transposed_right(low_ref[...], down_ref[...])).astype(BF16)


def outer_kernel(left_ref, right_ref, out_ref):
    out_ref[...] = transposed_left(left_ref[...], right_ref[...]).astype(out_ref.dtype)


def norm_backward(rows, gain, gradient):
    center = rows - jnp.mean(rows, axis=1, keepdims=True)
    rate = lax.rsqrt(jnp.mean(center * center, axis=1, keepdims=True) + EPSILON)
    unit = center * rate
    scaled = gradient * gain
    inner = scaled - jnp.mean(scaled, axis=1, keepdims=True)
    back = rate * (inner - unit * jnp.mean(scaled * unit, axis=1, keepdims=True))
    return (
        back,
        jnp.sum(gradient * unit, axis=0, keepdims=True),
        jnp.sum(gradient, axis=0, keepdims=True),
    )


def turn_kernel(*refs, devices, items, chunks, head_size, heads):
    part_refs = refs[:devices]
    mid_ref, cotangent_ref, gain_ref, merged_ref, log_ref, weight_ref = refs[
        devices : devices + 6
    ]
    message_ref, branch_ref, base_ref, sums_ref = refs[devices + 6 :]
    own, width = mid_ref.shape
    half = width // chunks
    gradient = total_of([x[...] for x in part_refs])
    back, gain_sum, bias_sum = norm_backward(mid_ref[...], gain_ref[...], gradient)
    grad_mid = cotangent_ref[...] + back
    sums_ref[...] = jnp.zeros(sums_ref.shape, F32)
    sums_ref[0:1, :] = gain_sum
    sums_ref[1:2, :] = bias_sum
    row_total = own // items
    base_ref[...] = total_of(
        [grad_mid[i * row_total : (i + 1) * row_total] for i in range(items)]
    )
    branch = grad_mid.astype(BF16)
    branch_ref[:, :width] = branch
    branch_ref[:, width:] = merged_ref[...].astype(BF16)
    grad_att = transposed_right(branch, weight_ref[...]).astype(BF16)
    expand = head_expand(half, head_size)
    lane, column = iota((6 * LANES, LANES), 0), iota((6 * LANES, LANES), 1)
    place = jnp.logical_and(
        lane % LANES < heads, column == (lane // LANES) * heads + lane % LANES
    ).astype(BF16)
    message_ref[:, :width] = grad_att
    for c in range(chunks):
        columns = slice(c * half, (c + 1) * half)
        delta = lax.dot_general(
            merged_ref[:, columns] * grad_att[:, columns].astype(F32),
            expand,
            (((1,), (1,)), ((), ())),
            precision=HIGHEST,
            preferred_element_type=F32,
        )
        terms = jnp.concatenate([t for x in (log_ref[c], delta) for t in split_terms(x)], 1)
        message_ref[:, width + c * LANES : width + (c + 1) * LANES] = matmul(
            terms, place
        ).astype(BF16)


def backward_kernel(
    *refs, frames, items, patches, scale, head_size, heads,
):
    flag_ref, both_ref, query_ref, top_ref = refs[:4]
    grad_refs = refs[4 : 4 + frames]
    mark_refs = refs[4 + frames : 4 + 2 * frames]
    out_ref, sum_ref, held_ref, note_ref = refs[4 + 2 * frames :]
    lats, width = query_ref.shape
    own = grad_refs[0].shape[0]
    row_total = own // items
    base = items * patches
    for s in range(frames):
        source = lax.rem(flag_ref[items + 1] + (frames - s), frames)
        rows = pl.ds(pl.multiple_of(source * row_total, row_total), row_total)
        block = grad_refs[s][...].astype(F32)
        mark = mark_refs[s][...].astype(F32)
        for i in range(items):
            held_ref[i, rows, :] = block[i * row_total : (i + 1) * row_total]
            note_ref[i, rows, :] = mark[i * row_total : (i + 1) * row_total]
    masks = head_masks(lats, width, head_size)
    queries = spread_heads(query_ref[...].astype(F32), masks).astype(BF16)
    lat_both = both_ref[base : base + lats, :]
    row, lane = iota((GROUP * 8, LANES), 0), iota((GROUP * 8, LANES), 1)
    pick = jnp.logical_and(
        jnp.logical_and(
            lane // heads // 3 == row % 8,
            lane % heads == pl.program_id(0) * GROUP + row // 8,
        ),
        lane < 6 * heads,
    ).astype(BF16)
    grad_query = jnp.zeros((queries.shape[0], width), F32)
    lat_grad_key = jnp.zeros((lats, width), F32)
    lat_grad_value = jnp.zeros((lats, width), F32)
    for i in range(items):
        rows = slice(i * patches, (i + 1) * patches)
        stats = transposed_right(pick, note_ref[i].astype(BF16))
        stats = jnp.concatenate([stats[h * 8 : (h + 1) * 8] for h in range(GROUP)], 1)
        log_total = stats[0:1]
        delta = stats[1:2]
        top = top_ref[0, i, 0:1, :]
        rescale = jnp.exp(top - log_total)
        both = jnp.concatenate([both_ref[rows, :], lat_both], 0)
        keys, values = both[:, :width], both[:, width:]
        grads = spread_heads(held_ref[i], masks).astype(BF16)
        live = live_rows(flag_ref, i, items, patches, lats, queries.shape[0])
        masked = jnp.where(live, scale * transposed_right(keys, queries), MASKED)
        probs = jnp.where(live, jnp.exp(masked - log_total), 0.0)
        block_exp = jnp.where(live, jnp.exp(masked - top), 0.0)
        weights = (block_exp.astype(BF16).astype(F32) * rescale).astype(BF16)
        grad_scores = (probs * (transposed_right(values, grads) - delta)).astype(BF16)
        grad_key = scale * matmul(grad_scores, queries)
        grad_value = matmul(weights, grads)
        out_ref[rows, :width] = grad_key[:patches].astype(BF16)
        out_ref[rows, width:] = grad_value[:patches].astype(BF16)
        grad_query = grad_query + transposed_left(grad_scores, keys)
        lat_grad_key = lat_grad_key + grad_key[patches:]
        lat_grad_value = lat_grad_value + grad_value[patches:]
    out_ref[base : base + lats, :width] = lat_grad_key.astype(BF16)
    out_ref[base : base + lats, width:] = lat_grad_value.astype(BF16)
    sum_ref[...] = scale * collect_heads(grad_query, masks)


def media_kernel(flag_ref, *refs, chunks, items, frames):
    grad_refs, lat_refs, weight_refs = [
        refs[k * chunks : (k + 1) * chunks] for k in range(3)
    ]
    media_ref, time_ref, gain_ref, out_ref, sums_ref, product_ref = refs[3 * chunks :]
    item = pl.program_id(0)

    @pl.when(item == 0)
    def _():
        sums_ref[...] = jnp.zeros(sums_ref.shape, F32)
        product_ref[...] = functools.reduce(
            jnp.add, [transposed_right(g[...], w[...]) for g, w in zip(lat_refs, weight_refs)]
        )

    gradient = functools.reduce(
        jnp.add, [transposed_right(g[...], w[...]) for g, w in zip(grad_refs, weight_refs)]
    )
    inputs = media_ref[...].astype(F32) + time_ref[pl.ds(item, 1), :]
    back, gain_sum, bias_sum = norm_backward(inputs, gain_ref[...], gradient)
    out_ref[...] = back.astype(BF16)
    place = iota((frames, 1), 0) == flag_ref[items + 2 + item]
    sums_ref[0:frames, :] += jnp.where(place, jnp.sum(back, axis=0, keepdims=True), 0.0)
    sums_ref[8:9, :] += gain_sum
    sums_ref[9:10, :] += bias_sum


def latent_kernel(flag_ref, *refs, chunks, items):
    query_refs = refs[:chunks]
    (
        product_ref, query_weight_ref, latent_ref, gain_ref, base_ref, ffn_ref, media_ref, out_ref,
    ) = refs[chunks:]
    lats, width = latent_ref.shape
    half = width // chunks
    gradient = product_ref[...]
    for c in range(chunks):
        gradient = gradient + transposed_right(
            query_refs[c][...].astype(BF16), query_weight_ref[:, c * half : (c + 1) * half]
        )
        out_ref[lats : 2 * lats, c * half : (c + 1) * half] = query_refs[c][...]
    back, gain_sum, bias_sum = norm_backward(latent_ref[...], gain_ref[...], gradient)
    out_ref[:lats, :] = back
    row_total = base_ref.shape[0]
    start = pl.multiple_of(flag_ref[items + 1] * row_total, row_total)
    out_ref[pl.ds(start, row_total), :] += base_ref[...]
    at = 2 * lats
    out_ref[at : at + 8, :] = ffn_ref[...]
    out_ref[at + 2 : at + 3, :] = gain_sum
    out_ref[at + 3 : at + 4, :] = bias_sum
    out_ref[at + 8 : at + 24, :] = media_ref[...]
    out_ref[at + 24 :, :] = jnp.zeros((out_ref.shape[0] - at - 24, width), F32)


def rows_kernel(flag_ref, *refs, count, frames, items):
    part_refs, out_refs, held_ref = refs[:count], refs[count:-1], refs[-1]
    rows = held_ref.shape[1]
    column = 0
    for part_ref in part_refs:
        total = total_of([part_ref[k] for k in range(part_ref.shape[0])])
        for f in range(frames):
            held_ref[f, :, column : column + total.shape[1]] = total[f * rows : (f + 1) * rows]
        column += total.shape[1]
    for s, out_ref in enumerate(out_refs):
        block = held_ref[lax.rem(flag_ref[items + 1] + s, frames)]
        out_ref[...] = block.astype(out_ref.dtype)


def place_kernel(flag_ref, *refs, chunks, frames, items, groups):
    chunk_refs = refs[: chunks * frames]
    key_ref, value_ref, out_ref = refs[chunks * frames :]
    width = key_ref.shape[2] // (chunks * groups)
    for s in range(frames):
        source = lax.rem(flag_ref[items + 1] + (frames - s), frames)
        out_ref[source] = chunk_refs[s][:, 2 * groups * width :].astype(F32)
        for c in range(chunks):
            for g in range(groups):
                at = (c * groups + g) * width
                block = chunk_refs[c * frames + s][:, 2 * g * width : 2 * (g + 1) * width]
                block = block.astype(F32)
                key_ref[source, :, at : at + width] = block[:, :width]
                value_ref[source, :, at : at + width] = block[:, width:]


def body(
    media,
    cotangent,
    frame_count,
    frame_start,
    latents,
    time_embed,
    media_gain,
    media_bias,
    latent_gain,
    latent_bias,
    ffn_gain,
    ffn_bias,
    query_weight,
    key_weight,
    value_weight,
    out_weight,
    up_weight,
    down_weight,
):
    items = media.shape[0]
    patches = media.shape[2]
    width = media.shape[3]
    lats = latents.shape[0]
    frame_total = time_embed.shape[0]
    row_total = cotangent.shape[1]
    own = items * row_total
    head_size = width // HEADS
    half = width // CHUNKS
    chunk_heads = HEADS // CHUNKS
    group_width = GROUP * head_size
    groups = chunk_heads // GROUP
    stack = GROUP * lats
    tokens = items * patches
    all_tokens = tokens + lats
    shard = query_weight.shape[0]
    hidden_shard = down_weight.shape[0]
    item_size = lax.axis_size("items")
    frame_size = lax.axis_size("frames")
    plane = item_size * own
    item_index = lax.axis_index("items")
    slot = lax.axis_index("frames")
    row_base = slot * row_total
    params = pltpu.CompilerParams(vmem_limit_bytes=56 * 2**20)
    smem = pl.BlockSpec(memory_space=pltpu.SMEM)
    whole = pl.BlockSpec(memory_space=pltpu.VMEM)
    sizes = dict(items=items, head_size=head_size, heads=chunk_heads)

    def struct(shape, kind):
        return jax.ShapeDtypeStruct(shape, kind)

    def cost(micros):
        return pl.CostEstimate(
            flops=int(micros * 1.15e9), bytes_accessed=int(micros * 3.6e6), transcendentals=0
        )

    def column_blocks(x):
        return jnp.transpose(x.reshape(-1, item_size, shard), (1, 0, 2))

    def scatter_exchange(x, axis):
        return jnp.sum(lax.all_to_all(x, axis, 0, 0).astype(F32), axis=0)

    grad_out = cotangent.reshape(own, width)
    low_columns = own * width // shard
    joined, grad_low = pl.pallas_call(
        functools.partial(join_kernel, width=group_width),
        out_shape=[struct((shard, 2 * width + low_columns), BF16), struct((own, width), BF16)],
        cost_estimate=cost(2.5),
        compiler_params=params,
    )(key_weight, value_weight, grad_out)
    kv_full = lax.all_gather(joined, "items", axis=0, tiled=True)
    low_frames = jnp.stack(spread_on(grad_low, "frames"))

    lat_norm = layer_norm(latents, latent_gain, latent_bias).astype(BF16)
    lat_cols = lax.dynamic_slice_in_dim(lat_norm, item_index * shard, shard, 1)
    query_blocks = column_blocks(matmul(lat_cols, query_weight))
    query_cols = scatter_exchange(query_blocks, "items").astype(BF16)
    query_spread = jnp.broadcast_to(query_cols[None], (item_size, lats, shard))
    queries = jnp.transpose(lax.all_to_all(query_spread, "items", 0, 0), (1, 0, 2)).reshape(
        lats, width
    )

    counts = lax.dynamic_slice_in_dim(frame_count, item_index * items, items)
    starts = lax.dynamic_slice_in_dim(frame_start, item_index * items, items)
    offset = (slot - starts) % frame_total
    flags = jnp.concatenate(
        [
            (offset < counts).astype(jnp.int32),
            (slot == 0).astype(jnp.int32)[None],
            slot.astype(jnp.int32)[None],
            offset.astype(jnp.int32),
            item_index.astype(jnp.int32)[None],
        ]
    )
    picker = (offset[:, None] == jnp.arange(frame_total, dtype=jnp.int32)[None, :]).astype(F32)
    time_rows = jnp.dot(picker, time_embed, precision=HIGHEST, preferred_element_type=F32)
    flat_media = media.reshape(tokens, width)
    steps = tokens // lats
    all_rows = pl.pallas_call(
        functools.partial(norm_kernel, steps=steps, per_item=patches // lats),
        grid=(steps + 1,),
        in_specs=[
            pl.BlockSpec((lats, width), lambda i: (jnp.minimum(i, steps - 1), 0)),
            whole,
            whole,
            whole,
            whole,
        ],
        out_specs=pl.BlockSpec((lats, width), lambda i: (i, 0)),
        out_shape=struct((all_tokens, width), BF16),
        cost_estimate=cost(12),
        compiler_params=params,
    )(
        after(flat_media, query_blocks),
        time_rows,
        media_gain[None],
        media_bias[None],
        lat_norm,
    )
    out_full = lax.all_gather(after(out_weight, all_rows), "items", axis=0, tiled=True)

    core = item_index % 2
    rows_across = after(all_rows, query_cols).T.reshape(item_size // 2, 2, shard, all_tokens)
    send_rows, keep_rows = [
        jnp.concatenate(
            [
                lax.dynamic_slice(
                    rows_across, (k, which, 0, 0), (1, 1, shard, all_tokens)
                ).reshape(shard, all_tokens)
                for k in range(item_size // 2)
            ],
            0,
        )
        for which in (1 - core, core)
    ]
    boths, tops, messages = [], [], []
    for c in range(CHUNKS):

        def block_of(g, c=c):
            return (0, c * groups + g)

        if c:
            rows = after(all_rows, tops[-1])
        else:
            rows = after(all_rows, queries, send_rows, keep_rows)
        both = matmul(rows, kv_full[:, 2 * c * half : 2 * (c + 1) * half]).astype(BF16)
        if c == 0:
            up_slice = lax.all_to_all(after(up_weight, both), "items", 1, 0, tiled=True)
        top, *parts = pl.pallas_call(
            functools.partial(
                forward_kernel, patches=patches, scale=head_size**-0.5, **sizes
            ),
            grid=(groups,),
            in_specs=[
                smem,
                pl.BlockSpec((all_tokens, 2 * group_width), lambda g: (0, g)),
                pl.BlockSpec((lats, group_width), block_of),
            ],
            out_specs=[pl.BlockSpec((1, items, 8, stack), lambda g: (g, 0, 0, 0))]
            + [pl.BlockSpec((own, half + LANES), lambda g: (0, 0))] * frame_size,
            out_shape=[struct((groups, items, 8, stack), F32)]
            + [struct((own, half + LANES), BF16)] * frame_size,
            scratch_shapes=[
                pltpu.VMEM((items, lats, group_width), F32),
                pltpu.VMEM((items, lats, LANES), F32),
            ],
            cost_estimate=cost(7.8),
            compiler_params=params,
        )(flags, after(both, up_slice, *messages) if c else both, queries)
        boths.append(both)
        tops.append(top)
        messages += [p if s == 0 else send_on(p, "frames", s) for s, p in enumerate(parts)]
    low_all = lax.all_gather(after(low_frames, tops[1]), "items", axis=0).reshape(-1, width)

    base_rows = lax.dynamic_slice_in_dim(latents, row_base, row_total, 0)
    merged, mid_rows, ffn_in, logs, entropy_wide = pl.pallas_call(
        functools.partial(merge_kernel, chunks=CHUNKS, frames=frame_size, **sizes),
        out_shape=[
            struct((own, width), F32),
            struct((own, width), F32),
            struct((own, width), BF16),
            struct((CHUNKS, own, LANES), F32),
            struct((own, LANES), F32),
        ],
        cost_estimate=cost(6.3),
        compiler_params=params,
    )(*messages, base_rows, out_full, ffn_gain[None], ffn_bias[None])
    entropy = entropy_wide[:, 0].reshape(items, row_total)

    ffn_blocks = spread_across(ffn_in, "items")
    ffn_frames = spread_on(after(ffn_in, *ffn_blocks), "frames")
    result_part, *parts = pl.pallas_call(
        functools.partial(feed_kernel, devices=item_size, items=items),
        grid=(1,),
        in_specs=[smem]
        + [whole] * item_size
        + [
            pl.BlockSpec((width, low_columns), lambda i: (0, 2 * width // low_columns)),
            whole,
            whole,
        ],
        out_specs=[whole] * (1 + item_size),
        out_shape=[struct((item_size, own, width), BF16)]
        + [struct((own, width), BF16)] * item_size,
        scratch_shapes=[pltpu.VMEM((plane, width), BF16)] * 2,
        cost_estimate=cost(10),
        compiler_params=params,
    )(flags, *ffn_blocks, kv_full, up_slice, down_weight)
    grad_blocks = collect_across(parts, "items")
    grad_blocks[0] = after(grad_blocks[0], *ffn_frames)
    query_full = lax.all_gather(after(query_weight, parts[0]), "items", axis=0, tiled=True)

    turn, grad_branch, grad_base, ffn_sums = pl.pallas_call(
        functools.partial(turn_kernel, devices=item_size, chunks=CHUNKS, **sizes),
        out_shape=[
            struct((own, width + CHUNKS * LANES), BF16),
            struct((own, 2 * width), BF16),
            struct((row_total, width), F32),
            struct((8, width), F32),
        ],
        cost_estimate=cost(7.6),
        compiler_params=params,
    )(*grad_blocks, mid_rows, grad_out, ffn_gain[None], merged, logs, out_full)
    turns = spread_on(turn, "frames")
    ffn_all = lax.all_gather(
        jnp.stack([after(f, grad_branch) for f in ffn_frames]), "items", axis=0
    ).reshape(-1, width)
    branch_plane = lax.all_gather(after(grad_branch, turns[1]), "items", axis=0, tiled=True)
    att_plane = lax.dynamic_slice_in_dim(
        branch_plane, width + item_index * shard, shard, 1
    )
    turns[0] = after(turns[0], low_all, query_full)

    chunk_grads, chunk_queries = [], []

    def weight_terms(c):
        send = matmul(send_rows, chunk_grads[c]).astype(BF16)
        received = send_across(send, "items", 1).reshape(-1, shard, 2 * half)
        keep = matmul(after(keep_rows, send), chunk_grads[c]).astype(BF16)
        return send, keep.reshape(-1, shard, 2 * half), received

    def chip_terms(keep, received):
        return (keep.astype(F32) + received.astype(F32)).astype(BF16)

    def exchange_chips(x):
        groups_of = [list(range(k, item_size, 2)) for k in range(2)]
        return lax.all_to_all(x, "items", 0, 0, axis_index_groups=groups_of)

    def frame_rows(ranges):
        rows = shard // frame_size
        columns = sum(x.shape[-1] for x in ranges)
        return pl.pallas_call(
            functools.partial(rows_kernel, count=len(ranges), frames=frame_size, items=items),
            in_specs=[smem] + [whole] * len(ranges),
            out_specs=[whole] * frame_size,
            out_shape=[struct((rows, columns), F32)]
            + [struct((rows, columns), BF16)] * (frame_size - 1),
            scratch_shapes=[pltpu.VMEM((frame_size, rows, columns), F32)],
            cost_estimate=cost(3.5),
            compiler_params=params,
        )(flags, *ranges)

    def send_rows_on(rows):
        return [rows[0]] + [send_on(p, "frames", s) for s, p in enumerate(rows) if s]

    for c in range(CHUNKS):

        def block_of(g, c=c):
            return (0, c * groups + g)

        chunk_grad, chunk_query = pl.pallas_call(
            functools.partial(
                backward_kernel, frames=frame_size, patches=patches, scale=head_size**-0.5, **sizes
            ),
            grid=(groups,),
            in_specs=[
                smem,
                pl.BlockSpec((all_tokens, 2 * group_width), lambda g: (0, g)),
                pl.BlockSpec((lats, group_width), block_of),
                pl.BlockSpec((1, items, 8, stack), lambda g: (g, 0, 0, 0)),
            ]
            + [pl.BlockSpec((own, group_width), block_of)] * frame_size
            + [pl.BlockSpec((own, LANES), lambda g, c=c: (0, width // LANES + c))] * frame_size,
            out_specs=[
                pl.BlockSpec((all_tokens, 2 * group_width), lambda g: (0, g)),
                pl.BlockSpec((lats, group_width), lambda g: (0, g)),
            ],
            out_shape=[
                struct((all_tokens, 2 * half), BF16),
                struct((lats, half), F32),
            ],
            scratch_shapes=[
                pltpu.VMEM((items, lats, group_width), F32),
                pltpu.VMEM((items, lats, LANES), F32),
            ],
            cost_estimate=cost(8),
            compiler_params=params,
        )(flags, after(boths[c], *held) if c else boths[c], queries, tops[c], *turns, *turns)
        chunk_grads.append(chunk_grad)
        chunk_queries.append(chunk_query)
        if c == 0:
            first_send, first_keep, first_received = weight_terms(0)
            held = (first_send,)
    first_terms = chip_terms(after(first_keep, chunk_grads[-1]), first_received)
    first_moved = exchange_chips(first_terms)

    last_block = pl.BlockSpec((lats, 2 * half), lambda i: (tokens // lats, 0))
    media_grad, media_sums, lat_product = pl.pallas_call(
        functools.partial(media_kernel, chunks=CHUNKS, items=items, frames=frame_total),
        grid=(items,),
        in_specs=[smem]
        + [pl.BlockSpec((patches, 2 * half), lambda i: (i, 0))] * CHUNKS
        + [last_block] * CHUNKS
        + [pl.BlockSpec((width, 2 * half), lambda i, c=c: (0, c)) for c in range(CHUNKS)]
        + [pl.BlockSpec((patches, width), lambda i: (i, 0)), whole, whole],
        out_specs=[
            pl.BlockSpec((patches, width), lambda i: (i, 0)),
            pl.BlockSpec((16, width), lambda i: (0, 0)),
            pl.BlockSpec((lats, width), lambda i: (0, 0)),
        ],
        out_shape=[
            struct((tokens, width), BF16),
            struct((16, width), F32),
            struct((lats, width), F32),
        ],
        cost_estimate=cost(21),
        compiler_params=params,
    )(
        flags,
        *chunk_grads[:-1],
        after(chunk_grads[-1], first_terms),
        *chunk_grads,
        *[kv_full] * CHUNKS,
        flat_media,
        time_rows,
        media_gain[None],
    )

    sum_rows = 2 * lats + 24
    sum_rows += -sum_rows % (8 * item_size)
    payload = pl.pallas_call(
        functools.partial(latent_kernel, chunks=CHUNKS, items=items),
        in_specs=[smem] + [whole] * (CHUNKS + 7),
        out_specs=whole,
        out_shape=struct((sum_rows, width), F32),
        cost_estimate=cost(3),
        compiler_params=params,
    )(
        flags,
        *chunk_queries,
        after(lat_product, first_moved),
        query_full,
        latents,
        latent_gain[None],
        grad_base,
        ffn_sums,
        media_sums,
    )
    payload_part = lax.psum_scatter(payload, "items", scatter_dimension=0, tiled=True)

    chunk_grads[-1] = after(chunk_grads[-1], payload)
    last_send, last_keep, last_received = weight_terms(CHUNKS - 1)
    last_terms = chip_terms(after(last_keep, first_moved), last_received)
    last_moved = exchange_chips(last_terms)
    out_part = transposed_left(att_plane, after(branch_plane, last_send)[:, :width])
    first_rows = frame_rows([after(first_moved, last_terms), out_part[None]])
    first_frames = send_rows_on(first_rows)
    all_plane = plane * frame_size
    block_rows = min(512, all_plane)
    row_block = pl.BlockSpec((block_rows, width), lambda i: (i, 0))
    hidden_block = pl.BlockSpec((block_rows, hidden_shard), lambda i: (i, 0))
    hidden, grad_up = pl.pallas_call(
        feed_back_kernel,
        grid=(all_plane // block_rows,),
        in_specs=[row_block, row_block, whole, whole],
        out_specs=[hidden_block, hidden_block],
        out_shape=[struct((all_plane, hidden_shard), BF16)] * 2,
        cost_estimate=cost(15),
        compiler_params=params,
    )(after(ffn_all, *first_rows), low_all, up_slice, down_weight)

    def outer(left, right, tile, kind):
        rows, columns = left.shape
        shape = (columns, right.shape[1])
        return pl.pallas_call(
            outer_kernel,
            grid=(columns // tile,),
            in_specs=[pl.BlockSpec((rows, tile), lambda i: (0, i)), whole],
            out_specs=pl.BlockSpec((tile, shape[1]), lambda i: (i, 0)),
            out_shape=struct(shape, kind),
            cost_estimate=cost(9.5),
            compiler_params=params,
        )(left, right)

    first_total = total_of(first_frames).astype(BF16)
    first_placed = spread_on(first_total, "frames")
    last_rows = frame_rows([after(last_moved, hidden)])
    last_frames = send_rows_on(last_rows)
    up_part = outer(ffn_all, after(grad_up, first_total, *last_rows), width // 4, BF16)
    result_pieces = lax.all_to_all(after(result_part, last_moved), "items", 0, 0)
    up_grad = lax.all_to_all(
        after(up_part, result_pieces), "items", 0, 1, tiled=True
    ).astype(F32)
    last_total = total_of(last_frames).astype(BF16)
    last_placed = spread_on(last_total, "frames")
    down_grad = outer(
        after(hidden, up_part, last_total, *first_placed),
        low_all,
        256 if hidden_shard % 256 == 0 else hidden_shard,
        F32,
    )
    placed = first_placed + last_placed
    payload_part = after(payload_part, up_part)
    payload_others = spread_on(payload_part.astype(BF16), "frames")[1:]
    sums = lax.all_gather(
        total_of([payload_part] + payload_others), "items", axis=0, tiled=True
    )
    latents_grad = sums[:lats]
    query_grad = transposed_left(lat_cols, sums[lats : 2 * lats].astype(BF16))
    at = 2 * lats
    column_sums = lax.dynamic_slice_in_dim(
        sums[at + 8 : at + 24], item_index * shard, shard, 1
    )

    key_grad, value_grad, out_grad = pl.pallas_call(
        functools.partial(
            place_kernel, chunks=CHUNKS, frames=frame_size, items=items, groups=groups
        ),
        in_specs=[smem] + [whole] * len(placed),
        out_specs=[whole] * 3,
        out_shape=[struct((frame_size, shard // frame_size, width), F32)] * 3,
        cost_estimate=cost(3.4),
        compiler_params=params,
    )(flags, *placed)

    result = mid_rows + total_of([result_pieces[d] for d in range(item_size)])
    return (
        result.reshape(items, row_total, width),
        entropy,
        media_grad.reshape(media.shape),
        latents_grad,
        column_sums[:frame_total],
        column_sums[8],
        column_sums[9],
        sums[at + 2],
        sums[at + 3],
        sums[at],
        sums[at + 1],
        query_grad,
        key_grad.reshape(shard, width),
        value_grad.reshape(shard, width),
        out_grad.reshape(shard, width),
        up_grad,
        down_grad,
    )


def solution(mesh):
    return jax.shard_map(
        body,
        mesh=mesh,
        in_specs=(
            P("items", "frames", None, None),
            P("items", "frames", None),
            P(),
            P(),
            P(),
            P(),
            P(),
            P(),
            P(),
            P(),
            P(),
            P(),
            P("items", None),
            P("items", None),
            P("items", None),
            P("items", None),
            P("items", None),
            P("items", None),
        ),
        out_specs=(
            P("items", "frames", None),
            P("items", "frames"),
            P("items", "frames", None, None),
            P(),
            P(None, "items"),
            P("items"),
            P("items"),
            P(),
            P(),
            P(),
            P(),
            P("items", None),
            P("items", None),
            P("items", None),
            P("items", None),
            P("items", None),
            P("items", None),
        ),
        check_vma=False,
    )
```

```python
import functools
import math

import jax
import jax.numpy as jnp
from jax import lax
from jax.experimental import pallas as pl
from jax.experimental.pallas import tpu as pltpu
from jax.sharding import PartitionSpec as P

HEADS = 16
GROUP = 4
CHUNKS = 2
LANES = 128
EPSILON = 1e-05
MASKED = -1e30
F32 = jnp.float32
BF16 = jnp.bfloat16
HIGHEST = lax.Precision.HIGHEST


def layer_norm(inputs, norm_gain, norm_bias):
    center = inputs - jnp.mean(inputs, axis=-1, keepdims=True)
    spread = jnp.mean(center * center, axis=-1, keepdims=True)
    return center * lax.rsqrt(spread + EPSILON) * norm_gain + norm_bias


def matmul(left_side, right_side):
    return jnp.dot(left_side, right_side, preferred_element_type=F32)


def transposed_left(left_side, right_side):
    return lax.dot_general(
        left_side, right_side, (((0,), (0,)), ((), ())), preferred_element_type=F32
    )


def transposed_right(left_side, right_side):
    return lax.dot_general(
        left_side, right_side, (((1,), (1,)), ((), ())), preferred_element_type=F32
    )


def send_on(x, axis, step):
    size = lax.axis_size(axis)
    return lax.ppermute(x, axis, [(i, (i + step) % size) for i in range(size)])


def send_across(x, axis, distance):
    return lax.ppermute(x, axis, [(i, i ^ distance) for i in range(lax.axis_size(axis))])


def spread_on(x, axis):
    return [x] + [send_on(x, axis, s) for s in range(1, lax.axis_size(axis))]


def spread_across(x, axis):
    chips = [x] + [send_across(x, axis, d) for d in range(2, lax.axis_size(axis), 2)]
    return [b for block in chips for b in (block, send_across(block, axis, 1))]


def collect_across(pieces, axis):
    return [pieces[0]] + [send_across(p, axis, d) for d, p in enumerate(pieces) if d]


def total_of(pieces):
    return functools.reduce(jnp.add, [p.astype(F32) for p in pieces])


def after(x, *earlier):
    return lax.optimization_barrier((x,) + earlier)[0]


def split_terms(x):
    high = x.astype(BF16)
    rest = x - high.astype(F32)
    middle = rest.astype(BF16)
    return high, middle, (rest - middle.astype(F32)).astype(BF16)


def iota(shape, dim):
    return lax.broadcasted_iota(jnp.int32, shape, dim)


def head_masks(rows, width, head_size):
    lane = iota((rows, width), 1)
    return [
        jnp.logical_and(lane >= h * head_size, lane < (h + 1) * head_size)
        for h in range(width // head_size)
    ]


def spread_heads(block, masks):
    return jnp.concatenate([jnp.where(m, block, jnp.zeros_like(block)) for m in masks], 0)


def collect_heads(block, masks):
    rows = block.shape[0] // len(masks)
    total = jnp.where(masks[0], block[:rows], 0.0)
    for h in range(1, len(masks)):
        total = total + jnp.where(masks[h], block[h * rows : (h + 1) * rows], 0.0)
    return total


def head_expand(width, head_size):
    row, column = iota((LANES, width), 0), iota((LANES, width), 1)
    return jnp.logical_and(column >= row * head_size, column < (row + 1) * head_size).astype(F32)


def live_rows(flag_ref, item, items, patches, lats, columns):
    row = iota((patches + lats, columns), 0)
    media = jnp.logical_and(row < patches, flag_ref[item] > 0)
    return jnp.logical_or(media, jnp.logical_and(row >= patches, flag_ref[items] > 0))


def pack_shape(own, shard, width):
    unit = math.gcd(own, shard)
    return unit, width * unit // shard


def join_kernel(key_ref, value_ref, cotangent_ref, out_ref, low_ref, *, width):
    for g in range(key_ref.shape[1] // width):
        columns = slice(g * width, (g + 1) * width)
        out_ref[:, 2 * g * width : (2 * g + 1) * width] = key_ref[:, columns]
        out_ref[:, (2 * g + 1) * width : (2 * g + 2) * width] = value_ref[:, columns]
    low = cotangent_ref[...].astype(BF16)
    low_ref[...] = low
    own, span = low.shape
    unit, piece = pack_shape(own, out_ref.shape[0], span)
    for a in range(own // unit):
        for b in range(span // piece):
            at = 2 * span + a * piece
            out_ref[b * unit : (b + 1) * unit, at : at + piece] = low[
                a * unit : (a + 1) * unit, b * piece : (b + 1) * piece
            ]


def norm_kernel(media_ref, time_ref, gain_ref, bias_ref, lat_ref, out_ref, *, steps, per_item):
    step = pl.program_id(0)

    @pl.when(step < steps)
    def _():
        rows = media_ref[...].astype(F32) + time_ref[pl.ds(step // per_item, 1), :]
        out_ref[...] = layer_norm(rows, gain_ref[...], bias_ref[...]).astype(BF16)

    @pl.when(step == steps)
    def _():
        out_ref[...] = lat_ref[...]


def forward_kernel(
    flag_ref, both_ref, query_ref, top_ref, *refs, items, patches, scale, head_size, heads,
):
    message_refs, (part_ref, mark_ref) = refs[:-2], refs[-2:]
    lats, width = query_ref.shape
    frames = len(message_refs)
    own = message_refs[0].shape[0]
    row_total = own // items
    masks = head_masks(lats, width, head_size)
    queries = spread_heads(query_ref[...].astype(F32), masks).astype(BF16)
    base = items * patches
    lat_both = both_ref[base : base + lats, :]
    group = pl.program_id(0)
    term, lane = iota((16, GROUP * LANES), 0), iota((16, GROUP * LANES), 1)
    place = jnp.logical_and(
        lane % LANES == term * heads + group * GROUP + lane // LANES, term < 9
    ).astype(BF16)
    for i in range(items):
        both = jnp.concatenate([both_ref[i * patches : (i + 1) * patches, :], lat_both], 0)
        live = live_rows(flag_ref, i, items, patches, lats, queries.shape[0])
        scores = scale * transposed_right(both[:, :width], queries)
        masked = jnp.where(live, scores, MASKED)
        top = jnp.max(masked, axis=0, keepdims=True)
        block_exp = jnp.where(live, jnp.exp(masked - top), 0.0)
        total = jnp.sum(block_exp, axis=0, keepdims=True)
        moment = jnp.sum(block_exp * scores, axis=0, keepdims=True)
        part = transposed_left(block_exp.astype(BF16), both[:, width:])
        part_ref[i] = collect_heads(part, masks)
        top_ref[0, i] = jnp.broadcast_to(top, top_ref.shape[2:])
        terms = jnp.concatenate(
            [t.astype(F32) for x in (top, total, moment) for t in split_terms(x)]
            + [jnp.zeros((7, top.shape[1]), F32)],
            0,
        ).astype(BF16)
        wide = transposed_left(terms, place)
        mark = wide[:lats, :LANES]
        for h in range(1, GROUP):
            mark = mark + wide[h * lats : (h + 1) * lats, h * LANES : (h + 1) * LANES]
        mark_ref[i] = mark

    end = message_refs[0].shape[1] - LANES
    for s, message_ref in enumerate(message_refs):
        start = pl.multiple_of(lax.rem(flag_ref[items + 1] + s, frames) * row_total, row_total)
        rows = pl.ds(start, row_total)
        block = jnp.concatenate([part_ref[i, rows, :] for i in range(items)], 0).astype(BF16)
        mark = jnp.concatenate([mark_ref[i, rows, :] for i in range(items)], 0).astype(BF16)
        for g in range(end // width):

            @pl.when(group == g)
            def _():
                message_ref[:, g * width : (g + 1) * width] = block
                if g == 0:
                    message_ref[:, end:] = mark
                else:
                    message_ref[:, end:] = message_ref[:, end:] + mark


def merge_kernel(*refs, chunks, frames, items, head_size, heads):
    message_refs = refs[: chunks * frames]
    base_ref, weight_ref, gain_ref, bias_ref = refs[chunks * frames : chunks * frames + 4]
    merged_ref, mid_ref, ffn_ref, log_ref, entropy_ref = refs[chunks * frames + 4 :]
    own, columns = message_refs[0].shape
    half = columns - LANES
    lane, column = iota((LANES, 3 * LANES), 0), iota((LANES, 3 * LANES), 1)
    gather = jnp.logical_and(
        jnp.logical_and(lane // heads // 3 == column // LANES, lane % heads == column % LANES),
        lane < 9 * heads,
    ).astype(BF16)
    expand = head_expand(half, head_size)
    live = iota((own, LANES), 1) < heads
    spread = jnp.zeros((own, LANES), F32)
    for c in range(chunks):
        sources = message_refs[c * frames : (c + 1) * frames]
        stats = [matmul(x[:, half:], gather) for x in sources]
        tops = [x[:, :LANES] for x in stats]
        peak = functools.reduce(jnp.maximum, tops)
        factors = [jnp.exp(t - peak) for t in tops]
        whole = sum(f * x[:, LANES : 2 * LANES] for f, x in zip(factors, stats))
        moment = sum(f * x[:, 2 * LANES :] for f, x in zip(factors, stats))
        whole = jnp.where(live, whole, 1.0)
        log_total = jnp.where(live, peak + jnp.log(whole), 0.0)
        log_ref[c] = log_total
        spread = spread + jnp.where(live, log_total - moment / whole, 0.0)
        merged = jnp.zeros((own, half), F32)
        for x, factor in zip(sources, factors):
            share = jnp.where(live, factor / whole, 0.0)
            wide = jnp.dot(share, expand, precision=HIGHEST, preferred_element_type=F32)
            merged = merged + x[:, :half].astype(F32) * wide
        merged_ref[:, c * half : (c + 1) * half] = merged
    entropy_ref[...] = jnp.broadcast_to(
        jnp.sum(spread, axis=1, keepdims=True) * (1.0 / HEADS), entropy_ref.shape
    )
    base = jnp.concatenate([base_ref[...]] * items, 0)
    mid = base + matmul(merged_ref[...].astype(BF16), weight_ref[...])
    mid_ref[...] = mid
    ffn_ref[...] = layer_norm(mid, gain_ref[...], bias_ref[...]).astype(BF16)


def gelu_parts(x):
    share = 0.5 * (1.0 + lax.erf(x * (0.5**0.5)))
    slope = share + x * jnp.exp(-0.5 * x * x) * ((2.0 * jnp.pi) ** -0.5)
    return x * share, slope


def feed_kernel(flag_ref, *refs, devices, items):
    row_refs = refs[:devices]
    low_ref, up_ref, down_ref, result_ref = refs[devices : devices + 4]
    grad_refs, (plane_ref, plane_low_ref) = refs[devices + 4 : -2], refs[-2:]
    own, width = row_refs[0].shape
    shard = low_ref.shape[0] // devices
    unit, piece = pack_shape(own, shard, width)
    me = flag_ref[2 * items + 2]
    for d in range(devices):
        plane_ref[d * own : (d + 1) * own, :] = row_refs[d][...]
        source = jnp.bitwise_xor(me, d) * shard
        for a in range(own // unit):
            rows = slice(d * own + a * unit, d * own + (a + 1) * unit)
            for b in range(shard // unit):
                start = pl.multiple_of(source + b * unit, unit)
                plane_low_ref[rows, b * piece : (b + 1) * piece] = low_ref[
                    pl.ds(start, unit), a * piece : (a + 1) * piece
                ]
    upward = matmul(plane_ref[...], up_ref[...])
    hidden, slope = gelu_parts(upward)
    grad_up = (slope * transposed_right(plane_low_ref[...], down_ref[...])).astype(BF16)
    grad = transposed_right(grad_up, up_ref[...]).astype(BF16)
    result = matmul(hidden.astype(BF16), down_ref[...]).astype(BF16)
    for d in range(devices):
        grad_refs[d][...] = grad[d * own : (d + 1) * own, :]
        result_ref[jnp.bitwise_xor(me, d)] = result[d * own : (d + 1) * own, :]


def feed_back_kernel(row_ref, low_ref, up_ref, down_ref, hidden_ref, grad_ref):
    hidden, slope = gelu_parts(matmul(row_ref[...], up_ref[...]))
    hidden_ref[...] = hidden.astype(BF16)
    grad_ref[...] = (slope * transposed_right(low_ref[...], down_ref[...])).astype(BF16)


def outer_kernel(left_ref, right_ref, out_ref):
    out_ref[...] = transposed_left(left_ref[...], right_ref[...]).astype(out_ref.dtype)


def norm_backward(rows, gain, gradient):
    center = rows - jnp.mean(rows, axis=1, keepdims=True)
    rate = lax.rsqrt(jnp.mean(center * center, axis=1, keepdims=True) + EPSILON)
    unit = center * rate
    scaled = gradient * gain
    inner = scaled - jnp.mean(scaled, axis=1, keepdims=True)
    back = rate * (inner - unit * jnp.mean(scaled * unit, axis=1, keepdims=True))
    return (
        back,
        jnp.sum(gradient * unit, axis=0, keepdims=True),
        jnp.sum(gradient, axis=0, keepdims=True),
    )


def turn_kernel(*refs, devices, items, chunks, head_size, heads):
    part_refs = refs[:devices]
    mid_ref, cotangent_ref, gain_ref, merged_ref, log_ref, weight_ref = refs[
        devices : devices + 6
    ]
    message_ref, branch_ref, base_ref, sums_ref = refs[devices + 6 :]
    own, width = mid_ref.shape
    half = width // chunks
    gradient = total_of([x[...] for x in part_refs])
    back, gain_sum, bias_sum = norm_backward(mid_ref[...], gain_ref[...], gradient)
    grad_mid = cotangent_ref[...] + back
    sums_ref[...] = jnp.zeros(sums_ref.shape, F32)
    sums_ref[0:1, :] = gain_sum
    sums_ref[1:2, :] = bias_sum
    row_total = own // items
    base_ref[...] = total_of(
        [grad_mid[i * row_total : (i + 1) * row_total] for i in range(items)]
    )
    branch = grad_mid.astype(BF16)
    branch_ref[:, :width] = branch
    branch_ref[:, width:] = merged_ref[...].astype(BF16)
    grad_att = transposed_right(branch, weight_ref[...]).astype(BF16)
    expand = head_expand(half, head_size)
    lane, column = iota((6 * LANES, LANES), 0), iota((6 * LANES, LANES), 1)
    place = jnp.logical_and(
        lane % LANES < heads, column == (lane // LANES) * heads + lane % LANES
    ).astype(BF16)
    message_ref[:, :width] = grad_att
    for c in range(chunks):
        columns = slice(c * half, (c + 1) * half)
        delta = lax.dot_general(
            merged_ref[:, columns] * grad_att[:, columns].astype(F32),
            expand,
            (((1,), (1,)), ((), ())),
            precision=HIGHEST,
            preferred_element_type=F32,
        )
        terms = jnp.concatenate([t for x in (log_ref[c], delta) for t in split_terms(x)], 1)
        message_ref[:, width + c * LANES : width + (c + 1) * LANES] = matmul(
            terms, place
        ).astype(BF16)


def backward_kernel(
    *refs, frames, items, patches, scale, head_size, heads,
):
    flag_ref, both_ref, query_ref, top_ref = refs[:4]
    grad_refs = refs[4 : 4 + frames]
    mark_refs = refs[4 + frames : 4 + 2 * frames]
    out_ref, sum_ref, held_ref, note_ref = refs[4 + 2 * frames :]
    lats, width = query_ref.shape
    own = grad_refs[0].shape[0]
    row_total = own // items
    base = items * patches
    for s in range(frames):
        source = lax.rem(flag_ref[items + 1] + (frames - s), frames)
        rows = pl.ds(pl.multiple_of(source * row_total, row_total), row_total)
        block = grad_refs[s][...].astype(F32)
        mark = mark_refs[s][...].astype(F32)
        for i in range(items):
            held_ref[i, rows, :] = block[i * row_total : (i + 1) * row_total]
            note_ref[i, rows, :] = mark[i * row_total : (i + 1) * row_total]
    masks = head_masks(lats, width, head_size)
    queries = spread_heads(query_ref[...].astype(F32), masks).astype(BF16)
    lat_both = both_ref[base : base + lats, :]
    row, lane = iota((GROUP * 8, LANES), 0), iota((GROUP * 8, LANES), 1)
    pick = jnp.logical_and(
        jnp.logical_and(
            lane // heads // 3 == row % 8,
            lane % heads == pl.program_id(0) * GROUP + row // 8,
        ),
        lane < 6 * heads,
    ).astype(BF16)
    grad_query = jnp.zeros((queries.shape[0], width), F32)
    lat_grad_key = jnp.zeros((lats, width), F32)
    lat_grad_value = jnp.zeros((lats, width), F32)
    for i in range(items):
        rows = slice(i * patches, (i + 1) * patches)
        stats = transposed_right(pick, note_ref[i].astype(BF16))
        stats = jnp.concatenate([stats[h * 8 : (h + 1) * 8] for h in range(GROUP)], 1)
        log_total = stats[0:1]
        delta = stats[1:2]
        top = top_ref[0, i, 0:1, :]
        rescale = jnp.exp(top - log_total)
        both = jnp.concatenate([both_ref[rows, :], lat_both], 0)
        keys, values = both[:, :width], both[:, width:]
        grads = spread_heads(held_ref[i], masks).astype(BF16)
        live = live_rows(flag_ref, i, items, patches, lats, queries.shape[0])
        masked = jnp.where(live, scale * transposed_right(keys, queries), MASKED)
        probs = jnp.where(live, jnp.exp(masked - log_total), 0.0)
        block_exp = jnp.where(live, jnp.exp(masked - top), 0.0)
        weights = (block_exp.astype(BF16).astype(F32) * rescale).astype(BF16)
        grad_scores = (probs * (transposed_right(values, grads) - delta)).astype(BF16)
        grad_key = scale * matmul(grad_scores, queries)
        grad_value = matmul(weights, grads)
        out_ref[rows, :width] = grad_key[:patches].astype(BF16)
        out_ref[rows, width:] = grad_value[:patches].astype(BF16)
        grad_query = grad_query + transposed_left(grad_scores, keys)
        lat_grad_key = lat_grad_key + grad_key[patches:]
        lat_grad_value = lat_grad_value + grad_value[patches:]
    out_ref[base : base + lats, :width] = lat_grad_key.astype(BF16)
    out_ref[base : base + lats, width:] = lat_grad_value.astype(BF16)
    sum_ref[...] = scale * collect_heads(grad_query, masks)


def media_kernel(flag_ref, *refs, chunks, items, frames):
    grad_refs, lat_refs, weight_refs = [
        refs[k * chunks : (k + 1) * chunks] for k in range(3)
    ]
    media_ref, time_ref, gain_ref, out_ref, sums_ref, product_ref = refs[3 * chunks :]
    item = pl.program_id(0)

    @pl.when(item == 0)
    def _():
        sums_ref[...] = jnp.zeros(sums_ref.shape, F32)
        product_ref[...] = functools.reduce(
            jnp.add, [transposed_right(g[...], w[...]) for g, w in zip(lat_refs, weight_refs)]
        )

    gradient = functools.reduce(
        jnp.add, [transposed_right(g[...], w[...]) for g, w in zip(grad_refs, weight_refs)]
    )
    inputs = media_ref[...].astype(F32) + time_ref[pl.ds(item, 1), :]
    back, gain_sum, bias_sum = norm_backward(inputs, gain_ref[...], gradient)
    out_ref[...] = back.astype(BF16)
    place = iota((frames, 1), 0) == flag_ref[items + 2 + item]
    sums_ref[0:frames, :] += jnp.where(place, jnp.sum(back, axis=0, keepdims=True), 0.0)
    sums_ref[8:9, :] += gain_sum
    sums_ref[9:10, :] += bias_sum


def latent_kernel(flag_ref, *refs, chunks, items):
    query_refs = refs[:chunks]
    (
        product_ref, query_weight_ref, latent_ref, gain_ref, base_ref, ffn_ref, media_ref, out_ref,
    ) = refs[chunks:]
    lats, width = latent_ref.shape
    half = width // chunks
    gradient = product_ref[...]
    for c in range(chunks):
        gradient = gradient + transposed_right(
            query_refs[c][...].astype(BF16), query_weight_ref[:, c * half : (c + 1) * half]
        )
        out_ref[lats : 2 * lats, c * half : (c + 1) * half] = query_refs[c][...]
    back, gain_sum, bias_sum = norm_backward(latent_ref[...], gain_ref[...], gradient)
    out_ref[:lats, :] = back
    row_total = base_ref.shape[0]
    start = pl.multiple_of(flag_ref[items + 1] * row_total, row_total)
    out_ref[pl.ds(start, row_total), :] += base_ref[...]
    at = 2 * lats
    out_ref[at : at + 8, :] = ffn_ref[...]
    out_ref[at + 2 : at + 3, :] = gain_sum
    out_ref[at + 3 : at + 4, :] = bias_sum
    out_ref[at + 8 : at + 24, :] = media_ref[...]
    out_ref[at + 24 :, :] = jnp.zeros((out_ref.shape[0] - at - 24, width), F32)


def rows_kernel(flag_ref, *refs, counts, frames, items):
    part_refs, out_refs, held_ref = refs[: sum(counts)], refs[sum(counts) : -1], refs[-1]
    rows = held_ref.shape[1]
    first = column = 0
    for count in counts:
        parts = []
        for part_ref in part_refs[first : first + count]:
            if len(part_ref.shape) == 3:
                parts += [part_ref[k] for k in range(part_ref.shape[0])]
            else:
                parts.append(part_ref[...])
        total = total_of(parts)
        for f in range(frames):
            held_ref[f, :, column : column + total.shape[1]] = total[f * rows : (f + 1) * rows]
        first += count
        column += total.shape[1]
    for s, out_ref in enumerate(out_refs):
        block = held_ref[lax.rem(flag_ref[items + 1] + s, frames)]
        out_ref[...] = block.astype(out_ref.dtype)


def place_kernel(flag_ref, *refs, chunks, frames, items, groups):
    chunk_refs = refs[: chunks * frames]
    key_ref, value_ref, out_ref = refs[chunks * frames :]
    width = key_ref.shape[2] // (chunks * groups)
    for s in range(frames):
        source = lax.rem(flag_ref[items + 1] + (frames - s), frames)
        out_ref[source] = chunk_refs[s][:, 2 * groups * width :].astype(F32)
        for c in range(chunks):
            for g in range(groups):
                at = (c * groups + g) * width
                block = chunk_refs[c * frames + s][:, 2 * g * width : 2 * (g + 1) * width]
                block = block.astype(F32)
                key_ref[source, :, at : at + width] = block[:, :width]
                value_ref[source, :, at : at + width] = block[:, width:]


def body(
    media,
    cotangent,
    frame_count,
    frame_start,
    latents,
    time_embed,
    media_gain,
    media_bias,
    latent_gain,
    latent_bias,
    ffn_gain,
    ffn_bias,
    query_weight,
    key_weight,
    value_weight,
    out_weight,
    up_weight,
    down_weight,
):
    items = media.shape[0]
    patches = media.shape[2]
    width = media.shape[3]
    lats = latents.shape[0]
    frame_total = time_embed.shape[0]
    row_total = cotangent.shape[1]
    own = items * row_total
    head_size = width // HEADS
    half = width // CHUNKS
    chunk_heads = HEADS // CHUNKS
    group_width = GROUP * head_size
    groups = chunk_heads // GROUP
    stack = GROUP * lats
    tokens = items * patches
    all_tokens = tokens + lats
    shard = query_weight.shape[0]
    hidden_shard = down_weight.shape[0]
    item_size = lax.axis_size("items")
    frame_size = lax.axis_size("frames")
    plane = item_size * own
    item_index = lax.axis_index("items")
    slot = lax.axis_index("frames")
    row_base = slot * row_total
    params = pltpu.CompilerParams(vmem_limit_bytes=56 * 2**20)
    smem = pl.BlockSpec(memory_space=pltpu.SMEM)
    whole = pl.BlockSpec(memory_space=pltpu.VMEM)
    sizes = dict(items=items, head_size=head_size, heads=chunk_heads)

    def struct(shape, kind):
        return jax.ShapeDtypeStruct(shape, kind)

    def cost(micros):
        return pl.CostEstimate(
            flops=int(micros * 1.15e9), bytes_accessed=int(micros * 3.6e6), transcendentals=0
        )

    def column_blocks(x):
        return jnp.transpose(x.reshape(-1, item_size, shard), (1, 0, 2))

    def scatter_exchange(x, axis):
        return jnp.sum(lax.all_to_all(x, axis, 0, 0).astype(F32), axis=0)

    grad_out = cotangent.reshape(own, width)
    low_columns = own * width // shard
    joined, grad_low = pl.pallas_call(
        functools.partial(join_kernel, width=group_width),
        out_shape=[struct((shard, 2 * width + low_columns), BF16), struct((own, width), BF16)],
        cost_estimate=cost(2.5),
        compiler_params=params,
    )(key_weight, value_weight, grad_out)
    kv_full = lax.all_gather(joined, "items", axis=0, tiled=True)
    low_frames = jnp.stack(spread_on(grad_low, "frames"))

    lat_norm = layer_norm(latents, latent_gain, latent_bias).astype(BF16)
    lat_cols = lax.dynamic_slice_in_dim(lat_norm, item_index * shard, shard, 1)
    query_blocks = column_blocks(matmul(lat_cols, query_weight))
    query_cols = scatter_exchange(query_blocks, "items").astype(BF16)
    query_spread = jnp.broadcast_to(query_cols[None], (item_size, lats, shard))
    queries = jnp.transpose(lax.all_to_all(query_spread, "items", 0, 0), (1, 0, 2)).reshape(
        lats, width
    )

    counts = lax.dynamic_slice_in_dim(frame_count, item_index * items, items)
    starts = lax.dynamic_slice_in_dim(frame_start, item_index * items, items)
    offset = (slot - starts) % frame_total
    flags = jnp.concatenate(
        [
            (offset < counts).astype(jnp.int32),
            (slot == 0).astype(jnp.int32)[None],
            slot.astype(jnp.int32)[None],
            offset.astype(jnp.int32),
            item_index.astype(jnp.int32)[None],
        ]
    )
    picker = (offset[:, None] == jnp.arange(frame_total, dtype=jnp.int32)[None, :]).astype(F32)
    time_rows = jnp.dot(picker, time_embed, precision=HIGHEST, preferred_element_type=F32)
    flat_media = media.reshape(tokens, width)
    steps = tokens // lats
    all_rows = pl.pallas_call(
        functools.partial(norm_kernel, steps=steps, per_item=patches // lats),
        grid=(steps + 1,),
        in_specs=[
            pl.BlockSpec((lats, width), lambda i: (jnp.minimum(i, steps - 1), 0)),
            whole,
            whole,
            whole,
            whole,
        ],
        out_specs=pl.BlockSpec((lats, width), lambda i: (i, 0)),
        out_shape=struct((all_tokens, width), BF16),
        cost_estimate=cost(12),
        compiler_params=params,
    )(
        after(flat_media, query_blocks),
        time_rows,
        media_gain[None],
        media_bias[None],
        lat_norm,
    )
    out_full = lax.all_gather(after(out_weight, all_rows), "items", axis=0, tiled=True)

    core = item_index % 2
    rows_across = after(all_rows, query_cols).T.reshape(item_size // 2, 2, shard, all_tokens)
    send_rows, keep_rows = [
        jnp.concatenate(
            [
                lax.dynamic_slice(
                    rows_across, (k, which, 0, 0), (1, 1, shard, all_tokens)
                ).reshape(shard, all_tokens)
                for k in range(item_size // 2)
            ],
            0,
        )
        for which in (1 - core, core)
    ]
    boths, tops, messages = [], [], []
    for c in range(CHUNKS):

        def block_of(g, c=c):
            return (0, c * groups + g)

        if c:
            rows = after(all_rows, tops[-1])
        else:
            rows = after(all_rows, queries, send_rows, keep_rows, low_frames)
        both = matmul(rows, kv_full[:, 2 * c * half : 2 * (c + 1) * half]).astype(BF16)
        if c == 0:
            up_slice = lax.all_to_all(after(up_weight, both), "items", 1, 0, tiled=True)
        top, *parts = pl.pallas_call(
            functools.partial(
                forward_kernel, patches=patches, scale=head_size**-0.5, **sizes
            ),
            grid=(groups,),
            in_specs=[
                smem,
                pl.BlockSpec((all_tokens, 2 * group_width), lambda g: (0, g)),
                pl.BlockSpec((lats, group_width), block_of),
            ],
            out_specs=[pl.BlockSpec((1, items, 8, stack), lambda g: (g, 0, 0, 0))]
            + [pl.BlockSpec((own, half + LANES), lambda g: (0, 0))] * frame_size,
            out_shape=[struct((groups, items, 8, stack), F32)]
            + [struct((own, half + LANES), BF16)] * frame_size,
            scratch_shapes=[
                pltpu.VMEM((items, lats, group_width), F32),
                pltpu.VMEM((items, lats, LANES), F32),
            ],
            cost_estimate=cost(7.8),
            compiler_params=params,
        )(flags, after(both, *messages) if c else both, queries)
        boths.append(both)
        tops.append(top)
        messages += [p if s == 0 else send_on(p, "frames", s) for s, p in enumerate(parts)]
    low_all = lax.all_gather(after(low_frames, tops[1]), "items", axis=0).reshape(-1, width)

    base_rows = lax.dynamic_slice_in_dim(latents, row_base, row_total, 0)
    merged, mid_rows, ffn_in, logs, entropy_wide = pl.pallas_call(
        functools.partial(merge_kernel, chunks=CHUNKS, frames=frame_size, **sizes),
        out_shape=[
            struct((own, width), F32),
            struct((own, width), F32),
            struct((own, width), BF16),
            struct((CHUNKS, own, LANES), F32),
            struct((own, LANES), F32),
        ],
        cost_estimate=cost(6.3),
        compiler_params=params,
    )(after(messages[0], up_slice), *messages[1:], base_rows, out_full, ffn_gain[None], ffn_bias[None])
    entropy = entropy_wide[:, 0].reshape(items, row_total)

    ffn_blocks = spread_across(ffn_in, "items")
    ffn_frames = spread_on(after(ffn_in, *ffn_blocks), "frames")
    result_part, *parts = pl.pallas_call(
        functools.partial(feed_kernel, devices=item_size, items=items),
        grid=(1,),
        in_specs=[smem]
        + [whole] * item_size
        + [
            pl.BlockSpec((width, low_columns), lambda i: (0, 2 * width // low_columns)),
            whole,
            whole,
        ],
        out_specs=[whole] * (1 + item_size),
        out_shape=[struct((item_size, own, width), BF16)]
        + [struct((own, width), BF16)] * item_size,
        scratch_shapes=[pltpu.VMEM((plane, width), BF16)] * 2,
        cost_estimate=cost(10),
        compiler_params=params,
    )(flags, *ffn_blocks, kv_full, up_slice, down_weight)
    grad_blocks = collect_across(parts, "items")
    grad_blocks[0] = after(grad_blocks[0], *ffn_frames)
    query_full = lax.all_gather(after(query_weight, parts[0]), "items", axis=0, tiled=True)

    turn, grad_branch, grad_base, ffn_sums = pl.pallas_call(
        functools.partial(turn_kernel, devices=item_size, chunks=CHUNKS, **sizes),
        out_shape=[
            struct((own, width + CHUNKS * LANES), BF16),
            struct((own, 2 * width), BF16),
            struct((row_total, width), F32),
            struct((8, width), F32),
        ],
        cost_estimate=cost(7.6),
        compiler_params=params,
    )(*grad_blocks, mid_rows, grad_out, ffn_gain[None], merged, logs, out_full)
    turns = spread_on(turn, "frames")
    ffn_all = lax.all_gather(
        jnp.stack([after(f, turns[1]) for f in ffn_frames]), "items", axis=0
    ).reshape(-1, width)
    branch_plane = lax.all_gather(grad_branch, "items", axis=0, tiled=True)
    att_plane = lax.dynamic_slice_in_dim(
        branch_plane, width + item_index * shard, shard, 1
    )
    turns[0] = after(turns[0], low_all)

    chunk_grads, chunk_queries = [], []

    def weight_terms(c):
        send = matmul(send_rows, chunk_grads[c]).astype(BF16)
        received = send_across(send, "items", 1).reshape(-1, shard, 2 * half)
        keep = matmul(after(keep_rows, send), chunk_grads[c]).astype(BF16)
        return send, keep.reshape(-1, shard, 2 * half), received

    def chip_terms(keep, received):
        return (keep.astype(F32) + received.astype(F32)).astype(BF16)

    def exchange_chips(x):
        groups_of = [list(range(k, item_size, 2)) for k in range(2)]
        return lax.all_to_all(x, "items", 0, 0, axis_index_groups=groups_of)

    def permute_chips(x):
        chip = item_index // 2
        out = []
        for k in range(item_size // 2):
            piece = lax.dynamic_index_in_dim(x, chip ^ k, 0, False)
            out.append(send_across(piece, "items", 2 * k) if k else piece)
        return out

    def frame_rows(ranges):
        rows = shard // frame_size
        columns = sum(parts[0].shape[-1] for parts in ranges)
        return pl.pallas_call(
            functools.partial(
                rows_kernel,
                counts=tuple(len(parts) for parts in ranges),
                frames=frame_size,
                items=items,
            ),
            in_specs=[smem] + [whole] * sum(len(parts) for parts in ranges),
            out_specs=[whole] * frame_size,
            out_shape=[struct((rows, columns), F32)]
            + [struct((rows, columns), BF16)] * (frame_size - 1),
            scratch_shapes=[pltpu.VMEM((frame_size, rows, columns), F32)],
            cost_estimate=cost(3.5),
            compiler_params=params,
        )(flags, *[part for parts in ranges for part in parts])

    def send_rows_on(rows):
        return [rows[0]] + [send_on(p, "frames", s) for s, p in enumerate(rows) if s]

    for c in range(CHUNKS):

        def block_of(g, c=c):
            return (0, c * groups + g)

        chunk_grad, chunk_query = pl.pallas_call(
            functools.partial(
                backward_kernel, frames=frame_size, patches=patches, scale=head_size**-0.5, **sizes
            ),
            grid=(groups,),
            in_specs=[
                smem,
                pl.BlockSpec((all_tokens, 2 * group_width), lambda g: (0, g)),
                pl.BlockSpec((lats, group_width), block_of),
                pl.BlockSpec((1, items, 8, stack), lambda g: (g, 0, 0, 0)),
            ]
            + [pl.BlockSpec((own, group_width), block_of)] * frame_size
            + [pl.BlockSpec((own, LANES), lambda g, c=c: (0, width // LANES + c))] * frame_size,
            out_specs=[
                pl.BlockSpec((all_tokens, 2 * group_width), lambda g: (0, g)),
                pl.BlockSpec((lats, group_width), lambda g: (0, g)),
            ],
            out_shape=[
                struct((all_tokens, 2 * half), BF16),
                struct((lats, half), F32),
            ],
            scratch_shapes=[
                pltpu.VMEM((items, lats, group_width), F32),
                pltpu.VMEM((items, lats, LANES), F32),
            ],
            cost_estimate=cost(8),
            compiler_params=params,
        )(flags, after(boths[c], *held) if c else boths[c], queries, tops[c], *turns, *turns)
        chunk_grads.append(chunk_grad)
        chunk_queries.append(chunk_query)
        if c == 0:
            first_send, first_keep, first_received = weight_terms(0)
            result_pieces = lax.all_to_all(after(result_part, first_send), "items", 0, 0)
            held = (first_send,)
    first_terms = chip_terms(after(first_keep, chunk_grads[-1]), first_received)
    first_moved = permute_chips(first_terms)
    last_grad = chunk_grads[-1]
    chunk_grads[-1] = after(last_grad, first_terms)
    last_send, last_keep, last_received = weight_terms(CHUNKS - 1)
    last_terms = chip_terms(after(last_keep, result_pieces), last_received)
    last_moved = exchange_chips(last_terms)
    chunk_grads[-1] = last_grad
    out_part = transposed_left(att_plane, after(branch_plane, last_send)[:, :width])

    last_block = pl.BlockSpec((lats, 2 * half), lambda i: (tokens // lats, 0))
    media_grad, media_sums, lat_product = pl.pallas_call(
        functools.partial(media_kernel, chunks=CHUNKS, items=items, frames=frame_total),
        grid=(items,),
        in_specs=[smem]
        + [pl.BlockSpec((patches, 2 * half), lambda i: (i, 0))] * CHUNKS
        + [last_block] * CHUNKS
        + [pl.BlockSpec((width, 2 * half), lambda i, c=c: (0, c)) for c in range(CHUNKS)]
        + [pl.BlockSpec((patches, width), lambda i: (i, 0)), whole, whole],
        out_specs=[
            pl.BlockSpec((patches, width), lambda i: (i, 0)),
            pl.BlockSpec((16, width), lambda i: (0, 0)),
            pl.BlockSpec((lats, width), lambda i: (0, 0)),
        ],
        out_shape=[
            struct((tokens, width), BF16),
            struct((16, width), F32),
            struct((lats, width), F32),
        ],
        cost_estimate=cost(21),
        compiler_params=params,
    )(
        flags,
        *chunk_grads[:-1],
        after(chunk_grads[-1], last_terms),
        *chunk_grads,
        *[kv_full] * CHUNKS,
        flat_media,
        time_rows,
        media_gain[None],
    )

    sum_rows = 2 * lats + 24
    sum_rows += -sum_rows % (8 * item_size)
    payload = pl.pallas_call(
        functools.partial(latent_kernel, chunks=CHUNKS, items=items),
        in_specs=[smem] + [whole] * (CHUNKS + 7),
        out_specs=whole,
        out_shape=struct((sum_rows, width), F32),
        cost_estimate=cost(3),
        compiler_params=params,
    )(
        flags,
        *chunk_queries,
        after(lat_product, *first_moved),
        query_full,
        latents,
        latent_gain[None],
        grad_base,
        ffn_sums,
        media_sums,
    )
    payload_part = lax.psum_scatter(payload, "items", scatter_dimension=0, tiled=True)

    first_rows = frame_rows([[after(first_moved[0], payload), *first_moved[1:]], [out_part]])
    first_frames = send_rows_on(first_rows)
    all_plane = plane * frame_size
    block_rows = min(512, all_plane)
    row_block = pl.BlockSpec((block_rows, width), lambda i: (i, 0))
    hidden_block = pl.BlockSpec((block_rows, hidden_shard), lambda i: (i, 0))
    hidden, grad_up = pl.pallas_call(
        feed_back_kernel,
        grid=(all_plane // block_rows,),
        in_specs=[row_block, row_block, whole, whole],
        out_specs=[hidden_block, hidden_block],
        out_shape=[struct((all_plane, hidden_shard), BF16)] * 2,
        cost_estimate=cost(15),
        compiler_params=params,
    )(after(ffn_all, last_moved, *first_rows), low_all, up_slice, down_weight)

    def outer(left, right, tile, kind):
        rows, columns = left.shape
        shape = (columns, right.shape[1])
        return pl.pallas_call(
            outer_kernel,
            grid=(columns // tile,),
            in_specs=[pl.BlockSpec((rows, tile), lambda i: (0, i)), whole],
            out_specs=pl.BlockSpec((tile, shape[1]), lambda i: (i, 0)),
            out_shape=struct(shape, kind),
            cost_estimate=cost(9.5),
            compiler_params=params,
        )(left, right)

    first_total = total_of(first_frames).astype(BF16)
    first_placed = spread_on(first_total, "frames")
    last_rows = frame_rows([[after(last_moved, hidden)]])
    last_frames = send_rows_on(last_rows)
    up_part = outer(ffn_all, after(grad_up, first_total, *last_rows), width // 4, BF16)
    up_grad = lax.all_to_all(up_part, "items", 0, 1, tiled=True).astype(F32)
    last_total = total_of(last_frames).astype(BF16)
    last_placed = spread_on(last_total, "frames")
    down_grad = outer(
        after(hidden, up_part, last_total, *first_placed),
        low_all,
        256 if hidden_shard % 256 == 0 else hidden_shard,
        F32,
    )
    placed = first_placed + last_placed
    payload_part = after(payload_part, up_part)
    payload_others = spread_on(payload_part.astype(BF16), "frames")[1:]
    sums = lax.all_gather(
        total_of([payload_part] + payload_others), "items", axis=0, tiled=True
    )
    latents_grad = sums[:lats]
    query_grad = transposed_left(lat_cols, sums[lats : 2 * lats].astype(BF16))
    at = 2 * lats
    column_sums = lax.dynamic_slice_in_dim(
        sums[at + 8 : at + 24], item_index * shard, shard, 1
    )

    key_grad, value_grad, out_grad = pl.pallas_call(
        functools.partial(
            place_kernel, chunks=CHUNKS, frames=frame_size, items=items, groups=groups
        ),
        in_specs=[smem] + [whole] * len(placed),
        out_specs=[whole] * 3,
        out_shape=[struct((frame_size, shard // frame_size, width), F32)] * 3,
        cost_estimate=cost(3.4),
        compiler_params=params,
    )(flags, *placed)

    result = mid_rows + total_of([result_pieces[d] for d in range(item_size)])
    return (
        result.reshape(items, row_total, width),
        entropy,
        media_grad.reshape(media.shape),
        latents_grad,
        column_sums[:frame_total],
        column_sums[8],
        column_sums[9],
        sums[at + 2],
        sums[at + 3],
        sums[at],
        sums[at + 1],
        query_grad,
        key_grad.reshape(shard, width),
        value_grad.reshape(shard, width),
        out_grad.reshape(shard, width),
        up_grad,
        down_grad,
    )


def solution(mesh):
    return jax.shard_map(
        body,
        mesh=mesh,
        in_specs=(
            P("items", "frames", None, None),
            P("items", "frames", None),
            P(),
            P(),
            P(),
            P(),
            P(),
            P(),
            P(),
            P(),
            P(),
            P(),
            P("items", None),
            P("items", None),
            P("items", None),
            P("items", None),
            P("items", None),
            P("items", None),
        ),
        out_specs=(
            P("items", "frames", None),
            P("items", "frames"),
            P("items", "frames", None, None),
            P(),
            P(None, "items"),
            P("items"),
            P("items"),
            P(),
            P(),
            P(),
            P(),
            P("items", None),
            P("items", None),
            P("items", None),
            P("items", None),
            P("items", None),
            P("items", None),
        ),
        check_vma=False,
    )
```

```python
import functools
import math

import jax
import jax.numpy as jnp
from jax import lax
from jax.experimental import pallas as pl
from jax.experimental.pallas import tpu as pltpu
from jax.sharding import PartitionSpec as P

HEADS = 16
GROUP = 4
CHUNKS = 2
LANES = 128
EPSILON = 1e-05
MASKED = -1e30
F32 = jnp.float32
BF16 = jnp.bfloat16
HIGHEST = lax.Precision.HIGHEST


def layer_norm(inputs, norm_gain, norm_bias):
    center = inputs - jnp.mean(inputs, axis=-1, keepdims=True)
    spread = jnp.mean(center * center, axis=-1, keepdims=True)
    return center * lax.rsqrt(spread + EPSILON) * norm_gain + norm_bias


def matmul(left_side, right_side):
    return jnp.dot(left_side, right_side, preferred_element_type=F32)


def transposed_left(left_side, right_side):
    return lax.dot_general(
        left_side, right_side, (((0,), (0,)), ((), ())), preferred_element_type=F32
    )


def transposed_right(left_side, right_side):
    return lax.dot_general(
        left_side, right_side, (((1,), (1,)), ((), ())), preferred_element_type=F32
    )


def send_on(x, axis, step):
    size = lax.axis_size(axis)
    return lax.ppermute(x, axis, [(i, (i + step) % size) for i in range(size)])


def send_across(x, axis, distance):
    return lax.ppermute(x, axis, [(i, i ^ distance) for i in range(lax.axis_size(axis))])


def spread_on(x, axis):
    return [x] + [send_on(x, axis, s) for s in range(1, lax.axis_size(axis))]


def spread_across(x, axis):
    chips = [x] + [send_across(x, axis, d) for d in range(2, lax.axis_size(axis), 2)]
    return [b for block in chips for b in (block, send_across(block, axis, 1))]


def collect_across(pieces, axis):
    return [pieces[0]] + [send_across(p, axis, d) for d, p in enumerate(pieces) if d]


def total_of(pieces):
    return functools.reduce(jnp.add, [p.astype(F32) for p in pieces])


def after(x, *earlier):
    return lax.optimization_barrier((x,) + earlier)[0]


def split_terms(x):
    high = x.astype(BF16)
    rest = x - high.astype(F32)
    middle = rest.astype(BF16)
    return high, middle, (rest - middle.astype(F32)).astype(BF16)


def iota(shape, dim):
    return lax.broadcasted_iota(jnp.int32, shape, dim)


def head_masks(rows, width, head_size):
    lane = iota((rows, width), 1)
    return [
        jnp.logical_and(lane >= h * head_size, lane < (h + 1) * head_size)
        for h in range(width // head_size)
    ]


def spread_heads(block, masks):
    return jnp.concatenate([jnp.where(m, block, jnp.zeros_like(block)) for m in masks], 0)


def collect_heads(block, masks):
    rows = block.shape[0] // len(masks)
    total = jnp.where(masks[0], block[:rows], 0.0)
    for h in range(1, len(masks)):
        total = total + jnp.where(masks[h], block[h * rows : (h + 1) * rows], 0.0)
    return total


def head_expand(width, head_size):
    row, column = iota((LANES, width), 0), iota((LANES, width), 1)
    return jnp.logical_and(column >= row * head_size, column < (row + 1) * head_size).astype(F32)


def live_rows(flag_ref, item, items, patches, lats, columns):
    row = iota((patches + lats, columns), 0)
    media = jnp.logical_and(row < patches, flag_ref[item] > 0)
    return jnp.logical_or(media, jnp.logical_and(row >= patches, flag_ref[items] > 0))


def pack_shape(own, shard, width):
    unit = math.gcd(own, shard)
    return unit, width * unit // shard


def join_kernel(key_ref, value_ref, cotangent_ref, out_ref, low_ref, *, width):
    for g in range(key_ref.shape[1] // width):
        columns = slice(g * width, (g + 1) * width)
        out_ref[:, 2 * g * width : (2 * g + 1) * width] = key_ref[:, columns]
        out_ref[:, (2 * g + 1) * width : (2 * g + 2) * width] = value_ref[:, columns]
    low = cotangent_ref[...].astype(BF16)
    low_ref[...] = low
    own, span = low.shape
    unit, piece = pack_shape(own, out_ref.shape[0], span)
    for a in range(own // unit):
        for b in range(span // piece):
            at = 2 * span + a * piece
            out_ref[b * unit : (b + 1) * unit, at : at + piece] = low[
                a * unit : (a + 1) * unit, b * piece : (b + 1) * piece
            ]


def norm_kernel(media_ref, time_ref, gain_ref, bias_ref, lat_ref, out_ref, *, steps, per_item):
    step = pl.program_id(0)

    @pl.when(step < steps)
    def _():
        rows = media_ref[...].astype(F32) + time_ref[pl.ds(step // per_item, 1), :]
        out_ref[...] = layer_norm(rows, gain_ref[...], bias_ref[...]).astype(BF16)

    @pl.when(step == steps)
    def _():
        out_ref[...] = lat_ref[...]


def forward_kernel(
    flag_ref, both_ref, query_ref, top_ref, *refs, items, patches, scale, head_size, heads,
):
    message_refs, (part_ref, mark_ref) = refs[:-2], refs[-2:]
    lats, width = query_ref.shape
    frames = len(message_refs)
    own = message_refs[0].shape[0]
    row_total = own // items
    masks = head_masks(lats, width, head_size)
    queries = spread_heads(query_ref[...].astype(F32), masks).astype(BF16)
    base = items * patches
    lat_both = both_ref[base : base + lats, :]
    group = pl.program_id(0)
    term, lane = iota((16, GROUP * LANES), 0), iota((16, GROUP * LANES), 1)
    place = jnp.logical_and(
        lane % LANES == term * heads + group * GROUP + lane // LANES, term < 9
    ).astype(BF16)
    for i in range(items):
        both = jnp.concatenate([both_ref[i * patches : (i + 1) * patches, :], lat_both], 0)
        live = live_rows(flag_ref, i, items, patches, lats, queries.shape[0])
        scores = scale * transposed_right(both[:, :width], queries)
        masked = jnp.where(live, scores, MASKED)
        top = jnp.max(masked, axis=0, keepdims=True)
        block_exp = jnp.where(live, jnp.exp(masked - top), 0.0)
        total = jnp.sum(block_exp, axis=0, keepdims=True)
        moment = jnp.sum(block_exp * scores, axis=0, keepdims=True)
        part = transposed_left(block_exp.astype(BF16), both[:, width:])
        part_ref[i] = collect_heads(part, masks)
        top_ref[0, i] = jnp.broadcast_to(top, top_ref.shape[2:])
        terms = jnp.concatenate(
            [t.astype(F32) for x in (top, total, moment) for t in split_terms(x)]
            + [jnp.zeros((7, top.shape[1]), F32)],
            0,
        ).astype(BF16)
        wide = transposed_left(terms, place)
        mark = wide[:lats, :LANES]
        for h in range(1, GROUP):
            mark = mark + wide[h * lats : (h + 1) * lats, h * LANES : (h + 1) * LANES]
        mark_ref[i] = mark

    end = message_refs[0].shape[1] - LANES
    for s, message_ref in enumerate(message_refs):
        start = pl.multiple_of(lax.rem(flag_ref[items + 1] + s, frames) * row_total, row_total)
        rows = pl.ds(start, row_total)
        block = jnp.concatenate([part_ref[i, rows, :] for i in range(items)], 0).astype(BF16)
        mark = jnp.concatenate([mark_ref[i, rows, :] for i in range(items)], 0).astype(BF16)
        for g in range(end // width):

            @pl.when(group == g)
            def _():
                message_ref[:, g * width : (g + 1) * width] = block
                if g == 0:
                    message_ref[:, end:] = mark
                else:
                    message_ref[:, end:] = message_ref[:, end:] + mark


def merge_kernel(*refs, chunks, frames, items, head_size, heads):
    message_refs = refs[: chunks * frames]
    base_ref, weight_ref, gain_ref, bias_ref = refs[chunks * frames : chunks * frames + 4]
    merged_ref, mid_ref, ffn_ref, log_ref, entropy_ref = refs[chunks * frames + 4 :]
    own, columns = message_refs[0].shape
    half = columns - LANES
    lane, column = iota((LANES, 3 * LANES), 0), iota((LANES, 3 * LANES), 1)
    gather = jnp.logical_and(
        jnp.logical_and(lane // heads // 3 == column // LANES, lane % heads == column % LANES),
        lane < 9 * heads,
    ).astype(BF16)
    expand = head_expand(half, head_size)
    live = iota((own, LANES), 1) < heads
    spread = jnp.zeros((own, LANES), F32)
    for c in range(chunks):
        sources = message_refs[c * frames : (c + 1) * frames]
        stats = [matmul(x[:, half:], gather) for x in sources]
        tops = [x[:, :LANES] for x in stats]
        peak = functools.reduce(jnp.maximum, tops)
        factors = [jnp.exp(t - peak) for t in tops]
        whole = sum(f * x[:, LANES : 2 * LANES] for f, x in zip(factors, stats))
        moment = sum(f * x[:, 2 * LANES :] for f, x in zip(factors, stats))
        whole = jnp.where(live, whole, 1.0)
        log_total = jnp.where(live, peak + jnp.log(whole), 0.0)
        log_ref[c] = log_total
        spread = spread + jnp.where(live, log_total - moment / whole, 0.0)
        merged = jnp.zeros((own, half), F32)
        for x, factor in zip(sources, factors):
            share = jnp.where(live, factor / whole, 0.0)
            wide = jnp.dot(share, expand, precision=HIGHEST, preferred_element_type=F32)
            merged = merged + x[:, :half].astype(F32) * wide
        merged_ref[:, c * half : (c + 1) * half] = merged
    entropy_ref[...] = jnp.broadcast_to(
        jnp.sum(spread, axis=1, keepdims=True) * (1.0 / HEADS), entropy_ref.shape
    )
    base = jnp.concatenate([base_ref[...]] * items, 0)
    mid = base + matmul(merged_ref[...].astype(BF16), weight_ref[...])
    mid_ref[...] = mid
    ffn_ref[...] = layer_norm(mid, gain_ref[...], bias_ref[...]).astype(BF16)


def gelu_parts(x):
    share = 0.5 * (1.0 + lax.erf(x * (0.5**0.5)))
    slope = share + x * jnp.exp(-0.5 * x * x) * ((2.0 * jnp.pi) ** -0.5)
    return x * share, slope


def feed_kernel(flag_ref, *refs, devices, items):
    row_refs = refs[:devices]
    low_ref, up_ref, down_ref, result_ref = refs[devices : devices + 4]
    grad_refs, (plane_ref, plane_low_ref) = refs[devices + 4 : -2], refs[-2:]
    own, width = row_refs[0].shape
    shard = low_ref.shape[0] // devices
    unit, piece = pack_shape(own, shard, width)
    me = flag_ref[2 * items + 2]
    for d in range(devices):
        plane_ref[d * own : (d + 1) * own, :] = row_refs[d][...]
        source = jnp.bitwise_xor(me, d) * shard
        for a in range(own // unit):
            rows = slice(d * own + a * unit, d * own + (a + 1) * unit)
            for b in range(shard // unit):
                start = pl.multiple_of(source + b * unit, unit)
                plane_low_ref[rows, b * piece : (b + 1) * piece] = low_ref[
                    pl.ds(start, unit), a * piece : (a + 1) * piece
                ]
    upward = matmul(plane_ref[...], up_ref[...])
    hidden, slope = gelu_parts(upward)
    grad_up = (slope * transposed_right(plane_low_ref[...], down_ref[...])).astype(BF16)
    grad = transposed_right(grad_up, up_ref[...]).astype(BF16)
    result = matmul(hidden.astype(BF16), down_ref[...]).astype(BF16)
    for d in range(devices):
        grad_refs[d][...] = grad[d * own : (d + 1) * own, :]
        result_ref[jnp.bitwise_xor(me, d)] = result[d * own : (d + 1) * own, :]


def feed_back_kernel(row_ref, low_ref, up_ref, down_ref, hidden_ref, grad_ref):
    hidden, slope = gelu_parts(matmul(row_ref[...], up_ref[...]))
    hidden_ref[...] = hidden.astype(BF16)
    grad_ref[...] = (slope * transposed_right(low_ref[...], down_ref[...])).astype(BF16)


def outer_kernel(left_ref, right_ref, out_ref):
    out_ref[...] = transposed_left(left_ref[...], right_ref[...]).astype(out_ref.dtype)


def norm_backward(rows, gain, gradient):
    center = rows - jnp.mean(rows, axis=1, keepdims=True)
    rate = lax.rsqrt(jnp.mean(center * center, axis=1, keepdims=True) + EPSILON)
    unit = center * rate
    scaled = gradient * gain
    inner = scaled - jnp.mean(scaled, axis=1, keepdims=True)
    back = rate * (inner - unit * jnp.mean(scaled * unit, axis=1, keepdims=True))
    return (
        back,
        jnp.sum(gradient * unit, axis=0, keepdims=True),
        jnp.sum(gradient, axis=0, keepdims=True),
    )


def turn_kernel(*refs, devices, items, chunks, head_size, heads):
    part_refs = refs[:devices]
    mid_ref, cotangent_ref, gain_ref, merged_ref, log_ref, weight_ref = refs[
        devices : devices + 6
    ]
    message_ref, branch_ref, base_ref, sums_ref = refs[devices + 6 :]
    own, width = mid_ref.shape
    half = width // chunks
    gradient = total_of([x[...] for x in part_refs])
    back, gain_sum, bias_sum = norm_backward(mid_ref[...], gain_ref[...], gradient)
    grad_mid = cotangent_ref[...] + back
    sums_ref[...] = jnp.zeros(sums_ref.shape, F32)
    sums_ref[0:1, :] = gain_sum
    sums_ref[1:2, :] = bias_sum
    row_total = own // items
    base_ref[...] = total_of(
        [grad_mid[i * row_total : (i + 1) * row_total] for i in range(items)]
    )
    branch = grad_mid.astype(BF16)
    branch_ref[:, :width] = branch
    branch_ref[:, width:] = merged_ref[...].astype(BF16)
    grad_att = transposed_right(branch, weight_ref[...]).astype(BF16)
    expand = head_expand(half, head_size)
    lane, column = iota((6 * LANES, LANES), 0), iota((6 * LANES, LANES), 1)
    place = jnp.logical_and(
        lane % LANES < heads, column == (lane // LANES) * heads + lane % LANES
    ).astype(BF16)
    message_ref[:, :width] = grad_att
    for c in range(chunks):
        columns = slice(c * half, (c + 1) * half)
        delta = lax.dot_general(
            merged_ref[:, columns] * grad_att[:, columns].astype(F32),
            expand,
            (((1,), (1,)), ((), ())),
            precision=HIGHEST,
            preferred_element_type=F32,
        )
        terms = jnp.concatenate([t for x in (log_ref[c], delta) for t in split_terms(x)], 1)
        message_ref[:, width + c * LANES : width + (c + 1) * LANES] = matmul(
            terms, place
        ).astype(BF16)


def backward_kernel(
    *refs, frames, items, patches, scale, head_size, heads,
):
    flag_ref, both_ref, query_ref, top_ref = refs[:4]
    grad_refs = refs[4 : 4 + frames]
    mark_refs = refs[4 + frames : 4 + 2 * frames]
    out_ref, sum_ref, held_ref, note_ref = refs[4 + 2 * frames :]
    lats, width = query_ref.shape
    own = grad_refs[0].shape[0]
    row_total = own // items
    base = items * patches
    for s in range(frames):
        source = lax.rem(flag_ref[items + 1] + (frames - s), frames)
        rows = pl.ds(pl.multiple_of(source * row_total, row_total), row_total)
        block = grad_refs[s][...].astype(F32)
        mark = mark_refs[s][...].astype(F32)
        for i in range(items):
            held_ref[i, rows, :] = block[i * row_total : (i + 1) * row_total]
            note_ref[i, rows, :] = mark[i * row_total : (i + 1) * row_total]
    masks = head_masks(lats, width, head_size)
    queries = spread_heads(query_ref[...].astype(F32), masks).astype(BF16)
    lat_both = both_ref[base : base + lats, :]
    row, lane = iota((GROUP * 8, LANES), 0), iota((GROUP * 8, LANES), 1)
    pick = jnp.logical_and(
        jnp.logical_and(
            lane // heads // 3 == row % 8,
            lane % heads == pl.program_id(0) * GROUP + row // 8,
        ),
        lane < 6 * heads,
    ).astype(BF16)
    grad_query = jnp.zeros((queries.shape[0], width), F32)
    lat_grad_key = jnp.zeros((lats, width), F32)
    lat_grad_value = jnp.zeros((lats, width), F32)
    for i in range(items):
        rows = slice(i * patches, (i + 1) * patches)
        stats = transposed_right(pick, note_ref[i].astype(BF16))
        stats = jnp.concatenate([stats[h * 8 : (h + 1) * 8] for h in range(GROUP)], 1)
        log_total = stats[0:1]
        delta = stats[1:2]
        top = top_ref[0, i, 0:1, :]
        rescale = jnp.exp(top - log_total)
        both = jnp.concatenate([both_ref[rows, :], lat_both], 0)
        keys, values = both[:, :width], both[:, width:]
        grads = spread_heads(held_ref[i], masks).astype(BF16)
        live = live_rows(flag_ref, i, items, patches, lats, queries.shape[0])
        masked = jnp.where(live, scale * transposed_right(keys, queries), MASKED)
        probs = jnp.where(live, jnp.exp(masked - log_total), 0.0)
        block_exp = jnp.where(live, jnp.exp(masked - top), 0.0)
        weights = (block_exp.astype(BF16).astype(F32) * rescale).astype(BF16)
        grad_scores = (probs * (transposed_right(values, grads) - delta)).astype(BF16)
        grad_key = scale * matmul(grad_scores, queries)
        grad_value = matmul(weights, grads)
        out_ref[rows, :width] = grad_key[:patches].astype(BF16)
        out_ref[rows, width:] = grad_value[:patches].astype(BF16)
        grad_query = grad_query + transposed_left(grad_scores, keys)
        lat_grad_key = lat_grad_key + grad_key[patches:]
        lat_grad_value = lat_grad_value + grad_value[patches:]
    out_ref[base : base + lats, :width] = lat_grad_key.astype(BF16)
    out_ref[base : base + lats, width:] = lat_grad_value.astype(BF16)
    sum_ref[...] = scale * collect_heads(grad_query, masks)


def media_kernel(flag_ref, *refs, chunks, items, frames):
    grad_refs, lat_refs, weight_refs = [
        refs[k * chunks : (k + 1) * chunks] for k in range(3)
    ]
    media_ref, time_ref, gain_ref, out_ref, sums_ref, product_ref = refs[3 * chunks :]
    item = pl.program_id(0)

    @pl.when(item == 0)
    def _():
        sums_ref[...] = jnp.zeros(sums_ref.shape, F32)
        product_ref[...] = functools.reduce(
            jnp.add, [transposed_right(g[...], w[...]) for g, w in zip(lat_refs, weight_refs)]
        )

    gradient = functools.reduce(
        jnp.add, [transposed_right(g[...], w[...]) for g, w in zip(grad_refs, weight_refs)]
    )
    inputs = media_ref[...].astype(F32) + time_ref[pl.ds(item, 1), :]
    back, gain_sum, bias_sum = norm_backward(inputs, gain_ref[...], gradient)
    out_ref[...] = back.astype(BF16)
    place = iota((frames, 1), 0) == flag_ref[items + 2 + item]
    sums_ref[0:frames, :] += jnp.where(place, jnp.sum(back, axis=0, keepdims=True), 0.0)
    sums_ref[8:9, :] += gain_sum
    sums_ref[9:10, :] += bias_sum


def latent_kernel(flag_ref, *refs, chunks, items):
    query_refs = refs[:chunks]
    (
        product_ref, latent_ref, gain_ref, base_ref, ffn_ref, media_ref, out_ref,
    ) = refs[chunks:]
    lats, width = latent_ref.shape
    half = width // chunks
    gradient = product_ref[...]
    for c in range(chunks):
        out_ref[lats : 2 * lats, c * half : (c + 1) * half] = query_refs[c][...]
    back, gain_sum, bias_sum = norm_backward(latent_ref[...], gain_ref[...], gradient)
    out_ref[:lats, :] = back
    row_total = base_ref.shape[0]
    start = pl.multiple_of(flag_ref[items + 1] * row_total, row_total)
    out_ref[pl.ds(start, row_total), :] += base_ref[...]
    at = 2 * lats
    out_ref[at : at + 8, :] = ffn_ref[...]
    out_ref[at + 2 : at + 3, :] = gain_sum
    out_ref[at + 3 : at + 4, :] = bias_sum
    out_ref[at + 8 : at + 24, :] = media_ref[...]
    out_ref[at + 24 :, :] = jnp.zeros((out_ref.shape[0] - at - 24, width), F32)


def query_norm_kernel(flag_ref, *refs, devices, items):
    column_refs = refs[:devices]
    latent_ref, gain_ref, sum_ref, out_ref, out_gain_ref, out_bias_ref, held_ref = refs[devices:]
    for d in range(devices):
        held_ref[jnp.bitwise_xor(flag_ref[2 * items + 2], d)] = column_refs[d][...]
    gradient = jnp.concatenate([held_ref[k] for k in range(devices)], 1)
    back, gain_sum, bias_sum = norm_backward(latent_ref[...], gain_ref[...], gradient)
    lats = latent_ref.shape[0]
    out_ref[...] = sum_ref[:lats, :] + back
    out_gain_ref[...] = sum_ref[2 * lats + 2 : 2 * lats + 3, :] + gain_sum
    out_bias_ref[...] = sum_ref[2 * lats + 3 : 2 * lats + 4, :] + bias_sum


def rows_kernel(flag_ref, *refs, count, frames, items):
    part_refs, out_refs, held_ref = refs[:count], refs[count:-1], refs[-1]
    rows = held_ref.shape[1]
    column = 0
    for part_ref in part_refs:
        total = total_of([part_ref[k] for k in range(part_ref.shape[0])])
        for f in range(frames):
            held_ref[f, :, column : column + total.shape[1]] = total[f * rows : (f + 1) * rows]
        column += total.shape[1]
    for s, out_ref in enumerate(out_refs):
        block = held_ref[lax.rem(flag_ref[items + 1] + s, frames)]
        out_ref[...] = block.astype(out_ref.dtype)


def place_kernel(flag_ref, *refs, chunks, frames, items, groups):
    chunk_refs = refs[: chunks * frames]
    key_ref, value_ref, out_ref = refs[chunks * frames :]
    width = key_ref.shape[2] // (chunks * groups)
    for s in range(frames):
        source = lax.rem(flag_ref[items + 1] + (frames - s), frames)
        out_ref[source] = chunk_refs[s][:, 2 * groups * width :].astype(F32)
        for c in range(chunks):
            for g in range(groups):
                at = (c * groups + g) * width
                block = chunk_refs[c * frames + s][:, 2 * g * width : 2 * (g + 1) * width]
                block = block.astype(F32)
                key_ref[source, :, at : at + width] = block[:, :width]
                value_ref[source, :, at : at + width] = block[:, width:]


def body(
    media,
    cotangent,
    frame_count,
    frame_start,
    latents,
    time_embed,
    media_gain,
    media_bias,
    latent_gain,
    latent_bias,
    ffn_gain,
    ffn_bias,
    query_weight,
    key_weight,
    value_weight,
    out_weight,
    up_weight,
    down_weight,
):
    items = media.shape[0]
    patches = media.shape[2]
    width = media.shape[3]
    lats = latents.shape[0]
    frame_total = time_embed.shape[0]
    row_total = cotangent.shape[1]
    own = items * row_total
    head_size = width // HEADS
    half = width // CHUNKS
    chunk_heads = HEADS // CHUNKS
    group_width = GROUP * head_size
    groups = chunk_heads // GROUP
    stack = GROUP * lats
    tokens = items * patches
    all_tokens = tokens + lats
    shard = query_weight.shape[0]
    hidden_shard = down_weight.shape[0]
    item_size = lax.axis_size("items")
    frame_size = lax.axis_size("frames")
    plane = item_size * own
    item_index = lax.axis_index("items")
    slot = lax.axis_index("frames")
    row_base = slot * row_total
    params = pltpu.CompilerParams(vmem_limit_bytes=56 * 2**20)
    smem = pl.BlockSpec(memory_space=pltpu.SMEM)
    whole = pl.BlockSpec(memory_space=pltpu.VMEM)
    sizes = dict(items=items, head_size=head_size, heads=chunk_heads)

    def struct(shape, kind):
        return jax.ShapeDtypeStruct(shape, kind)

    def cost(micros):
        return pl.CostEstimate(
            flops=int(micros * 1.15e9), bytes_accessed=int(micros * 3.6e6), transcendentals=0
        )

    def column_blocks(x):
        return jnp.transpose(x.reshape(-1, item_size, shard), (1, 0, 2))

    def scatter_exchange(x, axis):
        return jnp.sum(lax.all_to_all(x, axis, 0, 0).astype(F32), axis=0)

    grad_out = cotangent.reshape(own, width)
    low_columns = own * width // shard
    joined, grad_low = pl.pallas_call(
        functools.partial(join_kernel, width=group_width),
        out_shape=[struct((shard, 2 * width + low_columns), BF16), struct((own, width), BF16)],
        cost_estimate=cost(2.5),
        compiler_params=params,
    )(key_weight, value_weight, grad_out)
    kv_full = lax.all_gather(joined, "items", axis=0, tiled=True)
    low_frames = jnp.stack(spread_on(grad_low, "frames"))

    lat_norm = layer_norm(latents, latent_gain, latent_bias).astype(BF16)
    lat_cols = lax.dynamic_slice_in_dim(lat_norm, item_index * shard, shard, 1)
    query_blocks = column_blocks(matmul(lat_cols, query_weight))
    query_cols = scatter_exchange(query_blocks, "items").astype(BF16)
    query_spread = jnp.broadcast_to(query_cols[None], (item_size, lats, shard))
    queries = jnp.transpose(lax.all_to_all(query_spread, "items", 0, 0), (1, 0, 2)).reshape(
        lats, width
    )

    counts = lax.dynamic_slice_in_dim(frame_count, item_index * items, items)
    starts = lax.dynamic_slice_in_dim(frame_start, item_index * items, items)
    offset = (slot - starts) % frame_total
    flags = jnp.concatenate(
        [
            (offset < counts).astype(jnp.int32),
            (slot == 0).astype(jnp.int32)[None],
            slot.astype(jnp.int32)[None],
            offset.astype(jnp.int32),
            item_index.astype(jnp.int32)[None],
        ]
    )
    picker = (offset[:, None] == jnp.arange(frame_total, dtype=jnp.int32)[None, :]).astype(F32)
    time_rows = jnp.dot(picker, time_embed, precision=HIGHEST, preferred_element_type=F32)
    flat_media = media.reshape(tokens, width)
    steps = tokens // lats
    all_rows = pl.pallas_call(
        functools.partial(norm_kernel, steps=steps, per_item=patches // lats),
        grid=(steps + 1,),
        in_specs=[
            pl.BlockSpec((lats, width), lambda i: (jnp.minimum(i, steps - 1), 0)),
            whole,
            whole,
            whole,
            whole,
        ],
        out_specs=pl.BlockSpec((lats, width), lambda i: (i, 0)),
        out_shape=struct((all_tokens, width), BF16),
        cost_estimate=cost(12),
        compiler_params=params,
    )(
        after(flat_media, query_blocks),
        time_rows,
        media_gain[None],
        media_bias[None],
        lat_norm,
    )
    out_full = lax.all_gather(after(out_weight, all_rows), "items", axis=0, tiled=True)

    core = item_index % 2
    rows_across = after(all_rows, query_cols).T.reshape(item_size // 2, 2, shard, all_tokens)
    send_rows, keep_rows = [
        jnp.concatenate(
            [
                lax.dynamic_slice(
                    rows_across, (k, which, 0, 0), (1, 1, shard, all_tokens)
                ).reshape(shard, all_tokens)
                for k in range(item_size // 2)
            ],
            0,
        )
        for which in (1 - core, core)
    ]
    boths, tops, messages = [], [], []
    for c in range(CHUNKS):

        def block_of(g, c=c):
            return (0, c * groups + g)

        if c:
            rows = after(all_rows, tops[-1])
        else:
            rows = after(all_rows, queries, send_rows, keep_rows)
        both = matmul(rows, kv_full[:, 2 * c * half : 2 * (c + 1) * half]).astype(BF16)
        top, *parts = pl.pallas_call(
            functools.partial(
                forward_kernel, patches=patches, scale=head_size**-0.5, **sizes
            ),
            grid=(groups,),
            in_specs=[
                smem,
                pl.BlockSpec((all_tokens, 2 * group_width), lambda g: (0, g)),
                pl.BlockSpec((lats, group_width), block_of),
            ],
            out_specs=[pl.BlockSpec((1, items, 8, stack), lambda g: (g, 0, 0, 0))]
            + [pl.BlockSpec((own, half + LANES), lambda g: (0, 0))] * frame_size,
            out_shape=[struct((groups, items, 8, stack), F32)]
            + [struct((own, half + LANES), BF16)] * frame_size,
            scratch_shapes=[
                pltpu.VMEM((items, lats, group_width), F32),
                pltpu.VMEM((items, lats, LANES), F32),
            ],
            cost_estimate=cost(7.8),
            compiler_params=params,
        )(flags, both, queries)
        boths.append(both)
        tops.append(top)
        messages += [p if s == 0 else send_on(p, "frames", s) for s, p in enumerate(parts)]
    up_slice = lax.all_to_all(after(up_weight, boths[0]), "items", 1, 0, tiled=True)
    low_all = lax.all_gather(after(low_frames, tops[1]), "items", axis=0).reshape(-1, width)

    base_rows = lax.dynamic_slice_in_dim(latents, row_base, row_total, 0)
    merged, mid_rows, ffn_in, logs, entropy_wide = pl.pallas_call(
        functools.partial(merge_kernel, chunks=CHUNKS, frames=frame_size, **sizes),
        out_shape=[
            struct((own, width), F32),
            struct((own, width), F32),
            struct((own, width), BF16),
            struct((CHUNKS, own, LANES), F32),
            struct((own, LANES), F32),
        ],
        cost_estimate=cost(6.3),
        compiler_params=params,
    )(*messages, base_rows, out_full, ffn_gain[None], ffn_bias[None])
    entropy = entropy_wide[:, 0].reshape(items, row_total)

    ffn_blocks = spread_across(ffn_in, "items")
    ffn_frames = spread_on(after(ffn_in, *ffn_blocks), "frames")
    result_part, *parts = pl.pallas_call(
        functools.partial(feed_kernel, devices=item_size, items=items),
        grid=(1,),
        in_specs=[smem]
        + [whole] * item_size
        + [
            pl.BlockSpec((width, low_columns), lambda i: (0, 2 * width // low_columns)),
            whole,
            whole,
        ],
        out_specs=[whole] * (1 + item_size),
        out_shape=[struct((item_size, own, width), BF16)]
        + [struct((own, width), BF16)] * item_size,
        scratch_shapes=[pltpu.VMEM((plane, width), BF16)] * 2,
        cost_estimate=cost(10),
        compiler_params=params,
    )(flags, *ffn_blocks, kv_full, up_slice, down_weight)
    grad_blocks = collect_across(parts, "items")
    grad_blocks[0] = after(grad_blocks[0], *ffn_frames)

    turn, grad_branch, grad_base, ffn_sums = pl.pallas_call(
        functools.partial(turn_kernel, devices=item_size, chunks=CHUNKS, **sizes),
        out_shape=[
            struct((own, width + CHUNKS * LANES), BF16),
            struct((own, 2 * width), BF16),
            struct((row_total, width), F32),
            struct((8, width), F32),
        ],
        cost_estimate=cost(7.6),
        compiler_params=params,
    )(*grad_blocks, mid_rows, grad_out, ffn_gain[None], merged, logs, out_full)
    turns = spread_on(turn, "frames")
    branch_plane = lax.all_gather(grad_branch, "items", axis=0, tiled=True)
    ffn_all = lax.all_gather(
        after(jnp.stack(ffn_frames), grad_branch), "items", axis=0
    ).reshape(-1, width)
    att_plane = lax.dynamic_slice_in_dim(
        branch_plane, width + item_index * shard, shard, 1
    )
    turns[0] = after(turns[0], low_all)

    chunk_grads, chunk_queries = [], []

    def weight_terms(c):
        send = matmul(send_rows, chunk_grads[c]).astype(BF16)
        received = send_across(send, "items", 1).reshape(-1, shard, 2 * half)
        keep = matmul(after(keep_rows, send), chunk_grads[c]).astype(BF16)
        return send, keep.reshape(-1, shard, 2 * half), received

    def chip_terms(keep, received):
        return (keep.astype(F32) + received.astype(F32)).astype(BF16)

    def exchange_chips(x):
        groups_of = [list(range(k, item_size, 2)) for k in range(2)]
        return lax.all_to_all(x, "items", 0, 0, axis_index_groups=groups_of)

    def frame_rows(ranges):
        rows = shard // frame_size
        columns = sum(x.shape[-1] for x in ranges)
        return pl.pallas_call(
            functools.partial(rows_kernel, count=len(ranges), frames=frame_size, items=items),
            in_specs=[smem] + [whole] * len(ranges),
            out_specs=[whole] * frame_size,
            out_shape=[struct((rows, columns), F32)]
            + [struct((rows, columns), BF16)] * (frame_size - 1),
            scratch_shapes=[pltpu.VMEM((frame_size, rows, columns), F32)],
            cost_estimate=cost(3.5),
            compiler_params=params,
        )(flags, *ranges)

    def send_rows_on(rows):
        return [rows[0]] + [send_on(p, "frames", s) for s, p in enumerate(rows) if s]

    for c in range(CHUNKS):

        def block_of(g, c=c):
            return (0, c * groups + g)

        chunk_grad, chunk_query = pl.pallas_call(
            functools.partial(
                backward_kernel, frames=frame_size, patches=patches, scale=head_size**-0.5, **sizes
            ),
            grid=(groups,),
            in_specs=[
                smem,
                pl.BlockSpec((all_tokens, 2 * group_width), lambda g: (0, g)),
                pl.BlockSpec((lats, group_width), block_of),
                pl.BlockSpec((1, items, 8, stack), lambda g: (g, 0, 0, 0)),
            ]
            + [pl.BlockSpec((own, group_width), block_of)] * frame_size
            + [pl.BlockSpec((own, LANES), lambda g, c=c: (0, width // LANES + c))] * frame_size,
            out_specs=[
                pl.BlockSpec((all_tokens, 2 * group_width), lambda g: (0, g)),
                pl.BlockSpec((lats, group_width), lambda g: (0, g)),
            ],
            out_shape=[
                struct((all_tokens, 2 * half), BF16),
                struct((lats, half), F32),
            ],
            scratch_shapes=[
                pltpu.VMEM((items, lats, group_width), F32),
                pltpu.VMEM((items, lats, LANES), F32),
            ],
            cost_estimate=cost(8),
            compiler_params=params,
        )(flags, after(boths[c], *held) if c else boths[c], queries, tops[c], *turns, *turns)
        chunk_grads.append(chunk_grad)
        chunk_queries.append(chunk_query)
        if c == 0:
            first_send, first_keep, first_received = weight_terms(0)
            held = (first_send,)
    first_terms = chip_terms(after(first_keep, chunk_grads[-1]), first_received)
    first_moved = exchange_chips(first_terms)

    last_block = pl.BlockSpec((lats, 2 * half), lambda i: (tokens // lats, 0))
    media_grad, media_sums, lat_product = pl.pallas_call(
        functools.partial(media_kernel, chunks=CHUNKS, items=items, frames=frame_total),
        grid=(items,),
        in_specs=[smem]
        + [pl.BlockSpec((patches, 2 * half), lambda i: (i, 0))] * CHUNKS
        + [last_block] * CHUNKS
        + [pl.BlockSpec((width, 2 * half), lambda i, c=c: (0, c)) for c in range(CHUNKS)]
        + [pl.BlockSpec((patches, width), lambda i: (i, 0)), whole, whole],
        out_specs=[
            pl.BlockSpec((patches, width), lambda i: (i, 0)),
            pl.BlockSpec((16, width), lambda i: (0, 0)),
            pl.BlockSpec((lats, width), lambda i: (0, 0)),
        ],
        out_shape=[
            struct((tokens, width), BF16),
            struct((16, width), F32),
            struct((lats, width), F32),
        ],
        cost_estimate=cost(21),
        compiler_params=params,
    )(
        flags,
        *chunk_grads[:-1],
        after(chunk_grads[-1], first_terms),
        *chunk_grads,
        *[kv_full] * CHUNKS,
        flat_media,
        time_rows,
        media_gain[None],
    )

    sum_rows = 2 * lats + 24
    sum_rows += -sum_rows % (8 * item_size)
    payload = pl.pallas_call(
        functools.partial(latent_kernel, chunks=CHUNKS, items=items),
        in_specs=[smem] + [whole] * (CHUNKS + 6),
        out_specs=whole,
        out_shape=struct((sum_rows, width), F32),
        cost_estimate=cost(3),
        compiler_params=params,
    )(
        flags,
        *chunk_queries,
        after(lat_product, first_moved),
        latents,
        latent_gain[None],
        grad_base,
        ffn_sums,
        media_sums,
    )
    payload_part = lax.psum_scatter(payload, "items", scatter_dimension=0, tiled=True)

    chunk_grads[-1] = after(chunk_grads[-1], payload)
    last_send, last_keep, last_received = weight_terms(CHUNKS - 1)
    last_terms = chip_terms(after(last_keep, first_moved), last_received)
    last_moved = exchange_chips(last_terms)
    out_part = transposed_left(att_plane, after(branch_plane, last_send)[:, :width])
    first_rows = frame_rows([after(first_moved, last_terms), out_part[None]])
    first_frames = send_rows_on(first_rows)
    all_plane = plane * frame_size
    block_rows = min(512, all_plane)
    row_block = pl.BlockSpec((block_rows, width), lambda i: (i, 0))
    hidden_block = pl.BlockSpec((block_rows, hidden_shard), lambda i: (i, 0))
    hidden, grad_up = pl.pallas_call(
        feed_back_kernel,
        grid=(all_plane // block_rows,),
        in_specs=[row_block, row_block, whole, whole],
        out_specs=[hidden_block, hidden_block],
        out_shape=[struct((all_plane, hidden_shard), BF16)] * 2,
        cost_estimate=cost(15),
        compiler_params=params,
    )(after(ffn_all, *first_rows), low_all, up_slice, down_weight)

    def outer(left, right, tile, kind):
        rows, columns = left.shape
        shape = (columns, right.shape[1])
        return pl.pallas_call(
            outer_kernel,
            grid=(columns // tile,),
            in_specs=[pl.BlockSpec((rows, tile), lambda i: (0, i)), whole],
            out_specs=pl.BlockSpec((tile, shape[1]), lambda i: (i, 0)),
            out_shape=struct(shape, kind),
            cost_estimate=cost(9.5),
            compiler_params=params,
        )(left, right)

    first_total = total_of(first_frames).astype(BF16)
    first_placed = spread_on(first_total, "frames")
    last_rows = frame_rows([after(last_moved, hidden)])
    last_frames = send_rows_on(last_rows)
    up_part = outer(ffn_all, after(grad_up, first_total, *last_rows), width // 4, BF16)
    up_moved = lax.all_to_all(up_part, "items", 0, 1, tiled=True)
    up_grad = up_moved.astype(F32)
    result_pieces = lax.all_to_all(after(result_part, up_moved), "items", 0, 0)
    last_total = total_of(last_frames).astype(BF16)
    last_placed = spread_on(last_total, "frames")
    down_grad = outer(
        after(hidden, up_part, last_total, *first_placed),
        low_all,
        256 if hidden_shard % 256 == 0 else hidden_shard,
        F32,
    )
    placed = first_placed + last_placed
    payload_part = after(payload_part, up_part)
    payload_others = spread_on(payload_part.astype(BF16), "frames")[1:]
    sums = lax.all_gather(
        total_of([payload_part] + payload_others), "items", axis=0, tiled=True
    )
    query_low = sums[lats : 2 * lats].astype(BF16)
    query_grad = transposed_left(lat_cols, query_low)
    norm_cols = transposed_right(query_low, query_weight)
    latents_grad, lat_gain, lat_bias = pl.pallas_call(
        functools.partial(query_norm_kernel, devices=item_size, items=items),
        in_specs=[smem] + [whole] * (item_size + 3),
        out_specs=[whole] * 3,
        out_shape=[struct((lats, width), F32), struct((1, width), F32), struct((1, width), F32)],
        scratch_shapes=[pltpu.VMEM((item_size, lats, shard), F32)],
        cost_estimate=cost(3),
        compiler_params=params,
    )(flags, *spread_across(norm_cols, "items"), latents, latent_gain[None], sums)
    at = 2 * lats
    column_sums = lax.dynamic_slice_in_dim(
        sums[at + 8 : at + 24], item_index * shard, shard, 1
    )

    key_grad, value_grad, out_grad = pl.pallas_call(
        functools.partial(
            place_kernel, chunks=CHUNKS, frames=frame_size, items=items, groups=groups
        ),
        in_specs=[smem] + [whole] * len(placed),
        out_specs=[whole] * 3,
        out_shape=[struct((frame_size, shard // frame_size, width), F32)] * 3,
        cost_estimate=cost(3.4),
        compiler_params=params,
    )(flags, after(placed[0], latents_grad), *placed[1:])

    result = mid_rows + total_of([result_pieces[d] for d in range(item_size)])
    return (
        result.reshape(items, row_total, width),
        entropy,
        media_grad.reshape(media.shape),
        latents_grad,
        column_sums[:frame_total],
        column_sums[8],
        column_sums[9],
        lat_gain[0],
        lat_bias[0],
        sums[at],
        sums[at + 1],
        query_grad,
        key_grad.reshape(shard, width),
        value_grad.reshape(shard, width),
        out_grad.reshape(shard, width),
        up_grad,
        down_grad,
    )


def solution(mesh):
    return jax.shard_map(
        body,
        mesh=mesh,
        in_specs=(
            P("items", "frames", None, None),
            P("items", "frames", None),
            P(),
            P(),
            P(),
            P(),
            P(),
            P(),
            P(),
            P(),
            P(),
            P(),
            P("items", None),
            P("items", None),
            P("items", None),
            P("items", None),
            P("items", None),
            P("items", None),
        ),
        out_specs=(
            P("items", "frames", None),
            P("items", "frames"),
            P("items", "frames", None, None),
            P(),
            P(None, "items"),
            P("items"),
            P("items"),
            P(),
            P(),
            P(),
            P(),
            P("items", None),
            P("items", None),
            P("items", None),
            P("items", None),
            P("items", None),
            P("items", None),
        ),
        check_vma=False,
    )
```

```python
import functools
import math

import jax
import jax.numpy as jnp
from jax import lax
from jax.experimental import pallas as pl
from jax.experimental.pallas import tpu as pltpu
from jax.sharding import PartitionSpec as P

HEADS = 16
GROUP = 4
CHUNKS = 2
LANES = 128
EPSILON = 1e-05
MASKED = -1e30
F32 = jnp.float32
BF16 = jnp.bfloat16
HIGHEST = lax.Precision.HIGHEST


def layer_norm(inputs, norm_gain, norm_bias):
    center = inputs - jnp.mean(inputs, axis=-1, keepdims=True)
    spread = jnp.mean(center * center, axis=-1, keepdims=True)
    return center * lax.rsqrt(spread + EPSILON) * norm_gain + norm_bias


def matmul(left_side, right_side):
    return jnp.dot(left_side, right_side, preferred_element_type=F32)


def transposed_left(left_side, right_side):
    return lax.dot_general(
        left_side, right_side, (((0,), (0,)), ((), ())), preferred_element_type=F32
    )


def transposed_right(left_side, right_side):
    return lax.dot_general(
        left_side, right_side, (((1,), (1,)), ((), ())), preferred_element_type=F32
    )


def send_on(x, axis, step):
    size = lax.axis_size(axis)
    return lax.ppermute(x, axis, [(i, (i + step) % size) for i in range(size)])


def send_across(x, axis, distance):
    return lax.ppermute(x, axis, [(i, i ^ distance) for i in range(lax.axis_size(axis))])


def spread_on(x, axis):
    return [x] + [send_on(x, axis, s) for s in range(1, lax.axis_size(axis))]


def spread_across(x, axis):
    chips = [x] + [send_across(x, axis, d) for d in range(2, lax.axis_size(axis), 2)]
    return [b for block in chips for b in (block, send_across(block, axis, 1))]


def collect_across(pieces, axis):
    return [pieces[0]] + [send_across(p, axis, d) for d, p in enumerate(pieces) if d]


def total_of(pieces):
    return functools.reduce(jnp.add, [p.astype(F32) for p in pieces])


def after(x, *earlier):
    return lax.optimization_barrier((x,) + earlier)[0]


def split_terms(x):
    high = x.astype(BF16)
    rest = x - high.astype(F32)
    middle = rest.astype(BF16)
    return high, middle, (rest - middle.astype(F32)).astype(BF16)


def iota(shape, dim):
    return lax.broadcasted_iota(jnp.int32, shape, dim)


def head_masks(rows, width, head_size):
    lane = iota((rows, width), 1)
    return [
        jnp.logical_and(lane >= h * head_size, lane < (h + 1) * head_size)
        for h in range(width // head_size)
    ]


def spread_heads(block, masks):
    return jnp.concatenate([jnp.where(m, block, jnp.zeros_like(block)) for m in masks], 0)


def collect_heads(block, masks):
    rows = block.shape[0] // len(masks)
    total = jnp.where(masks[0], block[:rows], 0.0)
    for h in range(1, len(masks)):
        total = total + jnp.where(masks[h], block[h * rows : (h + 1) * rows], 0.0)
    return total


def head_expand(width, head_size):
    row, column = iota((LANES, width), 0), iota((LANES, width), 1)
    return jnp.logical_and(column >= row * head_size, column < (row + 1) * head_size).astype(F32)


def live_rows(flag_ref, item, items, patches, lats, columns):
    row = iota((patches + lats, columns), 0)
    media = jnp.logical_and(row < patches, flag_ref[item] > 0)
    return jnp.logical_or(media, jnp.logical_and(row >= patches, flag_ref[items] > 0))


def pack_shape(own, shard, width):
    unit = math.gcd(own, shard)
    return unit, width * unit // shard


def join_kernel(key_ref, value_ref, cotangent_ref, out_ref, low_ref, *, width):
    for g in range(key_ref.shape[1] // width):
        columns = slice(g * width, (g + 1) * width)
        out_ref[:, 2 * g * width : (2 * g + 1) * width] = key_ref[:, columns]
        out_ref[:, (2 * g + 1) * width : (2 * g + 2) * width] = value_ref[:, columns]
    low = cotangent_ref[...].astype(BF16)
    low_ref[...] = low
    own, span = low.shape
    unit, piece = pack_shape(own, out_ref.shape[0], span)
    for a in range(own // unit):
        for b in range(span // piece):
            at = 2 * span + a * piece
            out_ref[b * unit : (b + 1) * unit, at : at + piece] = low[
                a * unit : (a + 1) * unit, b * piece : (b + 1) * piece
            ]


def norm_kernel(media_ref, time_ref, gain_ref, bias_ref, lat_ref, out_ref, *, steps, per_item):
    step = pl.program_id(0)

    @pl.when(step < steps)
    def _():
        rows = media_ref[...].astype(F32) + time_ref[pl.ds(step // per_item, 1), :]
        out_ref[...] = layer_norm(rows, gain_ref[...], bias_ref[...]).astype(BF16)

    @pl.when(step == steps)
    def _():
        out_ref[...] = lat_ref[...]


def forward_kernel(
    flag_ref, both_ref, query_ref, top_ref, *refs, items, patches, scale, head_size, heads,
):
    message_refs, (part_ref, mark_ref) = refs[:-2], refs[-2:]
    lats, width = query_ref.shape
    frames = len(message_refs)
    own = message_refs[0].shape[0]
    row_total = own // items
    masks = head_masks(lats, width, head_size)
    queries = spread_heads(query_ref[...].astype(F32), masks).astype(BF16)
    base = items * patches
    lat_both = both_ref[base : base + lats, :]
    group = pl.program_id(0)
    term, lane = iota((16, GROUP * LANES), 0), iota((16, GROUP * LANES), 1)
    place = jnp.logical_and(
        lane % LANES == term * heads + group * GROUP + lane // LANES, term < 9
    ).astype(BF16)
    for i in range(items):
        both = jnp.concatenate([both_ref[i * patches : (i + 1) * patches, :], lat_both], 0)
        live = live_rows(flag_ref, i, items, patches, lats, queries.shape[0])
        scores = scale * transposed_right(both[:, :width], queries)
        masked = jnp.where(live, scores, MASKED)
        top = jnp.max(masked, axis=0, keepdims=True)
        block_exp = jnp.where(live, jnp.exp(masked - top), 0.0)
        total = jnp.sum(block_exp, axis=0, keepdims=True)
        moment = jnp.sum(block_exp * scores, axis=0, keepdims=True)
        part = transposed_left(block_exp.astype(BF16), both[:, width:])
        part_ref[i] = collect_heads(part, masks)
        top_ref[0, i] = jnp.broadcast_to(top, top_ref.shape[2:])
        terms = jnp.concatenate(
            [t.astype(F32) for x in (top, total, moment) for t in split_terms(x)]
            + [jnp.zeros((7, top.shape[1]), F32)],
            0,
        ).astype(BF16)
        wide = transposed_left(terms, place)
        mark = wide[:lats, :LANES]
        for h in range(1, GROUP):
            mark = mark + wide[h * lats : (h + 1) * lats, h * LANES : (h + 1) * LANES]
        mark_ref[i] = mark

    end = message_refs[0].shape[1] - LANES
    for s, message_ref in enumerate(message_refs):
        start = pl.multiple_of(lax.rem(flag_ref[items + 1] + s, frames) * row_total, row_total)
        rows = pl.ds(start, row_total)
        block = jnp.concatenate([part_ref[i, rows, :] for i in range(items)], 0).astype(BF16)
        mark = jnp.concatenate([mark_ref[i, rows, :] for i in range(items)], 0).astype(BF16)
        for g in range(end // width):

            @pl.when(group == g)
            def _():
                message_ref[:, g * width : (g + 1) * width] = block
                if g == 0:
                    message_ref[:, end:] = mark
                else:
                    message_ref[:, end:] = message_ref[:, end:] + mark


def merge_kernel(*refs, chunks, frames, items, head_size, heads):
    message_refs = refs[: chunks * frames]
    base_ref, weight_ref, gain_ref, bias_ref = refs[chunks * frames : chunks * frames + 4]
    merged_ref, mid_ref, ffn_ref, log_ref, entropy_ref = refs[chunks * frames + 4 :]
    own, columns = message_refs[0].shape
    half = columns - LANES
    lane, column = iota((LANES, 3 * LANES), 0), iota((LANES, 3 * LANES), 1)
    gather = jnp.logical_and(
        jnp.logical_and(lane // heads // 3 == column // LANES, lane % heads == column % LANES),
        lane < 9 * heads,
    ).astype(BF16)
    expand = head_expand(half, head_size)
    live = iota((own, LANES), 1) < heads
    spread = jnp.zeros((own, LANES), F32)
    for c in range(chunks):
        sources = message_refs[c * frames : (c + 1) * frames]
        stats = [matmul(x[:, half:], gather) for x in sources]
        tops = [x[:, :LANES] for x in stats]
        peak = functools.reduce(jnp.maximum, tops)
        factors = [jnp.exp(t - peak) for t in tops]
        whole = sum(f * x[:, LANES : 2 * LANES] for f, x in zip(factors, stats))
        moment = sum(f * x[:, 2 * LANES :] for f, x in zip(factors, stats))
        whole = jnp.where(live, whole, 1.0)
        log_total = jnp.where(live, peak + jnp.log(whole), 0.0)
        log_ref[c] = log_total
        spread = spread + jnp.where(live, log_total - moment / whole, 0.0)
        merged = jnp.zeros((own, half), F32)
        for x, factor in zip(sources, factors):
            share = jnp.where(live, factor / whole, 0.0)
            wide = jnp.dot(share, expand, precision=HIGHEST, preferred_element_type=F32)
            merged = merged + x[:, :half].astype(F32) * wide
        merged_ref[:, c * half : (c + 1) * half] = merged
    entropy_ref[...] = jnp.broadcast_to(
        jnp.sum(spread, axis=1, keepdims=True) * (1.0 / HEADS), entropy_ref.shape
    )
    base = jnp.concatenate([base_ref[...]] * items, 0)
    mid = base + matmul(merged_ref[...].astype(BF16), weight_ref[...])
    mid_ref[...] = mid
    ffn_ref[...] = layer_norm(mid, gain_ref[...], bias_ref[...]).astype(BF16)


def gelu_parts(x):
    share = 0.5 * (1.0 + lax.erf(x * (0.5**0.5)))
    slope = share + x * jnp.exp(-0.5 * x * x) * ((2.0 * jnp.pi) ** -0.5)
    return x * share, slope


def feed_kernel(flag_ref, *refs, devices, items):
    row_refs = refs[:devices]
    low_ref, up_ref, down_ref, result_ref = refs[devices : devices + 4]
    grad_refs, (plane_ref, plane_low_ref) = refs[devices + 4 : -2], refs[-2:]
    own, width = row_refs[0].shape
    shard = low_ref.shape[0] // devices
    unit, piece = pack_shape(own, shard, width)
    me = flag_ref[2 * items + 2]
    for d in range(devices):
        plane_ref[d * own : (d + 1) * own, :] = row_refs[d][...]
        source = jnp.bitwise_xor(me, d) * shard
        for a in range(own // unit):
            rows = slice(d * own + a * unit, d * own + (a + 1) * unit)
            for b in range(shard // unit):
                start = pl.multiple_of(source + b * unit, unit)
                plane_low_ref[rows, b * piece : (b + 1) * piece] = low_ref[
                    pl.ds(start, unit), a * piece : (a + 1) * piece
                ]
    upward = matmul(plane_ref[...], up_ref[...])
    hidden, slope = gelu_parts(upward)
    grad_up = (slope * transposed_right(plane_low_ref[...], down_ref[...])).astype(BF16)
    grad = transposed_right(grad_up, up_ref[...]).astype(BF16)
    result = matmul(hidden.astype(BF16), down_ref[...]).astype(BF16)
    for d in range(devices):
        grad_refs[d][...] = grad[d * own : (d + 1) * own, :]
        result_ref[jnp.bitwise_xor(me, d)] = result[d * own : (d + 1) * own, :]


def feed_back_kernel(row_ref, low_ref, up_ref, down_ref, hidden_ref, grad_ref):
    hidden, slope = gelu_parts(matmul(row_ref[...], up_ref[...]))
    hidden_ref[...] = hidden.astype(BF16)
    grad_ref[...] = (slope * transposed_right(low_ref[...], down_ref[...])).astype(BF16)


def outer_kernel(left_ref, right_ref, out_ref):
    out_ref[...] = transposed_left(left_ref[...], right_ref[...]).astype(out_ref.dtype)


def norm_backward(rows, gain, gradient):
    center = rows - jnp.mean(rows, axis=1, keepdims=True)
    rate = lax.rsqrt(jnp.mean(center * center, axis=1, keepdims=True) + EPSILON)
    unit = center * rate
    scaled = gradient * gain
    inner = scaled - jnp.mean(scaled, axis=1, keepdims=True)
    back = rate * (inner - unit * jnp.mean(scaled * unit, axis=1, keepdims=True))
    return (
        back,
        jnp.sum(gradient * unit, axis=0, keepdims=True),
        jnp.sum(gradient, axis=0, keepdims=True),
    )


def turn_kernel(*refs, devices, items, chunks, head_size, heads):
    part_refs = refs[:devices]
    mid_ref, cotangent_ref, gain_ref, merged_ref, log_ref, weight_ref = refs[
        devices : devices + 6
    ]
    message_ref, branch_ref, base_ref, sums_ref = refs[devices + 6 :]
    own, width = mid_ref.shape
    half = width // chunks
    gradient = total_of([x[...] for x in part_refs])
    back, gain_sum, bias_sum = norm_backward(mid_ref[...], gain_ref[...], gradient)
    grad_mid = cotangent_ref[...] + back
    sums_ref[...] = jnp.zeros(sums_ref.shape, F32)
    sums_ref[0:1, :] = gain_sum
    sums_ref[1:2, :] = bias_sum
    row_total = own // items
    base_ref[...] = total_of(
        [grad_mid[i * row_total : (i + 1) * row_total] for i in range(items)]
    )
    branch = grad_mid.astype(BF16)
    branch_ref[:, :width] = branch
    branch_ref[:, width:] = merged_ref[...].astype(BF16)
    grad_att = transposed_right(branch, weight_ref[...]).astype(BF16)
    expand = head_expand(half, head_size)
    lane, column = iota((6 * LANES, LANES), 0), iota((6 * LANES, LANES), 1)
    place = jnp.logical_and(
        lane % LANES < heads, column == (lane // LANES) * heads + lane % LANES
    ).astype(BF16)
    message_ref[:, :width] = grad_att
    for c in range(chunks):
        columns = slice(c * half, (c + 1) * half)
        delta = lax.dot_general(
            merged_ref[:, columns] * grad_att[:, columns].astype(F32),
            expand,
            (((1,), (1,)), ((), ())),
            precision=HIGHEST,
            preferred_element_type=F32,
        )
        terms = jnp.concatenate([t for x in (log_ref[c], delta) for t in split_terms(x)], 1)
        message_ref[:, width + c * LANES : width + (c + 1) * LANES] = matmul(
            terms, place
        ).astype(BF16)


def backward_kernel(
    *refs, frames, items, patches, scale, head_size, heads,
):
    flag_ref, both_ref, query_ref, top_ref = refs[:4]
    grad_refs = refs[4 : 4 + frames]
    mark_refs = refs[4 + frames : 4 + 2 * frames]
    out_ref, sum_ref, held_ref, note_ref = refs[4 + 2 * frames :]
    lats, width = query_ref.shape
    own = grad_refs[0].shape[0]
    row_total = own // items
    base = items * patches
    for s in range(frames):
        source = lax.rem(flag_ref[items + 1] + (frames - s), frames)
        rows = pl.ds(pl.multiple_of(source * row_total, row_total), row_total)
        block = grad_refs[s][...].astype(F32)
        mark = mark_refs[s][...].astype(F32)
        for i in range(items):
            held_ref[i, rows, :] = block[i * row_total : (i + 1) * row_total]
            note_ref[i, rows, :] = mark[i * row_total : (i + 1) * row_total]
    masks = head_masks(lats, width, head_size)
    queries = spread_heads(query_ref[...].astype(F32), masks).astype(BF16)
    lat_both = both_ref[base : base + lats, :]
    row, lane = iota((GROUP * 8, LANES), 0), iota((GROUP * 8, LANES), 1)
    pick = jnp.logical_and(
        jnp.logical_and(
            lane // heads // 3 == row % 8,
            lane % heads == pl.program_id(0) * GROUP + row // 8,
        ),
        lane < 6 * heads,
    ).astype(BF16)
    grad_query = jnp.zeros((queries.shape[0], width), F32)
    lat_grad_key = jnp.zeros((lats, width), F32)
    lat_grad_value = jnp.zeros((lats, width), F32)
    for i in range(items):
        rows = slice(i * patches, (i + 1) * patches)
        stats = transposed_right(pick, note_ref[i].astype(BF16))
        stats = jnp.concatenate([stats[h * 8 : (h + 1) * 8] for h in range(GROUP)], 1)
        log_total = stats[0:1]
        delta = stats[1:2]
        top = top_ref[0, i, 0:1, :]
        rescale = jnp.exp(top - log_total)
        both = jnp.concatenate([both_ref[rows, :], lat_both], 0)
        keys, values = both[:, :width], both[:, width:]
        grads = spread_heads(held_ref[i], masks).astype(BF16)
        live = live_rows(flag_ref, i, items, patches, lats, queries.shape[0])
        masked = jnp.where(live, scale * transposed_right(keys, queries), MASKED)
        probs = jnp.where(live, jnp.exp(masked - log_total), 0.0)
        block_exp = jnp.where(live, jnp.exp(masked - top), 0.0)
        weights = (block_exp.astype(BF16).astype(F32) * rescale).astype(BF16)
        grad_scores = (probs * (transposed_right(values, grads) - delta)).astype(BF16)
        grad_key = scale * matmul(grad_scores, queries)
        grad_value = matmul(weights, grads)
        out_ref[rows, :width] = grad_key[:patches].astype(BF16)
        out_ref[rows, width:] = grad_value[:patches].astype(BF16)
        grad_query = grad_query + transposed_left(grad_scores, keys)
        lat_grad_key = lat_grad_key + grad_key[patches:]
        lat_grad_value = lat_grad_value + grad_value[patches:]
    out_ref[base : base + lats, :width] = lat_grad_key.astype(BF16)
    out_ref[base : base + lats, width:] = lat_grad_value.astype(BF16)
    sum_ref[...] = scale * collect_heads(grad_query, masks)


def media_kernel(flag_ref, *refs, chunks, items, frames):
    grad_refs, lat_refs, weight_refs = [
        refs[k * chunks : (k + 1) * chunks] for k in range(3)
    ]
    media_ref, time_ref, gain_ref, out_ref, sums_ref, product_ref = refs[3 * chunks :]
    item = pl.program_id(0)

    @pl.when(item == 0)
    def _():
        sums_ref[...] = jnp.zeros(sums_ref.shape, F32)
        product_ref[...] = functools.reduce(
            jnp.add, [transposed_right(g[...], w[...]) for g, w in zip(lat_refs, weight_refs)]
        )

    gradient = functools.reduce(
        jnp.add, [transposed_right(g[...], w[...]) for g, w in zip(grad_refs, weight_refs)]
    )
    inputs = media_ref[...].astype(F32) + time_ref[pl.ds(item, 1), :]
    back, gain_sum, bias_sum = norm_backward(inputs, gain_ref[...], gradient)
    out_ref[...] = back.astype(BF16)
    place = iota((frames, 1), 0) == flag_ref[items + 2 + item]
    sums_ref[0:frames, :] += jnp.where(place, jnp.sum(back, axis=0, keepdims=True), 0.0)
    sums_ref[8:9, :] += gain_sum
    sums_ref[9:10, :] += bias_sum


def latent_kernel(flag_ref, *refs, chunks, items):
    query_refs = refs[:chunks]
    (
        product_ref, latent_ref, gain_ref, base_ref, ffn_ref, media_ref, out_ref,
    ) = refs[chunks:]
    lats, width = latent_ref.shape
    half = width // chunks
    gradient = product_ref[...]
    for c in range(chunks):
        out_ref[lats : 2 * lats, c * half : (c + 1) * half] = query_refs[c][...]
    back, gain_sum, bias_sum = norm_backward(latent_ref[...], gain_ref[...], gradient)
    out_ref[:lats, :] = back
    row_total = base_ref.shape[0]
    start = pl.multiple_of(flag_ref[items + 1] * row_total, row_total)
    out_ref[pl.ds(start, row_total), :] += base_ref[...]
    at = 2 * lats
    out_ref[at : at + 8, :] = ffn_ref[...]
    out_ref[at + 2 : at + 3, :] = gain_sum
    out_ref[at + 3 : at + 4, :] = bias_sum
    out_ref[at + 8 : at + 24, :] = media_ref[...]
    out_ref[at + 24 :, :] = jnp.zeros((out_ref.shape[0] - at - 24, width), F32)


def query_norm_kernel(flag_ref, *refs, devices, items):
    column_refs = refs[:devices]
    latent_ref, gain_ref, sum_ref, out_ref, out_gain_ref, out_bias_ref, held_ref = refs[devices:]
    for d in range(devices):
        held_ref[jnp.bitwise_xor(flag_ref[2 * items + 2], d)] = column_refs[d][...]
    gradient = jnp.concatenate([held_ref[k] for k in range(devices)], 1)
    back, gain_sum, bias_sum = norm_backward(latent_ref[...], gain_ref[...], gradient)
    lats = latent_ref.shape[0]
    out_ref[...] = sum_ref[:lats, :] + back
    out_gain_ref[...] = sum_ref[2 * lats + 2 : 2 * lats + 3, :] + gain_sum
    out_bias_ref[...] = sum_ref[2 * lats + 3 : 2 * lats + 4, :] + bias_sum


def rows_kernel(flag_ref, *refs, count, frames, items):
    part_refs, out_refs, held_ref = refs[:count], refs[count:-1], refs[-1]
    rows = held_ref.shape[1]
    column = 0
    for part_ref in part_refs:
        total = total_of([part_ref[k] for k in range(part_ref.shape[0])])
        for f in range(frames):
            held_ref[f, :, column : column + total.shape[1]] = total[f * rows : (f + 1) * rows]
        column += total.shape[1]
    for s, out_ref in enumerate(out_refs):
        block = held_ref[lax.rem(flag_ref[items + 1] + s, frames)]
        out_ref[...] = block.astype(out_ref.dtype)


def place_kernel(flag_ref, *refs, chunks, frames, items, groups):
    chunk_refs = refs[: chunks * frames]
    key_ref, value_ref, out_ref = refs[chunks * frames :]
    width = key_ref.shape[2] // (chunks * groups)
    for s in range(frames):
        source = lax.rem(flag_ref[items + 1] + (frames - s), frames)
        out_ref[source] = chunk_refs[s][:, 2 * groups * width :].astype(F32)
        for c in range(chunks):
            for g in range(groups):
                at = (c * groups + g) * width
                block = chunk_refs[c * frames + s][:, 2 * g * width : 2 * (g + 1) * width]
                block = block.astype(F32)
                key_ref[source, :, at : at + width] = block[:, :width]
                value_ref[source, :, at : at + width] = block[:, width:]


def body(
    media,
    cotangent,
    frame_count,
    frame_start,
    latents,
    time_embed,
    media_gain,
    media_bias,
    latent_gain,
    latent_bias,
    ffn_gain,
    ffn_bias,
    query_weight,
    key_weight,
    value_weight,
    out_weight,
    up_weight,
    down_weight,
):
    items = media.shape[0]
    patches = media.shape[2]
    width = media.shape[3]
    lats = latents.shape[0]
    frame_total = time_embed.shape[0]
    row_total = cotangent.shape[1]
    own = items * row_total
    head_size = width // HEADS
    half = width // CHUNKS
    chunk_heads = HEADS // CHUNKS
    group_width = GROUP * head_size
    groups = chunk_heads // GROUP
    stack = GROUP * lats
    tokens = items * patches
    all_tokens = tokens + lats
    shard = query_weight.shape[0]
    hidden_shard = down_weight.shape[0]
    item_size = lax.axis_size("items")
    frame_size = lax.axis_size("frames")
    plane = item_size * own
    item_index = lax.axis_index("items")
    slot = lax.axis_index("frames")
    row_base = slot * row_total
    params = pltpu.CompilerParams(vmem_limit_bytes=56 * 2**20)
    smem = pl.BlockSpec(memory_space=pltpu.SMEM)
    whole = pl.BlockSpec(memory_space=pltpu.VMEM)
    sizes = dict(items=items, head_size=head_size, heads=chunk_heads)

    def struct(shape, kind):
        return jax.ShapeDtypeStruct(shape, kind)

    def cost(micros):
        return pl.CostEstimate(
            flops=int(micros * 1.15e9), bytes_accessed=int(micros * 3.6e6), transcendentals=0
        )

    def column_blocks(x):
        return jnp.transpose(x.reshape(-1, item_size, shard), (1, 0, 2))

    def scatter_exchange(x, axis):
        return jnp.sum(lax.all_to_all(x, axis, 0, 0).astype(F32), axis=0)

    grad_out = cotangent.reshape(own, width)
    low_columns = own * width // shard
    joined, grad_low = pl.pallas_call(
        functools.partial(join_kernel, width=group_width),
        out_shape=[struct((shard, 2 * width + low_columns), BF16), struct((own, width), BF16)],
        cost_estimate=cost(2.5),
        compiler_params=params,
    )(key_weight, value_weight, grad_out)
    kv_full = lax.all_gather(joined, "items", axis=0, tiled=True)
    low_frames = jnp.stack(spread_on(grad_low, "frames"))

    lat_norm = layer_norm(latents, latent_gain, latent_bias).astype(BF16)
    lat_cols = lax.dynamic_slice_in_dim(lat_norm, item_index * shard, shard, 1)
    query_blocks = column_blocks(matmul(lat_cols, query_weight))
    query_cols = scatter_exchange(query_blocks, "items").astype(BF16)
    query_spread = jnp.broadcast_to(query_cols[None], (item_size, lats, shard))
    queries = jnp.transpose(lax.all_to_all(query_spread, "items", 0, 0), (1, 0, 2)).reshape(
        lats, width
    )

    counts = lax.dynamic_slice_in_dim(frame_count, item_index * items, items)
    starts = lax.dynamic_slice_in_dim(frame_start, item_index * items, items)
    offset = (slot - starts) % frame_total
    flags = jnp.concatenate(
        [
            (offset < counts).astype(jnp.int32),
            (slot == 0).astype(jnp.int32)[None],
            slot.astype(jnp.int32)[None],
            offset.astype(jnp.int32),
            item_index.astype(jnp.int32)[None],
        ]
    )
    picker = (offset[:, None] == jnp.arange(frame_total, dtype=jnp.int32)[None, :]).astype(F32)
    time_rows = jnp.dot(picker, time_embed, precision=HIGHEST, preferred_element_type=F32)
    flat_media = media.reshape(tokens, width)
    steps = tokens // lats
    all_rows = pl.pallas_call(
        functools.partial(norm_kernel, steps=steps, per_item=patches // lats),
        grid=(steps + 1,),
        in_specs=[
            pl.BlockSpec((lats, width), lambda i: (jnp.minimum(i, steps - 1), 0)),
            whole,
            whole,
            whole,
            whole,
        ],
        out_specs=pl.BlockSpec((lats, width), lambda i: (i, 0)),
        out_shape=struct((all_tokens, width), BF16),
        cost_estimate=cost(12),
        compiler_params=params,
    )(
        after(flat_media, query_blocks),
        time_rows,
        media_gain[None],
        media_bias[None],
        lat_norm,
    )
    out_full = lax.all_gather(after(out_weight, all_rows), "items", axis=0, tiled=True)

    core = item_index % 2
    rows_across = after(all_rows, query_cols).T.reshape(item_size // 2, 2, shard, all_tokens)
    send_rows, keep_rows = [
        jnp.concatenate(
            [
                lax.dynamic_slice(
                    rows_across, (k, which, 0, 0), (1, 1, shard, all_tokens)
                ).reshape(shard, all_tokens)
                for k in range(item_size // 2)
            ],
            0,
        )
        for which in (1 - core, core)
    ]
    boths, tops, messages = [], [], []
    for c in range(CHUNKS):

        def block_of(g, c=c):
            return (0, c * groups + g)

        if c:
            rows = after(all_rows, tops[-1])
        else:
            rows = after(all_rows, queries, send_rows, keep_rows)
        both = matmul(rows, kv_full[:, 2 * c * half : 2 * (c + 1) * half]).astype(BF16)
        top, *parts = pl.pallas_call(
            functools.partial(
                forward_kernel, patches=patches, scale=head_size**-0.5, **sizes
            ),
            grid=(groups,),
            in_specs=[
                smem,
                pl.BlockSpec((all_tokens, 2 * group_width), lambda g: (0, g)),
                pl.BlockSpec((lats, group_width), block_of),
            ],
            out_specs=[pl.BlockSpec((1, items, 8, stack), lambda g: (g, 0, 0, 0))]
            + [pl.BlockSpec((own, half + LANES), lambda g: (0, 0))] * frame_size,
            out_shape=[struct((groups, items, 8, stack), F32)]
            + [struct((own, half + LANES), BF16)] * frame_size,
            scratch_shapes=[
                pltpu.VMEM((items, lats, group_width), F32),
                pltpu.VMEM((items, lats, LANES), F32),
            ],
            cost_estimate=cost(7.8),
            compiler_params=params,
        )(flags, both, queries)
        boths.append(both)
        tops.append(top)
        messages += [p if s == 0 else send_on(p, "frames", s) for s, p in enumerate(parts)]
    up_slice = lax.all_to_all(after(up_weight, boths[0]), "items", 1, 0, tiled=True)
    low_all = lax.all_gather(after(low_frames, tops[1]), "items", axis=0).reshape(-1, width)

    base_rows = lax.dynamic_slice_in_dim(latents, row_base, row_total, 0)
    merged, mid_rows, ffn_in, logs, entropy_wide = pl.pallas_call(
        functools.partial(merge_kernel, chunks=CHUNKS, frames=frame_size, **sizes),
        out_shape=[
            struct((own, width), F32),
            struct((own, width), F32),
            struct((own, width), BF16),
            struct((CHUNKS, own, LANES), F32),
            struct((own, LANES), F32),
        ],
        cost_estimate=cost(6.3),
        compiler_params=params,
    )(*messages, base_rows, out_full, ffn_gain[None], ffn_bias[None])
    entropy = entropy_wide[:, 0].reshape(items, row_total)

    ffn_blocks = spread_across(ffn_in, "items")
    ffn_frames = spread_on(after(ffn_in, *ffn_blocks), "frames")
    result_part, *parts = pl.pallas_call(
        functools.partial(feed_kernel, devices=item_size, items=items),
        grid=(1,),
        in_specs=[smem]
        + [whole] * item_size
        + [
            pl.BlockSpec((width, low_columns), lambda i: (0, 2 * width // low_columns)),
            whole,
            whole,
        ],
        out_specs=[whole] * (1 + item_size),
        out_shape=[struct((item_size, own, width), BF16)]
        + [struct((own, width), BF16)] * item_size,
        scratch_shapes=[pltpu.VMEM((plane, width), BF16)] * 2,
        cost_estimate=cost(10),
        compiler_params=params,
    )(flags, *ffn_blocks, kv_full, up_slice, down_weight)
    grad_blocks = collect_across(parts, "items")
    grad_blocks[0] = after(grad_blocks[0], *ffn_frames)

    turn, grad_branch, grad_base, ffn_sums = pl.pallas_call(
        functools.partial(turn_kernel, devices=item_size, chunks=CHUNKS, **sizes),
        out_shape=[
            struct((own, width + CHUNKS * LANES), BF16),
            struct((own, 2 * width), BF16),
            struct((row_total, width), F32),
            struct((8, width), F32),
        ],
        cost_estimate=cost(7.6),
        compiler_params=params,
    )(*grad_blocks, mid_rows, grad_out, ffn_gain[None], merged, logs, out_full)
    turns = spread_on(turn, "frames")
    ffn_all = lax.all_gather(
        after(jnp.stack(ffn_frames), grad_branch), "items", axis=0
    ).reshape(-1, width)
    turns[0] = after(turns[0], low_all)

    chunk_grads, chunk_queries = [], []

    def weight_terms(c):
        send = matmul(send_rows, chunk_grads[c]).astype(BF16)
        received = send_across(send, "items", 1).reshape(-1, shard, 2 * half)
        keep = matmul(after(keep_rows, send), chunk_grads[c]).astype(BF16)
        return send, keep.reshape(-1, shard, 2 * half), received

    def chip_terms(keep, received):
        return (keep.astype(F32) + received.astype(F32)).astype(BF16)

    def exchange_chips(x):
        groups_of = [list(range(k, item_size, 2)) for k in range(2)]
        return lax.all_to_all(x, "items", 0, 0, axis_index_groups=groups_of)

    def frame_rows(ranges):
        rows = shard // frame_size
        columns = sum(x.shape[-1] for x in ranges)
        return pl.pallas_call(
            functools.partial(rows_kernel, count=len(ranges), frames=frame_size, items=items),
            in_specs=[smem] + [whole] * len(ranges),
            out_specs=[whole] * frame_size,
            out_shape=[struct((rows, columns), F32)]
            + [struct((rows, columns), BF16)] * (frame_size - 1),
            scratch_shapes=[pltpu.VMEM((frame_size, rows, columns), F32)],
            cost_estimate=cost(3.5),
            compiler_params=params,
        )(flags, *ranges)

    def send_rows_on(rows):
        return [rows[0]] + [send_on(p, "frames", s) for s, p in enumerate(rows) if s]

    for c in range(CHUNKS):

        def block_of(g, c=c):
            return (0, c * groups + g)

        chunk_grad, chunk_query = pl.pallas_call(
            functools.partial(
                backward_kernel, frames=frame_size, patches=patches, scale=head_size**-0.5, **sizes
            ),
            grid=(groups,),
            in_specs=[
                smem,
                pl.BlockSpec((all_tokens, 2 * group_width), lambda g: (0, g)),
                pl.BlockSpec((lats, group_width), block_of),
                pl.BlockSpec((1, items, 8, stack), lambda g: (g, 0, 0, 0)),
            ]
            + [pl.BlockSpec((own, group_width), block_of)] * frame_size
            + [pl.BlockSpec((own, LANES), lambda g, c=c: (0, width // LANES + c))] * frame_size,
            out_specs=[
                pl.BlockSpec((all_tokens, 2 * group_width), lambda g: (0, g)),
                pl.BlockSpec((lats, group_width), lambda g: (0, g)),
            ],
            out_shape=[
                struct((all_tokens, 2 * half), BF16),
                struct((lats, half), F32),
            ],
            scratch_shapes=[
                pltpu.VMEM((items, lats, group_width), F32),
                pltpu.VMEM((items, lats, LANES), F32),
            ],
            cost_estimate=cost(8),
            compiler_params=params,
        )(flags, after(boths[c], *held) if c else boths[c], queries, tops[c], *turns, *turns)
        chunk_grads.append(chunk_grad)
        chunk_queries.append(chunk_query)
        if c == 0:
            first_send, first_keep, first_received = weight_terms(0)
            held = (first_send,)
    first_terms = chip_terms(after(first_keep, chunk_grads[-1]), first_received)
    first_moved = exchange_chips(first_terms)

    last_block = pl.BlockSpec((lats, 2 * half), lambda i: (tokens // lats, 0))
    media_grad, media_sums, lat_product = pl.pallas_call(
        functools.partial(media_kernel, chunks=CHUNKS, items=items, frames=frame_total),
        grid=(items,),
        in_specs=[smem]
        + [pl.BlockSpec((patches, 2 * half), lambda i: (i, 0))] * CHUNKS
        + [last_block] * CHUNKS
        + [pl.BlockSpec((width, 2 * half), lambda i, c=c: (0, c)) for c in range(CHUNKS)]
        + [pl.BlockSpec((patches, width), lambda i: (i, 0)), whole, whole],
        out_specs=[
            pl.BlockSpec((patches, width), lambda i: (i, 0)),
            pl.BlockSpec((16, width), lambda i: (0, 0)),
            pl.BlockSpec((lats, width), lambda i: (0, 0)),
        ],
        out_shape=[
            struct((tokens, width), BF16),
            struct((16, width), F32),
            struct((lats, width), F32),
        ],
        cost_estimate=cost(21),
        compiler_params=params,
    )(
        flags,
        *chunk_grads[:-1],
        after(chunk_grads[-1], first_terms),
        *chunk_grads,
        *[kv_full] * CHUNKS,
        flat_media,
        time_rows,
        media_gain[None],
    )

    branch_plane = lax.all_gather(
        after(grad_branch, lat_product), "items", axis=0, tiled=True
    )
    att_plane = lax.dynamic_slice_in_dim(
        branch_plane, width + item_index * shard, shard, 1
    )

    sum_rows = 2 * lats + 24
    sum_rows += -sum_rows % (8 * item_size)
    payload = pl.pallas_call(
        functools.partial(latent_kernel, chunks=CHUNKS, items=items),
        in_specs=[smem] + [whole] * (CHUNKS + 6),
        out_specs=whole,
        out_shape=struct((sum_rows, width), F32),
        cost_estimate=cost(3),
        compiler_params=params,
    )(
        flags,
        *chunk_queries,
        after(lat_product, first_moved),
        latents,
        latent_gain[None],
        grad_base,
        ffn_sums,
        media_sums,
    )
    payload_part = lax.psum_scatter(payload, "items", scatter_dimension=0, tiled=True)

    chunk_grads[-1] = after(chunk_grads[-1], payload)
    last_send, last_keep, last_received = weight_terms(CHUNKS - 1)
    last_terms = chip_terms(after(last_keep, first_moved), last_received)
    last_moved = exchange_chips(last_terms)
    out_part = transposed_left(att_plane, after(branch_plane, last_terms)[:, :width])
    first_rows = frame_rows([after(first_moved, last_terms), out_part[None]])
    first_frames = send_rows_on(first_rows)
    all_plane = plane * frame_size
    block_rows = min(512, all_plane)
    row_block = pl.BlockSpec((block_rows, width), lambda i: (i, 0))
    hidden_block = pl.BlockSpec((block_rows, hidden_shard), lambda i: (i, 0))
    hidden, grad_up = pl.pallas_call(
        feed_back_kernel,
        grid=(all_plane // block_rows,),
        in_specs=[row_block, row_block, whole, whole],
        out_specs=[hidden_block, hidden_block],
        out_shape=[struct((all_plane, hidden_shard), BF16)] * 2,
        cost_estimate=cost(15),
        compiler_params=params,
    )(after(ffn_all, *first_rows), low_all, up_slice, down_weight)

    def outer(left, right, tile, kind):
        rows, columns = left.shape
        shape = (columns, right.shape[1])
        return pl.pallas_call(
            outer_kernel,
            grid=(columns // tile,),
            in_specs=[pl.BlockSpec((rows, tile), lambda i: (0, i)), whole],
            out_specs=pl.BlockSpec((tile, shape[1]), lambda i: (i, 0)),
            out_shape=struct(shape, kind),
            cost_estimate=cost(9.5),
            compiler_params=params,
        )(left, right)

    first_total = total_of(first_frames).astype(BF16)
    first_placed = spread_on(first_total, "frames")
    last_rows = frame_rows([after(last_moved, hidden)])
    last_frames = send_rows_on(last_rows)
    down_grad = outer(
        after(hidden, first_total, *last_rows),
        low_all,
        256 if hidden_shard % 256 == 0 else hidden_shard,
        F32,
    )
    last_total = total_of(last_frames).astype(BF16)
    last_placed = spread_on(last_total, "frames")
    up_part = outer(
        ffn_all, after(grad_up, down_grad, last_total, *first_placed), width // 4, BF16
    )
    up_grad = lax.all_to_all(up_part, "items", 0, 1, tiled=True).astype(F32)
    placed = first_placed + last_placed
    payload_part = after(payload_part, down_grad)
    payload_others = spread_on(payload_part.astype(BF16), "frames")[1:]
    sums = lax.all_gather(
        total_of([payload_part] + payload_others), "items", axis=0, tiled=True
    )
    query_low = sums[lats : 2 * lats].astype(BF16)
    query_grad = transposed_left(lat_cols, query_low)
    norm_cols = after(transposed_right(query_low, query_weight), *last_placed)
    latents_grad, lat_gain, lat_bias = pl.pallas_call(
        functools.partial(query_norm_kernel, devices=item_size, items=items),
        in_specs=[smem] + [whole] * (item_size + 3),
        out_specs=[whole] * 3,
        out_shape=[struct((lats, width), F32), struct((1, width), F32), struct((1, width), F32)],
        scratch_shapes=[pltpu.VMEM((item_size, lats, shard), F32)],
        cost_estimate=cost(3),
        compiler_params=params,
    )(flags, *spread_across(norm_cols, "items"), latents, latent_gain[None], sums)
    at = 2 * lats
    column_sums = lax.dynamic_slice_in_dim(
        sums[at + 8 : at + 24], item_index * shard, shard, 1
    )

    key_grad, value_grad, out_grad = pl.pallas_call(
        functools.partial(
            place_kernel, chunks=CHUNKS, frames=frame_size, items=items, groups=groups
        ),
        in_specs=[smem] + [whole] * len(placed),
        out_specs=[whole] * 3,
        out_shape=[struct((frame_size, shard // frame_size, width), F32)] * 3,
        cost_estimate=cost(3.4),
        compiler_params=params,
    )(flags, *placed)

    result_sum = lax.psum_scatter(
        after(result_part, sums).reshape(-1, width), "items", scatter_dimension=0, tiled=True
    )
    result = mid_rows + result_sum.astype(F32)
    return (
        result.reshape(items, row_total, width),
        entropy,
        media_grad.reshape(media.shape),
        latents_grad,
        column_sums[:frame_total],
        column_sums[8],
        column_sums[9],
        lat_gain[0],
        lat_bias[0],
        sums[at],
        sums[at + 1],
        query_grad,
        key_grad.reshape(shard, width),
        value_grad.reshape(shard, width),
        out_grad.reshape(shard, width),
        up_grad,
        down_grad,
    )


def solution(mesh):
    return jax.shard_map(
        body,
        mesh=mesh,
        in_specs=(
            P("items", "frames", None, None),
            P("items", "frames", None),
            P(),
            P(),
            P(),
            P(),
            P(),
            P(),
            P(),
            P(),
            P(),
            P(),
            P("items", None),
            P("items", None),
            P("items", None),
            P("items", None),
            P("items", None),
            P("items", None),
        ),
        out_specs=(
            P("items", "frames", None),
            P("items", "frames"),
            P("items", "frames", None, None),
            P(),
            P(None, "items"),
            P("items"),
            P("items"),
            P(),
            P(),
            P(),
            P(),
            P("items", None),
            P("items", None),
            P("items", None),
            P("items", None),
            P("items", None),
            P("items", None),
        ),
        check_vma=False,
    )
```

```python
import functools
import math

import jax
import jax.numpy as jnp
from jax import lax
from jax.experimental import pallas as pl
from jax.experimental.pallas import tpu as pltpu
from jax.sharding import PartitionSpec as P

HEADS = 16
GROUP = 4
CHUNKS = 2
LANES = 128
EPSILON = 1e-05
MASKED = -1e30
F32 = jnp.float32
BF16 = jnp.bfloat16
HIGHEST = lax.Precision.HIGHEST


def layer_norm(inputs, norm_gain, norm_bias):
    center = inputs - jnp.mean(inputs, axis=-1, keepdims=True)
    spread = jnp.mean(center * center, axis=-1, keepdims=True)
    return center * lax.rsqrt(spread + EPSILON) * norm_gain + norm_bias


def matmul(left_side, right_side):
    return jnp.dot(left_side, right_side, preferred_element_type=F32)


def transposed_left(left_side, right_side):
    return lax.dot_general(
        left_side, right_side, (((0,), (0,)), ((), ())), preferred_element_type=F32
    )


def transposed_right(left_side, right_side):
    return lax.dot_general(
        left_side, right_side, (((1,), (1,)), ((), ())), preferred_element_type=F32
    )


def send_on(x, axis, step):
    size = lax.axis_size(axis)
    return lax.ppermute(x, axis, [(i, (i + step) % size) for i in range(size)])


def send_across(x, axis, distance):
    return lax.ppermute(x, axis, [(i, i ^ distance) for i in range(lax.axis_size(axis))])


def spread_on(x, axis):
    return [x] + [send_on(x, axis, s) for s in range(1, lax.axis_size(axis))]


def spread_across(x, axis):
    chips = [x] + [send_across(x, axis, d) for d in range(2, lax.axis_size(axis), 2)]
    return [b for block in chips for b in (block, send_across(block, axis, 1))]


def collect_across(pieces, axis):
    return [pieces[0]] + [send_across(p, axis, d) for d, p in enumerate(pieces) if d]


def total_of(pieces):
    return functools.reduce(jnp.add, [p.astype(F32) for p in pieces])


def after(x, *earlier):
    return lax.optimization_barrier((x,) + earlier)[0]


def split_terms(x):
    high = x.astype(BF16)
    rest = x - high.astype(F32)
    middle = rest.astype(BF16)
    return high, middle, (rest - middle.astype(F32)).astype(BF16)


def iota(shape, dim):
    return lax.broadcasted_iota(jnp.int32, shape, dim)


def head_masks(rows, width, head_size):
    lane = iota((rows, width), 1)
    return [
        jnp.logical_and(lane >= h * head_size, lane < (h + 1) * head_size)
        for h in range(width // head_size)
    ]


def spread_heads(block, masks):
    return jnp.concatenate([jnp.where(m, block, jnp.zeros_like(block)) for m in masks], 0)


def collect_heads(block, masks):
    rows = block.shape[0] // len(masks)
    total = jnp.where(masks[0], block[:rows], 0.0)
    for h in range(1, len(masks)):
        total = total + jnp.where(masks[h], block[h * rows : (h + 1) * rows], 0.0)
    return total


def head_expand(width, head_size):
    row, column = iota((LANES, width), 0), iota((LANES, width), 1)
    return jnp.logical_and(column >= row * head_size, column < (row + 1) * head_size).astype(F32)


def live_rows(flag_ref, item, items, patches, lats, columns):
    row = iota((patches + lats, columns), 0)
    media = jnp.logical_and(row < patches, flag_ref[item] > 0)
    return jnp.logical_or(media, jnp.logical_and(row >= patches, flag_ref[items] > 0))


def pack_shape(own, shard, width):
    unit = math.gcd(own, shard)
    return unit, width * unit // shard


def join_kernel(key_ref, value_ref, cotangent_ref, out_ref, low_ref, *, width):
    for g in range(key_ref.shape[1] // width):
        columns = slice(g * width, (g + 1) * width)
        out_ref[:, 2 * g * width : (2 * g + 1) * width] = key_ref[:, columns]
        out_ref[:, (2 * g + 1) * width : (2 * g + 2) * width] = value_ref[:, columns]
    low = cotangent_ref[...].astype(BF16)
    low_ref[...] = low
    own, span = low.shape
    unit, piece = pack_shape(own, out_ref.shape[0], span)
    for a in range(own // unit):
        for b in range(span // piece):
            at = 2 * span + a * piece
            out_ref[b * unit : (b + 1) * unit, at : at + piece] = low[
                a * unit : (a + 1) * unit, b * piece : (b + 1) * piece
            ]


def norm_kernel(media_ref, time_ref, gain_ref, bias_ref, lat_ref, out_ref, *, steps, per_item):
    step = pl.program_id(0)

    @pl.when(step < steps)
    def _():
        rows = media_ref[...].astype(F32) + time_ref[pl.ds(step // per_item, 1), :]
        out_ref[...] = layer_norm(rows, gain_ref[...], bias_ref[...]).astype(BF16)

    @pl.when(step == steps)
    def _():
        out_ref[...] = lat_ref[...]


def forward_kernel(
    flag_ref, both_ref, query_ref, top_ref, *refs, items, patches, scale, head_size, heads,
):
    message_refs, (part_ref, mark_ref) = refs[:-2], refs[-2:]
    lats, width = query_ref.shape
    frames = len(message_refs)
    own = message_refs[0].shape[0]
    row_total = own // items
    masks = head_masks(lats, width, head_size)
    queries = spread_heads(query_ref[...].astype(F32), masks).astype(BF16)
    base = items * patches
    lat_both = both_ref[base : base + lats, :]
    group = pl.program_id(0)
    term, lane = iota((16, GROUP * LANES), 0), iota((16, GROUP * LANES), 1)
    place = jnp.logical_and(
        lane % LANES == term * heads + group * GROUP + lane // LANES, term < 9
    ).astype(BF16)
    for i in range(items):
        both = jnp.concatenate([both_ref[i * patches : (i + 1) * patches, :], lat_both], 0)
        live = live_rows(flag_ref, i, items, patches, lats, queries.shape[0])
        scores = scale * transposed_right(both[:, :width], queries)
        masked = jnp.where(live, scores, MASKED)
        top = jnp.max(masked, axis=0, keepdims=True)
        block_exp = jnp.where(live, jnp.exp(masked - top), 0.0)
        total = jnp.sum(block_exp, axis=0, keepdims=True)
        moment = jnp.sum(block_exp * scores, axis=0, keepdims=True)
        part = transposed_left(block_exp.astype(BF16), both[:, width:])
        part_ref[i] = collect_heads(part, masks)
        top_ref[0, i] = jnp.broadcast_to(top, top_ref.shape[2:])
        terms = jnp.concatenate(
            [t.astype(F32) for x in (top, total, moment) for t in split_terms(x)]
            + [jnp.zeros((7, top.shape[1]), F32)],
            0,
        ).astype(BF16)
        wide = transposed_left(terms, place)
        mark = wide[:lats, :LANES]
        for h in range(1, GROUP):
            mark = mark + wide[h * lats : (h + 1) * lats, h * LANES : (h + 1) * LANES]
        mark_ref[i] = mark

    end = message_refs[0].shape[1] - LANES
    for s, message_ref in enumerate(message_refs):
        start = pl.multiple_of(lax.rem(flag_ref[items + 1] + s, frames) * row_total, row_total)
        rows = pl.ds(start, row_total)
        block = jnp.concatenate([part_ref[i, rows, :] for i in range(items)], 0).astype(BF16)
        mark = jnp.concatenate([mark_ref[i, rows, :] for i in range(items)], 0).astype(BF16)
        for g in range(end // width):

            @pl.when(group == g)
            def _():
                message_ref[:, g * width : (g + 1) * width] = block
                if g == 0:
                    message_ref[:, end:] = mark
                else:
                    message_ref[:, end:] = message_ref[:, end:] + mark


def merge_kernel(*refs, chunks, frames, items, head_size, heads):
    message_refs = refs[: chunks * frames]
    base_ref, weight_ref, gain_ref, bias_ref = refs[chunks * frames : chunks * frames + 4]
    merged_ref, mid_ref, ffn_ref, log_ref, entropy_ref = refs[chunks * frames + 4 :]
    own, columns = message_refs[0].shape
    half = columns - LANES
    lane, column = iota((LANES, 3 * LANES), 0), iota((LANES, 3 * LANES), 1)
    gather = jnp.logical_and(
        jnp.logical_and(lane // heads // 3 == column // LANES, lane % heads == column % LANES),
        lane < 9 * heads,
    ).astype(BF16)
    expand = head_expand(half, head_size)
    live = iota((own, LANES), 1) < heads
    spread = jnp.zeros((own, LANES), F32)
    for c in range(chunks):
        sources = message_refs[c * frames : (c + 1) * frames]
        stats = [matmul(x[:, half:], gather) for x in sources]
        tops = [x[:, :LANES] for x in stats]
        peak = functools.reduce(jnp.maximum, tops)
        factors = [jnp.exp(t - peak) for t in tops]
        whole = sum(f * x[:, LANES : 2 * LANES] for f, x in zip(factors, stats))
        moment = sum(f * x[:, 2 * LANES :] for f, x in zip(factors, stats))
        whole = jnp.where(live, whole, 1.0)
        log_total = jnp.where(live, peak + jnp.log(whole), 0.0)
        log_ref[c] = log_total
        spread = spread + jnp.where(live, log_total - moment / whole, 0.0)
        merged = jnp.zeros((own, half), F32)
        for x, factor in zip(sources, factors):
            share = jnp.where(live, factor / whole, 0.0)
            wide = jnp.dot(share, expand, precision=HIGHEST, preferred_element_type=F32)
            merged = merged + x[:, :half].astype(F32) * wide
        merged_ref[:, c * half : (c + 1) * half] = merged
    entropy_ref[...] = jnp.broadcast_to(
        jnp.sum(spread, axis=1, keepdims=True) * (1.0 / HEADS), entropy_ref.shape
    )
    base = jnp.concatenate([base_ref[...]] * items, 0)
    mid = base + matmul(merged_ref[...].astype(BF16), weight_ref[...])
    mid_ref[...] = mid
    ffn_ref[...] = layer_norm(mid, gain_ref[...], bias_ref[...]).astype(BF16)


def gelu_parts(x):
    share = 0.5 * (1.0 + lax.erf(x * (0.5**0.5)))
    slope = share + x * jnp.exp(-0.5 * x * x) * ((2.0 * jnp.pi) ** -0.5)
    return x * share, slope


def feed_kernel(flag_ref, *refs, devices, items):
    row_refs = refs[:devices]
    low_ref, up_ref, down_ref, result_ref = refs[devices : devices + 4]
    grad_refs, (plane_ref, plane_low_ref) = refs[devices + 4 : -2], refs[-2:]
    own, width = row_refs[0].shape
    shard = low_ref.shape[0] // devices
    unit, piece = pack_shape(own, shard, width)
    me = flag_ref[2 * items + 2]
    for d in range(devices):
        plane_ref[d * own : (d + 1) * own, :] = row_refs[d][...]
        source = jnp.bitwise_xor(me, d) * shard
        for a in range(own // unit):
            rows = slice(d * own + a * unit, d * own + (a + 1) * unit)
            for b in range(shard // unit):
                start = pl.multiple_of(source + b * unit, unit)
                plane_low_ref[rows, b * piece : (b + 1) * piece] = low_ref[
                    pl.ds(start, unit), a * piece : (a + 1) * piece
                ]
    upward = matmul(plane_ref[...], up_ref[...])
    hidden, slope = gelu_parts(upward)
    grad_up = (slope * transposed_right(plane_low_ref[...], down_ref[...])).astype(BF16)
    grad = transposed_right(grad_up, up_ref[...]).astype(BF16)
    result = matmul(hidden.astype(BF16), down_ref[...]).astype(BF16)
    for d in range(devices):
        grad_refs[d][...] = grad[d * own : (d + 1) * own, :]
        result_ref[jnp.bitwise_xor(me, d)] = result[d * own : (d + 1) * own, :]


def feed_back_kernel(row_ref, low_ref, up_ref, down_ref, hidden_ref, grad_ref):
    hidden, slope = gelu_parts(matmul(row_ref[...], up_ref[...]))
    hidden_ref[...] = hidden.astype(BF16)
    grad_ref[...] = (slope * transposed_right(low_ref[...], down_ref[...])).astype(BF16)


def outer_kernel(left_ref, right_ref, out_ref):
    out_ref[...] = transposed_left(left_ref[...], right_ref[...]).astype(out_ref.dtype)


def norm_backward(rows, gain, gradient):
    center = rows - jnp.mean(rows, axis=1, keepdims=True)
    rate = lax.rsqrt(jnp.mean(center * center, axis=1, keepdims=True) + EPSILON)
    unit = center * rate
    scaled = gradient * gain
    inner = scaled - jnp.mean(scaled, axis=1, keepdims=True)
    back = rate * (inner - unit * jnp.mean(scaled * unit, axis=1, keepdims=True))
    return (
        back,
        jnp.sum(gradient * unit, axis=0, keepdims=True),
        jnp.sum(gradient, axis=0, keepdims=True),
    )


def turn_kernel(*refs, devices, items, chunks, head_size, heads):
    part_refs = refs[:devices]
    mid_ref, cotangent_ref, gain_ref, merged_ref, log_ref, weight_ref = refs[
        devices : devices + 6
    ]
    message_ref, branch_ref, base_ref, sums_ref = refs[devices + 6 :]
    own, width = mid_ref.shape
    half = width // chunks
    gradient = total_of([x[...] for x in part_refs])
    back, gain_sum, bias_sum = norm_backward(mid_ref[...], gain_ref[...], gradient)
    grad_mid = cotangent_ref[...] + back
    sums_ref[...] = jnp.zeros(sums_ref.shape, F32)
    sums_ref[0:1, :] = gain_sum
    sums_ref[1:2, :] = bias_sum
    row_total = own // items
    base_ref[...] = total_of(
        [grad_mid[i * row_total : (i + 1) * row_total] for i in range(items)]
    )
    branch = grad_mid.astype(BF16)
    branch_ref[:, :width] = branch
    branch_ref[:, width:] = merged_ref[...].astype(BF16)
    grad_att = transposed_right(branch, weight_ref[...]).astype(BF16)
    expand = head_expand(half, head_size)
    lane, column = iota((6 * LANES, LANES), 0), iota((6 * LANES, LANES), 1)
    place = jnp.logical_and(
        lane % LANES < heads, column == (lane // LANES) * heads + lane % LANES
    ).astype(BF16)
    message_ref[:, :width] = grad_att
    for c in range(chunks):
        columns = slice(c * half, (c + 1) * half)
        delta = lax.dot_general(
            merged_ref[:, columns] * grad_att[:, columns].astype(F32),
            expand,
            (((1,), (1,)), ((), ())),
            precision=HIGHEST,
            preferred_element_type=F32,
        )
        terms = jnp.concatenate([t for x in (log_ref[c], delta) for t in split_terms(x)], 1)
        message_ref[:, width + c * LANES : width + (c + 1) * LANES] = matmul(
            terms, place
        ).astype(BF16)


def backward_kernel(
    *refs, frames, items, patches, scale, head_size, heads,
):
    flag_ref, both_ref, query_ref, top_ref = refs[:4]
    grad_refs = refs[4 : 4 + frames]
    mark_refs = refs[4 + frames : 4 + 2 * frames]
    out_ref, sum_ref, held_ref, note_ref = refs[4 + 2 * frames :]
    lats, width = query_ref.shape
    own = grad_refs[0].shape[0]
    row_total = own // items
    base = items * patches
    for s in range(frames):
        source = lax.rem(flag_ref[items + 1] + (frames - s), frames)
        rows = pl.ds(pl.multiple_of(source * row_total, row_total), row_total)
        block = grad_refs[s][...].astype(F32)
        mark = mark_refs[s][...].astype(F32)
        for i in range(items):
            held_ref[i, rows, :] = block[i * row_total : (i + 1) * row_total]
            note_ref[i, rows, :] = mark[i * row_total : (i + 1) * row_total]
    masks = head_masks(lats, width, head_size)
    queries = spread_heads(query_ref[...].astype(F32), masks).astype(BF16)
    lat_both = both_ref[base : base + lats, :]
    row, lane = iota((GROUP * 8, LANES), 0), iota((GROUP * 8, LANES), 1)
    pick = jnp.logical_and(
        jnp.logical_and(
            lane // heads // 3 == row % 8,
            lane % heads == pl.program_id(0) * GROUP + row // 8,
        ),
        lane < 6 * heads,
    ).astype(BF16)
    grad_query = jnp.zeros((queries.shape[0], width), F32)
    lat_grad_key = jnp.zeros((lats, width), F32)
    lat_grad_value = jnp.zeros((lats, width), F32)
    for i in range(items):
        rows = slice(i * patches, (i + 1) * patches)
        stats = transposed_right(pick, note_ref[i].astype(BF16))
        stats = jnp.concatenate([stats[h * 8 : (h + 1) * 8] for h in range(GROUP)], 1)
        log_total = stats[0:1]
        delta = stats[1:2]
        top = top_ref[0, i, 0:1, :]
        rescale = jnp.exp(top - log_total)
        both = jnp.concatenate([both_ref[rows, :], lat_both], 0)
        keys, values = both[:, :width], both[:, width:]
        grads = spread_heads(held_ref[i], masks).astype(BF16)
        live = live_rows(flag_ref, i, items, patches, lats, queries.shape[0])
        masked = jnp.where(live, scale * transposed_right(keys, queries), MASKED)
        probs = jnp.where(live, jnp.exp(masked - log_total), 0.0)
        block_exp = jnp.where(live, jnp.exp(masked - top), 0.0)
        weights = (block_exp.astype(BF16).astype(F32) * rescale).astype(BF16)
        grad_scores = (probs * (transposed_right(values, grads) - delta)).astype(BF16)
        grad_key = scale * matmul(grad_scores, queries)
        grad_value = matmul(weights, grads)
        out_ref[rows, :width] = grad_key[:patches].astype(BF16)
        out_ref[rows, width:] = grad_value[:patches].astype(BF16)
        grad_query = grad_query + transposed_left(grad_scores, keys)
        lat_grad_key = lat_grad_key + grad_key[patches:]
        lat_grad_value = lat_grad_value + grad_value[patches:]
    out_ref[base : base + lats, :width] = lat_grad_key.astype(BF16)
    out_ref[base : base + lats, width:] = lat_grad_value.astype(BF16)
    sum_ref[...] = scale * collect_heads(grad_query, masks)


def media_kernel(flag_ref, *refs, chunks, items, frames):
    grad_refs, lat_refs, weight_refs = [
        refs[k * chunks : (k + 1) * chunks] for k in range(3)
    ]
    media_ref, time_ref, gain_ref, out_ref, sums_ref, product_ref = refs[3 * chunks :]
    item = pl.program_id(0)

    @pl.when(item == 0)
    def _():
        sums_ref[...] = jnp.zeros(sums_ref.shape, F32)
        product_ref[...] = functools.reduce(
            jnp.add, [transposed_right(g[...], w[...]) for g, w in zip(lat_refs, weight_refs)]
        )

    gradient = functools.reduce(
        jnp.add, [transposed_right(g[...], w[...]) for g, w in zip(grad_refs, weight_refs)]
    )
    inputs = media_ref[...].astype(F32) + time_ref[pl.ds(item, 1), :]
    back, gain_sum, bias_sum = norm_backward(inputs, gain_ref[...], gradient)
    out_ref[...] = back.astype(BF16)
    place = iota((frames, 1), 0) == flag_ref[items + 2 + item]
    sums_ref[0:frames, :] += jnp.where(place, jnp.sum(back, axis=0, keepdims=True), 0.0)
    sums_ref[8:9, :] += gain_sum
    sums_ref[9:10, :] += bias_sum


def latent_kernel(flag_ref, *refs, chunks, items):
    query_refs = refs[:chunks]
    (
        product_ref, latent_ref, gain_ref, base_ref, ffn_ref, media_ref, out_ref,
    ) = refs[chunks:]
    lats, width = latent_ref.shape
    half = width // chunks
    gradient = product_ref[...]
    for c in range(chunks):
        out_ref[lats : 2 * lats, c * half : (c + 1) * half] = query_refs[c][...]
    back, gain_sum, bias_sum = norm_backward(latent_ref[...], gain_ref[...], gradient)
    out_ref[:lats, :] = back
    row_total = base_ref.shape[0]
    start = pl.multiple_of(flag_ref[items + 1] * row_total, row_total)
    out_ref[pl.ds(start, row_total), :] += base_ref[...]
    at = 2 * lats
    out_ref[at : at + 8, :] = ffn_ref[...]
    out_ref[at + 2 : at + 3, :] = gain_sum
    out_ref[at + 3 : at + 4, :] = bias_sum
    out_ref[at + 8 : at + 24, :] = media_ref[...]
    out_ref[at + 24 :, :] = jnp.zeros((out_ref.shape[0] - at - 24, width), F32)


def query_norm_kernel(flag_ref, *refs, devices, items):
    column_refs = refs[:devices]
    latent_ref, gain_ref, sum_ref, out_ref, out_gain_ref, out_bias_ref, held_ref = refs[devices:]
    for d in range(devices):
        held_ref[jnp.bitwise_xor(flag_ref[2 * items + 2], d)] = column_refs[d][...]
    gradient = jnp.concatenate([held_ref[k] for k in range(devices)], 1)
    back, gain_sum, bias_sum = norm_backward(latent_ref[...], gain_ref[...], gradient)
    lats = latent_ref.shape[0]
    out_ref[...] = sum_ref[:lats, :] + back
    out_gain_ref[...] = sum_ref[2 * lats + 2 : 2 * lats + 3, :] + gain_sum
    out_bias_ref[...] = sum_ref[2 * lats + 3 : 2 * lats + 4, :] + bias_sum


def rows_kernel(flag_ref, *refs, count, frames, items):
    part_refs, out_refs, held_ref = refs[:count], refs[count:-1], refs[-1]
    rows = held_ref.shape[1]
    column = 0
    for part_ref in part_refs:
        total = total_of([part_ref[k] for k in range(part_ref.shape[0])])
        for f in range(frames):
            held_ref[f, :, column : column + total.shape[1]] = total[f * rows : (f + 1) * rows]
        column += total.shape[1]
    for s, out_ref in enumerate(out_refs):
        block = held_ref[lax.rem(flag_ref[items + 1] + s, frames)]
        out_ref[...] = block.astype(out_ref.dtype)


def place_kernel(flag_ref, *refs, chunks, frames, items, groups):
    chunk_refs = refs[: chunks * frames]
    key_ref, value_ref, out_ref = refs[chunks * frames :]
    width = key_ref.shape[2] // (chunks * groups)
    for s in range(frames):
        source = lax.rem(flag_ref[items + 1] + (frames - s), frames)
        out_ref[source] = chunk_refs[s][:, 2 * groups * width :].astype(F32)
        for c in range(chunks):
            for g in range(groups):
                at = (c * groups + g) * width
                block = chunk_refs[c * frames + s][:, 2 * g * width : 2 * (g + 1) * width]
                block = block.astype(F32)
                key_ref[source, :, at : at + width] = block[:, :width]
                value_ref[source, :, at : at + width] = block[:, width:]


def body(
    media,
    cotangent,
    frame_count,
    frame_start,
    latents,
    time_embed,
    media_gain,
    media_bias,
    latent_gain,
    latent_bias,
    ffn_gain,
    ffn_bias,
    query_weight,
    key_weight,
    value_weight,
    out_weight,
    up_weight,
    down_weight,
):
    items = media.shape[0]
    patches = media.shape[2]
    width = media.shape[3]
    lats = latents.shape[0]
    frame_total = time_embed.shape[0]
    row_total = cotangent.shape[1]
    own = items * row_total
    head_size = width // HEADS
    half = width // CHUNKS
    chunk_heads = HEADS // CHUNKS
    group_width = GROUP * head_size
    groups = chunk_heads // GROUP
    stack = GROUP * lats
    tokens = items * patches
    all_tokens = tokens + lats
    shard = query_weight.shape[0]
    hidden_shard = down_weight.shape[0]
    item_size = lax.axis_size("items")
    frame_size = lax.axis_size("frames")
    plane = item_size * own
    item_index = lax.axis_index("items")
    slot = lax.axis_index("frames")
    row_base = slot * row_total
    params = pltpu.CompilerParams(vmem_limit_bytes=56 * 2**20)
    smem = pl.BlockSpec(memory_space=pltpu.SMEM)
    whole = pl.BlockSpec(memory_space=pltpu.VMEM)
    sizes = dict(items=items, head_size=head_size, heads=chunk_heads)

    def struct(shape, kind):
        return jax.ShapeDtypeStruct(shape, kind)

    def cost(micros):
        return pl.CostEstimate(
            flops=int(micros * 1.15e9), bytes_accessed=int(micros * 3.6e6), transcendentals=0
        )

    def column_blocks(x):
        return jnp.transpose(x.reshape(-1, item_size, shard), (1, 0, 2))

    def scatter_exchange(x, axis):
        return jnp.sum(lax.all_to_all(x, axis, 0, 0).astype(F32), axis=0)

    grad_out = cotangent.reshape(own, width)
    low_columns = own * width // shard
    joined, grad_low = pl.pallas_call(
        functools.partial(join_kernel, width=group_width),
        out_shape=[struct((shard, 2 * width + low_columns), BF16), struct((own, width), BF16)],
        cost_estimate=cost(2.5),
        compiler_params=params,
    )(key_weight, value_weight, grad_out)
    kv_full = lax.all_gather(joined, "items", axis=0, tiled=True)
    low_frames = jnp.stack(spread_on(grad_low, "frames"))

    lat_norm = layer_norm(latents, latent_gain, latent_bias).astype(BF16)
    lat_cols = lax.dynamic_slice_in_dim(lat_norm, item_index * shard, shard, 1)
    query_blocks = column_blocks(matmul(lat_cols, query_weight))
    query_cols = scatter_exchange(query_blocks, "items").astype(BF16)
    query_spread = jnp.broadcast_to(query_cols[None], (item_size, lats, shard))
    queries = jnp.transpose(lax.all_to_all(query_spread, "items", 0, 0), (1, 0, 2)).reshape(
        lats, width
    )

    counts = lax.dynamic_slice_in_dim(frame_count, item_index * items, items)
    starts = lax.dynamic_slice_in_dim(frame_start, item_index * items, items)
    offset = (slot - starts) % frame_total
    flags = jnp.concatenate(
        [
            (offset < counts).astype(jnp.int32),
            (slot == 0).astype(jnp.int32)[None],
            slot.astype(jnp.int32)[None],
            offset.astype(jnp.int32),
            item_index.astype(jnp.int32)[None],
        ]
    )
    picker = (offset[:, None] == jnp.arange(frame_total, dtype=jnp.int32)[None, :]).astype(F32)
    time_rows = jnp.dot(picker, time_embed, precision=HIGHEST, preferred_element_type=F32)
    flat_media = media.reshape(tokens, width)
    steps = tokens // lats
    all_rows = pl.pallas_call(
        functools.partial(norm_kernel, steps=steps, per_item=patches // lats),
        grid=(steps + 1,),
        in_specs=[
            pl.BlockSpec((lats, width), lambda i: (jnp.minimum(i, steps - 1), 0)),
            whole,
            whole,
            whole,
            whole,
        ],
        out_specs=pl.BlockSpec((lats, width), lambda i: (i, 0)),
        out_shape=struct((all_tokens, width), BF16),
        cost_estimate=cost(12),
        compiler_params=params,
    )(
        after(flat_media, query_blocks),
        time_rows,
        media_gain[None],
        media_bias[None],
        lat_norm,
    )
    out_full = lax.all_gather(after(out_weight, all_rows), "items", axis=0, tiled=True)

    core = item_index % 2
    rows_across = after(all_rows, query_cols).T.reshape(item_size // 2, 2, shard, all_tokens)
    send_rows, keep_rows = [
        jnp.concatenate(
            [
                lax.dynamic_slice(
                    rows_across, (k, which, 0, 0), (1, 1, shard, all_tokens)
                ).reshape(shard, all_tokens)
                for k in range(item_size // 2)
            ],
            0,
        )
        for which in (1 - core, core)
    ]
    boths, tops, messages = [], [], []
    for c in range(CHUNKS):

        def block_of(g, c=c):
            return (0, c * groups + g)

        if c:
            rows = after(all_rows, tops[-1])
        else:
            rows = after(all_rows, queries, send_rows, keep_rows)
        both = matmul(rows, kv_full[:, 2 * c * half : 2 * (c + 1) * half]).astype(BF16)
        top, *parts = pl.pallas_call(
            functools.partial(
                forward_kernel, patches=patches, scale=head_size**-0.5, **sizes
            ),
            grid=(groups,),
            in_specs=[
                smem,
                pl.BlockSpec((all_tokens, 2 * group_width), lambda g: (0, g)),
                pl.BlockSpec((lats, group_width), block_of),
            ],
            out_specs=[pl.BlockSpec((1, items, 8, stack), lambda g: (g, 0, 0, 0))]
            + [pl.BlockSpec((own, half + LANES), lambda g: (0, 0))] * frame_size,
            out_shape=[struct((groups, items, 8, stack), F32)]
            + [struct((own, half + LANES), BF16)] * frame_size,
            scratch_shapes=[
                pltpu.VMEM((items, lats, group_width), F32),
                pltpu.VMEM((items, lats, LANES), F32),
            ],
            cost_estimate=cost(7.8),
            compiler_params=params,
        )(flags, both, queries)
        boths.append(both)
        tops.append(top)
        messages += [p if s == 0 else send_on(p, "frames", s) for s, p in enumerate(parts)]
    up_slice = lax.all_to_all(after(up_weight, boths[0]), "items", 1, 0, tiled=True)
    low_all = lax.all_gather(after(low_frames, tops[1]), "items", axis=0).reshape(-1, width)

    base_rows = lax.dynamic_slice_in_dim(latents, row_base, row_total, 0)
    merged, mid_rows, ffn_in, logs, entropy_wide = pl.pallas_call(
        functools.partial(merge_kernel, chunks=CHUNKS, frames=frame_size, **sizes),
        out_shape=[
            struct((own, width), F32),
            struct((own, width), F32),
            struct((own, width), BF16),
            struct((CHUNKS, own, LANES), F32),
            struct((own, LANES), F32),
        ],
        cost_estimate=cost(6.3),
        compiler_params=params,
    )(*messages, base_rows, out_full, ffn_gain[None], ffn_bias[None])
    entropy = entropy_wide[:, 0].reshape(items, row_total)

    ffn_blocks = spread_across(ffn_in, "items")
    ffn_frames = spread_on(after(ffn_in, *ffn_blocks), "frames")
    result_part, *parts = pl.pallas_call(
        functools.partial(feed_kernel, devices=item_size, items=items),
        grid=(1,),
        in_specs=[smem]
        + [whole] * item_size
        + [
            pl.BlockSpec((width, low_columns), lambda i: (0, 2 * width // low_columns)),
            whole,
            whole,
        ],
        out_specs=[whole] * (1 + item_size),
        out_shape=[struct((item_size, own, width), BF16)]
        + [struct((own, width), BF16)] * item_size,
        scratch_shapes=[pltpu.VMEM((plane, width), BF16)] * 2,
        cost_estimate=cost(10),
        compiler_params=params,
    )(flags, *ffn_blocks, kv_full, up_slice, down_weight)
    grad_blocks = collect_across(parts, "items")
    grad_blocks[0] = after(grad_blocks[0], *ffn_frames)

    turn, grad_branch, grad_base, ffn_sums = pl.pallas_call(
        functools.partial(turn_kernel, devices=item_size, chunks=CHUNKS, **sizes),
        out_shape=[
            struct((own, width + CHUNKS * LANES), BF16),
            struct((own, 2 * width), BF16),
            struct((row_total, width), F32),
            struct((8, width), F32),
        ],
        cost_estimate=cost(7.6),
        compiler_params=params,
    )(*grad_blocks, mid_rows, grad_out, ffn_gain[None], merged, logs, out_full)
    turns = spread_on(turn, "frames")
    branch_plane = lax.all_gather(grad_branch, "items", axis=0, tiled=True)
    ffn_all = lax.all_gather(
        after(jnp.stack(ffn_frames), grad_branch), "items", axis=0
    ).reshape(-1, width)
    att_plane = lax.dynamic_slice_in_dim(
        branch_plane, width + item_index * shard, shard, 1
    )
    turns[0] = after(turns[0], low_all)

    chunk_grads, chunk_queries = [], []

    def weight_terms(c):
        send = matmul(send_rows, chunk_grads[c]).astype(BF16)
        received = send_across(send, "items", 1).reshape(-1, shard, 2 * half)
        keep = matmul(after(keep_rows, send), chunk_grads[c]).astype(BF16)
        return send, keep.reshape(-1, shard, 2 * half), received

    def chip_terms(keep, received):
        return (keep.astype(F32) + received.astype(F32)).astype(BF16)

    def exchange_chips(x):
        groups_of = [list(range(k, item_size, 2)) for k in range(2)]
        return lax.all_to_all(x, "items", 0, 0, axis_index_groups=groups_of)

    def frame_rows(ranges):
        rows = shard // frame_size
        columns = sum(x.shape[-1] for x in ranges)
        return pl.pallas_call(
            functools.partial(rows_kernel, count=len(ranges), frames=frame_size, items=items),
            in_specs=[smem] + [whole] * len(ranges),
            out_specs=[whole] * frame_size,
            out_shape=[struct((rows, columns), F32)]
            + [struct((rows, columns), BF16)] * (frame_size - 1),
            scratch_shapes=[pltpu.VMEM((frame_size, rows, columns), F32)],
            cost_estimate=cost(3.5),
            compiler_params=params,
        )(flags, *ranges)

    def send_rows_on(rows):
        return [rows[0]] + [send_on(p, "frames", s) for s, p in enumerate(rows) if s]

    for c in range(CHUNKS):

        def block_of(g, c=c):
            return (0, c * groups + g)

        chunk_grad, chunk_query = pl.pallas_call(
            functools.partial(
                backward_kernel, frames=frame_size, patches=patches, scale=head_size**-0.5, **sizes
            ),
            grid=(groups,),
            in_specs=[
                smem,
                pl.BlockSpec((all_tokens, 2 * group_width), lambda g: (0, g)),
                pl.BlockSpec((lats, group_width), block_of),
                pl.BlockSpec((1, items, 8, stack), lambda g: (g, 0, 0, 0)),
            ]
            + [pl.BlockSpec((own, group_width), block_of)] * frame_size
            + [pl.BlockSpec((own, LANES), lambda g, c=c: (0, width // LANES + c))] * frame_size,
            out_specs=[
                pl.BlockSpec((all_tokens, 2 * group_width), lambda g: (0, g)),
                pl.BlockSpec((lats, group_width), lambda g: (0, g)),
            ],
            out_shape=[
                struct((all_tokens, 2 * half), BF16),
                struct((lats, half), F32),
            ],
            scratch_shapes=[
                pltpu.VMEM((items, lats, group_width), F32),
                pltpu.VMEM((items, lats, LANES), F32),
            ],
            cost_estimate=cost(8),
            compiler_params=params,
        )(flags, after(boths[c], *held) if c else boths[c], queries, tops[c], *turns, *turns)
        chunk_grads.append(chunk_grad)
        chunk_queries.append(chunk_query)
        if c == 0:
            first_send, first_keep, first_received = weight_terms(0)
            held = (first_send,)
    first_terms = chip_terms(after(first_keep, chunk_grads[-1]), first_received)
    first_moved = exchange_chips(first_terms)

    last_block = pl.BlockSpec((lats, 2 * half), lambda i: (tokens // lats, 0))
    media_grad, media_sums, lat_product = pl.pallas_call(
        functools.partial(media_kernel, chunks=CHUNKS, items=items, frames=frame_total),
        grid=(items,),
        in_specs=[smem]
        + [pl.BlockSpec((patches, 2 * half), lambda i: (i, 0))] * CHUNKS
        + [last_block] * CHUNKS
        + [pl.BlockSpec((width, 2 * half), lambda i, c=c: (0, c)) for c in range(CHUNKS)]
        + [pl.BlockSpec((patches, width), lambda i: (i, 0)), whole, whole],
        out_specs=[
            pl.BlockSpec((patches, width), lambda i: (i, 0)),
            pl.BlockSpec((16, width), lambda i: (0, 0)),
            pl.BlockSpec((lats, width), lambda i: (0, 0)),
        ],
        out_shape=[
            struct((tokens, width), BF16),
            struct((16, width), F32),
            struct((lats, width), F32),
        ],
        cost_estimate=cost(21),
        compiler_params=params,
    )(
        flags,
        *chunk_grads[:-1],
        after(chunk_grads[-1], first_terms),
        *chunk_grads,
        *[kv_full] * CHUNKS,
        flat_media,
        time_rows,
        media_gain[None],
    )

    sum_rows = 2 * lats + 24
    sum_rows += -sum_rows % (8 * item_size)
    payload = pl.pallas_call(
        functools.partial(latent_kernel, chunks=CHUNKS, items=items),
        in_specs=[smem] + [whole] * (CHUNKS + 6),
        out_specs=whole,
        out_shape=struct((sum_rows, width), F32),
        cost_estimate=cost(3),
        compiler_params=params,
    )(
        flags,
        *chunk_queries,
        after(lat_product, first_moved),
        latents,
        latent_gain[None],
        grad_base,
        ffn_sums,
        media_sums,
    )
    payload_part = lax.psum_scatter(payload, "items", scatter_dimension=0, tiled=True)

    chunk_grads[-1] = after(chunk_grads[-1], payload)
    last_send, last_keep, last_received = weight_terms(CHUNKS - 1)
    last_terms = chip_terms(after(last_keep, first_moved), last_received)
    last_moved = exchange_chips(last_terms)
    out_part = transposed_left(att_plane, after(branch_plane, last_send)[:, :width])
    first_rows = frame_rows([after(first_moved, last_terms), out_part[None]])
    first_frames = send_rows_on(first_rows)
    all_plane = plane * frame_size
    block_rows = min(512, all_plane)
    row_block = pl.BlockSpec((block_rows, width), lambda i: (i, 0))
    hidden_block = pl.BlockSpec((block_rows, hidden_shard), lambda i: (i, 0))
    hidden, grad_up = pl.pallas_call(
        feed_back_kernel,
        grid=(all_plane // block_rows,),
        in_specs=[row_block, row_block, whole, whole],
        out_specs=[hidden_block, hidden_block],
        out_shape=[struct((all_plane, hidden_shard), BF16)] * 2,
        cost_estimate=cost(15),
        compiler_params=params,
    )(after(ffn_all, *first_rows), low_all, up_slice, down_weight)

    def outer(left, right, tile, kind):
        rows, columns = left.shape
        shape = (columns, right.shape[1])
        return pl.pallas_call(
            outer_kernel,
            grid=(columns // tile,),
            in_specs=[pl.BlockSpec((rows, tile), lambda i: (0, i)), whole],
            out_specs=pl.BlockSpec((tile, shape[1]), lambda i: (i, 0)),
            out_shape=struct(shape, kind),
            cost_estimate=cost(9.5),
            compiler_params=params,
        )(left, right)

    first_total = total_of(first_frames).astype(BF16)
    first_placed = spread_on(first_total, "frames")
    last_rows = frame_rows([after(last_moved, hidden)])
    last_frames = send_rows_on(last_rows)
    up_part = outer(ffn_all, after(grad_up, first_total, *last_rows), width // 4, BF16)
    result_pieces = lax.all_to_all(after(result_part, last_moved), "items", 0, 0)
    up_grad = lax.all_to_all(
        after(up_part, result_pieces), "items", 0, 1, tiled=True
    ).astype(F32)
    last_total = total_of(last_frames).astype(BF16)
    last_placed = spread_on(last_total, "frames")
    down_grad = outer(
        after(hidden, up_part, last_total, *first_placed),
        low_all,
        256 if hidden_shard % 256 == 0 else hidden_shard,
        F32,
    )
    placed = first_placed + last_placed
    payload_part = after(payload_part, down_grad)
    payload_others = spread_on(payload_part.astype(BF16), "frames")[1:]
    sums = lax.all_gather(
        total_of([payload_part] + payload_others), "items", axis=0, tiled=True
    )
    query_low = sums[lats : 2 * lats].astype(BF16)
    query_grad = transposed_left(lat_cols, query_low)
    norm_cols = after(transposed_right(query_low, query_weight), *last_placed)
    latents_grad, lat_gain, lat_bias = pl.pallas_call(
        functools.partial(query_norm_kernel, devices=item_size, items=items),
        in_specs=[smem] + [whole] * (item_size + 3),
        out_specs=[whole] * 3,
        out_shape=[struct((lats, width), F32), struct((1, width), F32), struct((1, width), F32)],
        scratch_shapes=[pltpu.VMEM((item_size, lats, shard), F32)],
        cost_estimate=cost(3),
        compiler_params=params,
    )(flags, *spread_across(norm_cols, "items"), latents, latent_gain[None], sums)
    at = 2 * lats
    column_sums = lax.dynamic_slice_in_dim(
        sums[at + 8 : at + 24], item_index * shard, shard, 1
    )

    key_grad, value_grad, out_grad = pl.pallas_call(
        functools.partial(
            place_kernel, chunks=CHUNKS, frames=frame_size, items=items, groups=groups
        ),
        in_specs=[smem] + [whole] * len(placed),
        out_specs=[whole] * 3,
        out_shape=[struct((frame_size, shard // frame_size, width), F32)] * 3,
        cost_estimate=cost(3.4),
        compiler_params=params,
    )(flags, *placed)

    result = mid_rows + total_of([result_pieces[d] for d in range(item_size)])
    return (
        result.reshape(items, row_total, width),
        entropy,
        media_grad.reshape(media.shape),
        latents_grad,
        column_sums[:frame_total],
        column_sums[8],
        column_sums[9],
        lat_gain.reshape(width),
        lat_bias.reshape(width),
        sums[at],
        sums[at + 1],
        query_grad,
        key_grad.reshape(shard, width),
        value_grad.reshape(shard, width),
        out_grad.reshape(shard, width),
        up_grad,
        down_grad,
    )


def solution(mesh):
    return jax.shard_map(
        body,
        mesh=mesh,
        in_specs=(
            P("items", "frames", None, None),
            P("items", "frames", None),
            P(),
            P(),
            P(),
            P(),
            P(),
            P(),
            P(),
            P(),
            P(),
            P(),
            P("items", None),
            P("items", None),
            P("items", None),
            P("items", None),
            P("items", None),
            P("items", None),
        ),
        out_specs=(
            P("items", "frames", None),
            P("items", "frames"),
            P("items", "frames", None, None),
            P(),
            P(None, "items"),
            P("items"),
            P("items"),
            P(),
            P(),
            P(),
            P(),
            P("items", None),
            P("items", None),
            P("items", None),
            P("items", None),
            P("items", None),
            P("items", None),
        ),
        check_vma=False,
    )
```

```python
import functools
import math

import jax
import jax.numpy as jnp
from jax import lax
from jax.experimental import pallas as pl
from jax.experimental.pallas import tpu as pltpu
from jax.sharding import PartitionSpec as P

HEADS = 16
GROUP = 4
CHUNKS = 2
LANES = 128
EPSILON = 1e-05
MASKED = -1e30
F32 = jnp.float32
BF16 = jnp.bfloat16
HIGHEST = lax.Precision.HIGHEST


def layer_norm(inputs, norm_gain, norm_bias):
    center = inputs - jnp.mean(inputs, axis=-1, keepdims=True)
    spread = jnp.mean(center * center, axis=-1, keepdims=True)
    return center * lax.rsqrt(spread + EPSILON) * norm_gain + norm_bias


def matmul(left_side, right_side):
    return jnp.dot(left_side, right_side, preferred_element_type=F32)


def transposed_left(left_side, right_side):
    return lax.dot_general(
        left_side, right_side, (((0,), (0,)), ((), ())), preferred_element_type=F32
    )


def transposed_right(left_side, right_side):
    return lax.dot_general(
        left_side, right_side, (((1,), (1,)), ((), ())), preferred_element_type=F32
    )


def send_on(x, axis, step):
    size = lax.axis_size(axis)
    return lax.ppermute(x, axis, [(i, (i + step) % size) for i in range(size)])


def send_across(x, axis, distance):
    return lax.ppermute(x, axis, [(i, i ^ distance) for i in range(lax.axis_size(axis))])


def spread_on(x, axis):
    return [x] + [send_on(x, axis, s) for s in range(1, lax.axis_size(axis))]


def spread_across(x, axis):
    chips = [x] + [send_across(x, axis, d) for d in range(2, lax.axis_size(axis), 2)]
    return [b for block in chips for b in (block, send_across(block, axis, 1))]


def collect_across(pieces, axis):
    return [pieces[0]] + [send_across(p, axis, d) for d, p in enumerate(pieces) if d]


def total_of(pieces):
    return functools.reduce(jnp.add, [p.astype(F32) for p in pieces])


def after(x, *earlier):
    return lax.optimization_barrier((x,) + earlier)[0]


def split_terms(x):
    high = x.astype(BF16)
    rest = x - high.astype(F32)
    middle = rest.astype(BF16)
    return high, middle, (rest - middle.astype(F32)).astype(BF16)


def iota(shape, dim):
    return lax.broadcasted_iota(jnp.int32, shape, dim)


def head_masks(rows, width, head_size):
    lane = iota((rows, width), 1)
    return [
        jnp.logical_and(lane >= h * head_size, lane < (h + 1) * head_size)
        for h in range(width // head_size)
    ]


def spread_heads(block, masks):
    return jnp.concatenate([jnp.where(m, block, jnp.zeros_like(block)) for m in masks], 0)


def collect_heads(block, masks):
    rows = block.shape[0] // len(masks)
    total = jnp.where(masks[0], block[:rows], 0.0)
    for h in range(1, len(masks)):
        total = total + jnp.where(masks[h], block[h * rows : (h + 1) * rows], 0.0)
    return total


def head_expand(width, head_size):
    row, column = iota((LANES, width), 0), iota((LANES, width), 1)
    return jnp.logical_and(column >= row * head_size, column < (row + 1) * head_size).astype(F32)


def live_rows(flag_ref, item, items, patches, lats, columns):
    row = iota((patches + lats, columns), 0)
    media = jnp.logical_and(row < patches, flag_ref[item] > 0)
    return jnp.logical_or(media, jnp.logical_and(row >= patches, flag_ref[items] > 0))


def pack_shape(own, shard, width):
    unit = math.gcd(own, shard)
    return unit, width * unit // shard


def join_kernel(key_ref, value_ref, cotangent_ref, out_ref, low_ref, *, width):
    for g in range(key_ref.shape[1] // width):
        columns = slice(g * width, (g + 1) * width)
        out_ref[:, 2 * g * width : (2 * g + 1) * width] = key_ref[:, columns]
        out_ref[:, (2 * g + 1) * width : (2 * g + 2) * width] = value_ref[:, columns]
    low = cotangent_ref[...].astype(BF16)
    low_ref[...] = low
    own, span = low.shape
    unit, piece = pack_shape(own, out_ref.shape[0], span)
    for a in range(own // unit):
        for b in range(span // piece):
            at = 2 * span + a * piece
            out_ref[b * unit : (b + 1) * unit, at : at + piece] = low[
                a * unit : (a + 1) * unit, b * piece : (b + 1) * piece
            ]


def norm_kernel(media_ref, time_ref, gain_ref, bias_ref, lat_ref, out_ref, *, steps, per_item):
    step = pl.program_id(0)

    @pl.when(step < steps)
    def _():
        rows = media_ref[...].astype(F32) + time_ref[pl.ds(step // per_item, 1), :]
        out_ref[...] = layer_norm(rows, gain_ref[...], bias_ref[...]).astype(BF16)

    @pl.when(step == steps)
    def _():
        out_ref[...] = lat_ref[...]


def forward_kernel(
    flag_ref, both_ref, query_ref, top_ref, *refs, items, patches, scale, head_size, heads,
):
    message_refs, (part_ref, mark_ref) = refs[:-2], refs[-2:]
    lats, width = query_ref.shape
    frames = len(message_refs)
    own = message_refs[0].shape[0]
    row_total = own // items
    masks = head_masks(lats, width, head_size)
    queries = spread_heads(query_ref[...].astype(F32), masks).astype(BF16)
    base = items * patches
    lat_both = both_ref[base : base + lats, :]
    group = pl.program_id(0)
    term, lane = iota((16, GROUP * LANES), 0), iota((16, GROUP * LANES), 1)
    place = jnp.logical_and(
        lane % LANES == term * heads + group * GROUP + lane // LANES, term < 9
    ).astype(BF16)
    for i in range(items):
        both = jnp.concatenate([both_ref[i * patches : (i + 1) * patches, :], lat_both], 0)
        live = live_rows(flag_ref, i, items, patches, lats, queries.shape[0])
        scores = scale * transposed_right(both[:, :width], queries)
        masked = jnp.where(live, scores, MASKED)
        top = jnp.max(masked, axis=0, keepdims=True)
        block_exp = jnp.where(live, jnp.exp(masked - top), 0.0)
        total = jnp.sum(block_exp, axis=0, keepdims=True)
        moment = jnp.sum(block_exp * scores, axis=0, keepdims=True)
        part = transposed_left(block_exp.astype(BF16), both[:, width:])
        part_ref[i] = collect_heads(part, masks)
        top_ref[0, i] = jnp.broadcast_to(top, top_ref.shape[2:])
        terms = jnp.concatenate(
            [t.astype(F32) for x in (top, total, moment) for t in split_terms(x)]
            + [jnp.zeros((7, top.shape[1]), F32)],
            0,
        ).astype(BF16)
        wide = transposed_left(terms, place)
        mark = wide[:lats, :LANES]
        for h in range(1, GROUP):
            mark = mark + wide[h * lats : (h + 1) * lats, h * LANES : (h + 1) * LANES]
        mark_ref[i] = mark

    end = message_refs[0].shape[1] - LANES
    for s, message_ref in enumerate(message_refs):
        start = pl.multiple_of(lax.rem(flag_ref[items + 1] + s, frames) * row_total, row_total)
        rows = pl.ds(start, row_total)
        block = jnp.concatenate([part_ref[i, rows, :] for i in range(items)], 0).astype(BF16)
        mark = jnp.concatenate([mark_ref[i, rows, :] for i in range(items)], 0).astype(BF16)
        for g in range(end // width):

            @pl.when(group == g)
            def _():
                message_ref[:, g * width : (g + 1) * width] = block
                if g == 0:
                    message_ref[:, end:] = mark
                else:
                    message_ref[:, end:] = message_ref[:, end:] + mark


def merge_kernel(*refs, chunks, frames, items, head_size, heads):
    message_refs = refs[: chunks * frames]
    base_ref, weight_ref, gain_ref, bias_ref = refs[chunks * frames : chunks * frames + 4]
    merged_ref, mid_ref, ffn_ref, log_ref, entropy_ref = refs[chunks * frames + 4 :]
    own, columns = message_refs[0].shape
    half = columns - LANES
    lane, column = iota((LANES, 3 * LANES), 0), iota((LANES, 3 * LANES), 1)
    gather = jnp.logical_and(
        jnp.logical_and(lane // heads // 3 == column // LANES, lane % heads == column % LANES),
        lane < 9 * heads,
    ).astype(BF16)
    expand = head_expand(half, head_size)
    live = iota((own, LANES), 1) < heads
    spread = jnp.zeros((own, LANES), F32)
    for c in range(chunks):
        sources = message_refs[c * frames : (c + 1) * frames]
        stats = [matmul(x[:, half:], gather) for x in sources]
        tops = [x[:, :LANES] for x in stats]
        peak = functools.reduce(jnp.maximum, tops)
        factors = [jnp.exp(t - peak) for t in tops]
        whole = sum(f * x[:, LANES : 2 * LANES] for f, x in zip(factors, stats))
        moment = sum(f * x[:, 2 * LANES :] for f, x in zip(factors, stats))
        whole = jnp.where(live, whole, 1.0)
        log_total = jnp.where(live, peak + jnp.log(whole), 0.0)
        log_ref[c] = log_total
        spread = spread + jnp.where(live, log_total - moment / whole, 0.0)
        merged = jnp.zeros((own, half), F32)
        for x, factor in zip(sources, factors):
            share = jnp.where(live, factor / whole, 0.0)
            wide = jnp.dot(share, expand, precision=HIGHEST, preferred_element_type=F32)
            merged = merged + x[:, :half].astype(F32) * wide
        merged_ref[:, c * half : (c + 1) * half] = merged
    entropy_ref[...] = jnp.broadcast_to(
        jnp.sum(spread, axis=1, keepdims=True) * (1.0 / HEADS), entropy_ref.shape
    )
    base = jnp.concatenate([base_ref[...]] * items, 0)
    mid = base + matmul(merged_ref[...].astype(BF16), weight_ref[...])
    mid_ref[...] = mid
    ffn_ref[...] = layer_norm(mid, gain_ref[...], bias_ref[...]).astype(BF16)


def gelu_parts(x):
    share = 0.5 * (1.0 + lax.erf(x * (0.5**0.5)))
    slope = share + x * jnp.exp(-0.5 * x * x) * ((2.0 * jnp.pi) ** -0.5)
    return x * share, slope


def feed_kernel(flag_ref, *refs, devices, items):
    row_refs = refs[:devices]
    low_ref, up_ref, down_ref, result_ref = refs[devices : devices + 4]
    grad_refs, (plane_ref, plane_low_ref) = refs[devices + 4 : -2], refs[-2:]
    own, width = row_refs[0].shape
    shard = low_ref.shape[0] // devices
    unit, piece = pack_shape(own, shard, width)
    me = flag_ref[2 * items + 2]
    for d in range(devices):
        plane_ref[d * own : (d + 1) * own, :] = row_refs[d][...]
        source = jnp.bitwise_xor(me, d) * shard
        for a in range(own // unit):
            rows = slice(d * own + a * unit, d * own + (a + 1) * unit)
            for b in range(shard // unit):
                start = pl.multiple_of(source + b * unit, unit)
                plane_low_ref[rows, b * piece : (b + 1) * piece] = low_ref[
                    pl.ds(start, unit), a * piece : (a + 1) * piece
                ]
    upward = matmul(plane_ref[...], up_ref[...])
    hidden, slope = gelu_parts(upward)
    grad_up = (slope * transposed_right(plane_low_ref[...], down_ref[...])).astype(BF16)
    grad = transposed_right(grad_up, up_ref[...]).astype(BF16)
    result = matmul(hidden.astype(BF16), down_ref[...]).astype(BF16)
    for d in range(devices):
        grad_refs[d][...] = grad[d * own : (d + 1) * own, :]
        result_ref[jnp.bitwise_xor(me, d)] = result[d * own : (d + 1) * own, :]


def feed_back_kernel(row_ref, low_ref, up_ref, down_ref, hidden_ref, grad_ref):
    hidden, slope = gelu_parts(matmul(row_ref[...], up_ref[...]))
    hidden_ref[...] = hidden.astype(BF16)
    grad_ref[...] = (slope * transposed_right(low_ref[...], down_ref[...])).astype(BF16)


def outer_kernel(left_ref, right_ref, out_ref):
    out_ref[...] = transposed_left(left_ref[...], right_ref[...]).astype(out_ref.dtype)


def norm_backward(rows, gain, gradient):
    center = rows - jnp.mean(rows, axis=1, keepdims=True)
    rate = lax.rsqrt(jnp.mean(center * center, axis=1, keepdims=True) + EPSILON)
    unit = center * rate
    scaled = gradient * gain
    inner = scaled - jnp.mean(scaled, axis=1, keepdims=True)
    back = rate * (inner - unit * jnp.mean(scaled * unit, axis=1, keepdims=True))
    return (
        back,
        jnp.sum(gradient * unit, axis=0, keepdims=True),
        jnp.sum(gradient, axis=0, keepdims=True),
    )


def turn_kernel(*refs, devices, items, chunks, head_size, heads):
    part_refs = refs[:devices]
    mid_ref, cotangent_ref, gain_ref, merged_ref, log_ref, weight_ref = refs[
        devices : devices + 6
    ]
    message_ref, branch_ref, base_ref, sums_ref = refs[devices + 6 :]
    own, width = mid_ref.shape
    half = width // chunks
    gradient = total_of([x[...] for x in part_refs])
    back, gain_sum, bias_sum = norm_backward(mid_ref[...], gain_ref[...], gradient)
    grad_mid = cotangent_ref[...] + back
    sums_ref[...] = jnp.zeros(sums_ref.shape, F32)
    sums_ref[0:1, :] = gain_sum
    sums_ref[1:2, :] = bias_sum
    row_total = own // items
    base_ref[...] = total_of(
        [grad_mid[i * row_total : (i + 1) * row_total] for i in range(items)]
    )
    branch = grad_mid.astype(BF16)
    branch_ref[:, :width] = branch
    branch_ref[:, width:] = merged_ref[...].astype(BF16)
    grad_att = transposed_right(branch, weight_ref[...]).astype(BF16)
    expand = head_expand(half, head_size)
    lane, column = iota((6 * LANES, LANES), 0), iota((6 * LANES, LANES), 1)
    place = jnp.logical_and(
        lane % LANES < heads, column == (lane // LANES) * heads + lane % LANES
    ).astype(BF16)
    message_ref[:, :width] = grad_att
    for c in range(chunks):
        columns = slice(c * half, (c + 1) * half)
        delta = lax.dot_general(
            merged_ref[:, columns] * grad_att[:, columns].astype(F32),
            expand,
            (((1,), (1,)), ((), ())),
            precision=HIGHEST,
            preferred_element_type=F32,
        )
        terms = jnp.concatenate([t for x in (log_ref[c], delta) for t in split_terms(x)], 1)
        message_ref[:, width + c * LANES : width + (c + 1) * LANES] = matmul(
            terms, place
        ).astype(BF16)


def backward_kernel(
    *refs, frames, items, patches, scale, head_size, heads,
):
    flag_ref, both_ref, query_ref, top_ref = refs[:4]
    grad_refs = refs[4 : 4 + frames]
    mark_refs = refs[4 + frames : 4 + 2 * frames]
    out_ref, sum_ref, held_ref, note_ref = refs[4 + 2 * frames :]
    lats, width = query_ref.shape
    own = grad_refs[0].shape[0]
    row_total = own // items
    base = items * patches
    for s in range(frames):
        source = lax.rem(flag_ref[items + 1] + (frames - s), frames)
        rows = pl.ds(pl.multiple_of(source * row_total, row_total), row_total)
        block = grad_refs[s][...].astype(F32)
        mark = mark_refs[s][...].astype(F32)
        for i in range(items):
            held_ref[i, rows, :] = block[i * row_total : (i + 1) * row_total]
            note_ref[i, rows, :] = mark[i * row_total : (i + 1) * row_total]
    masks = head_masks(lats, width, head_size)
    queries = spread_heads(query_ref[...].astype(F32), masks).astype(BF16)
    lat_both = both_ref[base : base + lats, :]
    row, lane = iota((GROUP * 8, LANES), 0), iota((GROUP * 8, LANES), 1)
    pick = jnp.logical_and(
        jnp.logical_and(
            lane // heads // 3 == row % 8,
            lane % heads == pl.program_id(0) * GROUP + row // 8,
        ),
        lane < 6 * heads,
    ).astype(BF16)
    grad_query = jnp.zeros((queries.shape[0], width), F32)
    lat_grad_key = jnp.zeros((lats, width), F32)
    lat_grad_value = jnp.zeros((lats, width), F32)
    for i in range(items):
        rows = slice(i * patches, (i + 1) * patches)
        stats = transposed_right(pick, note_ref[i].astype(BF16))
        stats = jnp.concatenate([stats[h * 8 : (h + 1) * 8] for h in range(GROUP)], 1)
        log_total = stats[0:1]
        delta = stats[1:2]
        top = top_ref[0, i, 0:1, :]
        rescale = jnp.exp(top - log_total)
        both = jnp.concatenate([both_ref[rows, :], lat_both], 0)
        keys, values = both[:, :width], both[:, width:]
        grads = spread_heads(held_ref[i], masks).astype(BF16)
        live = live_rows(flag_ref, i, items, patches, lats, queries.shape[0])
        masked = jnp.where(live, scale * transposed_right(keys, queries), MASKED)
        probs = jnp.where(live, jnp.exp(masked - log_total), 0.0)
        block_exp = jnp.where(live, jnp.exp(masked - top), 0.0)
        weights = (block_exp.astype(BF16).astype(F32) * rescale).astype(BF16)
        grad_scores = (probs * (transposed_right(values, grads) - delta)).astype(BF16)
        grad_key = scale * matmul(grad_scores, queries)
        grad_value = matmul(weights, grads)
        out_ref[rows, :width] = grad_key[:patches].astype(BF16)
        out_ref[rows, width:] = grad_value[:patches].astype(BF16)
        grad_query = grad_query + transposed_left(grad_scores, keys)
        lat_grad_key = lat_grad_key + grad_key[patches:]
        lat_grad_value = lat_grad_value + grad_value[patches:]
    out_ref[base : base + lats, :width] = lat_grad_key.astype(BF16)
    out_ref[base : base + lats, width:] = lat_grad_value.astype(BF16)
    sum_ref[...] = scale * collect_heads(grad_query, masks)


def media_kernel(flag_ref, *refs, chunks, items, frames):
    grad_refs, lat_refs, weight_refs = [
        refs[k * chunks : (k + 1) * chunks] for k in range(3)
    ]
    media_ref, time_ref, gain_ref, out_ref, sums_ref, product_ref = refs[3 * chunks :]
    item = pl.program_id(0)

    @pl.when(item == 0)
    def _():
        sums_ref[...] = jnp.zeros(sums_ref.shape, F32)
        product_ref[...] = functools.reduce(
            jnp.add, [transposed_right(g[...], w[...]) for g, w in zip(lat_refs, weight_refs)]
        )

    gradient = functools.reduce(
        jnp.add, [transposed_right(g[...], w[...]) for g, w in zip(grad_refs, weight_refs)]
    )
    inputs = media_ref[...].astype(F32) + time_ref[pl.ds(item, 1), :]
    back, gain_sum, bias_sum = norm_backward(inputs, gain_ref[...], gradient)
    out_ref[...] = back.astype(BF16)
    place = iota((frames, 1), 0) == flag_ref[items + 2 + item]
    sums_ref[0:frames, :] += jnp.where(place, jnp.sum(back, axis=0, keepdims=True), 0.0)
    sums_ref[8:9, :] += gain_sum
    sums_ref[9:10, :] += bias_sum


def latent_kernel(flag_ref, *refs, chunks, items):
    query_refs = refs[:chunks]
    (
        product_ref, latent_ref, gain_ref, base_ref, ffn_ref, media_ref, out_ref,
    ) = refs[chunks:]
    lats, width = latent_ref.shape
    half = width // chunks
    gradient = product_ref[...]
    for c in range(chunks):
        out_ref[lats : 2 * lats, c * half : (c + 1) * half] = query_refs[c][...]
    back, gain_sum, bias_sum = norm_backward(latent_ref[...], gain_ref[...], gradient)
    out_ref[:lats, :] = back
    row_total = base_ref.shape[0]
    start = pl.multiple_of(flag_ref[items + 1] * row_total, row_total)
    out_ref[pl.ds(start, row_total), :] += base_ref[...]
    at = 2 * lats
    out_ref[at : at + 8, :] = ffn_ref[...]
    out_ref[at + 2 : at + 3, :] = gain_sum
    out_ref[at + 3 : at + 4, :] = bias_sum
    out_ref[at + 8 : at + 24, :] = media_ref[...]
    out_ref[at + 24 :, :] = jnp.zeros((out_ref.shape[0] - at - 24, width), F32)


def query_norm_kernel(flag_ref, *refs, devices, items):
    column_refs = refs[:devices]
    latent_ref, gain_ref, sum_ref, out_ref, out_gain_ref, out_bias_ref, held_ref = refs[devices:]
    for d in range(devices):
        held_ref[jnp.bitwise_xor(flag_ref[2 * items + 2], d)] = column_refs[d][...]
    gradient = jnp.concatenate([held_ref[k] for k in range(devices)], 1)
    back, gain_sum, bias_sum = norm_backward(latent_ref[...], gain_ref[...], gradient)
    lats = latent_ref.shape[0]
    out_ref[...] = sum_ref[:lats, :] + back
    out_gain_ref[...] = sum_ref[2 * lats + 2 : 2 * lats + 3, :] + gain_sum
    out_bias_ref[...] = sum_ref[2 * lats + 3 : 2 * lats + 4, :] + bias_sum


def rows_kernel(flag_ref, *refs, count, frames, items):
    part_refs, out_refs, held_ref = refs[:count], refs[count:-1], refs[-1]
    rows = held_ref.shape[1]
    column = 0
    for part_ref in part_refs:
        total = total_of([part_ref[k] for k in range(part_ref.shape[0])])
        for f in range(frames):
            held_ref[f, :, column : column + total.shape[1]] = total[f * rows : (f + 1) * rows]
        column += total.shape[1]
    for s, out_ref in enumerate(out_refs):
        block = held_ref[lax.rem(flag_ref[items + 1] + s, frames)]
        out_ref[...] = block.astype(out_ref.dtype)


def place_kernel(flag_ref, *refs, chunks, frames, items, groups):
    chunk_refs = refs[: chunks * frames]
    key_ref, value_ref, out_ref = refs[chunks * frames :]
    width = key_ref.shape[2] // (chunks * groups)
    for s in range(frames):
        source = lax.rem(flag_ref[items + 1] + (frames - s), frames)
        out_ref[source] = chunk_refs[s][:, 2 * groups * width :].astype(F32)
        for c in range(chunks):
            for g in range(groups):
                at = (c * groups + g) * width
                block = chunk_refs[c * frames + s][:, 2 * g * width : 2 * (g + 1) * width]
                block = block.astype(F32)
                key_ref[source, :, at : at + width] = block[:, :width]
                value_ref[source, :, at : at + width] = block[:, width:]


def body(
    media,
    cotangent,
    frame_count,
    frame_start,
    latents,
    time_embed,
    media_gain,
    media_bias,
    latent_gain,
    latent_bias,
    ffn_gain,
    ffn_bias,
    query_weight,
    key_weight,
    value_weight,
    out_weight,
    up_weight,
    down_weight,
):
    items = media.shape[0]
    patches = media.shape[2]
    width = media.shape[3]
    lats = latents.shape[0]
    frame_total = time_embed.shape[0]
    row_total = cotangent.shape[1]
    own = items * row_total
    head_size = width // HEADS
    half = width // CHUNKS
    chunk_heads = HEADS // CHUNKS
    group_width = GROUP * head_size
    groups = chunk_heads // GROUP
    stack = GROUP * lats
    tokens = items * patches
    all_tokens = tokens + lats
    shard = query_weight.shape[0]
    hidden_shard = down_weight.shape[0]
    item_size = lax.axis_size("items")
    frame_size = lax.axis_size("frames")
    plane = item_size * own
    item_index = lax.axis_index("items")
    slot = lax.axis_index("frames")
    row_base = slot * row_total
    params = pltpu.CompilerParams(vmem_limit_bytes=56 * 2**20)
    smem = pl.BlockSpec(memory_space=pltpu.SMEM)
    whole = pl.BlockSpec(memory_space=pltpu.VMEM)
    sizes = dict(items=items, head_size=head_size, heads=chunk_heads)

    def struct(shape, kind):
        return jax.ShapeDtypeStruct(shape, kind)

    def cost(micros):
        return pl.CostEstimate(
            flops=int(micros * 1.15e9), bytes_accessed=int(micros * 3.6e6), transcendentals=0
        )

    def column_blocks(x):
        return jnp.transpose(x.reshape(-1, item_size, shard), (1, 0, 2))

    def scatter_exchange(x, axis):
        return jnp.sum(lax.all_to_all(x, axis, 0, 0).astype(F32), axis=0)

    grad_out = cotangent.reshape(own, width)
    low_columns = own * width // shard
    joined, grad_low = pl.pallas_call(
        functools.partial(join_kernel, width=group_width),
        out_shape=[struct((shard, 2 * width + low_columns), BF16), struct((own, width), BF16)],
        cost_estimate=cost(2.5),
        compiler_params=params,
    )(key_weight, value_weight, grad_out)
    kv_full = lax.all_gather(joined, "items", axis=0, tiled=True)
    low_frames = jnp.stack(spread_on(grad_low, "frames"))

    lat_norm = layer_norm(latents, latent_gain, latent_bias).astype(BF16)
    lat_cols = lax.dynamic_slice_in_dim(lat_norm, item_index * shard, shard, 1)
    query_blocks = column_blocks(matmul(lat_cols, query_weight))
    query_cols = scatter_exchange(query_blocks, "items").astype(BF16)
    query_spread = jnp.broadcast_to(query_cols[None], (item_size, lats, shard))
    queries = jnp.transpose(lax.all_to_all(query_spread, "items", 0, 0), (1, 0, 2)).reshape(
        lats, width
    )

    counts = lax.dynamic_slice_in_dim(frame_count, item_index * items, items)
    starts = lax.dynamic_slice_in_dim(frame_start, item_index * items, items)
    offset = (slot - starts) % frame_total
    flags = jnp.concatenate(
        [
            (offset < counts).astype(jnp.int32),
            (slot == 0).astype(jnp.int32)[None],
            slot.astype(jnp.int32)[None],
            offset.astype(jnp.int32),
            item_index.astype(jnp.int32)[None],
        ]
    )
    picker = (offset[:, None] == jnp.arange(frame_total, dtype=jnp.int32)[None, :]).astype(F32)
    time_rows = jnp.dot(picker, time_embed, precision=HIGHEST, preferred_element_type=F32)
    flat_media = media.reshape(tokens, width)
    steps = tokens // lats
    all_rows = pl.pallas_call(
        functools.partial(norm_kernel, steps=steps, per_item=patches // lats),
        grid=(steps + 1,),
        in_specs=[
            pl.BlockSpec((lats, width), lambda i: (jnp.minimum(i, steps - 1), 0)),
            whole,
            whole,
            whole,
            whole,
        ],
        out_specs=pl.BlockSpec((lats, width), lambda i: (i, 0)),
        out_shape=struct((all_tokens, width), BF16),
        cost_estimate=cost(12),
        compiler_params=params,
    )(
        after(flat_media, query_blocks),
        time_rows,
        media_gain[None],
        media_bias[None],
        lat_norm,
    )
    out_full = lax.all_gather(after(out_weight, all_rows), "items", axis=0, tiled=True)

    core = item_index % 2
    rows_across = after(all_rows, query_cols).T.reshape(item_size // 2, 2, shard, all_tokens)
    send_rows, keep_rows = [
        jnp.concatenate(
            [
                lax.dynamic_slice(
                    rows_across, (k, which, 0, 0), (1, 1, shard, all_tokens)
                ).reshape(shard, all_tokens)
                for k in range(item_size // 2)
            ],
            0,
        )
        for which in (1 - core, core)
    ]
    boths, tops, messages = [], [], []
    for c in range(CHUNKS):

        def block_of(g, c=c):
            return (0, c * groups + g)

        if c:
            rows = after(all_rows, tops[-1])
        else:
            rows = after(all_rows, queries, send_rows, keep_rows)
        both = matmul(rows, kv_full[:, 2 * c * half : 2 * (c + 1) * half]).astype(BF16)
        top, *parts = pl.pallas_call(
            functools.partial(
                forward_kernel, patches=patches, scale=head_size**-0.5, **sizes
            ),
            grid=(groups,),
            in_specs=[
                smem,
                pl.BlockSpec((all_tokens, 2 * group_width), lambda g: (0, g)),
                pl.BlockSpec((lats, group_width), block_of),
            ],
            out_specs=[pl.BlockSpec((1, items, 8, stack), lambda g: (g, 0, 0, 0))]
            + [pl.BlockSpec((own, half + LANES), lambda g: (0, 0))] * frame_size,
            out_shape=[struct((groups, items, 8, stack), F32)]
            + [struct((own, half + LANES), BF16)] * frame_size,
            scratch_shapes=[
                pltpu.VMEM((items, lats, group_width), F32),
                pltpu.VMEM((items, lats, LANES), F32),
            ],
            cost_estimate=cost(7.8),
            compiler_params=params,
        )(flags, both, queries)
        boths.append(both)
        tops.append(top)
        messages += [p if s == 0 else send_on(p, "frames", s) for s, p in enumerate(parts)]
    up_slice = lax.all_to_all(after(up_weight, boths[0]), "items", 1, 0, tiled=True)
    low_all = lax.all_gather(after(low_frames, tops[1]), "items", axis=0).reshape(-1, width)

    base_rows = lax.dynamic_slice_in_dim(latents, row_base, row_total, 0)
    merged, mid_rows, ffn_in, logs, entropy_wide = pl.pallas_call(
        functools.partial(merge_kernel, chunks=CHUNKS, frames=frame_size, **sizes),
        out_shape=[
            struct((own, width), F32),
            struct((own, width), F32),
            struct((own, width), BF16),
            struct((CHUNKS, own, LANES), F32),
            struct((own, LANES), F32),
        ],
        cost_estimate=cost(6.3),
        compiler_params=params,
    )(*messages, base_rows, out_full, ffn_gain[None], ffn_bias[None])
    entropy = entropy_wide[:, 0].reshape(items, row_total)

    ffn_blocks = spread_across(ffn_in, "items")
    ffn_frames = spread_on(after(ffn_in, *ffn_blocks), "frames")
    result_part, *parts = pl.pallas_call(
        functools.partial(feed_kernel, devices=item_size, items=items),
        grid=(1,),
        in_specs=[smem]
        + [whole] * item_size
        + [
            pl.BlockSpec((width, low_columns), lambda i: (0, 2 * width // low_columns)),
            whole,
            whole,
        ],
        out_specs=[whole] * (1 + item_size),
        out_shape=[struct((item_size, own, width), BF16)]
        + [struct((own, width), BF16)] * item_size,
        scratch_shapes=[pltpu.VMEM((plane, width), BF16)] * 2,
        cost_estimate=cost(10),
        compiler_params=params,
    )(flags, *ffn_blocks, kv_full, up_slice, down_weight)
    grad_blocks = collect_across(parts, "items")
    grad_blocks[0] = after(grad_blocks[0], *ffn_frames)

    turn, grad_branch, grad_base, ffn_sums = pl.pallas_call(
        functools.partial(turn_kernel, devices=item_size, chunks=CHUNKS, **sizes),
        out_shape=[
            struct((own, width + CHUNKS * LANES), BF16),
            struct((own, 2 * width), BF16),
            struct((row_total, width), F32),
            struct((8, width), F32),
        ],
        cost_estimate=cost(7.6),
        compiler_params=params,
    )(*grad_blocks, mid_rows, grad_out, ffn_gain[None], merged, logs, out_full)
    turns = spread_on(turn, "frames")
    branch_plane = lax.all_gather(grad_branch, "items", axis=0, tiled=True)
    ffn_all = lax.all_gather(
        after(jnp.stack(ffn_frames), grad_branch), "items", axis=0
    ).reshape(-1, width)
    att_plane = lax.dynamic_slice_in_dim(
        branch_plane, width + item_index * shard, shard, 1
    )
    turns[0] = after(turns[0], low_all)

    chunk_grads, chunk_queries = [], []

    def weight_terms(c):
        send = matmul(send_rows, chunk_grads[c]).astype(BF16)
        received = send_across(send, "items", 1).reshape(-1, shard, 2 * half)
        keep = matmul(after(keep_rows, send), chunk_grads[c]).astype(BF16)
        return send, keep.reshape(-1, shard, 2 * half), received

    def chip_terms(keep, received):
        return (keep.astype(F32) + received.astype(F32)).astype(BF16)

    def exchange_chips(x):
        groups_of = [list(range(k, item_size, 2)) for k in range(2)]
        return lax.all_to_all(x, "items", 0, 0, axis_index_groups=groups_of)

    def frame_rows(ranges):
        rows = shard // frame_size
        columns = sum(x.shape[-1] for x in ranges)
        return pl.pallas_call(
            functools.partial(rows_kernel, count=len(ranges), frames=frame_size, items=items),
            in_specs=[smem] + [whole] * len(ranges),
            out_specs=[whole] * frame_size,
            out_shape=[struct((rows, columns), F32)]
            + [struct((rows, columns), BF16)] * (frame_size - 1),
            scratch_shapes=[pltpu.VMEM((frame_size, rows, columns), F32)],
            cost_estimate=cost(3.5),
            compiler_params=params,
        )(flags, *ranges)

    def send_rows_on(rows):
        return [rows[0]] + [send_on(p, "frames", s) for s, p in enumerate(rows) if s]

    for c in range(CHUNKS):

        def block_of(g, c=c):
            return (0, c * groups + g)

        chunk_grad, chunk_query = pl.pallas_call(
            functools.partial(
                backward_kernel, frames=frame_size, patches=patches, scale=head_size**-0.5, **sizes
            ),
            grid=(groups,),
            in_specs=[
                smem,
                pl.BlockSpec((all_tokens, 2 * group_width), lambda g: (0, g)),
                pl.BlockSpec((lats, group_width), block_of),
                pl.BlockSpec((1, items, 8, stack), lambda g: (g, 0, 0, 0)),
            ]
            + [pl.BlockSpec((own, group_width), block_of)] * frame_size
            + [pl.BlockSpec((own, LANES), lambda g, c=c: (0, width // LANES + c))] * frame_size,
            out_specs=[
                pl.BlockSpec((all_tokens, 2 * group_width), lambda g: (0, g)),
                pl.BlockSpec((lats, group_width), lambda g: (0, g)),
            ],
            out_shape=[
                struct((all_tokens, 2 * half), BF16),
                struct((lats, half), F32),
            ],
            scratch_shapes=[
                pltpu.VMEM((items, lats, group_width), F32),
                pltpu.VMEM((items, lats, LANES), F32),
            ],
            cost_estimate=cost(8),
            compiler_params=params,
        )(flags, after(boths[c], *held) if c else boths[c], queries, tops[c], *turns, *turns)
        chunk_grads.append(chunk_grad)
        chunk_queries.append(chunk_query)
        if c == 0:
            first_send, first_keep, first_received = weight_terms(0)
            held = (first_send,)
    first_terms = chip_terms(after(first_keep, chunk_grads[-1]), first_received)
    first_moved = exchange_chips(first_terms)

    last_block = pl.BlockSpec((lats, 2 * half), lambda i: (tokens // lats, 0))
    media_grad, media_sums, lat_product = pl.pallas_call(
        functools.partial(media_kernel, chunks=CHUNKS, items=items, frames=frame_total),
        grid=(items,),
        in_specs=[smem]
        + [pl.BlockSpec((patches, 2 * half), lambda i: (i, 0))] * CHUNKS
        + [last_block] * CHUNKS
        + [pl.BlockSpec((width, 2 * half), lambda i, c=c: (0, c)) for c in range(CHUNKS)]
        + [pl.BlockSpec((patches, width), lambda i: (i, 0)), whole, whole],
        out_specs=[
            pl.BlockSpec((patches, width), lambda i: (i, 0)),
            pl.BlockSpec((16, width), lambda i: (0, 0)),
            pl.BlockSpec((lats, width), lambda i: (0, 0)),
        ],
        out_shape=[
            struct((tokens, width), BF16),
            struct((16, width), F32),
            struct((lats, width), F32),
        ],
        cost_estimate=cost(21),
        compiler_params=params,
    )(
        flags,
        *chunk_grads[:-1],
        after(chunk_grads[-1], first_terms),
        *chunk_grads,
        *[kv_full] * CHUNKS,
        flat_media,
        time_rows,
        media_gain[None],
    )

    sum_rows = 2 * lats + 24
    sum_rows += -sum_rows % (8 * item_size)
    payload = pl.pallas_call(
        functools.partial(latent_kernel, chunks=CHUNKS, items=items),
        in_specs=[smem] + [whole] * (CHUNKS + 6),
        out_specs=whole,
        out_shape=struct((sum_rows, width), F32),
        cost_estimate=cost(3),
        compiler_params=params,
    )(
        flags,
        *chunk_queries,
        after(lat_product, first_moved),
        latents,
        latent_gain[None],
        grad_base,
        ffn_sums,
        media_sums,
    )
    payload_part = lax.psum_scatter(payload, "items", scatter_dimension=0, tiled=True)

    chunk_grads[-1] = after(chunk_grads[-1], payload)
    last_send, last_keep, last_received = weight_terms(CHUNKS - 1)
    last_terms = chip_terms(after(last_keep, first_moved), last_received)
    last_moved = exchange_chips(last_terms)
    out_part = transposed_left(att_plane, after(branch_plane, last_send)[:, :width])
    first_rows = frame_rows([after(first_moved, last_terms), out_part[None]])
    first_frames = send_rows_on(first_rows)
    all_plane = plane * frame_size
    block_rows = min(512, all_plane)
    row_block = pl.BlockSpec((block_rows, width), lambda i: (i, 0))
    hidden_block = pl.BlockSpec((block_rows, hidden_shard), lambda i: (i, 0))
    hidden, grad_up = pl.pallas_call(
        feed_back_kernel,
        grid=(all_plane // block_rows,),
        in_specs=[row_block, row_block, whole, whole],
        out_specs=[hidden_block, hidden_block],
        out_shape=[struct((all_plane, hidden_shard), BF16)] * 2,
        cost_estimate=cost(15),
        compiler_params=params,
    )(after(ffn_all, *first_rows), low_all, up_slice, down_weight)

    def outer(left, right, tile, kind):
        rows, columns = left.shape
        shape = (columns, right.shape[1])
        return pl.pallas_call(
            outer_kernel,
            grid=(columns // tile,),
            in_specs=[pl.BlockSpec((rows, tile), lambda i: (0, i)), whole],
            out_specs=pl.BlockSpec((tile, shape[1]), lambda i: (i, 0)),
            out_shape=struct(shape, kind),
            cost_estimate=cost(9.5),
            compiler_params=params,
        )(left, right)

    first_total = total_of(first_frames).astype(BF16)
    first_placed = spread_on(first_total, "frames")
    last_rows = frame_rows([after(last_moved, hidden)])
    last_frames = send_rows_on(last_rows)
    up_part = outer(ffn_all, after(grad_up, first_total, *last_rows), width // 4, BF16)
    result_sum = lax.psum_scatter(
        after(result_part, hidden).reshape(-1, width), "items", scatter_dimension=0, tiled=True
    )
    up_moved = lax.all_to_all(up_part, "items", 0, 1, tiled=True)
    up_grad = up_moved.astype(F32)
    last_total = total_of(last_frames).astype(BF16)
    last_placed = spread_on(last_total, "frames")
    down_grad = outer(
        after(hidden, up_part, last_total, *first_placed),
        low_all,
        256 if hidden_shard % 256 == 0 else hidden_shard,
        F32,
    )
    placed = first_placed + last_placed
    payload_part = after(payload_part, last_total)
    payload_others = spread_on(payload_part.astype(BF16), "frames")[1:]
    sums = lax.all_gather(
        total_of([payload_part] + payload_others), "items", axis=0, tiled=True
    )
    query_low = sums[lats : 2 * lats].astype(BF16)
    query_grad = transposed_left(lat_cols, query_low)
    norm_cols = after(transposed_right(query_low, query_weight), up_moved, *last_placed)
    latents_grad, lat_gain, lat_bias = pl.pallas_call(
        functools.partial(query_norm_kernel, devices=item_size, items=items),
        in_specs=[smem] + [whole] * (item_size + 3),
        out_specs=[whole] * 3,
        out_shape=[struct((lats, width), F32), struct((1, width), F32), struct((1, width), F32)],
        scratch_shapes=[pltpu.VMEM((item_size, lats, shard), F32)],
        cost_estimate=cost(3),
        compiler_params=params,
    )(flags, *spread_across(norm_cols, "items"), latents, latent_gain[None], sums)
    at = 2 * lats
    column_sums = lax.dynamic_slice_in_dim(
        sums[at + 8 : at + 24], item_index * shard, shard, 1
    )

    key_grad, value_grad, out_grad = pl.pallas_call(
        functools.partial(
            place_kernel, chunks=CHUNKS, frames=frame_size, items=items, groups=groups
        ),
        in_specs=[smem] + [whole] * len(placed),
        out_specs=[whole] * 3,
        out_shape=[struct((frame_size, shard // frame_size, width), F32)] * 3,
        cost_estimate=cost(3.4),
        compiler_params=params,
    )(flags, *placed)

    result = mid_rows + result_sum.astype(F32)
    return (
        result.reshape(items, row_total, width),
        entropy,
        media_grad.reshape(media.shape),
        latents_grad,
        column_sums[:frame_total],
        column_sums[8],
        column_sums[9],
        lat_gain.reshape(width),
        lat_bias.reshape(width),
        sums[at],
        sums[at + 1],
        query_grad,
        key_grad.reshape(shard, width),
        value_grad.reshape(shard, width),
        out_grad.reshape(shard, width),
        up_grad,
        down_grad,
    )


def solution(mesh):
    return jax.shard_map(
        body,
        mesh=mesh,
        in_specs=(
            P("items", "frames", None, None),
            P("items", "frames", None),
            P(),
            P(),
            P(),
            P(),
            P(),
            P(),
            P(),
            P(),
            P(),
            P(),
            P("items", None),
            P("items", None),
            P("items", None),
            P("items", None),
            P("items", None),
            P("items", None),
        ),
        out_specs=(
            P("items", "frames", None),
            P("items", "frames"),
            P("items", "frames", None, None),
            P(),
            P(None, "items"),
            P("items"),
            P("items"),
            P(),
            P(),
            P(),
            P(),
            P("items", None),
            P("items", None),
            P("items", None),
            P("items", None),
            P("items", None),
            P("items", None),
        ),
        check_vma=False,
    )
```

```python
import functools
import math

import jax
import jax.numpy as jnp
from jax import lax
from jax.experimental import pallas as pl
from jax.experimental.pallas import tpu as pltpu
from jax.sharding import PartitionSpec as P

HEADS = 16
GROUP = 4
CHUNKS = 2
LANES = 128
EPSILON = 1e-05
MASKED = -1e30
F32 = jnp.float32
BF16 = jnp.bfloat16
HIGHEST = lax.Precision.HIGHEST


def layer_norm(inputs, norm_gain, norm_bias):
    center = inputs - jnp.mean(inputs, axis=-1, keepdims=True)
    spread = jnp.mean(center * center, axis=-1, keepdims=True)
    return center * lax.rsqrt(spread + EPSILON) * norm_gain + norm_bias


def matmul(left_side, right_side):
    return jnp.dot(left_side, right_side, preferred_element_type=F32)


def transposed_left(left_side, right_side):
    return lax.dot_general(
        left_side, right_side, (((0,), (0,)), ((), ())), preferred_element_type=F32
    )


def transposed_right(left_side, right_side):
    return lax.dot_general(
        left_side, right_side, (((1,), (1,)), ((), ())), preferred_element_type=F32
    )


def send_on(x, axis, step):
    size = lax.axis_size(axis)
    return lax.ppermute(x, axis, [(i, (i + step) % size) for i in range(size)])


def send_across(x, axis, distance):
    return lax.ppermute(x, axis, [(i, i ^ distance) for i in range(lax.axis_size(axis))])


def spread_on(x, axis):
    return [x] + [send_on(x, axis, s) for s in range(1, lax.axis_size(axis))]


def spread_across(x, axis):
    chips = [x] + [send_across(x, axis, d) for d in range(2, lax.axis_size(axis), 2)]
    return [b for block in chips for b in (block, send_across(block, axis, 1))]


def collect_across(pieces, axis):
    return [pieces[0]] + [send_across(p, axis, d) for d, p in enumerate(pieces) if d]


def total_of(pieces):
    return functools.reduce(jnp.add, [p.astype(F32) for p in pieces])


def after(x, *earlier):
    return lax.optimization_barrier((x,) + earlier)[0]


def split_terms(x):
    high = x.astype(BF16)
    rest = x - high.astype(F32)
    middle = rest.astype(BF16)
    return high, middle, (rest - middle.astype(F32)).astype(BF16)


def iota(shape, dim):
    return lax.broadcasted_iota(jnp.int32, shape, dim)


def head_masks(rows, width, head_size):
    lane = iota((rows, width), 1)
    return [
        jnp.logical_and(lane >= h * head_size, lane < (h + 1) * head_size)
        for h in range(width // head_size)
    ]


def spread_heads(block, masks):
    return jnp.concatenate([jnp.where(m, block, jnp.zeros_like(block)) for m in masks], 0)


def collect_heads(block, masks):
    rows = block.shape[0] // len(masks)
    total = jnp.where(masks[0], block[:rows], 0.0)
    for h in range(1, len(masks)):
        total = total + jnp.where(masks[h], block[h * rows : (h + 1) * rows], 0.0)
    return total


def head_expand(width, head_size):
    row, column = iota((LANES, width), 0), iota((LANES, width), 1)
    return jnp.logical_and(column >= row * head_size, column < (row + 1) * head_size).astype(F32)


def live_rows(flag_ref, item, items, patches, lats, columns):
    row = iota((patches + lats, columns), 0)
    media = jnp.logical_and(row < patches, flag_ref[item] > 0)
    return jnp.logical_or(media, jnp.logical_and(row >= patches, flag_ref[items] > 0))


def pack_shape(own, shard, width):
    unit = math.gcd(own, shard)
    return unit, width * unit // shard


def join_kernel(key_ref, value_ref, cotangent_ref, out_ref, low_ref, *, width):
    for g in range(key_ref.shape[1] // width):
        columns = slice(g * width, (g + 1) * width)
        out_ref[:, 2 * g * width : (2 * g + 1) * width] = key_ref[:, columns]
        out_ref[:, (2 * g + 1) * width : (2 * g + 2) * width] = value_ref[:, columns]
    low = cotangent_ref[...].astype(BF16)
    low_ref[...] = low
    own, span = low.shape
    unit, piece = pack_shape(own, out_ref.shape[0], span)
    for a in range(own // unit):
        for b in range(span // piece):
            at = 2 * span + a * piece
            out_ref[b * unit : (b + 1) * unit, at : at + piece] = low[
                a * unit : (a + 1) * unit, b * piece : (b + 1) * piece
            ]


def norm_kernel(media_ref, time_ref, gain_ref, bias_ref, lat_ref, out_ref, *, steps, per_item):
    step = pl.program_id(0)

    @pl.when(step < steps)
    def _():
        rows = media_ref[...].astype(F32) + time_ref[pl.ds(step // per_item, 1), :]
        out_ref[...] = layer_norm(rows, gain_ref[...], bias_ref[...]).astype(BF16)

    @pl.when(step == steps)
    def _():
        out_ref[...] = lat_ref[...]


def forward_kernel(
    flag_ref, both_ref, query_ref, top_ref, *refs, items, patches, scale, head_size, heads,
):
    message_refs, (part_ref, mark_ref) = refs[:-2], refs[-2:]
    lats, width = query_ref.shape
    frames = len(message_refs)
    own = message_refs[0].shape[0]
    row_total = own // items
    masks = head_masks(lats, width, head_size)
    queries = spread_heads(query_ref[...].astype(F32), masks).astype(BF16)
    base = items * patches
    lat_both = both_ref[base : base + lats, :]
    group = pl.program_id(0)
    term, lane = iota((16, GROUP * LANES), 0), iota((16, GROUP * LANES), 1)
    place = jnp.logical_and(
        lane % LANES == term * heads + group * GROUP + lane // LANES, term < 9
    ).astype(BF16)
    for i in range(items):
        both = jnp.concatenate([both_ref[i * patches : (i + 1) * patches, :], lat_both], 0)
        live = live_rows(flag_ref, i, items, patches, lats, queries.shape[0])
        scores = scale * transposed_right(both[:, :width], queries)
        masked = jnp.where(live, scores, MASKED)
        top = jnp.max(masked, axis=0, keepdims=True)
        block_exp = jnp.where(live, jnp.exp(masked - top), 0.0)
        total = jnp.sum(block_exp, axis=0, keepdims=True)
        moment = jnp.sum(block_exp * scores, axis=0, keepdims=True)
        part = transposed_left(block_exp.astype(BF16), both[:, width:])
        part_ref[i] = collect_heads(part, masks)
        top_ref[0, i] = jnp.broadcast_to(top, top_ref.shape[2:])
        terms = jnp.concatenate(
            [t.astype(F32) for x in (top, total, moment) for t in split_terms(x)]
            + [jnp.zeros((7, top.shape[1]), F32)],
            0,
        ).astype(BF16)
        wide = transposed_left(terms, place)
        mark = wide[:lats, :LANES]
        for h in range(1, GROUP):
            mark = mark + wide[h * lats : (h + 1) * lats, h * LANES : (h + 1) * LANES]
        mark_ref[i] = mark

    end = message_refs[0].shape[1] - LANES
    for s, message_ref in enumerate(message_refs):
        start = pl.multiple_of(lax.rem(flag_ref[items + 1] + s, frames) * row_total, row_total)
        rows = pl.ds(start, row_total)
        block = jnp.concatenate([part_ref[i, rows, :] for i in range(items)], 0).astype(BF16)
        mark = jnp.concatenate([mark_ref[i, rows, :] for i in range(items)], 0).astype(BF16)
        for g in range(end // width):

            @pl.when(group == g)
            def _():
                message_ref[:, g * width : (g + 1) * width] = block
                if g == 0:
                    message_ref[:, end:] = mark
                else:
                    message_ref[:, end:] = message_ref[:, end:] + mark


def merge_kernel(*refs, chunks, frames, items, head_size, heads):
    message_refs = refs[: chunks * frames]
    base_ref, weight_ref, gain_ref, bias_ref = refs[chunks * frames : chunks * frames + 4]
    merged_ref, mid_ref, ffn_ref, log_ref, entropy_ref = refs[chunks * frames + 4 :]
    own, columns = message_refs[0].shape
    half = columns - LANES
    lane, column = iota((LANES, 3 * LANES), 0), iota((LANES, 3 * LANES), 1)
    gather = jnp.logical_and(
        jnp.logical_and(lane // heads // 3 == column // LANES, lane % heads == column % LANES),
        lane < 9 * heads,
    ).astype(BF16)
    expand = head_expand(half, head_size)
    live = iota((own, LANES), 1) < heads
    spread = jnp.zeros((own, LANES), F32)
    for c in range(chunks):
        sources = message_refs[c * frames : (c + 1) * frames]
        stats = [matmul(x[:, half:], gather) for x in sources]
        tops = [x[:, :LANES] for x in stats]
        peak = functools.reduce(jnp.maximum, tops)
        factors = [jnp.exp(t - peak) for t in tops]
        whole = sum(f * x[:, LANES : 2 * LANES] for f, x in zip(factors, stats))
        moment = sum(f * x[:, 2 * LANES :] for f, x in zip(factors, stats))
        whole = jnp.where(live, whole, 1.0)
        log_total = jnp.where(live, peak + jnp.log(whole), 0.0)
        log_ref[c] = log_total
        spread = spread + jnp.where(live, log_total - moment / whole, 0.0)
        merged = jnp.zeros((own, half), F32)
        for x, factor in zip(sources, factors):
            share = jnp.where(live, factor / whole, 0.0)
            wide = jnp.dot(share, expand, precision=HIGHEST, preferred_element_type=F32)
            merged = merged + x[:, :half].astype(F32) * wide
        merged_ref[:, c * half : (c + 1) * half] = merged
    entropy_ref[...] = jnp.broadcast_to(
        jnp.sum(spread, axis=1, keepdims=True) * (1.0 / HEADS), entropy_ref.shape
    )
    base = jnp.concatenate([base_ref[...]] * items, 0)
    mid = base + matmul(merged_ref[...].astype(BF16), weight_ref[...])
    mid_ref[...] = mid
    ffn_ref[...] = layer_norm(mid, gain_ref[...], bias_ref[...]).astype(BF16)


def gelu_parts(x):
    share = 0.5 * (1.0 + lax.erf(x * (0.5**0.5)))
    slope = share + x * jnp.exp(-0.5 * x * x) * ((2.0 * jnp.pi) ** -0.5)
    return x * share, slope


def feed_kernel(flag_ref, *refs, devices, items):
    row_refs = refs[:devices]
    low_ref, up_ref, down_ref, result_ref = refs[devices : devices + 4]
    grad_refs, (plane_ref, plane_low_ref) = refs[devices + 4 : -2], refs[-2:]
    own, width = row_refs[0].shape
    shard = low_ref.shape[0] // devices
    unit, piece = pack_shape(own, shard, width)
    me = flag_ref[2 * items + 2]
    for d in range(devices):
        plane_ref[d * own : (d + 1) * own, :] = row_refs[d][...]
        source = jnp.bitwise_xor(me, d) * shard
        for a in range(own // unit):
            rows = slice(d * own + a * unit, d * own + (a + 1) * unit)
            for b in range(shard // unit):
                start = pl.multiple_of(source + b * unit, unit)
                plane_low_ref[rows, b * piece : (b + 1) * piece] = low_ref[
                    pl.ds(start, unit), a * piece : (a + 1) * piece
                ]
    upward = matmul(plane_ref[...], up_ref[...])
    hidden, slope = gelu_parts(upward)
    grad_up = (slope * transposed_right(plane_low_ref[...], down_ref[...])).astype(BF16)
    grad = transposed_right(grad_up, up_ref[...]).astype(BF16)
    result = matmul(hidden.astype(BF16), down_ref[...]).astype(BF16)
    for d in range(devices):
        grad_refs[d][...] = grad[d * own : (d + 1) * own, :]
        result_ref[jnp.bitwise_xor(me, d)] = result[d * own : (d + 1) * own, :]


def feed_back_kernel(row_ref, low_ref, up_ref, down_ref, hidden_ref, grad_ref):
    hidden, slope = gelu_parts(matmul(row_ref[...], up_ref[...]))
    hidden_ref[...] = hidden.astype(BF16)
    grad_ref[...] = (slope * transposed_right(low_ref[...], down_ref[...])).astype(BF16)


def outer_kernel(left_ref, right_ref, out_ref):
    out_ref[...] = transposed_left(left_ref[...], right_ref[...]).astype(out_ref.dtype)


def norm_backward(rows, gain, gradient):
    center = rows - jnp.mean(rows, axis=1, keepdims=True)
    rate = lax.rsqrt(jnp.mean(center * center, axis=1, keepdims=True) + EPSILON)
    unit = center * rate
    scaled = gradient * gain
    inner = scaled - jnp.mean(scaled, axis=1, keepdims=True)
    back = rate * (inner - unit * jnp.mean(scaled * unit, axis=1, keepdims=True))
    return (
        back,
        jnp.sum(gradient * unit, axis=0, keepdims=True),
        jnp.sum(gradient, axis=0, keepdims=True),
    )


def turn_kernel(*refs, devices, items, chunks, head_size, heads):
    part_refs = refs[:devices]
    mid_ref, cotangent_ref, gain_ref, merged_ref, log_ref, weight_ref = refs[
        devices : devices + 6
    ]
    message_ref, branch_ref, base_ref, sums_ref = refs[devices + 6 :]
    own, width = mid_ref.shape
    half = width // chunks
    gradient = total_of([x[...] for x in part_refs])
    back, gain_sum, bias_sum = norm_backward(mid_ref[...], gain_ref[...], gradient)
    grad_mid = cotangent_ref[...] + back
    sums_ref[...] = jnp.zeros(sums_ref.shape, F32)
    sums_ref[0:1, :] = gain_sum
    sums_ref[1:2, :] = bias_sum
    row_total = own // items
    base_ref[...] = total_of(
        [grad_mid[i * row_total : (i + 1) * row_total] for i in range(items)]
    )
    branch = grad_mid.astype(BF16)
    branch_ref[:, :width] = branch
    branch_ref[:, width:] = merged_ref[...].astype(BF16)
    grad_att = transposed_right(branch, weight_ref[...]).astype(BF16)
    expand = head_expand(half, head_size)
    lane, column = iota((6 * LANES, LANES), 0), iota((6 * LANES, LANES), 1)
    place = jnp.logical_and(
        lane % LANES < heads, column == (lane // LANES) * heads + lane % LANES
    ).astype(BF16)
    message_ref[:, :width] = grad_att
    for c in range(chunks):
        columns = slice(c * half, (c + 1) * half)
        delta = lax.dot_general(
            merged_ref[:, columns] * grad_att[:, columns].astype(F32),
            expand,
            (((1,), (1,)), ((), ())),
            precision=HIGHEST,
            preferred_element_type=F32,
        )
        terms = jnp.concatenate([t for x in (log_ref[c], delta) for t in split_terms(x)], 1)
        message_ref[:, width + c * LANES : width + (c + 1) * LANES] = matmul(
            terms, place
        ).astype(BF16)


def backward_kernel(
    *refs, frames, items, patches, scale, head_size, heads,
):
    flag_ref, both_ref, query_ref, top_ref = refs[:4]
    grad_refs = refs[4 : 4 + frames]
    mark_refs = refs[4 + frames : 4 + 2 * frames]
    out_ref, sum_ref, held_ref, note_ref = refs[4 + 2 * frames :]
    lats, width = query_ref.shape
    own = grad_refs[0].shape[0]
    row_total = own // items
    base = items * patches
    for s in range(frames):
        source = lax.rem(flag_ref[items + 1] + (frames - s), frames)
        rows = pl.ds(pl.multiple_of(source * row_total, row_total), row_total)
        block = grad_refs[s][...].astype(F32)
        mark = mark_refs[s][...].astype(F32)
        for i in range(items):
            held_ref[i, rows, :] = block[i * row_total : (i + 1) * row_total]
            note_ref[i, rows, :] = mark[i * row_total : (i + 1) * row_total]
    masks = head_masks(lats, width, head_size)
    queries = spread_heads(query_ref[...].astype(F32), masks).astype(BF16)
    lat_both = both_ref[base : base + lats, :]
    row, lane = iota((GROUP * 8, LANES), 0), iota((GROUP * 8, LANES), 1)
    pick = jnp.logical_and(
        jnp.logical_and(
            lane // heads // 3 == row % 8,
            lane % heads == pl.program_id(0) * GROUP + row // 8,
        ),
        lane < 6 * heads,
    ).astype(BF16)
    grad_query = jnp.zeros((queries.shape[0], width), F32)
    lat_grad_key = jnp.zeros((lats, width), F32)
    lat_grad_value = jnp.zeros((lats, width), F32)
    for i in range(items):
        rows = slice(i * patches, (i + 1) * patches)
        stats = transposed_right(pick, note_ref[i].astype(BF16))
        stats = jnp.concatenate([stats[h * 8 : (h + 1) * 8] for h in range(GROUP)], 1)
        log_total = stats[0:1]
        delta = stats[1:2]
        top = top_ref[0, i, 0:1, :]
        rescale = jnp.exp(top - log_total)
        both = jnp.concatenate([both_ref[rows, :], lat_both], 0)
        keys, values = both[:, :width], both[:, width:]
        grads = spread_heads(held_ref[i], masks).astype(BF16)
        live = live_rows(flag_ref, i, items, patches, lats, queries.shape[0])
        masked = jnp.where(live, scale * transposed_right(keys, queries), MASKED)
        probs = jnp.where(live, jnp.exp(masked - log_total), 0.0)
        block_exp = jnp.where(live, jnp.exp(masked - top), 0.0)
        weights = (block_exp.astype(BF16).astype(F32) * rescale).astype(BF16)
        grad_scores = (probs * (transposed_right(values, grads) - delta)).astype(BF16)
        grad_key = scale * matmul(grad_scores, queries)
        grad_value = matmul(weights, grads)
        out_ref[rows, :width] = grad_key[:patches].astype(BF16)
        out_ref[rows, width:] = grad_value[:patches].astype(BF16)
        grad_query = grad_query + transposed_left(grad_scores, keys)
        lat_grad_key = lat_grad_key + grad_key[patches:]
        lat_grad_value = lat_grad_value + grad_value[patches:]
    out_ref[base : base + lats, :width] = lat_grad_key.astype(BF16)
    out_ref[base : base + lats, width:] = lat_grad_value.astype(BF16)
    sum_ref[...] = scale * collect_heads(grad_query, masks)


def media_kernel(flag_ref, *refs, chunks, items, frames):
    grad_refs, lat_refs, weight_refs = [
        refs[k * chunks : (k + 1) * chunks] for k in range(3)
    ]
    media_ref, time_ref, gain_ref, out_ref, sums_ref, product_ref = refs[3 * chunks :]
    item = pl.program_id(0)

    @pl.when(item == 0)
    def _():
        sums_ref[...] = jnp.zeros(sums_ref.shape, F32)
        product_ref[...] = functools.reduce(
            jnp.add, [transposed_right(g[...], w[...]) for g, w in zip(lat_refs, weight_refs)]
        )

    gradient = functools.reduce(
        jnp.add, [transposed_right(g[...], w[...]) for g, w in zip(grad_refs, weight_refs)]
    )
    inputs = media_ref[...].astype(F32) + time_ref[pl.ds(item, 1), :]
    back, gain_sum, bias_sum = norm_backward(inputs, gain_ref[...], gradient)
    out_ref[...] = back.astype(BF16)
    place = iota((frames, 1), 0) == flag_ref[items + 2 + item]
    sums_ref[0:frames, :] += jnp.where(place, jnp.sum(back, axis=0, keepdims=True), 0.0)
    sums_ref[8:9, :] += gain_sum
    sums_ref[9:10, :] += bias_sum


def latent_kernel(flag_ref, *refs, chunks, items):
    query_refs = refs[:chunks]
    (
        product_ref, latent_ref, gain_ref, base_ref, ffn_ref, media_ref, out_ref,
    ) = refs[chunks:]
    lats, width = latent_ref.shape
    half = width // chunks
    gradient = product_ref[...]
    for c in range(chunks):
        out_ref[lats : 2 * lats, c * half : (c + 1) * half] = query_refs[c][...]
    back, gain_sum, bias_sum = norm_backward(latent_ref[...], gain_ref[...], gradient)
    out_ref[:lats, :] = back
    row_total = base_ref.shape[0]
    start = pl.multiple_of(flag_ref[items + 1] * row_total, row_total)
    out_ref[pl.ds(start, row_total), :] += base_ref[...]
    at = 2 * lats
    out_ref[at : at + 8, :] = ffn_ref[...]
    out_ref[at + 2 : at + 3, :] = gain_sum
    out_ref[at + 3 : at + 4, :] = bias_sum
    out_ref[at + 8 : at + 24, :] = media_ref[...]
    out_ref[at + 24 :, :] = jnp.zeros((out_ref.shape[0] - at - 24, width), F32)


def query_norm_kernel(flag_ref, *refs, devices, items):
    column_refs = refs[:devices]
    latent_ref, gain_ref, sum_ref, out_ref, out_gain_ref, out_bias_ref, held_ref = refs[devices:]
    for d in range(devices):
        held_ref[jnp.bitwise_xor(flag_ref[2 * items + 2], d)] = column_refs[d][...]
    gradient = jnp.concatenate([held_ref[k] for k in range(devices)], 1)
    back, gain_sum, bias_sum = norm_backward(latent_ref[...], gain_ref[...], gradient)
    lats = latent_ref.shape[0]
    out_ref[...] = sum_ref[:lats, :] + back
    out_gain_ref[...] = sum_ref[2 * lats + 2 : 2 * lats + 3, :] + gain_sum
    out_bias_ref[...] = sum_ref[2 * lats + 3 : 2 * lats + 4, :] + bias_sum


def rows_kernel(flag_ref, *refs, count, frames, items):
    part_refs, out_refs, held_ref = refs[:count], refs[count:-1], refs[-1]
    rows = held_ref.shape[1]
    column = 0
    for part_ref in part_refs:
        total = total_of([part_ref[k] for k in range(part_ref.shape[0])])
        for f in range(frames):
            held_ref[f, :, column : column + total.shape[1]] = total[f * rows : (f + 1) * rows]
        column += total.shape[1]
    for s, out_ref in enumerate(out_refs):
        block = held_ref[lax.rem(flag_ref[items + 1] + s, frames)]
        out_ref[...] = block.astype(out_ref.dtype)


def place_kernel(flag_ref, *refs, chunks, frames, items, groups):
    chunk_refs = refs[: chunks * frames]
    key_ref, value_ref, out_ref = refs[chunks * frames :]
    width = key_ref.shape[2] // (chunks * groups)
    for s in range(frames):
        source = lax.rem(flag_ref[items + 1] + (frames - s), frames)
        out_ref[source] = chunk_refs[s][:, 2 * groups * width :].astype(F32)
        for c in range(chunks):
            for g in range(groups):
                at = (c * groups + g) * width
                block = chunk_refs[c * frames + s][:, 2 * g * width : 2 * (g + 1) * width]
                block = block.astype(F32)
                key_ref[source, :, at : at + width] = block[:, :width]
                value_ref[source, :, at : at + width] = block[:, width:]


def body(
    media,
    cotangent,
    frame_count,
    frame_start,
    latents,
    time_embed,
    media_gain,
    media_bias,
    latent_gain,
    latent_bias,
    ffn_gain,
    ffn_bias,
    query_weight,
    key_weight,
    value_weight,
    out_weight,
    up_weight,
    down_weight,
):
    items = media.shape[0]
    patches = media.shape[2]
    width = media.shape[3]
    lats = latents.shape[0]
    frame_total = time_embed.shape[0]
    row_total = cotangent.shape[1]
    own = items * row_total
    head_size = width // HEADS
    half = width // CHUNKS
    chunk_heads = HEADS // CHUNKS
    group_width = GROUP * head_size
    groups = chunk_heads // GROUP
    stack = GROUP * lats
    tokens = items * patches
    all_tokens = tokens + lats
    shard = query_weight.shape[0]
    hidden_shard = down_weight.shape[0]
    item_size = lax.axis_size("items")
    frame_size = lax.axis_size("frames")
    plane = item_size * own
    item_index = lax.axis_index("items")
    slot = lax.axis_index("frames")
    row_base = slot * row_total
    params = pltpu.CompilerParams(vmem_limit_bytes=56 * 2**20)
    smem = pl.BlockSpec(memory_space=pltpu.SMEM)
    whole = pl.BlockSpec(memory_space=pltpu.VMEM)
    sizes = dict(items=items, head_size=head_size, heads=chunk_heads)

    def struct(shape, kind):
        return jax.ShapeDtypeStruct(shape, kind)

    def cost(micros):
        return pl.CostEstimate(
            flops=int(micros * 1.15e9), bytes_accessed=int(micros * 3.6e6), transcendentals=0
        )

    def column_blocks(x):
        return jnp.transpose(x.reshape(-1, item_size, shard), (1, 0, 2))

    def scatter_exchange(x, axis):
        return jnp.sum(lax.all_to_all(x, axis, 0, 0).astype(F32), axis=0)

    grad_out = cotangent.reshape(own, width)
    low_columns = own * width // shard
    joined, grad_low = pl.pallas_call(
        functools.partial(join_kernel, width=group_width),
        out_shape=[struct((shard, 2 * width + low_columns), BF16), struct((own, width), BF16)],
        cost_estimate=cost(2.5),
        compiler_params=params,
    )(key_weight, value_weight, grad_out)
    kv_full = lax.all_gather(joined, "items", axis=0, tiled=True)
    low_frames = jnp.stack(spread_on(grad_low, "frames"))

    lat_norm = layer_norm(latents, latent_gain, latent_bias).astype(BF16)
    lat_cols = lax.dynamic_slice_in_dim(lat_norm, item_index * shard, shard, 1)
    query_blocks = column_blocks(matmul(lat_cols, query_weight))
    query_cols = scatter_exchange(query_blocks, "items").astype(BF16)
    query_spread = jnp.broadcast_to(query_cols[None], (item_size, lats, shard))
    queries = jnp.transpose(lax.all_to_all(query_spread, "items", 0, 0), (1, 0, 2)).reshape(
        lats, width
    )

    counts = lax.dynamic_slice_in_dim(frame_count, item_index * items, items)
    starts = lax.dynamic_slice_in_dim(frame_start, item_index * items, items)
    offset = (slot - starts) % frame_total
    flags = jnp.concatenate(
        [
            (offset < counts).astype(jnp.int32),
            (slot == 0).astype(jnp.int32)[None],
            slot.astype(jnp.int32)[None],
            offset.astype(jnp.int32),
            item_index.astype(jnp.int32)[None],
        ]
    )
    picker = (offset[:, None] == jnp.arange(frame_total, dtype=jnp.int32)[None, :]).astype(F32)
    time_rows = jnp.dot(picker, time_embed, precision=HIGHEST, preferred_element_type=F32)
    flat_media = media.reshape(tokens, width)
    steps = tokens // lats
    all_rows = pl.pallas_call(
        functools.partial(norm_kernel, steps=steps, per_item=patches // lats),
        grid=(steps + 1,),
        in_specs=[
            pl.BlockSpec((lats, width), lambda i: (jnp.minimum(i, steps - 1), 0)),
            whole,
            whole,
            whole,
            whole,
        ],
        out_specs=pl.BlockSpec((lats, width), lambda i: (i, 0)),
        out_shape=struct((all_tokens, width), BF16),
        cost_estimate=cost(12),
        compiler_params=params,
    )(
        after(flat_media, query_blocks),
        time_rows,
        media_gain[None],
        media_bias[None],
        lat_norm,
    )
    out_full = lax.all_gather(after(out_weight, all_rows), "items", axis=0, tiled=True)

    core = item_index % 2
    rows_across = after(all_rows, query_cols).T.reshape(item_size // 2, 2, shard, all_tokens)
    send_rows, keep_rows = [
        jnp.concatenate(
            [
                lax.dynamic_slice(
                    rows_across, (k, which, 0, 0), (1, 1, shard, all_tokens)
                ).reshape(shard, all_tokens)
                for k in range(item_size // 2)
            ],
            0,
        )
        for which in (1 - core, core)
    ]
    boths, tops, messages = [], [], []
    for c in range(CHUNKS):

        def block_of(g, c=c):
            return (0, c * groups + g)

        if c:
            rows = after(all_rows, tops[-1])
        else:
            rows = after(all_rows, queries, send_rows, keep_rows)
        both = matmul(rows, kv_full[:, 2 * c * half : 2 * (c + 1) * half]).astype(BF16)
        top, *parts = pl.pallas_call(
            functools.partial(
                forward_kernel, patches=patches, scale=head_size**-0.5, **sizes
            ),
            grid=(groups,),
            in_specs=[
                smem,
                pl.BlockSpec((all_tokens, 2 * group_width), lambda g: (0, g)),
                pl.BlockSpec((lats, group_width), block_of),
            ],
            out_specs=[pl.BlockSpec((1, items, 8, stack), lambda g: (g, 0, 0, 0))]
            + [pl.BlockSpec((own, half + LANES), lambda g: (0, 0))] * frame_size,
            out_shape=[struct((groups, items, 8, stack), F32)]
            + [struct((own, half + LANES), BF16)] * frame_size,
            scratch_shapes=[
                pltpu.VMEM((items, lats, group_width), F32),
                pltpu.VMEM((items, lats, LANES), F32),
            ],
            cost_estimate=cost(7.8),
            compiler_params=params,
        )(flags, both, queries)
        boths.append(both)
        tops.append(top)
        messages += [p if s == 0 else send_on(p, "frames", s) for s, p in enumerate(parts)]
    up_slice = lax.all_to_all(after(up_weight, boths[0]), "items", 1, 0, tiled=True)
    low_all = lax.all_gather(after(low_frames, tops[1]), "items", axis=0).reshape(-1, width)

    base_rows = lax.dynamic_slice_in_dim(latents, row_base, row_total, 0)
    merged, mid_rows, ffn_in, logs, entropy_wide = pl.pallas_call(
        functools.partial(merge_kernel, chunks=CHUNKS, frames=frame_size, **sizes),
        out_shape=[
            struct((own, width), F32),
            struct((own, width), F32),
            struct((own, width), BF16),
            struct((CHUNKS, own, LANES), F32),
            struct((own, LANES), F32),
        ],
        cost_estimate=cost(6.3),
        compiler_params=params,
    )(*messages, base_rows, out_full, ffn_gain[None], ffn_bias[None])
    entropy = entropy_wide[:, 0].reshape(items, row_total)

    ffn_blocks = spread_across(ffn_in, "items")
    ffn_frames = spread_on(after(ffn_in, *ffn_blocks), "frames")
    result_part, *parts = pl.pallas_call(
        functools.partial(feed_kernel, devices=item_size, items=items),
        grid=(1,),
        in_specs=[smem]
        + [whole] * item_size
        + [
            pl.BlockSpec((width, low_columns), lambda i: (0, 2 * width // low_columns)),
            whole,
            whole,
        ],
        out_specs=[whole] * (1 + item_size),
        out_shape=[struct((item_size, own, width), BF16)]
        + [struct((own, width), BF16)] * item_size,
        scratch_shapes=[pltpu.VMEM((plane, width), BF16)] * 2,
        cost_estimate=cost(10),
        compiler_params=params,
    )(flags, *ffn_blocks, kv_full, up_slice, down_weight)
    grad_blocks = collect_across(parts, "items")
    grad_blocks[0] = after(grad_blocks[0], *ffn_frames)

    turn, grad_branch, grad_base, ffn_sums = pl.pallas_call(
        functools.partial(turn_kernel, devices=item_size, chunks=CHUNKS, **sizes),
        out_shape=[
            struct((own, width + CHUNKS * LANES), BF16),
            struct((own, 2 * width), BF16),
            struct((row_total, width), F32),
            struct((8, width), F32),
        ],
        cost_estimate=cost(7.6),
        compiler_params=params,
    )(*grad_blocks, mid_rows, grad_out, ffn_gain[None], merged, logs, out_full)
    turns = spread_on(turn, "frames")
    branch_plane = lax.all_gather(grad_branch, "items", axis=0, tiled=True)
    ffn_all = lax.all_gather(
        after(jnp.stack(ffn_frames), grad_branch), "items", axis=0
    ).reshape(-1, width)
    att_plane = lax.dynamic_slice_in_dim(
        branch_plane, width + item_index * shard, shard, 1
    )
    turns[0] = after(turns[0], low_all)

    chunk_grads, chunk_queries = [], []

    def weight_terms(c):
        send = matmul(send_rows, chunk_grads[c]).astype(BF16)
        received = send_across(send, "items", 1).reshape(-1, shard, 2 * half)
        keep = matmul(after(keep_rows, send), chunk_grads[c]).astype(BF16)
        return send, keep.reshape(-1, shard, 2 * half), received

    def chip_terms(keep, received):
        return (keep.astype(F32) + received.astype(F32)).astype(BF16)

    def exchange_chips(x):
        groups_of = [list(range(k, item_size, 2)) for k in range(2)]
        return lax.all_to_all(x, "items", 0, 0, axis_index_groups=groups_of)

    def frame_rows(ranges):
        rows = shard // frame_size
        columns = sum(x.shape[-1] for x in ranges)
        return pl.pallas_call(
            functools.partial(rows_kernel, count=len(ranges), frames=frame_size, items=items),
            in_specs=[smem] + [whole] * len(ranges),
            out_specs=[whole] * frame_size,
            out_shape=[struct((rows, columns), F32)]
            + [struct((rows, columns), BF16)] * (frame_size - 1),
            scratch_shapes=[pltpu.VMEM((frame_size, rows, columns), F32)],
            cost_estimate=cost(3.5),
            compiler_params=params,
        )(flags, *ranges)

    def send_rows_on(rows):
        return [rows[0]] + [send_on(p, "frames", s) for s, p in enumerate(rows) if s]

    for c in range(CHUNKS):

        def block_of(g, c=c):
            return (0, c * groups + g)

        chunk_grad, chunk_query = pl.pallas_call(
            functools.partial(
                backward_kernel, frames=frame_size, patches=patches, scale=head_size**-0.5, **sizes
            ),
            grid=(groups,),
            in_specs=[
                smem,
                pl.BlockSpec((all_tokens, 2 * group_width), lambda g: (0, g)),
                pl.BlockSpec((lats, group_width), block_of),
                pl.BlockSpec((1, items, 8, stack), lambda g: (g, 0, 0, 0)),
            ]
            + [pl.BlockSpec((own, group_width), block_of)] * frame_size
            + [pl.BlockSpec((own, LANES), lambda g, c=c: (0, width // LANES + c))] * frame_size,
            out_specs=[
                pl.BlockSpec((all_tokens, 2 * group_width), lambda g: (0, g)),
                pl.BlockSpec((lats, group_width), lambda g: (0, g)),
            ],
            out_shape=[
                struct((all_tokens, 2 * half), BF16),
                struct((lats, half), F32),
            ],
            scratch_shapes=[
                pltpu.VMEM((items, lats, group_width), F32),
                pltpu.VMEM((items, lats, LANES), F32),
            ],
            cost_estimate=cost(8),
            compiler_params=params,
        )(flags, after(boths[c], *held) if c else boths[c], queries, tops[c], *turns, *turns)
        chunk_grads.append(chunk_grad)
        chunk_queries.append(chunk_query)
        if c == 0:
            first_send, first_keep, first_received = weight_terms(0)
            held = (first_send,)
    first_terms = chip_terms(after(first_keep, chunk_grads[-1]), first_received)
    first_moved = exchange_chips(first_terms)

    last_block = pl.BlockSpec((lats, 2 * half), lambda i: (tokens // lats, 0))
    media_grad, media_sums, lat_product = pl.pallas_call(
        functools.partial(media_kernel, chunks=CHUNKS, items=items, frames=frame_total),
        grid=(items,),
        in_specs=[smem]
        + [pl.BlockSpec((patches, 2 * half), lambda i: (i, 0))] * CHUNKS
        + [last_block] * CHUNKS
        + [pl.BlockSpec((width, 2 * half), lambda i, c=c: (0, c)) for c in range(CHUNKS)]
        + [pl.BlockSpec((patches, width), lambda i: (i, 0)), whole, whole],
        out_specs=[
            pl.BlockSpec((patches, width), lambda i: (i, 0)),
            pl.BlockSpec((16, width), lambda i: (0, 0)),
            pl.BlockSpec((lats, width), lambda i: (0, 0)),
        ],
        out_shape=[
            struct((tokens, width), BF16),
            struct((16, width), F32),
            struct((lats, width), F32),
        ],
        cost_estimate=cost(21),
        compiler_params=params,
    )(
        flags,
        *chunk_grads[:-1],
        after(chunk_grads[-1], first_terms),
        *chunk_grads,
        *[kv_full] * CHUNKS,
        flat_media,
        time_rows,
        media_gain[None],
    )

    sum_rows = 2 * lats + 24
    sum_rows += -sum_rows % (8 * item_size)
    payload = pl.pallas_call(
        functools.partial(latent_kernel, chunks=CHUNKS, items=items),
        in_specs=[smem] + [whole] * (CHUNKS + 6),
        out_specs=whole,
        out_shape=struct((sum_rows, width), F32),
        cost_estimate=cost(3),
        compiler_params=params,
    )(
        flags,
        *chunk_queries,
        after(lat_product, first_moved),
        latents,
        latent_gain[None],
        grad_base,
        ffn_sums,
        media_sums,
    )
    payload_part = lax.psum_scatter(payload, "items", scatter_dimension=0, tiled=True)

    chunk_grads[-1] = after(chunk_grads[-1], payload)
    last_send, last_keep, last_received = weight_terms(CHUNKS - 1)
    last_terms = chip_terms(after(last_keep, first_moved), last_received)
    last_moved = exchange_chips(last_terms)
    out_part = transposed_left(att_plane, after(branch_plane, last_send)[:, :width])
    first_rows = frame_rows([after(first_moved, last_terms), out_part[None]])
    first_frames = send_rows_on(first_rows)
    all_plane = plane * frame_size
    block_rows = min(512, all_plane)
    row_block = pl.BlockSpec((block_rows, width), lambda i: (i, 0))
    hidden_block = pl.BlockSpec((block_rows, hidden_shard), lambda i: (i, 0))
    hidden, grad_up = pl.pallas_call(
        feed_back_kernel,
        grid=(all_plane // block_rows,),
        in_specs=[row_block, row_block, whole, whole],
        out_specs=[hidden_block, hidden_block],
        out_shape=[struct((all_plane, hidden_shard), BF16)] * 2,
        cost_estimate=cost(15),
        compiler_params=params,
    )(after(ffn_all, *first_rows), low_all, up_slice, down_weight)

    def outer(left, right, tile, kind):
        rows, columns = left.shape
        shape = (columns, right.shape[1])
        return pl.pallas_call(
            outer_kernel,
            grid=(columns // tile,),
            in_specs=[pl.BlockSpec((rows, tile), lambda i: (0, i)), whole],
            out_specs=pl.BlockSpec((tile, shape[1]), lambda i: (i, 0)),
            out_shape=struct(shape, kind),
            cost_estimate=cost(9.5),
            compiler_params=params,
        )(left, right)

    first_total = total_of(first_frames).astype(BF16)
    first_placed = spread_on(first_total, "frames")
    last_rows = frame_rows([after(last_moved, hidden)])
    last_frames = send_rows_on(last_rows)
    up_part = outer(ffn_all, after(grad_up, first_total, *last_rows), width // 4, BF16)
    result_sum = lax.psum_scatter(
        after(result_part, hidden).reshape(-1, width), "items", scatter_dimension=0, tiled=True
    )
    up_moved = lax.all_to_all(up_part, "items", 0, 1, tiled=True)
    up_grad = up_moved.astype(F32)
    last_total = total_of(last_frames).astype(BF16)
    last_placed = spread_on(last_total, "frames")
    down_grad = outer(
        after(hidden, up_part, last_total, *first_placed),
        low_all,
        256 if hidden_shard % 256 == 0 else hidden_shard,
        F32,
    )
    placed = first_placed + last_placed
    payload_part = after(payload_part, last_total, up_part)
    payload_others = spread_on(payload_part.astype(BF16), "frames")[1:]
    sums = lax.all_gather(
        total_of([payload_part] + payload_others), "items", axis=0, tiled=True
    )
    query_low = sums[lats : 2 * lats].astype(BF16)
    query_grad = transposed_left(lat_cols, query_low)
    norm_cols = after(transposed_right(query_low, query_weight), up_moved, *last_placed)
    latents_grad, lat_gain, lat_bias = pl.pallas_call(
        functools.partial(query_norm_kernel, devices=item_size, items=items),
        in_specs=[smem] + [whole] * (item_size + 3),
        out_specs=[whole] * 3,
        out_shape=[struct((lats, width), F32), struct((1, width), F32), struct((1, width), F32)],
        scratch_shapes=[pltpu.VMEM((item_size, lats, shard), F32)],
        cost_estimate=cost(3),
        compiler_params=params,
    )(flags, *spread_across(norm_cols, "items"), latents, latent_gain[None], sums)
    at = 2 * lats
    column_sums = lax.dynamic_slice_in_dim(
        sums[at + 8 : at + 24], item_index * shard, shard, 1
    )

    key_grad, value_grad, out_grad = pl.pallas_call(
        functools.partial(
            place_kernel, chunks=CHUNKS, frames=frame_size, items=items, groups=groups
        ),
        in_specs=[smem] + [whole] * len(placed),
        out_specs=[whole] * 3,
        out_shape=[struct((frame_size, shard // frame_size, width), F32)] * 3,
        cost_estimate=cost(3.4),
        compiler_params=params,
    )(flags, *placed)

    result = mid_rows + result_sum.astype(F32)
    return (
        result.reshape(items, row_total, width),
        entropy,
        media_grad.reshape(media.shape),
        latents_grad,
        column_sums[:frame_total],
        column_sums[8],
        column_sums[9],
        lat_gain.reshape(width),
        lat_bias.reshape(width),
        sums[at],
        sums[at + 1],
        query_grad,
        key_grad.reshape(shard, width),
        value_grad.reshape(shard, width),
        out_grad.reshape(shard, width),
        up_grad,
        down_grad,
    )


def solution(mesh):
    return jax.shard_map(
        body,
        mesh=mesh,
        in_specs=(
            P("items", "frames", None, None),
            P("items", "frames", None),
            P(),
            P(),
            P(),
            P(),
            P(),
            P(),
            P(),
            P(),
            P(),
            P(),
            P("items", None),
            P("items", None),
            P("items", None),
            P("items", None),
            P("items", None),
            P("items", None),
        ),
        out_specs=(
            P("items", "frames", None),
            P("items", "frames"),
            P("items", "frames", None, None),
            P(),
            P(None, "items"),
            P("items"),
            P("items"),
            P(),
            P(),
            P(),
            P(),
            P("items", None),
            P("items", None),
            P("items", None),
            P("items", None),
            P("items", None),
            P("items", None),
        ),
        check_vma=False,
    )
```
